32 devices in a mesh: fsdp: 4 (over y, core), context: 2 (over x), tensor: 4 (over z).
Axes of the slice: x: 2, y: 2, z: 4, core: 2. Of those that a mesh axis runs over, the one named last changes fastest.
Arguments:
- tokens: bfloat16 [6144, 2048], P(('fsdp', 'context'), 'tensor'), may hold values from -45 to 45
- w_qkv: bfloat16 [2048, 3, 2048], P('fsdp', None, 'tensor'), may hold values from -0.125 to 0.125
- w_out: bfloat16 [2048, 2048], P('tensor', 'fsdp'), may hold values from -2 to 2
- w_gate_up: bfloat16 [2048, 2, 8192], P('fsdp', None, 'tensor'), may hold values from -0.125 to 0.125
- w_down: bfloat16 [8192, 2048], P('tensor', 'fsdp'), may hold values from -0.125 to 0.125
- gains: bfloat16 [2, 2048], P(None, ('tensor', 'fsdp')), may hold values from 0.5 to 1.5
- seq_lengths: int32 [4, 6], P('fsdp'), may hold values from 0 to 1024, as said below
- cotangent: bfloat16 [6144, 2048], P(('fsdp', 'context'), 'tensor'), may hold values from -6 to 6
Outputs:
- block_out: bfloat16 [6144, 2048], P(('fsdp', 'context'), 'tensor')
- grad_tokens: bfloat16 [6144, 2048], P(('fsdp', 'context'), 'tensor')
- grad_qkv: float32 [2048, 3, 2048], P('fsdp', None, 'tensor')
- grad_out: float32 [2048, 2048], P('tensor', 'fsdp')
- grad_gate_up: float32 [2048, 2, 8192], P('fsdp', None, 'tensor')
- grad_down: float32 [8192, 2048], P('tensor', 'fsdp')
- grad_gains: float32 [2, 2048], P(None, ('tensor', 'fsdp'))
The draws below stay inside these ranges and needn't reach their ends.
Inputs may be any that keep to these rules, and one draw needn't show every extreme that they name: `seq_lengths`: row g lists in order the lengths of the causal sequences packed into the tokens of group g; each row sums to 1536; zeros are unused slots; the largest entry of each row is exactly 1024, and that sequence holds the places 768 - 1 and 768 of its group.
All inputs are finite; a program needn't handle non-finite values.
Results may differ from the reference program's by a relative error of at most 0.015.
Values may be sent and summed in bfloat16 or wider, within the bound.
No kernel may reach another device: no remote copies, remote signals or barrier semaphores. Data moves between devices by JAX's collectives and lax.ppermute only.
A program may use at most 256 MiB of HBM per device.

```python
import jax
import jax.numpy as jnp
from jax import lax

D = 2048
HEADS = 32
FF = 8192
TOK_DEV = 768
QBLOCK = 512
SEQ_MAX = 1024
GROUP_TOK = 1536
GROUPS = 4
TOKENS = 6144
SEQS = 6


def draw_tokens(key, part):
    key = jax.random.fold_in(key, 11)
    noise_key, row_key, column_key = jax.random.split(key, 3)
    noise = jax.random.truncated_normal(noise_key, -4.0, 4.0, (TOKENS, D), jnp.float32)
    row_scales = jnp.exp(jax.random.uniform(row_key, (TOKENS, 1), jnp.float32, -1.2, 1.2))
    column_scales = jnp.exp(jax.random.uniform(column_key, (1, D), jnp.float32, -1.2, 1.2))
    return (noise * row_scales * column_scales).astype(jnp.bfloat16)


def draw_seq_lengths(key, part):
    key = jax.random.fold_in(key, 7)
    start_key, piece_key = jax.random.split(key, 2)
    lowest = max(1, TOK_DEV + 1 - SEQ_MAX)
    highest = min(TOK_DEV - 1, GROUP_TOK - SEQ_MAX, SEQ_MAX)
    leading = jax.random.randint(start_key, (GROUPS,), lowest, highest + 1).astype(jnp.int32)
    trailing = (GROUP_TOK - SEQ_MAX - leading).astype(jnp.int32)
    tail_count = SEQS - 2
    reaches = jax.random.randint(piece_key, (GROUPS, tail_count), SEQ_MAX // 2, SEQ_MAX + 1).astype(jnp.int32)
    before = (jnp.cumsum(reaches, axis=1) - reaches).astype(jnp.int32)
    pieces = jnp.clip(trailing[:, None] - before, 0, reaches).astype(jnp.int32)
    longest = jnp.full((GROUPS, 1), SEQ_MAX, jnp.int32)
    return jnp.concatenate([leading[:, None], longest, pieces], axis=1).astype(jnp.int32)


def levels(own_key, extent, cuts, smallest, largest):
    loudness = 1.0
    for dim, blocks in cuts:
        heights = jax.random.uniform(jax.random.fold_in(jax.random.fold_in(own_key, 6), dim), (blocks,), jnp.float32, smallest / len(cuts), largest / len(cuts))
        loudness = loudness * jnp.repeat(jnp.exp(heights), extent[dim] // blocks).reshape((-1,) + (1,) * (len(extent) - 1 - dim))
    return loudness


def centred(rng, dims, width, bound, shards=(), held_as=jnp.bfloat16):
    array = width * jax.random.normal(rng, dims, jnp.float32)
    if shards:
        array = array * levels(rng, dims, shards, -0.22, 0.18)
    return jnp.clip(array, -bound, bound).astype(held_as)


def setup_inputs(seed: int = 0) -> dict:
    arg_keys = jax.random.split(jax.random.key(seed), 9)
    tokens = draw_tokens(jax.random.fold_in(arg_keys[8], 71), 0)
    w_qkv = centred(arg_keys[1], (D, 3, D), D ** -0.5, 0.125, ((0, 4), (2, 4)))
    w_out = centred(arg_keys[2], (D, D), (max(1, D // 256)) ** -0.5, 2.0, ((0, 4), (1, 4)))
    w_gate_up = centred(arg_keys[3], (D, 2, FF), D ** -0.5, 0.125, ((0, 4), (2, 4)))
    w_down = centred(arg_keys[4], (FF, D), (FF // 4) ** -0.5, 0.125, ((0, 4), (1, 4)))
    gains = jnp.clip(1.0 + 0.1 * jax.random.normal(arg_keys[5], (2, D), jnp.float32), 0.5, 1.5).astype(jnp.bfloat16)
    seq_lengths = draw_seq_lengths(jax.random.fold_in(arg_keys[8], 71), 0)
    cotangent = centred(arg_keys[7], (TOKENS, D), 1.0, 6.0, ((0, 8), (1, 4)))
    return dict(tokens=tokens, w_qkv=w_qkv, w_out=w_out, w_gate_up=w_gate_up, w_down=w_down, gains=gains, seq_lengths=seq_lengths, cotangent=cotangent)


@jax.custom_vjp
def low(v):
    return lax.optimization_barrier(v.astype(jnp.bfloat16)).astype(jnp.float32)

@jax.custom_vjp
def low_back(v):
    return v

def low_keep(v):
    return (low(v), None)

def low_pass(kept, grad):
    return (grad,)

def back_keep(v):
    return (v, None)

def back_low(kept, grad):
    return (low(grad),)
low.defvjp(low_keep, low_pass)
low_back.defvjp(back_keep, back_low)
precise = lax.Precision.HIGHEST
norm_eps = 1e-05
rope_base = 130000.0
masked_score = -1e+30

def sequence_layout(lengths_row, row_count):
    ending = jnp.cumsum(lengths_row).astype(jnp.int32)
    starts = (ending - lengths_row).astype(jnp.int32)
    places = jnp.arange(row_count, dtype=jnp.int32)
    seg_ids = lax.optimization_barrier(jnp.sum((ending[None, :] <= places[:, None]).astype(jnp.int32), axis=1)).astype(jnp.int32)
    first_token = lax.optimization_barrier(jnp.max(jnp.where(starts[None, :] <= places[:, None], starts[None, :], 0), axis=1)).astype(jnp.int32)
    return (seg_ids, (places - first_token).astype(jnp.int32))

def rotary(values_in, positions, direction):
    half_dim = values_in.shape[-1] // 2
    frequencies = rope_base ** (-2.0 * jnp.arange(half_dim, dtype=jnp.float32) / values_in.shape[-1])
    angles = positions.astype(jnp.float32)[:, None] * frequencies[None, :]
    cosine = jnp.cos(angles)[:, None, :]
    sine_part = direction * jnp.sin(angles)[:, None, :]
    first_half = values_in[..., :half_dim]
    second_half = values_in[..., half_dim:]
    return jnp.concatenate([first_half * cosine - second_half * sine_part, second_half * cosine + first_half * sine_part], axis=-1)

def block_mask(seg_ids, q_start, k_start, q_count, band_rows):
    q_ids = lax.dynamic_slice_in_dim(seg_ids, q_start, q_count)
    k_ids = lax.dynamic_slice_in_dim(seg_ids, k_start, band_rows)
    q_place = q_start + jnp.arange(q_count, dtype=jnp.int32)
    k_place = k_start + jnp.arange(band_rows, dtype=jnp.int32)
    return (q_ids[:, None] == k_ids[None, :]) & (k_place[None, :] <= q_place[:, None])

def attention(queries, keys_in, values_in, seg_ids):
    row_count = queries.shape[0]
    band_rows = SEQ_MAX + QBLOCK
    scaling = queries.shape[-1] ** (-0.5)

    def one_block(block_index):
        q_start = (block_index * QBLOCK).astype(jnp.int32)
        k_start = jnp.clip(q_start - SEQ_MAX, 0, row_count - band_rows).astype(jnp.int32)
        q_block = lax.dynamic_slice_in_dim(queries, q_start, QBLOCK, 0)
        k_band = lax.dynamic_slice_in_dim(keys_in, k_start, band_rows, 0)
        v_band = lax.dynamic_slice_in_dim(values_in, k_start, band_rows, 0)
        raw_scores = jnp.einsum('qhd,khd->hqk', q_block, k_band, precision=precise) * scaling
        scores = low_back(raw_scores)
        allowed = block_mask(seg_ids, q_start, k_start, QBLOCK, band_rows)
        scores = jnp.where(allowed[None], scores, masked_score)
        peak_score = lax.optimization_barrier(jnp.max(scores, axis=2, keepdims=True))
        weights_exp = jnp.exp(scores - peak_score)
        attn_probs = weights_exp / lax.optimization_barrier(jnp.sum(weights_exp, axis=2, keepdims=True))
        return jnp.einsum('hqk,khd->qhd', low(attn_probs), v_band, precision=precise)
    blocks = lax.map(jax.checkpoint(one_block), jnp.arange(row_count // QBLOCK, dtype=jnp.int32))
    return blocks.reshape(row_count, queries.shape[1], queries.shape[2])

def rms_scale(stream):
    return lax.rsqrt(lax.optimization_barrier(jnp.mean(stream * stream, axis=1, keepdims=True)) + norm_eps)

def group_forward(stream, params, lengths_row):
    w_qkv, w_out, w_gate_up, w_down, gains = params
    row_count = stream.shape[0]
    width_all = stream.shape[1]
    seg_ids, positions = sequence_layout(lengths_row, row_count)
    normed_in = low(stream * rms_scale(stream) * gains[0])
    projected = jnp.einsum('td,dce->tce', normed_in, w_qkv, precision=precise).reshape(row_count, 3, HEADS, width_all // HEADS)
    queries = low(rotary(low_back(projected[:, 0]), positions, 1.0))
    keys_rot = low(rotary(low_back(projected[:, 1]), positions, 1.0))
    values_in = low_back(low(projected[:, 2]))
    attended = low_back(low(attention(queries, keys_rot, values_in, seg_ids).reshape(row_count, width_all)))
    branch = low_back(jnp.dot(attended, w_out, precision=precise))
    hidden_state = stream + branch
    normed_mid = low(hidden_state * rms_scale(hidden_state) * gains[1])
    gate_up = jnp.einsum('td,dcf->tcf', normed_mid, w_gate_up, precision=precise)
    gate_val = low_back(gate_up[:, 0])
    up_val = low_back(gate_up[:, 1])
    activated = low(gate_val * jax.nn.sigmoid(gate_val) * up_val)
    mlp_out = low_back(jnp.dot(activated, w_down, precision=precise))
    return hidden_state + mlp_out

def reference(tokens, w_qkv, w_out, w_gate_up, w_down, gains, seq_lengths, cotangent):
    params = (w_qkv.astype(jnp.float32), w_out.astype(jnp.float32), w_gate_up.astype(jnp.float32), w_down.astype(jnp.float32), gains.astype(jnp.float32))
    group_rows = tokens.shape[0] // GROUPS
    streams = tokens.astype(jnp.float32).reshape(GROUPS, group_rows, tokens.shape[1])
    cot_groups = cotangent.astype(jnp.float32).reshape(GROUPS, group_rows, tokens.shape[1])

    def one_group(totals, inputs):
        stream, lengths_row, cot_rows = inputs

        def forward(stream_in, params_in):
            return group_forward(stream_in, params_in, lengths_row)
        outputs, pullback = jax.vjp(forward, stream, params)
        grad_stream, grad_params = pullback(cot_rows)
        totals = jax.tree.map(lambda left, right: left + right, totals, grad_params)
        return (totals, (outputs.astype(jnp.bfloat16), grad_stream.astype(jnp.bfloat16)))
    zero_grads = jax.tree.map(jnp.zeros_like, params)
    totals, (outputs, grad_streams) = lax.scan(one_group, zero_grads, (streams, seq_lengths, cot_groups))
    return (outputs.reshape(tokens.shape), grad_streams.reshape(tokens.shape), totals[0], totals[1], totals[2], totals[3], totals[4])
```

```python
import functools

import jax
import jax.numpy as jnp
from jax import lax
from jax.experimental import pallas as pl
from jax.experimental.pallas import tpu as pltpu
from jax.sharding import PartitionSpec as P

HDIM = 64
LANES = 128
QROWS = 256
norm_eps = 1e-05
rope_base = 130000.0
masked_score = -1e30
BF = jnp.bfloat16
F32 = jnp.float32
VMEM_BYTES = 56 * 1024 * 1024


def dotf(a, b, dims):
    return lax.dot_general(a, b, (dims, ((), ())), preferred_element_type=F32)


NN = ((1,), (0,))
NT = ((1,), (1,))
TN = ((0,), (0,))


def swap(value, axis, bit):
    count = lax.axis_size(axis)
    return lax.ppermute(value, axis, [(i, i ^ bit) for i in range(count)])


def assemble_kernel(axis, *refs):
    pieces, out, sems = refs[:-2], refs[-2], refs[-1]
    me = lax.axis_index("fsdp")
    size = pieces[0].shape[axis]
    copies = []
    for j, piece in enumerate(pieces):
        start = pl.multiple_of((me ^ j) * size, size)
        window = [slice(None)] * len(out.shape)
        window[axis] = pl.ds(start, size)
        copies.append(pltpu.make_async_copy(piece, out.at[tuple(window)], sems.at[j]))
    for copy in copies:
        copy.start()
    for copy in copies:
        copy.wait()


def assemble(pieces, axis):
    shape = list(pieces[0].shape)
    shape[axis] *= len(pieces)
    return pl.pallas_call(
        functools.partial(assemble_kernel, axis),
        out_shape=jax.ShapeDtypeStruct(tuple(shape), pieces[0].dtype),
        in_specs=[pl.BlockSpec(memory_space=pl.ANY)] * len(pieces),
        out_specs=pl.BlockSpec(memory_space=pl.ANY),
        scratch_shapes=[pltpu.SemaphoreType.DMA((len(pieces),))],
    )(*pieces)


def gather_fsdp(own, axis):
    far = swap(own, "fsdp", 2)
    near = swap(own, "fsdp", 1)
    far_near = swap(far, "fsdp", 1)
    return assemble([own, near, far, far_near], axis)


def swap_halves(block):
    lane = lax.broadcasted_iota(jnp.int32, block.shape, 1)
    up = pltpu.roll(block, LANES - HDIM // 2, 1)
    down = pltpu.roll(block, HDIM // 2, 1)
    return jnp.where((lane & (HDIM - 1)) < HDIM // 2, up, down)


def rope_tables(positions):
    lane = jnp.arange(LANES, dtype=jnp.int32)
    half = lane % (HDIM // 2)
    frequencies = rope_base ** (-2.0 * half.astype(F32) / HDIM)
    angles = positions.astype(F32)[:, None] * frequencies[None, :]
    sign = jnp.where((lane % HDIM) < HDIM // 2, -1.0, 1.0)
    return jnp.cos(angles), jnp.sin(angles) * sign[None, :]


def project_kernel(kinds, x_ref, w_ref, cos_ref, sin_ref, out_ref):
    rows, width = out_ref.shape[1:]
    step = pl.program_id(0)
    for index, scale in enumerate(kinds):

        @pl.when(step == index)
        def _():
            for r in range(0, rows, QROWS):
                part = dotf(x_ref[r : r + QROWS, :], w_ref[0], NN)
                for c in range(0, width, LANES):
                    block = part[:, c : c + LANES]
                    if scale:
                        cos, sin = cos_ref[r : r + QROWS, :], sin_ref[r : r + QROWS, :]
                        block = block * cos + swap_halves(block) * sin
                    low = block.astype(BF)
                    if scale and scale != 1.0:
                        low = low * jnp.asarray(scale, BF)
                    out_ref[0, r : r + QROWS, c : c + LANES] = low


def project(x, w, cos, sin, kinds, first):
    rows, depth = x.shape
    width = w.shape[2]
    flops = 2 * len(kinds) * rows * depth * width
    return pl.pallas_call(
        functools.partial(project_kernel, kinds),
        grid=(len(kinds),),
        out_shape=jax.ShapeDtypeStruct((len(kinds), rows, width), BF),
        in_specs=[
            pl.BlockSpec((rows, depth), lambda i: (0, 0)),
            pl.BlockSpec((1, depth, width), lambda i: (i + first, 0, 0)),
            pl.BlockSpec((rows, LANES), lambda i: (0, 0)),
            pl.BlockSpec((rows, LANES), lambda i: (0, 0)),
        ],
        out_specs=pl.BlockSpec((1, rows, width), lambda i: (i, 0, 0)),
        compiler_params=pltpu.CompilerParams(vmem_limit_bytes=VMEM_BYTES),
        cost_estimate=pl.CostEstimate(
            flops=flops, bytes_accessed=2 * (x.size + w.size), transcendentals=0
        ),
    )(x, w, cos, sin)


def head_mask(block, head):
    lane = lax.broadcasted_iota(jnp.int32, block.shape, 1)
    inside = (lane < HDIM) if head == 0 else (lane >= HDIM)
    return jnp.where(inside, block, jnp.zeros_like(block))


def own_mask(key_count, row0, low_row):
    key = lax.broadcasted_iota(jnp.int32, (key_count, QROWS), 0)
    query = row0 + lax.broadcasted_iota(jnp.int32, (key_count, QROWS), 1)
    return (key >= low_row) & (key <= query)


def peer_mask(key_count, low_row, offset):
    key = lax.broadcasted_iota(jnp.int32, (key_count, QROWS), 0) - offset
    return key >= low_row


def own_forward_kernel(q_ref, k_ref, v_ref, low_ref, out_ref, log_ref):
    rows = q_ref.shape[0]
    v_t = v_ref[...].T
    for r in range(0, rows, QROWS):
        count = r + QROWS
        allowed = own_mask(count, r, low_ref[:, r : r + QROWS])
        keys = k_ref[0:count, :]
        outs = []
        for head in range(LANES // HDIM):
            scores = dotf(keys, head_mask(q_ref[r : r + QROWS, :], head), NT)
            scores = jnp.where(allowed, scores, masked_score)
            peak = jnp.max(scores, axis=0, keepdims=True)
            weights = jnp.exp(scores - peak)
            total = jnp.sum(weights, axis=0, keepdims=True)
            part = dotf(v_t[head * HDIM : (head + 1) * HDIM, 0:count], weights.astype(BF), NN)
            outs.append(part / total)
            log_ref[0, head : head + 1, r : r + QROWS] = peak + jnp.log(total)
        out_ref[r : r + QROWS, :] = jnp.concatenate(outs, axis=0).T


def peer_forward_kernel(
    need_ref, q_ref, k_ref, v_ref, low_ref, part_ref, log_in_ref, out_ref, log_ref
):
    rows = q_ref.shape[0]
    key_count = k_ref.shape[0]
    for index, r in enumerate(range(0, rows, QROWS)):
        needed = need_ref[index] < 0

        @pl.when(needed)
        def _():
            v_t = v_ref[...].T
            allowed = peer_mask(key_count, low_ref[:, r : r + QROWS], key_count)
            before = part_ref[r : r + QROWS, :].T
            outs = []
            for head in range(LANES // HDIM):
                scores = dotf(k_ref[...], head_mask(q_ref[r : r + QROWS, :], head), NT)
                scores = jnp.where(allowed, scores, masked_score)
                log_own = log_in_ref[0, head : head + 1, r : r + QROWS]
                peak = jnp.maximum(jnp.max(scores, axis=0, keepdims=True), log_own)
                weights = jnp.exp(scores - peak)
                own_weight = jnp.exp(log_own - peak)
                total = jnp.sum(weights, axis=0, keepdims=True) + own_weight
                rows_h = slice(head * HDIM, (head + 1) * HDIM)
                part = dotf(v_t[rows_h, :], weights.astype(BF), NN)
                outs.append((part + before[rows_h, :] * own_weight) / total)
                log_ref[0, head : head + 1, r : r + QROWS] = peak + jnp.log(total)
            out_ref[r : r + QROWS, :] = jnp.concatenate(outs, axis=0).T.astype(BF)

        @pl.when(jnp.logical_not(needed))
        def _():
            out_ref[r : r + QROWS, :] = part_ref[r : r + QROWS, :].astype(BF)
            log_ref[:, :, r : r + QROWS] = log_in_ref[:, :, r : r + QROWS]


def pair_spec(rows):
    return pl.BlockSpec((rows, LANES), lambda i: (0, i))


def log_spec(rows):
    return pl.BlockSpec((1, LANES // HDIM, rows), lambda i: (i, 0, 0))


def low_spec(rows):
    return pl.BlockSpec((1, rows), lambda i: (0, 0))


def attention_cost(rows, width, dots):
    area = rows * rows * width
    return pl.CostEstimate(
        flops=2 * dots * area, bytes_accessed=8 * rows * width, transcendentals=area // HDIM
    )


def own_forward(q, k, v, low_row):
    rows, width = q.shape
    pairs = width // LANES
    return pl.pallas_call(
        own_forward_kernel,
        grid=(pairs,),
        out_shape=(
            jax.ShapeDtypeStruct((rows, width), F32),
            jax.ShapeDtypeStruct((pairs, LANES // HDIM, rows), F32),
        ),
        in_specs=[pair_spec(rows)] * 3 + [low_spec(rows)],
        out_specs=(pair_spec(rows), log_spec(rows)),
        compiler_params=pltpu.CompilerParams(vmem_limit_bytes=VMEM_BYTES),
        cost_estimate=attention_cost(rows, width, 2),
    )(q, k, v, low_row)


SMEM_SPEC = pl.BlockSpec(memory_space=pltpu.SMEM)


def peer_forward(need, q, k, v, low_row, part, log_in):
    rows, width = q.shape
    pairs = width // LANES
    return pl.pallas_call(
        peer_forward_kernel,
        grid=(pairs,),
        out_shape=(
            jax.ShapeDtypeStruct((rows, width), BF),
            jax.ShapeDtypeStruct((pairs, LANES // HDIM, rows), F32),
        ),
        in_specs=[SMEM_SPEC]
        + [pair_spec(rows)] * 3
        + [low_spec(rows), pair_spec(rows), log_spec(rows)],
        out_specs=(pair_spec(rows), log_spec(rows)),
        compiler_params=pltpu.CompilerParams(vmem_limit_bytes=VMEM_BYTES),
        cost_estimate=attention_cost(rows, width, 2),
    )(need, q, k, v, low_row, part, log_in)


def backward_block(q_rows, k_rows, v_rows, k_t, do_rows, do_o_t, logs, allowed):
    d_query, d_key, d_value = [], None, None
    for head in range(LANES // HDIM):
        rows_h = slice(head * HDIM, (head + 1) * HDIM)
        q_head = head_mask(q_rows, head)
        do_head = head_mask(do_rows, head)
        scores = dotf(k_rows, q_head, NT)
        probs = jnp.exp(jnp.where(allowed, scores, masked_score) - logs[head])
        delta = jnp.sum(do_o_t[rows_h, :], axis=0, keepdims=True)
        d_probs = dotf(v_rows, do_head, NT)
        d_scores = (probs * (d_probs - delta)).astype(BF)
        d_v = dotf(probs.astype(BF), do_head, NN)
        d_k = dotf(d_scores, q_head, NN)
        d_value = d_v if d_value is None else d_value + d_v
        d_key = d_k if d_key is None else d_key + d_k
        d_query.append(dotf(k_t[rows_h, :], d_scores, NN))
    return jnp.concatenate(d_query, axis=0), d_key, d_value


def output_product(do_ref, o_ref, window):
    product = do_ref[window].astype(F32) * o_ref[window].astype(F32)
    return product.T


def peer_backward_kernel(
    need_ref, q_ref, k_ref, v_ref, do_ref, o_ref, low_ref, log_ref, dq_ref, dk_ref, dv_ref, sums
):
    rows = q_ref.shape[0]
    key_count = k_ref.shape[0]
    sums[...] = jnp.zeros_like(sums)
    for index, r in enumerate(range(0, rows, QROWS)):
        needed = need_ref[index] < 0
        window = (slice(r, r + QROWS), slice(None))

        @pl.when(needed)
        def _():
            allowed = peer_mask(key_count, low_ref[:, r : r + QROWS], key_count)
            logs = [log_ref[0, h : h + 1, r : r + QROWS] for h in range(LANES // HDIM)]
            d_query, d_key, d_value = backward_block(
                q_ref[window],
                k_ref[...],
                v_ref[...],
                k_ref[...].T,
                do_ref[window],
                output_product(do_ref, o_ref, window),
                logs,
                allowed,
            )
            dq_ref[window] = d_query.T
            sums[0] += d_key
            sums[1] += d_value

        @pl.when(jnp.logical_not(needed))
        def _():
            dq_ref[window] = jnp.zeros((QROWS, LANES), F32)

    dk_ref[...] = sums[0].astype(BF)
    dv_ref[...] = sums[1].astype(BF)


def peer_backward(need, q, k, v, do, o, low_row, logs):
    rows, width = q.shape
    pairs = width // LANES
    return pl.pallas_call(
        peer_backward_kernel,
        grid=(pairs,),
        out_shape=(
            jax.ShapeDtypeStruct((rows, width), F32),
            jax.ShapeDtypeStruct((rows, width), BF),
            jax.ShapeDtypeStruct((rows, width), BF),
        ),
        in_specs=[SMEM_SPEC] + [pair_spec(rows)] * 5 + [low_spec(rows), log_spec(rows)],
        out_specs=(pair_spec(rows),) * 3,
        scratch_shapes=[pltpu.VMEM((2, rows, LANES), F32)],
        compiler_params=pltpu.CompilerParams(vmem_limit_bytes=VMEM_BYTES),
        cost_estimate=attention_cost(rows, width, 5),
    )(need, q, k, v, do, o, low_row, logs)


def own_backward_kernel(
    q_ref,
    k_ref,
    v_ref,
    do_ref,
    o_ref,
    low_ref,
    log_ref,
    dq_in_ref,
    cos_ref,
    sin_ref,
    dq_ref,
    dk_ref,
    dv_ref,
    sums,
):
    rows = q_ref.shape[0]
    sums[...] = jnp.zeros_like(sums)
    k_t = k_ref[...].T
    for r in range(0, rows, QROWS):
        count = r + QROWS
        window = (slice(r, r + QROWS), slice(None))
        allowed = own_mask(count, r, low_ref[:, r : r + QROWS])
        logs = [log_ref[0, h : h + 1, r : r + QROWS] for h in range(LANES // HDIM)]
        d_query, d_key, d_value = backward_block(
            q_ref[window],
            k_ref[0:count, :],
            v_ref[0:count, :],
            k_t[:, 0:count],
            do_ref[window],
            output_product(do_ref, o_ref, window),
            logs,
            allowed,
        )
        rotated = (d_query.T + dq_in_ref[window]) * (HDIM**-0.5)
        turned = rotated * cos_ref[window] - swap_halves(rotated) * sin_ref[window]
        dq_ref[window] = turned.astype(BF)
        sums[0, 0:count] += d_key
        sums[1, 0:count] += d_value
    dk_ref[...] = sums[0]
    dv_ref[...] = sums[1]


def own_backward(q, k, v, do, o, low_row, logs, dq_in, cos, sin):
    rows, width = q.shape
    pairs = width // LANES
    table = pl.BlockSpec((rows, LANES), lambda i: (0, 0))
    return pl.pallas_call(
        own_backward_kernel,
        grid=(pairs,),
        out_shape=(
            jax.ShapeDtypeStruct((rows, width), BF),
            jax.ShapeDtypeStruct((rows, width), F32),
            jax.ShapeDtypeStruct((rows, width), F32),
        ),
        in_specs=[pair_spec(rows)] * 5
        + [low_spec(rows), log_spec(rows), pair_spec(rows), table, table],
        out_specs=(pair_spec(rows),) * 3,
        scratch_shapes=[pltpu.VMEM((2, rows, LANES), F32)],
        compiler_params=pltpu.CompilerParams(vmem_limit_bytes=VMEM_BYTES),
        cost_estimate=attention_cost(rows, width, 5),
    )(q, k, v, do, o, low_row, logs, dq_in, cos, sin)


def finish_keys_kernel(dk_ref, dv_ref, dk_in_ref, dv_in_ref, cos_ref, sin_ref, dk_out, dv_out):
    total = dk_ref[...] + dk_in_ref[...].astype(F32)
    turned = total * cos_ref[...] - swap_halves(total) * sin_ref[...]
    dk_out[...] = turned.astype(BF)
    dv_out[...] = (dv_ref[...] + dv_in_ref[...].astype(F32)).astype(BF)


def finish_keys(dk, dv, dk_in, dv_in, cos, sin):
    rows, width = dk.shape
    pairs = width // LANES
    table = pl.BlockSpec((rows, LANES), lambda i: (0, 0))
    return pl.pallas_call(
        finish_keys_kernel,
        grid=(pairs,),
        out_shape=(jax.ShapeDtypeStruct((rows, width), BF),) * 2,
        in_specs=[pair_spec(rows)] * 4 + [table, table],
        out_specs=(pair_spec(rows),) * 2,
        cost_estimate=pl.CostEstimate(
            flops=8 * rows * width, bytes_accessed=16 * rows * width, transcendentals=0
        ),
    )(dk, dv, dk_in, dv_in, cos, sin)


def hidden_kernel(x_ref, cot_ref, wgu_ref, wd_ref, act_ref, dg_ref, du_ref):
    rows = x_ref.shape[0]
    for r in range(0, rows, QROWS):
        part = slice(r, r + QROWS)
        gate = dotf(x_ref[part, :], wgu_ref[0], NN)
        up = dotf(x_ref[part, :], wgu_ref[1], NN)
        d_act = dotf(cot_ref[part, :], wd_ref[...], NT)
        sig = jax.nn.sigmoid(gate)
        silu = gate * sig
        act_ref[part, :] = (silu * up).astype(BF)
        dg_ref[part, :] = (d_act * up * sig * (1.0 + gate * (1.0 - sig))).astype(BF)
        du_ref[part, :] = (d_act * silu).astype(BF)


def hidden_units(x, cot, w_gate_up, w_down):
    rows, depth = x.shape
    units = w_down.shape[0]
    tile = 256
    whole = pl.BlockSpec((rows, depth), lambda i: (0, 0))
    part = pl.BlockSpec((rows, tile), lambda i: (0, i))
    return pl.pallas_call(
        hidden_kernel,
        grid=(units // tile,),
        out_shape=(jax.ShapeDtypeStruct((rows, units), BF),) * 3,
        in_specs=[
            whole,
            whole,
            pl.BlockSpec((2, depth, tile), lambda i: (0, 0, i)),
            pl.BlockSpec((tile, depth), lambda i: (i, 0)),
        ],
        out_specs=(part,) * 3,
        compiler_params=pltpu.CompilerParams(vmem_limit_bytes=VMEM_BYTES),
        cost_estimate=pl.CostEstimate(
            flops=6 * rows * depth * units,
            bytes_accessed=2 * (2 * x.size + 3 * w_down.size + 3 * rows * units),
            transcendentals=rows * units,
        ),
    )(x, cot, w_gate_up, w_down)


def block_of(x, j, count):
    size = x.shape[1] // count
    return lax.dynamic_slice_in_dim(x, (lax.axis_index("fsdp") ^ j) * size, size, 1)


def reduce_grad(make):
    sent = jnp.stack([make(1).astype(BF), make(3).astype(BF)])
    got = swap(sent, "fsdp", 1).astype(F32)
    far = swap((make(2) + got[1]).astype(BF), "fsdp", 2).astype(F32)
    mine = (make(0) + got[0] + far).astype(BF)
    other = swap(mine, "context", 1)
    return mine.astype(F32) + other.astype(F32)


def row_sum(values_in):
    return jnp.sum(values_in, axis=1, keepdims=True)


def per_device(tokens, w_qkv, w_out, w_gate_up, w_down, gains, seq_lengths, cotangent):
    row_count, part_width = tokens.shape
    tensor_index = lax.axis_index("tensor")
    context_index = lax.axis_index("context")
    shards = lax.axis_size("fsdp")
    full_width = part_width * lax.axis_size("tensor")

    def features(part_in):
        return lax.all_gather(part_in, "tensor", axis=1, tiled=True)

    def feature_sum(term):
        return lax.psum_scatter(term.astype(BF), "tensor", scatter_dimension=1, tiled=True)

    def own_features(full):
        return lax.dynamic_slice_in_dim(full, tensor_index * part_width, part_width, 1)

    ending = jnp.cumsum(seq_lengths[0])
    starts = ending - seq_lengths[0]
    places = context_index * row_count + jnp.arange(row_count, dtype=jnp.int32)
    first_token = jnp.max(jnp.where(starts[None, :] <= places[:, None], starts[None, :], 0), axis=1)
    cos, sin = rope_tables(places - first_token)
    low = first_token - context_index * row_count
    low_row = low[None, :]
    need = low[::QROWS]

    gain_full = lax.all_gather(gains, ("tensor", "fsdp"), axis=1, tiled=True).astype(F32)
    gain_attn, gain_mlp = gain_full[0:1], gain_full[1:2]
    token_low = features(tokens)
    qkv_full = gather_fsdp(jnp.swapaxes(w_qkv, 0, 1), 1)
    out_rows = lax.all_gather(w_out, "tensor", axis=0, tiled=True)
    gate_up_full = gather_fsdp(jnp.swapaxes(w_gate_up, 0, 1), 1)
    out_full = gather_fsdp(out_rows, 1)
    down_full = gather_fsdp(w_down, 1)
    cot_full = features(cotangent)

    stream = token_low.astype(F32)
    scale_attn = lax.rsqrt(row_sum(stream * stream) / full_width + norm_eps)
    normed_in = (stream * scale_attn * gain_attn).astype(BF)
    keys_values = project(normed_in, qkv_full, cos, sin, (1.0, None), 1)
    keys, values = keys_values[0], keys_values[1]
    to_later = [(0, 1)]
    peer_keys = lax.ppermute(keys_values, "context", to_later)
    queries = project(normed_in, qkv_full, cos, sin, (HDIM**-0.5,), 0)[0]
    part, part_log = own_forward(queries, keys, values, low_row)
    attended, logs = peer_forward(
        need, queries, peer_keys[0], peer_keys[1], low_row, part, part_log
    )
    attended_full = features(attended)
    hidden = stream + dotf(attended_full, out_full, NN)

    scale_mlp = lax.rsqrt(row_sum(hidden * hidden) / full_width + norm_eps)
    normed_mid = (hidden * scale_mlp * gain_mlp).astype(BF)
    activated, d_gate, d_up = hidden_units(normed_mid, cot_full, gate_up_full, down_full)
    d_mid_term = dotf(d_gate, gate_up_full[0], NT) + dotf(d_up, gate_up_full[1], NT)
    d_mid = features(feature_sum(d_mid_term)).astype(F32)
    mlp_out = feature_sum(dotf(activated, down_full, NN)).astype(F32)
    block_out = (own_features(hidden) + mlp_out).astype(BF)

    grad_down = reduce_grad(lambda j: dotf(activated, block_of(cot_full, j, shards), TN))
    grad_gate = reduce_grad(lambda j: dotf(block_of(normed_mid, j, shards), d_gate, TN))
    grad_up = reduce_grad(lambda j: dotf(block_of(normed_mid, j, shards), d_up, TN))

    weighted = d_mid * gain_mlp
    inner = row_sum(weighted * hidden) / full_width
    d_hidden = (
        cot_full.astype(F32)
        + scale_mlp * weighted
        - hidden * scale_mlp * scale_mlp * scale_mlp * inner
    )
    gain_mlp_term = jnp.sum(d_mid * hidden * scale_mlp, axis=0)
    d_branch = d_hidden.astype(BF)

    out_own = lax.dynamic_slice_in_dim(
        out_full, tensor_index * attended.shape[1], attended.shape[1], 0
    )
    d_attended = dotf(d_branch, out_own, NT).astype(BF)
    dq_peer, dk_peer, dv_peer = peer_backward(
        need, queries, peer_keys[0], peer_keys[1], d_attended, attended, low_row, logs
    )
    to_earlier = [(1, 0)]
    dk_in = lax.ppermute(dk_peer, "context", to_earlier)
    dv_in = lax.ppermute(dv_peer, "context", to_earlier)
    d_query, dk_own, dv_own = own_backward(
        queries, keys, values, d_attended, attended, low_row, logs, dq_peer, cos, sin
    )
    d_key, d_value = finish_keys(dk_own, dv_own, dk_in, dv_in, cos, sin)
    d_parts = (d_query, d_key, d_value)

    grad_out = reduce_grad(lambda j: dotf(attended, block_of(d_branch, j, shards), TN))
    grad_qkv = jnp.stack(
        [
            reduce_grad(lambda j, d=d: dotf(block_of(normed_in, j, shards), d, TN))
            for d in d_parts
        ],
        axis=1,
    )
    d_in_term = sum(dotf(d_parts[c], qkv_full[c], NT) for c in range(3))
    d_in = feature_sum(d_in_term).astype(F32)
    inner_in = lax.psum(row_sum(d_in_term * gain_attn * stream), "tensor") / full_width
    gain_attn_term = jnp.sum(d_in_term * stream * scale_attn, axis=0)

    own_tokens = tokens.astype(F32)
    grad_tokens = (
        own_features(d_hidden)
        + scale_attn * own_features(gain_attn) * d_in
        - own_tokens * scale_attn * scale_attn * scale_attn * inner_in
    ).astype(BF)

    column = jnp.arange(full_width, dtype=jnp.int32)
    mine = column // part_width == tensor_index
    gain_terms = jnp.stack([gain_attn_term, jnp.where(mine, gain_mlp_term, 0.0)])
    gain_sums = lax.psum(gain_terms, ("fsdp", "context", "tensor"))
    gain_width = gains.shape[1]
    place = (tensor_index * shards + lax.axis_index("fsdp")) * gain_width
    grad_gains = lax.dynamic_slice_in_dim(gain_sums, place, gain_width, 1)

    grad_gate_up = jnp.stack([grad_gate, grad_up], axis=1)
    return (block_out, grad_tokens, grad_qkv, grad_out, grad_gate_up, grad_down, grad_gains)


def solution(mesh):
    rows = P(("fsdp", "context"), "tensor")
    inner = P("fsdp", None, "tensor")
    outer = P("tensor", "fsdp")
    gain = P(None, ("tensor", "fsdp"))
    return jax.shard_map(
        per_device,
        mesh=mesh,
        in_specs=(rows, inner, outer, inner, outer, gain, P("fsdp", None), rows),
        out_specs=(rows, rows, inner, outer, inner, outer, gain),
        check_vma=False,
    )
```

```python
import functools

import jax
import jax.numpy as jnp
from jax import lax
from jax.experimental import pallas as pl
from jax.experimental.pallas import tpu as pltpu
from jax.sharding import PartitionSpec as P

HDIM = 64
LANES = 128
QROWS = 256
norm_eps = 1e-05
rope_base = 130000.0
masked_score = -1e30
BF = jnp.bfloat16
F32 = jnp.float32
VMEM_BYTES = 56 * 1024 * 1024


def dotf(a, b, dims):
    return lax.dot_general(a, b, (dims, ((), ())), preferred_element_type=F32)


NN = ((1,), (0,))
NT = ((1,), (1,))
TN = ((0,), (0,))


def swap(value, axis, bit):
    count = lax.axis_size(axis)
    return lax.ppermute(value, axis, [(i, i ^ bit) for i in range(count)])


def gather_fsdp(own, after=None):
    if after is not None:
        own = lax.optimization_barrier((own, after))[0]
    far = swap(own, "fsdp", 2)
    near = swap(own, "fsdp", 1)
    far_near = swap(far, "fsdp", 1)
    return (own, near, far, far_near)


def piece_columns(j, size):
    return pl.ds(pl.multiple_of((lax.axis_index("fsdp") ^ j) * size, size), size)


def swap_halves(block):
    lane = lax.broadcasted_iota(jnp.int32, block.shape, 1)
    up = pltpu.roll(block, LANES - HDIM // 2, 1)
    down = pltpu.roll(block, HDIM // 2, 1)
    return jnp.where((lane & (HDIM - 1)) < HDIM // 2, up, down)


def rope_tables(positions):
    lane = jnp.arange(LANES, dtype=jnp.int32)
    half = lane % (HDIM // 2)
    frequencies = rope_base ** (-2.0 * half.astype(F32) / HDIM)
    angles = positions.astype(F32)[:, None] * frequencies[None, :]
    sign = jnp.where((lane % HDIM) < HDIM // 2, -1.0, 1.0)
    return jnp.cos(angles), jnp.sin(angles) * sign[None, :]


def piece_dot(x_ref, rows, pieces, dims=NN):
    total = None
    for j, piece in enumerate(pieces):
        size = piece.shape[dims[1][0]]
        term = dotf(x_ref[rows, piece_columns(j, size)], piece, dims)
        total = term if total is None else total + term
    return total


def project_kernel(kinds, normalize, x_ref, *refs):
    pieces, (cos_ref, sin_ref, gain_ref), outs = refs[:4], refs[4:7], refs[7:]
    out_ref = outs[0]
    rows, width = out_ref.shape[1:]
    step = pl.program_id(0)
    if normalize:
        normed_ref, scale_ref = outs[1], outs[2]

        @pl.when(step == 0)
        def _():
            for r in range(0, rows, QROWS):
                part = slice(r, r + QROWS)
                stream = x_ref[part, :].astype(F32)
                mean = jnp.sum(stream * stream, axis=1, keepdims=True) / x_ref.shape[1]
                scale = lax.rsqrt(mean + norm_eps)
                scale_ref[part, :] = scale
                normed_ref[part, :] = (stream * scale * gain_ref[...]).astype(BF)

        x_ref = normed_ref
    for index, scale in enumerate(kinds):

        @pl.when(step == index)
        def _():
            for r in range(0, rows, QROWS):
                part = slice(r, r + QROWS)
                result = piece_dot(x_ref, part, [piece[0] for piece in pieces])
                for c in range(0, width, LANES):
                    block = result[:, c : c + LANES]
                    if scale:
                        block = block * cos_ref[part, :] + swap_halves(block) * sin_ref[part, :]
                    low = block.astype(BF)
                    if scale and scale != 1.0:
                        low = low * jnp.asarray(scale, BF)
                    out_ref[0, part, c : c + LANES] = low


def project(x, pieces, cos, sin, gain, kinds, first, normalize):
    rows, depth = x.shape
    _, size, width = pieces[0].shape
    flops = 2 * len(kinds) * rows * depth * width
    whole = pl.BlockSpec((rows, depth), lambda i: (0, 0))
    table = pl.BlockSpec((rows, LANES), lambda i: (0, 0))
    out_shape = [jax.ShapeDtypeStruct((len(kinds), rows, width), BF)]
    out_specs = [pl.BlockSpec((1, rows, width), lambda i: (i, 0, 0))]
    if normalize:
        out_shape += [jax.ShapeDtypeStruct((rows, depth), BF), jax.ShapeDtypeStruct((rows, 1), F32)]
        out_specs += [whole, pl.BlockSpec((rows, 1), lambda i: (0, 0))]
    return pl.pallas_call(
        functools.partial(project_kernel, kinds, normalize),
        grid=(len(kinds),),
        out_shape=out_shape,
        in_specs=[whole]
        + [pl.BlockSpec((1, size, width), lambda i: (i + first, 0, 0))] * 4
        + [table, table, pl.BlockSpec((1, depth), lambda i: (0, 0))],
        out_specs=out_specs,
        compiler_params=pltpu.CompilerParams(vmem_limit_bytes=VMEM_BYTES),
        cost_estimate=pl.CostEstimate(
            flops=flops, bytes_accessed=2 * (x.size + depth * width * len(kinds)), transcendentals=0
        ),
    )(x, *pieces, cos, sin, gain)


def head_mask(block, head):
    lane = lax.broadcasted_iota(jnp.int32, block.shape, 1)
    inside = (lane < HDIM) if head == 0 else (lane >= HDIM)
    return jnp.where(inside, block, jnp.zeros_like(block))


def own_mask(key_count, row0, low_row):
    key = lax.broadcasted_iota(jnp.int32, (key_count, QROWS), 0)
    query = row0 + lax.broadcasted_iota(jnp.int32, (key_count, QROWS), 1)
    return (key >= low_row) & (key <= query)


def peer_mask(key_count, low_row, offset):
    key = lax.broadcasted_iota(jnp.int32, (key_count, QROWS), 0) - offset
    return key >= low_row


def own_forward_kernel(q_ref, k_ref, v_ref, low_ref, out_ref, log_ref):
    rows = q_ref.shape[0]
    v_t = v_ref[...].T
    for r in range(0, rows, QROWS):
        count = r + QROWS
        allowed = own_mask(count, r, low_ref[:, r : r + QROWS])
        keys = k_ref[0:count, :]
        outs = []
        for head in range(LANES // HDIM):
            scores = dotf(keys, head_mask(q_ref[r : r + QROWS, :], head), NT)
            scores = jnp.where(allowed, scores, masked_score)
            peak = jnp.max(scores, axis=0, keepdims=True)
            weights = jnp.exp(scores - peak)
            total = jnp.sum(weights, axis=0, keepdims=True)
            part = dotf(v_t[head * HDIM : (head + 1) * HDIM, 0:count], weights.astype(BF), NN)
            outs.append(part / total)
            log_ref[0, head : head + 1, r : r + QROWS] = peak + jnp.log(total)
        out_ref[r : r + QROWS, :] = jnp.concatenate(outs, axis=0).T


def peer_forward_kernel(
    need_ref, q_ref, k_ref, v_ref, low_ref, part_ref, log_in_ref, out_ref, log_ref
):
    rows = q_ref.shape[0]
    key_count = k_ref.shape[0]
    for index, r in enumerate(range(0, rows, QROWS)):
        needed = need_ref[index] < 0

        @pl.when(needed)
        def _():
            v_t = v_ref[...].T
            allowed = peer_mask(key_count, low_ref[:, r : r + QROWS], key_count)
            before = part_ref[r : r + QROWS, :].T
            outs = []
            for head in range(LANES // HDIM):
                scores = dotf(k_ref[...], head_mask(q_ref[r : r + QROWS, :], head), NT)
                scores = jnp.where(allowed, scores, masked_score)
                log_own = log_in_ref[0, head : head + 1, r : r + QROWS]
                peak = jnp.maximum(jnp.max(scores, axis=0, keepdims=True), log_own)
                weights = jnp.exp(scores - peak)
                own_weight = jnp.exp(log_own - peak)
                total = jnp.sum(weights, axis=0, keepdims=True) + own_weight
                rows_h = slice(head * HDIM, (head + 1) * HDIM)
                part = dotf(v_t[rows_h, :], weights.astype(BF), NN)
                outs.append((part + before[rows_h, :] * own_weight) / total)
                log_ref[0, head : head + 1, r : r + QROWS] = peak + jnp.log(total)
            out_ref[r : r + QROWS, :] = jnp.concatenate(outs, axis=0).T.astype(BF)

        @pl.when(jnp.logical_not(needed))
        def _():
            out_ref[r : r + QROWS, :] = part_ref[r : r + QROWS, :].astype(BF)
            log_ref[:, :, r : r + QROWS] = log_in_ref[:, :, r : r + QROWS]


def pair_spec(rows):
    return pl.BlockSpec((rows, LANES), lambda i: (0, i))


def stacked_spec(rows, part):
    return pl.BlockSpec((None, rows, LANES), lambda i: (part, 0, i))


def log_spec(rows):
    return pl.BlockSpec((1, LANES // HDIM, rows), lambda i: (i, 0, 0))


def low_spec(rows):
    return pl.BlockSpec((1, rows), lambda i: (0, 0))


def attention_cost(rows, width, dots):
    area = rows * rows * width
    return pl.CostEstimate(
        flops=2 * dots * area, bytes_accessed=8 * rows * width, transcendentals=area // HDIM
    )


def own_forward(q, kv, low_row):
    rows, width = q.shape
    pairs = width // LANES
    return pl.pallas_call(
        own_forward_kernel,
        grid=(pairs,),
        out_shape=(
            jax.ShapeDtypeStruct((rows, width), F32),
            jax.ShapeDtypeStruct((pairs, LANES // HDIM, rows), F32),
        ),
        in_specs=[
            pair_spec(rows),
            stacked_spec(rows, 0),
            stacked_spec(rows, 1),
            low_spec(rows),
        ],
        out_specs=(pair_spec(rows), log_spec(rows)),
        compiler_params=pltpu.CompilerParams(vmem_limit_bytes=VMEM_BYTES),
        cost_estimate=attention_cost(rows, width, 2),
    )(q, kv, kv, low_row)


SMEM_SPEC = pl.BlockSpec(memory_space=pltpu.SMEM)


def peer_forward(need, q, kv, low_row, part, log_in):
    rows, width = q.shape
    pairs = width // LANES
    return pl.pallas_call(
        peer_forward_kernel,
        grid=(pairs,),
        out_shape=(
            jax.ShapeDtypeStruct((rows, width), BF),
            jax.ShapeDtypeStruct((pairs, LANES // HDIM, rows), F32),
        ),
        in_specs=[
            SMEM_SPEC,
            pair_spec(rows),
            stacked_spec(rows, 0),
            stacked_spec(rows, 1),
            low_spec(rows),
            pair_spec(rows),
            log_spec(rows),
        ],
        out_specs=(pair_spec(rows), log_spec(rows)),
        compiler_params=pltpu.CompilerParams(vmem_limit_bytes=VMEM_BYTES),
        cost_estimate=attention_cost(rows, width, 2),
    )(need, q, kv, kv, low_row, part, log_in)


def backward_block(q_rows, k_rows, v_rows, k_t, do_rows, do_o_t, logs, allowed):
    d_query, d_key, d_value = [], None, None
    for head in range(LANES // HDIM):
        rows_h = slice(head * HDIM, (head + 1) * HDIM)
        q_head = head_mask(q_rows, head)
        do_head = head_mask(do_rows, head)
        scores = dotf(k_rows, q_head, NT)
        probs = jnp.exp(jnp.where(allowed, scores, masked_score) - logs[head])
        delta = jnp.sum(do_o_t[rows_h, :], axis=0, keepdims=True)
        d_probs = dotf(v_rows, do_head, NT)
        d_scores = (probs * (d_probs - delta)).astype(BF)
        d_v = dotf(probs.astype(BF), do_head, NN)
        d_k = dotf(d_scores, q_head, NN)
        d_value = d_v if d_value is None else d_value + d_v
        d_key = d_k if d_key is None else d_key + d_k
        d_query.append(dotf(k_t[rows_h, :], d_scores, NN))
    return jnp.concatenate(d_query, axis=0), d_key, d_value


def output_product(do_ref, o_ref, window):
    product = do_ref[window].astype(F32) * o_ref[window].astype(F32)
    return product.T


def peer_backward_kernel(
    need_ref, q_ref, k_ref, v_ref, do_ref, o_ref, low_ref, log_ref, dq_ref, dkv_ref, sums
):
    rows = q_ref.shape[0]
    key_count = k_ref.shape[0]
    sums[...] = jnp.zeros_like(sums)
    for index, r in enumerate(range(0, rows, QROWS)):
        needed = need_ref[index] < 0
        window = (slice(r, r + QROWS), slice(None))

        @pl.when(needed)
        def _():
            allowed = peer_mask(key_count, low_ref[:, r : r + QROWS], key_count)
            logs = [log_ref[0, h : h + 1, r : r + QROWS] for h in range(LANES // HDIM)]
            d_query, d_key, d_value = backward_block(
                q_ref[window],
                k_ref[...],
                v_ref[...],
                k_ref[...].T,
                do_ref[window],
                output_product(do_ref, o_ref, window),
                logs,
                allowed,
            )
            dq_ref[window] = d_query.T
            sums[0] += d_key
            sums[1] += d_value

        @pl.when(jnp.logical_not(needed))
        def _():
            dq_ref[window] = jnp.zeros((QROWS, LANES), F32)

    dkv_ref[...] = sums[...].astype(BF)


def peer_backward(need, q, kv, do, o, low_row, logs):
    rows, width = q.shape
    pairs = width // LANES
    return pl.pallas_call(
        peer_backward_kernel,
        grid=(pairs,),
        out_shape=(
            jax.ShapeDtypeStruct((rows, width), F32),
            jax.ShapeDtypeStruct((2, rows, width), BF),
        ),
        in_specs=[
            SMEM_SPEC,
            pair_spec(rows),
            stacked_spec(rows, 0),
            stacked_spec(rows, 1),
            pair_spec(rows),
            pair_spec(rows),
            low_spec(rows),
            log_spec(rows),
        ],
        out_specs=(pair_spec(rows), pl.BlockSpec((2, rows, LANES), lambda i: (0, 0, i))),
        scratch_shapes=[pltpu.VMEM((2, rows, LANES), F32)],
        compiler_params=pltpu.CompilerParams(vmem_limit_bytes=VMEM_BYTES),
        cost_estimate=attention_cost(rows, width, 5),
    )(need, q, kv, kv, do, o, low_row, logs)


def own_backward_kernel(
    q_ref,
    k_ref,
    v_ref,
    do_ref,
    o_ref,
    low_ref,
    log_ref,
    dq_in_ref,
    cos_ref,
    sin_ref,
    dq_ref,
    dk_ref,
    dv_ref,
    sums,
):
    rows = q_ref.shape[0]
    sums[...] = jnp.zeros_like(sums)
    k_t = k_ref[...].T
    for r in range(0, rows, QROWS):
        count = r + QROWS
        window = (slice(r, r + QROWS), slice(None))
        allowed = own_mask(count, r, low_ref[:, r : r + QROWS])
        logs = [log_ref[0, h : h + 1, r : r + QROWS] for h in range(LANES // HDIM)]
        d_query, d_key, d_value = backward_block(
            q_ref[window],
            k_ref[0:count, :],
            v_ref[0:count, :],
            k_t[:, 0:count],
            do_ref[window],
            output_product(do_ref, o_ref, window),
            logs,
            allowed,
        )
        rotated = (d_query.T + dq_in_ref[window]) * (HDIM**-0.5)
        turned = rotated * cos_ref[window] - swap_halves(rotated) * sin_ref[window]
        dq_ref[window] = turned.astype(BF)
        sums[0, 0:count] += d_key
        sums[1, 0:count] += d_value
    dk_ref[...] = sums[0]
    dv_ref[...] = sums[1]


def own_backward(q, kv, do, o, low_row, logs, dq_in, cos, sin):
    rows, width = q.shape
    pairs = width // LANES
    table = pl.BlockSpec((rows, LANES), lambda i: (0, 0))
    return pl.pallas_call(
        own_backward_kernel,
        grid=(pairs,),
        out_shape=(
            jax.ShapeDtypeStruct((rows, width), BF),
            jax.ShapeDtypeStruct((rows, width), F32),
            jax.ShapeDtypeStruct((rows, width), F32),
        ),
        in_specs=[
            pair_spec(rows),
            stacked_spec(rows, 0),
            stacked_spec(rows, 1),
            pair_spec(rows),
            pair_spec(rows),
            low_spec(rows),
            log_spec(rows),
            pair_spec(rows),
            table,
            table,
        ],
        out_specs=(pair_spec(rows),) * 3,
        scratch_shapes=[pltpu.VMEM((2, rows, LANES), F32)],
        compiler_params=pltpu.CompilerParams(vmem_limit_bytes=VMEM_BYTES),
        cost_estimate=attention_cost(rows, width, 5),
    )(q, kv, kv, do, o, low_row, logs, dq_in, cos, sin)


def finish_keys_kernel(dk_ref, dv_ref, dk_in_ref, dv_in_ref, cos_ref, sin_ref, dk_out, dv_out):
    total = dk_ref[...] + dk_in_ref[...].astype(F32)
    turned = total * cos_ref[...] - swap_halves(total) * sin_ref[...]
    dk_out[...] = turned.astype(BF)
    dv_out[...] = (dv_ref[...] + dv_in_ref[...].astype(F32)).astype(BF)


def finish_keys(dk, dv, dkv_in, cos, sin):
    rows, width = dk.shape
    pairs = width // LANES
    table = pl.BlockSpec((rows, LANES), lambda i: (0, 0))
    return pl.pallas_call(
        finish_keys_kernel,
        grid=(pairs,),
        out_shape=(jax.ShapeDtypeStruct((rows, width), BF),) * 2,
        in_specs=[pair_spec(rows), pair_spec(rows), stacked_spec(rows, 0), stacked_spec(rows, 1)]
        + [table, table],
        out_specs=(pair_spec(rows),) * 2,
        cost_estimate=pl.CostEstimate(
            flops=8 * rows * width, bytes_accessed=16 * rows * width, transcendentals=0
        ),
    )(dk, dv, dkv_in, dkv_in, cos, sin)


def branch_kernel(stream_ref, att_ref, gain_ref, *refs):
    pieces, (hidden_ref, normed_ref, scale_ref) = refs[:4], refs[4:]
    for j, piece in enumerate(pieces):
        columns = piece_columns(j, piece.shape[1])
        term = dotf(att_ref[...], piece[...], NN)
        hidden_ref[:, columns] = stream_ref[:, columns].astype(F32) + term
    hidden = hidden_ref[...]
    mean = jnp.sum(hidden * hidden, axis=1, keepdims=True) / hidden.shape[1]
    scale = lax.rsqrt(mean + norm_eps)
    scale_ref[...] = scale
    normed_ref[...] = (hidden * scale * gain_ref[...]).astype(BF)


def add_branch(stream, att, gain, pieces):
    rows, depth = stream.shape
    heads = att.shape[1]
    tile = pl.BlockSpec((QROWS, depth), lambda i: (i, 0))
    return pl.pallas_call(
        branch_kernel,
        grid=(rows // QROWS,),
        out_shape=(
            jax.ShapeDtypeStruct((rows, depth), F32),
            jax.ShapeDtypeStruct((rows, depth), BF),
            jax.ShapeDtypeStruct((rows, 1), F32),
        ),
        in_specs=[
            tile,
            pl.BlockSpec((QROWS, heads), lambda i: (i, 0)),
            pl.BlockSpec((1, depth), lambda i: (0, 0)),
        ]
        + [pl.BlockSpec(pieces[0].shape, lambda i: (0, 0))] * 4,
        out_specs=(tile, tile, pl.BlockSpec((QROWS, 1), lambda i: (i, 0))),
        compiler_params=pltpu.CompilerParams(vmem_limit_bytes=VMEM_BYTES),
        cost_estimate=pl.CostEstimate(
            flops=2 * rows * heads * depth,
            bytes_accessed=2 * (heads * depth + 5 * rows * depth),
            transcendentals=0,
        ),
    )(stream, att, gain, *pieces)


def hidden_kernel(x_ref, cot_ref, *refs):
    w_in, w_down, (act_ref, dg_ref, du_ref) = refs[:4], refs[4:8], refs[8:]
    rows = x_ref.shape[0]
    for r in range(0, rows, QROWS):
        part = slice(r, r + QROWS)
        gate = piece_dot(x_ref, part, [piece[0] for piece in w_in])
        up = piece_dot(x_ref, part, [piece[1] for piece in w_in])
        d_act = piece_dot(cot_ref, part, [piece[...] for piece in w_down], NT)
        sig = jax.nn.sigmoid(gate)
        silu = gate * sig
        act_ref[part, :] = (silu * up).astype(BF)
        dg_ref[part, :] = (d_act * up * sig * (1.0 + gate * (1.0 - sig))).astype(BF)
        du_ref[part, :] = (d_act * silu).astype(BF)


def hidden_units(x, cot, w_in, w_down):
    rows, depth = x.shape
    units, size = w_down[0].shape
    tile = 256
    whole = pl.BlockSpec((rows, depth), lambda i: (0, 0))
    part = pl.BlockSpec((rows, tile), lambda i: (0, i))
    return pl.pallas_call(
        hidden_kernel,
        grid=(units // tile,),
        out_shape=(jax.ShapeDtypeStruct((rows, units), BF),) * 3,
        in_specs=[whole, whole]
        + [pl.BlockSpec((2, size, tile), lambda i: (0, 0, i))] * 4
        + [pl.BlockSpec((tile, size), lambda i: (i, 0))] * 4,
        out_specs=(part,) * 3,
        compiler_params=pltpu.CompilerParams(vmem_limit_bytes=VMEM_BYTES),
        cost_estimate=pl.CostEstimate(
            flops=6 * rows * depth * units,
            bytes_accessed=2 * (2 * x.size + 3 * units * depth + 3 * rows * units),
            transcendentals=rows * units,
        ),
    )(x, cot, *w_in, *w_down)


def phased(i, block, make_index, tiles):
    def index_map(j, t):
        return make_index(jnp.where(j < i, 0, jnp.where(j == i, t, tiles - 1)))

    return pl.BlockSpec(block, index_map)


def columns_call(kernel_dot, lefts, pieces, block, make_index, size, flops, name):
    rows = lefts[0].shape[0]
    tile = min(size, 256)
    tiles = size // tile
    depth = size * 4

    def kernel(*refs):
        left_refs, piece_refs, out_ref = refs[: len(lefts)], refs[len(lefts) : -1], refs[-1]
        for j, piece in enumerate(piece_refs):

            @pl.when(pl.program_id(0) == j)
            def _():
                for r in range(0, rows, QROWS):
                    out_ref[r : r + QROWS, :] = kernel_dot(
                        [left[r : r + QROWS, :] for left in left_refs], piece
                    ).astype(BF)

    def out_index(j, t):
        return (0, (lax.axis_index("fsdp") ^ j) * tiles + t)

    return pl.pallas_call(
        kernel,
        grid=(4, tiles),
        out_shape=jax.ShapeDtypeStruct((rows, depth), BF),
        in_specs=[pl.BlockSpec(left.shape, lambda j, t: (0, 0)) for left in lefts]
        + [phased(i, block(tile), make_index, tiles) for i in range(4)],
        out_specs=pl.BlockSpec((rows, tile), out_index),
        compiler_params=pltpu.CompilerParams(vmem_limit_bytes=VMEM_BYTES),
        cost_estimate=pl.CostEstimate(
            flops=flops, bytes_accessed=2 * (4 * pieces[0].size + rows * depth), transcendentals=0
        ),
        name=name,
    )(*lefts, *pieces)


def stacked_columns(lefts, pieces, name):
    count, size, inner = pieces[0].shape

    def product(parts, piece):
        return sum(dotf(parts[c], piece[c], NT) for c in range(count))

    return columns_call(
        product,
        lefts,
        pieces,
        lambda tile: (count, tile, inner),
        lambda t: (0, t, 0),
        size,
        8 * lefts[0].shape[0] * size * inner * count,
        name,
    )


def plain_columns(left, pieces, name):
    inner, size = pieces[0].shape
    return columns_call(
        lambda parts, piece: dotf(parts[0], piece[...], NN),
        [left],
        pieces,
        lambda tile: (inner, tile),
        lambda t: (0, t),
        size,
        8 * left.shape[0] * size * inner,
        name,
    )


def branch_back_kernel(
    tensor_index_ref, d_mid_ref, hidden_ref, cot_ref, scale_ref, gain_ref, *refs
):
    pieces, (d_own_ref, d_branch_ref, d_att_ref, gain_out_ref) = refs[:4], refs[4:8]
    d_mid = d_mid_ref[...].astype(F32)
    hidden = hidden_ref[...]
    scale = scale_ref[...]
    weighted = d_mid * gain_ref[...]
    inner = jnp.sum(weighted * hidden, axis=1, keepdims=True) / hidden.shape[1]
    d_hidden = (
        cot_ref[...].astype(F32) + scale * weighted - hidden * (scale * scale * scale * inner)
    )
    gain_term = jnp.sum(d_mid * hidden * scale, axis=0, keepdims=True)

    @pl.when(pl.program_id(0) == 0)
    def _():
        gain_out_ref[...] = gain_term

    @pl.when(pl.program_id(0) != 0)
    def _():
        gain_out_ref[...] += gain_term

    d_branch_ref[...] = d_hidden.astype(BF)
    width = d_own_ref.shape[1]
    for z in range(hidden.shape[1] // width):

        @pl.when(tensor_index_ref[0] == z)
        def _():
            d_own_ref[...] = d_hidden[:, z * width : (z + 1) * width]

    d_att_ref[...] = piece_dot(
        d_branch_ref, slice(None), [piece[...] for piece in pieces], NT
    ).astype(BF)


def branch_back(tensor_index, d_mid, hidden, cot, scale, gain, pieces, own_width):
    rows, depth = hidden.shape
    heads, size = pieces[0].shape[0] // (depth // own_width), pieces[0].shape[1]
    tile = pl.BlockSpec((QROWS, depth), lambda i, s: (i, 0))
    row = pl.BlockSpec((1, depth), lambda i, s: (0, 0))
    own = pl.BlockSpec((QROWS, own_width), lambda i, s: (i, 0))
    return pl.pallas_call(
        branch_back_kernel,
        grid_spec=pltpu.PrefetchScalarGridSpec(
            num_scalar_prefetch=1,
            grid=(rows // QROWS,),
            in_specs=[tile, tile, tile, pl.BlockSpec((QROWS, 1), lambda i, s: (i, 0)), row]
            + [pl.BlockSpec((heads, size), lambda i, s: (s[0], 0))] * 4,
            out_specs=(own, tile, pl.BlockSpec((QROWS, heads), lambda i, s: (i, 0)), row),
        ),
        out_shape=(
            jax.ShapeDtypeStruct((rows, own_width), F32),
            jax.ShapeDtypeStruct((rows, depth), BF),
            jax.ShapeDtypeStruct((rows, heads), BF),
            jax.ShapeDtypeStruct((1, depth), F32),
        ),
        compiler_params=pltpu.CompilerParams(vmem_limit_bytes=VMEM_BYTES),
        cost_estimate=pl.CostEstimate(
            flops=2 * rows * heads * depth,
            bytes_accessed=2 * (heads * depth + 6 * rows * depth),
            transcendentals=0,
        ),
    )(tensor_index, d_mid, hidden, cot, scale, gain, *pieces)


def block_of(x, j, count):
    size = x.shape[1] // count
    return lax.dynamic_slice_in_dim(x, (lax.axis_index("fsdp") ^ j) * size, size, 1)


def reduce_grad(make):
    sent = jnp.stack([make(1).astype(BF), make(3).astype(BF)])
    got = swap(sent, "fsdp", 1).astype(F32)
    far = swap((make(2) + got[1]).astype(BF), "fsdp", 2).astype(F32)
    mine = (make(0) + got[0] + far).astype(BF)
    other = swap(mine, "context", 1)
    return mine.astype(F32) + other.astype(F32)


def row_sum(values_in):
    return jnp.sum(values_in, axis=1, keepdims=True)


def per_device(tokens, w_qkv, w_out, w_gate_up, w_down, gains, seq_lengths, cotangent):
    row_count, part_width = tokens.shape
    tensor_index = lax.axis_index("tensor")
    context_index = lax.axis_index("context")
    shards = lax.axis_size("fsdp")
    full_width = part_width * lax.axis_size("tensor")

    def features(part_in):
        return lax.all_gather(part_in, "tensor", axis=1, tiled=True)

    def feature_sum(term):
        return lax.psum_scatter(term.astype(BF), "tensor", scatter_dimension=1, tiled=True)

    def own_features(full):
        return lax.dynamic_slice_in_dim(full, tensor_index * part_width, part_width, 1)

    ending = jnp.cumsum(seq_lengths[0])
    starts = ending - seq_lengths[0]
    places = context_index * row_count + jnp.arange(row_count, dtype=jnp.int32)
    first_token = jnp.max(jnp.where(starts[None, :] <= places[:, None], starts[None, :], 0), axis=1)
    cos, sin = rope_tables(places - first_token)
    low = first_token - context_index * row_count
    low_row = low[None, :]
    need = low[::QROWS]

    gain_full = lax.all_gather(gains, ("tensor", "fsdp"), axis=1, tiled=True).astype(F32)
    gain_attn, gain_mlp = gain_full[0:1], gain_full[1:2]
    token_low = features(tokens)
    qkv = gather_fsdp(jnp.swapaxes(w_qkv, 0, 1))
    gate_up = gather_fsdp(jnp.swapaxes(w_gate_up, 0, 1), qkv[2])
    down = gather_fsdp(w_down, qkv[2])
    out = gather_fsdp(lax.all_gather(w_out, "tensor", axis=0, tiled=True))
    cot_full = features(cotangent)

    keys_values, normed_in, scale_attn = project(
        token_low, qkv, cos, sin, gain_attn, (1.0, None), 1, True
    )
    peer_kv = lax.ppermute(keys_values, "context", [(0, 1)])
    queries = project(normed_in, qkv, cos, sin, gain_attn, (HDIM**-0.5,), 0, False)[0][0]
    part, part_log = own_forward(queries, keys_values, low_row)
    attended, logs = peer_forward(need, queries, peer_kv, low_row, part, part_log)
    hidden, normed_mid, scale_mlp = add_branch(token_low, features(attended), gain_mlp, out)

    activated, d_gate, d_up = hidden_units(normed_mid, cot_full, gate_up, down)
    d_mid = features(feature_sum(stacked_columns([d_gate, d_up], gate_up, "d_mid")))
    mlp_term = plain_columns(activated, down, "mlp_out")
    mlp_term = lax.optimization_barrier((mlp_term, d_mid))[0]
    mlp_out = feature_sum(mlp_term).astype(F32)
    block_out = (own_features(hidden) + mlp_out).astype(BF)

    grad_down = reduce_grad(lambda j: dotf(activated, block_of(cot_full, j, shards), TN))
    grad_gate = reduce_grad(lambda j: dotf(block_of(normed_mid, j, shards), d_gate, TN))
    grad_up = reduce_grad(lambda j: dotf(block_of(normed_mid, j, shards), d_up, TN))

    d_hidden_own, d_branch, d_attended, gain_mlp_term = branch_back(
        tensor_index[None], d_mid, hidden, cot_full, scale_mlp, gain_mlp, out, part_width
    )
    dq_peer, dkv_peer = peer_backward(
        need, queries, peer_kv, d_attended, attended, low_row, logs
    )
    dkv_in = lax.ppermute(dkv_peer, "context", [(1, 0)])
    d_query, dk_own, dv_own = own_backward(
        queries, keys_values, d_attended, attended, low_row, logs, dq_peer, cos, sin
    )
    d_key, d_value = finish_keys(dk_own, dv_own, dkv_in, cos, sin)
    d_parts = (d_query, d_key, d_value)

    grad_out = reduce_grad(lambda j: dotf(attended, block_of(d_branch, j, shards), TN))
    grad_qkv = jnp.stack(
        [
            reduce_grad(lambda j, d=d: dotf(block_of(normed_in, j, shards), d, TN))
            for d in d_parts
        ],
        axis=1,
    )
    d_in_term = stacked_columns(list(d_parts), qkv, "d_in")
    d_in = feature_sum(d_in_term).astype(F32)
    stream = token_low.astype(F32)
    d_in_wide = d_in_term.astype(F32)
    inner_in = lax.psum(row_sum(d_in_wide * gain_attn * stream), "tensor") / full_width
    gain_attn_term = jnp.sum(d_in_wide * stream * scale_attn, axis=0)

    own_tokens = tokens.astype(F32)
    grad_tokens = (
        d_hidden_own
        + scale_attn * own_features(gain_attn) * d_in
        - own_tokens * scale_attn * scale_attn * scale_attn * inner_in
    ).astype(BF)

    column = jnp.arange(full_width, dtype=jnp.int32)
    mine = column // part_width == tensor_index
    gain_terms = jnp.stack([gain_attn_term, jnp.where(mine, gain_mlp_term[0], 0.0)])
    gain_sums = lax.psum(gain_terms, ("fsdp", "context", "tensor"))
    gain_width = gains.shape[1]
    place = (tensor_index * shards + lax.axis_index("fsdp")) * gain_width
    grad_gains = lax.dynamic_slice_in_dim(gain_sums, place, gain_width, 1)

    grad_gate_up = jnp.stack([grad_gate, grad_up], axis=1)
    return (block_out, grad_tokens, grad_qkv, grad_out, grad_gate_up, grad_down, grad_gains)


def solution(mesh):
    rows = P(("fsdp", "context"), "tensor")
    inner = P("fsdp", None, "tensor")
    outer = P("tensor", "fsdp")
    gain = P(None, ("tensor", "fsdp"))
    return jax.shard_map(
        per_device,
        mesh=mesh,
        in_specs=(rows, inner, outer, inner, outer, gain, P("fsdp", None), rows),
        out_specs=(rows, rows, inner, outer, inner, outer, gain),
        check_vma=False,
    )
```

```python
import functools

import jax
import jax.numpy as jnp
from jax import lax
from jax.experimental import pallas as pl
from jax.experimental.pallas import tpu as pltpu
from jax.sharding import PartitionSpec as P

HDIM = 64
LANES = 128
QROWS = 256
norm_eps = 1e-05
rope_base = 130000.0
masked_score = -1e30
BF = jnp.bfloat16
F32 = jnp.float32
VMEM_BYTES = 56 * 1024 * 1024
LIGHT = pl.CostEstimate(flops=1, bytes_accessed=1, transcendentals=0)


def dotf(a, b, dims):
    return lax.dot_general(a, b, (dims, ((), ())), preferred_element_type=F32)


NN = ((1,), (0,))
NT = ((1,), (1,))
TN = ((0,), (0,))


def swap(value, axis, bit):
    count = lax.axis_size(axis)
    return lax.ppermute(value, axis, [(i, i ^ bit) for i in range(count)])


def after(value, *others):
    return lax.optimization_barrier((value, *others))[0]


def shifted(value, axis):
    count = lax.axis_size(axis)
    return [
        lax.ppermute(value, axis, [(i, (i + step) % count) for i in range(count)])
        for step in range(1, count)
    ]


def small_sum(value, axis):
    if lax.axis_size(axis) > 4:
        return lax.psum(value, axis)
    return value + sum(shifted(value, axis))


def piece_columns(j, size):
    return pl.ds(pl.multiple_of((lax.axis_index("fsdp") ^ j) * size, size), size)


def swap_halves(block):
    lane = lax.broadcasted_iota(jnp.int32, block.shape, 1)
    up = pltpu.roll(block, LANES - HDIM // 2, 1)
    down = pltpu.roll(block, HDIM // 2, 1)
    return jnp.where((lane & (HDIM - 1)) < HDIM // 2, up, down)


def rope_tables(positions):
    lane = jnp.arange(LANES, dtype=jnp.int32)
    half = lane % (HDIM // 2)
    frequencies = rope_base ** (-2.0 * half.astype(F32) / HDIM)
    angles = positions.astype(F32)[:, None] * frequencies[None, :]
    sign = jnp.where((lane % HDIM) < HDIM // 2, -1.0, 1.0)
    return jnp.cos(angles), jnp.sin(angles) * sign[None, :]


def piece_dot(x_ref, rows, pieces, dims=NN):
    total = None
    for j, piece in enumerate(pieces):
        size = piece.shape[dims[1][0]]
        term = dotf(x_ref[rows, piece_columns(j, size)], piece, dims)
        total = term if total is None else total + term
    return total


def project_kernel(kinds, normalize, x_ref, *refs):
    pieces, (cos_ref, sin_ref, gain_ref), outs = refs[:4], refs[4:7], refs[7:]
    out_ref = outs[0]
    rows, width = out_ref.shape[1:]
    step = pl.program_id(0)
    if normalize:
        normed_ref, scale_ref = outs[1], outs[2]

        @pl.when(step == 0)
        def _():
            for r in range(0, rows, QROWS):
                part = slice(r, r + QROWS)
                stream = x_ref[part, :].astype(F32)
                mean = jnp.sum(stream * stream, axis=1, keepdims=True) / x_ref.shape[1]
                scale = lax.rsqrt(mean + norm_eps)
                scale_ref[part, :] = scale
                normed_ref[part, :] = (stream * scale * gain_ref[...]).astype(BF)

        x_ref = normed_ref
    for index, scale in enumerate(kinds):

        @pl.when(step == index)
        def _():
            for r in range(0, rows, QROWS):
                part = slice(r, r + QROWS)
                result = piece_dot(x_ref, part, [piece[0] for piece in pieces])
                for c in range(0, width, LANES):
                    block = result[:, c : c + LANES]
                    if scale:
                        block = block * cos_ref[part, :] + swap_halves(block) * sin_ref[part, :]
                    low = block.astype(BF)
                    if scale and scale != 1.0:
                        low = low * jnp.asarray(scale, BF)
                    out_ref[0, part, c : c + LANES] = low


def project(x, pieces, cos, sin, gain, kinds, first, normalize):
    rows, depth = x.shape
    _, size, width = pieces[0].shape
    flops = 2 * len(kinds) * rows * depth * width
    whole = pl.BlockSpec((rows, depth), lambda i: (0, 0))
    table = pl.BlockSpec((rows, LANES), lambda i: (0, 0))
    out_shape = [jax.ShapeDtypeStruct((len(kinds), rows, width), BF)]
    out_specs = [pl.BlockSpec((1, rows, width), lambda i: (i, 0, 0))]
    if normalize:
        out_shape += [jax.ShapeDtypeStruct((rows, depth), BF), jax.ShapeDtypeStruct((rows, 1), F32)]
        out_specs += [whole, pl.BlockSpec((rows, 1), lambda i: (0, 0))]
    return pl.pallas_call(
        functools.partial(project_kernel, kinds, normalize),
        name="project_kv" if normalize else "project_q",
        grid=(len(kinds),),
        out_shape=out_shape,
        in_specs=[whole]
        + [pl.BlockSpec((1, size, width), lambda i: (i + first, 0, 0))] * 4
        + [table, table, pl.BlockSpec((1, depth), lambda i: (0, 0))],
        out_specs=out_specs,
        compiler_params=pltpu.CompilerParams(vmem_limit_bytes=VMEM_BYTES),
        cost_estimate=LIGHT,
    )(x, *pieces, cos, sin, gain)


def head_mask(block, head):
    lane = lax.broadcasted_iota(jnp.int32, block.shape, 1)
    inside = (lane < HDIM) if head == 0 else (lane >= HDIM)
    return jnp.where(inside, block, jnp.zeros_like(block))


def own_mask(key_count, row0, low_row):
    key = lax.broadcasted_iota(jnp.int32, (key_count, QROWS), 0)
    query = row0 + lax.broadcasted_iota(jnp.int32, (key_count, QROWS), 1)
    return (key >= low_row) & (key <= query)


def peer_mask(key_count, low_row, offset):
    key = lax.broadcasted_iota(jnp.int32, (key_count, QROWS), 0) - offset
    return key >= low_row


def own_forward_kernel(q_ref, k_ref, v_ref, low_ref, out_ref, log_ref):
    rows = q_ref.shape[0]
    v_t = v_ref[...].T
    for r in range(0, rows, QROWS):
        count = r + QROWS
        allowed = own_mask(count, r, low_ref[:, r : r + QROWS])
        keys = k_ref[0:count, :]
        outs = []
        for head in range(LANES // HDIM):
            scores = dotf(keys, head_mask(q_ref[r : r + QROWS, :], head), NT)
            scores = jnp.where(allowed, scores, masked_score)
            peak = jnp.max(scores, axis=0, keepdims=True)
            weights = jnp.exp(scores - peak)
            total = jnp.sum(weights, axis=0, keepdims=True)
            part = dotf(v_t[head * HDIM : (head + 1) * HDIM, 0:count], weights.astype(BF), NN)
            outs.append(part / total)
            log_ref[0, head : head + 1, r : r + QROWS] = peak + jnp.log(total)
        out_ref[r : r + QROWS, :] = jnp.concatenate(outs, axis=0).T


def peer_forward_kernel(
    need_ref, q_ref, k_ref, v_ref, low_ref, part_ref, log_in_ref, out_ref, log_ref
):
    rows = q_ref.shape[0]
    key_count = k_ref.shape[0]
    for index, r in enumerate(range(0, rows, QROWS)):
        needed = need_ref[index] < 0

        @pl.when(needed)
        def _():
            v_t = v_ref[...].T
            allowed = peer_mask(key_count, low_ref[:, r : r + QROWS], key_count)
            before = part_ref[r : r + QROWS, :].T
            outs = []
            for head in range(LANES // HDIM):
                scores = dotf(k_ref[...], head_mask(q_ref[r : r + QROWS, :], head), NT)
                scores = jnp.where(allowed, scores, masked_score)
                log_own = log_in_ref[0, head : head + 1, r : r + QROWS]
                peak = jnp.maximum(jnp.max(scores, axis=0, keepdims=True), log_own)
                weights = jnp.exp(scores - peak)
                own_weight = jnp.exp(log_own - peak)
                total = jnp.sum(weights, axis=0, keepdims=True) + own_weight
                rows_h = slice(head * HDIM, (head + 1) * HDIM)
                part = dotf(v_t[rows_h, :], weights.astype(BF), NN)
                outs.append((part + before[rows_h, :] * own_weight) / total)
                log_ref[0, head : head + 1, r : r + QROWS] = peak + jnp.log(total)
            out_ref[r : r + QROWS, :] = jnp.concatenate(outs, axis=0).T.astype(BF)

        @pl.when(jnp.logical_not(needed))
        def _():
            out_ref[r : r + QROWS, :] = part_ref[r : r + QROWS, :].astype(BF)
            log_ref[:, :, r : r + QROWS] = log_in_ref[:, :, r : r + QROWS]


def pair_spec(rows):
    return pl.BlockSpec((rows, LANES), lambda i: (0, i))


def stacked_spec(rows, part):
    return pl.BlockSpec((None, rows, LANES), lambda i: (part, 0, i))


def log_spec(rows):
    return pl.BlockSpec((1, LANES // HDIM, rows), lambda i: (i, 0, 0))


def low_spec(rows):
    return pl.BlockSpec((1, rows), lambda i: (0, 0))


def own_forward(q, kv, low_row):
    rows, width = q.shape
    pairs = width // LANES
    return pl.pallas_call(
        own_forward_kernel,
        name="own_fwd",
        grid=(pairs,),
        out_shape=(
            jax.ShapeDtypeStruct((rows, width), F32),
            jax.ShapeDtypeStruct((pairs, LANES // HDIM, rows), F32),
        ),
        in_specs=[
            pair_spec(rows),
            stacked_spec(rows, 0),
            stacked_spec(rows, 1),
            low_spec(rows),
        ],
        out_specs=(pair_spec(rows), log_spec(rows)),
        compiler_params=pltpu.CompilerParams(vmem_limit_bytes=VMEM_BYTES),
        cost_estimate=LIGHT,
    )(q, kv, kv, low_row)


SMEM_SPEC = pl.BlockSpec(memory_space=pltpu.SMEM)


def peer_forward(need, q, kv, low_row, part, log_in):
    rows, width = q.shape
    pairs = width // LANES
    return pl.pallas_call(
        peer_forward_kernel,
        name="peer_fwd",
        grid=(pairs,),
        out_shape=(
            jax.ShapeDtypeStruct((rows, width), BF),
            jax.ShapeDtypeStruct((pairs, LANES // HDIM, rows), F32),
        ),
        in_specs=[
            SMEM_SPEC,
            pair_spec(rows),
            stacked_spec(rows, 0),
            stacked_spec(rows, 1),
            low_spec(rows),
            pair_spec(rows),
            log_spec(rows),
        ],
        out_specs=(pair_spec(rows), log_spec(rows)),
        compiler_params=pltpu.CompilerParams(vmem_limit_bytes=VMEM_BYTES),
        cost_estimate=LIGHT,
    )(need, q, kv, kv, low_row, part, log_in)


def backward_block(q_rows, k_rows, v_rows, k_t, do_rows, do_o_t, logs, allowed):
    d_query, d_key, d_value = [], None, None
    for head in range(LANES // HDIM):
        rows_h = slice(head * HDIM, (head + 1) * HDIM)
        q_head = head_mask(q_rows, head)
        do_head = head_mask(do_rows, head)
        scores = dotf(k_rows, q_head, NT)
        probs = jnp.exp(jnp.where(allowed, scores, masked_score) - logs[head])
        delta = jnp.sum(do_o_t[rows_h, :], axis=0, keepdims=True)
        d_probs = dotf(v_rows, do_head, NT)
        d_scores = (probs * (d_probs - delta)).astype(BF)
        d_v = dotf(probs.astype(BF), do_head, NN)
        d_k = dotf(d_scores, q_head, NN)
        d_value = d_v if d_value is None else d_value + d_v
        d_key = d_k if d_key is None else d_key + d_k
        d_query.append(dotf(k_t[rows_h, :], d_scores, NN))
    return jnp.concatenate(d_query, axis=0), d_key, d_value


def output_product(do_ref, o_ref, window):
    product = do_ref[window].astype(F32) * o_ref[window].astype(F32)
    return product.T


def peer_backward_kernel(
    need_ref, q_ref, k_ref, v_ref, do_ref, o_ref, low_ref, log_ref, dq_ref, dkv_ref, sums
):
    rows = q_ref.shape[0]
    key_count = k_ref.shape[0]
    sums[...] = jnp.zeros_like(sums)
    for index, r in enumerate(range(0, rows, QROWS)):
        needed = need_ref[index] < 0
        window = (slice(r, r + QROWS), slice(None))

        @pl.when(needed)
        def _():
            allowed = peer_mask(key_count, low_ref[:, r : r + QROWS], key_count)
            logs = [log_ref[0, h : h + 1, r : r + QROWS] for h in range(LANES // HDIM)]
            d_query, d_key, d_value = backward_block(
                q_ref[window],
                k_ref[...],
                v_ref[...],
                k_ref[...].T,
                do_ref[window],
                output_product(do_ref, o_ref, window),
                logs,
                allowed,
            )
            dq_ref[window] = d_query.T
            sums[0] += d_key
            sums[1] += d_value

        @pl.when(jnp.logical_not(needed))
        def _():
            dq_ref[window] = jnp.zeros((QROWS, LANES), F32)

    dkv_ref[...] = sums[...].astype(BF)


def peer_backward(need, q, kv, do, o, low_row, logs):
    rows, width = q.shape
    pairs = width // LANES
    return pl.pallas_call(
        peer_backward_kernel,
        name="peer_bwd",
        grid=(pairs,),
        out_shape=(
            jax.ShapeDtypeStruct((rows, width), F32),
            jax.ShapeDtypeStruct((2, rows, width), BF),
        ),
        in_specs=[
            SMEM_SPEC,
            pair_spec(rows),
            stacked_spec(rows, 0),
            stacked_spec(rows, 1),
            pair_spec(rows),
            pair_spec(rows),
            low_spec(rows),
            log_spec(rows),
        ],
        out_specs=(pair_spec(rows), pl.BlockSpec((2, rows, LANES), lambda i: (0, 0, i))),
        scratch_shapes=[pltpu.VMEM((2, rows, LANES), F32)],
        compiler_params=pltpu.CompilerParams(vmem_limit_bytes=VMEM_BYTES),
        cost_estimate=LIGHT,
    )(need, q, kv, kv, do, o, low_row, logs)


def own_backward_kernel(
    q_ref,
    k_ref,
    v_ref,
    do_ref,
    o_ref,
    low_ref,
    log_ref,
    dq_in_ref,
    cos_ref,
    sin_ref,
    dq_ref,
    dk_ref,
    dv_ref,
    sums,
):
    rows = q_ref.shape[0]
    sums[...] = jnp.zeros_like(sums)
    k_t = k_ref[...].T
    for r in range(0, rows, QROWS):
        count = r + QROWS
        window = (slice(r, r + QROWS), slice(None))
        allowed = own_mask(count, r, low_ref[:, r : r + QROWS])
        logs = [log_ref[0, h : h + 1, r : r + QROWS] for h in range(LANES // HDIM)]
        d_query, d_key, d_value = backward_block(
            q_ref[window],
            k_ref[0:count, :],
            v_ref[0:count, :],
            k_t[:, 0:count],
            do_ref[window],
            output_product(do_ref, o_ref, window),
            logs,
            allowed,
        )
        rotated = (d_query.T + dq_in_ref[window]) * (HDIM**-0.5)
        turned = rotated * cos_ref[window] - swap_halves(rotated) * sin_ref[window]
        dq_ref[window] = turned.astype(BF)
        sums[0, 0:count] += d_key
        sums[1, 0:count] += d_value
    dk_ref[...] = sums[0]
    dv_ref[...] = sums[1]


def own_backward(q, kv, do, o, low_row, logs, dq_in, cos, sin):
    rows, width = q.shape
    pairs = width // LANES
    table = pl.BlockSpec((rows, LANES), lambda i: (0, 0))
    return pl.pallas_call(
        own_backward_kernel,
        name="own_bwd",
        grid=(pairs,),
        out_shape=(
            jax.ShapeDtypeStruct((rows, width), BF),
            jax.ShapeDtypeStruct((rows, width), F32),
            jax.ShapeDtypeStruct((rows, width), F32),
        ),
        in_specs=[
            pair_spec(rows),
            stacked_spec(rows, 0),
            stacked_spec(rows, 1),
            pair_spec(rows),
            pair_spec(rows),
            low_spec(rows),
            log_spec(rows),
            pair_spec(rows),
            table,
            table,
        ],
        out_specs=(pair_spec(rows),) * 3,
        scratch_shapes=[pltpu.VMEM((2, rows, LANES), F32)],
        compiler_params=pltpu.CompilerParams(vmem_limit_bytes=VMEM_BYTES),
        cost_estimate=LIGHT,
    )(q, kv, kv, do, o, low_row, logs, dq_in, cos, sin)


def finish_keys_kernel(dk_ref, dv_ref, dk_in_ref, dv_in_ref, cos_ref, sin_ref, dk_out, dv_out):
    total = dk_ref[...] + dk_in_ref[...].astype(F32)
    turned = total * cos_ref[...] - swap_halves(total) * sin_ref[...]
    dk_out[...] = turned.astype(BF)
    dv_out[...] = (dv_ref[...] + dv_in_ref[...].astype(F32)).astype(BF)


def finish_keys(dk, dv, dkv_in, cos, sin):
    rows, width = dk.shape
    pairs = width // LANES
    table = pl.BlockSpec((rows, LANES), lambda i: (0, 0))
    return pl.pallas_call(
        finish_keys_kernel,
        name="finish_keys",
        grid=(pairs,),
        out_shape=(jax.ShapeDtypeStruct((rows, width), BF),) * 2,
        in_specs=[pair_spec(rows), pair_spec(rows), stacked_spec(rows, 0), stacked_spec(rows, 1)]
        + [table, table],
        out_specs=(pair_spec(rows),) * 2,
        cost_estimate=LIGHT,
    )(dk, dv, dkv_in, dkv_in, cos, sin)


def branch_kernel(stream_ref, att_ref, gain_ref, *refs):
    pieces, (hidden_ref, normed_ref, scale_ref) = refs[:4], refs[4:]
    for j, piece in enumerate(pieces):
        columns = piece_columns(j, piece.shape[1])
        term = dotf(att_ref[...], piece[...], NN)
        hidden_ref[:, columns] = stream_ref[:, columns].astype(F32) + term
    hidden = hidden_ref[...]
    mean = jnp.sum(hidden * hidden, axis=1, keepdims=True) / hidden.shape[1]
    scale = lax.rsqrt(mean + norm_eps)
    scale_ref[...] = scale
    normed_ref[...] = (hidden * scale * gain_ref[...]).astype(BF)


def add_branch(stream, att, gain, pieces):
    rows, depth = stream.shape
    heads = att.shape[1]
    tile = pl.BlockSpec((QROWS, depth), lambda i: (i, 0))
    return pl.pallas_call(
        branch_kernel,
        name="branch",
        grid=(rows // QROWS,),
        out_shape=(
            jax.ShapeDtypeStruct((rows, depth), F32),
            jax.ShapeDtypeStruct((rows, depth), BF),
            jax.ShapeDtypeStruct((rows, 1), F32),
        ),
        in_specs=[
            tile,
            pl.BlockSpec((QROWS, heads), lambda i: (i, 0)),
            pl.BlockSpec((1, depth), lambda i: (0, 0)),
        ]
        + [pl.BlockSpec(pieces[0].shape, lambda i: (0, 0))] * 4,
        out_specs=(tile, tile, pl.BlockSpec((QROWS, 1), lambda i: (i, 0))),
        compiler_params=pltpu.CompilerParams(vmem_limit_bytes=VMEM_BYTES),
        cost_estimate=LIGHT,
    )(stream, att, gain, *pieces)


def hidden_kernel(x_ref, *refs):
    w_in, (act_ref, by_gate_ref, by_up_ref) = refs[:4], refs[4:]
    rows = x_ref.shape[0]
    for r in range(0, rows, QROWS):
        part = slice(r, r + QROWS)
        gate = piece_dot(x_ref, part, [piece[0] for piece in w_in])
        up = piece_dot(x_ref, part, [piece[1] for piece in w_in])
        sig = jax.nn.sigmoid(gate)
        silu = gate * sig
        act_ref[part, :] = (silu * up).astype(BF)
        by_gate_ref[part, :] = (up * sig * (1.0 + gate * (1.0 - sig))).astype(BF)
        by_up_ref[part, :] = silu.astype(BF)


def hidden_units(x, w_in):
    rows, depth = x.shape
    _, size, units = w_in[0].shape
    tile = 256
    part = pl.BlockSpec((rows, tile), lambda i: (0, i))
    return pl.pallas_call(
        hidden_kernel,
        grid=(units // tile,),
        out_shape=(jax.ShapeDtypeStruct((rows, units), BF),) * 3,
        in_specs=[pl.BlockSpec((rows, depth), lambda i: (0, 0))]
        + [pl.BlockSpec((2, size, tile), lambda i: (0, 0, i))] * 4,
        out_specs=(part,) * 3,
        compiler_params=pltpu.CompilerParams(vmem_limit_bytes=VMEM_BYTES),
        cost_estimate=LIGHT,
        name="hidden",
    )(x, *w_in)


def hidden_back_kernel(cot_ref, by_gate_ref, by_up_ref, *refs):
    w_down, (dg_ref, du_ref) = refs[:4], refs[4:]
    rows = cot_ref.shape[0]
    for r in range(0, rows, QROWS):
        part = slice(r, r + QROWS)
        d_act = piece_dot(cot_ref, part, [piece[...] for piece in w_down], NT)
        dg_ref[part, :] = (d_act * by_gate_ref[part, :].astype(F32)).astype(BF)
        du_ref[part, :] = (d_act * by_up_ref[part, :].astype(F32)).astype(BF)


def hidden_back(cot, by_gate, by_up, w_down):
    rows, depth = cot.shape
    units, size = w_down[0].shape
    tile = 256
    part = pl.BlockSpec((rows, tile), lambda i: (0, i))
    return pl.pallas_call(
        hidden_back_kernel,
        grid=(units // tile,),
        out_shape=(jax.ShapeDtypeStruct((rows, units), BF),) * 2,
        in_specs=[pl.BlockSpec((rows, depth), lambda i: (0, 0)), part, part]
        + [pl.BlockSpec((tile, size), lambda i: (i, 0))] * 4,
        out_specs=(part,) * 2,
        compiler_params=pltpu.CompilerParams(vmem_limit_bytes=VMEM_BYTES),
        cost_estimate=LIGHT,
        name="hidden_back",
    )(cot, by_gate, by_up, *w_down)


def phased(i, block, make_index, tiles):
    def index_map(j, t):
        return make_index(jnp.where(j < i, 0, jnp.where(j == i, t, tiles - 1)))

    return pl.BlockSpec(block, index_map)


def columns_call(kernel_dot, lefts, pieces, block, make_index, size, flops, name):
    rows = lefts[0].shape[0]
    tile = min(size, 256)
    tiles = size // tile
    depth = size * 4

    def kernel(*refs):
        left_refs, piece_refs, out_ref = refs[: len(lefts)], refs[len(lefts) : -1], refs[-1]
        for j, piece in enumerate(piece_refs):

            @pl.when(pl.program_id(0) == j)
            def _():
                for r in range(0, rows, QROWS):
                    out_ref[r : r + QROWS, :] = kernel_dot(
                        [left[r : r + QROWS, :] for left in left_refs], piece
                    ).astype(BF)

    def out_index(j, t):
        return (0, (lax.axis_index("fsdp") ^ j) * tiles + t)

    return pl.pallas_call(
        kernel,
        grid=(4, tiles),
        out_shape=jax.ShapeDtypeStruct((rows, depth), BF),
        in_specs=[pl.BlockSpec(left.shape, lambda j, t: (0, 0)) for left in lefts]
        + [phased(i, block(tile), make_index, tiles) for i in range(4)],
        out_specs=pl.BlockSpec((rows, tile), out_index),
        compiler_params=pltpu.CompilerParams(vmem_limit_bytes=VMEM_BYTES),
        cost_estimate=LIGHT,
        name=name,
    )(*lefts, *pieces)


def stacked_columns(lefts, pieces, name):
    count, size, inner = pieces[0].shape

    def product(parts, piece):
        return sum(dotf(parts[c], piece[c], NT) for c in range(count))

    return columns_call(
        product,
        lefts,
        pieces,
        lambda tile: (count, tile, inner),
        lambda t: (0, t, 0),
        size,
        8 * lefts[0].shape[0] * size * inner * count,
        name,
    )


def plain_columns(left, pieces, name):
    inner, size = pieces[0].shape
    return columns_call(
        lambda parts, piece: dotf(parts[0], piece[...], NN),
        [left],
        pieces,
        lambda tile: (inner, tile),
        lambda t: (0, t),
        size,
        8 * left.shape[0] * size * inner,
        name,
    )


def branch_back_kernel(
    tensor_index_ref, d_mid_ref, hidden_ref, cot_ref, scale_ref, gain_ref, *refs
):
    pieces, (d_own_ref, d_branch_ref, d_att_ref, gain_out_ref) = refs[:4], refs[4:8]
    d_mid = d_mid_ref[...].astype(F32)
    hidden = hidden_ref[...]
    scale = scale_ref[...]
    weighted = d_mid * gain_ref[...]
    inner = jnp.sum(weighted * hidden, axis=1, keepdims=True) / hidden.shape[1]
    d_hidden = (
        cot_ref[...].astype(F32) + scale * weighted - hidden * (scale * scale * scale * inner)
    )
    gain_term = jnp.sum(d_mid * hidden * scale, axis=0, keepdims=True)

    @pl.when(pl.program_id(0) == 0)
    def _():
        gain_out_ref[...] = gain_term

    @pl.when(pl.program_id(0) != 0)
    def _():
        gain_out_ref[...] += gain_term

    d_branch_ref[...] = d_hidden.astype(BF)
    width = d_own_ref.shape[1]
    for z in range(hidden.shape[1] // width):

        @pl.when(tensor_index_ref[0] == z)
        def _():
            d_own_ref[...] = d_hidden[:, z * width : (z + 1) * width]

    d_att_ref[...] = piece_dot(
        d_branch_ref, slice(None), [piece[...] for piece in pieces], NT
    ).astype(BF)


def branch_back(tensor_index, d_mid, hidden, cot, scale, gain, pieces, own_width):
    rows, depth = hidden.shape
    heads, size = pieces[0].shape[0] // (depth // own_width), pieces[0].shape[1]
    tile = pl.BlockSpec((QROWS, depth), lambda i, s: (i, 0))
    row = pl.BlockSpec((1, depth), lambda i, s: (0, 0))
    own = pl.BlockSpec((QROWS, own_width), lambda i, s: (i, 0))
    return pl.pallas_call(
        branch_back_kernel,
        name="branch_back",
        grid_spec=pltpu.PrefetchScalarGridSpec(
            num_scalar_prefetch=1,
            grid=(rows // QROWS,),
            in_specs=[tile, tile, tile, pl.BlockSpec((QROWS, 1), lambda i, s: (i, 0)), row]
            + [pl.BlockSpec((heads, size), lambda i, s: (s[0], 0))] * 4,
            out_specs=(own, tile, pl.BlockSpec((QROWS, heads), lambda i, s: (i, 0)), row),
        ),
        out_shape=(
            jax.ShapeDtypeStruct((rows, own_width), F32),
            jax.ShapeDtypeStruct((rows, depth), BF),
            jax.ShapeDtypeStruct((rows, heads), BF),
            jax.ShapeDtypeStruct((1, depth), F32),
        ),
        compiler_params=pltpu.CompilerParams(vmem_limit_bytes=VMEM_BYTES),
        cost_estimate=LIGHT,
    )(tensor_index, d_mid, hidden, cot, scale, gain, *pieces)


def grad_call(left, right, cut, places, near=None, across=None, name="grad"):
    rows = left.shape[0]
    size = (left, right)[cut].shape[1] // 4
    height = size if cut == 0 else left.shape[1]
    width = right.shape[1] if cut == 0 else size
    swept = (width, height)[cut]
    tile = min(1024, swept)
    adds = []
    add_specs = []

    def owner(i):
        return lax.axis_index("fsdp") ^ (places[0] + 2 * i)

    block = (height, tile) if cut == 0 else (tile, width)

    def place(t):
        return (0, t) if cut == 0 else (t, 0)

    if near is not None:
        slot = places[0] // 2
        adds.append(near)
        add_specs.append(pl.BlockSpec((None, *block), lambda i, t: (slot, *place(t))))
    if across is not None:
        adds.append(across)
        add_specs.append(pl.BlockSpec(block, lambda i, t: place(t)))

    def kernel(left_ref, right_ref, *refs):
        add_refs, out_ref = refs[: len(adds)], refs[len(adds)]
        if cut == 0:
            turned = refs[-1]

            @pl.when(pl.program_id(1) == 0)
            def _():
                turned[...] = left_ref[...].T

            result = dotf(turned[...], right_ref[...], NN)
        else:
            result = dotf(left_ref[...].T, right_ref[...], NN)
        for add in add_refs:
            result = result + add[...].astype(F32)
        out_ref[...] = result.astype(BF)

    if cut == 0:
        left_spec = pl.BlockSpec((rows, size), lambda i, t: (0, owner(i)))
        right_spec = pl.BlockSpec((rows, tile), lambda i, t: (0, t))
    else:
        left_spec = pl.BlockSpec((rows, tile), lambda i, t: (0, t))
        right_spec = pl.BlockSpec((rows, size), lambda i, t: (0, owner(i)))
    if len(places) > 1:
        out_shape = jax.ShapeDtypeStruct((len(places), height, width), BF)
        out_spec = pl.BlockSpec((None, *block), lambda i, t: (i, *place(t)))
    else:
        out_shape = jax.ShapeDtypeStruct((height, width), BF)
        out_spec = pl.BlockSpec(block, lambda i, t: place(t))
    return pl.pallas_call(
        kernel,
        grid=(len(places), swept // tile),
        out_shape=out_shape,
        in_specs=[left_spec, right_spec] + add_specs,
        out_specs=out_spec,
        scratch_shapes=[pltpu.VMEM((size, rows), BF)] if cut == 0 else [],
        compiler_params=pltpu.CompilerParams(vmem_limit_bytes=VMEM_BYTES),
        cost_estimate=LIGHT,
        name=name,
    )(left, right, *adds)


class Reduction:
    def __init__(self, left, right, cut, name):
        self.args, self.name = (left, right, cut), name

    def call(self, places, deps, step, **adds):
        left, right, cut = self.args
        left = after(left, *deps) if deps else left
        return grad_call(left, right, cut, places, name=self.name + step, **adds)

    def near(self, *deps):
        self.beside = swap(self.call((1, 3), deps, "_near"), "fsdp", 1)

    def far(self, *deps):
        self.two = self.call((2,), deps, "_far", near=self.beside)

    def send_far(self, *deps):
        self.across = swap(after(self.two, *deps), "fsdp", 2)

    def mine(self, *deps):
        self.own = self.call((0,), deps, "_mine", near=self.beside, across=self.across)

    def send_context(self, *deps):
        self.other = swap(after(self.own, *deps), "context", 1)


def totals_kernel(slots, *refs):
    pairs, out_ref = refs[:-1], refs[-1]
    for slot in range(len(pairs) // 2):
        total = pairs[2 * slot][...].astype(F32) + pairs[2 * slot + 1][...].astype(F32)
        if slots == 0:
            out_ref[slot] = total
        else:
            out_ref[:, slot, :] = total


def totals(sums, slots, *deps):
    arrays = [array for part in sums for array in (part.own, part.other)]
    if deps:
        arrays[0] = after(arrays[0], *deps)
    rows, width = arrays[0].shape
    tile = 128
    shape = [rows, width]
    shape.insert(slots, len(sums))
    block = [tile, width]
    block.insert(slots, len(sums))
    return pl.pallas_call(
        functools.partial(totals_kernel, slots),
        grid=(rows // tile,),
        out_shape=jax.ShapeDtypeStruct(tuple(shape), F32),
        in_specs=[pl.BlockSpec((tile, width), lambda i: (i, 0))] * len(arrays),
        out_specs=pl.BlockSpec(
            tuple(block), (lambda i: (0, i, 0)) if slots == 0 else (lambda i: (i, 0, 0))
        ),
        compiler_params=pltpu.CompilerParams(vmem_limit_bytes=VMEM_BYTES),
        cost_estimate=LIGHT,
        name="totals",
    )(*arrays)


def row_sum(values_in):
    return jnp.sum(values_in, axis=1, keepdims=True)


def per_device(tokens, w_qkv, w_out, w_gate_up, w_down, gains, seq_lengths, cotangent):
    row_count, part_width = tokens.shape
    tensor_index = lax.axis_index("tensor")
    context_index = lax.axis_index("context")
    shards = lax.axis_size("fsdp")
    full_width = part_width * lax.axis_size("tensor")

    def features(part_in):
        return lax.all_gather(part_in, "tensor", axis=1, tiled=True)

    def feature_sum(term):
        return lax.psum_scatter(term.astype(BF), "tensor", scatter_dimension=1, tiled=True)

    def own_features(full):
        return lax.dynamic_slice_in_dim(full, tensor_index * part_width, part_width, 1)

    ending = jnp.cumsum(seq_lengths[0])
    starts = ending - seq_lengths[0]
    places = context_index * row_count + jnp.arange(row_count, dtype=jnp.int32)
    first_token = jnp.max(jnp.where(starts[None, :] <= places[:, None], starts[None, :], 0), axis=1)
    cos, sin = rope_tables(places - first_token)
    low = first_token - context_index * row_count
    low_row = low[None, :]
    need = low[::QROWS]

    gain_full = lax.all_gather(gains, ("tensor", "fsdp"), axis=1, tiled=True).astype(F32)
    gain_attn, gain_mlp = gain_full[0:1], gain_full[1:2]
    token_low = features(tokens)
    qkv_own = jnp.swapaxes(w_qkv, 0, 1)
    qkv_far = swap(qkv_own, "fsdp", 2)
    qkv_near = swap(qkv_own, "fsdp", 1)
    qkv = (qkv_own, qkv_near, qkv_far, swap(qkv_far, "fsdp", 1))

    gate_up_own = jnp.swapaxes(w_gate_up, 0, 1)
    third = gate_up_own.shape[1] * 11 // 32
    cuts = (0, third, gate_up_own.shape[1] - third, gate_up_own.shape[1])
    gate_up_parts = []
    last = qkv_far
    for lower, upper in zip(cuts[:-1], cuts[1:]):
        last = swap(after(gate_up_own[:, lower:upper], last), "fsdp", 2)
        gate_up_parts.append(last)

    keys_values, normed_in, scale_attn = project(
        after(token_low, gate_up_parts[0]), qkv, cos, sin, gain_attn, (1.0, None), 1, True
    )
    peer_kv = lax.ppermute(keys_values, "context", [(0, 1)])
    queries = project(normed_in, qkv, cos, sin, gain_attn, (HDIM**-0.5,), 0, False)[0][0]
    part, part_log = own_forward(after(queries, gate_up_parts[1]), keys_values, low_row)
    attended, logs = peer_forward(
        need, queries, peer_kv, low_row, after(part, gate_up_parts[2]), part_log
    )
    attended_full = features(attended)

    out_own = after(lax.all_gather(w_out, "tensor", axis=0, tiled=True), attended)
    out_far = swap(out_own, "fsdp", 2)
    down_own = after(w_down, attended_full)
    down_far = swap(down_own, "fsdp", 2)
    gate_up_own, *gate_up_parts = lax.optimization_barrier(
        (gate_up_own, *gate_up_parts, attended)
    )[:4]
    gate_up_far = jnp.concatenate(gate_up_parts, axis=1)
    gate_up_near = swap(gate_up_own, "fsdp", 1)
    gate_up = (gate_up_own, gate_up_near, gate_up_far, swap(gate_up_far, "fsdp", 1))
    out = (out_own, swap(out_own, "fsdp", 1), out_far, swap(out_far, "fsdp", 1))
    down_near = swap(after(w_down, attended), "fsdp", 1)
    down = (w_down, down_near, down_far, swap(down_far, "fsdp", 1))
    cot_full = features(after(cotangent, attended_full))
    hidden, normed_mid, scale_mlp = add_branch(token_low, attended_full, gain_mlp, out)

    activated, by_gate, by_up = hidden_units(normed_mid, gate_up)
    mlp_term = plain_columns(activated, down, "mlp_out")
    d_gate, d_up = hidden_back(after(cot_full, mlp_term), by_gate, by_up, down)
    d_mid_term = stacked_columns([d_gate, d_up], gate_up, "d_mid")
    d_mid_part = feature_sum(d_mid_term)
    d_mid = features(d_mid_part)

    grad_down = Reduction(activated, cot_full, 1, "grad_down")
    grad_gate = Reduction(normed_mid, d_gate, 0, "grad_gate")
    grad_up = Reduction(normed_mid, d_up, 0, "grad_up")
    grad_down.near(d_mid_term)
    grad_gate.near(d_mid_term)
    grad_up.near(d_mid_term)
    grad_down.far(d_mid_term)
    grad_down.send_far()
    grad_gate.far(grad_down.two)
    grad_up.far(grad_gate.two)
    grad_down.mine(d_mid_part, grad_up.two)
    grad_down.send_context()
    grad_gate.send_far(grad_down.across)

    d_hidden_own, d_branch, d_attended, gain_mlp_term = branch_back(
        tensor_index[None],
        after(d_mid, grad_gate.across, grad_down.own),
        hidden,
        cot_full,
        scale_mlp,
        gain_mlp,
        out,
        part_width,
    )
    grad_up.send_far(grad_gate.across)
    dq_peer, dkv_peer = peer_backward(
        need, queries, peer_kv, d_attended, attended, low_row, logs
    )
    dkv_in = lax.ppermute(dkv_peer, "context", [(1, 0)])
    d_query, dk_own, dv_own = own_backward(
        queries, keys_values, d_attended, attended, low_row, logs, dq_peer, cos, sin
    )
    grad_gate.mine(d_query)
    grad_gate.send_context(grad_down.other)
    mlp_out = feature_sum(after(mlp_term, d_mid)).astype(F32)
    d_key, d_value = finish_keys(dk_own, dv_own, after(dkv_in, grad_gate.own), cos, sin)
    d_parts = (d_query, d_key, d_value)
    d_in_term = stacked_columns(list(d_parts), qkv, "d_in")
    d_in = feature_sum(d_in_term).astype(F32)

    grad_parts = [Reduction(normed_in, d, 0, "grad_qkv") for d in d_parts]
    grad_out = Reduction(attended, d_branch, 1, "grad_out")
    tail = [grad_out] + grad_parts
    for part_sum in tail:
        part_sum.near(d_in_term)
    grad_up.mine(d_in_term)
    grad_up.send_context(grad_gate.other)
    sent = grad_up.across
    for part_sum in tail:
        part_sum.far(d_in_term)
        part_sum.send_far(sent)
        sent = part_sum.across
    sent = grad_up.other
    for part_sum in tail:
        part_sum.mine()
        part_sum.send_context()

    block_out = (own_features(hidden) + mlp_out).astype(BF)
    stream = token_low.astype(F32)
    d_in_wide = d_in_term.astype(F32)
    inner_term = jnp.sum(d_in_wide * gain_attn * stream, axis=1)[None, :]
    inner_in = small_sum(inner_term, "tensor")[0][:, None] / full_width
    gain_attn_term = jnp.sum(d_in_wide * stream * scale_attn, axis=0)

    own_tokens = tokens.astype(F32)
    grad_tokens = (
        d_hidden_own
        + scale_attn * own_features(gain_attn) * d_in
        - own_tokens * scale_attn * scale_attn * scale_attn * inner_in
    ).astype(BF)

    column = jnp.arange(full_width, dtype=jnp.int32)
    mine = column // part_width == tensor_index
    gain_terms = jnp.stack([gain_attn_term, jnp.where(mine, gain_mlp_term[0], 0.0)])
    gain_sums = lax.psum(gain_terms, ("fsdp", "context", "tensor"))
    gain_width = gains.shape[1]
    place = (tensor_index * shards + lax.axis_index("fsdp")) * gain_width
    grad_gains = lax.dynamic_slice_in_dim(gain_sums, place, gain_width, 1)

    return (
        block_out,
        grad_tokens,
        jnp.swapaxes(totals(grad_parts, 0), 0, 1),
        totals([grad_out], 0)[0],
        totals([grad_gate, grad_up], 1),
        totals([grad_down], 0, d_in_term)[0],
        grad_gains,
    )


def solution(mesh):
    rows = P(("fsdp", "context"), "tensor")
    inner = P("fsdp", None, "tensor")
    outer = P("tensor", "fsdp")
    gain = P(None, ("tensor", "fsdp"))
    return jax.shard_map(
        per_device,
        mesh=mesh,
        in_specs=(rows, inner, outer, inner, outer, gain, P("fsdp", None), rows),
        out_specs=(rows, rows, inner, outer, inner, outer, gain),
        check_vma=False,
    )
```

```python
import functools

import jax
import jax.numpy as jnp
from jax import lax
from jax.experimental import pallas as pl
from jax.experimental.pallas import tpu as pltpu
from jax.sharding import PartitionSpec as P

HDIM = 64
LANES = 128
QROWS = 256
norm_eps = 1e-05
rope_base = 130000.0
masked_score = -1e30
BF = jnp.bfloat16
F32 = jnp.float32
VMEM_BYTES = 56 * 1024 * 1024
LIGHT = pl.CostEstimate(flops=1, bytes_accessed=1, transcendentals=0)


def dotf(a, b, dims):
    return lax.dot_general(a, b, (dims, ((), ())), preferred_element_type=F32)


NN = ((1,), (0,))
NT = ((1,), (1,))
TN = ((0,), (0,))


def swap(value, axis, bit):
    count = lax.axis_size(axis)
    return lax.ppermute(value, axis, [(i, i ^ bit) for i in range(count)])


def after(value, *others):
    return lax.optimization_barrier((value, *others))[0]


def shifted(value, axis):
    count = lax.axis_size(axis)
    return [
        lax.ppermute(value, axis, [(i, (i + step) % count) for i in range(count)])
        for step in range(1, count)
    ]


def exchange(value, axis, bit):
    return value + swap(value, axis, bit)


def join_kernel(axis, mode, *refs):
    pieces, out_ref = refs[:-1], refs[-1]
    count = len(pieces)
    me = lax.axis_index(axis)
    for step, piece in enumerate(pieces):
        size = piece.shape[1]
        place = (me ^ step) if mode == "xor" else (me - step + count) % count
        out_ref[:, pl.ds(pl.multiple_of(place * size, size), size)] = piece[...]


def join(pieces, axis, mode):
    rows, size = pieces[0].shape
    return pl.pallas_call(
        functools.partial(join_kernel, axis, mode),
        out_shape=jax.ShapeDtypeStruct((rows, size * len(pieces)), pieces[0].dtype),
        cost_estimate=LIGHT,
        name="join",
    )(*pieces)


def gather_gains(gains):
    if lax.axis_size("tensor") > 4 or gains.shape[1] % LANES:
        return lax.all_gather(gains, ("tensor", "fsdp"), axis=1, tiled=True).astype(F32)
    own = gains.astype(F32)
    part = join([own] + [swap(own, "fsdp", bit) for bit in (1, 2, 3)], "fsdp", "xor")
    return join([part] + shifted(part, "tensor"), "tensor", "shift")


def block_totals(blocks):
    count = lax.axis_size("tensor")
    me = lax.axis_index("tensor")
    if count > 4:
        return lax.dynamic_index_in_dim(lax.psum(blocks, "tensor"), me, 1, keepdims=False)

    def pick(place):
        return lax.dynamic_index_in_dim(blocks, place, 1, keepdims=False)

    total = pick(me)
    for step in range(1, count):
        moves = [(i, (i + step) % count) for i in range(count)]
        total = total + lax.ppermute(pick((me + step) % count), "tensor", moves)
    return total


def piece_columns(j, size):
    return pl.ds(pl.multiple_of((lax.axis_index("fsdp") ^ j) * size, size), size)


def swap_halves(block):
    lane = lax.broadcasted_iota(jnp.int32, block.shape, 1)
    up = pltpu.roll(block, LANES - HDIM // 2, 1)
    down = pltpu.roll(block, HDIM // 2, 1)
    return jnp.where((lane & (HDIM - 1)) < HDIM // 2, up, down)


def rope_tables(positions):
    lane = jnp.arange(LANES, dtype=jnp.int32)
    half = lane % (HDIM // 2)
    frequencies = rope_base ** (-2.0 * half.astype(F32) / HDIM)
    angles = positions.astype(F32)[:, None] * frequencies[None, :]
    sign = jnp.where((lane % HDIM) < HDIM // 2, -1.0, 1.0)
    return jnp.cos(angles), jnp.sin(angles) * sign[None, :]


def piece_dot(x_ref, rows, pieces, dims=NN):
    total = None
    for j, piece in enumerate(pieces):
        size = piece.shape[dims[1][0]]
        term = dotf(x_ref[rows, piece_columns(j, size)], piece, dims)
        total = term if total is None else total + term
    return total


def project_kernel(kinds, normalize, x_ref, *refs):
    pieces, (cos_ref, sin_ref, gain_ref), outs = refs[:4], refs[4:7], refs[7:]
    out_ref = outs[0]
    rows, width = out_ref.shape[1:]
    step = pl.program_id(0)
    if normalize:
        normed_ref, scale_ref = outs[1], outs[2]

        @pl.when(step == 0)
        def _():
            for r in range(0, rows, QROWS):
                part = slice(r, r + QROWS)
                stream = x_ref[part, :].astype(F32)
                mean = jnp.sum(stream * stream, axis=1, keepdims=True) / x_ref.shape[1]
                scale = lax.rsqrt(mean + norm_eps)
                scale_ref[part, :] = scale
                normed_ref[part, :] = (stream * scale * gain_ref[...]).astype(BF)

        x_ref = normed_ref
    for index, scale in enumerate(kinds):

        @pl.when(step == index)
        def _():
            for r in range(0, rows, QROWS):
                part = slice(r, r + QROWS)
                result = piece_dot(x_ref, part, [piece[0] for piece in pieces])
                for c in range(0, width, LANES):
                    block = result[:, c : c + LANES]
                    if scale:
                        block = block * cos_ref[part, :] + swap_halves(block) * sin_ref[part, :]
                    low = block.astype(BF)
                    if scale and scale != 1.0:
                        low = low * jnp.asarray(scale, BF)
                    out_ref[0, part, c : c + LANES] = low


def project(x, pieces, cos, sin, gain, kinds, first, normalize):
    rows, depth = x.shape
    _, size, width = pieces[0].shape
    flops = 2 * len(kinds) * rows * depth * width
    whole = pl.BlockSpec((rows, depth), lambda i: (0, 0))
    table = pl.BlockSpec((rows, LANES), lambda i: (0, 0))
    out_shape = [jax.ShapeDtypeStruct((len(kinds), rows, width), BF)]
    out_specs = [pl.BlockSpec((1, rows, width), lambda i: (i, 0, 0))]
    if normalize:
        out_shape += [jax.ShapeDtypeStruct((rows, depth), BF), jax.ShapeDtypeStruct((rows, 1), F32)]
        out_specs += [whole, pl.BlockSpec((rows, 1), lambda i: (0, 0))]
    return pl.pallas_call(
        functools.partial(project_kernel, kinds, normalize),
        name="project_kv" if normalize else "project_q",
        grid=(len(kinds),),
        out_shape=out_shape,
        in_specs=[whole]
        + [pl.BlockSpec((1, size, width), lambda i: (i + first, 0, 0))] * 4
        + [table, table, pl.BlockSpec((1, depth), lambda i: (0, 0))],
        out_specs=out_specs,
        compiler_params=pltpu.CompilerParams(vmem_limit_bytes=VMEM_BYTES),
        cost_estimate=LIGHT,
    )(x, *pieces, cos, sin, gain)


def head_mask(block, head):
    lane = lax.broadcasted_iota(jnp.int32, block.shape, 1)
    inside = (lane < HDIM) if head == 0 else (lane >= HDIM)
    return jnp.where(inside, block, jnp.zeros_like(block))


def own_mask(key_count, row0, low_row):
    key = lax.broadcasted_iota(jnp.int32, (key_count, QROWS), 0)
    query = row0 + lax.broadcasted_iota(jnp.int32, (key_count, QROWS), 1)
    return (key >= low_row) & (key <= query)


def peer_mask(key_count, low_row, offset):
    key = lax.broadcasted_iota(jnp.int32, (key_count, QROWS), 0) - offset
    return key >= low_row


def own_forward_kernel(q_ref, k_ref, v_ref, low_ref, out_ref, log_ref):
    rows = q_ref.shape[0]
    v_t = v_ref[...].T
    for r in range(0, rows, QROWS):
        count = r + QROWS
        allowed = own_mask(count, r, low_ref[:, r : r + QROWS])
        keys = k_ref[0:count, :]
        outs = []
        for head in range(LANES // HDIM):
            scores = dotf(keys, head_mask(q_ref[r : r + QROWS, :], head), NT)
            scores = jnp.where(allowed, scores, masked_score)
            peak = jnp.max(scores, axis=0, keepdims=True)
            weights = jnp.exp(scores - peak)
            total = jnp.sum(weights, axis=0, keepdims=True)
            part = dotf(v_t[head * HDIM : (head + 1) * HDIM, 0:count], weights.astype(BF), NN)
            outs.append(part / total)
            log_ref[0, head : head + 1, r : r + QROWS] = peak + jnp.log(total)
        out_ref[r : r + QROWS, :] = jnp.concatenate(outs, axis=0).T


def peer_forward_kernel(
    need_ref, q_ref, k_ref, v_ref, low_ref, part_ref, log_in_ref, out_ref, log_ref
):
    rows = q_ref.shape[0]
    key_count = k_ref.shape[0]
    for index, r in enumerate(range(0, rows, QROWS)):
        needed = need_ref[index] < 0

        @pl.when(needed)
        def _():
            v_t = v_ref[...].T
            allowed = peer_mask(key_count, low_ref[:, r : r + QROWS], key_count)
            before = part_ref[r : r + QROWS, :].T
            outs = []
            for head in range(LANES // HDIM):
                scores = dotf(k_ref[...], head_mask(q_ref[r : r + QROWS, :], head), NT)
                scores = jnp.where(allowed, scores, masked_score)
                log_own = log_in_ref[0, head : head + 1, r : r + QROWS]
                peak = jnp.maximum(jnp.max(scores, axis=0, keepdims=True), log_own)
                weights = jnp.exp(scores - peak)
                own_weight = jnp.exp(log_own - peak)
                total = jnp.sum(weights, axis=0, keepdims=True) + own_weight
                rows_h = slice(head * HDIM, (head + 1) * HDIM)
                part = dotf(v_t[rows_h, :], weights.astype(BF), NN)
                outs.append((part + before[rows_h, :] * own_weight) / total)
                log_ref[0, head : head + 1, r : r + QROWS] = peak + jnp.log(total)
            out_ref[r : r + QROWS, :] = jnp.concatenate(outs, axis=0).T.astype(BF)

        @pl.when(jnp.logical_not(needed))
        def _():
            out_ref[r : r + QROWS, :] = part_ref[r : r + QROWS, :].astype(BF)
            log_ref[:, :, r : r + QROWS] = log_in_ref[:, :, r : r + QROWS]


def pair_spec(rows):
    return pl.BlockSpec((rows, LANES), lambda i: (0, i))


def stacked_spec(rows, part):
    return pl.BlockSpec((None, rows, LANES), lambda i: (part, 0, i))


def log_spec(rows):
    return pl.BlockSpec((1, LANES // HDIM, rows), lambda i: (i, 0, 0))


def low_spec(rows):
    return pl.BlockSpec((1, rows), lambda i: (0, 0))


def own_forward(q, kv, low_row):
    rows, width = q.shape
    pairs = width // LANES
    return pl.pallas_call(
        own_forward_kernel,
        name="own_fwd",
        grid=(pairs,),
        out_shape=(
            jax.ShapeDtypeStruct((rows, width), F32),
            jax.ShapeDtypeStruct((pairs, LANES // HDIM, rows), F32),
        ),
        in_specs=[
            pair_spec(rows),
            stacked_spec(rows, 0),
            stacked_spec(rows, 1),
            low_spec(rows),
        ],
        out_specs=(pair_spec(rows), log_spec(rows)),
        compiler_params=pltpu.CompilerParams(vmem_limit_bytes=VMEM_BYTES),
        cost_estimate=LIGHT,
    )(q, kv, kv, low_row)


SMEM_SPEC = pl.BlockSpec(memory_space=pltpu.SMEM)


def peer_forward(need, q, kv, low_row, part, log_in):
    rows, width = q.shape
    pairs = width // LANES
    return pl.pallas_call(
        peer_forward_kernel,
        name="peer_fwd",
        grid=(pairs,),
        out_shape=(
            jax.ShapeDtypeStruct((rows, width), BF),
            jax.ShapeDtypeStruct((pairs, LANES // HDIM, rows), F32),
        ),
        in_specs=[
            SMEM_SPEC,
            pair_spec(rows),
            stacked_spec(rows, 0),
            stacked_spec(rows, 1),
            low_spec(rows),
            pair_spec(rows),
            log_spec(rows),
        ],
        out_specs=(pair_spec(rows), log_spec(rows)),
        compiler_params=pltpu.CompilerParams(vmem_limit_bytes=VMEM_BYTES),
        cost_estimate=LIGHT,
    )(need, q, kv, kv, low_row, part, log_in)


def backward_block(q_rows, k_rows, v_rows, k_t, do_rows, do_o_t, logs, allowed):
    d_query, d_key, d_value = [], None, None
    for head in range(LANES // HDIM):
        rows_h = slice(head * HDIM, (head + 1) * HDIM)
        q_head = head_mask(q_rows, head)
        do_head = head_mask(do_rows, head)
        scores = dotf(k_rows, q_head, NT)
        probs = jnp.exp(jnp.where(allowed, scores, masked_score) - logs[head])
        delta = jnp.sum(do_o_t[rows_h, :], axis=0, keepdims=True)
        d_probs = dotf(v_rows, do_head, NT)
        d_scores = (probs * (d_probs - delta)).astype(BF)
        d_v = dotf(probs.astype(BF), do_head, NN)
        d_k = dotf(d_scores, q_head, NN)
        d_value = d_v if d_value is None else d_value + d_v
        d_key = d_k if d_key is None else d_key + d_k
        d_query.append(dotf(k_t[rows_h, :], d_scores, NN))
    return jnp.concatenate(d_query, axis=0), d_key, d_value


def output_product(do_ref, o_ref, window):
    product = do_ref[window].astype(F32) * o_ref[window].astype(F32)
    return product.T


def peer_backward_kernel(
    need_ref, q_ref, k_ref, v_ref, do_ref, o_ref, low_ref, log_ref, dq_ref, dkv_ref, sums
):
    rows = q_ref.shape[0]
    key_count = k_ref.shape[0]
    sums[...] = jnp.zeros_like(sums)
    for index, r in enumerate(range(0, rows, QROWS)):
        needed = need_ref[index] < 0
        window = (slice(r, r + QROWS), slice(None))

        @pl.when(needed)
        def _():
            allowed = peer_mask(key_count, low_ref[:, r : r + QROWS], key_count)
            logs = [log_ref[0, h : h + 1, r : r + QROWS] for h in range(LANES // HDIM)]
            d_query, d_key, d_value = backward_block(
                q_ref[window],
                k_ref[...],
                v_ref[...],
                k_ref[...].T,
                do_ref[window],
                output_product(do_ref, o_ref, window),
                logs,
                allowed,
            )
            dq_ref[window] = d_query.T
            sums[0] += d_key
            sums[1] += d_value

        @pl.when(jnp.logical_not(needed))
        def _():
            dq_ref[window] = jnp.zeros((QROWS, LANES), F32)

    dkv_ref[...] = sums[...].astype(BF)


def peer_backward(need, q, kv, do, o, low_row, logs):
    rows, width = q.shape
    pairs = width // LANES
    return pl.pallas_call(
        peer_backward_kernel,
        name="peer_bwd",
        grid=(pairs,),
        out_shape=(
            jax.ShapeDtypeStruct((rows, width), F32),
            jax.ShapeDtypeStruct((2, rows, width), BF),
        ),
        in_specs=[
            SMEM_SPEC,
            pair_spec(rows),
            stacked_spec(rows, 0),
            stacked_spec(rows, 1),
            pair_spec(rows),
            pair_spec(rows),
            low_spec(rows),
            log_spec(rows),
        ],
        out_specs=(pair_spec(rows), pl.BlockSpec((2, rows, LANES), lambda i: (0, 0, i))),
        scratch_shapes=[pltpu.VMEM((2, rows, LANES), F32)],
        compiler_params=pltpu.CompilerParams(vmem_limit_bytes=VMEM_BYTES),
        cost_estimate=LIGHT,
    )(need, q, kv, kv, do, o, low_row, logs)


def own_backward_kernel(
    q_ref,
    k_ref,
    v_ref,
    do_ref,
    o_ref,
    low_ref,
    log_ref,
    dq_in_ref,
    cos_ref,
    sin_ref,
    dq_ref,
    dk_ref,
    dv_ref,
    sums,
):
    rows = q_ref.shape[0]
    sums[...] = jnp.zeros_like(sums)
    k_t = k_ref[...].T
    for r in range(0, rows, QROWS):
        count = r + QROWS
        window = (slice(r, r + QROWS), slice(None))
        allowed = own_mask(count, r, low_ref[:, r : r + QROWS])
        logs = [log_ref[0, h : h + 1, r : r + QROWS] for h in range(LANES // HDIM)]
        d_query, d_key, d_value = backward_block(
            q_ref[window],
            k_ref[0:count, :],
            v_ref[0:count, :],
            k_t[:, 0:count],
            do_ref[window],
            output_product(do_ref, o_ref, window),
            logs,
            allowed,
        )
        rotated = (d_query.T + dq_in_ref[window]) * (HDIM**-0.5)
        turned = rotated * cos_ref[window] - swap_halves(rotated) * sin_ref[window]
        dq_ref[window] = turned.astype(BF)
        sums[0, 0:count] += d_key
        sums[1, 0:count] += d_value
    dk_ref[...] = sums[0]
    dv_ref[...] = sums[1]


def own_backward(q, kv, do, o, low_row, logs, dq_in, cos, sin):
    rows, width = q.shape
    pairs = width // LANES
    table = pl.BlockSpec((rows, LANES), lambda i: (0, 0))
    return pl.pallas_call(
        own_backward_kernel,
        name="own_bwd",
        grid=(pairs,),
        out_shape=(
            jax.ShapeDtypeStruct((rows, width), BF),
            jax.ShapeDtypeStruct((rows, width), F32),
            jax.ShapeDtypeStruct((rows, width), F32),
        ),
        in_specs=[
            pair_spec(rows),
            stacked_spec(rows, 0),
            stacked_spec(rows, 1),
            pair_spec(rows),
            pair_spec(rows),
            low_spec(rows),
            log_spec(rows),
            pair_spec(rows),
            table,
            table,
        ],
        out_specs=(pair_spec(rows),) * 3,
        scratch_shapes=[pltpu.VMEM((2, rows, LANES), F32)],
        compiler_params=pltpu.CompilerParams(vmem_limit_bytes=VMEM_BYTES),
        cost_estimate=LIGHT,
    )(q, kv, kv, do, o, low_row, logs, dq_in, cos, sin)


def finish_keys_kernel(dk_ref, dv_ref, dk_in_ref, dv_in_ref, cos_ref, sin_ref, dk_out, dv_out):
    total = dk_ref[...] + dk_in_ref[...].astype(F32)
    turned = total * cos_ref[...] - swap_halves(total) * sin_ref[...]
    dk_out[...] = turned.astype(BF)
    dv_out[...] = (dv_ref[...] + dv_in_ref[...].astype(F32)).astype(BF)


def finish_keys(dk, dv, dkv_in, cos, sin):
    rows, width = dk.shape
    pairs = width // LANES
    table = pl.BlockSpec((rows, LANES), lambda i: (0, 0))
    return pl.pallas_call(
        finish_keys_kernel,
        name="finish_keys",
        grid=(pairs,),
        out_shape=(jax.ShapeDtypeStruct((rows, width), BF),) * 2,
        in_specs=[pair_spec(rows), pair_spec(rows), stacked_spec(rows, 0), stacked_spec(rows, 1)]
        + [table, table],
        out_specs=(pair_spec(rows),) * 2,
        cost_estimate=LIGHT,
    )(dk, dv, dkv_in, dkv_in, cos, sin)


def branch_kernel(stream_ref, att_ref, gain_ref, *refs):
    pieces, (hidden_ref, normed_ref, scale_ref) = refs[:4], refs[4:]
    for j, piece in enumerate(pieces):
        columns = piece_columns(j, piece.shape[1])
        term = dotf(att_ref[...], piece[...], NN)
        hidden_ref[:, columns] = stream_ref[:, columns].astype(F32) + term
    hidden = hidden_ref[...]
    mean = jnp.sum(hidden * hidden, axis=1, keepdims=True) / hidden.shape[1]
    scale = lax.rsqrt(mean + norm_eps)
    scale_ref[...] = scale
    normed_ref[...] = (hidden * scale * gain_ref[...]).astype(BF)


def add_branch(stream, att, gain, pieces):
    rows, depth = stream.shape
    heads = att.shape[1]
    tile = pl.BlockSpec((QROWS, depth), lambda i: (i, 0))
    return pl.pallas_call(
        branch_kernel,
        name="branch",
        grid=(rows // QROWS,),
        out_shape=(
            jax.ShapeDtypeStruct((rows, depth), F32),
            jax.ShapeDtypeStruct((rows, depth), BF),
            jax.ShapeDtypeStruct((rows, 1), F32),
        ),
        in_specs=[
            tile,
            pl.BlockSpec((QROWS, heads), lambda i: (i, 0)),
            pl.BlockSpec((1, depth), lambda i: (0, 0)),
        ]
        + [pl.BlockSpec(pieces[0].shape, lambda i: (0, 0))] * 4,
        out_specs=(tile, tile, pl.BlockSpec((QROWS, 1), lambda i: (i, 0))),
        compiler_params=pltpu.CompilerParams(vmem_limit_bytes=VMEM_BYTES),
        cost_estimate=LIGHT,
    )(stream, att, gain, *pieces)


def hidden_kernel(x_ref, *refs):
    w_in, (act_ref, by_gate_ref, by_up_ref) = refs[:4], refs[4:]
    rows = x_ref.shape[0]
    for r in range(0, rows, QROWS):
        part = slice(r, r + QROWS)
        gate = piece_dot(x_ref, part, [piece[0] for piece in w_in])
        up = piece_dot(x_ref, part, [piece[1] for piece in w_in])
        sig = jax.nn.sigmoid(gate)
        silu = gate * sig
        act_ref[part, :] = (silu * up).astype(BF)
        by_gate_ref[part, :] = (up * sig * (1.0 + gate * (1.0 - sig))).astype(BF)
        by_up_ref[part, :] = silu.astype(BF)


def hidden_units(x, w_in):
    rows, depth = x.shape
    _, size, units = w_in[0].shape
    tile = 256
    part = pl.BlockSpec((rows, tile), lambda i: (0, i))
    return pl.pallas_call(
        hidden_kernel,
        grid=(units // tile,),
        out_shape=(jax.ShapeDtypeStruct((rows, units), BF),) * 3,
        in_specs=[pl.BlockSpec((rows, depth), lambda i: (0, 0))]
        + [pl.BlockSpec((2, size, tile), lambda i: (0, 0, i))] * 4,
        out_specs=(part,) * 3,
        compiler_params=pltpu.CompilerParams(vmem_limit_bytes=VMEM_BYTES),
        cost_estimate=LIGHT,
        name="hidden",
    )(x, *w_in)


def hidden_back_kernel(cot_ref, by_gate_ref, by_up_ref, *refs):
    w_down, (dg_ref, du_ref) = refs[:4], refs[4:]
    rows = cot_ref.shape[0]
    for r in range(0, rows, QROWS):
        part = slice(r, r + QROWS)
        d_act = piece_dot(cot_ref, part, [piece[...] for piece in w_down], NT)
        dg_ref[part, :] = (d_act * by_gate_ref[part, :].astype(F32)).astype(BF)
        du_ref[part, :] = (d_act * by_up_ref[part, :].astype(F32)).astype(BF)


def hidden_back(cot, by_gate, by_up, w_down):
    rows, depth = cot.shape
    units, size = w_down[0].shape
    tile = 256
    part = pl.BlockSpec((rows, tile), lambda i: (0, i))
    return pl.pallas_call(
        hidden_back_kernel,
        grid=(units // tile,),
        out_shape=(jax.ShapeDtypeStruct((rows, units), BF),) * 2,
        in_specs=[pl.BlockSpec((rows, depth), lambda i: (0, 0)), part, part]
        + [pl.BlockSpec((tile, size), lambda i: (i, 0))] * 4,
        out_specs=(part,) * 2,
        compiler_params=pltpu.CompilerParams(vmem_limit_bytes=VMEM_BYTES),
        cost_estimate=LIGHT,
        name="hidden_back",
    )(cot, by_gate, by_up, *w_down)


def phased(i, block, make_index, tiles):
    def index_map(j, t):
        return make_index(jnp.where(j < i, 0, jnp.where(j == i, t, tiles - 1)))

    return pl.BlockSpec(block, index_map)


def columns_call(kernel_dot, lefts, pieces, block, make_index, size, flops, name):
    rows = lefts[0].shape[0]
    tile = min(size, 256)
    tiles = size // tile
    depth = size * 4

    def kernel(*refs):
        left_refs, piece_refs, out_ref = refs[: len(lefts)], refs[len(lefts) : -1], refs[-1]
        for j, piece in enumerate(piece_refs):

            @pl.when(pl.program_id(0) == j)
            def _():
                for r in range(0, rows, QROWS):
                    out_ref[r : r + QROWS, :] = kernel_dot(
                        [left[r : r + QROWS, :] for left in left_refs], piece
                    ).astype(BF)

    def out_index(j, t):
        return (0, (lax.axis_index("fsdp") ^ j) * tiles + t)

    return pl.pallas_call(
        kernel,
        grid=(4, tiles),
        out_shape=jax.ShapeDtypeStruct((rows, depth), BF),
        in_specs=[pl.BlockSpec(left.shape, lambda j, t: (0, 0)) for left in lefts]
        + [phased(i, block(tile), make_index, tiles) for i in range(4)],
        out_specs=pl.BlockSpec((rows, tile), out_index),
        compiler_params=pltpu.CompilerParams(vmem_limit_bytes=VMEM_BYTES),
        cost_estimate=LIGHT,
        name=name,
    )(*lefts, *pieces)


def stacked_columns(lefts, pieces, name):
    count, size, inner = pieces[0].shape

    def product(parts, piece):
        return sum(dotf(parts[c], piece[c], NT) for c in range(count))

    return columns_call(
        product,
        lefts,
        pieces,
        lambda tile: (count, tile, inner),
        lambda t: (0, t, 0),
        size,
        8 * lefts[0].shape[0] * size * inner * count,
        name,
    )


def plain_columns(left, pieces, name):
    inner, size = pieces[0].shape
    return columns_call(
        lambda parts, piece: dotf(parts[0], piece[...], NN),
        [left],
        pieces,
        lambda tile: (inner, tile),
        lambda t: (0, t),
        size,
        8 * left.shape[0] * size * inner,
        name,
    )


def branch_back_kernel(
    tensor_index_ref, d_mid_ref, hidden_ref, cot_ref, scale_ref, gain_ref, *refs
):
    pieces, (d_own_ref, d_branch_ref, d_att_ref, gain_out_ref) = refs[:4], refs[4:8]
    d_mid = d_mid_ref[...].astype(F32)
    hidden = hidden_ref[...]
    scale = scale_ref[...]
    weighted = d_mid * gain_ref[...]
    inner = jnp.sum(weighted * hidden, axis=1, keepdims=True) / hidden.shape[1]
    d_hidden = (
        cot_ref[...].astype(F32) + scale * weighted - hidden * (scale * scale * scale * inner)
    )
    gain_term = jnp.sum(d_mid * hidden * scale, axis=0, keepdims=True)

    @pl.when(pl.program_id(0) == 0)
    def _():
        gain_out_ref[...] = gain_term

    @pl.when(pl.program_id(0) != 0)
    def _():
        gain_out_ref[...] += gain_term

    d_branch_ref[...] = d_hidden.astype(BF)
    width = d_own_ref.shape[1]
    for z in range(hidden.shape[1] // width):

        @pl.when(tensor_index_ref[0] == z)
        def _():
            d_own_ref[...] = d_hidden[:, z * width : (z + 1) * width]

    d_att_ref[...] = piece_dot(
        d_branch_ref, slice(None), [piece[...] for piece in pieces], NT
    ).astype(BF)


def branch_back(tensor_index, d_mid, hidden, cot, scale, gain, pieces, own_width):
    rows, depth = hidden.shape
    heads, size = pieces[0].shape[0] // (depth // own_width), pieces[0].shape[1]
    tile = pl.BlockSpec((QROWS, depth), lambda i, s: (i, 0))
    row = pl.BlockSpec((1, depth), lambda i, s: (0, 0))
    own = pl.BlockSpec((QROWS, own_width), lambda i, s: (i, 0))
    return pl.pallas_call(
        branch_back_kernel,
        name="branch_back",
        grid_spec=pltpu.PrefetchScalarGridSpec(
            num_scalar_prefetch=1,
            grid=(rows // QROWS,),
            in_specs=[tile, tile, tile, pl.BlockSpec((QROWS, 1), lambda i, s: (i, 0)), row]
            + [pl.BlockSpec((heads, size), lambda i, s: (s[0], 0))] * 4,
            out_specs=(own, tile, pl.BlockSpec((QROWS, heads), lambda i, s: (i, 0)), row),
        ),
        out_shape=(
            jax.ShapeDtypeStruct((rows, own_width), F32),
            jax.ShapeDtypeStruct((rows, depth), BF),
            jax.ShapeDtypeStruct((rows, heads), BF),
            jax.ShapeDtypeStruct((1, depth), F32),
        ),
        compiler_params=pltpu.CompilerParams(vmem_limit_bytes=VMEM_BYTES),
        cost_estimate=LIGHT,
    )(tensor_index, d_mid, hidden, cot, scale, gain, *pieces)


def grad_call(left, right, cut, place, adds, name):
    rows = left.shape[0]
    size = (left, right)[cut].shape[1] // 4
    height = size if cut == 0 else left.shape[1]
    width = right.shape[1] if cut == 0 else size
    swept = (width, height)[cut]
    tile = min(1024, swept)
    block = (height, tile) if cut == 0 else (tile, width)

    def owner():
        return lax.axis_index("fsdp") ^ place

    def swept_index(t):
        return (0, t) if cut == 0 else (t, 0)

    def kernel(left_ref, right_ref, *refs):
        add_refs, out_ref = refs[: len(adds)], refs[len(adds)]
        if cut == 0:
            turned = refs[-1]

            @pl.when(pl.program_id(0) == 0)
            def _():
                turned[...] = left_ref[...].T

            result = dotf(turned[...], right_ref[...], NN)
        else:
            result = dotf(left_ref[...].T, right_ref[...], NN)
        for add in add_refs:
            result = result + add[...].astype(F32)
        out_ref[...] = result.astype(BF)

    fixed = pl.BlockSpec((rows, size), lambda t: (0, owner()))
    moving = pl.BlockSpec((rows, tile), lambda t: (0, t))
    return pl.pallas_call(
        kernel,
        grid=(swept // tile,),
        out_shape=jax.ShapeDtypeStruct((height, width), BF),
        in_specs=[fixed, moving] * (cut == 0)
        + [moving, fixed] * (cut == 1)
        + [pl.BlockSpec(block, swept_index)] * len(adds),
        out_specs=pl.BlockSpec(block, swept_index),
        scratch_shapes=[pltpu.VMEM((size, rows), BF)] if cut == 0 else [],
        compiler_params=pltpu.CompilerParams(vmem_limit_bytes=VMEM_BYTES),
        cost_estimate=LIGHT,
        name=name,
    )(left, right, *adds)


class Reduction:
    def __init__(self, left, right, cut, name):
        self.args, self.name = (left, right, cut), name

    def call(self, place, deps, step, adds=()):
        left, right, cut = self.args
        left = after(left, *deps) if deps else left
        return grad_call(left, right, cut, place, adds, self.name + step)

    def near_far(self, *deps):
        self.three = self.call(3, deps, "_3")
        self.for_two = swap(self.three, "fsdp", 1)

    def near(self, *deps):
        self.one = self.call(1, deps, "_1")
        self.for_own = swap(self.one, "fsdp", 1)

    def far(self, *deps):
        self.two = self.call(2, deps, "_2", [self.for_two])

    def send_far(self, *deps):
        self.across = swap(after(self.two, *deps), "fsdp", 2)

    def mine(self, *deps):
        self.own = self.call(0, deps, "_0", [self.for_own, self.across])

    def send_context(self, *deps):
        self.other = swap(after(self.own, *deps), "context", 1)


def totals_kernel(slots, *refs):
    pairs, out_ref = refs[:-1], refs[-1]
    for slot in range(len(pairs) // 2):
        total = pairs[2 * slot][...].astype(F32) + pairs[2 * slot + 1][...].astype(F32)
        if slots == 0:
            out_ref[slot] = total
        else:
            out_ref[:, slot, :] = total


def totals(sums, slots, *deps):
    arrays = [array for part in sums for array in (part.own, part.other)]
    if deps:
        arrays[0] = after(arrays[0], *deps)
    rows, width = arrays[0].shape
    tile = 128
    shape = [rows, width]
    shape.insert(slots, len(sums))
    block = [tile, width]
    block.insert(slots, len(sums))
    return pl.pallas_call(
        functools.partial(totals_kernel, slots),
        grid=(rows // tile,),
        out_shape=jax.ShapeDtypeStruct(tuple(shape), F32),
        in_specs=[pl.BlockSpec((tile, width), lambda i: (i, 0))] * len(arrays),
        out_specs=pl.BlockSpec(
            tuple(block), (lambda i: (0, i, 0)) if slots == 0 else (lambda i: (i, 0, 0))
        ),
        compiler_params=pltpu.CompilerParams(vmem_limit_bytes=VMEM_BYTES),
        cost_estimate=LIGHT,
        name="totals",
    )(*arrays)


def row_sum(values_in):
    return jnp.sum(values_in, axis=1, keepdims=True)


def per_device(tokens, w_qkv, w_out, w_gate_up, w_down, gains, seq_lengths, cotangent):
    row_count, part_width = tokens.shape
    tensor_index = lax.axis_index("tensor")
    context_index = lax.axis_index("context")
    full_width = part_width * lax.axis_size("tensor")

    def features(part_in):
        return lax.all_gather(part_in, "tensor", axis=1, tiled=True)

    def feature_sum(term):
        return lax.psum_scatter(term.astype(BF), "tensor", scatter_dimension=1, tiled=True)

    def own_features(full):
        return lax.dynamic_slice_in_dim(full, tensor_index * part_width, part_width, 1)

    ending = jnp.cumsum(seq_lengths[0])
    starts = ending - seq_lengths[0]
    places = context_index * row_count + jnp.arange(row_count, dtype=jnp.int32)
    first_token = jnp.max(jnp.where(starts[None, :] <= places[:, None], starts[None, :], 0), axis=1)
    cos, sin = rope_tables(places - first_token)
    low = first_token - context_index * row_count
    low_row = low[None, :]
    need = low[::QROWS]

    token_low = features(tokens)
    gain_full = gather_gains(gains)
    gain_attn, gain_mlp = gain_full[0:1], gain_full[1:2]

    qkv_own = jnp.swapaxes(w_qkv, 0, 1)
    half = qkv_own.shape[1] // 2
    far_half = swap(
        lax.dynamic_slice_in_dim(qkv_own, context_index * half, half, 1), "fsdp", 2
    )
    other_half = swap(far_half, "context", 1)
    qkv_far = jnp.where(
        context_index == 0,
        jnp.concatenate([far_half, other_half], axis=1),
        jnp.concatenate([other_half, far_half], axis=1),
    )
    qkv_near = swap(qkv_own, "fsdp", 1)
    qkv = (qkv_own, qkv_near, qkv_far, swap(qkv_far, "fsdp", 1))

    gate_up_own = jnp.swapaxes(w_gate_up, 0, 1)
    cut = gate_up_own.shape[1] * 19 // 32
    gate_up_a = swap(after(gate_up_own[:, :cut], far_half), "fsdp", 2)
    gate_up_b = swap(after(gate_up_own[:, cut:], gate_up_a), "fsdp", 2)

    keys_values, normed_in, scale_attn = project(
        after(token_low, gate_up_a), qkv, cos, sin, gain_attn, (1.0, None), 1, True
    )
    peer_kv = lax.ppermute(keys_values, "context", [(0, 1)])
    queries = project(normed_in, qkv, cos, sin, gain_attn, (HDIM**-0.5,), 0, False)[0][0]
    part, part_log = own_forward(queries, keys_values, low_row)
    attended, logs = peer_forward(
        need, queries, peer_kv, low_row, after(part, gate_up_b), part_log
    )
    attended_full = features(attended)

    out_own = after(lax.all_gather(w_out, "tensor", axis=0, tiled=True), attended)
    out_far = swap(out_own, "fsdp", 2)
    out = (out_own, swap(out_own, "fsdp", 1), out_far, swap(out_far, "fsdp", 1))
    gate_up_own, gate_up_a, gate_up_b = lax.optimization_barrier(
        (gate_up_own, gate_up_a, gate_up_b, attended)
    )[:3]
    gate_up_far = jnp.concatenate([gate_up_a, gate_up_b], axis=1)
    gate_up_near = swap(gate_up_own, "fsdp", 1)
    gate_up = (gate_up_own, gate_up_near, gate_up_far, swap(gate_up_far, "fsdp", 1))
    cot_full = features(after(cotangent, attended_full))
    down_far = swap(after(w_down, attended_full), "fsdp", 2)
    down_near = swap(after(w_down, attended_full), "fsdp", 1)
    hidden, normed_mid, scale_mlp = add_branch(token_low, attended_full, gain_mlp, out)

    activated, by_gate, by_up = hidden_units(normed_mid, gate_up)
    down_far = after(down_far, activated)
    down = (w_down, down_near, down_far, swap(down_far, "fsdp", 1))
    d_gate, d_up = hidden_back(cot_full, by_gate, by_up, down)
    d_mid_term = stacked_columns([d_gate, d_up], gate_up, "d_mid")
    d_mid_part = feature_sum(d_mid_term)

    grad_down = Reduction(activated, cot_full, 1, "grad_down")
    grad_gate = Reduction(normed_mid, d_gate, 0, "grad_gate")
    grad_up = Reduction(normed_mid, d_up, 0, "grad_up")
    grad_down.near_far(d_mid_term)
    grad_gate.near_far(grad_down.three)
    grad_up.near_far(grad_gate.three)
    grad_down.near(grad_up.three)
    grad_down.far(grad_down.one)
    grad_down.send_far()
    d_mid_part = after(d_mid_part, grad_down.two)
    d_mid = features(d_mid_part)
    grad_gate.near(grad_down.two)
    grad_gate.far(grad_gate.one)
    grad_up.near(grad_gate.two)
    grad_up.far(grad_up.one)
    mlp_term = plain_columns(after(activated, grad_up.two), down, "mlp_out")
    grad_down.mine(d_mid_part, mlp_term)
    grad_down.send_context()
    grad_gate.send_far(grad_down.across)
    grad_gate.mine(grad_down.own)
    grad_gate.send_context(grad_down.other)
    grad_up.send_far(grad_gate.across)

    d_hidden_own, d_branch, d_attended, gain_mlp_term = branch_back(
        tensor_index[None],
        after(d_mid, grad_gate.own),
        hidden,
        cot_full,
        scale_mlp,
        gain_mlp,
        out,
        part_width,
    )
    mlp_out = feature_sum(after(mlp_term, d_mid)).astype(F32)
    dq_peer, dkv_peer = peer_backward(
        need, queries, peer_kv, d_attended, attended, low_row, logs
    )
    dkv_in = lax.ppermute(dkv_peer, "context", [(1, 0)])
    d_query, dk_own, dv_own = own_backward(
        queries, keys_values, d_attended, attended, low_row, logs, dq_peer, cos, sin
    )
    grad_out = Reduction(attended, d_branch, 1, "grad_out")
    grad_query = Reduction(normed_in, d_query, 0, "grad_query")
    grad_out.near_far(d_query)
    grad_query.near_far(grad_out.three)
    grad_out.near(grad_query.three)
    grad_query.near(grad_out.one)
    grad_out.far(grad_query.one)
    grad_query.far(grad_out.two)
    d_key, d_value = finish_keys(dk_own, dv_own, after(dkv_in, grad_query.two), cos, sin)
    d_in_term = stacked_columns([d_query, d_key, d_value], qkv, "d_in")
    d_in = feature_sum(d_in_term).astype(F32)

    grad_up.mine(d_in_term)
    grad_up.send_context(grad_gate.other)
    grad_out.send_far(grad_up.across)
    grad_query.send_far(grad_up.across)
    grad_key = Reduction(normed_in, d_key, 0, "grad_key")
    grad_value = Reduction(normed_in, d_value, 0, "grad_value")
    grad_key.near_far(grad_up.own)
    grad_value.near_far(grad_key.three)
    grad_key.near(grad_value.three)
    grad_value.near(grad_key.one)
    grad_key.far(grad_value.one)
    grad_value.far(grad_key.two)
    grad_key.send_far(grad_query.across)
    grad_value.send_far(grad_query.across)

    stream = token_low.astype(F32)
    d_in_wide = after(d_in_term, grad_value.two).astype(F32)
    weighted = d_in_wide * stream
    inner_term = jnp.sum(weighted * gain_attn, axis=1)
    gain_attn_term = jnp.sum(weighted * scale_attn, axis=0)
    parts = lax.axis_size("tensor")
    totals_small = block_totals(
        jnp.concatenate(
            [
                jnp.broadcast_to(inner_term[None, :], (parts, row_count)),
                gain_attn_term.reshape(parts, part_width),
            ],
            axis=1,
        )[None]
    )
    inner_in = totals_small[0, :row_count][:, None] / full_width
    gain_sums = jnp.concatenate(
        [totals_small[:, row_count:], own_features(gain_mlp_term)], axis=0
    )
    gain_sums = exchange(gain_sums, "fsdp", 1)
    gain_sums = exchange(gain_sums, "fsdp", 2)
    gain_sums = exchange(gain_sums, "context", 1)
    gain_width = gains.shape[1]
    grad_gains = lax.dynamic_slice_in_dim(
        gain_sums, lax.axis_index("fsdp") * gain_width, gain_width, 1
    )

    grad_out.mine(d_in_wide)
    grad_query.mine(grad_out.own)
    grad_out.send_context()
    grad_query.send_context()
    grad_down_sum = totals([grad_down], 0, grad_query.own)[0]
    grad_key.mine(grad_down_sum, d_in)
    grad_value.mine(grad_key.own)
    grad_key.send_context()
    grad_value.send_context()
    grad_gate_up_sum = totals([grad_gate, grad_up], 1, grad_value.own)
    grad_out_sum = totals([grad_out], 0, grad_gate_up_sum)[0]
    grad_qkv = totals([grad_query, grad_key, grad_value], 0, grad_out_sum)

    block_out = (own_features(hidden) + mlp_out).astype(BF)
    own_tokens = tokens.astype(F32)
    grad_tokens = (
        d_hidden_own
        + scale_attn * own_features(gain_attn) * d_in
        - own_tokens * scale_attn * scale_attn * scale_attn * inner_in
    ).astype(BF)
    return (
        block_out,
        grad_tokens,
        jnp.swapaxes(grad_qkv, 0, 1),
        grad_out_sum,
        grad_gate_up_sum,
        grad_down_sum,
        grad_gains,
    )


def solution(mesh):
    rows = P(("fsdp", "context"), "tensor")
    inner = P("fsdp", None, "tensor")
    outer = P("tensor", "fsdp")
    gain = P(None, ("tensor", "fsdp"))
    return jax.shard_map(
        per_device,
        mesh=mesh,
        in_specs=(rows, inner, outer, inner, outer, gain, P("fsdp", None), rows),
        out_specs=(rows, rows, inner, outer, inner, outer, gain),
        check_vma=False,
    )
```

```python
import functools

import jax
import jax.numpy as jnp
from jax import lax
from jax.experimental import pallas as pl
from jax.experimental.pallas import tpu as pltpu
from jax.sharding import PartitionSpec as P

HDIM = 64
LANES = 128
QROWS = 256
norm_eps = 1e-05
rope_base = 130000.0
masked_score = -1e30
BF = jnp.bfloat16
F32 = jnp.float32
VMEM_BYTES = 56 * 1024 * 1024
LIGHT = pl.CostEstimate(flops=1, bytes_accessed=1, transcendentals=0)


def dotf(a, b, dims):
    return lax.dot_general(a, b, (dims, ((), ())), preferred_element_type=F32)


NN = ((1,), (0,))
NT = ((1,), (1,))
TN = ((0,), (0,))


def swap(value, axis, bit):
    count = lax.axis_size(axis)
    return lax.ppermute(value, axis, [(i, i ^ bit) for i in range(count)])


def after(value, *others):
    return lax.optimization_barrier((value, *others))[0]


def shifted(value, axis):
    count = lax.axis_size(axis)
    return [
        lax.ppermute(value, axis, [(i, (i + step) % count) for i in range(count)])
        for step in range(1, count)
    ]


def exchange(value, axis, bit):
    return value + swap(value, axis, bit)


def join_kernel(axis, mode, *refs):
    pieces, out_ref = refs[:-1], refs[-1]
    count = len(pieces)
    me = lax.axis_index(axis)
    for step, piece in enumerate(pieces):
        size = piece.shape[1]
        place = (me ^ step) if mode == "xor" else (me - step + count) % count
        out_ref[:, pl.ds(pl.multiple_of(place * size, size), size)] = piece[...]


def join(pieces, axis, mode):
    rows, size = pieces[0].shape
    return pl.pallas_call(
        functools.partial(join_kernel, axis, mode),
        out_shape=jax.ShapeDtypeStruct((rows, size * len(pieces)), pieces[0].dtype),
        cost_estimate=LIGHT,
        name="join",
    )(*pieces)


def gather_gains(gains):
    if lax.axis_size("tensor") > 4 or gains.shape[1] % LANES:
        whole = lax.all_gather(gains, ("tensor", "fsdp"), axis=1, tiled=True).astype(F32)
        return gains, whole
    own = gains.astype(F32)
    part = join([own] + [swap(own, "fsdp", bit) for bit in (1, 2, 3)], "fsdp", "xor")
    return part, join([part] + shifted(part, "tensor"), "tensor", "shift")


def block_totals(blocks):
    count = lax.axis_size("tensor")
    me = lax.axis_index("tensor")
    if count > 4:
        return lax.dynamic_index_in_dim(lax.psum(blocks, "tensor"), me, 1, keepdims=False)

    def pick(place):
        return lax.dynamic_index_in_dim(blocks, place, 1, keepdims=False)

    total = pick(me)
    for step in range(1, count):
        moves = [(i, (i + step) % count) for i in range(count)]
        total = total + lax.ppermute(pick((me + step) % count), "tensor", moves)
    return total


def piece_columns(j, size):
    return pl.ds(pl.multiple_of((lax.axis_index("fsdp") ^ j) * size, size), size)


def swap_halves(block):
    lane = lax.broadcasted_iota(jnp.int32, block.shape, 1)
    up = pltpu.roll(block, LANES - HDIM // 2, 1)
    down = pltpu.roll(block, HDIM // 2, 1)
    return jnp.where((lane & (HDIM - 1)) < HDIM // 2, up, down)


def rope_tables(positions):
    lane = jnp.arange(LANES, dtype=jnp.int32)
    half = lane % (HDIM // 2)
    frequencies = rope_base ** (-2.0 * half.astype(F32) / HDIM)
    angles = positions.astype(F32)[:, None] * frequencies[None, :]
    sign = jnp.where((lane % HDIM) < HDIM // 2, -1.0, 1.0)
    return jnp.cos(angles), jnp.sin(angles) * sign[None, :]


def piece_dot(x_ref, rows, pieces, dims=NN):
    total = None
    for j, piece in enumerate(pieces):
        size = piece.shape[dims[1][0]]
        term = dotf(x_ref[rows, piece_columns(j, size)], piece, dims)
        total = term if total is None else total + term
    return total


def project_kernel(kinds, normalize, x_ref, *refs):
    pieces, (cos_ref, sin_ref, gain_ref), outs = refs[:4], refs[4:7], refs[7:]
    out_ref = outs[0]
    rows, width = out_ref.shape[1:]
    step = pl.program_id(0)
    if normalize:
        normed_ref, scale_ref = outs[1], outs[2]

        @pl.when(step == 0)
        def _():
            for r in range(0, rows, QROWS):
                part = slice(r, r + QROWS)
                stream = x_ref[part, :].astype(F32)
                mean = jnp.sum(stream * stream, axis=1, keepdims=True) / x_ref.shape[1]
                scale = lax.rsqrt(mean + norm_eps)
                scale_ref[part, :] = scale
                normed_ref[part, :] = (stream * scale * gain_ref[...]).astype(BF)

        x_ref = normed_ref
    for index, scale in enumerate(kinds):

        @pl.when(step == index)
        def _():
            for r in range(0, rows, rows):
                part = slice(r, r + rows)
                result = piece_dot(x_ref, part, [piece[0] for piece in pieces])
                for c in range(0, width, LANES):
                    block = result[:, c : c + LANES]
                    if scale:
                        block = block * cos_ref[part, :] + swap_halves(block) * sin_ref[part, :]
                    low = block.astype(BF)
                    if scale and scale != 1.0:
                        low = low * jnp.asarray(scale, BF)
                    out_ref[0, part, c : c + LANES] = low


def project(x, pieces, cos, sin, gain, kinds, first, normalize):
    rows, depth = x.shape
    _, size, width = pieces[0].shape
    flops = 2 * len(kinds) * rows * depth * width
    whole = pl.BlockSpec((rows, depth), lambda i: (0, 0))
    table = pl.BlockSpec((rows, LANES), lambda i: (0, 0))
    out_shape = [jax.ShapeDtypeStruct((len(kinds), rows, width), BF)]
    out_specs = [pl.BlockSpec((1, rows, width), lambda i: (i, 0, 0))]
    if normalize:
        out_shape += [jax.ShapeDtypeStruct((rows, depth), BF), jax.ShapeDtypeStruct((rows, 1), F32)]
        out_specs += [whole, pl.BlockSpec((rows, 1), lambda i: (0, 0))]
    return pl.pallas_call(
        functools.partial(project_kernel, kinds, normalize),
        name="project_kv" if normalize else "project_q",
        grid=(len(kinds),),
        out_shape=out_shape,
        in_specs=[whole]
        + [pl.BlockSpec((1, size, width), lambda i: (i + first, 0, 0))] * 4
        + [table, table, pl.BlockSpec((1, depth), lambda i: (0, 0))],
        out_specs=out_specs,
        compiler_params=pltpu.CompilerParams(vmem_limit_bytes=VMEM_BYTES),
        cost_estimate=LIGHT,
    )(x, *pieces, cos, sin, gain)


def head_mask(block, head):
    lane = lax.broadcasted_iota(jnp.int32, block.shape, 1)
    inside = (lane < HDIM) if head == 0 else (lane >= HDIM)
    return jnp.where(inside, block, jnp.zeros_like(block))


def own_mask(key_count, row0, low_row):
    key = lax.broadcasted_iota(jnp.int32, (key_count, QROWS), 0)
    query = row0 + lax.broadcasted_iota(jnp.int32, (key_count, QROWS), 1)
    return (key >= low_row) & (key <= query)


def peer_mask(key_count, low_row, offset):
    key = lax.broadcasted_iota(jnp.int32, (key_count, QROWS), 0) - offset
    return key >= low_row


def own_forward_kernel(q_ref, k_ref, v_ref, low_ref, out_ref, log_ref):
    rows = q_ref.shape[0]
    v_t = v_ref[...].T
    for r in range(0, rows, QROWS):
        count = r + QROWS
        allowed = own_mask(count, r, low_ref[:, r : r + QROWS])
        keys = k_ref[0:count, :]
        outs = []
        for head in range(LANES // HDIM):
            scores = dotf(keys, head_mask(q_ref[r : r + QROWS, :], head), NT)
            scores = jnp.where(allowed, scores, masked_score)
            peak = jnp.max(scores, axis=0, keepdims=True)
            weights = jnp.exp(scores - peak)
            total = jnp.sum(weights, axis=0, keepdims=True)
            part = dotf(v_t[head * HDIM : (head + 1) * HDIM, 0:count], weights.astype(BF), NN)
            outs.append(part / total)
            log_ref[0, head : head + 1, r : r + QROWS] = peak + jnp.log(total)
        out_ref[r : r + QROWS, :] = jnp.concatenate(outs, axis=0).T


def peer_forward_kernel(
    need_ref, q_ref, k_ref, v_ref, low_ref, part_ref, log_in_ref, out_ref, log_ref
):
    rows = q_ref.shape[0]
    key_count = k_ref.shape[0]
    for index, r in enumerate(range(0, rows, QROWS)):
        needed = need_ref[index] < 0

        @pl.when(needed)
        def _():
            v_t = v_ref[...].T
            allowed = peer_mask(key_count, low_ref[:, r : r + QROWS], key_count)
            before = part_ref[r : r + QROWS, :].T
            outs = []
            for head in range(LANES // HDIM):
                scores = dotf(k_ref[...], head_mask(q_ref[r : r + QROWS, :], head), NT)
                scores = jnp.where(allowed, scores, masked_score)
                log_own = log_in_ref[0, head : head + 1, r : r + QROWS]
                peak = jnp.maximum(jnp.max(scores, axis=0, keepdims=True), log_own)
                weights = jnp.exp(scores - peak)
                own_weight = jnp.exp(log_own - peak)
                total = jnp.sum(weights, axis=0, keepdims=True) + own_weight
                rows_h = slice(head * HDIM, (head + 1) * HDIM)
                part = dotf(v_t[rows_h, :], weights.astype(BF), NN)
                outs.append((part + before[rows_h, :] * own_weight) / total)
                log_ref[0, head : head + 1, r : r + QROWS] = peak + jnp.log(total)
            out_ref[r : r + QROWS, :] = jnp.concatenate(outs, axis=0).T.astype(BF)

        @pl.when(jnp.logical_not(needed))
        def _():
            out_ref[r : r + QROWS, :] = part_ref[r : r + QROWS, :].astype(BF)
            log_ref[:, :, r : r + QROWS] = log_in_ref[:, :, r : r + QROWS]


def pair_spec(rows):
    return pl.BlockSpec((rows, LANES), lambda i: (0, i))


def stacked_spec(rows, part):
    return pl.BlockSpec((None, rows, LANES), lambda i: (part, 0, i))


def log_spec(rows):
    return pl.BlockSpec((1, LANES // HDIM, rows), lambda i: (i, 0, 0))


def low_spec(rows):
    return pl.BlockSpec((1, rows), lambda i: (0, 0))


def own_forward(q, kv, low_row):
    rows, width = q.shape
    pairs = width // LANES
    return pl.pallas_call(
        own_forward_kernel,
        name="own_fwd",
        grid=(pairs,),
        out_shape=(
            jax.ShapeDtypeStruct((rows, width), F32),
            jax.ShapeDtypeStruct((pairs, LANES // HDIM, rows), F32),
        ),
        in_specs=[
            pair_spec(rows),
            stacked_spec(rows, 0),
            stacked_spec(rows, 1),
            low_spec(rows),
        ],
        out_specs=(pair_spec(rows), log_spec(rows)),
        compiler_params=pltpu.CompilerParams(vmem_limit_bytes=VMEM_BYTES),
        cost_estimate=LIGHT,
    )(q, kv, kv, low_row)


SMEM_SPEC = pl.BlockSpec(memory_space=pltpu.SMEM)


def peer_forward(need, q, kv, low_row, part, log_in):
    rows, width = q.shape
    pairs = width // LANES
    return pl.pallas_call(
        peer_forward_kernel,
        name="peer_fwd",
        grid=(pairs,),
        out_shape=(
            jax.ShapeDtypeStruct((rows, width), BF),
            jax.ShapeDtypeStruct((pairs, LANES // HDIM, rows), F32),
        ),
        in_specs=[
            SMEM_SPEC,
            pair_spec(rows),
            stacked_spec(rows, 0),
            stacked_spec(rows, 1),
            low_spec(rows),
            pair_spec(rows),
            log_spec(rows),
        ],
        out_specs=(pair_spec(rows), log_spec(rows)),
        compiler_params=pltpu.CompilerParams(vmem_limit_bytes=VMEM_BYTES),
        cost_estimate=LIGHT,
    )(need, q, kv, kv, low_row, part, log_in)


def backward_block(q_rows, k_rows, v_rows, k_t, do_rows, do_o_t, logs, allowed):
    d_query, d_key, d_value = [], None, None
    for head in range(LANES // HDIM):
        rows_h = slice(head * HDIM, (head + 1) * HDIM)
        q_head = head_mask(q_rows, head)
        do_head = head_mask(do_rows, head)
        scores = dotf(k_rows, q_head, NT)
        probs = jnp.exp(jnp.where(allowed, scores, masked_score) - logs[head])
        delta = jnp.sum(do_o_t[rows_h, :], axis=0, keepdims=True)
        d_probs = dotf(v_rows, do_head, NT)
        d_scores = (probs * (d_probs - delta)).astype(BF)
        d_v = dotf(probs.astype(BF), do_head, NN)
        d_k = dotf(d_scores, q_head, NN)
        d_value = d_v if d_value is None else d_value + d_v
        d_key = d_k if d_key is None else d_key + d_k
        d_query.append(dotf(k_t[rows_h, :], d_scores, NN))
    return jnp.concatenate(d_query, axis=0), d_key, d_value


def output_product(do_ref, o_ref, window):
    product = do_ref[window].astype(F32) * o_ref[window].astype(F32)
    return product.T


def peer_backward_kernel(
    need_ref, q_ref, k_ref, v_ref, do_ref, o_ref, low_ref, log_ref, dq_ref, dkv_ref, sums
):
    rows = q_ref.shape[0]
    key_count = k_ref.shape[0]
    sums[...] = jnp.zeros_like(sums)
    for index, r in enumerate(range(0, rows, QROWS)):
        needed = need_ref[index] < 0
        window = (slice(r, r + QROWS), slice(None))

        @pl.when(needed)
        def _():
            allowed = peer_mask(key_count, low_ref[:, r : r + QROWS], key_count)
            logs = [log_ref[0, h : h + 1, r : r + QROWS] for h in range(LANES // HDIM)]
            d_query, d_key, d_value = backward_block(
                q_ref[window],
                k_ref[...],
                v_ref[...],
                k_ref[...].T,
                do_ref[window],
                output_product(do_ref, o_ref, window),
                logs,
                allowed,
            )
            dq_ref[window] = d_query.T
            sums[0] += d_key
            sums[1] += d_value

        @pl.when(jnp.logical_not(needed))
        def _():
            dq_ref[window] = jnp.zeros((QROWS, LANES), F32)

    dkv_ref[...] = sums[...].astype(BF)


def peer_backward(need, q, kv, do, o, low_row, logs):
    rows, width = q.shape
    pairs = width // LANES
    return pl.pallas_call(
        peer_backward_kernel,
        name="peer_bwd",
        grid=(pairs,),
        out_shape=(
            jax.ShapeDtypeStruct((rows, width), F32),
            jax.ShapeDtypeStruct((2, rows, width), BF),
        ),
        in_specs=[
            SMEM_SPEC,
            pair_spec(rows),
            stacked_spec(rows, 0),
            stacked_spec(rows, 1),
            pair_spec(rows),
            pair_spec(rows),
            low_spec(rows),
            log_spec(rows),
        ],
        out_specs=(pair_spec(rows), pl.BlockSpec((2, rows, LANES), lambda i: (0, 0, i))),
        scratch_shapes=[pltpu.VMEM((2, rows, LANES), F32)],
        compiler_params=pltpu.CompilerParams(vmem_limit_bytes=VMEM_BYTES),
        cost_estimate=LIGHT,
    )(need, q, kv, kv, do, o, low_row, logs)


def own_backward_kernel(
    q_ref,
    k_ref,
    v_ref,
    do_ref,
    o_ref,
    low_ref,
    log_ref,
    dq_in_ref,
    cos_ref,
    sin_ref,
    dq_ref,
    dk_ref,
    dv_ref,
    sums,
):
    rows = q_ref.shape[0]
    sums[...] = jnp.zeros_like(sums)
    k_t = k_ref[...].T
    for r in range(0, rows, QROWS):
        count = r + QROWS
        window = (slice(r, r + QROWS), slice(None))
        allowed = own_mask(count, r, low_ref[:, r : r + QROWS])
        logs = [log_ref[0, h : h + 1, r : r + QROWS] for h in range(LANES // HDIM)]
        d_query, d_key, d_value = backward_block(
            q_ref[window],
            k_ref[0:count, :],
            v_ref[0:count, :],
            k_t[:, 0:count],
            do_ref[window],
            output_product(do_ref, o_ref, window),
            logs,
            allowed,
        )
        rotated = (d_query.T + dq_in_ref[window]) * (HDIM**-0.5)
        turned = rotated * cos_ref[window] - swap_halves(rotated) * sin_ref[window]
        dq_ref[window] = turned.astype(BF)
        sums[0, 0:count] += d_key
        sums[1, 0:count] += d_value
    dk_ref[...] = sums[0]
    dv_ref[...] = sums[1]


def own_backward(q, kv, do, o, low_row, logs, dq_in, cos, sin):
    rows, width = q.shape
    pairs = width // LANES
    table = pl.BlockSpec((rows, LANES), lambda i: (0, 0))
    return pl.pallas_call(
        own_backward_kernel,
        name="own_bwd",
        grid=(pairs,),
        out_shape=(
            jax.ShapeDtypeStruct((rows, width), BF),
            jax.ShapeDtypeStruct((rows, width), F32),
            jax.ShapeDtypeStruct((rows, width), F32),
        ),
        in_specs=[
            pair_spec(rows),
            stacked_spec(rows, 0),
            stacked_spec(rows, 1),
            pair_spec(rows),
            pair_spec(rows),
            low_spec(rows),
            log_spec(rows),
            pair_spec(rows),
            table,
            table,
        ],
        out_specs=(pair_spec(rows),) * 3,
        scratch_shapes=[pltpu.VMEM((2, rows, LANES), F32)],
        compiler_params=pltpu.CompilerParams(vmem_limit_bytes=VMEM_BYTES),
        cost_estimate=LIGHT,
    )(q, kv, kv, do, o, low_row, logs, dq_in, cos, sin)


def finish_keys_kernel(dk_ref, dv_ref, dk_in_ref, dv_in_ref, cos_ref, sin_ref, dk_out, dv_out):
    total = dk_ref[...] + dk_in_ref[...].astype(F32)
    turned = total * cos_ref[...] - swap_halves(total) * sin_ref[...]
    dk_out[...] = turned.astype(BF)
    dv_out[...] = (dv_ref[...] + dv_in_ref[...].astype(F32)).astype(BF)


def finish_keys(dk, dv, dkv_in, cos, sin):
    rows, width = dk.shape
    pairs = width // LANES
    table = pl.BlockSpec((rows, LANES), lambda i: (0, 0))
    return pl.pallas_call(
        finish_keys_kernel,
        name="finish_keys",
        grid=(pairs,),
        out_shape=(jax.ShapeDtypeStruct((rows, width), BF),) * 2,
        in_specs=[pair_spec(rows), pair_spec(rows), stacked_spec(rows, 0), stacked_spec(rows, 1)]
        + [table, table],
        out_specs=(pair_spec(rows),) * 2,
        cost_estimate=LIGHT,
    )(dk, dv, dkv_in, dkv_in, cos, sin)


def branch_kernel(stream_ref, att_ref, gain_ref, *refs):
    pieces, (hidden_ref, normed_ref, scale_ref) = refs[:4], refs[4:]
    for j, piece in enumerate(pieces):
        columns = piece_columns(j, piece.shape[1])
        term = dotf(att_ref[...], piece[...], NN)
        hidden_ref[:, columns] = stream_ref[:, columns].astype(F32) + term
    hidden = hidden_ref[...]
    mean = jnp.sum(hidden * hidden, axis=1, keepdims=True) / hidden.shape[1]
    scale = lax.rsqrt(mean + norm_eps)
    scale_ref[...] = scale
    normed_ref[...] = (hidden * scale * gain_ref[...]).astype(BF)


def add_branch(stream, att, gain, pieces):
    rows, depth = stream.shape
    heads = att.shape[1]
    tile = pl.BlockSpec((QROWS, depth), lambda i: (i, 0))
    return pl.pallas_call(
        branch_kernel,
        name="branch",
        grid=(rows // QROWS,),
        out_shape=(
            jax.ShapeDtypeStruct((rows, depth), F32),
            jax.ShapeDtypeStruct((rows, depth), BF),
            jax.ShapeDtypeStruct((rows, 1), F32),
        ),
        in_specs=[
            tile,
            pl.BlockSpec((QROWS, heads), lambda i: (i, 0)),
            pl.BlockSpec((1, depth), lambda i: (0, 0)),
        ]
        + [pl.BlockSpec(pieces[0].shape, lambda i: (0, 0))] * 4,
        out_specs=(tile, tile, pl.BlockSpec((QROWS, 1), lambda i: (i, 0))),
        compiler_params=pltpu.CompilerParams(vmem_limit_bytes=VMEM_BYTES),
        cost_estimate=LIGHT,
    )(stream, att, gain, *pieces)


def hidden_kernel(x_ref, *refs):
    w_in, (act_ref, by_gate_ref, by_up_ref) = refs[:4], refs[4:]
    rows = x_ref.shape[0]
    for r in range(0, rows, rows):
        part = slice(r, r + rows)
        gate = piece_dot(x_ref, part, [piece[0] for piece in w_in])
        up = piece_dot(x_ref, part, [piece[1] for piece in w_in])
        sig = jax.nn.sigmoid(gate)
        silu = gate * sig
        act_ref[part, :] = (silu * up).astype(BF)
        by_gate_ref[part, :] = (up * sig * (1.0 + gate * (1.0 - sig))).astype(BF)
        by_up_ref[part, :] = silu.astype(BF)


def hidden_units(x, w_in):
    rows, depth = x.shape
    _, size, units = w_in[0].shape
    tile = 256
    part = pl.BlockSpec((rows, tile), lambda i: (0, i))
    return pl.pallas_call(
        hidden_kernel,
        grid=(units // tile,),
        out_shape=(jax.ShapeDtypeStruct((rows, units), BF),) * 3,
        in_specs=[pl.BlockSpec((rows, depth), lambda i: (0, 0))]
        + [pl.BlockSpec((2, size, tile), lambda i: (0, 0, i))] * 4,
        out_specs=(part,) * 3,
        compiler_params=pltpu.CompilerParams(vmem_limit_bytes=VMEM_BYTES),
        cost_estimate=LIGHT,
        name="hidden",
    )(x, *w_in)


def hidden_back_kernel(cot_ref, by_gate_ref, by_up_ref, *refs):
    w_down, (dg_ref, du_ref) = refs[:4], refs[4:]
    rows = cot_ref.shape[0]
    for r in range(0, rows, rows):
        part = slice(r, r + rows)
        d_act = piece_dot(cot_ref, part, [piece[...] for piece in w_down], NT)
        dg_ref[part, :] = (d_act * by_gate_ref[part, :].astype(F32)).astype(BF)
        du_ref[part, :] = (d_act * by_up_ref[part, :].astype(F32)).astype(BF)


def hidden_back(cot, by_gate, by_up, w_down):
    rows, depth = cot.shape
    units, size = w_down[0].shape
    tile = 256
    part = pl.BlockSpec((rows, tile), lambda i: (0, i))
    return pl.pallas_call(
        hidden_back_kernel,
        grid=(units // tile,),
        out_shape=(jax.ShapeDtypeStruct((rows, units), BF),) * 2,
        in_specs=[pl.BlockSpec((rows, depth), lambda i: (0, 0)), part, part]
        + [pl.BlockSpec((tile, size), lambda i: (i, 0))] * 4,
        out_specs=(part,) * 2,
        compiler_params=pltpu.CompilerParams(vmem_limit_bytes=VMEM_BYTES),
        cost_estimate=LIGHT,
        name="hidden_back",
    )(cot, by_gate, by_up, *w_down)


def phased(i, block, make_index, tiles):
    def index_map(j, t):
        return make_index(jnp.where(j < i, 0, jnp.where(j == i, t, tiles - 1)))

    return pl.BlockSpec(block, index_map)


def columns_call(kernel_dot, lefts, pieces, block, make_index, size, flops, name):
    rows = lefts[0].shape[0]
    tile = min(size, 256)
    tiles = size // tile
    depth = size * 4

    def kernel(*refs):
        left_refs, piece_refs, out_ref = refs[: len(lefts)], refs[len(lefts) : -1], refs[-1]
        for j, piece in enumerate(piece_refs):

            @pl.when(pl.program_id(0) == j)
            def _():
                out_ref[...] = kernel_dot([left[...] for left in left_refs], piece).astype(BF)

    def out_index(j, t):
        return (0, (lax.axis_index("fsdp") ^ j) * tiles + t)

    return pl.pallas_call(
        kernel,
        grid=(4, tiles),
        out_shape=jax.ShapeDtypeStruct((rows, depth), BF),
        in_specs=[pl.BlockSpec(left.shape, lambda j, t: (0, 0)) for left in lefts]
        + [phased(i, block(tile), make_index, tiles) for i in range(4)],
        out_specs=pl.BlockSpec((rows, tile), out_index),
        compiler_params=pltpu.CompilerParams(vmem_limit_bytes=VMEM_BYTES),
        cost_estimate=LIGHT,
        name=name,
    )(*lefts, *pieces)


def stacked_columns(lefts, pieces, name):
    count, size, inner = pieces[0].shape

    def product(parts, piece):
        return sum(dotf(parts[c], piece[c], NT) for c in range(count))

    return columns_call(
        product,
        lefts,
        pieces,
        lambda tile: (count, tile, inner),
        lambda t: (0, t, 0),
        size,
        8 * lefts[0].shape[0] * size * inner * count,
        name,
    )


def plain_columns(left, pieces, name):
    inner, size = pieces[0].shape
    return columns_call(
        lambda parts, piece: dotf(parts[0], piece[...], NN),
        [left],
        pieces,
        lambda tile: (inner, tile),
        lambda t: (0, t),
        size,
        8 * left.shape[0] * size * inner,
        name,
    )


def branch_back_kernel(
    tensor_index_ref, d_mid_ref, hidden_ref, cot_ref, scale_ref, gain_ref, *refs
):
    pieces, (d_own_ref, d_branch_ref, d_att_ref, gain_out_ref) = refs[:4], refs[4:8]
    d_mid = d_mid_ref[...].astype(F32)
    hidden = hidden_ref[...]
    scale = scale_ref[...]
    weighted = d_mid * gain_ref[...]
    inner = jnp.sum(weighted * hidden, axis=1, keepdims=True) / hidden.shape[1]
    d_hidden = (
        cot_ref[...].astype(F32) + scale * weighted - hidden * (scale * scale * scale * inner)
    )
    gain_term = jnp.sum(d_mid * hidden * scale, axis=0, keepdims=True)

    @pl.when(pl.program_id(0) == 0)
    def _():
        gain_out_ref[...] = gain_term

    @pl.when(pl.program_id(0) != 0)
    def _():
        gain_out_ref[...] += gain_term

    d_branch_ref[...] = d_hidden.astype(BF)
    width = d_own_ref.shape[1]
    for z in range(hidden.shape[1] // width):

        @pl.when(tensor_index_ref[0] == z)
        def _():
            d_own_ref[...] = d_hidden[:, z * width : (z + 1) * width]

    d_att_ref[...] = piece_dot(
        d_branch_ref, slice(None), [piece[...] for piece in pieces], NT
    ).astype(BF)


def branch_back(tensor_index, d_mid, hidden, cot, scale, gain, pieces, own_width):
    rows, depth = hidden.shape
    heads, size = pieces[0].shape[0] // (depth // own_width), pieces[0].shape[1]
    tile = pl.BlockSpec((QROWS, depth), lambda i, s: (i, 0))
    row = pl.BlockSpec((1, depth), lambda i, s: (0, 0))
    own = pl.BlockSpec((QROWS, own_width), lambda i, s: (i, 0))
    return pl.pallas_call(
        branch_back_kernel,
        name="branch_back",
        grid_spec=pltpu.PrefetchScalarGridSpec(
            num_scalar_prefetch=1,
            grid=(rows // QROWS,),
            in_specs=[tile, tile, tile, pl.BlockSpec((QROWS, 1), lambda i, s: (i, 0)), row]
            + [pl.BlockSpec((heads, size), lambda i, s: (s[0], 0))] * 4,
            out_specs=(own, tile, pl.BlockSpec((QROWS, heads), lambda i, s: (i, 0)), row),
        ),
        out_shape=(
            jax.ShapeDtypeStruct((rows, own_width), F32),
            jax.ShapeDtypeStruct((rows, depth), BF),
            jax.ShapeDtypeStruct((rows, heads), BF),
            jax.ShapeDtypeStruct((1, depth), F32),
        ),
        compiler_params=pltpu.CompilerParams(vmem_limit_bytes=VMEM_BYTES),
        cost_estimate=LIGHT,
    )(tensor_index, d_mid, hidden, cot, scale, gain, *pieces)


def grad_call(left, right, cut, place, adds, name, span=(0, 1)):
    rows = left.shape[0]
    size = (left, right)[cut].shape[1] // 4
    swept = (right, left)[cut].shape[1] // span[1]
    height, width = (size, swept) if cut == 0 else (swept, size)
    tile = min(1024, swept)
    offset = span[0] * (swept // tile)
    block = (height, tile) if cut == 0 else (tile, width)

    def owner():
        return lax.axis_index("fsdp") ^ place

    def swept_index(t):
        return (0, t) if cut == 0 else (t, 0)

    def kernel(left_ref, right_ref, *refs):
        add_refs, out_ref = refs[: len(adds)], refs[len(adds)]
        if cut == 0:
            turned = refs[-1]

            @pl.when(pl.program_id(0) == 0)
            def _():
                turned[...] = left_ref[...].T

            result = dotf(turned[...], right_ref[...], NN)
        else:
            result = dotf(left_ref[...].T, right_ref[...], NN)
        for add in add_refs:
            result = result + add[...].astype(F32)
        out_ref[...] = result.astype(BF)

    fixed = pl.BlockSpec((rows, size), lambda t: (0, owner()))
    moving = pl.BlockSpec((rows, tile), lambda t: (0, t + offset))
    return pl.pallas_call(
        kernel,
        grid=(swept // tile,),
        out_shape=jax.ShapeDtypeStruct((height, width), BF),
        in_specs=[fixed, moving] * (cut == 0)
        + [moving, fixed] * (cut == 1)
        + [pl.BlockSpec(block, swept_index)] * len(adds),
        out_specs=pl.BlockSpec(block, swept_index),
        scratch_shapes=[pltpu.VMEM((size, rows), BF)] if cut == 0 else [],
        compiler_params=pltpu.CompilerParams(vmem_limit_bytes=VMEM_BYTES),
        cost_estimate=LIGHT,
        name=name,
    )(left, right, *adds)


class Reduction:
    def __init__(self, left, right, cut, name, span=(0, 1)):
        self.args, self.name, self.span = (left, right, cut), name, span

    def call(self, place, deps, step, adds=()):
        left, right, cut = self.args
        left = after(left, *deps) if deps else left
        return grad_call(left, right, cut, place, adds, self.name + step, self.span)

    def near_far(self, *deps):
        self.three = self.call(3, deps, "_3")
        self.for_two = swap(self.three, "fsdp", 1)

    def near(self, *deps):
        self.one = self.call(1, deps, "_1")
        self.for_own = swap(self.one, "fsdp", 1)

    def far(self, *deps):
        self.two = self.call(2, deps, "_2", [self.for_two])

    def send_far(self, *deps):
        self.across = swap(after(self.two, *deps), "fsdp", 2)

    def mine(self, *deps):
        self.own = self.call(0, deps, "_0", [self.for_own, self.across])

    def send_context(self, *deps):
        self.other = swap(after(self.own, *deps), "context", 1)


def totals_kernel(slots, *refs):
    pairs, out_ref = refs[:-1], refs[-1]
    for slot in range(len(pairs) // 2):
        total = pairs[2 * slot][...].astype(F32) + pairs[2 * slot + 1][...].astype(F32)
        if slots == 0:
            out_ref[slot] = total
        else:
            out_ref[:, slot, :] = total


def totals(sums, slots, *deps):
    arrays = [array for part in sums for array in (part.own, part.other)]
    if deps:
        arrays[0] = after(arrays[0], *deps)
    rows, width = arrays[0].shape
    tile = 128
    shape = [rows, width]
    shape.insert(slots, len(sums))
    block = [tile, width]
    block.insert(slots, len(sums))
    return pl.pallas_call(
        functools.partial(totals_kernel, slots),
        grid=(rows // tile,),
        out_shape=jax.ShapeDtypeStruct(tuple(shape), F32),
        in_specs=[pl.BlockSpec((tile, width), lambda i: (i, 0))] * len(arrays),
        out_specs=pl.BlockSpec(
            tuple(block), (lambda i: (0, i, 0)) if slots == 0 else (lambda i: (i, 0, 0))
        ),
        compiler_params=pltpu.CompilerParams(vmem_limit_bytes=VMEM_BYTES),
        cost_estimate=LIGHT,
        name="totals",
    )(*arrays)


def row_sum(values_in):
    return jnp.sum(values_in, axis=1, keepdims=True)


def per_device(tokens, w_qkv, w_out, w_gate_up, w_down, gains, seq_lengths, cotangent):
    row_count, part_width = tokens.shape
    tensor_index = lax.axis_index("tensor")
    context_index = lax.axis_index("context")
    full_width = part_width * lax.axis_size("tensor")

    def features(part_in):
        return lax.all_gather(part_in, "tensor", axis=1, tiled=True)

    def feature_sum(term):
        return lax.psum_scatter(term.astype(BF), "tensor", scatter_dimension=1, tiled=True)

    def own_features(full):
        return lax.dynamic_slice_in_dim(full, tensor_index * part_width, part_width, 1)

    ending = jnp.cumsum(seq_lengths[0])
    starts = ending - seq_lengths[0]
    places = context_index * row_count + jnp.arange(row_count, dtype=jnp.int32)
    first_token = jnp.max(jnp.where(starts[None, :] <= places[:, None], starts[None, :], 0), axis=1)
    cos, sin = rope_tables(places - first_token)
    low = first_token - context_index * row_count
    low_row = low[None, :]
    need = low[::QROWS]

    token_low = features(tokens)
    gain_near, gain_full = gather_gains(gains)
    gain_attn, gain_mlp = gain_full[0:1], gain_full[1:2]

    qkv_own = jnp.swapaxes(w_qkv, 0, 1)
    half = qkv_own.shape[1] // 2
    far_half = swap(
        lax.dynamic_slice_in_dim(after(qkv_own, gain_near), context_index * half, half, 1),
        "fsdp",
        2,
    )
    other_half = swap(far_half, "context", 1)
    qkv_far = jnp.where(
        context_index == 0,
        jnp.concatenate([far_half, other_half], axis=1),
        jnp.concatenate([other_half, far_half], axis=1),
    )
    qkv_near = swap(qkv_own, "fsdp", 1)
    qkv = (qkv_own, qkv_near, qkv_far, swap(qkv_far, "fsdp", 1))

    gate_up_own = jnp.swapaxes(w_gate_up, 0, 1)
    cut = gate_up_own.shape[1] * 19 // 32
    gate_up_a = swap(after(gate_up_own[:, :cut], far_half), "fsdp", 2)
    gate_up_b = swap(after(gate_up_own[:, cut:], gate_up_a), "fsdp", 2)

    keys_values, normed_in, scale_attn = project(
        after(token_low, gate_up_a), qkv, cos, sin, gain_attn, (1.0, None), 1, True
    )
    peer_kv = lax.ppermute(keys_values, "context", [(0, 1)])
    queries = project(normed_in, qkv, cos, sin, gain_attn, (HDIM**-0.5,), 0, False)[0][0]
    part, part_log = own_forward(queries, keys_values, low_row)
    attended, logs = peer_forward(
        need, queries, peer_kv, low_row, after(part, gate_up_b), part_log
    )
    attended_full = features(attended)

    out_own = after(lax.all_gather(w_out, "tensor", axis=0, tiled=True), attended)
    out_far = swap(out_own, "fsdp", 2)
    out = (out_own, swap(out_own, "fsdp", 1), out_far, swap(out_far, "fsdp", 1))
    gate_up_own, gate_up_a, gate_up_b = lax.optimization_barrier(
        (gate_up_own, gate_up_a, gate_up_b, attended)
    )[:3]
    gate_up_far = jnp.concatenate([gate_up_a, gate_up_b], axis=1)
    gate_up_near = swap(gate_up_own, "fsdp", 1)
    gate_up = (gate_up_own, gate_up_near, gate_up_far, swap(gate_up_far, "fsdp", 1))
    cot_full = features(after(cotangent, attended_full))
    down_far = swap(after(w_down, attended_full), "fsdp", 2)
    down_near = swap(after(w_down, attended_full), "fsdp", 1)
    hidden, normed_mid, scale_mlp = add_branch(token_low, attended_full, gain_mlp, out)

    activated, by_gate, by_up = hidden_units(normed_mid, gate_up)
    down_far = after(down_far, activated)
    down = (w_down, down_near, down_far, swap(down_far, "fsdp", 1))
    d_gate, d_up = hidden_back(cot_full, by_gate, by_up, down)
    d_mid_term = stacked_columns([d_gate, d_up], gate_up, "d_mid")
    d_mid_part = feature_sum(d_mid_term)

    down_a, down_b = (
        Reduction(activated, cot_full, 1, "grad_down", (part_index, 2)) for part_index in (0, 1)
    )
    grad_gate = Reduction(normed_mid, d_gate, 0, "grad_gate")
    grad_up = Reduction(normed_mid, d_up, 0, "grad_up")
    down_a.near_far(d_mid_term)
    down_b.near_far(down_a.three)
    grad_gate.near_far(down_b.three)
    down_a.far(grad_gate.three)
    down_a.send_far()
    down_b.far(down_a.two)
    d_mid_part = after(d_mid_part, down_a.across, down_b.two)
    d_mid = features(d_mid_part)
    down_b.send_far(down_a.across)
    down_a.near(down_b.two)
    down_b.near(down_a.one)
    down_a.mine(down_b.one)
    down_a.send_context()
    grad_gate.near(down_a.own)
    grad_gate.far(grad_gate.one)
    grad_gate.send_far(down_b.across)
    down_b.mine(grad_gate.two)
    down_b.send_context(down_a.other)
    grad_up.near_far(down_b.own)
    grad_up.near(grad_up.three)
    grad_up.far(grad_up.one)
    mlp_term = plain_columns(after(activated, grad_up.two), down, "mlp_out")

    d_hidden_own, d_branch, d_attended, gain_mlp_term = branch_back(
        tensor_index[None],
        after(d_mid, mlp_term, down_b.own),
        hidden,
        cot_full,
        scale_mlp,
        gain_mlp,
        out,
        part_width,
    )
    mlp_out = feature_sum(after(mlp_term, d_branch)).astype(F32)
    dq_peer, dkv_peer = peer_backward(
        need, queries, peer_kv, d_attended, attended, low_row, logs
    )
    dkv_in = lax.ppermute(dkv_peer, "context", [(1, 0)])
    d_query, dk_own, dv_own = own_backward(
        queries, keys_values, d_attended, attended, low_row, logs, dq_peer, cos, sin
    )
    grad_out = Reduction(attended, d_branch, 1, "grad_out")
    grad_query = Reduction(normed_in, d_query, 0, "grad_query")
    grad_gate.mine(d_query)
    grad_gate.send_context(down_b.other)
    grad_up.send_far(grad_gate.across)
    grad_out.near_far(grad_gate.own)
    grad_query.near_far(grad_out.three)
    grad_out.near(grad_query.three)
    grad_query.near(grad_out.one)
    grad_out.far(grad_query.one)
    grad_query.far(grad_out.two)
    d_key, d_value = finish_keys(dk_own, dv_own, after(dkv_in, grad_query.two), cos, sin)
    d_in_term = stacked_columns([d_query, d_key, d_value], qkv, "d_in")
    d_in = feature_sum(d_in_term).astype(F32)

    grad_out.send_far(grad_up.across)
    grad_query.send_far(grad_up.across)
    grad_key = Reduction(normed_in, d_key, 0, "grad_key")
    grad_value = Reduction(normed_in, d_value, 0, "grad_value")
    grad_key.near_far(d_in_term)
    grad_value.near_far(grad_key.three)
    grad_key.near(grad_value.three)
    grad_value.near(grad_key.one)
    grad_key.far(grad_value.one)
    grad_value.far(grad_key.two)
    grad_key.send_far(grad_query.across)
    grad_value.send_far(grad_query.across)
    grad_up.mine(grad_value.two)
    grad_up.send_context(grad_gate.other)

    stream = token_low.astype(F32)
    d_in_wide = after(d_in_term, grad_up.own).astype(F32)
    weighted = d_in_wide * stream
    inner_term = jnp.sum(weighted * gain_attn, axis=1)
    gain_attn_term = jnp.sum(weighted * scale_attn, axis=0)
    parts = lax.axis_size("tensor")
    totals_small = block_totals(
        jnp.concatenate(
            [
                jnp.broadcast_to(inner_term[None, :], (parts, row_count)),
                gain_attn_term.reshape(parts, part_width),
            ],
            axis=1,
        )[None]
    )
    inner_in = totals_small[0, :row_count][:, None] / full_width
    gain_sums = jnp.concatenate(
        [totals_small[:, row_count:], own_features(gain_mlp_term)], axis=0
    )
    gain_sums = exchange(gain_sums, "fsdp", 1)
    gain_sums = exchange(gain_sums, "fsdp", 2)
    gain_sums = exchange(gain_sums, "context", 1)
    gain_width = gains.shape[1]
    grad_gains = lax.dynamic_slice_in_dim(
        gain_sums, lax.axis_index("fsdp") * gain_width, gain_width, 1
    )

    grad_out.mine(d_in_wide)
    grad_query.mine(grad_out.own)
    grad_out.send_context()
    grad_query.send_context()
    grad_down_sum = totals([down_a, down_b], 0, grad_query.own).reshape(w_down.shape)
    grad_key.mine(grad_down_sum, d_in)
    grad_value.mine(grad_key.own)
    grad_key.send_context()
    grad_value.send_context()
    grad_gate_up_sum = totals([grad_gate, grad_up], 1, grad_value.own)
    grad_out_sum = totals([grad_out], 0, grad_gate_up_sum)[0]
    grad_qkv = totals([grad_query, grad_key, grad_value], 0, grad_out_sum)

    block_out = (own_features(hidden) + mlp_out).astype(BF)
    own_tokens = tokens.astype(F32)
    grad_tokens = (
        d_hidden_own
        + scale_attn * own_features(gain_attn) * d_in
        - own_tokens * scale_attn * scale_attn * scale_attn * inner_in
    ).astype(BF)
    return (
        block_out,
        grad_tokens,
        jnp.swapaxes(grad_qkv, 0, 1),
        grad_out_sum,
        grad_gate_up_sum,
        grad_down_sum,
        grad_gains,
    )


def solution(mesh):
    rows = P(("fsdp", "context"), "tensor")
    inner = P("fsdp", None, "tensor")
    outer = P("tensor", "fsdp")
    gain = P(None, ("tensor", "fsdp"))
    return jax.shard_map(
        per_device,
        mesh=mesh,
        in_specs=(rows, inner, outer, inner, outer, gain, P("fsdp", None), rows),
        out_specs=(rows, rows, inner, outer, inner, outer, gain),
        check_vma=False,
    )
```

```python
import functools

import jax
import jax.numpy as jnp
from jax import lax
from jax.experimental import pallas as pl
from jax.experimental.pallas import tpu as pltpu
from jax.sharding import PartitionSpec as P

HDIM = 64
LANES = 128
QROWS = 256
norm_eps = 1e-05
rope_base = 130000.0
masked_score = -1e30
BF = jnp.bfloat16
F32 = jnp.float32
VMEM_BYTES = 56 * 1024 * 1024
LIGHT = pl.CostEstimate(flops=1, bytes_accessed=1, transcendentals=0)


def dotf(a, b, dims):
    return lax.dot_general(a, b, (dims, ((), ())), preferred_element_type=F32)


NN = ((1,), (0,))
NT = ((1,), (1,))
TN = ((0,), (0,))


def swap(value, axis, bit):
    count = lax.axis_size(axis)
    return lax.ppermute(value, axis, [(i, i ^ bit) for i in range(count)])


def after(value, *others):
    return lax.optimization_barrier((value, *others))[0]


def shifted(value, axis):
    count = lax.axis_size(axis)
    return [
        lax.ppermute(value, axis, [(i, (i + step) % count) for i in range(count)])
        for step in range(1, count)
    ]


def exchange(value, axis, bit):
    return value + swap(value, axis, bit)


def join_kernel(axis, mode, *refs):
    pieces, out_ref = refs[:-1], refs[-1]
    count = len(pieces)
    me = lax.axis_index(axis)
    for step, piece in enumerate(pieces):
        size = piece.shape[1]
        place = (me ^ step) if mode == "xor" else (me - step + count) % count
        out_ref[:, pl.ds(pl.multiple_of(place * size, size), size)] = piece[...]


def join(pieces, axis, mode):
    rows, size = pieces[0].shape
    return pl.pallas_call(
        functools.partial(join_kernel, axis, mode),
        out_shape=jax.ShapeDtypeStruct((rows, size * len(pieces)), pieces[0].dtype),
        cost_estimate=LIGHT,
        name="join",
    )(*pieces)


def gather_gains(gains):
    if lax.axis_size("tensor") > 4 or gains.shape[1] % LANES:
        whole = lax.all_gather(gains, ("tensor", "fsdp"), axis=1, tiled=True).astype(F32)
        return gains, whole
    own = gains.astype(F32)
    part = join([own] + [swap(own, "fsdp", bit) for bit in (1, 2, 3)], "fsdp", "xor")
    return part, join([part] + shifted(part, "tensor"), "tensor", "shift")


def block_totals(blocks):
    count = lax.axis_size("tensor")
    me = lax.axis_index("tensor")
    if count > 4:
        return lax.dynamic_index_in_dim(lax.psum(blocks, "tensor"), me, 1, keepdims=False)

    def pick(place):
        return lax.dynamic_index_in_dim(blocks, place, 1, keepdims=False)

    total = pick(me)
    for step in range(1, count):
        moves = [(i, (i + step) % count) for i in range(count)]
        total = total + lax.ppermute(pick((me + step) % count), "tensor", moves)
    return total


def piece_columns(j, size):
    return pl.ds(pl.multiple_of((lax.axis_index("fsdp") ^ j) * size, size), size)


def swap_halves(block):
    lane = lax.broadcasted_iota(jnp.int32, block.shape, 1)
    up = pltpu.roll(block, LANES - HDIM // 2, 1)
    down = pltpu.roll(block, HDIM // 2, 1)
    return jnp.where((lane & (HDIM - 1)) < HDIM // 2, up, down)


def rope_tables(positions):
    lane = jnp.arange(LANES, dtype=jnp.int32)
    half = lane % (HDIM // 2)
    frequencies = rope_base ** (-2.0 * half.astype(F32) / HDIM)
    angles = positions.astype(F32)[:, None] * frequencies[None, :]
    sign = jnp.where((lane % HDIM) < HDIM // 2, -1.0, 1.0)
    return jnp.cos(angles), jnp.sin(angles) * sign[None, :]


def piece_dot(x_ref, rows, pieces, dims=NN):
    total = None
    for j, piece in enumerate(pieces):
        size = piece.shape[dims[1][0]]
        term = dotf(x_ref[rows, piece_columns(j, size)], piece, dims)
        total = term if total is None else total + term
    return total


def project_kernel(kinds, normalize, x_ref, *refs):
    pieces, (cos_ref, sin_ref, gain_ref), outs = refs[:4], refs[4:7], refs[7:]
    out_ref = outs[0]
    rows, width = out_ref.shape[1:]
    step = pl.program_id(0)
    if normalize:
        normed_ref, scale_ref = outs[1], outs[2]

        @pl.when(step == 0)
        def _():
            for r in range(0, rows, QROWS):
                part = slice(r, r + QROWS)
                stream = x_ref[part, :].astype(F32)
                mean = jnp.sum(stream * stream, axis=1, keepdims=True) / x_ref.shape[1]
                scale = lax.rsqrt(mean + norm_eps)
                scale_ref[part, :] = scale
                normed_ref[part, :] = (stream * scale * gain_ref[...]).astype(BF)

        x_ref = normed_ref
    for index, scale in enumerate(kinds):

        @pl.when(step == index)
        def _():
            for r in range(0, rows, rows):
                part = slice(r, r + rows)
                result = piece_dot(x_ref, part, [piece[0] for piece in pieces])
                for c in range(0, width, LANES):
                    block = result[:, c : c + LANES]
                    if scale:
                        block = block * cos_ref[part, :] + swap_halves(block) * sin_ref[part, :]
                    low = block.astype(BF)
                    if scale and scale != 1.0:
                        low = low * jnp.asarray(scale, BF)
                    out_ref[0, part, c : c + LANES] = low


def project(x, pieces, cos, sin, gain, kinds, first, normalize):
    rows, depth = x.shape
    _, size, width = pieces[0].shape
    flops = 2 * len(kinds) * rows * depth * width
    whole = pl.BlockSpec((rows, depth), lambda i: (0, 0))
    table = pl.BlockSpec((rows, LANES), lambda i: (0, 0))
    out_shape = [jax.ShapeDtypeStruct((len(kinds), rows, width), BF)]
    out_specs = [pl.BlockSpec((1, rows, width), lambda i: (i, 0, 0))]
    if normalize:
        out_shape += [jax.ShapeDtypeStruct((rows, depth), BF), jax.ShapeDtypeStruct((rows, 1), F32)]
        out_specs += [whole, pl.BlockSpec((rows, 1), lambda i: (0, 0))]
    return pl.pallas_call(
        functools.partial(project_kernel, kinds, normalize),
        name="project_kv" if normalize else "project_q",
        grid=(len(kinds),),
        out_shape=out_shape,
        in_specs=[whole]
        + [pl.BlockSpec((1, size, width), lambda i: (i + first, 0, 0))] * 4
        + [table, table, pl.BlockSpec((1, depth), lambda i: (0, 0))],
        out_specs=out_specs,
        compiler_params=pltpu.CompilerParams(vmem_limit_bytes=VMEM_BYTES),
        cost_estimate=LIGHT,
    )(x, *pieces, cos, sin, gain)


def head_mask(block, head):
    lane = lax.broadcasted_iota(jnp.int32, block.shape, 1)
    inside = (lane < HDIM) if head == 0 else (lane >= HDIM)
    return jnp.where(inside, block, jnp.zeros_like(block))


def own_mask(key_count, row0, low_row):
    key = lax.broadcasted_iota(jnp.int32, (key_count, QROWS), 0)
    query = row0 + lax.broadcasted_iota(jnp.int32, (key_count, QROWS), 1)
    return (key >= low_row) & (key <= query)


def peer_mask(key_count, low_row, offset):
    key = lax.broadcasted_iota(jnp.int32, (key_count, QROWS), 0) - offset
    return key >= low_row


def own_forward_kernel(q_ref, k_ref, v_ref, low_ref, out_ref, log_ref):
    rows = q_ref.shape[0]
    v_t = v_ref[...].T
    for r in range(0, rows, QROWS):
        count = r + QROWS
        allowed = own_mask(count, r, low_ref[:, r : r + QROWS])
        keys = k_ref[0:count, :]
        outs = []
        for head in range(LANES // HDIM):
            scores = dotf(keys, head_mask(q_ref[r : r + QROWS, :], head), NT)
            scores = jnp.where(allowed, scores, masked_score)
            peak = jnp.max(scores, axis=0, keepdims=True)
            weights = jnp.exp(scores - peak)
            total = jnp.sum(weights, axis=0, keepdims=True)
            part = dotf(v_t[head * HDIM : (head + 1) * HDIM, 0:count], weights.astype(BF), NN)
            outs.append(part / total)
            log_ref[0, head : head + 1, r : r + QROWS] = peak + jnp.log(total)
        out_ref[r : r + QROWS, :] = jnp.concatenate(outs, axis=0).T


def peer_forward_kernel(
    need_ref, q_ref, k_ref, v_ref, low_ref, part_ref, log_in_ref, out_ref, log_ref
):
    rows = q_ref.shape[0]
    key_count = k_ref.shape[0]
    for index, r in enumerate(range(0, rows, QROWS)):
        needed = need_ref[index] < 0

        @pl.when(needed)
        def _():
            v_t = v_ref[...].T
            allowed = peer_mask(key_count, low_ref[:, r : r + QROWS], key_count)
            before = part_ref[r : r + QROWS, :].T
            outs = []
            for head in range(LANES // HDIM):
                scores = dotf(k_ref[...], head_mask(q_ref[r : r + QROWS, :], head), NT)
                scores = jnp.where(allowed, scores, masked_score)
                log_own = log_in_ref[0, head : head + 1, r : r + QROWS]
                peak = jnp.maximum(jnp.max(scores, axis=0, keepdims=True), log_own)
                weights = jnp.exp(scores - peak)
                own_weight = jnp.exp(log_own - peak)
                total = jnp.sum(weights, axis=0, keepdims=True) + own_weight
                rows_h = slice(head * HDIM, (head + 1) * HDIM)
                part = dotf(v_t[rows_h, :], weights.astype(BF), NN)
                outs.append((part + before[rows_h, :] * own_weight) / total)
                log_ref[0, head : head + 1, r : r + QROWS] = peak + jnp.log(total)
            out_ref[r : r + QROWS, :] = jnp.concatenate(outs, axis=0).T.astype(BF)

        @pl.when(jnp.logical_not(needed))
        def _():
            out_ref[r : r + QROWS, :] = part_ref[r : r + QROWS, :].astype(BF)
            log_ref[:, :, r : r + QROWS] = log_in_ref[:, :, r : r + QROWS]


def pair_spec(rows):
    return pl.BlockSpec((rows, LANES), lambda i: (0, i))


def stacked_spec(rows, part):
    return pl.BlockSpec((None, rows, LANES), lambda i: (part, 0, i))


def log_spec(rows):
    return pl.BlockSpec((1, LANES // HDIM, rows), lambda i: (i, 0, 0))


def low_spec(rows):
    return pl.BlockSpec((1, rows), lambda i: (0, 0))


def own_forward(q, kv, low_row):
    rows, width = q.shape
    pairs = width // LANES
    return pl.pallas_call(
        own_forward_kernel,
        name="own_fwd",
        grid=(pairs,),
        out_shape=(
            jax.ShapeDtypeStruct((rows, width), F32),
            jax.ShapeDtypeStruct((pairs, LANES // HDIM, rows), F32),
        ),
        in_specs=[
            pair_spec(rows),
            stacked_spec(rows, 0),
            stacked_spec(rows, 1),
            low_spec(rows),
        ],
        out_specs=(pair_spec(rows), log_spec(rows)),
        compiler_params=pltpu.CompilerParams(vmem_limit_bytes=VMEM_BYTES),
        cost_estimate=LIGHT,
    )(q, kv, kv, low_row)


SMEM_SPEC = pl.BlockSpec(memory_space=pltpu.SMEM)


def peer_forward(need, q, kv, low_row, part, log_in):
    rows, width = q.shape
    pairs = width // LANES
    return pl.pallas_call(
        peer_forward_kernel,
        name="peer_fwd",
        grid=(pairs,),
        out_shape=(
            jax.ShapeDtypeStruct((rows, width), BF),
            jax.ShapeDtypeStruct((pairs, LANES // HDIM, rows), F32),
        ),
        in_specs=[
            SMEM_SPEC,
            pair_spec(rows),
            stacked_spec(rows, 0),
            stacked_spec(rows, 1),
            low_spec(rows),
            pair_spec(rows),
            log_spec(rows),
        ],
        out_specs=(pair_spec(rows), log_spec(rows)),
        compiler_params=pltpu.CompilerParams(vmem_limit_bytes=VMEM_BYTES),
        cost_estimate=LIGHT,
    )(need, q, kv, kv, low_row, part, log_in)


def backward_block(q_rows, k_rows, v_rows, k_t, do_rows, do_o_t, logs, allowed):
    d_query, d_key, d_value = [], None, None
    for head in range(LANES // HDIM):
        rows_h = slice(head * HDIM, (head + 1) * HDIM)
        q_head = head_mask(q_rows, head)
        do_head = head_mask(do_rows, head)
        scores = dotf(k_rows, q_head, NT)
        probs = jnp.exp(jnp.where(allowed, scores, masked_score) - logs[head])
        delta = jnp.sum(do_o_t[rows_h, :], axis=0, keepdims=True)
        d_probs = dotf(v_rows, do_head, NT)
        d_scores = (probs * (d_probs - delta)).astype(BF)
        d_v = dotf(probs.astype(BF), do_head, NN)
        d_k = dotf(d_scores, q_head, NN)
        d_value = d_v if d_value is None else d_value + d_v
        d_key = d_k if d_key is None else d_key + d_k
        d_query.append(dotf(k_t[rows_h, :], d_scores, NN))
    return jnp.concatenate(d_query, axis=0), d_key, d_value


def output_product(do_ref, o_ref, window):
    product = do_ref[window].astype(F32) * o_ref[window].astype(F32)
    return product.T


def peer_backward_kernel(
    need_ref, q_ref, k_ref, v_ref, do_ref, o_ref, low_ref, log_ref, dq_ref, dkv_ref, sums
):
    rows = q_ref.shape[0]
    key_count = k_ref.shape[0]
    sums[...] = jnp.zeros_like(sums)
    for index, r in enumerate(range(0, rows, QROWS)):
        needed = need_ref[index] < 0
        window = (slice(r, r + QROWS), slice(None))

        @pl.when(needed)
        def _():
            allowed = peer_mask(key_count, low_ref[:, r : r + QROWS], key_count)
            logs = [log_ref[0, h : h + 1, r : r + QROWS] for h in range(LANES // HDIM)]
            d_query, d_key, d_value = backward_block(
                q_ref[window],
                k_ref[...],
                v_ref[...],
                k_ref[...].T,
                do_ref[window],
                output_product(do_ref, o_ref, window),
                logs,
                allowed,
            )
            dq_ref[window] = d_query.T
            sums[0] += d_key
            sums[1] += d_value

        @pl.when(jnp.logical_not(needed))
        def _():
            dq_ref[window] = jnp.zeros((QROWS, LANES), F32)

    dkv_ref[...] = sums[...].astype(BF)


def peer_backward(need, q, kv, do, o, low_row, logs):
    rows, width = q.shape
    pairs = width // LANES
    return pl.pallas_call(
        peer_backward_kernel,
        name="peer_bwd",
        grid=(pairs,),
        out_shape=(
            jax.ShapeDtypeStruct((rows, width), F32),
            jax.ShapeDtypeStruct((2, rows, width), BF),
        ),
        in_specs=[
            SMEM_SPEC,
            pair_spec(rows),
            stacked_spec(rows, 0),
            stacked_spec(rows, 1),
            pair_spec(rows),
            pair_spec(rows),
            low_spec(rows),
            log_spec(rows),
        ],
        out_specs=(pair_spec(rows), pl.BlockSpec((2, rows, LANES), lambda i: (0, 0, i))),
        scratch_shapes=[pltpu.VMEM((2, rows, LANES), F32)],
        compiler_params=pltpu.CompilerParams(vmem_limit_bytes=VMEM_BYTES),
        cost_estimate=LIGHT,
    )(need, q, kv, kv, do, o, low_row, logs)


def own_backward_kernel(
    q_ref,
    k_ref,
    v_ref,
    do_ref,
    o_ref,
    low_ref,
    log_ref,
    dq_in_ref,
    cos_ref,
    sin_ref,
    dq_ref,
    dk_ref,
    dv_ref,
    sums,
):
    rows = q_ref.shape[0]
    sums[...] = jnp.zeros_like(sums)
    k_t = k_ref[...].T
    for r in range(0, rows, QROWS):
        count = r + QROWS
        window = (slice(r, r + QROWS), slice(None))
        allowed = own_mask(count, r, low_ref[:, r : r + QROWS])
        logs = [log_ref[0, h : h + 1, r : r + QROWS] for h in range(LANES // HDIM)]
        d_query, d_key, d_value = backward_block(
            q_ref[window],
            k_ref[0:count, :],
            v_ref[0:count, :],
            k_t[:, 0:count],
            do_ref[window],
            output_product(do_ref, o_ref, window),
            logs,
            allowed,
        )
        rotated = (d_query.T + dq_in_ref[window]) * (HDIM**-0.5)
        turned = rotated * cos_ref[window] - swap_halves(rotated) * sin_ref[window]
        dq_ref[window] = turned.astype(BF)
        sums[0, 0:count] += d_key
        sums[1, 0:count] += d_value
    dk_ref[...] = sums[0]
    dv_ref[...] = sums[1]


def own_backward(q, kv, do, o, low_row, logs, dq_in, cos, sin):
    rows, width = q.shape
    pairs = width // LANES
    table = pl.BlockSpec((rows, LANES), lambda i: (0, 0))
    return pl.pallas_call(
        own_backward_kernel,
        name="own_bwd",
        grid=(pairs,),
        out_shape=(
            jax.ShapeDtypeStruct((rows, width), BF),
            jax.ShapeDtypeStruct((rows, width), F32),
            jax.ShapeDtypeStruct((rows, width), F32),
        ),
        in_specs=[
            pair_spec(rows),
            stacked_spec(rows, 0),
            stacked_spec(rows, 1),
            pair_spec(rows),
            pair_spec(rows),
            low_spec(rows),
            log_spec(rows),
            pair_spec(rows),
            table,
            table,
        ],
        out_specs=(pair_spec(rows),) * 3,
        scratch_shapes=[pltpu.VMEM((2, rows, LANES), F32)],
        compiler_params=pltpu.CompilerParams(vmem_limit_bytes=VMEM_BYTES),
        cost_estimate=LIGHT,
    )(q, kv, kv, do, o, low_row, logs, dq_in, cos, sin)


def finish_keys_kernel(dk_ref, dv_ref, dk_in_ref, dv_in_ref, cos_ref, sin_ref, dk_out, dv_out):
    total = dk_ref[...] + dk_in_ref[...].astype(F32)
    turned = total * cos_ref[...] - swap_halves(total) * sin_ref[...]
    dk_out[...] = turned.astype(BF)
    dv_out[...] = (dv_ref[...] + dv_in_ref[...].astype(F32)).astype(BF)


def finish_keys(dk, dv, dkv_in, cos, sin):
    rows, width = dk.shape
    pairs = width // LANES
    table = pl.BlockSpec((rows, LANES), lambda i: (0, 0))
    return pl.pallas_call(
        finish_keys_kernel,
        name="finish_keys",
        grid=(pairs,),
        out_shape=(jax.ShapeDtypeStruct((rows, width), BF),) * 2,
        in_specs=[pair_spec(rows), pair_spec(rows), stacked_spec(rows, 0), stacked_spec(rows, 1)]
        + [table, table],
        out_specs=(pair_spec(rows),) * 2,
        cost_estimate=LIGHT,
    )(dk, dv, dkv_in, dkv_in, cos, sin)


def branch_kernel(stream_ref, att_ref, gain_ref, *refs):
    pieces, (hidden_ref, normed_ref, scale_ref) = refs[:4], refs[4:]
    for j, piece in enumerate(pieces):
        columns = piece_columns(j, piece.shape[1])
        term = dotf(att_ref[...], piece[...], NN)
        hidden_ref[:, columns] = stream_ref[:, columns].astype(F32) + term
    hidden = hidden_ref[...]
    mean = jnp.sum(hidden * hidden, axis=1, keepdims=True) / hidden.shape[1]
    scale = lax.rsqrt(mean + norm_eps)
    scale_ref[...] = scale
    normed_ref[...] = (hidden * scale * gain_ref[...]).astype(BF)


def add_branch(stream, att, gain, pieces):
    rows, depth = stream.shape
    heads = att.shape[1]
    tile = pl.BlockSpec((QROWS, depth), lambda i: (i, 0))
    return pl.pallas_call(
        branch_kernel,
        name="branch",
        grid=(rows // QROWS,),
        out_shape=(
            jax.ShapeDtypeStruct((rows, depth), F32),
            jax.ShapeDtypeStruct((rows, depth), BF),
            jax.ShapeDtypeStruct((rows, 1), F32),
        ),
        in_specs=[
            tile,
            pl.BlockSpec((QROWS, heads), lambda i: (i, 0)),
            pl.BlockSpec((1, depth), lambda i: (0, 0)),
        ]
        + [pl.BlockSpec(pieces[0].shape, lambda i: (0, 0))] * 4,
        out_specs=(tile, tile, pl.BlockSpec((QROWS, 1), lambda i: (i, 0))),
        compiler_params=pltpu.CompilerParams(vmem_limit_bytes=VMEM_BYTES),
        cost_estimate=LIGHT,
    )(stream, att, gain, *pieces)


def hidden_kernel(x_ref, *refs):
    w_in, (act_ref, by_gate_ref, by_up_ref) = refs[:4], refs[4:]
    rows = x_ref.shape[0]
    for r in range(0, rows, rows):
        part = slice(r, r + rows)
        gate = piece_dot(x_ref, part, [piece[0] for piece in w_in])
        up = piece_dot(x_ref, part, [piece[1] for piece in w_in])
        sig = jax.nn.sigmoid(gate)
        silu = gate * sig
        act_ref[part, :] = (silu * up).astype(BF)
        by_gate_ref[part, :] = (up * sig * (1.0 + gate * (1.0 - sig))).astype(BF)
        by_up_ref[part, :] = silu.astype(BF)


def hidden_units(x, w_in):
    rows, depth = x.shape
    _, size, units = w_in[0].shape
    tile = 256
    part = pl.BlockSpec((rows, tile), lambda i: (0, i))
    return pl.pallas_call(
        hidden_kernel,
        grid=(units // tile,),
        out_shape=(jax.ShapeDtypeStruct((rows, units), BF),) * 3,
        in_specs=[pl.BlockSpec((rows, depth), lambda i: (0, 0))]
        + [pl.BlockSpec((2, size, tile), lambda i: (0, 0, i))] * 4,
        out_specs=(part,) * 3,
        compiler_params=pltpu.CompilerParams(vmem_limit_bytes=VMEM_BYTES),
        cost_estimate=LIGHT,
        name="hidden",
    )(x, *w_in)


def hidden_back_kernel(cot_ref, by_gate_ref, by_up_ref, *refs):
    w_down, (dg_ref, du_ref) = refs[:4], refs[4:]
    rows = cot_ref.shape[0]
    for r in range(0, rows, rows):
        part = slice(r, r + rows)
        d_act = piece_dot(cot_ref, part, [piece[...] for piece in w_down], NT)
        dg_ref[part, :] = (d_act * by_gate_ref[part, :].astype(F32)).astype(BF)
        du_ref[part, :] = (d_act * by_up_ref[part, :].astype(F32)).astype(BF)


def hidden_back(cot, by_gate, by_up, w_down):
    rows, depth = cot.shape
    units, size = w_down[0].shape
    tile = 256
    part = pl.BlockSpec((rows, tile), lambda i: (0, i))
    return pl.pallas_call(
        hidden_back_kernel,
        grid=(units // tile,),
        out_shape=(jax.ShapeDtypeStruct((rows, units), BF),) * 2,
        in_specs=[pl.BlockSpec((rows, depth), lambda i: (0, 0)), part, part]
        + [pl.BlockSpec((tile, size), lambda i: (i, 0))] * 4,
        out_specs=(part,) * 2,
        compiler_params=pltpu.CompilerParams(vmem_limit_bytes=VMEM_BYTES),
        cost_estimate=LIGHT,
        name="hidden_back",
    )(cot, by_gate, by_up, *w_down)


def phased(i, block, make_index, tiles):
    def index_map(j, t):
        return make_index(jnp.where(j < i, 0, jnp.where(j == i, t, tiles - 1)))

    return pl.BlockSpec(block, index_map)


def columns_call(kernel_dot, lefts, pieces, block, make_index, size, flops, name):
    rows = lefts[0].shape[0]
    tile = min(size, 256)
    tiles = size // tile
    depth = size * 4

    def kernel(*refs):
        left_refs, piece_refs, out_ref = refs[: len(lefts)], refs[len(lefts) : -1], refs[-1]
        for j, piece in enumerate(piece_refs):

            @pl.when(pl.program_id(0) == j)
            def _():
                out_ref[...] = kernel_dot([left[...] for left in left_refs], piece).astype(BF)

    def out_index(j, t):
        return (0, (lax.axis_index("fsdp") ^ j) * tiles + t)

    return pl.pallas_call(
        kernel,
        grid=(4, tiles),
        out_shape=jax.ShapeDtypeStruct((rows, depth), BF),
        in_specs=[pl.BlockSpec(left.shape, lambda j, t: (0, 0)) for left in lefts]
        + [phased(i, block(tile), make_index, tiles) for i in range(4)],
        out_specs=pl.BlockSpec((rows, tile), out_index),
        compiler_params=pltpu.CompilerParams(vmem_limit_bytes=VMEM_BYTES),
        cost_estimate=LIGHT,
        name=name,
    )(*lefts, *pieces)


def stacked_columns(lefts, pieces, name):
    count, size, inner = pieces[0].shape

    def product(parts, piece):
        return sum(dotf(parts[c], piece[c], NT) for c in range(count))

    return columns_call(
        product,
        lefts,
        pieces,
        lambda tile: (count, tile, inner),
        lambda t: (0, t, 0),
        size,
        8 * lefts[0].shape[0] * size * inner * count,
        name,
    )


def plain_columns(left, pieces, name):
    inner, size = pieces[0].shape
    return columns_call(
        lambda parts, piece: dotf(parts[0], piece[...], NN),
        [left],
        pieces,
        lambda tile: (inner, tile),
        lambda t: (0, t),
        size,
        8 * left.shape[0] * size * inner,
        name,
    )


def branch_back_kernel(shares, d_mid_ref, hidden_ref, cot_ref, scale_ref, gain_ref, *refs):
    pieces, (d_hidden_ref, d_att_ref, gain_out_ref) = refs[:4], refs[4:7]
    d_mid = d_mid_ref[...].astype(F32)
    hidden = hidden_ref[...]
    scale = scale_ref[...]
    weighted = d_mid * gain_ref[...]
    inner = jnp.sum(weighted * hidden, axis=1, keepdims=True) / hidden.shape[1]
    d_hidden = (
        cot_ref[...].astype(F32) * (1.0 / shares)
        + scale * weighted
        - hidden * (scale * scale * scale * inner)
    )
    gain_term = jnp.sum(d_mid * hidden * scale, axis=0, keepdims=True)

    @pl.when(pl.program_id(0) == 0)
    def _():
        gain_out_ref[...] = gain_term

    @pl.when(pl.program_id(0) != 0)
    def _():
        gain_out_ref[...] += gain_term

    d_hidden_ref[...] = d_hidden.astype(BF)
    heads = d_att_ref.shape[1]
    for e in range(0, heads, 512):
        columns = slice(e, e + 512)
        d_att_ref[:, columns] = piece_dot(
            d_hidden_ref, slice(None), [piece[columns, :] for piece in pieces], NT
        ).astype(BF)


def branch_back(d_mid, hidden, cot, scale, gain, pieces):
    rows, depth = hidden.shape
    heads, size = pieces[0].shape
    tile = pl.BlockSpec((QROWS, depth), lambda i: (i, 0))
    row = pl.BlockSpec((1, depth), lambda i: (0, 0))
    return pl.pallas_call(
        functools.partial(branch_back_kernel, lax.axis_size("tensor")),
        name="branch_back",
        grid=(rows // QROWS,),
        in_specs=[tile, tile, tile, pl.BlockSpec((QROWS, 1), lambda i: (i, 0)), row]
        + [pl.BlockSpec((heads, size), lambda i: (0, 0))] * 4,
        out_specs=(tile, pl.BlockSpec((QROWS, heads), lambda i: (i, 0)), row),
        out_shape=(
            jax.ShapeDtypeStruct((rows, depth), BF),
            jax.ShapeDtypeStruct((rows, heads), BF),
            jax.ShapeDtypeStruct((1, depth), F32),
        ),
        compiler_params=pltpu.CompilerParams(vmem_limit_bytes=VMEM_BYTES),
        cost_estimate=LIGHT,
    )(d_mid, hidden, cot, scale, gain, *pieces)


def grad_call(left, right, cut, place, adds, name, span=(0, 1)):
    rows = left.shape[0]
    size = (left, right)[cut].shape[1] // 4
    swept = (right, left)[cut].shape[1] // span[1]
    height, width = (size, swept) if cut == 0 else (swept, size)
    tile = min(1024, swept)
    offset = span[0] * (swept // tile)
    block = (height, tile) if cut == 0 else (tile, width)

    def owner():
        return lax.axis_index("fsdp") ^ place

    def swept_index(t):
        return (0, t) if cut == 0 else (t, 0)

    def kernel(left_ref, right_ref, *refs):
        add_refs, out_ref = refs[: len(adds)], refs[len(adds)]
        if cut == 0:
            turned = refs[-1]

            @pl.when(pl.program_id(0) == 0)
            def _():
                turned[...] = left_ref[...].T

            result = dotf(turned[...], right_ref[...], NN)
        else:
            result = dotf(left_ref[...].T, right_ref[...], NN)
        for add in add_refs:
            result = result + add[...].astype(F32)
        out_ref[...] = result.astype(BF)

    fixed = pl.BlockSpec((rows, size), lambda t: (0, owner()))
    moving = pl.BlockSpec((rows, tile), lambda t: (0, t + offset))
    return pl.pallas_call(
        kernel,
        grid=(swept // tile,),
        out_shape=jax.ShapeDtypeStruct((height, width), BF),
        in_specs=[fixed, moving] * (cut == 0)
        + [moving, fixed] * (cut == 1)
        + [pl.BlockSpec(block, swept_index)] * len(adds),
        out_specs=pl.BlockSpec(block, swept_index),
        scratch_shapes=[pltpu.VMEM((size, rows), BF)] if cut == 0 else [],
        compiler_params=pltpu.CompilerParams(vmem_limit_bytes=VMEM_BYTES),
        cost_estimate=LIGHT,
        name=name,
    )(left, right, *adds)


class Reduction:
    def __init__(self, left, right, cut, name, span=(0, 1)):
        self.args, self.name, self.span = (left, right, cut), name, span

    def call(self, place, deps, step, adds=()):
        left, right, cut = self.args
        left = after(left, *deps) if deps else left
        return grad_call(left, right, cut, place, adds, self.name + step, self.span)

    def near_far(self, *deps):
        self.three = self.call(3, deps, "_3")
        self.for_two = swap(self.three, "fsdp", 1)

    def near(self, *deps):
        self.one = self.call(1, deps, "_1")
        self.for_own = swap(self.one, "fsdp", 1)

    def far(self, *deps):
        self.two = self.call(2, deps, "_2", [self.for_two])

    def send_far(self, *deps):
        self.across = swap(after(self.two, *deps), "fsdp", 2)

    def mine(self, *deps):
        self.own = self.call(0, deps, "_0", [self.for_own, self.across])

    def send_context(self, *deps):
        self.other = swap(after(self.own, *deps), "context", 1)


def totals_kernel(slots, *refs):
    pairs, out_ref = refs[:-1], refs[-1]
    for slot in range(len(pairs) // 2):
        total = pairs[2 * slot][...].astype(F32) + pairs[2 * slot + 1][...].astype(F32)
        if slots == 0:
            out_ref[slot] = total
        else:
            out_ref[:, slot, :] = total


def totals(sums, slots, *deps):
    arrays = [array for part in sums for array in (part.own, part.other)]
    if deps:
        arrays[0] = after(arrays[0], *deps)
    rows, width = arrays[0].shape
    tile = 128
    shape = [rows, width]
    shape.insert(slots, len(sums))
    block = [tile, width]
    block.insert(slots, len(sums))
    return pl.pallas_call(
        functools.partial(totals_kernel, slots),
        grid=(rows // tile,),
        out_shape=jax.ShapeDtypeStruct(tuple(shape), F32),
        in_specs=[pl.BlockSpec((tile, width), lambda i: (i, 0))] * len(arrays),
        out_specs=pl.BlockSpec(
            tuple(block), (lambda i: (0, i, 0)) if slots == 0 else (lambda i: (i, 0, 0))
        ),
        compiler_params=pltpu.CompilerParams(vmem_limit_bytes=VMEM_BYTES),
        cost_estimate=LIGHT,
        name="totals",
    )(*arrays)


def row_sum(values_in):
    return jnp.sum(values_in, axis=1, keepdims=True)


def per_device(tokens, w_qkv, w_out, w_gate_up, w_down, gains, seq_lengths, cotangent):
    row_count, part_width = tokens.shape
    tensor_index = lax.axis_index("tensor")
    context_index = lax.axis_index("context")
    full_width = part_width * lax.axis_size("tensor")

    def features(part_in):
        return lax.all_gather(part_in, "tensor", axis=1, tiled=True)

    def feature_sum(term):
        return lax.psum_scatter(term.astype(BF), "tensor", scatter_dimension=1, tiled=True)

    def own_features(full):
        return lax.dynamic_slice_in_dim(full, tensor_index * part_width, part_width, 1)

    ending = jnp.cumsum(seq_lengths[0])
    starts = ending - seq_lengths[0]
    places = context_index * row_count + jnp.arange(row_count, dtype=jnp.int32)
    first_token = jnp.max(jnp.where(starts[None, :] <= places[:, None], starts[None, :], 0), axis=1)
    cos, sin = rope_tables(places - first_token)
    low = first_token - context_index * row_count
    low_row = low[None, :]
    need = low[::QROWS]

    token_low = features(tokens)
    gain_near, gain_full = gather_gains(gains)
    gain_attn, gain_mlp = gain_full[0:1], gain_full[1:2]

    qkv_own = jnp.swapaxes(w_qkv, 0, 1)
    half = qkv_own.shape[1] // 2
    far_half = swap(
        lax.dynamic_slice_in_dim(after(qkv_own, gain_near), context_index * half, half, 1),
        "fsdp",
        2,
    )
    other_half = swap(far_half, "context", 1)
    qkv_far = jnp.where(
        context_index == 0,
        jnp.concatenate([far_half, other_half], axis=1),
        jnp.concatenate([other_half, far_half], axis=1),
    )
    qkv_near = swap(qkv_own, "fsdp", 1)
    qkv = (qkv_own, qkv_near, qkv_far, swap(qkv_far, "fsdp", 1))

    gate_up_own = jnp.swapaxes(w_gate_up, 0, 1)
    cut = gate_up_own.shape[1] * 15 // 32
    gate_up_a = swap(after(gate_up_own[:, :cut], far_half), "fsdp", 2)
    gate_up_b = swap(after(gate_up_own[:, cut:], gate_up_a), "fsdp", 2)

    keys_values, normed_in, scale_attn = project(
        after(token_low, gate_up_a), qkv, cos, sin, gain_attn, (1.0, None), 1, True
    )
    peer_kv = lax.ppermute(keys_values, "context", [(0, 1)])
    queries = project(normed_in, qkv, cos, sin, gain_attn, (HDIM**-0.5,), 0, False)[0][0]
    part, part_log = own_forward(queries, keys_values, low_row)
    out_own = lax.all_gather(w_out, "tensor", axis=0, tiled=True)
    out_near = swap(out_own, "fsdp", 1)
    attended, logs = peer_forward(
        need, queries, peer_kv, low_row, after(part, gate_up_b, out_near), part_log
    )
    attended_full = features(attended)

    out_far = swap(after(out_own, attended), "fsdp", 2)
    out_far_near = swap(out_far, "fsdp", 1)
    out = (out_own, out_near, out_far, out_far_near)
    gate_up_own, gate_up_a, gate_up_b = lax.optimization_barrier(
        (gate_up_own, gate_up_a, gate_up_b, attended)
    )[:3]
    gate_up_far = jnp.concatenate([gate_up_a, gate_up_b], axis=1)
    gate_up_near = swap(gate_up_own, "fsdp", 1)
    gate_up = (gate_up_own, gate_up_near, gate_up_far, swap(gate_up_far, "fsdp", 1))
    cot_full = features(after(cotangent, attended_full, out_far_near))
    down_far = swap(after(w_down, attended_full, out_far_near), "fsdp", 2)
    down_near = swap(after(w_down, attended_full), "fsdp", 1)
    hidden, normed_mid, scale_mlp = add_branch(token_low, attended_full, gain_mlp, out)

    activated, by_gate, by_up = hidden_units(normed_mid, gate_up)
    down_far = after(down_far, activated)
    down = (w_down, down_near, down_far, swap(down_far, "fsdp", 1))
    mlp_term = plain_columns(activated, down, "mlp_out")
    mlp_out = feature_sum(mlp_term)
    d_gate, d_up = hidden_back(after(cot_full, mlp_term), by_gate, by_up, down)
    d_mid_term = stacked_columns([d_gate, d_up], gate_up, "d_mid")
    d_hidden_term, d_att_term, gain_mlp_term = branch_back(
        d_mid_term, hidden, cot_full, scale_mlp, gain_mlp, out
    )
    d_attended = feature_sum(after(d_att_term, mlp_out))
    d_hidden_own = feature_sum(after(d_hidden_term, d_att_term))

    down_a, down_b = (
        Reduction(activated, cot_full, 1, "grad_down", (part_index, 2)) for part_index in (0, 1)
    )
    grad_gate = Reduction(normed_mid, d_gate, 0, "grad_gate")
    grad_up = Reduction(normed_mid, d_up, 0, "grad_up")
    down_a.near_far(d_att_term)
    down_b.near_far(down_a.three)
    grad_gate.near_far(down_b.three)
    down_a.far(grad_gate.three)
    down_a.send_far()
    down_b.far(down_a.two)
    down_a.near(down_b.two)
    down_b.near(down_a.one)
    down_b.send_far(down_a.across)
    down_a.mine(down_b.one)
    down_a.send_context()
    grad_gate.near(down_a.own)
    grad_gate.far(grad_gate.one)
    grad_up.near_far(grad_gate.two)
    grad_up.near(grad_up.three)
    grad_up.far(grad_up.one)
    grad_gate.send_far(down_b.across)
    down_b.mine(grad_up.two)
    down_b.send_context(down_a.other)

    dq_peer, dkv_peer = peer_backward(
        need, queries, peer_kv, after(d_attended, down_b.own), attended, low_row, logs
    )
    dkv_in = lax.ppermute(dkv_peer, "context", [(1, 0)])
    d_query, dk_own, dv_own = own_backward(
        queries, keys_values, d_attended, attended, low_row, logs, dq_peer, cos, sin
    )
    grad_query = Reduction(normed_in, d_query, 0, "grad_query")
    grad_gate.mine(d_query)
    grad_gate.send_context(down_b.other)
    grad_up.send_far(grad_gate.own)
    grad_query.near_far(grad_gate.own)
    grad_query.near(grad_query.three)
    d_key, d_value = finish_keys(
        dk_own, dv_own, after(dkv_in, grad_query.one, d_hidden_own), cos, sin
    )
    d_in_term = stacked_columns([d_query, d_key, d_value], qkv, "d_in")
    d_in = feature_sum(d_in_term).astype(F32)

    square = lax.axis_size("tensor") == lax.axis_size("fsdp")
    if square:
        grad_out = Reduction(attended_full, d_hidden_own, 0, "grad_out")
    else:
        grad_out = Reduction(attended, features(d_hidden_own), 1, "grad_out")
    grad_query.far(d_in_term)
    grad_query.send_far(grad_up.across)
    grad_key = Reduction(normed_in, d_key, 0, "grad_key")
    grad_value = Reduction(normed_in, d_value, 0, "grad_value")
    grad_key.near_far(grad_query.two)
    grad_value.near_far(grad_key.three)
    grad_out.near_far(grad_value.three)
    grad_key.near(grad_out.three)
    grad_value.near(grad_key.one)
    grad_out.near(grad_value.one)
    grad_key.far(grad_out.one)
    grad_value.far(grad_key.two)
    grad_out.far(grad_value.two)
    grad_key.send_far(grad_up.across)
    grad_value.send_far(grad_up.across)
    grad_out.send_far(grad_up.across)
    grad_up.mine(grad_out.two)
    grad_up.send_context(grad_gate.other)

    stream = token_low.astype(F32)
    d_in_wide = after(d_in_term, grad_up.own).astype(F32)
    weighted = d_in_wide * stream
    inner_term = jnp.sum(weighted * gain_attn, axis=1)
    gain_attn_term = jnp.sum(weighted * scale_attn, axis=0)
    parts = lax.axis_size("tensor")
    totals_small = block_totals(
        jnp.concatenate(
            [
                jnp.broadcast_to(inner_term[None, :], (parts, row_count)),
                gain_attn_term.reshape(parts, part_width),
                gain_mlp_term.reshape(parts, part_width),
            ],
            axis=1,
        )[None]
    )
    inner_in = totals_small[0, :row_count][:, None] / full_width
    gain_sums = totals_small[0, row_count:].reshape(2, part_width)
    gain_sums = exchange(gain_sums, "fsdp", 1)
    gain_sums = exchange(gain_sums, "fsdp", 2)
    gain_sums = exchange(gain_sums, "context", 1)
    gain_width = gains.shape[1]
    grad_gains = lax.dynamic_slice_in_dim(
        gain_sums, lax.axis_index("fsdp") * gain_width, gain_width, 1
    )

    grad_query.mine(d_in_wide)
    grad_query.send_context()
    grad_down_sum = totals([down_a, down_b], 0, grad_query.own).reshape(w_down.shape)
    grad_key.mine(grad_down_sum)
    grad_key.send_context()
    grad_value.mine(grad_key.own, d_in)
    grad_value.send_context()
    grad_out.mine(grad_value.own)
    if square:
        count = lax.axis_size("fsdp")
        across = [(i, (i % count) * count + i // count) for i in range(count * count)]
        grad_out.own = lax.ppermute(grad_out.own, ("fsdp", "tensor"), across)
    grad_out.send_context()
    grad_gate_up_sum = totals([grad_gate, grad_up], 1, grad_value.own)
    grad_qkv = totals([grad_query, grad_key, grad_value], 0, grad_gate_up_sum)
    grad_out_sum = totals([grad_out], 0, grad_qkv)[0]

    block_out = (own_features(hidden) + mlp_out.astype(F32)).astype(BF)
    own_tokens = tokens.astype(F32)
    grad_tokens = (
        d_hidden_own.astype(F32)
        + scale_attn * own_features(gain_attn) * d_in
        - own_tokens * scale_attn * scale_attn * scale_attn * inner_in
    ).astype(BF)
    return (
        block_out,
        grad_tokens,
        jnp.swapaxes(grad_qkv, 0, 1),
        grad_out_sum,
        grad_gate_up_sum,
        grad_down_sum,
        grad_gains,
    )


def solution(mesh):
    rows = P(("fsdp", "context"), "tensor")
    inner = P("fsdp", None, "tensor")
    outer = P("tensor", "fsdp")
    gain = P(None, ("tensor", "fsdp"))
    return jax.shard_map(
        per_device,
        mesh=mesh,
        in_specs=(rows, inner, outer, inner, outer, gain, P("fsdp", None), rows),
        out_specs=(rows, rows, inner, outer, inner, outer, gain),
        check_vma=False,
    )
```

```python
import functools

import jax
import jax.numpy as jnp
from jax import lax
from jax.experimental import pallas as pl
from jax.experimental.pallas import tpu as pltpu
from jax.sharding import PartitionSpec as P

HDIM = 64
LANES = 128
QROWS = 256
norm_eps = 1e-05
rope_base = 130000.0
masked_score = -1e30
BF = jnp.bfloat16
F32 = jnp.float32
VMEM_BYTES = 56 * 1024 * 1024
LIGHT = pl.CostEstimate(flops=1, bytes_accessed=1, transcendentals=0)


def dotf(a, b, dims):
    return lax.dot_general(a, b, (dims, ((), ())), preferred_element_type=F32)


NN = ((1,), (0,))
NT = ((1,), (1,))
TN = ((0,), (0,))


def swap(value, axis, bit):
    count = lax.axis_size(axis)
    return lax.ppermute(value, axis, [(i, i ^ bit) for i in range(count)])


def after(value, *others):
    return lax.optimization_barrier((value, *others))[0]


def shifted(value, axis):
    count = lax.axis_size(axis)
    return [
        lax.ppermute(value, axis, [(i, (i + step) % count) for i in range(count)])
        for step in range(1, count)
    ]


def exchange(value, axis, bit):
    return value + swap(value, axis, bit)


def join_kernel(axis, mode, *refs):
    pieces, out_ref = refs[:-1], refs[-1]
    count = len(pieces)
    me = lax.axis_index(axis)
    for step, piece in enumerate(pieces):
        size = piece.shape[1]
        place = (me ^ step) if mode == "xor" else (me - step + count) % count
        out_ref[:, pl.ds(pl.multiple_of(place * size, size), size)] = piece[...]


def join(pieces, axis, mode):
    rows, size = pieces[0].shape
    return pl.pallas_call(
        functools.partial(join_kernel, axis, mode),
        out_shape=jax.ShapeDtypeStruct((rows, size * len(pieces)), pieces[0].dtype),
        cost_estimate=LIGHT,
        name="join",
    )(*pieces)


def gather_gains(gains):
    if lax.axis_size("tensor") > 4 or gains.shape[1] % LANES:
        whole = lax.all_gather(gains, ("tensor", "fsdp"), axis=1, tiled=True).astype(F32)
        return gains, whole
    own = gains.astype(F32)
    part = join([own] + [swap(own, "fsdp", bit) for bit in (1, 2, 3)], "fsdp", "xor")
    return part, join([part] + shifted(part, "tensor"), "tensor", "shift")


def block_totals(blocks):
    count = lax.axis_size("tensor")
    me = lax.axis_index("tensor")
    if count > 4:
        return lax.dynamic_index_in_dim(lax.psum(blocks, "tensor"), me, 1, keepdims=False)

    def pick(place):
        return lax.dynamic_index_in_dim(blocks, place, 1, keepdims=False)

    total = pick(me)
    for step in range(1, count):
        moves = [(i, (i + step) % count) for i in range(count)]
        total = total + lax.ppermute(pick((me + step) % count), "tensor", moves)
    return total


def piece_columns(j, size):
    return pl.ds(pl.multiple_of((lax.axis_index("fsdp") ^ j) * size, size), size)


def swap_halves(block):
    lane = lax.broadcasted_iota(jnp.int32, block.shape, 1)
    up = pltpu.roll(block, LANES - HDIM // 2, 1)
    down = pltpu.roll(block, HDIM // 2, 1)
    return jnp.where((lane & (HDIM - 1)) < HDIM // 2, up, down)


def rope_tables(positions):
    lane = jnp.arange(LANES, dtype=jnp.int32)
    half = lane % (HDIM // 2)
    frequencies = rope_base ** (-2.0 * half.astype(F32) / HDIM)
    angles = positions.astype(F32)[:, None] * frequencies[None, :]
    sign = jnp.where((lane % HDIM) < HDIM // 2, -1.0, 1.0)
    return jnp.cos(angles), jnp.sin(angles) * sign[None, :]


def piece_dot(x_ref, rows, pieces, dims=NN):
    total = None
    for j, piece in enumerate(pieces):
        size = piece.shape[dims[1][0]]
        term = dotf(x_ref[rows, piece_columns(j, size)], piece, dims)
        total = term if total is None else total + term
    return total


def project_kernel(kinds, normalize, x_ref, *refs):
    pieces, (cos_ref, sin_ref, gain_ref), outs = refs[:4], refs[4:7], refs[7:]
    out_ref = outs[0]
    rows, width = out_ref.shape[1:]
    step = pl.program_id(0)
    if normalize:
        normed_ref, scale_ref = outs[1], outs[2]

        @pl.when(step == 0)
        def _():
            for r in range(0, rows, QROWS):
                part = slice(r, r + QROWS)
                stream = x_ref[part, :].astype(F32)
                mean = jnp.sum(stream * stream, axis=1, keepdims=True) / x_ref.shape[1]
                scale = lax.rsqrt(mean + norm_eps)
                scale_ref[part, :] = scale
                normed_ref[part, :] = (stream * scale * gain_ref[...]).astype(BF)

        x_ref = normed_ref
    for index, scale in enumerate(kinds):

        @pl.when(step == index)
        def _():
            for r in range(0, rows, rows):
                part = slice(r, r + rows)
                result = piece_dot(x_ref, part, [piece[0] for piece in pieces])
                for c in range(0, width, LANES):
                    block = result[:, c : c + LANES]
                    if scale:
                        block = block * cos_ref[part, :] + swap_halves(block) * sin_ref[part, :]
                    low = block.astype(BF)
                    if scale and scale != 1.0:
                        low = low * jnp.asarray(scale, BF)
                    out_ref[0, part, c : c + LANES] = low


def project(x, pieces, cos, sin, gain, kinds, first, normalize):
    rows, depth = x.shape
    _, size, width = pieces[0].shape
    flops = 2 * len(kinds) * rows * depth * width
    whole = pl.BlockSpec((rows, depth), lambda i: (0, 0))
    table = pl.BlockSpec((rows, LANES), lambda i: (0, 0))
    out_shape = [jax.ShapeDtypeStruct((len(kinds), rows, width), BF)]
    out_specs = [pl.BlockSpec((1, rows, width), lambda i: (i, 0, 0))]
    if normalize:
        out_shape += [jax.ShapeDtypeStruct((rows, depth), BF), jax.ShapeDtypeStruct((rows, 1), F32)]
        out_specs += [whole, pl.BlockSpec((rows, 1), lambda i: (0, 0))]
    return pl.pallas_call(
        functools.partial(project_kernel, kinds, normalize),
        name="project_kv" if normalize else "project_q",
        grid=(len(kinds),),
        out_shape=out_shape,
        in_specs=[whole]
        + [pl.BlockSpec((1, size, width), lambda i: (i + first, 0, 0))] * 4
        + [table, table, pl.BlockSpec((1, depth), lambda i: (0, 0))],
        out_specs=out_specs,
        compiler_params=pltpu.CompilerParams(vmem_limit_bytes=VMEM_BYTES),
        cost_estimate=LIGHT,
    )(x, *pieces, cos, sin, gain)


def head_mask(block, head):
    lane = lax.broadcasted_iota(jnp.int32, block.shape, 1)
    inside = (lane < HDIM) if head == 0 else (lane >= HDIM)
    return jnp.where(inside, block, jnp.zeros_like(block))


def own_mask(key_count, row0, low_row):
    key = lax.broadcasted_iota(jnp.int32, (key_count, QROWS), 0)
    query = row0 + lax.broadcasted_iota(jnp.int32, (key_count, QROWS), 1)
    return (key >= low_row) & (key <= query)


def peer_mask(key_count, low_row, offset):
    key = lax.broadcasted_iota(jnp.int32, (key_count, QROWS), 0) - offset
    return key >= low_row


def own_forward_kernel(q_ref, k_ref, v_ref, low_ref, out_ref, log_ref):
    rows = q_ref.shape[0]
    v_t = v_ref[...].T
    for r in range(0, rows, QROWS):
        count = r + QROWS
        allowed = own_mask(count, r, low_ref[:, r : r + QROWS])
        keys = k_ref[0:count, :]
        outs = []
        for head in range(LANES // HDIM):
            scores = dotf(keys, head_mask(q_ref[r : r + QROWS, :], head), NT)
            scores = jnp.where(allowed, scores, masked_score)
            peak = jnp.max(scores, axis=0, keepdims=True)
            weights = jnp.exp(scores - peak)
            total = jnp.sum(weights, axis=0, keepdims=True)
            part = dotf(v_t[head * HDIM : (head + 1) * HDIM, 0:count], weights.astype(BF), NN)
            outs.append(part / total)
            log_ref[0, head : head + 1, r : r + QROWS] = peak + jnp.log(total)
        out_ref[r : r + QROWS, :] = jnp.concatenate(outs, axis=0).T


def peer_forward_kernel(
    need_ref, q_ref, k_ref, v_ref, low_ref, part_ref, log_in_ref, out_ref, log_ref
):
    rows = q_ref.shape[0]
    key_count = k_ref.shape[0]
    for index, r in enumerate(range(0, rows, QROWS)):
        needed = need_ref[index] < 0

        @pl.when(needed)
        def _():
            v_t = v_ref[...].T
            allowed = peer_mask(key_count, low_ref[:, r : r + QROWS], key_count)
            before = part_ref[r : r + QROWS, :].T
            outs = []
            for head in range(LANES // HDIM):
                scores = dotf(k_ref[...], head_mask(q_ref[r : r + QROWS, :], head), NT)
                scores = jnp.where(allowed, scores, masked_score)
                log_own = log_in_ref[0, head : head + 1, r : r + QROWS]
                peak = jnp.maximum(jnp.max(scores, axis=0, keepdims=True), log_own)
                weights = jnp.exp(scores - peak)
                own_weight = jnp.exp(log_own - peak)
                total = jnp.sum(weights, axis=0, keepdims=True) + own_weight
                rows_h = slice(head * HDIM, (head + 1) * HDIM)
                part = dotf(v_t[rows_h, :], weights.astype(BF), NN)
                outs.append((part + before[rows_h, :] * own_weight) / total)
                log_ref[0, head : head + 1, r : r + QROWS] = peak + jnp.log(total)
            out_ref[r : r + QROWS, :] = jnp.concatenate(outs, axis=0).T.astype(BF)

        @pl.when(jnp.logical_not(needed))
        def _():
            out_ref[r : r + QROWS, :] = part_ref[r : r + QROWS, :].astype(BF)
            log_ref[:, :, r : r + QROWS] = log_in_ref[:, :, r : r + QROWS]


def pair_spec(rows):
    return pl.BlockSpec((rows, LANES), lambda i: (0, i))


def stacked_spec(rows, part):
    return pl.BlockSpec((None, rows, LANES), lambda i: (part, 0, i))


def log_spec(rows):
    return pl.BlockSpec((1, LANES // HDIM, rows), lambda i: (i, 0, 0))


def low_spec(rows):
    return pl.BlockSpec((1, rows), lambda i: (0, 0))


def own_forward(q, kv, low_row):
    rows, width = q.shape
    pairs = width // LANES
    return pl.pallas_call(
        own_forward_kernel,
        name="own_fwd",
        grid=(pairs,),
        out_shape=(
            jax.ShapeDtypeStruct((rows, width), F32),
            jax.ShapeDtypeStruct((pairs, LANES // HDIM, rows), F32),
        ),
        in_specs=[
            pair_spec(rows),
            stacked_spec(rows, 0),
            stacked_spec(rows, 1),
            low_spec(rows),
        ],
        out_specs=(pair_spec(rows), log_spec(rows)),
        compiler_params=pltpu.CompilerParams(vmem_limit_bytes=VMEM_BYTES),
        cost_estimate=LIGHT,
    )(q, kv, kv, low_row)


SMEM_SPEC = pl.BlockSpec(memory_space=pltpu.SMEM)


def peer_forward(need, q, kv, low_row, part, log_in):
    rows, width = q.shape
    pairs = width // LANES
    return pl.pallas_call(
        peer_forward_kernel,
        name="peer_fwd",
        grid=(pairs,),
        out_shape=(
            jax.ShapeDtypeStruct((rows, width), BF),
            jax.ShapeDtypeStruct((pairs, LANES // HDIM, rows), F32),
        ),
        in_specs=[
            SMEM_SPEC,
            pair_spec(rows),
            stacked_spec(rows, 0),
            stacked_spec(rows, 1),
            low_spec(rows),
            pair_spec(rows),
            log_spec(rows),
        ],
        out_specs=(pair_spec(rows), log_spec(rows)),
        compiler_params=pltpu.CompilerParams(vmem_limit_bytes=VMEM_BYTES),
        cost_estimate=LIGHT,
    )(need, q, kv, kv, low_row, part, log_in)


def backward_block(q_rows, k_rows, v_rows, k_t, do_rows, do_o_t, logs, allowed):
    d_query, d_key, d_value = [], None, None
    for head in range(LANES // HDIM):
        rows_h = slice(head * HDIM, (head + 1) * HDIM)
        q_head = head_mask(q_rows, head)
        do_head = head_mask(do_rows, head)
        scores = dotf(k_rows, q_head, NT)
        probs = jnp.exp(jnp.where(allowed, scores, masked_score) - logs[head])
        delta = jnp.sum(do_o_t[rows_h, :], axis=0, keepdims=True)
        d_probs = dotf(v_rows, do_head, NT)
        d_scores = (probs * (d_probs - delta)).astype(BF)
        d_v = dotf(probs.astype(BF), do_head, NN)
        d_k = dotf(d_scores, q_head, NN)
        d_value = d_v if d_value is None else d_value + d_v
        d_key = d_k if d_key is None else d_key + d_k
        d_query.append(dotf(k_t[rows_h, :], d_scores, NN))
    return jnp.concatenate(d_query, axis=0), d_key, d_value


def output_product(do_ref, o_ref, window):
    product = do_ref[window].astype(F32) * o_ref[window].astype(F32)
    return product.T


def peer_backward_kernel(
    need_ref, q_ref, k_ref, v_ref, do_ref, o_ref, low_ref, log_ref, dq_ref, dkv_ref, sums
):
    rows = q_ref.shape[0]
    key_count = k_ref.shape[0]
    sums[...] = jnp.zeros_like(sums)
    for index, r in enumerate(range(0, rows, QROWS)):
        needed = need_ref[index] < 0
        window = (slice(r, r + QROWS), slice(None))

        @pl.when(needed)
        def _():
            allowed = peer_mask(key_count, low_ref[:, r : r + QROWS], key_count)
            logs = [log_ref[0, h : h + 1, r : r + QROWS] for h in range(LANES // HDIM)]
            d_query, d_key, d_value = backward_block(
                q_ref[window],
                k_ref[...],
                v_ref[...],
                k_ref[...].T,
                do_ref[window],
                output_product(do_ref, o_ref, window),
                logs,
                allowed,
            )
            dq_ref[window] = d_query.T
            sums[0] += d_key
            sums[1] += d_value

        @pl.when(jnp.logical_not(needed))
        def _():
            dq_ref[window] = jnp.zeros((QROWS, LANES), F32)

    dkv_ref[...] = sums[...].astype(BF)


def peer_backward(need, q, kv, do, o, low_row, logs):
    rows, width = q.shape
    pairs = width // LANES
    return pl.pallas_call(
        peer_backward_kernel,
        name="peer_bwd",
        grid=(pairs,),
        out_shape=(
            jax.ShapeDtypeStruct((rows, width), F32),
            jax.ShapeDtypeStruct((2, rows, width), BF),
        ),
        in_specs=[
            SMEM_SPEC,
            pair_spec(rows),
            stacked_spec(rows, 0),
            stacked_spec(rows, 1),
            pair_spec(rows),
            pair_spec(rows),
            low_spec(rows),
            log_spec(rows),
        ],
        out_specs=(pair_spec(rows), pl.BlockSpec((2, rows, LANES), lambda i: (0, 0, i))),
        scratch_shapes=[pltpu.VMEM((2, rows, LANES), F32)],
        compiler_params=pltpu.CompilerParams(vmem_limit_bytes=VMEM_BYTES),
        cost_estimate=LIGHT,
    )(need, q, kv, kv, do, o, low_row, logs)


def own_backward_kernel(
    q_ref,
    k_ref,
    v_ref,
    do_ref,
    o_ref,
    low_ref,
    log_ref,
    dq_in_ref,
    cos_ref,
    sin_ref,
    dq_ref,
    dk_ref,
    dv_ref,
    sums,
):
    rows = q_ref.shape[0]
    sums[...] = jnp.zeros_like(sums)
    k_t = k_ref[...].T
    for r in range(0, rows, QROWS):
        count = r + QROWS
        window = (slice(r, r + QROWS), slice(None))
        allowed = own_mask(count, r, low_ref[:, r : r + QROWS])
        logs = [log_ref[0, h : h + 1, r : r + QROWS] for h in range(LANES // HDIM)]
        d_query, d_key, d_value = backward_block(
            q_ref[window],
            k_ref[0:count, :],
            v_ref[0:count, :],
            k_t[:, 0:count],
            do_ref[window],
            output_product(do_ref, o_ref, window),
            logs,
            allowed,
        )
        rotated = (d_query.T + dq_in_ref[window]) * (HDIM**-0.5)
        turned = rotated * cos_ref[window] - swap_halves(rotated) * sin_ref[window]
        dq_ref[window] = turned.astype(BF)
        sums[0, 0:count] += d_key
        sums[1, 0:count] += d_value
    dk_ref[...] = sums[0]
    dv_ref[...] = sums[1]


def own_backward(q, kv, do, o, low_row, logs, dq_in, cos, sin):
    rows, width = q.shape
    pairs = width // LANES
    table = pl.BlockSpec((rows, LANES), lambda i: (0, 0))
    return pl.pallas_call(
        own_backward_kernel,
        name="own_bwd",
        grid=(pairs,),
        out_shape=(
            jax.ShapeDtypeStruct((rows, width), BF),
            jax.ShapeDtypeStruct((rows, width), F32),
            jax.ShapeDtypeStruct((rows, width), F32),
        ),
        in_specs=[
            pair_spec(rows),
            stacked_spec(rows, 0),
            stacked_spec(rows, 1),
            pair_spec(rows),
            pair_spec(rows),
            low_spec(rows),
            log_spec(rows),
            pair_spec(rows),
            table,
            table,
        ],
        out_specs=(pair_spec(rows),) * 3,
        scratch_shapes=[pltpu.VMEM((2, rows, LANES), F32)],
        compiler_params=pltpu.CompilerParams(vmem_limit_bytes=VMEM_BYTES),
        cost_estimate=LIGHT,
    )(q, kv, kv, do, o, low_row, logs, dq_in, cos, sin)


def finish_keys_kernel(dk_ref, dv_ref, dk_in_ref, dv_in_ref, cos_ref, sin_ref, dk_out, dv_out):
    total = dk_ref[...] + dk_in_ref[...].astype(F32)
    turned = total * cos_ref[...] - swap_halves(total) * sin_ref[...]
    dk_out[...] = turned.astype(BF)
    dv_out[...] = (dv_ref[...] + dv_in_ref[...].astype(F32)).astype(BF)


def finish_keys(dk, dv, dkv_in, cos, sin):
    rows, width = dk.shape
    pairs = width // LANES
    table = pl.BlockSpec((rows, LANES), lambda i: (0, 0))
    return pl.pallas_call(
        finish_keys_kernel,
        name="finish_keys",
        grid=(pairs,),
        out_shape=(jax.ShapeDtypeStruct((rows, width), BF),) * 2,
        in_specs=[pair_spec(rows), pair_spec(rows), stacked_spec(rows, 0), stacked_spec(rows, 1)]
        + [table, table],
        out_specs=(pair_spec(rows),) * 2,
        cost_estimate=LIGHT,
    )(dk, dv, dkv_in, dkv_in, cos, sin)


def branch_kernel(stream_ref, att_ref, gain_ref, *refs):
    pieces, (hidden_ref, normed_ref, scale_ref) = refs[:4], refs[4:]
    for j, piece in enumerate(pieces):
        columns = piece_columns(j, piece.shape[1])
        term = dotf(att_ref[...], piece[...], NN)
        hidden_ref[:, columns] = stream_ref[:, columns].astype(F32) + term
    hidden = hidden_ref[...]
    mean = jnp.sum(hidden * hidden, axis=1, keepdims=True) / hidden.shape[1]
    scale = lax.rsqrt(mean + norm_eps)
    scale_ref[...] = scale
    normed_ref[...] = (hidden * scale * gain_ref[...]).astype(BF)


def add_branch(stream, att, gain, pieces):
    rows, depth = stream.shape
    heads = att.shape[1]
    tile = pl.BlockSpec((QROWS, depth), lambda i: (i, 0))
    return pl.pallas_call(
        branch_kernel,
        name="branch",
        grid=(rows // QROWS,),
        out_shape=(
            jax.ShapeDtypeStruct((rows, depth), F32),
            jax.ShapeDtypeStruct((rows, depth), BF),
            jax.ShapeDtypeStruct((rows, 1), F32),
        ),
        in_specs=[
            tile,
            pl.BlockSpec((QROWS, heads), lambda i: (i, 0)),
            pl.BlockSpec((1, depth), lambda i: (0, 0)),
        ]
        + [pl.BlockSpec(pieces[0].shape, lambda i: (0, 0))] * 4,
        out_specs=(tile, tile, pl.BlockSpec((QROWS, 1), lambda i: (i, 0))),
        compiler_params=pltpu.CompilerParams(vmem_limit_bytes=VMEM_BYTES),
        cost_estimate=LIGHT,
    )(stream, att, gain, *pieces)


def hidden_kernel(x_ref, *refs):
    w_in, (act_ref, by_gate_ref, by_up_ref) = refs[:4], refs[4:]
    rows = x_ref.shape[0]
    for r in range(0, rows, rows):
        part = slice(r, r + rows)
        gate = piece_dot(x_ref, part, [piece[0] for piece in w_in])
        up = piece_dot(x_ref, part, [piece[1] for piece in w_in])
        sig = jax.nn.sigmoid(gate)
        silu = gate * sig
        act_ref[part, :] = (silu * up).astype(BF)
        by_gate_ref[part, :] = (up * sig * (1.0 + gate * (1.0 - sig))).astype(BF)
        by_up_ref[part, :] = silu.astype(BF)


def hidden_units(x, w_in):
    rows, depth = x.shape
    _, size, units = w_in[0].shape
    tile = 256
    part = pl.BlockSpec((rows, tile), lambda i: (0, i))
    return pl.pallas_call(
        hidden_kernel,
        grid=(units // tile,),
        out_shape=(jax.ShapeDtypeStruct((rows, units), BF),) * 3,
        in_specs=[pl.BlockSpec((rows, depth), lambda i: (0, 0))]
        + [pl.BlockSpec((2, size, tile), lambda i: (0, 0, i))] * 4,
        out_specs=(part,) * 3,
        compiler_params=pltpu.CompilerParams(vmem_limit_bytes=VMEM_BYTES),
        cost_estimate=LIGHT,
        name="hidden",
    )(x, *w_in)


def hidden_back_kernel(cot_ref, by_gate_ref, by_up_ref, *refs):
    w_down, (dg_ref, du_ref) = refs[:4], refs[4:]
    rows = cot_ref.shape[0]
    for r in range(0, rows, rows):
        part = slice(r, r + rows)
        d_act = piece_dot(cot_ref, part, [piece[...] for piece in w_down], NT)
        dg_ref[part, :] = (d_act * by_gate_ref[part, :].astype(F32)).astype(BF)
        du_ref[part, :] = (d_act * by_up_ref[part, :].astype(F32)).astype(BF)


def hidden_back(cot, by_gate, by_up, w_down):
    rows, depth = cot.shape
    units, size = w_down[0].shape
    tile = 256
    part = pl.BlockSpec((rows, tile), lambda i: (0, i))
    return pl.pallas_call(
        hidden_back_kernel,
        grid=(units // tile,),
        out_shape=(jax.ShapeDtypeStruct((rows, units), BF),) * 2,
        in_specs=[pl.BlockSpec((rows, depth), lambda i: (0, 0)), part, part]
        + [pl.BlockSpec((tile, size), lambda i: (i, 0))] * 4,
        out_specs=(part,) * 2,
        compiler_params=pltpu.CompilerParams(vmem_limit_bytes=VMEM_BYTES),
        cost_estimate=LIGHT,
        name="hidden_back",
    )(cot, by_gate, by_up, *w_down)


def phased(i, block, make_index, tiles):
    def index_map(j, t):
        return make_index(jnp.where(j < i, 0, jnp.where(j == i, t, tiles - 1)))

    return pl.BlockSpec(block, index_map)


def columns_call(kernel_dot, lefts, pieces, block, make_index, size, flops, name):
    rows = lefts[0].shape[0]
    tile = min(size, 256)
    tiles = size // tile
    depth = size * 4

    def kernel(*refs):
        left_refs, piece_refs, out_ref = refs[: len(lefts)], refs[len(lefts) : -1], refs[-1]
        for j, piece in enumerate(piece_refs):

            @pl.when(pl.program_id(0) == j)
            def _():
                out_ref[...] = kernel_dot([left[...] for left in left_refs], piece).astype(BF)

    def out_index(j, t):
        return (0, (lax.axis_index("fsdp") ^ j) * tiles + t)

    return pl.pallas_call(
        kernel,
        grid=(4, tiles),
        out_shape=jax.ShapeDtypeStruct((rows, depth), BF),
        in_specs=[pl.BlockSpec(left.shape, lambda j, t: (0, 0)) for left in lefts]
        + [phased(i, block(tile), make_index, tiles) for i in range(4)],
        out_specs=pl.BlockSpec((rows, tile), out_index),
        compiler_params=pltpu.CompilerParams(vmem_limit_bytes=VMEM_BYTES),
        cost_estimate=LIGHT,
        name=name,
    )(*lefts, *pieces)


def stacked_columns(lefts, pieces, name):
    count, size, inner = pieces[0].shape

    def product(parts, piece):
        return sum(dotf(parts[c], piece[c], NT) for c in range(count))

    return columns_call(
        product,
        lefts,
        pieces,
        lambda tile: (count, tile, inner),
        lambda t: (0, t, 0),
        size,
        8 * lefts[0].shape[0] * size * inner * count,
        name,
    )


def plain_columns(left, pieces, name):
    inner, size = pieces[0].shape
    return columns_call(
        lambda parts, piece: dotf(parts[0], piece[...], NN),
        [left],
        pieces,
        lambda tile: (inner, tile),
        lambda t: (0, t),
        size,
        8 * left.shape[0] * size * inner,
        name,
    )


def branch_back_kernel(shares, d_mid_ref, hidden_ref, cot_ref, scale_ref, gain_ref, *refs):
    pieces, (d_hidden_ref, d_att_ref, gain_out_ref) = refs[:4], refs[4:7]
    d_mid = d_mid_ref[...].astype(F32)
    hidden = hidden_ref[...]
    scale = scale_ref[...]
    weighted = d_mid * gain_ref[...]
    inner = jnp.sum(weighted * hidden, axis=1, keepdims=True) / hidden.shape[1]
    d_hidden = (
        cot_ref[...].astype(F32) * (1.0 / shares)
        + scale * weighted
        - hidden * (scale * scale * scale * inner)
    )
    gain_term = jnp.sum(d_mid * hidden * scale, axis=0, keepdims=True)

    @pl.when(pl.program_id(0) == 0)
    def _():
        gain_out_ref[...] = gain_term

    @pl.when(pl.program_id(0) != 0)
    def _():
        gain_out_ref[...] += gain_term

    d_hidden_ref[...] = d_hidden.astype(BF)
    heads = d_att_ref.shape[1]
    for e in range(0, heads, 512):
        columns = slice(e, e + 512)
        d_att_ref[:, columns] = piece_dot(
            d_hidden_ref, slice(None), [piece[columns, :] for piece in pieces], NT
        ).astype(BF)


def branch_back(d_mid, hidden, cot, scale, gain, pieces):
    rows, depth = hidden.shape
    heads, size = pieces[0].shape
    tile = pl.BlockSpec((QROWS, depth), lambda i: (i, 0))
    row = pl.BlockSpec((1, depth), lambda i: (0, 0))
    return pl.pallas_call(
        functools.partial(branch_back_kernel, lax.axis_size("tensor")),
        name="branch_back",
        grid=(rows // QROWS,),
        in_specs=[tile, tile, tile, pl.BlockSpec((QROWS, 1), lambda i: (i, 0)), row]
        + [pl.BlockSpec((heads, size), lambda i: (0, 0))] * 4,
        out_specs=(tile, pl.BlockSpec((QROWS, heads), lambda i: (i, 0)), row),
        out_shape=(
            jax.ShapeDtypeStruct((rows, depth), BF),
            jax.ShapeDtypeStruct((rows, heads), BF),
            jax.ShapeDtypeStruct((1, depth), F32),
        ),
        compiler_params=pltpu.CompilerParams(vmem_limit_bytes=VMEM_BYTES),
        cost_estimate=LIGHT,
    )(d_mid, hidden, cot, scale, gain, *pieces)


def grad_call(left, right, cut, place, adds, name, span=(0, 1)):
    rows = left.shape[0]
    size = (left, right)[cut].shape[1] // 4
    swept = (right, left)[cut].shape[1] // span[1]
    height, width = (size, swept) if cut == 0 else (swept, size)
    tile = min(1024, swept)
    offset = span[0] * (swept // tile)
    block = (height, tile) if cut == 0 else (tile, width)

    def owner():
        return lax.axis_index("fsdp") ^ place

    def swept_index(t):
        return (0, t) if cut == 0 else (t, 0)

    def kernel(left_ref, right_ref, *refs):
        add_refs, out_ref = refs[: len(adds)], refs[len(adds)]
        if cut == 0:
            turned = refs[-1]

            @pl.when(pl.program_id(0) == 0)
            def _():
                turned[...] = left_ref[...].T

            result = dotf(turned[...], right_ref[...], NN)
        else:
            result = dotf(left_ref[...].T, right_ref[...], NN)
        for add in add_refs:
            result = result + add[...].astype(F32)
        out_ref[...] = result.astype(BF)

    fixed = pl.BlockSpec((rows, size), lambda t: (0, owner()))
    moving = pl.BlockSpec((rows, tile), lambda t: (0, t + offset))
    return pl.pallas_call(
        kernel,
        grid=(swept // tile,),
        out_shape=jax.ShapeDtypeStruct((height, width), BF),
        in_specs=[fixed, moving] * (cut == 0)
        + [moving, fixed] * (cut == 1)
        + [pl.BlockSpec(block, swept_index)] * len(adds),
        out_specs=pl.BlockSpec(block, swept_index),
        scratch_shapes=[pltpu.VMEM((size, rows), BF)] if cut == 0 else [],
        compiler_params=pltpu.CompilerParams(vmem_limit_bytes=VMEM_BYTES),
        cost_estimate=LIGHT,
        name=name,
    )(left, right, *adds)


class Reduction:
    def __init__(self, left, right, cut, name, span=(0, 1)):
        self.args, self.name, self.span = (left, right, cut), name, span

    def call(self, place, deps, step, adds=()):
        left, right, cut = self.args
        left = after(left, *deps) if deps else left
        return grad_call(left, right, cut, place, adds, self.name + step, self.span)

    def near_far(self, *deps):
        self.three = self.call(3, deps, "_3")
        self.for_two = swap(self.three, "fsdp", 1)

    def near(self, *deps):
        self.one = self.call(1, deps, "_1")
        self.for_own = swap(self.one, "fsdp", 1)

    def far(self, *deps):
        self.two = self.call(2, deps, "_2", [self.for_two])

    def send_far(self, *deps):
        self.across = swap(after(self.two, *deps), "fsdp", 2)

    def mine(self, *deps):
        self.own = self.call(0, deps, "_0", [self.for_own, self.across])

    def send_context(self, *deps):
        self.other = swap(after(self.own, *deps), "context", 1)


def totals_kernel(slots, *refs):
    pairs, out_ref = refs[:-1], refs[-1]
    for slot in range(len(pairs) // 2):
        total = pairs[2 * slot][...].astype(F32) + pairs[2 * slot + 1][...].astype(F32)
        if slots == 0:
            out_ref[slot] = total
        else:
            out_ref[:, slot, :] = total


def totals(sums, slots, *deps):
    arrays = [array for part in sums for array in (part.own, part.other)]
    if deps:
        arrays[0] = after(arrays[0], *deps)
    rows, width = arrays[0].shape
    tile = 128
    shape = [rows, width]
    shape.insert(slots, len(sums))
    block = [tile, width]
    block.insert(slots, len(sums))
    return pl.pallas_call(
        functools.partial(totals_kernel, slots),
        grid=(rows // tile,),
        out_shape=jax.ShapeDtypeStruct(tuple(shape), F32),
        in_specs=[pl.BlockSpec((tile, width), lambda i: (i, 0))] * len(arrays),
        out_specs=pl.BlockSpec(
            tuple(block), (lambda i: (0, i, 0)) if slots == 0 else (lambda i: (i, 0, 0))
        ),
        compiler_params=pltpu.CompilerParams(vmem_limit_bytes=VMEM_BYTES),
        cost_estimate=LIGHT,
        name="totals",
    )(*arrays)


def row_sum(values_in):
    return jnp.sum(values_in, axis=1, keepdims=True)


def per_device(tokens, w_qkv, w_out, w_gate_up, w_down, gains, seq_lengths, cotangent):
    row_count, part_width = tokens.shape
    tensor_index = lax.axis_index("tensor")
    context_index = lax.axis_index("context")
    full_width = part_width * lax.axis_size("tensor")

    def features(part_in):
        return lax.all_gather(part_in, "tensor", axis=1, tiled=True)

    def feature_sum(term):
        return lax.psum_scatter(term.astype(BF), "tensor", scatter_dimension=1, tiled=True)

    def own_features(full):
        return lax.dynamic_slice_in_dim(full, tensor_index * part_width, part_width, 1)

    ending = jnp.cumsum(seq_lengths[0])
    starts = ending - seq_lengths[0]
    places = context_index * row_count + jnp.arange(row_count, dtype=jnp.int32)
    first_token = jnp.max(jnp.where(starts[None, :] <= places[:, None], starts[None, :], 0), axis=1)
    cos, sin = rope_tables(places - first_token)
    low = first_token - context_index * row_count
    low_row = low[None, :]
    need = low[::QROWS]

    token_low = features(tokens)
    gain_near, gain_full = gather_gains(gains)
    gain_attn, gain_mlp = gain_full[0:1], gain_full[1:2]

    qkv_own = jnp.swapaxes(w_qkv, 0, 1)
    half = qkv_own.shape[1] // 2
    far_half = swap(
        lax.dynamic_slice_in_dim(after(qkv_own, gain_near), context_index * half, half, 1),
        "fsdp",
        2,
    )
    other_half = swap(far_half, "context", 1)
    qkv_far = jnp.where(
        context_index == 0,
        jnp.concatenate([far_half, other_half], axis=1),
        jnp.concatenate([other_half, far_half], axis=1),
    )
    qkv_near = swap(qkv_own, "fsdp", 1)
    qkv = (qkv_own, qkv_near, qkv_far, swap(qkv_far, "fsdp", 1))

    gate_up_own = jnp.swapaxes(w_gate_up, 0, 1)
    cut = gate_up_own.shape[1] * 12 // 32
    gate_up_a = swap(after(gate_up_own[:, :cut], far_half), "fsdp", 2)
    gate_up_b = swap(after(gate_up_own[:, cut:], gate_up_a), "fsdp", 2)

    keys_values, normed_in, scale_attn = project(
        after(token_low, gate_up_a), qkv, cos, sin, gain_attn, (1.0, None), 1, True
    )
    peer_kv = lax.ppermute(keys_values, "context", [(0, 1)])
    queries = project(normed_in, qkv, cos, sin, gain_attn, (HDIM**-0.5,), 0, False)[0][0]
    part, part_log = own_forward(queries, keys_values, low_row)
    out_own = lax.all_gather(after(w_out, token_low), "tensor", axis=0, tiled=True)
    out_near = swap(out_own, "fsdp", 1)
    attended, logs = peer_forward(
        need, queries, peer_kv, low_row, after(part, gate_up_b, out_near), part_log
    )
    attended_full = features(attended)

    out_far = swap(after(out_own, attended), "fsdp", 2)
    out_far_near = swap(out_far, "fsdp", 1)
    out = (out_own, out_near, out_far, out_far_near)
    gate_up_own, gate_up_a, gate_up_b = lax.optimization_barrier(
        (gate_up_own, gate_up_a, gate_up_b, attended)
    )[:3]
    gate_up_far = jnp.concatenate([gate_up_a, gate_up_b], axis=1)
    gate_up_near = swap(gate_up_own, "fsdp", 1)
    gate_up = (gate_up_own, gate_up_near, gate_up_far, swap(gate_up_far, "fsdp", 1))
    cot_full = features(after(cotangent, attended_full, out_far_near))
    down_far = swap(after(w_down, attended_full, out_far_near), "fsdp", 2)
    down_near = swap(after(w_down, attended_full), "fsdp", 1)
    hidden, normed_mid, scale_mlp = add_branch(token_low, attended_full, gain_mlp, out)

    activated, by_gate, by_up = hidden_units(normed_mid, gate_up)
    down_far = after(down_far, activated)
    down = (w_down, down_near, down_far, swap(down_far, "fsdp", 1))
    mlp_term = plain_columns(activated, down, "mlp_out")
    mlp_out = feature_sum(mlp_term)
    d_gate, d_up = hidden_back(after(cot_full, mlp_term), by_gate, by_up, down)
    d_mid_term = stacked_columns([d_gate, d_up], gate_up, "d_mid")
    d_hidden_term, d_att_term, gain_mlp_term = branch_back(
        d_mid_term, hidden, cot_full, scale_mlp, gain_mlp, out
    )
    d_attended = feature_sum(after(d_att_term, mlp_out))
    d_hidden_own = feature_sum(after(d_hidden_term, d_att_term))

    down_a, down_b = (
        Reduction(activated, cot_full, 1, "grad_down", (part_index, 2)) for part_index in (0, 1)
    )
    grad_gate = Reduction(normed_mid, d_gate, 0, "grad_gate")
    grad_up = Reduction(normed_mid, d_up, 0, "grad_up")
    square = lax.axis_size("tensor") == lax.axis_size("fsdp")
    down_a.near_far(d_att_term)
    down_b.near_far(down_a.three)
    grad_gate.near_far(down_b.three)
    down_a.far(grad_gate.three)
    down_a.send_far()
    down_b.far(down_a.two)
    down_b.send_far()
    down_a.near(down_b.two)
    down_b.near(down_a.one)
    grad_gate.far(down_b.one)
    grad_gate.send_far()
    grad_gate.near(grad_gate.two)
    down_a.mine(grad_gate.one)
    down_a.send_context()
    grad_up.near_far(down_a.own)
    grad_up.near(grad_up.three)
    grad_up.far(grad_up.one)
    grad_up.send_far()
    down_b.mine(grad_up.two)
    down_b.send_context()

    dq_peer, dkv_peer = peer_backward(
        need, queries, peer_kv, after(d_attended, down_b.own), attended, low_row, logs
    )
    dkv_in = lax.ppermute(dkv_peer, "context", [(1, 0)])
    d_query, dk_own, dv_own = own_backward(
        queries,
        keys_values,
        d_attended,
        attended,
        low_row,
        logs,
        after(dq_peer, down_a.other),
        cos,
        sin,
    )
    grad_query = Reduction(normed_in, d_query, 0, "grad_query")
    grad_query.near_far(down_b.other)
    grad_query.near(grad_query.three)
    grad_gate.mine(grad_query.one)
    grad_gate.send_context()
    d_key, d_value = finish_keys(
        dk_own, dv_own, after(dkv_in, grad_gate.own, d_hidden_own), cos, sin
    )
    d_in_term = stacked_columns([d_query, d_key, d_value], qkv, "d_in")
    d_in = feature_sum(d_in_term).astype(F32)

    if square:
        grad_out = Reduction(attended_full, d_hidden_own, 0, "grad_out")
    else:
        grad_out = Reduction(attended, features(d_hidden_own), 1, "grad_out")
    grad_query.far(d_in_term)
    grad_query.send_far()
    grad_key = Reduction(normed_in, d_key, 0, "grad_key")
    grad_value = Reduction(normed_in, d_value, 0, "grad_value")
    grad_key.near_far(grad_query.two)
    grad_value.near_far(grad_key.three)
    grad_key.near(grad_value.three)
    grad_value.near(grad_key.one)
    grad_up.mine(grad_value.one)
    grad_up.send_context()
    grad_key.far(grad_up.own)
    grad_key.send_far()
    grad_value.far(grad_key.two)
    grad_value.send_far()
    grad_out.near_far(grad_value.two, grad_gate.other)
    grad_out.near(grad_out.three)
    grad_out.far(grad_out.one)
    grad_out.send_far()
    grad_query.mine(grad_out.two)
    grad_query.send_context()

    stream = token_low.astype(F32)
    d_in_wide = after(d_in_term, grad_query.own).astype(F32)
    weighted = d_in_wide * stream
    inner_term = jnp.sum(weighted * gain_attn, axis=1)
    gain_attn_term = jnp.sum(weighted * scale_attn, axis=0)
    parts = lax.axis_size("tensor")
    totals_small = block_totals(
        jnp.concatenate(
            [
                jnp.broadcast_to(inner_term[None, :], (parts, row_count)),
                gain_attn_term.reshape(parts, part_width),
                gain_mlp_term.reshape(parts, part_width),
            ],
            axis=1,
        )[None]
    )
    inner_in = totals_small[0, :row_count][:, None] / full_width
    gain_sums = totals_small[0, row_count:].reshape(2, part_width)
    gain_sums = exchange(gain_sums, "fsdp", 1)
    gain_sums = exchange(gain_sums, "fsdp", 2)
    gain_sums = exchange(gain_sums, "context", 1)
    gain_width = gains.shape[1]
    grad_gains = lax.dynamic_slice_in_dim(
        gain_sums, lax.axis_index("fsdp") * gain_width, gain_width, 1
    )

    grad_down_sum = totals([down_a, down_b], 0, d_in_wide).reshape(w_down.shape)
    grad_key.mine(grad_down_sum, grad_up.other)
    grad_key.send_context()
    grad_value.mine(grad_key.own)
    grad_value.send_context()
    grad_out.mine(grad_value.own)
    if square:
        count = lax.axis_size("fsdp")
        across = [(i, (i % count) * count + i // count) for i in range(count * count)]
        grad_out.own = lax.ppermute(grad_out.own, ("fsdp", "tensor"), across)
    grad_out.send_context()
    grad_gate_up_sum = totals([grad_gate, grad_up], 1, grad_value.own)
    grad_qkv = totals([grad_query, grad_key, grad_value], 0, grad_gate_up_sum)
    grad_out_sum = totals([grad_out], 0, grad_qkv)[0]

    block_out = (own_features(hidden) + mlp_out.astype(F32)).astype(BF)
    own_tokens = tokens.astype(F32)
    grad_tokens = (
        d_hidden_own.astype(F32)
        + scale_attn * own_features(gain_attn) * d_in
        - own_tokens * scale_attn * scale_attn * scale_attn * inner_in
    ).astype(BF)
    return (
        block_out,
        grad_tokens,
        jnp.swapaxes(grad_qkv, 0, 1),
        grad_out_sum,
        grad_gate_up_sum,
        grad_down_sum,
        grad_gains,
    )


def solution(mesh):
    rows = P(("fsdp", "context"), "tensor")
    inner = P("fsdp", None, "tensor")
    outer = P("tensor", "fsdp")
    gain = P(None, ("tensor", "fsdp"))
    return jax.shard_map(
        per_device,
        mesh=mesh,
        in_specs=(rows, inner, outer, inner, outer, gain, P("fsdp", None), rows),
        out_specs=(rows, rows, inner, outer, inner, outer, gain),
        check_vma=False,
    )
```

```python
import functools

import jax
import jax.numpy as jnp
from jax import lax
from jax.experimental import pallas as pl
from jax.experimental.pallas import tpu as pltpu
from jax.sharding import PartitionSpec as P

HDIM = 64
LANES = 128
QROWS = 256
norm_eps = 1e-05
rope_base = 130000.0
masked_score = -1e30
BF = jnp.bfloat16
F32 = jnp.float32
VMEM_BYTES = 56 * 1024 * 1024
LIGHT = pl.CostEstimate(flops=1, bytes_accessed=1, transcendentals=0)


def dotf(a, b, dims):
    return lax.dot_general(a, b, (dims, ((), ())), preferred_element_type=F32)


NN = ((1,), (0,))
NT = ((1,), (1,))
TN = ((0,), (0,))


def swap(value, axis, bit):
    count = lax.axis_size(axis)
    return lax.ppermute(value, axis, [(i, i ^ bit) for i in range(count)])


def after(value, *others):
    return lax.optimization_barrier((value, *others))[0]


def shifted(value, axis):
    count = lax.axis_size(axis)
    return [
        lax.ppermute(value, axis, [(i, (i + step) % count) for i in range(count)])
        for step in range(1, count)
    ]


def exchange(value, axis, bit):
    return value + swap(value, axis, bit)


def join_kernel(axis, mode, *refs):
    pieces, out_ref = refs[:-1], refs[-1]
    count = len(pieces)
    me = lax.axis_index(axis)
    for step, piece in enumerate(pieces):
        size = piece.shape[1]
        place = (me ^ step) if mode == "xor" else (me - step + count) % count
        out_ref[:, pl.ds(pl.multiple_of(place * size, size), size)] = piece[...]


def join(pieces, axis, mode):
    rows, size = pieces[0].shape
    return pl.pallas_call(
        functools.partial(join_kernel, axis, mode),
        out_shape=jax.ShapeDtypeStruct((rows, size * len(pieces)), pieces[0].dtype),
        cost_estimate=LIGHT,
        name="join",
    )(*pieces)


def gather_gains(gains):
    if lax.axis_size("tensor") > 4 or gains.shape[1] % LANES:
        whole = lax.all_gather(gains, ("tensor", "fsdp"), axis=1, tiled=True).astype(F32)
        return gains, whole
    own = gains.astype(F32)
    part = join([own] + [swap(own, "fsdp", bit) for bit in (1, 2, 3)], "fsdp", "xor")
    return part, join([part] + shifted(part, "tensor"), "tensor", "shift")


def block_totals(blocks):
    count = lax.axis_size("tensor")
    me = lax.axis_index("tensor")
    if count > 4:
        return lax.dynamic_index_in_dim(lax.psum(blocks, "tensor"), me, 1, keepdims=False)

    def pick(place):
        return lax.dynamic_index_in_dim(blocks, place, 1, keepdims=False)

    total = pick(me)
    for step in range(1, count):
        moves = [(i, (i + step) % count) for i in range(count)]
        total = total + lax.ppermute(pick((me + step) % count), "tensor", moves)
    return total


def piece_columns(j, size):
    return pl.ds(pl.multiple_of((lax.axis_index("fsdp") ^ j) * size, size), size)


def swap_halves(block):
    lane = lax.broadcasted_iota(jnp.int32, block.shape, 1)
    up = pltpu.roll(block, LANES - HDIM // 2, 1)
    down = pltpu.roll(block, HDIM // 2, 1)
    return jnp.where((lane & (HDIM - 1)) < HDIM // 2, up, down)


def rope_tables(positions):
    lane = jnp.arange(LANES, dtype=jnp.int32)
    half = lane % (HDIM // 2)
    frequencies = rope_base ** (-2.0 * half.astype(F32) / HDIM)
    angles = positions.astype(F32)[:, None] * frequencies[None, :]
    sign = jnp.where((lane % HDIM) < HDIM // 2, -1.0, 1.0)
    return jnp.cos(angles), jnp.sin(angles) * sign[None, :]


def piece_dot(x_ref, rows, pieces, dims=NN):
    total = None
    for j, piece in enumerate(pieces):
        size = piece.shape[dims[1][0]]
        term = dotf(x_ref[rows, piece_columns(j, size)], piece, dims)
        total = term if total is None else total + term
    return total


def project_kernel(kinds, normalize, x_ref, *refs):
    pieces, (cos_ref, sin_ref, gain_ref), outs = refs[:4], refs[4:7], refs[7:]
    out_ref = outs[0]
    rows, width = out_ref.shape[1:]
    step = pl.program_id(0)
    if normalize:
        normed_ref, scale_ref = outs[1], outs[2]

        @pl.when(step == 0)
        def _():
            for r in range(0, rows, QROWS):
                part = slice(r, r + QROWS)
                stream = x_ref[part, :].astype(F32)
                mean = jnp.sum(stream * stream, axis=1, keepdims=True) / x_ref.shape[1]
                scale = lax.rsqrt(mean + norm_eps)
                scale_ref[part, :] = scale
                normed_ref[part, :] = (stream * scale * gain_ref[...]).astype(BF)

        x_ref = normed_ref
    for index, scale in enumerate(kinds):

        @pl.when(step == index)
        def _():
            for r in range(0, rows, rows):
                part = slice(r, r + rows)
                result = piece_dot(x_ref, part, [piece[0] for piece in pieces])
                for c in range(0, width, LANES):
                    block = result[:, c : c + LANES]
                    if scale:
                        block = block * cos_ref[part, :] + swap_halves(block) * sin_ref[part, :]
                    low = block.astype(BF)
                    if scale and scale != 1.0:
                        low = low * jnp.asarray(scale, BF)
                    out_ref[0, part, c : c + LANES] = low


def project(x, pieces, cos, sin, gain, kinds, first, normalize):
    rows, depth = x.shape
    _, size, width = pieces[0].shape
    flops = 2 * len(kinds) * rows * depth * width
    whole = pl.BlockSpec((rows, depth), lambda i: (0, 0))
    table = pl.BlockSpec((rows, LANES), lambda i: (0, 0))
    out_shape = [jax.ShapeDtypeStruct((len(kinds), rows, width), BF)]
    out_specs = [pl.BlockSpec((1, rows, width), lambda i: (i, 0, 0))]
    if normalize:
        out_shape += [jax.ShapeDtypeStruct((rows, depth), BF), jax.ShapeDtypeStruct((rows, 1), F32)]
        out_specs += [whole, pl.BlockSpec((rows, 1), lambda i: (0, 0))]
    return pl.pallas_call(
        functools.partial(project_kernel, kinds, normalize),
        name="project_kv" if normalize else "project_q",
        grid=(len(kinds),),
        out_shape=out_shape,
        in_specs=[whole]
        + [pl.BlockSpec((1, size, width), lambda i: (i + first, 0, 0))] * 4
        + [table, table, pl.BlockSpec((1, depth), lambda i: (0, 0))],
        out_specs=out_specs,
        compiler_params=pltpu.CompilerParams(vmem_limit_bytes=VMEM_BYTES),
        cost_estimate=LIGHT,
    )(x, *pieces, cos, sin, gain)


def head_mask(block, head):
    lane = lax.broadcasted_iota(jnp.int32, block.shape, 1)
    inside = (lane < HDIM) if head == 0 else (lane >= HDIM)
    return jnp.where(inside, block, jnp.zeros_like(block))


def own_mask(key_count, row0, low_row):
    key = lax.broadcasted_iota(jnp.int32, (key_count, QROWS), 0)
    query = row0 + lax.broadcasted_iota(jnp.int32, (key_count, QROWS), 1)
    return (key >= low_row) & (key <= query)


def peer_mask(key_count, low_row, offset):
    key = lax.broadcasted_iota(jnp.int32, (key_count, QROWS), 0) - offset
    return key >= low_row


def own_forward_kernel(q_ref, k_ref, v_ref, low_ref, out_ref, log_ref):
    rows = q_ref.shape[0]
    v_t = v_ref[...].T
    for r in range(0, rows, QROWS):
        count = r + QROWS
        allowed = own_mask(count, r, low_ref[:, r : r + QROWS])
        keys = k_ref[0:count, :]
        outs = []
        for head in range(LANES // HDIM):
            scores = dotf(keys, head_mask(q_ref[r : r + QROWS, :], head), NT)
            scores = jnp.where(allowed, scores, masked_score)
            peak = jnp.max(scores, axis=0, keepdims=True)
            weights = jnp.exp(scores - peak)
            total = jnp.sum(weights, axis=0, keepdims=True)
            part = dotf(v_t[head * HDIM : (head + 1) * HDIM, 0:count], weights.astype(BF), NN)
            outs.append(part / total)
            log_ref[0, head : head + 1, r : r + QROWS] = peak + jnp.log(total)
        out_ref[r : r + QROWS, :] = jnp.concatenate(outs, axis=0).T


def peer_forward_kernel(
    need_ref, q_ref, k_ref, v_ref, low_ref, part_ref, log_in_ref, out_ref, log_ref
):
    rows = q_ref.shape[0]
    key_count = k_ref.shape[0]
    for index, r in enumerate(range(0, rows, QROWS)):
        needed = need_ref[index] < 0

        @pl.when(needed)
        def _():
            v_t = v_ref[...].T
            allowed = peer_mask(key_count, low_ref[:, r : r + QROWS], key_count)
            before = part_ref[r : r + QROWS, :].T
            outs = []
            for head in range(LANES // HDIM):
                scores = dotf(k_ref[...], head_mask(q_ref[r : r + QROWS, :], head), NT)
                scores = jnp.where(allowed, scores, masked_score)
                log_own = log_in_ref[0, head : head + 1, r : r + QROWS]
                peak = jnp.maximum(jnp.max(scores, axis=0, keepdims=True), log_own)
                weights = jnp.exp(scores - peak)
                own_weight = jnp.exp(log_own - peak)
                total = jnp.sum(weights, axis=0, keepdims=True) + own_weight
                rows_h = slice(head * HDIM, (head + 1) * HDIM)
                part = dotf(v_t[rows_h, :], weights.astype(BF), NN)
                outs.append((part + before[rows_h, :] * own_weight) / total)
                log_ref[0, head : head + 1, r : r + QROWS] = peak + jnp.log(total)
            out_ref[r : r + QROWS, :] = jnp.concatenate(outs, axis=0).T.astype(BF)

        @pl.when(jnp.logical_not(needed))
        def _():
            out_ref[r : r + QROWS, :] = part_ref[r : r + QROWS, :].astype(BF)
            log_ref[:, :, r : r + QROWS] = log_in_ref[:, :, r : r + QROWS]


def pair_spec(rows):
    return pl.BlockSpec((rows, LANES), lambda i: (0, i))


def stacked_spec(rows, part):
    return pl.BlockSpec((None, rows, LANES), lambda i: (part, 0, i))


def log_spec(rows):
    return pl.BlockSpec((1, LANES // HDIM, rows), lambda i: (i, 0, 0))


def low_spec(rows):
    return pl.BlockSpec((1, rows), lambda i: (0, 0))


def own_forward(q, kv, low_row):
    rows, width = q.shape
    pairs = width // LANES
    return pl.pallas_call(
        own_forward_kernel,
        name="own_fwd",
        grid=(pairs,),
        out_shape=(
            jax.ShapeDtypeStruct((rows, width), F32),
            jax.ShapeDtypeStruct((pairs, LANES // HDIM, rows), F32),
        ),
        in_specs=[
            pair_spec(rows),
            stacked_spec(rows, 0),
            stacked_spec(rows, 1),
            low_spec(rows),
        ],
        out_specs=(pair_spec(rows), log_spec(rows)),
        compiler_params=pltpu.CompilerParams(vmem_limit_bytes=VMEM_BYTES),
        cost_estimate=LIGHT,
    )(q, kv, kv, low_row)


SMEM_SPEC = pl.BlockSpec(memory_space=pltpu.SMEM)


def peer_forward(need, q, kv, low_row, part, log_in):
    rows, width = q.shape
    pairs = width // LANES
    return pl.pallas_call(
        peer_forward_kernel,
        name="peer_fwd",
        grid=(pairs,),
        out_shape=(
            jax.ShapeDtypeStruct((rows, width), BF),
            jax.ShapeDtypeStruct((pairs, LANES // HDIM, rows), F32),
        ),
        in_specs=[
            SMEM_SPEC,
            pair_spec(rows),
            stacked_spec(rows, 0),
            stacked_spec(rows, 1),
            low_spec(rows),
            pair_spec(rows),
            log_spec(rows),
        ],
        out_specs=(pair_spec(rows), log_spec(rows)),
        compiler_params=pltpu.CompilerParams(vmem_limit_bytes=VMEM_BYTES),
        cost_estimate=LIGHT,
    )(need, q, kv, kv, low_row, part, log_in)


def backward_block(q_rows, k_rows, v_rows, k_t, do_rows, do_o_t, logs, allowed):
    d_query, d_key, d_value = [], None, None
    for head in range(LANES // HDIM):
        rows_h = slice(head * HDIM, (head + 1) * HDIM)
        q_head = head_mask(q_rows, head)
        do_head = head_mask(do_rows, head)
        scores = dotf(k_rows, q_head, NT)
        probs = jnp.exp(jnp.where(allowed, scores, masked_score) - logs[head])
        delta = jnp.sum(do_o_t[rows_h, :], axis=0, keepdims=True)
        d_probs = dotf(v_rows, do_head, NT)
        d_scores = (probs * (d_probs - delta)).astype(BF)
        d_v = dotf(probs.astype(BF), do_head, NN)
        d_k = dotf(d_scores, q_head, NN)
        d_value = d_v if d_value is None else d_value + d_v
        d_key = d_k if d_key is None else d_key + d_k
        d_query.append(dotf(k_t[rows_h, :], d_scores, NN))
    return jnp.concatenate(d_query, axis=0), d_key, d_value


def output_product(do_ref, o_ref, window):
    product = do_ref[window].astype(F32) * o_ref[window].astype(F32)
    return product.T


def peer_backward_kernel(
    need_ref, q_ref, k_ref, v_ref, do_ref, o_ref, low_ref, log_ref, dq_ref, dkv_ref, sums
):
    rows = q_ref.shape[0]
    key_count = k_ref.shape[0]
    sums[...] = jnp.zeros_like(sums)
    for index, r in enumerate(range(0, rows, QROWS)):
        needed = need_ref[index] < 0
        window = (slice(r, r + QROWS), slice(None))

        @pl.when(needed)
        def _():
            allowed = peer_mask(key_count, low_ref[:, r : r + QROWS], key_count)
            logs = [log_ref[0, h : h + 1, r : r + QROWS] for h in range(LANES // HDIM)]
            d_query, d_key, d_value = backward_block(
                q_ref[window],
                k_ref[...],
                v_ref[...],
                k_ref[...].T,
                do_ref[window],
                output_product(do_ref, o_ref, window),
                logs,
                allowed,
            )
            dq_ref[window] = d_query.T
            sums[0] += d_key
            sums[1] += d_value

        @pl.when(jnp.logical_not(needed))
        def _():
            dq_ref[window] = jnp.zeros((QROWS, LANES), F32)

    dkv_ref[...] = sums[...].astype(BF)


def peer_backward(need, q, kv, do, o, low_row, logs):
    rows, width = q.shape
    pairs = width // LANES
    return pl.pallas_call(
        peer_backward_kernel,
        name="peer_bwd",
        grid=(pairs,),
        out_shape=(
            jax.ShapeDtypeStruct((rows, width), F32),
            jax.ShapeDtypeStruct((2, rows, width), BF),
        ),
        in_specs=[
            SMEM_SPEC,
            pair_spec(rows),
            stacked_spec(rows, 0),
            stacked_spec(rows, 1),
            pair_spec(rows),
            pair_spec(rows),
            low_spec(rows),
            log_spec(rows),
        ],
        out_specs=(pair_spec(rows), pl.BlockSpec((2, rows, LANES), lambda i: (0, 0, i))),
        scratch_shapes=[pltpu.VMEM((2, rows, LANES), F32)],
        compiler_params=pltpu.CompilerParams(vmem_limit_bytes=VMEM_BYTES),
        cost_estimate=LIGHT,
    )(need, q, kv, kv, do, o, low_row, logs)


def own_backward_kernel(
    q_ref,
    k_ref,
    v_ref,
    do_ref,
    o_ref,
    low_ref,
    log_ref,
    dq_in_ref,
    cos_ref,
    sin_ref,
    dq_ref,
    dk_ref,
    dv_ref,
    sums,
):
    rows = q_ref.shape[0]
    sums[...] = jnp.zeros_like(sums)
    k_t = k_ref[...].T
    for r in range(0, rows, QROWS):
        count = r + QROWS
        window = (slice(r, r + QROWS), slice(None))
        allowed = own_mask(count, r, low_ref[:, r : r + QROWS])
        logs = [log_ref[0, h : h + 1, r : r + QROWS] for h in range(LANES // HDIM)]
        d_query, d_key, d_value = backward_block(
            q_ref[window],
            k_ref[0:count, :],
            v_ref[0:count, :],
            k_t[:, 0:count],
            do_ref[window],
            output_product(do_ref, o_ref, window),
            logs,
            allowed,
        )
        rotated = (d_query.T + dq_in_ref[window]) * (HDIM**-0.5)
        turned = rotated * cos_ref[window] - swap_halves(rotated) * sin_ref[window]
        dq_ref[window] = turned.astype(BF)
        sums[0, 0:count] += d_key
        sums[1, 0:count] += d_value
    dk_ref[...] = sums[0]
    dv_ref[...] = sums[1]


def own_backward(q, kv, do, o, low_row, logs, dq_in, cos, sin):
    rows, width = q.shape
    pairs = width // LANES
    table = pl.BlockSpec((rows, LANES), lambda i: (0, 0))
    return pl.pallas_call(
        own_backward_kernel,
        name="own_bwd",
        grid=(pairs,),
        out_shape=(
            jax.ShapeDtypeStruct((rows, width), BF),
            jax.ShapeDtypeStruct((rows, width), F32),
            jax.ShapeDtypeStruct((rows, width), F32),
        ),
        in_specs=[
            pair_spec(rows),
            stacked_spec(rows, 0),
            stacked_spec(rows, 1),
            pair_spec(rows),
            pair_spec(rows),
            low_spec(rows),
            log_spec(rows),
            pair_spec(rows),
            table,
            table,
        ],
        out_specs=(pair_spec(rows),) * 3,
        scratch_shapes=[pltpu.VMEM((2, rows, LANES), F32)],
        compiler_params=pltpu.CompilerParams(vmem_limit_bytes=VMEM_BYTES),
        cost_estimate=LIGHT,
    )(q, kv, kv, do, o, low_row, logs, dq_in, cos, sin)


def finish_keys_kernel(dk_ref, dv_ref, dk_in_ref, dv_in_ref, cos_ref, sin_ref, dk_out, dv_out):
    total = dk_ref[...] + dk_in_ref[...].astype(F32)
    turned = total * cos_ref[...] - swap_halves(total) * sin_ref[...]
    dk_out[...] = turned.astype(BF)
    dv_out[...] = (dv_ref[...] + dv_in_ref[...].astype(F32)).astype(BF)


def finish_keys(dk, dv, dkv_in, cos, sin):
    rows, width = dk.shape
    pairs = width // LANES
    table = pl.BlockSpec((rows, LANES), lambda i: (0, 0))
    return pl.pallas_call(
        finish_keys_kernel,
        name="finish_keys",
        grid=(pairs,),
        out_shape=(jax.ShapeDtypeStruct((rows, width), BF),) * 2,
        in_specs=[pair_spec(rows), pair_spec(rows), stacked_spec(rows, 0), stacked_spec(rows, 1)]
        + [table, table],
        out_specs=(pair_spec(rows),) * 2,
        cost_estimate=LIGHT,
    )(dk, dv, dkv_in, dkv_in, cos, sin)


def branch_kernel(stream_ref, att_ref, gain_ref, *refs):
    pieces, (hidden_ref, normed_ref, scale_ref) = refs[:4], refs[4:]
    for j, piece in enumerate(pieces):
        columns = piece_columns(j, piece.shape[1])
        term = dotf(att_ref[...], piece[...], NN)
        hidden_ref[:, columns] = stream_ref[:, columns].astype(F32) + term
    hidden = hidden_ref[...]
    mean = jnp.sum(hidden * hidden, axis=1, keepdims=True) / hidden.shape[1]
    scale = lax.rsqrt(mean + norm_eps)
    scale_ref[...] = scale
    normed_ref[...] = (hidden * scale * gain_ref[...]).astype(BF)


def add_branch(stream, att, gain, pieces):
    rows, depth = stream.shape
    heads = att.shape[1]
    tile = pl.BlockSpec((QROWS, depth), lambda i: (i, 0))
    return pl.pallas_call(
        branch_kernel,
        name="branch",
        grid=(rows // QROWS,),
        out_shape=(
            jax.ShapeDtypeStruct((rows, depth), F32),
            jax.ShapeDtypeStruct((rows, depth), BF),
            jax.ShapeDtypeStruct((rows, 1), F32),
        ),
        in_specs=[
            tile,
            pl.BlockSpec((QROWS, heads), lambda i: (i, 0)),
            pl.BlockSpec((1, depth), lambda i: (0, 0)),
        ]
        + [pl.BlockSpec(pieces[0].shape, lambda i: (0, 0))] * 4,
        out_specs=(tile, tile, pl.BlockSpec((QROWS, 1), lambda i: (i, 0))),
        compiler_params=pltpu.CompilerParams(vmem_limit_bytes=VMEM_BYTES),
        cost_estimate=LIGHT,
    )(stream, att, gain, *pieces)


def hidden_kernel(x_ref, *refs):
    w_in, (act_ref, by_gate_ref, by_up_ref) = refs[:4], refs[4:]
    rows = x_ref.shape[0]
    for r in range(0, rows, rows):
        part = slice(r, r + rows)
        gate = piece_dot(x_ref, part, [piece[0] for piece in w_in])
        up = piece_dot(x_ref, part, [piece[1] for piece in w_in])
        sig = jax.nn.sigmoid(gate)
        silu = gate * sig
        act_ref[part, :] = (silu * up).astype(BF)
        by_gate_ref[part, :] = (up * sig * (1.0 + gate * (1.0 - sig))).astype(BF)
        by_up_ref[part, :] = silu.astype(BF)


def hidden_units(x, w_in):
    rows, depth = x.shape
    _, size, units = w_in[0].shape
    tile = 256
    part = pl.BlockSpec((rows, tile), lambda i: (0, i))
    return pl.pallas_call(
        hidden_kernel,
        grid=(units // tile,),
        out_shape=(jax.ShapeDtypeStruct((rows, units), BF),) * 3,
        in_specs=[pl.BlockSpec((rows, depth), lambda i: (0, 0))]
        + [pl.BlockSpec((2, size, tile), lambda i: (0, 0, i))] * 4,
        out_specs=(part,) * 3,
        compiler_params=pltpu.CompilerParams(vmem_limit_bytes=VMEM_BYTES),
        cost_estimate=LIGHT,
        name="hidden",
    )(x, *w_in)


def hidden_back_kernel(cot_ref, by_gate_ref, by_up_ref, *refs):
    w_down, (dg_ref, du_ref) = refs[:4], refs[4:]
    rows = cot_ref.shape[0]
    for r in range(0, rows, rows):
        part = slice(r, r + rows)
        d_act = piece_dot(cot_ref, part, [piece[...] for piece in w_down], NT)
        dg_ref[part, :] = (d_act * by_gate_ref[part, :].astype(F32)).astype(BF)
        du_ref[part, :] = (d_act * by_up_ref[part, :].astype(F32)).astype(BF)


def hidden_back(cot, by_gate, by_up, w_down):
    rows, depth = cot.shape
    units, size = w_down[0].shape
    tile = 256
    part = pl.BlockSpec((rows, tile), lambda i: (0, i))
    return pl.pallas_call(
        hidden_back_kernel,
        grid=(units // tile,),
        out_shape=(jax.ShapeDtypeStruct((rows, units), BF),) * 2,
        in_specs=[pl.BlockSpec((rows, depth), lambda i: (0, 0)), part, part]
        + [pl.BlockSpec((tile, size), lambda i: (i, 0))] * 4,
        out_specs=(part,) * 2,
        compiler_params=pltpu.CompilerParams(vmem_limit_bytes=VMEM_BYTES),
        cost_estimate=LIGHT,
        name="hidden_back",
    )(cot, by_gate, by_up, *w_down)


def phased(i, block, make_index, tiles):
    def index_map(j, t):
        return make_index(jnp.where(j < i, 0, jnp.where(j == i, t, tiles - 1)))

    return pl.BlockSpec(block, index_map)


def columns_call(kernel_dot, lefts, pieces, block, make_index, size, flops, name):
    rows = lefts[0].shape[0]
    tile = min(size, 256)
    tiles = size // tile
    depth = size * 4

    def kernel(*refs):
        left_refs, piece_refs, out_ref = refs[: len(lefts)], refs[len(lefts) : -1], refs[-1]
        for j, piece in enumerate(piece_refs):

            @pl.when(pl.program_id(0) == j)
            def _():
                out_ref[...] = kernel_dot([left[...] for left in left_refs], piece).astype(BF)

    def out_index(j, t):
        return (0, (lax.axis_index("fsdp") ^ j) * tiles + t)

    return pl.pallas_call(
        kernel,
        grid=(4, tiles),
        out_shape=jax.ShapeDtypeStruct((rows, depth), BF),
        in_specs=[pl.BlockSpec(left.shape, lambda j, t: (0, 0)) for left in lefts]
        + [phased(i, block(tile), make_index, tiles) for i in range(4)],
        out_specs=pl.BlockSpec((rows, tile), out_index),
        compiler_params=pltpu.CompilerParams(vmem_limit_bytes=VMEM_BYTES),
        cost_estimate=LIGHT,
        name=name,
    )(*lefts, *pieces)


def stacked_columns(lefts, pieces, name):
    count, size, inner = pieces[0].shape

    def product(parts, piece):
        return sum(dotf(parts[c], piece[c], NT) for c in range(count))

    return columns_call(
        product,
        lefts,
        pieces,
        lambda tile: (count, tile, inner),
        lambda t: (0, t, 0),
        size,
        8 * lefts[0].shape[0] * size * inner * count,
        name,
    )


def plain_columns(left, pieces, name):
    inner, size = pieces[0].shape
    return columns_call(
        lambda parts, piece: dotf(parts[0], piece[...], NN),
        [left],
        pieces,
        lambda tile: (inner, tile),
        lambda t: (0, t),
        size,
        8 * left.shape[0] * size * inner,
        name,
    )


def branch_back_kernel(shares, d_mid_ref, hidden_ref, cot_ref, scale_ref, gain_ref, *refs):
    pieces, (d_hidden_ref, d_att_ref, gain_out_ref) = refs[:4], refs[4:7]
    d_mid = d_mid_ref[...].astype(F32)
    hidden = hidden_ref[...]
    scale = scale_ref[...]
    weighted = d_mid * gain_ref[...]
    inner = jnp.sum(weighted * hidden, axis=1, keepdims=True) / hidden.shape[1]
    d_hidden = (
        cot_ref[...].astype(F32) * (1.0 / shares)
        + scale * weighted
        - hidden * (scale * scale * scale * inner)
    )
    gain_term = jnp.sum(d_mid * hidden * scale, axis=0, keepdims=True)

    @pl.when(pl.program_id(0) == 0)
    def _():
        gain_out_ref[...] = gain_term

    @pl.when(pl.program_id(0) != 0)
    def _():
        gain_out_ref[...] += gain_term

    d_hidden_ref[...] = d_hidden.astype(BF)
    heads = d_att_ref.shape[1]
    for e in range(0, heads, 512):
        columns = slice(e, e + 512)
        d_att_ref[:, columns] = piece_dot(
            d_hidden_ref, slice(None), [piece[columns, :] for piece in pieces], NT
        ).astype(BF)


def branch_back(d_mid, hidden, cot, scale, gain, pieces):
    rows, depth = hidden.shape
    heads, size = pieces[0].shape
    tile = pl.BlockSpec((QROWS, depth), lambda i: (i, 0))
    row = pl.BlockSpec((1, depth), lambda i: (0, 0))
    return pl.pallas_call(
        functools.partial(branch_back_kernel, lax.axis_size("tensor")),
        name="branch_back",
        grid=(rows // QROWS,),
        in_specs=[tile, tile, tile, pl.BlockSpec((QROWS, 1), lambda i: (i, 0)), row]
        + [pl.BlockSpec((heads, size), lambda i: (0, 0))] * 4,
        out_specs=(tile, pl.BlockSpec((QROWS, heads), lambda i: (i, 0)), row),
        out_shape=(
            jax.ShapeDtypeStruct((rows, depth), BF),
            jax.ShapeDtypeStruct((rows, heads), BF),
            jax.ShapeDtypeStruct((1, depth), F32),
        ),
        compiler_params=pltpu.CompilerParams(vmem_limit_bytes=VMEM_BYTES),
        cost_estimate=LIGHT,
    )(d_mid, hidden, cot, scale, gain, *pieces)


def grad_call(left, right, cut, place, adds, name, span=(0, 1)):
    rows = left.shape[0]
    size = (left, right)[cut].shape[1] // 4
    swept = (right, left)[cut].shape[1] // span[1]
    height, width = (size, swept) if cut == 0 else (swept, size)
    tile = min(1024, swept)
    offset = span[0] * (swept // tile)
    block = (height, tile) if cut == 0 else (tile, width)

    def owner():
        return lax.axis_index("fsdp") ^ place

    def swept_index(t):
        return (0, t) if cut == 0 else (t, 0)

    def kernel(left_ref, right_ref, *refs):
        add_refs, out_ref = refs[: len(adds)], refs[len(adds)]
        if cut == 0:
            turned = refs[-1]

            @pl.when(pl.program_id(0) == 0)
            def _():
                turned[...] = left_ref[...].T

            result = dotf(turned[...], right_ref[...], NN)
        else:
            result = dotf(left_ref[...].T, right_ref[...], NN)
        for add in add_refs:
            result = result + add[...].astype(F32)
        out_ref[...] = result.astype(BF)

    fixed = pl.BlockSpec((rows, size), lambda t: (0, owner()))
    moving = pl.BlockSpec((rows, tile), lambda t: (0, t + offset))
    return pl.pallas_call(
        kernel,
        grid=(swept // tile,),
        out_shape=jax.ShapeDtypeStruct((height, width), BF),
        in_specs=[fixed, moving] * (cut == 0)
        + [moving, fixed] * (cut == 1)
        + [pl.BlockSpec(block, swept_index)] * len(adds),
        out_specs=pl.BlockSpec(block, swept_index),
        scratch_shapes=[pltpu.VMEM((size, rows), BF)] if cut == 0 else [],
        compiler_params=pltpu.CompilerParams(vmem_limit_bytes=VMEM_BYTES),
        cost_estimate=LIGHT,
        name=name,
    )(left, right, *adds)


class Reduction:
    def __init__(self, left, right, cut, name, span=(0, 1)):
        self.args, self.name, self.span = (left, right, cut), name, span

    def call(self, place, deps, step, adds=()):
        left, right, cut = self.args
        left = after(left, *deps) if deps else left
        return grad_call(left, right, cut, place, adds, self.name + step, self.span)

    def near_far(self, *deps):
        self.three = self.call(3, deps, "_3")
        self.for_two = swap(self.three, "fsdp", 1)

    def near(self, *deps):
        self.one = self.call(1, deps, "_1")
        self.for_own = swap(self.one, "fsdp", 1)

    def far(self, *deps):
        self.two = self.call(2, deps, "_2", [self.for_two])

    def send_far(self, *deps):
        self.across = swap(after(self.two, *deps), "fsdp", 2)

    def mine(self, *deps):
        self.own = self.call(0, deps, "_0", [self.for_own, self.across])

    def send_context(self, *deps):
        self.other = swap(after(self.own, *deps), "context", 1)


def totals_kernel(slots, *refs):
    pairs, out_ref = refs[:-1], refs[-1]
    for slot in range(len(pairs) // 2):
        total = pairs[2 * slot][...].astype(F32) + pairs[2 * slot + 1][...].astype(F32)
        if slots == 0:
            out_ref[slot] = total
        else:
            out_ref[:, slot, :] = total


def totals(sums, slots, *deps):
    arrays = [array for part in sums for array in (part.own, part.other)]
    if deps:
        arrays[0] = after(arrays[0], *deps)
    rows, width = arrays[0].shape
    tile = 128
    shape = [rows, width]
    shape.insert(slots, len(sums))
    block = [tile, width]
    block.insert(slots, len(sums))
    return pl.pallas_call(
        functools.partial(totals_kernel, slots),
        grid=(rows // tile,),
        out_shape=jax.ShapeDtypeStruct(tuple(shape), F32),
        in_specs=[pl.BlockSpec((tile, width), lambda i: (i, 0))] * len(arrays),
        out_specs=pl.BlockSpec(
            tuple(block), (lambda i: (0, i, 0)) if slots == 0 else (lambda i: (i, 0, 0))
        ),
        compiler_params=pltpu.CompilerParams(vmem_limit_bytes=VMEM_BYTES),
        cost_estimate=LIGHT,
        name="totals",
    )(*arrays)


def row_sum(values_in):
    return jnp.sum(values_in, axis=1, keepdims=True)


def per_device(tokens, w_qkv, w_out, w_gate_up, w_down, gains, seq_lengths, cotangent):
    row_count, part_width = tokens.shape
    tensor_index = lax.axis_index("tensor")
    context_index = lax.axis_index("context")
    full_width = part_width * lax.axis_size("tensor")

    def features(part_in):
        return lax.all_gather(part_in, "tensor", axis=1, tiled=True)

    def feature_sum(term):
        return lax.psum_scatter(term.astype(BF), "tensor", scatter_dimension=1, tiled=True)

    def own_features(full):
        return lax.dynamic_slice_in_dim(full, tensor_index * part_width, part_width, 1)

    ending = jnp.cumsum(seq_lengths[0])
    starts = ending - seq_lengths[0]
    places = context_index * row_count + jnp.arange(row_count, dtype=jnp.int32)
    first_token = jnp.max(jnp.where(starts[None, :] <= places[:, None], starts[None, :], 0), axis=1)
    cos, sin = rope_tables(places - first_token)
    low = first_token - context_index * row_count
    low_row = low[None, :]
    need = low[::QROWS]

    token_low = features(tokens)
    gain_near, gain_full = gather_gains(gains)
    gain_attn, gain_mlp = gain_full[0:1], gain_full[1:2]

    qkv_own = jnp.swapaxes(w_qkv, 0, 1)
    half = qkv_own.shape[1] // 2
    far_half = swap(
        lax.dynamic_slice_in_dim(after(qkv_own, gain_near), context_index * half, half, 1),
        "fsdp",
        2,
    )
    other_half = swap(far_half, "context", 1)
    qkv_far = jnp.where(
        context_index == 0,
        jnp.concatenate([far_half, other_half], axis=1),
        jnp.concatenate([other_half, far_half], axis=1),
    )
    qkv_near = swap(qkv_own, "fsdp", 1)
    qkv = (qkv_own, qkv_near, qkv_far, swap(qkv_far, "fsdp", 1))

    gate_up_own = jnp.swapaxes(w_gate_up, 0, 1)
    cut = gate_up_own.shape[1] * 12 // 32
    gate_up_a = swap(after(gate_up_own[:, :cut], far_half), "fsdp", 2)
    gate_up_b = swap(after(gate_up_own[:, cut:], gate_up_a), "fsdp", 2)

    keys_values, normed_in, scale_attn = project(
        after(token_low, gate_up_a), qkv, cos, sin, gain_attn, (1.0, None), 1, True
    )
    peer_kv = lax.ppermute(keys_values, "context", [(0, 1)])
    queries = project(normed_in, qkv, cos, sin, gain_attn, (HDIM**-0.5,), 0, False)[0][0]
    part, part_log = own_forward(queries, keys_values, low_row)
    attended, logs = peer_forward(
        need, queries, peer_kv, low_row, after(part, gate_up_b), part_log
    )
    attended_full = features(attended)

    out_own = after(lax.all_gather(w_out, "tensor", axis=0, tiled=True), attended)
    out_near = swap(out_own, "fsdp", 1)
    out_far = swap(out_own, "fsdp", 2)
    out_far_near = swap(out_far, "fsdp", 1)
    out = (out_own, out_near, out_far, out_far_near)
    gate_up_own, gate_up_a, gate_up_b = lax.optimization_barrier(
        (gate_up_own, gate_up_a, gate_up_b, attended)
    )[:3]
    gate_up_far = jnp.concatenate([gate_up_a, gate_up_b], axis=1)
    gate_up_near = swap(gate_up_own, "fsdp", 1)
    gate_up = (gate_up_own, gate_up_near, gate_up_far, swap(gate_up_far, "fsdp", 1))
    cot_full = features(after(cotangent, attended_full, out_far_near, out_near))
    down_far = swap(after(w_down, attended_full, out_far_near), "fsdp", 2)
    down_near = swap(after(w_down, attended_full), "fsdp", 1)
    hidden, normed_mid, scale_mlp = add_branch(token_low, attended_full, gain_mlp, out)

    activated, by_gate, by_up = hidden_units(normed_mid, gate_up)
    down_far = after(down_far, activated)
    down = (w_down, down_near, down_far, swap(down_far, "fsdp", 1))
    mlp_term = plain_columns(activated, down, "mlp_out")
    mlp_out = feature_sum(mlp_term)
    d_gate, d_up = hidden_back(after(cot_full, mlp_term), by_gate, by_up, down)
    d_mid_term = stacked_columns([d_gate, d_up], gate_up, "d_mid")
    d_hidden_term, d_att_term, gain_mlp_term = branch_back(
        d_mid_term, hidden, cot_full, scale_mlp, gain_mlp, out
    )
    d_attended = feature_sum(after(d_att_term, mlp_out))
    d_hidden_own = feature_sum(after(d_hidden_term, d_att_term))

    down_a, down_b = (
        Reduction(activated, cot_full, 1, "grad_down", (part_index, 2)) for part_index in (0, 1)
    )
    grad_gate = Reduction(normed_mid, d_gate, 0, "grad_gate")
    grad_up = Reduction(normed_mid, d_up, 0, "grad_up")
    square = lax.axis_size("tensor") == lax.axis_size("fsdp")
    down_a.near_far(d_att_term)
    down_b.near_far(down_a.three)
    grad_gate.near_far(down_b.three)
    down_a.far(grad_gate.three)
    down_a.send_far()
    down_b.far(down_a.two)
    down_b.send_far()
    down_a.near(down_b.two)
    down_b.near(down_a.one)
    grad_gate.far(down_b.one)
    grad_gate.send_far()
    grad_gate.near(grad_gate.two)
    down_a.mine(grad_gate.one)
    down_a.send_context()
    grad_up.near_far(down_a.own)
    grad_up.near(grad_up.three)
    grad_up.far(grad_up.one)
    grad_up.send_far()

    dq_peer, dkv_peer = peer_backward(
        need, queries, peer_kv, after(d_attended, grad_up.two, down_a.other), attended, low_row, logs
    )
    dkv_in = lax.ppermute(dkv_peer, "context", [(1, 0)])
    d_query, dk_own, dv_own = own_backward(
        queries,
        keys_values,
        d_attended,
        attended,
        low_row,
        logs,
        dq_peer,
        cos,
        sin,
    )
    grad_query = Reduction(normed_in, d_query, 0, "grad_query")
    down_b.mine(d_query)
    down_b.send_context()
    grad_query.near_far(down_b.own)
    grad_query.near(grad_query.three)
    d_key, d_value = finish_keys(
        dk_own, dv_own, after(dkv_in, grad_query.one, d_hidden_own), cos, sin
    )
    d_in_term = stacked_columns([d_query, d_key, d_value], qkv, "d_in")
    d_in = feature_sum(d_in_term).astype(F32)

    if square:
        grad_out = Reduction(attended_full, d_hidden_own, 0, "grad_out")
    else:
        grad_out = Reduction(attended, features(d_hidden_own), 1, "grad_out")
    grad_gate.mine(d_in_term, down_b.other)
    grad_gate.send_context()
    grad_query.far(grad_gate.own)
    grad_query.send_far()
    grad_key = Reduction(normed_in, d_key, 0, "grad_key")
    grad_value = Reduction(normed_in, d_value, 0, "grad_value")
    grad_key.near_far(grad_query.two)
    grad_value.near_far(grad_key.three)
    grad_key.near(grad_value.three)
    grad_value.near(grad_key.one)
    grad_up.mine(grad_value.one)
    grad_up.send_context()
    grad_key.far(grad_up.own)
    grad_key.send_far()
    grad_value.far(grad_key.two)
    grad_value.send_far()
    grad_out.near_far(grad_value.two, grad_gate.other)
    grad_out.near(grad_out.three)
    grad_out.far(grad_out.one)
    grad_out.send_far()
    grad_query.mine(grad_out.two)
    grad_query.send_context()

    stream = token_low.astype(F32)
    d_in_wide = after(d_in_term, grad_query.own).astype(F32)
    weighted = d_in_wide * stream
    inner_term = jnp.sum(weighted * gain_attn, axis=1)
    gain_attn_term = jnp.sum(weighted * scale_attn, axis=0)
    parts = lax.axis_size("tensor")
    totals_small = block_totals(
        jnp.concatenate(
            [
                jnp.broadcast_to(inner_term[None, :], (parts, row_count)),
                gain_attn_term.reshape(parts, part_width),
                gain_mlp_term.reshape(parts, part_width),
            ],
            axis=1,
        )[None]
    )
    inner_in = totals_small[0, :row_count][:, None] / full_width
    gain_sums = totals_small[0, row_count:].reshape(2, part_width)
    gain_sums = exchange(gain_sums, "fsdp", 1)
    gain_sums = exchange(gain_sums, "fsdp", 2)
    gain_sums = exchange(gain_sums, "context", 1)
    gain_width = gains.shape[1]
    grad_gains = lax.dynamic_slice_in_dim(
        gain_sums, lax.axis_index("fsdp") * gain_width, gain_width, 1
    )

    grad_down_sum = totals([down_a, down_b], 0, d_in_wide).reshape(w_down.shape)
    grad_key.mine(grad_down_sum, grad_up.other)
    grad_key.send_context()
    grad_value.mine(grad_key.own)
    grad_value.send_context()
    grad_out.mine(grad_value.own)
    if square:
        count = lax.axis_size("fsdp")
        across = [(i, (i % count) * count + i // count) for i in range(count * count)]
        grad_out.own = lax.ppermute(grad_out.own, ("fsdp", "tensor"), across)
    grad_out.send_context()
    grad_gate_up_sum = totals([grad_gate, grad_up], 1, grad_value.own)
    grad_qkv = totals([grad_query, grad_key, grad_value], 0, grad_gate_up_sum)
    grad_out_sum = totals([grad_out], 0, grad_qkv)[0]

    block_out = (own_features(hidden) + mlp_out.astype(F32)).astype(BF)
    own_tokens = tokens.astype(F32)
    grad_tokens = (
        d_hidden_own.astype(F32)
        + scale_attn * own_features(gain_attn) * d_in
        - own_tokens * scale_attn * scale_attn * scale_attn * inner_in
    ).astype(BF)
    return (
        block_out,
        grad_tokens,
        jnp.swapaxes(grad_qkv, 0, 1),
        grad_out_sum,
        grad_gate_up_sum,
        grad_down_sum,
        grad_gains,
    )


def solution(mesh):
    rows = P(("fsdp", "context"), "tensor")
    inner = P("fsdp", None, "tensor")
    outer = P("tensor", "fsdp")
    gain = P(None, ("tensor", "fsdp"))
    return jax.shard_map(
        per_device,
        mesh=mesh,
        in_specs=(rows, inner, outer, inner, outer, gain, P("fsdp", None), rows),
        out_specs=(rows, rows, inner, outer, inner, outer, gain),
        check_vma=False,
    )
```

```python
import functools

import jax
import jax.numpy as jnp
from jax import lax
from jax.experimental import pallas as pl
from jax.experimental.pallas import tpu as pltpu
from jax.sharding import PartitionSpec as P

HDIM = 64
LANES = 128
QROWS = 256
norm_eps = 1e-05
rope_base = 130000.0
masked_score = -1e30
BF = jnp.bfloat16
F32 = jnp.float32
VMEM_BYTES = 56 * 1024 * 1024
LIGHT = pl.CostEstimate(flops=1, bytes_accessed=1, transcendentals=0)


def dotf(a, b, dims):
    return lax.dot_general(a, b, (dims, ((), ())), preferred_element_type=F32)


NN = ((1,), (0,))
NT = ((1,), (1,))
TN = ((0,), (0,))


def swap(value, axis, bit):
    count = lax.axis_size(axis)
    return lax.ppermute(value, axis, [(i, i ^ bit) for i in range(count)])


def after(value, *others):
    return lax.optimization_barrier((value, *others))[0]


def shifted(value, axis):
    count = lax.axis_size(axis)
    return [
        lax.ppermute(value, axis, [(i, (i + step) % count) for i in range(count)])
        for step in range(1, count)
    ]


def exchange(value, axis, bit):
    return value + swap(value, axis, bit)


def join_kernel(axis, mode, *refs):
    pieces, out_ref = refs[:-1], refs[-1]
    count = len(pieces)
    me = lax.axis_index(axis)
    for step, piece in enumerate(pieces):
        size = piece.shape[1]
        place = (me ^ step) if mode == "xor" else (me - step + count) % count
        out_ref[:, pl.ds(pl.multiple_of(place * size, size), size)] = piece[...]


def join(pieces, axis, mode):
    rows, size = pieces[0].shape
    return pl.pallas_call(
        functools.partial(join_kernel, axis, mode),
        out_shape=jax.ShapeDtypeStruct((rows, size * len(pieces)), pieces[0].dtype),
        cost_estimate=LIGHT,
        name="join",
    )(*pieces)


def gather_gains(gains):
    if lax.axis_size("tensor") > 4 or gains.shape[1] % LANES:
        whole = lax.all_gather(gains, ("tensor", "fsdp"), axis=1, tiled=True).astype(F32)
        return gains, whole
    own = gains.astype(F32)
    part = join([own] + [swap(own, "fsdp", bit) for bit in (1, 2, 3)], "fsdp", "xor")
    return part, join([part] + shifted(part, "tensor"), "tensor", "shift")


def block_totals(blocks):
    count = lax.axis_size("tensor")
    me = lax.axis_index("tensor")
    if count > 4:
        return lax.dynamic_index_in_dim(lax.psum(blocks, "tensor"), me, 1, keepdims=False)

    def pick(place):
        return lax.dynamic_index_in_dim(blocks, place, 1, keepdims=False)

    total = pick(me)
    for step in range(1, count):
        moves = [(i, (i + step) % count) for i in range(count)]
        total = total + lax.ppermute(pick((me + step) % count), "tensor", moves)
    return total


def piece_columns(j, size):
    return pl.ds(pl.multiple_of((lax.axis_index("fsdp") ^ j) * size, size), size)


def swap_halves(block):
    lane = lax.broadcasted_iota(jnp.int32, block.shape, 1)
    up = pltpu.roll(block, LANES - HDIM // 2, 1)
    down = pltpu.roll(block, HDIM // 2, 1)
    return jnp.where((lane & (HDIM - 1)) < HDIM // 2, up, down)


def rope_tables(positions):
    lane = jnp.arange(LANES, dtype=jnp.int32)
    half = lane % (HDIM // 2)
    frequencies = rope_base ** (-2.0 * half.astype(F32) / HDIM)
    angles = positions.astype(F32)[:, None] * frequencies[None, :]
    sign = jnp.where((lane % HDIM) < HDIM // 2, -1.0, 1.0)
    return jnp.cos(angles), jnp.sin(angles) * sign[None, :]


def piece_dot(x_ref, rows, pieces, dims=NN):
    total = None
    for j, piece in enumerate(pieces):
        size = piece.shape[dims[1][0]]
        term = dotf(x_ref[rows, piece_columns(j, size)], piece, dims)
        total = term if total is None else total + term
    return total


def project_kernel(kinds, normalize, x_ref, *refs):
    pieces, (cos_ref, sin_ref, gain_ref), outs = refs[:4], refs[4:7], refs[7:]
    out_ref = outs[0]
    rows, width = out_ref.shape[1:]
    step = pl.program_id(0)
    if normalize:
        normed_ref, scale_ref = outs[1], outs[2]

        @pl.when(step == 0)
        def _():
            for r in range(0, rows, QROWS):
                part = slice(r, r + QROWS)
                stream = x_ref[part, :].astype(F32)
                mean = jnp.sum(stream * stream, axis=1, keepdims=True) / x_ref.shape[1]
                scale = lax.rsqrt(mean + norm_eps)
                scale_ref[part, :] = scale
                normed_ref[part, :] = (stream * scale * gain_ref[...]).astype(BF)

        x_ref = normed_ref
    for index, scale in enumerate(kinds):

        @pl.when(step == index)
        def _():
            for r in range(0, rows, rows):
                part = slice(r, r + rows)
                result = piece_dot(x_ref, part, [piece[0] for piece in pieces])
                for c in range(0, width, LANES):
                    block = result[:, c : c + LANES]
                    if scale:
                        block = block * cos_ref[part, :] + swap_halves(block) * sin_ref[part, :]
                    low = block.astype(BF)
                    if scale and scale != 1.0:
                        low = low * jnp.asarray(scale, BF)
                    out_ref[0, part, c : c + LANES] = low


def project(x, pieces, cos, sin, gain, kinds, first, normalize):
    rows, depth = x.shape
    _, size, width = pieces[0].shape
    flops = 2 * len(kinds) * rows * depth * width
    whole = pl.BlockSpec((rows, depth), lambda i: (0, 0))
    table = pl.BlockSpec((rows, LANES), lambda i: (0, 0))
    out_shape = [jax.ShapeDtypeStruct((len(kinds), rows, width), BF)]
    out_specs = [pl.BlockSpec((1, rows, width), lambda i: (i, 0, 0))]
    if normalize:
        out_shape += [jax.ShapeDtypeStruct((rows, depth), BF), jax.ShapeDtypeStruct((rows, 1), F32)]
        out_specs += [whole, pl.BlockSpec((rows, 1), lambda i: (0, 0))]
    return pl.pallas_call(
        functools.partial(project_kernel, kinds, normalize),
        name="project_kv" if normalize else "project_q",
        grid=(len(kinds),),
        out_shape=out_shape,
        in_specs=[whole]
        + [pl.BlockSpec((1, size, width), lambda i: (i + first, 0, 0))] * 4
        + [table, table, pl.BlockSpec((1, depth), lambda i: (0, 0))],
        out_specs=out_specs,
        compiler_params=pltpu.CompilerParams(vmem_limit_bytes=VMEM_BYTES),
        cost_estimate=LIGHT,
    )(x, *pieces, cos, sin, gain)


def head_mask(block, head):
    lane = lax.broadcasted_iota(jnp.int32, block.shape, 1)
    inside = (lane < HDIM) if head == 0 else (lane >= HDIM)
    return jnp.where(inside, block, jnp.zeros_like(block))


def own_mask(key_count, row0, low_row):
    key = lax.broadcasted_iota(jnp.int32, (key_count, QROWS), 0)
    query = row0 + lax.broadcasted_iota(jnp.int32, (key_count, QROWS), 1)
    return (key >= low_row) & (key <= query)


def peer_mask(key_count, low_row, offset):
    key = lax.broadcasted_iota(jnp.int32, (key_count, QROWS), 0) - offset
    return key >= low_row


def key_windows(need, total):
    counts = list(range(QROWS, total + 1, QROWS))
    for place, count in enumerate(counts):
        chosen = need < 0 if place == 0 else need < -counts[place - 1]
        if count < total:
            chosen = jnp.logical_and(chosen, need >= -count)
        yield count, chosen


def own_forward_kernel(q_ref, k_ref, v_ref, low_ref, out_ref, log_ref):
    rows = q_ref.shape[0]
    v_t = v_ref[...].T
    for r in range(0, rows, QROWS):
        count = r + QROWS
        allowed = own_mask(count, r, low_ref[:, r : r + QROWS])
        keys = k_ref[0:count, :]
        outs = []
        for head in range(LANES // HDIM):
            scores = dotf(keys, head_mask(q_ref[r : r + QROWS, :], head), NT)
            scores = jnp.where(allowed, scores, masked_score)
            peak = jnp.max(scores, axis=0, keepdims=True)
            weights = jnp.exp(scores - peak)
            total = jnp.sum(weights, axis=0, keepdims=True)
            part = dotf(v_t[head * HDIM : (head + 1) * HDIM, 0:count], weights.astype(BF), NN)
            outs.append(part / total)
            log_ref[0, head : head + 1, r : r + QROWS] = peak + jnp.log(total)
        out_ref[r : r + QROWS, :] = jnp.concatenate(outs, axis=0).T


def peer_forward_kernel(
    need_ref, q_ref, k_ref, v_ref, low_ref, part_ref, log_in_ref, out_ref, log_ref
):
    rows = q_ref.shape[0]
    key_total = k_ref.shape[0]
    for index, r in enumerate(range(0, rows, QROWS)):
        for key_count, chosen in key_windows(need_ref[index], key_total):

            @pl.when(chosen)
            def _():
                window = slice(key_total - key_count, key_total)
                v_t = v_ref[window, :].T
                allowed = peer_mask(key_count, low_ref[:, r : r + QROWS], key_count)
                before = part_ref[r : r + QROWS, :].T
                outs = []
                for head in range(LANES // HDIM):
                    scores = dotf(k_ref[window, :], head_mask(q_ref[r : r + QROWS, :], head), NT)
                    scores = jnp.where(allowed, scores, masked_score)
                    log_own = log_in_ref[0, head : head + 1, r : r + QROWS]
                    peak = jnp.maximum(jnp.max(scores, axis=0, keepdims=True), log_own)
                    weights = jnp.exp(scores - peak)
                    own_weight = jnp.exp(log_own - peak)
                    total = jnp.sum(weights, axis=0, keepdims=True) + own_weight
                    rows_h = slice(head * HDIM, (head + 1) * HDIM)
                    part = dotf(v_t[rows_h, :], weights.astype(BF), NN)
                    outs.append((part + before[rows_h, :] * own_weight) / total)
                    log_ref[0, head : head + 1, r : r + QROWS] = peak + jnp.log(total)
                out_ref[r : r + QROWS, :] = jnp.concatenate(outs, axis=0).T.astype(BF)

        @pl.when(need_ref[index] >= 0)
        def _():
            out_ref[r : r + QROWS, :] = part_ref[r : r + QROWS, :].astype(BF)
            log_ref[:, :, r : r + QROWS] = log_in_ref[:, :, r : r + QROWS]


def pair_spec(rows):
    return pl.BlockSpec((rows, LANES), lambda i: (0, i))


def stacked_spec(rows, part):
    return pl.BlockSpec((None, rows, LANES), lambda i: (part, 0, i))


def log_spec(rows):
    return pl.BlockSpec((1, LANES // HDIM, rows), lambda i: (i, 0, 0))


def low_spec(rows):
    return pl.BlockSpec((1, rows), lambda i: (0, 0))


def own_forward(q, kv, low_row):
    rows, width = q.shape
    pairs = width // LANES
    return pl.pallas_call(
        own_forward_kernel,
        name="own_fwd",
        grid=(pairs,),
        out_shape=(
            jax.ShapeDtypeStruct((rows, width), F32),
            jax.ShapeDtypeStruct((pairs, LANES // HDIM, rows), F32),
        ),
        in_specs=[
            pair_spec(rows),
            stacked_spec(rows, 0),
            stacked_spec(rows, 1),
            low_spec(rows),
        ],
        out_specs=(pair_spec(rows), log_spec(rows)),
        compiler_params=pltpu.CompilerParams(vmem_limit_bytes=VMEM_BYTES),
        cost_estimate=LIGHT,
    )(q, kv, kv, low_row)


SMEM_SPEC = pl.BlockSpec(memory_space=pltpu.SMEM)


def peer_forward(need, q, kv, low_row, part, log_in):
    rows, width = q.shape
    pairs = width // LANES
    return pl.pallas_call(
        peer_forward_kernel,
        name="peer_fwd",
        grid=(pairs,),
        out_shape=(
            jax.ShapeDtypeStruct((rows, width), BF),
            jax.ShapeDtypeStruct((pairs, LANES // HDIM, rows), F32),
        ),
        in_specs=[
            SMEM_SPEC,
            pair_spec(rows),
            stacked_spec(rows, 0),
            stacked_spec(rows, 1),
            low_spec(rows),
            pair_spec(rows),
            log_spec(rows),
        ],
        out_specs=(pair_spec(rows), log_spec(rows)),
        compiler_params=pltpu.CompilerParams(vmem_limit_bytes=VMEM_BYTES),
        cost_estimate=LIGHT,
    )(need, q, kv, kv, low_row, part, log_in)


def backward_block(q_rows, k_rows, v_rows, k_t, do_rows, do_o_t, logs, allowed):
    d_query, d_key, d_value = [], None, None
    for head in range(LANES // HDIM):
        rows_h = slice(head * HDIM, (head + 1) * HDIM)
        q_head = head_mask(q_rows, head)
        do_head = head_mask(do_rows, head)
        scores = dotf(k_rows, q_head, NT)
        probs = jnp.exp(jnp.where(allowed, scores, masked_score) - logs[head])
        delta = jnp.sum(do_o_t[rows_h, :], axis=0, keepdims=True)
        d_probs = dotf(v_rows, do_head, NT)
        d_scores = (probs * (d_probs - delta)).astype(BF)
        d_v = dotf(probs.astype(BF), do_head, NN)
        d_k = dotf(d_scores, q_head, NN)
        d_value = d_v if d_value is None else d_value + d_v
        d_key = d_k if d_key is None else d_key + d_k
        d_query.append(dotf(k_t[rows_h, :], d_scores, NN))
    return jnp.concatenate(d_query, axis=0), d_key, d_value


def output_product(do_ref, o_ref, window):
    product = do_ref[window].astype(F32) * o_ref[window].astype(F32)
    return product.T


def peer_backward_kernel(
    need_ref, q_ref, k_ref, v_ref, do_ref, o_ref, low_ref, log_ref, dq_ref, dkv_ref, sums
):
    rows = q_ref.shape[0]
    key_total = k_ref.shape[0]
    sums[...] = jnp.zeros_like(sums)
    for index, r in enumerate(range(0, rows, QROWS)):
        rows_q = (slice(r, r + QROWS), slice(None))
        for key_count, chosen in key_windows(need_ref[index], key_total):

            @pl.when(chosen)
            def _():
                window = slice(key_total - key_count, key_total)
                allowed = peer_mask(key_count, low_ref[:, r : r + QROWS], key_count)
                logs = [log_ref[0, h : h + 1, r : r + QROWS] for h in range(LANES // HDIM)]
                d_query, d_key, d_value = backward_block(
                    q_ref[rows_q],
                    k_ref[window, :],
                    v_ref[window, :],
                    k_ref[window, :].T,
                    do_ref[rows_q],
                    output_product(do_ref, o_ref, rows_q),
                    logs,
                    allowed,
                )
                dq_ref[rows_q] = d_query.T
                sums[0, window] += d_key
                sums[1, window] += d_value

        @pl.when(need_ref[index] >= 0)
        def _():
            dq_ref[rows_q] = jnp.zeros((QROWS, LANES), F32)

    dkv_ref[...] = sums[...].astype(BF)


def peer_backward(need, q, kv, do, o, low_row, logs):
    rows, width = q.shape
    pairs = width // LANES
    return pl.pallas_call(
        peer_backward_kernel,
        name="peer_bwd",
        grid=(pairs,),
        out_shape=(
            jax.ShapeDtypeStruct((rows, width), F32),
            jax.ShapeDtypeStruct((2, rows, width), BF),
        ),
        in_specs=[
            SMEM_SPEC,
            pair_spec(rows),
            stacked_spec(rows, 0),
            stacked_spec(rows, 1),
            pair_spec(rows),
            pair_spec(rows),
            low_spec(rows),
            log_spec(rows),
        ],
        out_specs=(pair_spec(rows), pl.BlockSpec((2, rows, LANES), lambda i: (0, 0, i))),
        scratch_shapes=[pltpu.VMEM((2, rows, LANES), F32)],
        compiler_params=pltpu.CompilerParams(vmem_limit_bytes=VMEM_BYTES),
        cost_estimate=LIGHT,
    )(need, q, kv, kv, do, o, low_row, logs)


def own_backward_kernel(
    q_ref,
    k_ref,
    v_ref,
    do_ref,
    o_ref,
    low_ref,
    log_ref,
    dq_in_ref,
    cos_ref,
    sin_ref,
    dq_ref,
    dk_ref,
    dv_ref,
    sums,
):
    rows = q_ref.shape[0]
    sums[...] = jnp.zeros_like(sums)
    k_t = k_ref[...].T
    for r in range(0, rows, QROWS):
        count = r + QROWS
        window = (slice(r, r + QROWS), slice(None))
        allowed = own_mask(count, r, low_ref[:, r : r + QROWS])
        logs = [log_ref[0, h : h + 1, r : r + QROWS] for h in range(LANES // HDIM)]
        d_query, d_key, d_value = backward_block(
            q_ref[window],
            k_ref[0:count, :],
            v_ref[0:count, :],
            k_t[:, 0:count],
            do_ref[window],
            output_product(do_ref, o_ref, window),
            logs,
            allowed,
        )
        rotated = (d_query.T + dq_in_ref[window]) * (HDIM**-0.5)
        turned = rotated * cos_ref[window] - swap_halves(rotated) * sin_ref[window]
        dq_ref[window] = turned.astype(BF)
        sums[0, 0:count] += d_key
        sums[1, 0:count] += d_value
    dk_ref[...] = sums[0]
    dv_ref[...] = sums[1]


def own_backward(q, kv, do, o, low_row, logs, dq_in, cos, sin):
    rows, width = q.shape
    pairs = width // LANES
    table = pl.BlockSpec((rows, LANES), lambda i: (0, 0))
    return pl.pallas_call(
        own_backward_kernel,
        name="own_bwd",
        grid=(pairs,),
        out_shape=(
            jax.ShapeDtypeStruct((rows, width), BF),
            jax.ShapeDtypeStruct((rows, width), F32),
            jax.ShapeDtypeStruct((rows, width), F32),
        ),
        in_specs=[
            pair_spec(rows),
            stacked_spec(rows, 0),
            stacked_spec(rows, 1),
            pair_spec(rows),
            pair_spec(rows),
            low_spec(rows),
            log_spec(rows),
            pair_spec(rows),
            table,
            table,
        ],
        out_specs=(pair_spec(rows),) * 3,
        scratch_shapes=[pltpu.VMEM((2, rows, LANES), F32)],
        compiler_params=pltpu.CompilerParams(vmem_limit_bytes=VMEM_BYTES),
        cost_estimate=LIGHT,
    )(q, kv, kv, do, o, low_row, logs, dq_in, cos, sin)


def finish_keys_kernel(dk_ref, dv_ref, dk_in_ref, dv_in_ref, cos_ref, sin_ref, dk_out, dv_out):
    total = dk_ref[...] + dk_in_ref[...].astype(F32)
    turned = total * cos_ref[...] - swap_halves(total) * sin_ref[...]
    dk_out[...] = turned.astype(BF)
    dv_out[...] = (dv_ref[...] + dv_in_ref[...].astype(F32)).astype(BF)


def finish_keys(dk, dv, dkv_in, cos, sin):
    rows, width = dk.shape
    pairs = width // LANES
    table = pl.BlockSpec((rows, LANES), lambda i: (0, 0))
    return pl.pallas_call(
        finish_keys_kernel,
        name="finish_keys",
        grid=(pairs,),
        out_shape=(jax.ShapeDtypeStruct((rows, width), BF),) * 2,
        in_specs=[pair_spec(rows), pair_spec(rows), stacked_spec(rows, 0), stacked_spec(rows, 1)]
        + [table, table],
        out_specs=(pair_spec(rows),) * 2,
        cost_estimate=LIGHT,
    )(dk, dv, dkv_in, dkv_in, cos, sin)


def branch_kernel(stream_ref, att_ref, gain_ref, *refs):
    pieces, (hidden_ref, normed_ref, scale_ref) = refs[:4], refs[4:]
    for j, piece in enumerate(pieces):
        columns = piece_columns(j, piece.shape[1])
        term = dotf(att_ref[...], piece[...], NN)
        hidden_ref[:, columns] = stream_ref[:, columns].astype(F32) + term
    hidden = hidden_ref[...]
    mean = jnp.sum(hidden * hidden, axis=1, keepdims=True) / hidden.shape[1]
    scale = lax.rsqrt(mean + norm_eps)
    scale_ref[...] = scale
    normed_ref[...] = (hidden * scale * gain_ref[...]).astype(BF)


def add_branch(stream, att, gain, pieces):
    rows, depth = stream.shape
    heads = att.shape[1]
    tile = pl.BlockSpec((QROWS, depth), lambda i: (i, 0))
    return pl.pallas_call(
        branch_kernel,
        name="branch",
        grid=(rows // QROWS,),
        out_shape=(
            jax.ShapeDtypeStruct((rows, depth), F32),
            jax.ShapeDtypeStruct((rows, depth), BF),
            jax.ShapeDtypeStruct((rows, 1), F32),
        ),
        in_specs=[
            tile,
            pl.BlockSpec((QROWS, heads), lambda i: (i, 0)),
            pl.BlockSpec((1, depth), lambda i: (0, 0)),
        ]
        + [pl.BlockSpec(pieces[0].shape, lambda i: (0, 0))] * 4,
        out_specs=(tile, tile, pl.BlockSpec((QROWS, 1), lambda i: (i, 0))),
        compiler_params=pltpu.CompilerParams(vmem_limit_bytes=VMEM_BYTES),
        cost_estimate=LIGHT,
    )(stream, att, gain, *pieces)


def hidden_kernel(x_ref, *refs):
    w_in, (act_ref, by_gate_ref, by_up_ref) = refs[:4], refs[4:]
    rows = x_ref.shape[0]
    for r in range(0, rows, rows):
        part = slice(r, r + rows)
        gate = piece_dot(x_ref, part, [piece[0] for piece in w_in])
        up = piece_dot(x_ref, part, [piece[1] for piece in w_in])
        sig = jax.nn.sigmoid(gate)
        silu = gate * sig
        act_ref[part, :] = (silu * up).astype(BF)
        by_gate_ref[part, :] = (up * sig * (1.0 + gate * (1.0 - sig))).astype(BF)
        by_up_ref[part, :] = silu.astype(BF)


def hidden_units(x, w_in):
    rows, depth = x.shape
    _, size, units = w_in[0].shape
    tile = 256
    part = pl.BlockSpec((rows, tile), lambda i: (0, i))
    return pl.pallas_call(
        hidden_kernel,
        grid=(units // tile,),
        out_shape=(jax.ShapeDtypeStruct((rows, units), BF),) * 3,
        in_specs=[pl.BlockSpec((rows, depth), lambda i: (0, 0))]
        + [pl.BlockSpec((2, size, tile), lambda i: (0, 0, i))] * 4,
        out_specs=(part,) * 3,
        compiler_params=pltpu.CompilerParams(vmem_limit_bytes=VMEM_BYTES),
        cost_estimate=LIGHT,
        name="hidden",
    )(x, *w_in)


def hidden_back_kernel(cot_ref, by_gate_ref, by_up_ref, *refs):
    w_down, (dg_ref, du_ref) = refs[:4], refs[4:]
    rows = cot_ref.shape[0]
    for r in range(0, rows, rows):
        part = slice(r, r + rows)
        d_act = piece_dot(cot_ref, part, [piece[...] for piece in w_down], NT)
        dg_ref[part, :] = (d_act * by_gate_ref[part, :].astype(F32)).astype(BF)
        du_ref[part, :] = (d_act * by_up_ref[part, :].astype(F32)).astype(BF)


def hidden_back(cot, by_gate, by_up, w_down):
    rows, depth = cot.shape
    units, size = w_down[0].shape
    tile = 256
    part = pl.BlockSpec((rows, tile), lambda i: (0, i))
    return pl.pallas_call(
        hidden_back_kernel,
        grid=(units // tile,),
        out_shape=(jax.ShapeDtypeStruct((rows, units), BF),) * 2,
        in_specs=[pl.BlockSpec((rows, depth), lambda i: (0, 0)), part, part]
        + [pl.BlockSpec((tile, size), lambda i: (i, 0))] * 4,
        out_specs=(part,) * 2,
        compiler_params=pltpu.CompilerParams(vmem_limit_bytes=VMEM_BYTES),
        cost_estimate=LIGHT,
        name="hidden_back",
    )(cot, by_gate, by_up, *w_down)


def phased(i, block, make_index, tiles):
    def index_map(j, t):
        return make_index(jnp.where(j < i, 0, jnp.where(j == i, t, tiles - 1)))

    return pl.BlockSpec(block, index_map)


def columns_call(kernel_dot, lefts, pieces, block, make_index, size, flops, name):
    rows = lefts[0].shape[0]
    tile = min(size, 256)
    tiles = size // tile
    depth = size * 4

    def kernel(*refs):
        left_refs, piece_refs, out_ref = refs[: len(lefts)], refs[len(lefts) : -1], refs[-1]
        for j, piece in enumerate(piece_refs):

            @pl.when(pl.program_id(0) == j)
            def _():
                out_ref[...] = kernel_dot([left[...] for left in left_refs], piece).astype(BF)

    def out_index(j, t):
        return (0, (lax.axis_index("fsdp") ^ j) * tiles + t)

    return pl.pallas_call(
        kernel,
        grid=(4, tiles),
        out_shape=jax.ShapeDtypeStruct((rows, depth), BF),
        in_specs=[pl.BlockSpec(left.shape, lambda j, t: (0, 0)) for left in lefts]
        + [phased(i, block(tile), make_index, tiles) for i in range(4)],
        out_specs=pl.BlockSpec((rows, tile), out_index),
        compiler_params=pltpu.CompilerParams(vmem_limit_bytes=VMEM_BYTES),
        cost_estimate=LIGHT,
        name=name,
    )(*lefts, *pieces)


def stacked_columns(lefts, pieces, name):
    count, size, inner = pieces[0].shape

    def product(parts, piece):
        return sum(dotf(parts[c], piece[c], NT) for c in range(count))

    return columns_call(
        product,
        lefts,
        pieces,
        lambda tile: (count, tile, inner),
        lambda t: (0, t, 0),
        size,
        8 * lefts[0].shape[0] * size * inner * count,
        name,
    )


def plain_columns(left, pieces, name):
    inner, size = pieces[0].shape
    return columns_call(
        lambda parts, piece: dotf(parts[0], piece[...], NN),
        [left],
        pieces,
        lambda tile: (inner, tile),
        lambda t: (0, t),
        size,
        8 * left.shape[0] * size * inner,
        name,
    )


def branch_back_kernel(shares, d_mid_ref, hidden_ref, cot_ref, scale_ref, gain_ref, *refs):
    pieces, (d_hidden_ref, d_att_ref, gain_out_ref) = refs[:4], refs[4:7]
    d_mid = d_mid_ref[...].astype(F32)
    hidden = hidden_ref[...]
    scale = scale_ref[...]
    weighted = d_mid * gain_ref[...]
    inner = jnp.sum(weighted * hidden, axis=1, keepdims=True) / hidden.shape[1]
    d_hidden = (
        cot_ref[...].astype(F32) * (1.0 / shares)
        + scale * weighted
        - hidden * (scale * scale * scale * inner)
    )
    gain_term = jnp.sum(d_mid * hidden * scale, axis=0, keepdims=True)

    @pl.when(pl.program_id(0) == 0)
    def _():
        gain_out_ref[...] = gain_term

    @pl.when(pl.program_id(0) != 0)
    def _():
        gain_out_ref[...] += gain_term

    d_hidden_ref[...] = d_hidden.astype(BF)
    heads = d_att_ref.shape[1]
    for e in range(0, heads, 512):
        columns = slice(e, e + 512)
        d_att_ref[:, columns] = piece_dot(
            d_hidden_ref, slice(None), [piece[columns, :] for piece in pieces], NT
        ).astype(BF)


def branch_back(d_mid, hidden, cot, scale, gain, pieces):
    rows, depth = hidden.shape
    heads, size = pieces[0].shape
    tile = pl.BlockSpec((QROWS, depth), lambda i: (i, 0))
    row = pl.BlockSpec((1, depth), lambda i: (0, 0))
    return pl.pallas_call(
        functools.partial(branch_back_kernel, lax.axis_size("tensor")),
        name="branch_back",
        grid=(rows // QROWS,),
        in_specs=[tile, tile, tile, pl.BlockSpec((QROWS, 1), lambda i: (i, 0)), row]
        + [pl.BlockSpec((heads, size), lambda i: (0, 0))] * 4,
        out_specs=(tile, pl.BlockSpec((QROWS, heads), lambda i: (i, 0)), row),
        out_shape=(
            jax.ShapeDtypeStruct((rows, depth), BF),
            jax.ShapeDtypeStruct((rows, heads), BF),
            jax.ShapeDtypeStruct((1, depth), F32),
        ),
        compiler_params=pltpu.CompilerParams(vmem_limit_bytes=VMEM_BYTES),
        cost_estimate=LIGHT,
    )(d_mid, hidden, cot, scale, gain, *pieces)


def grad_call(left, right, cut, place, adds, name, span=(0, 1)):
    rows = left.shape[0]
    size = (left, right)[cut].shape[1] // 4
    swept = (right, left)[cut].shape[1] // span[1]
    height, width = (size, swept) if cut == 0 else (swept, size)
    tile = min(1024, swept)
    offset = span[0] * (swept // tile)
    block = (height, tile) if cut == 0 else (tile, width)

    def owner():
        return lax.axis_index("fsdp") ^ place

    def swept_index(t):
        return (0, t) if cut == 0 else (t, 0)

    def kernel(left_ref, right_ref, *refs):
        add_refs, out_ref = refs[: len(adds)], refs[len(adds)]
        if cut == 0:
            turned = refs[-1]

            @pl.when(pl.program_id(0) == 0)
            def _():
                turned[...] = left_ref[...].T

            result = dotf(turned[...], right_ref[...], NN)
        else:
            result = dotf(left_ref[...].T, right_ref[...], NN)
        for add in add_refs:
            result = result + add[...].astype(F32)
        out_ref[...] = result.astype(BF)

    fixed = pl.BlockSpec((rows, size), lambda t: (0, owner()))
    moving = pl.BlockSpec((rows, tile), lambda t: (0, t + offset))
    return pl.pallas_call(
        kernel,
        grid=(swept // tile,),
        out_shape=jax.ShapeDtypeStruct((height, width), BF),
        in_specs=[fixed, moving] * (cut == 0)
        + [moving, fixed] * (cut == 1)
        + [pl.BlockSpec(block, swept_index)] * len(adds),
        out_specs=pl.BlockSpec(block, swept_index),
        scratch_shapes=[pltpu.VMEM((size, rows), BF)] if cut == 0 else [],
        compiler_params=pltpu.CompilerParams(vmem_limit_bytes=VMEM_BYTES),
        cost_estimate=LIGHT,
        name=name,
    )(left, right, *adds)


class Reduction:
    def __init__(self, left, right, cut, name, span=(0, 1)):
        self.args, self.name, self.span = (left, right, cut), name, span

    def call(self, place, deps, step, adds=()):
        left, right, cut = self.args
        left = after(left, *deps) if deps else left
        return grad_call(left, right, cut, place, adds, self.name + step, self.span)

    def near_far(self, *deps):
        self.three = self.call(3, deps, "_3")
        self.for_two = swap(self.three, "fsdp", 1)

    def near(self, *deps):
        self.one = self.call(1, deps, "_1")
        self.for_own = swap(self.one, "fsdp", 1)

    def far(self, *deps):
        self.two = self.call(2, deps, "_2", [self.for_two])

    def send_far(self, *deps):
        self.across = swap(after(self.two, *deps), "fsdp", 2)

    def mine(self, *deps):
        self.own = self.call(0, deps, "_0", [self.for_own, self.across])

    def send_context(self, *deps):
        self.other = swap(after(self.own, *deps), "context", 1)


def totals_kernel(slots, *refs):
    pairs, out_ref = refs[:-1], refs[-1]
    for slot in range(len(pairs) // 2):
        total = pairs[2 * slot][...].astype(F32) + pairs[2 * slot + 1][...].astype(F32)
        if slots == 0:
            out_ref[slot] = total
        else:
            out_ref[:, slot, :] = total


def totals(sums, slots, *deps):
    arrays = [array for part in sums for array in (part.own, part.other)]
    if deps:
        arrays[0] = after(arrays[0], *deps)
    rows, width = arrays[0].shape
    tile = 128
    shape = [rows, width]
    shape.insert(slots, len(sums))
    block = [tile, width]
    block.insert(slots, len(sums))
    return pl.pallas_call(
        functools.partial(totals_kernel, slots),
        grid=(rows // tile,),
        out_shape=jax.ShapeDtypeStruct(tuple(shape), F32),
        in_specs=[pl.BlockSpec((tile, width), lambda i: (i, 0))] * len(arrays),
        out_specs=pl.BlockSpec(
            tuple(block), (lambda i: (0, i, 0)) if slots == 0 else (lambda i: (i, 0, 0))
        ),
        compiler_params=pltpu.CompilerParams(vmem_limit_bytes=VMEM_BYTES),
        cost_estimate=LIGHT,
        name="totals",
    )(*arrays)


def row_sum(values_in):
    return jnp.sum(values_in, axis=1, keepdims=True)


def per_device(tokens, w_qkv, w_out, w_gate_up, w_down, gains, seq_lengths, cotangent):
    row_count, part_width = tokens.shape
    tensor_index = lax.axis_index("tensor")
    context_index = lax.axis_index("context")
    full_width = part_width * lax.axis_size("tensor")

    def features(part_in):
        return lax.all_gather(part_in, "tensor", axis=1, tiled=True)

    def feature_sum(term):
        return lax.psum_scatter(term.astype(BF), "tensor", scatter_dimension=1, tiled=True)

    def own_features(full):
        return lax.dynamic_slice_in_dim(full, tensor_index * part_width, part_width, 1)

    ending = jnp.cumsum(seq_lengths[0])
    starts = ending - seq_lengths[0]
    places = context_index * row_count + jnp.arange(row_count, dtype=jnp.int32)
    first_token = jnp.max(jnp.where(starts[None, :] <= places[:, None], starts[None, :], 0), axis=1)
    cos, sin = rope_tables(places - first_token)
    low = first_token - context_index * row_count
    low_row = low[None, :]
    need = low[::QROWS]

    token_low = features(tokens)
    gain_near, gain_full = gather_gains(gains)
    gain_attn, gain_mlp = gain_full[0:1], gain_full[1:2]

    qkv_own = jnp.swapaxes(w_qkv, 0, 1)
    half = qkv_own.shape[1] // 2
    far_half = swap(
        lax.dynamic_slice_in_dim(after(qkv_own, gain_near), context_index * half, half, 1),
        "fsdp",
        2,
    )
    other_half = swap(far_half, "context", 1)
    qkv_far = jnp.where(
        context_index == 0,
        jnp.concatenate([far_half, other_half], axis=1),
        jnp.concatenate([other_half, far_half], axis=1),
    )
    qkv_near = swap(qkv_own, "fsdp", 1)
    qkv = (qkv_own, qkv_near, qkv_far, swap(qkv_far, "fsdp", 1))

    gate_up_own = jnp.swapaxes(w_gate_up, 0, 1)
    cut = gate_up_own.shape[1] * 12 // 32
    gate_up_a = swap(after(gate_up_own[:, :cut], far_half), "fsdp", 2)
    gate_up_b = swap(after(gate_up_own[:, cut:], gate_up_a), "fsdp", 2)

    keys_values, normed_in, scale_attn = project(
        after(token_low, gate_up_a), qkv, cos, sin, gain_attn, (1.0, None), 1, True
    )
    peer_kv = lax.ppermute(keys_values, "context", [(0, 1)])
    queries = project(normed_in, qkv, cos, sin, gain_attn, (HDIM**-0.5,), 0, False)[0][0]
    part, part_log = own_forward(queries, keys_values, low_row)
    attended, logs = peer_forward(
        need, queries, peer_kv, low_row, after(part, gate_up_b), part_log
    )
    cot_first = features(after(cotangent[:QROWS], gate_up_a))
    attended_full = features(after(attended, cot_first))

    out_own = lax.all_gather(after(w_out, gate_up_a), "tensor", axis=0, tiled=True)
    out_near = swap(out_own, "fsdp", 1)
    out_far = swap(out_own, "fsdp", 2)
    out_far_near = swap(out_far, "fsdp", 1)
    out = (out_own, out_near, out_far, out_far_near)
    gate_up_own, gate_up_a, gate_up_b = lax.optimization_barrier(
        (gate_up_own, gate_up_a, gate_up_b, attended)
    )[:3]
    gate_up_far = jnp.concatenate([gate_up_a, gate_up_b], axis=1)
    gate_up_near = swap(gate_up_own, "fsdp", 1)
    gate_up = (gate_up_own, gate_up_near, gate_up_far, swap(gate_up_far, "fsdp", 1))
    cot_rest = features(after(cotangent[QROWS:], attended_full, out_far_near, out_near))
    cot_full = jnp.concatenate([cot_first, cot_rest], axis=0)
    down_far = swap(after(w_down, attended_full, out_far_near), "fsdp", 2)
    down_near = swap(after(w_down, attended_full), "fsdp", 1)
    hidden, normed_mid, scale_mlp = add_branch(token_low, attended_full, gain_mlp, out)

    activated, by_gate, by_up = hidden_units(normed_mid, gate_up)
    down_far = after(down_far, activated)
    down = (w_down, down_near, down_far, swap(down_far, "fsdp", 1))
    mlp_term = plain_columns(activated, down, "mlp_out")
    mlp_out = feature_sum(mlp_term)
    d_gate, d_up = hidden_back(after(cot_full, mlp_term), by_gate, by_up, down)
    down_a, down_b = (
        Reduction(activated, cot_full, 1, "grad_down", (part_index, 2)) for part_index in (0, 1)
    )
    down_a.near_far(d_gate)
    down_b.near_far(down_a.three)
    d_mid_term = stacked_columns([d_gate, after(d_up, down_b.three)], gate_up, "d_mid")
    down_a.far(d_mid_term)
    down_a.send_far()
    down_b.far(down_a.two)
    down_b.send_far()
    d_hidden_term, d_att_term, gain_mlp_term = branch_back(
        after(d_mid_term, down_b.two), hidden, cot_full, scale_mlp, gain_mlp, out
    )
    d_attended = feature_sum(after(d_att_term, mlp_out))
    d_hidden_own = feature_sum(after(d_hidden_term, d_att_term))

    square = lax.axis_size("tensor") == lax.axis_size("fsdp")
    grad_gate = Reduction(normed_mid, d_gate, 0, "grad_gate")
    grad_up = Reduction(normed_mid, d_up, 0, "grad_up")
    down_a.near(d_att_term)
    down_b.near(down_a.one)
    down_a.mine(down_b.one)
    down_a.send_context()
    grad_gate.near_far(down_a.own)
    down_b.mine(grad_gate.three)
    down_b.send_context()
    grad_up.near_far(down_b.own)
    grad_gate.near(grad_up.three)
    grad_gate.far(grad_gate.one)
    grad_gate.send_far()
    grad_up.near(grad_gate.two)
    grad_up.far(grad_up.one)
    grad_up.send_far()

    dq_peer, dkv_peer = peer_backward(
        need, queries, peer_kv, after(d_attended, grad_up.two, down_a.other, down_b.other), attended, low_row, logs
    )
    dkv_in = lax.ppermute(dkv_peer, "context", [(1, 0)])
    d_query, dk_own, dv_own = own_backward(
        queries,
        keys_values,
        d_attended,
        attended,
        low_row,
        logs,
        dq_peer,
        cos,
        sin,
    )
    grad_query = Reduction(normed_in, d_query, 0, "grad_query")
    grad_query.near_far(d_query)
    grad_query.near(grad_query.three)
    grad_gate.mine(grad_query.one)
    grad_gate.send_context()
    d_key, d_value = finish_keys(
        dk_own, dv_own, after(dkv_in, grad_gate.own, d_hidden_own), cos, sin
    )
    d_in_term = stacked_columns([d_query, d_key, d_value], qkv, "d_in")
    d_in = feature_sum(d_in_term).astype(F32)

    if square:
        grad_out = Reduction(attended_full, d_hidden_own, 0, "grad_out")
    else:
        grad_out = Reduction(attended, features(d_hidden_own), 1, "grad_out")
    grad_query.far(d_in_term)
    grad_query.send_far()
    grad_key = Reduction(normed_in, d_key, 0, "grad_key")
    grad_value = Reduction(normed_in, d_value, 0, "grad_value")
    grad_key.near_far(grad_query.two)
    grad_value.near_far(grad_key.three)
    grad_up.mine(grad_value.three)
    grad_up.send_context()
    grad_key.near(grad_up.own)
    grad_value.near(grad_key.one)
    grad_key.far(grad_value.one)
    grad_key.send_far()
    grad_value.far(grad_key.two)
    grad_value.send_far()
    grad_out.near_far(grad_value.two, grad_gate.other)
    grad_out.near(grad_out.three)
    grad_out.far(grad_out.one)
    grad_out.send_far()
    grad_query.mine(grad_out.two)
    grad_query.send_context()

    stream = token_low.astype(F32)
    d_in_wide = after(d_in_term, grad_query.own).astype(F32)
    weighted = d_in_wide * stream
    inner_term = jnp.sum(weighted * gain_attn, axis=1)
    gain_attn_term = jnp.sum(weighted * scale_attn, axis=0)
    parts = lax.axis_size("tensor")
    totals_small = block_totals(
        jnp.concatenate(
            [
                jnp.broadcast_to(inner_term[None, :], (parts, row_count)),
                gain_attn_term.reshape(parts, part_width),
                gain_mlp_term.reshape(parts, part_width),
            ],
            axis=1,
        )[None]
    )
    inner_in = totals_small[0, :row_count][:, None] / full_width
    gain_sums = totals_small[0, row_count:].reshape(2, part_width)
    gain_sums = exchange(gain_sums, "fsdp", 1)
    gain_sums = exchange(gain_sums, "fsdp", 2)
    gain_sums = exchange(gain_sums, "context", 1)
    gain_width = gains.shape[1]
    grad_gains = lax.dynamic_slice_in_dim(
        gain_sums, lax.axis_index("fsdp") * gain_width, gain_width, 1
    )

    grad_down_sum = totals([down_a, down_b], 0, d_in_wide).reshape(w_down.shape)
    grad_key.mine(grad_down_sum, grad_up.other)
    grad_key.send_context()
    grad_value.mine(grad_key.own)
    grad_value.send_context()
    grad_out.mine(grad_value.own)
    if square:
        count = lax.axis_size("fsdp")
        across = [(i, (i % count) * count + i // count) for i in range(count * count)]
        grad_out.own = lax.ppermute(grad_out.own, ("fsdp", "tensor"), across)
    grad_out.send_context()
    grad_gate_up_sum = totals([grad_gate, grad_up], 1, grad_value.own)
    grad_qkv = totals([grad_query, grad_key, grad_value], 0, grad_gate_up_sum)
    grad_out_sum = totals([grad_out], 0, grad_qkv)[0]

    block_out = (own_features(hidden) + mlp_out.astype(F32)).astype(BF)
    own_tokens = tokens.astype(F32)
    grad_tokens = (
        d_hidden_own.astype(F32)
        + scale_attn * own_features(gain_attn) * d_in
        - own_tokens * scale_attn * scale_attn * scale_attn * inner_in
    ).astype(BF)
    return (
        block_out,
        grad_tokens,
        jnp.swapaxes(grad_qkv, 0, 1),
        grad_out_sum,
        grad_gate_up_sum,
        grad_down_sum,
        grad_gains,
    )


def solution(mesh):
    rows = P(("fsdp", "context"), "tensor")
    inner = P("fsdp", None, "tensor")
    outer = P("tensor", "fsdp")
    gain = P(None, ("tensor", "fsdp"))
    return jax.shard_map(
        per_device,
        mesh=mesh,
        in_specs=(rows, inner, outer, inner, outer, gain, P("fsdp", None), rows),
        out_specs=(rows, rows, inner, outer, inner, outer, gain),
        check_vma=False,
    )
```

```python
import functools

import jax
import jax.numpy as jnp
from jax import lax
from jax.experimental import pallas as pl
from jax.experimental.pallas import tpu as pltpu
from jax.sharding import PartitionSpec as P

HDIM = 64
LANES = 128
QROWS = 256
norm_eps = 1e-05
rope_base = 130000.0
masked_score = -1e30
BF = jnp.bfloat16
F32 = jnp.float32
VMEM_BYTES = 56 * 1024 * 1024
LIGHT = pl.CostEstimate(flops=1, bytes_accessed=1, transcendentals=0)


def dotf(a, b, dims):
    return lax.dot_general(a, b, (dims, ((), ())), preferred_element_type=F32)


NN = ((1,), (0,))
NT = ((1,), (1,))
TN = ((0,), (0,))


def swap(value, axis, bit):
    count = lax.axis_size(axis)
    return lax.ppermute(value, axis, [(i, i ^ bit) for i in range(count)])


def after(value, *others):
    return lax.optimization_barrier((value, *others))[0]


def shifted(value, axis):
    count = lax.axis_size(axis)
    return [
        lax.ppermute(value, axis, [(i, (i + step) % count) for i in range(count)])
        for step in range(1, count)
    ]


def exchange(value, axis, bit):
    return value + swap(value, axis, bit)


def join_kernel(axis, mode, *refs):
    pieces, out_ref = refs[:-1], refs[-1]
    count = len(pieces)
    me = lax.axis_index(axis)
    for step, piece in enumerate(pieces):
        size = piece.shape[1]
        place = (me ^ step) if mode == "xor" else (me - step + count) % count
        out_ref[:, pl.ds(pl.multiple_of(place * size, size), size)] = piece[...]


def join(pieces, axis, mode):
    rows, size = pieces[0].shape
    return pl.pallas_call(
        functools.partial(join_kernel, axis, mode),
        out_shape=jax.ShapeDtypeStruct((rows, size * len(pieces)), pieces[0].dtype),
        cost_estimate=LIGHT,
        name="join",
    )(*pieces)


def gather_gains(gains):
    if lax.axis_size("tensor") > 4 or gains.shape[1] % LANES:
        whole = lax.all_gather(gains, ("tensor", "fsdp"), axis=1, tiled=True).astype(F32)
        return gains, whole
    own = gains.astype(F32)
    part = join([own] + [swap(own, "fsdp", bit) for bit in (1, 2, 3)], "fsdp", "xor")
    return part, join([part] + shifted(part, "tensor"), "tensor", "shift")


def block_totals(blocks):
    count = lax.axis_size("tensor")
    me = lax.axis_index("tensor")
    if count > 4:
        return lax.dynamic_index_in_dim(lax.psum(blocks, "tensor"), me, 1, keepdims=False)

    def pick(place):
        return lax.dynamic_index_in_dim(blocks, place, 1, keepdims=False)

    total = pick(me)
    for step in range(1, count):
        moves = [(i, (i + step) % count) for i in range(count)]
        total = total + lax.ppermute(pick((me + step) % count), "tensor", moves)
    return total


def piece_columns(j, size):
    return pl.ds(pl.multiple_of((lax.axis_index("fsdp") ^ j) * size, size), size)


def swap_halves(block):
    lane = lax.broadcasted_iota(jnp.int32, block.shape, 1)
    up = pltpu.roll(block, LANES - HDIM // 2, 1)
    down = pltpu.roll(block, HDIM // 2, 1)
    return jnp.where((lane & (HDIM - 1)) < HDIM // 2, up, down)


def rope_tables(positions):
    lane = jnp.arange(LANES, dtype=jnp.int32)
    half = lane % (HDIM // 2)
    frequencies = rope_base ** (-2.0 * half.astype(F32) / HDIM)
    angles = positions.astype(F32)[:, None] * frequencies[None, :]
    sign = jnp.where((lane % HDIM) < HDIM // 2, -1.0, 1.0)
    return jnp.cos(angles), jnp.sin(angles) * sign[None, :]


def piece_dot(x_ref, rows, pieces, dims=NN):
    total = None
    for j, piece in enumerate(pieces):
        size = piece.shape[dims[1][0]]
        term = dotf(x_ref[rows, piece_columns(j, size)], piece, dims)
        total = term if total is None else total + term
    return total


def project_kernel(kinds, normalize, x_ref, *refs):
    pieces, (cos_ref, sin_ref, gain_ref), outs = refs[:4], refs[4:7], refs[7:]
    out_ref = outs[0]
    rows, width = out_ref.shape[1:]
    step = pl.program_id(0)
    if normalize:
        normed_ref, scale_ref = outs[1], outs[2]

        @pl.when(step == 0)
        def _():
            for r in range(0, rows, QROWS):
                part = slice(r, r + QROWS)
                stream = x_ref[part, :].astype(F32)
                mean = jnp.sum(stream * stream, axis=1, keepdims=True) / x_ref.shape[1]
                scale = lax.rsqrt(mean + norm_eps)
                scale_ref[part, :] = scale
                normed_ref[part, :] = (stream * scale * gain_ref[...]).astype(BF)

        x_ref = normed_ref
    for index, scale in enumerate(kinds):

        @pl.when(step == index)
        def _():
            for r in range(0, rows, rows):
                part = slice(r, r + rows)
                result = piece_dot(x_ref, part, [piece[0] for piece in pieces])
                for c in range(0, width, LANES):
                    block = result[:, c : c + LANES]
                    if scale:
                        block = block * cos_ref[part, :] + swap_halves(block) * sin_ref[part, :]
                    low = block.astype(BF)
                    if scale and scale != 1.0:
                        low = low * jnp.asarray(scale, BF)
                    out_ref[0, part, c : c + LANES] = low


def project(x, pieces, cos, sin, gain, kinds, first, normalize):
    rows, depth = x.shape
    _, size, width = pieces[0].shape
    flops = 2 * len(kinds) * rows * depth * width
    whole = pl.BlockSpec((rows, depth), lambda i: (0, 0))
    table = pl.BlockSpec((rows, LANES), lambda i: (0, 0))
    out_shape = [jax.ShapeDtypeStruct((len(kinds), rows, width), BF)]
    out_specs = [pl.BlockSpec((1, rows, width), lambda i: (i, 0, 0))]
    if normalize:
        out_shape += [jax.ShapeDtypeStruct((rows, depth), BF), jax.ShapeDtypeStruct((rows, 1), F32)]
        out_specs += [whole, pl.BlockSpec((rows, 1), lambda i: (0, 0))]
    return pl.pallas_call(
        functools.partial(project_kernel, kinds, normalize),
        name="project_kv" if normalize else "project_q",
        grid=(len(kinds),),
        out_shape=out_shape,
        in_specs=[whole]
        + [pl.BlockSpec((1, size, width), lambda i: (i + first, 0, 0))] * 4
        + [table, table, pl.BlockSpec((1, depth), lambda i: (0, 0))],
        out_specs=out_specs,
        compiler_params=pltpu.CompilerParams(vmem_limit_bytes=VMEM_BYTES),
        cost_estimate=LIGHT,
    )(x, *pieces, cos, sin, gain)


def head_mask(block, head):
    lane = lax.broadcasted_iota(jnp.int32, block.shape, 1)
    inside = (lane < HDIM) if head == 0 else (lane >= HDIM)
    return jnp.where(inside, block, jnp.zeros_like(block))


def own_mask(key_count, row0, low_row):
    key = lax.broadcasted_iota(jnp.int32, (key_count, QROWS), 0)
    query = row0 + lax.broadcasted_iota(jnp.int32, (key_count, QROWS), 1)
    return (key >= low_row) & (key <= query)


def peer_mask(key_count, low_row, offset):
    key = lax.broadcasted_iota(jnp.int32, (key_count, QROWS), 0) - offset
    return key >= low_row


def key_windows(need, total):
    counts = list(range(QROWS, total + 1, QROWS))
    for place, count in enumerate(counts):
        chosen = need < 0 if place == 0 else need < -counts[place - 1]
        if count < total:
            chosen = jnp.logical_and(chosen, need >= -count)
        yield count, chosen


def own_forward_kernel(q_ref, k_ref, v_ref, low_ref, out_ref, log_ref):
    rows = q_ref.shape[0]
    v_t = v_ref[...].T
    for r in range(0, rows, QROWS):
        count = r + QROWS
        allowed = own_mask(count, r, low_ref[:, r : r + QROWS])
        keys = k_ref[0:count, :]
        outs = []
        for head in range(LANES // HDIM):
            scores = dotf(keys, head_mask(q_ref[r : r + QROWS, :], head), NT)
            scores = jnp.where(allowed, scores, masked_score)
            peak = jnp.max(scores, axis=0, keepdims=True)
            weights = jnp.exp(scores - peak)
            total = jnp.sum(weights, axis=0, keepdims=True)
            part = dotf(v_t[head * HDIM : (head + 1) * HDIM, 0:count], weights.astype(BF), NN)
            outs.append(part / total)
            log_ref[0, head : head + 1, r : r + QROWS] = peak + jnp.log(total)
        out_ref[r : r + QROWS, :] = jnp.concatenate(outs, axis=0).T


def peer_forward_kernel(
    need_ref, q_ref, k_ref, v_ref, low_ref, part_ref, log_in_ref, out_ref, log_ref
):
    rows = q_ref.shape[0]
    key_total = k_ref.shape[0]
    for index, r in enumerate(range(0, rows, QROWS)):
        for key_count, chosen in key_windows(need_ref[index], key_total):

            @pl.when(chosen)
            def _():
                window = slice(key_total - key_count, key_total)
                v_t = v_ref[window, :].T
                allowed = peer_mask(key_count, low_ref[:, r : r + QROWS], key_count)
                before = part_ref[r : r + QROWS, :].T
                outs = []
                for head in range(LANES // HDIM):
                    scores = dotf(k_ref[window, :], head_mask(q_ref[r : r + QROWS, :], head), NT)
                    scores = jnp.where(allowed, scores, masked_score)
                    log_own = log_in_ref[0, head : head + 1, r : r + QROWS]
                    peak = jnp.maximum(jnp.max(scores, axis=0, keepdims=True), log_own)
                    weights = jnp.exp(scores - peak)
                    own_weight = jnp.exp(log_own - peak)
                    total = jnp.sum(weights, axis=0, keepdims=True) + own_weight
                    rows_h = slice(head * HDIM, (head + 1) * HDIM)
                    part = dotf(v_t[rows_h, :], weights.astype(BF), NN)
                    outs.append((part + before[rows_h, :] * own_weight) / total)
                    log_ref[0, head : head + 1, r : r + QROWS] = peak + jnp.log(total)
                out_ref[r : r + QROWS, :] = jnp.concatenate(outs, axis=0).T.astype(BF)

        @pl.when(need_ref[index] >= 0)
        def _():
            out_ref[r : r + QROWS, :] = part_ref[r : r + QROWS, :].astype(BF)
            log_ref[:, :, r : r + QROWS] = log_in_ref[:, :, r : r + QROWS]


def pair_spec(rows):
    return pl.BlockSpec((rows, LANES), lambda i: (0, i))


def stacked_spec(rows, part):
    return pl.BlockSpec((None, rows, LANES), lambda i: (part, 0, i))


def log_spec(rows):
    return pl.BlockSpec((1, LANES // HDIM, rows), lambda i: (i, 0, 0))


def low_spec(rows):
    return pl.BlockSpec((1, rows), lambda i: (0, 0))


def own_forward(q, kv, low_row):
    rows, width = q.shape
    pairs = width // LANES
    return pl.pallas_call(
        own_forward_kernel,
        name="own_fwd",
        grid=(pairs,),
        out_shape=(
            jax.ShapeDtypeStruct((rows, width), F32),
            jax.ShapeDtypeStruct((pairs, LANES // HDIM, rows), F32),
        ),
        in_specs=[
            pair_spec(rows),
            stacked_spec(rows, 0),
            stacked_spec(rows, 1),
            low_spec(rows),
        ],
        out_specs=(pair_spec(rows), log_spec(rows)),
        compiler_params=pltpu.CompilerParams(vmem_limit_bytes=VMEM_BYTES),
        cost_estimate=LIGHT,
    )(q, kv, kv, low_row)


SMEM_SPEC = pl.BlockSpec(memory_space=pltpu.SMEM)


def peer_forward(need, q, kv, low_row, part, log_in):
    rows, width = q.shape
    pairs = width // LANES
    return pl.pallas_call(
        peer_forward_kernel,
        name="peer_fwd",
        grid=(pairs,),
        out_shape=(
            jax.ShapeDtypeStruct((rows, width), BF),
            jax.ShapeDtypeStruct((pairs, LANES // HDIM, rows), F32),
        ),
        in_specs=[
            SMEM_SPEC,
            pair_spec(rows),
            stacked_spec(rows, 0),
            stacked_spec(rows, 1),
            low_spec(rows),
            pair_spec(rows),
            log_spec(rows),
        ],
        out_specs=(pair_spec(rows), log_spec(rows)),
        compiler_params=pltpu.CompilerParams(vmem_limit_bytes=VMEM_BYTES),
        cost_estimate=LIGHT,
    )(need, q, kv, kv, low_row, part, log_in)


def backward_block(q_rows, k_rows, v_rows, k_t, do_rows, do_o_t, logs, allowed):
    d_query, d_key, d_value = [], None, None
    for head in range(LANES // HDIM):
        rows_h = slice(head * HDIM, (head + 1) * HDIM)
        q_head = head_mask(q_rows, head)
        do_head = head_mask(do_rows, head)
        scores = dotf(k_rows, q_head, NT)
        probs = jnp.exp(jnp.where(allowed, scores, masked_score) - logs[head])
        delta = jnp.sum(do_o_t[rows_h, :], axis=0, keepdims=True)
        d_probs = dotf(v_rows, do_head, NT)
        d_scores = (probs * (d_probs - delta)).astype(BF)
        d_v = dotf(probs.astype(BF), do_head, NN)
        d_k = dotf(d_scores, q_head, NN)
        d_value = d_v if d_value is None else d_value + d_v
        d_key = d_k if d_key is None else d_key + d_k
        d_query.append(dotf(k_t[rows_h, :], d_scores, NN))
    return jnp.concatenate(d_query, axis=0), d_key, d_value


def output_product(do_ref, o_ref, window):
    product = do_ref[window].astype(F32) * o_ref[window].astype(F32)
    return product.T


def peer_backward_kernel(
    need_ref, q_ref, k_ref, v_ref, do_ref, o_ref, low_ref, log_ref, dq_ref, dkv_ref, sums
):
    rows = q_ref.shape[0]
    key_total = k_ref.shape[0]
    sums[...] = jnp.zeros_like(sums)
    for index, r in enumerate(range(0, rows, QROWS)):
        rows_q = (slice(r, r + QROWS), slice(None))
        for key_count, chosen in key_windows(need_ref[index], key_total):

            @pl.when(chosen)
            def _():
                window = slice(key_total - key_count, key_total)
                allowed = peer_mask(key_count, low_ref[:, r : r + QROWS], key_count)
                logs = [log_ref[0, h : h + 1, r : r + QROWS] for h in range(LANES // HDIM)]
                d_query, d_key, d_value = backward_block(
                    q_ref[rows_q],
                    k_ref[window, :],
                    v_ref[window, :],
                    k_ref[window, :].T,
                    do_ref[rows_q],
                    output_product(do_ref, o_ref, rows_q),
                    logs,
                    allowed,
                )
                dq_ref[rows_q] = d_query.T
                sums[0, window] += d_key
                sums[1, window] += d_value

        @pl.when(need_ref[index] >= 0)
        def _():
            dq_ref[rows_q] = jnp.zeros((QROWS, LANES), F32)

    dkv_ref[...] = sums[...].astype(BF)


def peer_backward(need, q, kv, do, o, low_row, logs):
    rows, width = q.shape
    pairs = width // LANES
    return pl.pallas_call(
        peer_backward_kernel,
        name="peer_bwd",
        grid=(pairs,),
        out_shape=(
            jax.ShapeDtypeStruct((rows, width), F32),
            jax.ShapeDtypeStruct((2, rows, width), BF),
        ),
        in_specs=[
            SMEM_SPEC,
            pair_spec(rows),
            stacked_spec(rows, 0),
            stacked_spec(rows, 1),
            pair_spec(rows),
            pair_spec(rows),
            low_spec(rows),
            log_spec(rows),
        ],
        out_specs=(pair_spec(rows), pl.BlockSpec((2, rows, LANES), lambda i: (0, 0, i))),
        scratch_shapes=[pltpu.VMEM((2, rows, LANES), F32)],
        compiler_params=pltpu.CompilerParams(vmem_limit_bytes=VMEM_BYTES),
        cost_estimate=LIGHT,
    )(need, q, kv, kv, do, o, low_row, logs)


def own_backward_kernel(
    q_ref,
    k_ref,
    v_ref,
    do_ref,
    o_ref,
    low_ref,
    log_ref,
    dq_in_ref,
    cos_ref,
    sin_ref,
    dq_ref,
    dk_ref,
    dv_ref,
    sums,
):
    rows = q_ref.shape[0]
    sums[...] = jnp.zeros_like(sums)
    k_t = k_ref[...].T
    for r in range(0, rows, QROWS):
        count = r + QROWS
        window = (slice(r, r + QROWS), slice(None))
        allowed = own_mask(count, r, low_ref[:, r : r + QROWS])
        logs = [log_ref[0, h : h + 1, r : r + QROWS] for h in range(LANES // HDIM)]
        d_query, d_key, d_value = backward_block(
            q_ref[window],
            k_ref[0:count, :],
            v_ref[0:count, :],
            k_t[:, 0:count],
            do_ref[window],
            output_product(do_ref, o_ref, window),
            logs,
            allowed,
        )
        rotated = (d_query.T + dq_in_ref[window]) * (HDIM**-0.5)
        turned = rotated * cos_ref[window] - swap_halves(rotated) * sin_ref[window]
        dq_ref[window] = turned.astype(BF)
        sums[0, 0:count] += d_key
        sums[1, 0:count] += d_value
    dk_ref[...] = sums[0]
    dv_ref[...] = sums[1]


def own_backward(q, kv, do, o, low_row, logs, dq_in, cos, sin):
    rows, width = q.shape
    pairs = width // LANES
    table = pl.BlockSpec((rows, LANES), lambda i: (0, 0))
    return pl.pallas_call(
        own_backward_kernel,
        name="own_bwd",
        grid=(pairs,),
        out_shape=(
            jax.ShapeDtypeStruct((rows, width), BF),
            jax.ShapeDtypeStruct((rows, width), F32),
            jax.ShapeDtypeStruct((rows, width), F32),
        ),
        in_specs=[
            pair_spec(rows),
            stacked_spec(rows, 0),
            stacked_spec(rows, 1),
            pair_spec(rows),
            pair_spec(rows),
            low_spec(rows),
            log_spec(rows),
            pair_spec(rows),
            table,
            table,
        ],
        out_specs=(pair_spec(rows),) * 3,
        scratch_shapes=[pltpu.VMEM((2, rows, LANES), F32)],
        compiler_params=pltpu.CompilerParams(vmem_limit_bytes=VMEM_BYTES),
        cost_estimate=LIGHT,
    )(q, kv, kv, do, o, low_row, logs, dq_in, cos, sin)


def finish_keys_kernel(dk_ref, dv_ref, dk_in_ref, dv_in_ref, cos_ref, sin_ref, dk_out, dv_out):
    total = dk_ref[...] + dk_in_ref[...].astype(F32)
    turned = total * cos_ref[...] - swap_halves(total) * sin_ref[...]
    dk_out[...] = turned.astype(BF)
    dv_out[...] = (dv_ref[...] + dv_in_ref[...].astype(F32)).astype(BF)


def finish_keys(dk, dv, dkv_in, cos, sin):
    rows, width = dk.shape
    pairs = width // LANES
    table = pl.BlockSpec((rows, LANES), lambda i: (0, 0))
    return pl.pallas_call(
        finish_keys_kernel,
        name="finish_keys",
        grid=(pairs,),
        out_shape=(jax.ShapeDtypeStruct((rows, width), BF),) * 2,
        in_specs=[pair_spec(rows), pair_spec(rows), stacked_spec(rows, 0), stacked_spec(rows, 1)]
        + [table, table],
        out_specs=(pair_spec(rows),) * 2,
        cost_estimate=LIGHT,
    )(dk, dv, dkv_in, dkv_in, cos, sin)


def branch_kernel(stream_ref, att_ref, gain_ref, *refs):
    pieces, (hidden_ref, normed_ref, scale_ref) = refs[:4], refs[4:]
    for j, piece in enumerate(pieces):
        columns = piece_columns(j, piece.shape[1])
        term = dotf(att_ref[...], piece[...], NN)
        hidden_ref[:, columns] = stream_ref[:, columns].astype(F32) + term
    hidden = hidden_ref[...]
    mean = jnp.sum(hidden * hidden, axis=1, keepdims=True) / hidden.shape[1]
    scale = lax.rsqrt(mean + norm_eps)
    scale_ref[...] = scale
    normed_ref[...] = (hidden * scale * gain_ref[...]).astype(BF)


def add_branch(stream, att, gain, pieces):
    rows, depth = stream.shape
    heads = att.shape[1]
    tile = pl.BlockSpec((QROWS, depth), lambda i: (i, 0))
    return pl.pallas_call(
        branch_kernel,
        name="branch",
        grid=(rows // QROWS,),
        out_shape=(
            jax.ShapeDtypeStruct((rows, depth), F32),
            jax.ShapeDtypeStruct((rows, depth), BF),
            jax.ShapeDtypeStruct((rows, 1), F32),
        ),
        in_specs=[
            tile,
            pl.BlockSpec((QROWS, heads), lambda i: (i, 0)),
            pl.BlockSpec((1, depth), lambda i: (0, 0)),
        ]
        + [pl.BlockSpec(pieces[0].shape, lambda i: (0, 0))] * 4,
        out_specs=(tile, tile, pl.BlockSpec((QROWS, 1), lambda i: (i, 0))),
        compiler_params=pltpu.CompilerParams(vmem_limit_bytes=VMEM_BYTES),
        cost_estimate=LIGHT,
    )(stream, att, gain, *pieces)


def hidden_kernel(x_ref, *refs):
    w_in, (act_ref, by_gate_ref, by_up_ref) = refs[:4], refs[4:]
    rows = x_ref.shape[0]
    for r in range(0, rows, rows):
        part = slice(r, r + rows)
        gate = piece_dot(x_ref, part, [piece[0] for piece in w_in])
        up = piece_dot(x_ref, part, [piece[1] for piece in w_in])
        sig = jax.nn.sigmoid(gate)
        silu = gate * sig
        act_ref[part, :] = (silu * up).astype(BF)
        by_gate_ref[part, :] = (up * sig * (1.0 + gate * (1.0 - sig))).astype(BF)
        by_up_ref[part, :] = silu.astype(BF)


def hidden_units(x, w_in):
    rows, depth = x.shape
    _, size, units = w_in[0].shape
    tile = 256
    part = pl.BlockSpec((rows, tile), lambda i: (0, i))
    return pl.pallas_call(
        hidden_kernel,
        grid=(units // tile,),
        out_shape=(jax.ShapeDtypeStruct((rows, units), BF),) * 3,
        in_specs=[pl.BlockSpec((rows, depth), lambda i: (0, 0))]
        + [pl.BlockSpec((2, size, tile), lambda i: (0, 0, i))] * 4,
        out_specs=(part,) * 3,
        compiler_params=pltpu.CompilerParams(vmem_limit_bytes=VMEM_BYTES),
        cost_estimate=LIGHT,
        name="hidden",
    )(x, *w_in)


def hidden_back_kernel(cot_ref, by_gate_ref, by_up_ref, *refs):
    w_down, (dg_ref, du_ref) = refs[:4], refs[4:]
    rows = cot_ref.shape[0]
    for r in range(0, rows, rows):
        part = slice(r, r + rows)
        d_act = piece_dot(cot_ref, part, [piece[...] for piece in w_down], NT)
        dg_ref[part, :] = (d_act * by_gate_ref[part, :].astype(F32)).astype(BF)
        du_ref[part, :] = (d_act * by_up_ref[part, :].astype(F32)).astype(BF)


def hidden_back(cot, by_gate, by_up, w_down):
    rows, depth = cot.shape
    units, size = w_down[0].shape
    tile = 256
    part = pl.BlockSpec((rows, tile), lambda i: (0, i))
    return pl.pallas_call(
        hidden_back_kernel,
        grid=(units // tile,),
        out_shape=(jax.ShapeDtypeStruct((rows, units), BF),) * 2,
        in_specs=[pl.BlockSpec((rows, depth), lambda i: (0, 0)), part, part]
        + [pl.BlockSpec((tile, size), lambda i: (i, 0))] * 4,
        out_specs=(part,) * 2,
        compiler_params=pltpu.CompilerParams(vmem_limit_bytes=VMEM_BYTES),
        cost_estimate=LIGHT,
        name="hidden_back",
    )(cot, by_gate, by_up, *w_down)


def phased(i, block, make_index, tiles):
    def index_map(j, t):
        return make_index(jnp.where(j < i, 0, jnp.where(j == i, t, tiles - 1)))

    return pl.BlockSpec(block, index_map)


def columns_call(kernel_dot, lefts, pieces, block, make_index, size, flops, name):
    rows = lefts[0].shape[0]
    tile = min(size, 256)
    tiles = size // tile
    depth = size * 4

    def kernel(*refs):
        left_refs, piece_refs, out_ref = refs[: len(lefts)], refs[len(lefts) : -1], refs[-1]
        for j, piece in enumerate(piece_refs):

            @pl.when(pl.program_id(0) == j)
            def _():
                out_ref[...] = kernel_dot([left[...] for left in left_refs], piece).astype(BF)

    def out_index(j, t):
        return (0, (lax.axis_index("fsdp") ^ j) * tiles + t)

    return pl.pallas_call(
        kernel,
        grid=(4, tiles),
        out_shape=jax.ShapeDtypeStruct((rows, depth), BF),
        in_specs=[pl.BlockSpec(left.shape, lambda j, t: (0, 0)) for left in lefts]
        + [phased(i, block(tile), make_index, tiles) for i in range(4)],
        out_specs=pl.BlockSpec((rows, tile), out_index),
        compiler_params=pltpu.CompilerParams(vmem_limit_bytes=VMEM_BYTES),
        cost_estimate=LIGHT,
        name=name,
    )(*lefts, *pieces)


def stacked_columns(lefts, pieces, name):
    count, size, inner = pieces[0].shape

    def product(parts, piece):
        return sum(dotf(parts[c], piece[c], NT) for c in range(count))

    return columns_call(
        product,
        lefts,
        pieces,
        lambda tile: (count, tile, inner),
        lambda t: (0, t, 0),
        size,
        8 * lefts[0].shape[0] * size * inner * count,
        name,
    )


def plain_columns(left, pieces, name):
    inner, size = pieces[0].shape
    return columns_call(
        lambda parts, piece: dotf(parts[0], piece[...], NN),
        [left],
        pieces,
        lambda tile: (inner, tile),
        lambda t: (0, t),
        size,
        8 * left.shape[0] * size * inner,
        name,
    )


def branch_back_kernel(shares, d_mid_ref, hidden_ref, cot_ref, scale_ref, gain_ref, *refs):
    pieces, (d_hidden_ref, d_att_ref, gain_out_ref) = refs[:4], refs[4:7]
    d_mid = d_mid_ref[...].astype(F32)
    hidden = hidden_ref[...]
    scale = scale_ref[...]
    weighted = d_mid * gain_ref[...]
    inner = jnp.sum(weighted * hidden, axis=1, keepdims=True) / hidden.shape[1]
    d_hidden = (
        cot_ref[...].astype(F32) * (1.0 / shares)
        + scale * weighted
        - hidden * (scale * scale * scale * inner)
    )
    gain_term = jnp.sum(d_mid * hidden * scale, axis=0, keepdims=True)

    @pl.when(pl.program_id(0) == 0)
    def _():
        gain_out_ref[...] = gain_term

    @pl.when(pl.program_id(0) != 0)
    def _():
        gain_out_ref[...] += gain_term

    d_hidden_ref[...] = d_hidden.astype(BF)
    heads = d_att_ref.shape[1]
    for e in range(0, heads, 512):
        columns = slice(e, e + 512)
        d_att_ref[:, columns] = piece_dot(
            d_hidden_ref, slice(None), [piece[columns, :] for piece in pieces], NT
        ).astype(BF)


def branch_back(d_mid, hidden, cot, scale, gain, pieces):
    rows, depth = hidden.shape
    heads, size = pieces[0].shape
    tile = pl.BlockSpec((QROWS, depth), lambda i: (i, 0))
    row = pl.BlockSpec((1, depth), lambda i: (0, 0))
    return pl.pallas_call(
        functools.partial(branch_back_kernel, lax.axis_size("tensor")),
        name="branch_back",
        grid=(rows // QROWS,),
        in_specs=[tile, tile, tile, pl.BlockSpec((QROWS, 1), lambda i: (i, 0)), row]
        + [pl.BlockSpec((heads, size), lambda i: (0, 0))] * 4,
        out_specs=(tile, pl.BlockSpec((QROWS, heads), lambda i: (i, 0)), row),
        out_shape=(
            jax.ShapeDtypeStruct((rows, depth), BF),
            jax.ShapeDtypeStruct((rows, heads), BF),
            jax.ShapeDtypeStruct((1, depth), F32),
        ),
        compiler_params=pltpu.CompilerParams(vmem_limit_bytes=VMEM_BYTES),
        cost_estimate=LIGHT,
    )(d_mid, hidden, cot, scale, gain, *pieces)


def grad_call(left, right, cut, place, adds, name, span=(0, 1)):
    rows = left.shape[0]
    size = (left, right)[cut].shape[1] // 4
    swept = (right, left)[cut].shape[1] // span[1]
    height, width = (size, swept) if cut == 0 else (swept, size)
    tile = min(1024, swept)
    offset = span[0] * (swept // tile)
    block = (height, tile) if cut == 0 else (tile, width)

    def owner():
        return lax.axis_index("fsdp") ^ place

    def swept_index(t):
        return (0, t) if cut == 0 else (t, 0)

    def kernel(left_ref, right_ref, *refs):
        add_refs, out_ref = refs[: len(adds)], refs[len(adds)]
        if cut == 0:
            turned = refs[-1]

            @pl.when(pl.program_id(0) == 0)
            def _():
                turned[...] = left_ref[...].T

            result = dotf(turned[...], right_ref[...], NN)
        else:
            result = dotf(left_ref[...].T, right_ref[...], NN)
        for add in add_refs:
            result = result + add[...].astype(F32)
        out_ref[...] = result.astype(BF)

    fixed = pl.BlockSpec((rows, size), lambda t: (0, owner()))
    moving = pl.BlockSpec((rows, tile), lambda t: (0, t + offset))
    return pl.pallas_call(
        kernel,
        grid=(swept // tile,),
        out_shape=jax.ShapeDtypeStruct((height, width), BF),
        in_specs=[fixed, moving] * (cut == 0)
        + [moving, fixed] * (cut == 1)
        + [pl.BlockSpec(block, swept_index)] * len(adds),
        out_specs=pl.BlockSpec(block, swept_index),
        scratch_shapes=[pltpu.VMEM((size, rows), BF)] if cut == 0 else [],
        compiler_params=pltpu.CompilerParams(vmem_limit_bytes=VMEM_BYTES),
        cost_estimate=LIGHT,
        name=name,
    )(left, right, *adds)


class Reduction:
    def __init__(self, left, right, cut, name, span=(0, 1)):
        self.args, self.name, self.span = (left, right, cut), name, span

    def call(self, place, deps, step, adds=()):
        left, right, cut = self.args
        left = after(left, *deps) if deps else left
        return grad_call(left, right, cut, place, adds, self.name + step, self.span)

    def near_far(self, *deps):
        self.three = self.call(3, deps, "_3")
        self.for_two = swap(self.three, "fsdp", 1)

    def near(self, *deps):
        self.one = self.call(1, deps, "_1")
        self.for_own = swap(self.one, "fsdp", 1)

    def far(self, *deps):
        self.two = self.call(2, deps, "_2", [self.for_two])

    def send_far(self, *deps):
        self.across = swap(after(self.two, *deps), "fsdp", 2)

    def mine(self, *deps):
        self.own = self.call(0, deps, "_0", [self.for_own, self.across])

    def send_context(self, *deps):
        self.other = swap(after(self.own, *deps), "context", 1)


def totals_kernel(slots, *refs):
    pairs, out_ref = refs[:-1], refs[-1]
    for slot in range(len(pairs) // 2):
        total = pairs[2 * slot][...].astype(F32) + pairs[2 * slot + 1][...].astype(F32)
        if slots == 0:
            out_ref[slot] = total
        else:
            out_ref[:, slot, :] = total


def totals(sums, slots, *deps):
    arrays = [array for part in sums for array in (part.own, part.other)]
    if deps:
        arrays[0] = after(arrays[0], *deps)
    rows, width = arrays[0].shape
    tile = 128
    shape = [rows, width]
    shape.insert(slots, len(sums))
    block = [tile, width]
    block.insert(slots, len(sums))
    return pl.pallas_call(
        functools.partial(totals_kernel, slots),
        grid=(rows // tile,),
        out_shape=jax.ShapeDtypeStruct(tuple(shape), F32),
        in_specs=[pl.BlockSpec((tile, width), lambda i: (i, 0))] * len(arrays),
        out_specs=pl.BlockSpec(
            tuple(block), (lambda i: (0, i, 0)) if slots == 0 else (lambda i: (i, 0, 0))
        ),
        compiler_params=pltpu.CompilerParams(vmem_limit_bytes=VMEM_BYTES),
        cost_estimate=LIGHT,
        name="totals",
    )(*arrays)


def row_sum(values_in):
    return jnp.sum(values_in, axis=1, keepdims=True)


def per_device(tokens, w_qkv, w_out, w_gate_up, w_down, gains, seq_lengths, cotangent):
    row_count, part_width = tokens.shape
    tensor_index = lax.axis_index("tensor")
    context_index = lax.axis_index("context")
    full_width = part_width * lax.axis_size("tensor")

    def features(part_in):
        return lax.all_gather(part_in, "tensor", axis=1, tiled=True)

    def feature_sum(term):
        return lax.psum_scatter(term.astype(BF), "tensor", scatter_dimension=1, tiled=True)

    def own_features(full):
        return lax.dynamic_slice_in_dim(full, tensor_index * part_width, part_width, 1)

    ending = jnp.cumsum(seq_lengths[0])
    starts = ending - seq_lengths[0]
    places = context_index * row_count + jnp.arange(row_count, dtype=jnp.int32)
    first_token = jnp.max(jnp.where(starts[None, :] <= places[:, None], starts[None, :], 0), axis=1)
    cos, sin = rope_tables(places - first_token)
    low = first_token - context_index * row_count
    low_row = low[None, :]
    need = low[::QROWS]

    token_low = features(tokens)
    gain_near, gain_full = gather_gains(gains)
    gain_attn, gain_mlp = gain_full[0:1], gain_full[1:2]

    qkv_own = jnp.swapaxes(w_qkv, 0, 1)
    half = qkv_own.shape[1] // 2
    far_half = swap(
        lax.dynamic_slice_in_dim(after(qkv_own, gain_near), context_index * half, half, 1),
        "fsdp",
        2,
    )
    other_half = swap(far_half, "context", 1)
    qkv_far = jnp.where(
        context_index == 0,
        jnp.concatenate([far_half, other_half], axis=1),
        jnp.concatenate([other_half, far_half], axis=1),
    )
    qkv_near = swap(qkv_own, "fsdp", 1)
    qkv = (qkv_own, qkv_near, qkv_far, swap(qkv_far, "fsdp", 1))

    gate_up_own = jnp.swapaxes(w_gate_up, 0, 1)
    cut = gate_up_own.shape[1] * 12 // 32
    gate_up_a = swap(after(gate_up_own[:, :cut], far_half), "fsdp", 2)
    gate_up_b = swap(after(gate_up_own[:, cut:], gate_up_a), "fsdp", 2)

    keys_values, normed_in, scale_attn = project(
        after(token_low, gate_up_a), qkv, cos, sin, gain_attn, (1.0, None), 1, True
    )
    peer_kv = lax.ppermute(keys_values, "context", [(0, 1)])
    queries = project(normed_in, qkv, cos, sin, gain_attn, (HDIM**-0.5,), 0, False)[0][0]
    part, part_log = own_forward(queries, keys_values, low_row)
    attended, logs = peer_forward(
        need, queries, peer_kv, low_row, after(part, gate_up_b), part_log
    )
    cot_first = features(after(cotangent[:QROWS], other_half))
    attended_full = features(after(attended, cot_first))

    out_own = lax.all_gather(after(w_out, other_half), "tensor", axis=0, tiled=True)
    out_near = swap(out_own, "fsdp", 1)
    out_far = swap(out_own, "fsdp", 2)
    out_far_near = swap(out_far, "fsdp", 1)
    out = (out_own, out_near, out_far, out_far_near)
    gate_up_own, gate_up_a, gate_up_b = lax.optimization_barrier(
        (gate_up_own, gate_up_a, gate_up_b, attended)
    )[:3]
    gate_up_far = jnp.concatenate([gate_up_a, gate_up_b], axis=1)
    gate_up_near = swap(gate_up_own, "fsdp", 1)
    gate_up = (gate_up_own, gate_up_near, gate_up_far, swap(gate_up_far, "fsdp", 1))
    cot_rest = features(after(cotangent[QROWS:], attended_full, out_far_near, out_near))
    cot_full = jnp.concatenate([cot_first, cot_rest], axis=0)
    down_far = swap(after(w_down, attended_full, out_far_near), "fsdp", 2)
    down_near = swap(after(w_down, attended_full), "fsdp", 1)
    hidden, normed_mid, scale_mlp = add_branch(token_low, attended_full, gain_mlp, out)

    activated, by_gate, by_up = hidden_units(normed_mid, gate_up)
    down_far = after(down_far, activated)
    down = (w_down, down_near, down_far, swap(down_far, "fsdp", 1))
    d_gate, d_up = hidden_back(after(cot_full, activated), by_gate, by_up, down)
    d_mid_term = stacked_columns([d_gate, d_up], gate_up, "d_mid")
    d_hidden_term, d_att_term, gain_mlp_term = branch_back(
        d_mid_term, hidden, cot_full, scale_mlp, gain_mlp, out
    )
    d_attended = feature_sum(d_att_term)
    d_hidden_own = feature_sum(after(d_hidden_term, d_att_term))

    square = lax.axis_size("tensor") == lax.axis_size("fsdp")
    down_a, down_b = (
        Reduction(activated, cot_full, 1, "grad_down", (part_index, 2)) for part_index in (0, 1)
    )
    grad_gate = Reduction(normed_mid, d_gate, 0, "grad_gate")
    grad_up = Reduction(normed_mid, d_up, 0, "grad_up")
    down_a.near_far(d_att_term)
    down_b.near_far(down_a.three)
    grad_gate.near_far(down_b.three)
    down_a.far(grad_gate.three)
    down_a.send_far()
    down_b.far(down_a.two)
    down_b.send_far()
    down_a.near(down_b.two)
    down_b.near(down_a.one)
    grad_gate.far(down_b.one)
    grad_gate.send_far()
    grad_gate.near(grad_gate.two)
    down_a.mine(grad_gate.one)
    down_a.send_context()
    grad_up.near_far(down_a.own)
    grad_up.near(grad_up.three)
    down_b.mine(grad_up.one)
    down_b.send_context()

    dq_peer, dkv_peer = peer_backward(
        need, queries, peer_kv, after(d_attended, down_b.own, down_a.other), attended, low_row, logs
    )
    dkv_in = lax.ppermute(dkv_peer, "context", [(1, 0)])
    d_query, dk_own, dv_own = own_backward(
        queries, keys_values, d_attended, attended, low_row, logs, dq_peer, cos, sin
    )
    grad_query = Reduction(normed_in, d_query, 0, "grad_query")
    grad_up.far(d_query)
    grad_up.send_far()
    grad_query.near_far(grad_up.two)
    grad_query.near(grad_query.three)
    mlp_term = plain_columns(after(activated, grad_query.one), down, "mlp_out")
    grad_gate.mine(mlp_term, dkv_in, down_b.other)
    grad_gate.send_context()
    mlp_out = feature_sum(after(mlp_term, d_hidden_own))
    d_key, d_value = finish_keys(dk_own, dv_own, after(dkv_in, grad_gate.own), cos, sin)
    grad_up.mine(d_value)
    grad_up.send_context()
    d_in_term = stacked_columns(
        [d_query, d_key, after(d_value, grad_up.own, grad_gate.other)], qkv, "d_in"
    )
    d_in = feature_sum(d_in_term).astype(F32)

    if square:
        grad_out = Reduction(attended_full, d_hidden_own, 0, "grad_out")
    else:
        grad_out = Reduction(attended, features(d_hidden_own), 1, "grad_out")
    grad_query.far(d_in_term)
    grad_query.send_far()
    grad_key = Reduction(normed_in, d_key, 0, "grad_key")
    grad_value = Reduction(normed_in, d_value, 0, "grad_value")
    grad_key.near_far(grad_query.two)
    grad_value.near_far(grad_key.three)
    grad_key.near(grad_value.three)
    grad_value.near(grad_key.one)
    grad_key.far(grad_value.one)
    grad_key.send_far()
    grad_value.far(grad_key.two)
    grad_value.send_far()
    grad_out.near_far(grad_value.two)
    grad_out.near(grad_out.three)
    grad_out.far(grad_out.one)
    grad_out.send_far()
    grad_query.mine(grad_out.two)
    grad_query.send_context()

    stream = token_low.astype(F32)
    d_in_wide = after(d_in_term, grad_query.own).astype(F32)
    weighted = d_in_wide * stream
    inner_term = jnp.sum(weighted * gain_attn, axis=1)
    gain_attn_term = jnp.sum(weighted * scale_attn, axis=0)
    parts = lax.axis_size("tensor")
    totals_small = block_totals(
        jnp.concatenate(
            [
                jnp.broadcast_to(inner_term[None, :], (parts, row_count)),
                gain_attn_term.reshape(parts, part_width),
                gain_mlp_term.reshape(parts, part_width),
            ],
            axis=1,
        )[None]
    )
    inner_in = totals_small[0, :row_count][:, None] / full_width
    gain_sums = totals_small[0, row_count:].reshape(2, part_width)
    gain_sums = exchange(gain_sums, "fsdp", 1)
    gain_sums = exchange(gain_sums, "fsdp", 2)
    gain_sums = exchange(gain_sums, "context", 1)
    gain_width = gains.shape[1]
    grad_gains = lax.dynamic_slice_in_dim(
        gain_sums, lax.axis_index("fsdp") * gain_width, gain_width, 1
    )

    grad_down_sum = totals([down_a, down_b], 0, d_in_wide).reshape(w_down.shape)
    grad_key.mine(grad_down_sum, grad_up.other)
    grad_key.send_context()
    grad_value.mine(grad_key.own)
    grad_value.send_context()
    grad_out.mine(grad_value.own)
    if square:
        count = lax.axis_size("fsdp")
        across = [(i, (i % count) * count + i // count) for i in range(count * count)]
        grad_out.own = lax.ppermute(grad_out.own, ("fsdp", "tensor"), across)
    grad_out.send_context()
    grad_gate_up_sum = totals([grad_gate, grad_up], 1, grad_value.own)
    grad_qkv = totals([grad_query, grad_key, grad_value], 0, grad_gate_up_sum)
    grad_out_sum = totals([grad_out], 0, grad_qkv)[0]

    block_out = (own_features(hidden) + mlp_out.astype(F32)).astype(BF)
    own_tokens = tokens.astype(F32)
    grad_tokens = (
        d_hidden_own.astype(F32)
        + scale_attn * own_features(gain_attn) * d_in
        - own_tokens * scale_attn * scale_attn * scale_attn * inner_in
    ).astype(BF)
    return (
        block_out,
        grad_tokens,
        jnp.swapaxes(grad_qkv, 0, 1),
        grad_out_sum,
        grad_gate_up_sum,
        grad_down_sum,
        grad_gains,
    )


def solution(mesh):
    rows = P(("fsdp", "context"), "tensor")
    inner = P("fsdp", None, "tensor")
    outer = P("tensor", "fsdp")
    gain = P(None, ("tensor", "fsdp"))
    return jax.shard_map(
        per_device,
        mesh=mesh,
        in_specs=(rows, inner, outer, inner, outer, gain, P("fsdp", None), rows),
        out_specs=(rows, rows, inner, outer, inner, outer, gain),
        check_vma=False,
    )
```

```python
import functools

import jax
import jax.numpy as jnp
from jax import lax
from jax.experimental import pallas as pl
from jax.experimental.pallas import tpu as pltpu
from jax.sharding import PartitionSpec as P

HDIM = 64
LANES = 128
QROWS = 256
norm_eps = 1e-05
rope_base = 130000.0
masked_score = -1e30
BF = jnp.bfloat16
F32 = jnp.float32
VMEM_BYTES = 56 * 1024 * 1024
LIGHT = pl.CostEstimate(flops=1, bytes_accessed=1, transcendentals=0)


def dotf(a, b, dims):
    return lax.dot_general(a, b, (dims, ((), ())), preferred_element_type=F32)


NN = ((1,), (0,))
NT = ((1,), (1,))
TN = ((0,), (0,))


def swap(value, axis, bit):
    count = lax.axis_size(axis)
    return lax.ppermute(value, axis, [(i, i ^ bit) for i in range(count)])


def after(value, *others):
    return lax.optimization_barrier((value, *others))[0]


def shifted(value, axis):
    count = lax.axis_size(axis)
    return [
        lax.ppermute(value, axis, [(i, (i + step) % count) for i in range(count)])
        for step in range(1, count)
    ]


def exchange(value, axis, bit):
    return value + swap(value, axis, bit)


def join_kernel(axis, mode, *refs):
    pieces, out_ref = refs[:-1], refs[-1]
    count = len(pieces)
    me = lax.axis_index(axis)
    for step, piece in enumerate(pieces):
        size = piece.shape[1]
        place = (me ^ step) if mode == "xor" else (me - step + count) % count
        out_ref[:, pl.ds(pl.multiple_of(place * size, size), size)] = piece[...]


def join(pieces, axis, mode):
    rows, size = pieces[0].shape
    return pl.pallas_call(
        functools.partial(join_kernel, axis, mode),
        out_shape=jax.ShapeDtypeStruct((rows, size * len(pieces)), pieces[0].dtype),
        cost_estimate=LIGHT,
        name="join",
    )(*pieces)


def gather_gains(gains):
    if lax.axis_size("tensor") > 4 or gains.shape[1] % LANES:
        whole = lax.all_gather(gains, ("tensor", "fsdp"), axis=1, tiled=True).astype(F32)
        return gains, whole
    own = gains.astype(F32)
    part = join([own] + [swap(own, "fsdp", bit) for bit in (1, 2, 3)], "fsdp", "xor")
    return part, join([part] + shifted(part, "tensor"), "tensor", "shift")


def block_totals(blocks):
    count = lax.axis_size("tensor")
    me = lax.axis_index("tensor")
    if count > 4:
        return lax.dynamic_index_in_dim(lax.psum(blocks, "tensor"), me, 1, keepdims=False)

    def pick(place):
        return lax.dynamic_index_in_dim(blocks, place, 1, keepdims=False)

    total = pick(me)
    for step in range(1, count):
        moves = [(i, (i + step) % count) for i in range(count)]
        total = total + lax.ppermute(pick((me + step) % count), "tensor", moves)
    return total


def piece_columns(j, size):
    return pl.ds(pl.multiple_of((lax.axis_index("fsdp") ^ j) * size, size), size)


def swap_halves(block):
    lane = lax.broadcasted_iota(jnp.int32, block.shape, 1)
    up = pltpu.roll(block, LANES - HDIM // 2, 1)
    down = pltpu.roll(block, HDIM // 2, 1)
    return jnp.where((lane & (HDIM - 1)) < HDIM // 2, up, down)


def rope_tables(positions):
    lane = jnp.arange(LANES, dtype=jnp.int32)
    half = lane % (HDIM // 2)
    frequencies = rope_base ** (-2.0 * half.astype(F32) / HDIM)
    angles = positions.astype(F32)[:, None] * frequencies[None, :]
    sign = jnp.where((lane % HDIM) < HDIM // 2, -1.0, 1.0)
    return jnp.cos(angles), jnp.sin(angles) * sign[None, :]


def piece_dot(x_ref, rows, pieces, dims=NN):
    total = None
    for j, piece in enumerate(pieces):
        size = piece.shape[dims[1][0]]
        term = dotf(x_ref[rows, piece_columns(j, size)], piece, dims)
        total = term if total is None else total + term
    return total


def project_kernel(kinds, normalize, x_ref, *refs):
    pieces, (cos_ref, sin_ref, gain_ref), outs = refs[:4], refs[4:7], refs[7:]
    out_ref = outs[0]
    rows, width = out_ref.shape[1:]
    step = pl.program_id(0)
    if normalize:
        normed_ref, scale_ref = outs[1], outs[2]

        @pl.when(step == 0)
        def _():
            for r in range(0, rows, QROWS):
                part = slice(r, r + QROWS)
                stream = x_ref[part, :].astype(F32)
                mean = jnp.sum(stream * stream, axis=1, keepdims=True) / x_ref.shape[1]
                scale = lax.rsqrt(mean + norm_eps)
                scale_ref[part, :] = scale
                normed_ref[part, :] = (stream * scale * gain_ref[...]).astype(BF)

        x_ref = normed_ref
    for index, scale in enumerate(kinds):

        @pl.when(step == index)
        def _():
            for r in range(0, rows, rows):
                part = slice(r, r + rows)
                result = piece_dot(x_ref, part, [piece[0] for piece in pieces])
                for c in range(0, width, LANES):
                    block = result[:, c : c + LANES]
                    if scale:
                        block = block * cos_ref[part, :] + swap_halves(block) * sin_ref[part, :]
                    low = block.astype(BF)
                    if scale and scale != 1.0:
                        low = low * jnp.asarray(scale, BF)
                    out_ref[0, part, c : c + LANES] = low


def project(x, pieces, cos, sin, gain, kinds, first, normalize):
    rows, depth = x.shape
    _, size, width = pieces[0].shape
    flops = 2 * len(kinds) * rows * depth * width
    whole = pl.BlockSpec((rows, depth), lambda i: (0, 0))
    table = pl.BlockSpec((rows, LANES), lambda i: (0, 0))
    out_shape = [jax.ShapeDtypeStruct((len(kinds), rows, width), BF)]
    out_specs = [pl.BlockSpec((1, rows, width), lambda i: (i, 0, 0))]
    if normalize:
        out_shape += [jax.ShapeDtypeStruct((rows, depth), BF), jax.ShapeDtypeStruct((rows, 1), F32)]
        out_specs += [whole, pl.BlockSpec((rows, 1), lambda i: (0, 0))]
    return pl.pallas_call(
        functools.partial(project_kernel, kinds, normalize),
        name="project_kv" if normalize else "project_q",
        grid=(len(kinds),),
        out_shape=out_shape,
        in_specs=[whole]
        + [pl.BlockSpec((1, size, width), lambda i: (i + first, 0, 0))] * 4
        + [table, table, pl.BlockSpec((1, depth), lambda i: (0, 0))],
        out_specs=out_specs,
        compiler_params=pltpu.CompilerParams(vmem_limit_bytes=VMEM_BYTES),
        cost_estimate=LIGHT,
    )(x, *pieces, cos, sin, gain)


def head_mask(block, head):
    lane = lax.broadcasted_iota(jnp.int32, block.shape, 1)
    inside = (lane < HDIM) if head == 0 else (lane >= HDIM)
    return jnp.where(inside, block, jnp.zeros_like(block))


def own_mask(key_count, row0, low_row):
    key = lax.broadcasted_iota(jnp.int32, (key_count, QROWS), 0)
    query = row0 + lax.broadcasted_iota(jnp.int32, (key_count, QROWS), 1)
    return (key >= low_row) & (key <= query)


def peer_mask(key_count, low_row, offset):
    key = lax.broadcasted_iota(jnp.int32, (key_count, QROWS), 0) - offset
    return key >= low_row


def key_windows(need, total):
    counts = list(range(QROWS, total + 1, QROWS))
    for place, count in enumerate(counts):
        chosen = need < 0 if place == 0 else need < -counts[place - 1]
        if count < total:
            chosen = jnp.logical_and(chosen, need >= -count)
        yield count, chosen


def own_forward_kernel(q_ref, k_ref, v_ref, low_ref, out_ref, log_ref):
    rows = q_ref.shape[0]
    v_t = v_ref[...].T
    for r in range(0, rows, QROWS):
        count = r + QROWS
        allowed = own_mask(count, r, low_ref[:, r : r + QROWS])
        keys = k_ref[0:count, :]
        outs = []
        for head in range(LANES // HDIM):
            scores = dotf(keys, head_mask(q_ref[r : r + QROWS, :], head), NT)
            scores = jnp.where(allowed, scores, masked_score)
            peak = jnp.max(scores, axis=0, keepdims=True)
            weights = jnp.exp(scores - peak)
            total = jnp.sum(weights, axis=0, keepdims=True)
            part = dotf(v_t[head * HDIM : (head + 1) * HDIM, 0:count], weights.astype(BF), NN)
            outs.append(part / total)
            log_ref[0, head : head + 1, r : r + QROWS] = peak + jnp.log(total)
        out_ref[r : r + QROWS, :] = jnp.concatenate(outs, axis=0).T


def peer_forward_kernel(
    need_ref, q_ref, k_ref, v_ref, low_ref, part_ref, log_in_ref, out_ref, log_ref
):
    rows = q_ref.shape[0]
    key_total = k_ref.shape[0]
    for index, r in enumerate(range(0, rows, QROWS)):
        for key_count, chosen in key_windows(need_ref[index], key_total):

            @pl.when(chosen)
            def _():
                window = slice(key_total - key_count, key_total)
                v_t = v_ref[window, :].T
                allowed = peer_mask(key_count, low_ref[:, r : r + QROWS], key_count)
                before = part_ref[r : r + QROWS, :].T
                outs = []
                for head in range(LANES // HDIM):
                    scores = dotf(k_ref[window, :], head_mask(q_ref[r : r + QROWS, :], head), NT)
                    scores = jnp.where(allowed, scores, masked_score)
                    log_own = log_in_ref[0, head : head + 1, r : r + QROWS]
                    peak = jnp.maximum(jnp.max(scores, axis=0, keepdims=True), log_own)
                    weights = jnp.exp(scores - peak)
                    own_weight = jnp.exp(log_own - peak)
                    total = jnp.sum(weights, axis=0, keepdims=True) + own_weight
                    rows_h = slice(head * HDIM, (head + 1) * HDIM)
                    part = dotf(v_t[rows_h, :], weights.astype(BF), NN)
                    outs.append((part + before[rows_h, :] * own_weight) / total)
                    log_ref[0, head : head + 1, r : r + QROWS] = peak + jnp.log(total)
                out_ref[r : r + QROWS, :] = jnp.concatenate(outs, axis=0).T.astype(BF)

        @pl.when(need_ref[index] >= 0)
        def _():
            out_ref[r : r + QROWS, :] = part_ref[r : r + QROWS, :].astype(BF)
            log_ref[:, :, r : r + QROWS] = log_in_ref[:, :, r : r + QROWS]


def pair_spec(rows):
    return pl.BlockSpec((rows, LANES), lambda i: (0, i))


def stacked_spec(rows, part):
    return pl.BlockSpec((None, rows, LANES), lambda i: (part, 0, i))


def log_spec(rows):
    return pl.BlockSpec((1, LANES // HDIM, rows), lambda i: (i, 0, 0))


def low_spec(rows):
    return pl.BlockSpec((1, rows), lambda i: (0, 0))


def own_forward(q, kv, low_row):
    rows, width = q.shape
    pairs = width // LANES
    return pl.pallas_call(
        own_forward_kernel,
        name="own_fwd",
        grid=(pairs,),
        out_shape=(
            jax.ShapeDtypeStruct((rows, width), F32),
            jax.ShapeDtypeStruct((pairs, LANES // HDIM, rows), F32),
        ),
        in_specs=[
            pair_spec(rows),
            stacked_spec(rows, 0),
            stacked_spec(rows, 1),
            low_spec(rows),
        ],
        out_specs=(pair_spec(rows), log_spec(rows)),
        compiler_params=pltpu.CompilerParams(vmem_limit_bytes=VMEM_BYTES),
        cost_estimate=LIGHT,
    )(q, kv, kv, low_row)


SMEM_SPEC = pl.BlockSpec(memory_space=pltpu.SMEM)


def peer_forward(need, q, kv, low_row, part, log_in):
    rows, width = q.shape
    pairs = width // LANES
    return pl.pallas_call(
        peer_forward_kernel,
        name="peer_fwd",
        grid=(pairs,),
        out_shape=(
            jax.ShapeDtypeStruct((rows, width), BF),
            jax.ShapeDtypeStruct((pairs, LANES // HDIM, rows), F32),
        ),
        in_specs=[
            SMEM_SPEC,
            pair_spec(rows),
            stacked_spec(rows, 0),
            stacked_spec(rows, 1),
            low_spec(rows),
            pair_spec(rows),
            log_spec(rows),
        ],
        out_specs=(pair_spec(rows), log_spec(rows)),
        compiler_params=pltpu.CompilerParams(vmem_limit_bytes=VMEM_BYTES),
        cost_estimate=LIGHT,
    )(need, q, kv, kv, low_row, part, log_in)


def backward_block(q_rows, k_rows, v_rows, k_t, do_rows, do_o_t, logs, allowed):
    d_query, d_key, d_value = [], None, None
    for head in range(LANES // HDIM):
        rows_h = slice(head * HDIM, (head + 1) * HDIM)
        q_head = head_mask(q_rows, head)
        do_head = head_mask(do_rows, head)
        scores = dotf(k_rows, q_head, NT)
        probs = jnp.exp(jnp.where(allowed, scores, masked_score) - logs[head])
        delta = jnp.sum(do_o_t[rows_h, :], axis=0, keepdims=True)
        d_probs = dotf(v_rows, do_head, NT)
        d_scores = (probs * (d_probs - delta)).astype(BF)
        d_v = dotf(probs.astype(BF), do_head, NN)
        d_k = dotf(d_scores, q_head, NN)
        d_value = d_v if d_value is None else d_value + d_v
        d_key = d_k if d_key is None else d_key + d_k
        d_query.append(dotf(k_t[rows_h, :], d_scores, NN))
    return jnp.concatenate(d_query, axis=0), d_key, d_value


def output_product(do_ref, o_ref, window):
    product = do_ref[window].astype(F32) * o_ref[window].astype(F32)
    return product.T


def peer_backward_kernel(
    need_ref, q_ref, k_ref, v_ref, do_ref, o_ref, low_ref, log_ref, dq_ref, dkv_ref, sums
):
    rows = q_ref.shape[0]
    key_total = k_ref.shape[0]
    sums[...] = jnp.zeros_like(sums)
    for index, r in enumerate(range(0, rows, QROWS)):
        rows_q = (slice(r, r + QROWS), slice(None))
        for key_count, chosen in key_windows(need_ref[index], key_total):

            @pl.when(chosen)
            def _():
                window = slice(key_total - key_count, key_total)
                allowed = peer_mask(key_count, low_ref[:, r : r + QROWS], key_count)
                logs = [log_ref[0, h : h + 1, r : r + QROWS] for h in range(LANES // HDIM)]
                d_query, d_key, d_value = backward_block(
                    q_ref[rows_q],
                    k_ref[window, :],
                    v_ref[window, :],
                    k_ref[window, :].T,
                    do_ref[rows_q],
                    output_product(do_ref, o_ref, rows_q),
                    logs,
                    allowed,
                )
                dq_ref[rows_q] = d_query.T
                sums[0, window] += d_key
                sums[1, window] += d_value

        @pl.when(need_ref[index] >= 0)
        def _():
            dq_ref[rows_q] = jnp.zeros((QROWS, LANES), F32)

    dkv_ref[...] = sums[...].astype(BF)


def peer_backward(need, q, kv, do, o, low_row, logs):
    rows, width = q.shape
    pairs = width // LANES
    return pl.pallas_call(
        peer_backward_kernel,
        name="peer_bwd",
        grid=(pairs,),
        out_shape=(
            jax.ShapeDtypeStruct((rows, width), F32),
            jax.ShapeDtypeStruct((2, rows, width), BF),
        ),
        in_specs=[
            SMEM_SPEC,
            pair_spec(rows),
            stacked_spec(rows, 0),
            stacked_spec(rows, 1),
            pair_spec(rows),
            pair_spec(rows),
            low_spec(rows),
            log_spec(rows),
        ],
        out_specs=(pair_spec(rows), pl.BlockSpec((2, rows, LANES), lambda i: (0, 0, i))),
        scratch_shapes=[pltpu.VMEM((2, rows, LANES), F32)],
        compiler_params=pltpu.CompilerParams(vmem_limit_bytes=VMEM_BYTES),
        cost_estimate=LIGHT,
    )(need, q, kv, kv, do, o, low_row, logs)


def own_backward_kernel(
    q_ref,
    k_ref,
    v_ref,
    do_ref,
    o_ref,
    low_ref,
    log_ref,
    dq_in_ref,
    cos_ref,
    sin_ref,
    dq_ref,
    dk_ref,
    dv_ref,
    sums,
):
    rows = q_ref.shape[0]
    sums[...] = jnp.zeros_like(sums)
    k_t = k_ref[...].T
    for r in range(0, rows, QROWS):
        count = r + QROWS
        window = (slice(r, r + QROWS), slice(None))
        allowed = own_mask(count, r, low_ref[:, r : r + QROWS])
        logs = [log_ref[0, h : h + 1, r : r + QROWS] for h in range(LANES // HDIM)]
        d_query, d_key, d_value = backward_block(
            q_ref[window],
            k_ref[0:count, :],
            v_ref[0:count, :],
            k_t[:, 0:count],
            do_ref[window],
            output_product(do_ref, o_ref, window),
            logs,
            allowed,
        )
        rotated = (d_query.T + dq_in_ref[window]) * (HDIM**-0.5)
        turned = rotated * cos_ref[window] - swap_halves(rotated) * sin_ref[window]
        dq_ref[window] = turned.astype(BF)
        sums[0, 0:count] += d_key
        sums[1, 0:count] += d_value
    dk_ref[...] = sums[0]
    dv_ref[...] = sums[1]


def own_backward(q, kv, do, o, low_row, logs, dq_in, cos, sin):
    rows, width = q.shape
    pairs = width // LANES
    table = pl.BlockSpec((rows, LANES), lambda i: (0, 0))
    return pl.pallas_call(
        own_backward_kernel,
        name="own_bwd",
        grid=(pairs,),
        out_shape=(
            jax.ShapeDtypeStruct((rows, width), BF),
            jax.ShapeDtypeStruct((rows, width), F32),
            jax.ShapeDtypeStruct((rows, width), F32),
        ),
        in_specs=[
            pair_spec(rows),
            stacked_spec(rows, 0),
            stacked_spec(rows, 1),
            pair_spec(rows),
            pair_spec(rows),
            low_spec(rows),
            log_spec(rows),
            pair_spec(rows),
            table,
            table,
        ],
        out_specs=(pair_spec(rows),) * 3,
        scratch_shapes=[pltpu.VMEM((2, rows, LANES), F32)],
        compiler_params=pltpu.CompilerParams(vmem_limit_bytes=VMEM_BYTES),
        cost_estimate=LIGHT,
    )(q, kv, kv, do, o, low_row, logs, dq_in, cos, sin)


def finish_keys_kernel(dk_ref, dv_ref, dk_in_ref, dv_in_ref, cos_ref, sin_ref, dk_out, dv_out):
    total = dk_ref[...] + dk_in_ref[...].astype(F32)
    turned = total * cos_ref[...] - swap_halves(total) * sin_ref[...]
    dk_out[...] = turned.astype(BF)
    dv_out[...] = (dv_ref[...] + dv_in_ref[...].astype(F32)).astype(BF)


def finish_keys(dk, dv, dkv_in, cos, sin):
    rows, width = dk.shape
    pairs = width // LANES
    table = pl.BlockSpec((rows, LANES), lambda i: (0, 0))
    return pl.pallas_call(
        finish_keys_kernel,
        name="finish_keys",
        grid=(pairs,),
        out_shape=(jax.ShapeDtypeStruct((rows, width), BF),) * 2,
        in_specs=[pair_spec(rows), pair_spec(rows), stacked_spec(rows, 0), stacked_spec(rows, 1)]
        + [table, table],
        out_specs=(pair_spec(rows),) * 2,
        cost_estimate=LIGHT,
    )(dk, dv, dkv_in, dkv_in, cos, sin)


def branch_kernel(stream_ref, att_ref, gain_ref, *refs):
    pieces, (hidden_ref, normed_ref, scale_ref) = refs[:4], refs[4:]
    for j, piece in enumerate(pieces):
        columns = piece_columns(j, piece.shape[1])
        term = dotf(att_ref[...], piece[...], NN)
        hidden_ref[:, columns] = stream_ref[:, columns].astype(F32) + term
    hidden = hidden_ref[...]
    mean = jnp.sum(hidden * hidden, axis=1, keepdims=True) / hidden.shape[1]
    scale = lax.rsqrt(mean + norm_eps)
    scale_ref[...] = scale
    normed_ref[...] = (hidden * scale * gain_ref[...]).astype(BF)


def add_branch(stream, att, gain, pieces):
    rows, depth = stream.shape
    heads = att.shape[1]
    tile = pl.BlockSpec((QROWS, depth), lambda i: (i, 0))
    return pl.pallas_call(
        branch_kernel,
        name="branch",
        grid=(rows // QROWS,),
        out_shape=(
            jax.ShapeDtypeStruct((rows, depth), F32),
            jax.ShapeDtypeStruct((rows, depth), BF),
            jax.ShapeDtypeStruct((rows, 1), F32),
        ),
        in_specs=[
            tile,
            pl.BlockSpec((QROWS, heads), lambda i: (i, 0)),
            pl.BlockSpec((1, depth), lambda i: (0, 0)),
        ]
        + [pl.BlockSpec(pieces[0].shape, lambda i: (0, 0))] * 4,
        out_specs=(tile, tile, pl.BlockSpec((QROWS, 1), lambda i: (i, 0))),
        compiler_params=pltpu.CompilerParams(vmem_limit_bytes=VMEM_BYTES),
        cost_estimate=LIGHT,
    )(stream, att, gain, *pieces)


def hidden_kernel(x_ref, *refs):
    w_in, (act_ref, by_gate_ref, by_up_ref) = refs[:4], refs[4:]
    rows = x_ref.shape[0]
    for r in range(0, rows, rows):
        part = slice(r, r + rows)
        gate = piece_dot(x_ref, part, [piece[0] for piece in w_in])
        up = piece_dot(x_ref, part, [piece[1] for piece in w_in])
        sig = jax.nn.sigmoid(gate)
        silu = gate * sig
        act_ref[part, :] = (silu * up).astype(BF)
        by_gate_ref[part, :] = (up * sig * (1.0 + gate * (1.0 - sig))).astype(BF)
        by_up_ref[part, :] = silu.astype(BF)


def hidden_units(x, w_in):
    rows, depth = x.shape
    _, size, units = w_in[0].shape
    tile = 256
    part = pl.BlockSpec((rows, tile), lambda i: (0, i))
    return pl.pallas_call(
        hidden_kernel,
        grid=(units // tile,),
        out_shape=(jax.ShapeDtypeStruct((rows, units), BF),) * 3,
        in_specs=[pl.BlockSpec((rows, depth), lambda i: (0, 0))]
        + [pl.BlockSpec((2, size, tile), lambda i: (0, 0, i))] * 4,
        out_specs=(part,) * 3,
        compiler_params=pltpu.CompilerParams(vmem_limit_bytes=VMEM_BYTES),
        cost_estimate=LIGHT,
        name="hidden",
    )(x, *w_in)


def hidden_back_kernel(cot_ref, by_gate_ref, by_up_ref, *refs):
    w_down, (dg_ref, du_ref) = refs[:4], refs[4:]
    rows = cot_ref.shape[0]
    for r in range(0, rows, rows):
        part = slice(r, r + rows)
        d_act = piece_dot(cot_ref, part, [piece[...] for piece in w_down], NT)
        dg_ref[part, :] = (d_act * by_gate_ref[part, :].astype(F32)).astype(BF)
        du_ref[part, :] = (d_act * by_up_ref[part, :].astype(F32)).astype(BF)


def hidden_back(cot, by_gate, by_up, w_down):
    rows, depth = cot.shape
    units, size = w_down[0].shape
    tile = 256
    part = pl.BlockSpec((rows, tile), lambda i: (0, i))
    return pl.pallas_call(
        hidden_back_kernel,
        grid=(units // tile,),
        out_shape=(jax.ShapeDtypeStruct((rows, units), BF),) * 2,
        in_specs=[pl.BlockSpec((rows, depth), lambda i: (0, 0)), part, part]
        + [pl.BlockSpec((tile, size), lambda i: (i, 0))] * 4,
        out_specs=(part,) * 2,
        compiler_params=pltpu.CompilerParams(vmem_limit_bytes=VMEM_BYTES),
        cost_estimate=LIGHT,
        name="hidden_back",
    )(cot, by_gate, by_up, *w_down)


def phased(i, block, make_index, tiles):
    def index_map(j, t):
        return make_index(jnp.where(j < i, 0, jnp.where(j == i, t, tiles - 1)))

    return pl.BlockSpec(block, index_map)


def columns_call(kernel_dot, lefts, pieces, block, make_index, size, flops, name):
    rows = lefts[0].shape[0]
    tile = min(size, 256)
    tiles = size // tile
    depth = size * 4

    def kernel(*refs):
        left_refs, piece_refs, out_ref = refs[: len(lefts)], refs[len(lefts) : -1], refs[-1]
        for j, piece in enumerate(piece_refs):

            @pl.when(pl.program_id(0) == j)
            def _():
                out_ref[...] = kernel_dot([left[...] for left in left_refs], piece).astype(BF)

    def out_index(j, t):
        return (0, (lax.axis_index("fsdp") ^ j) * tiles + t)

    return pl.pallas_call(
        kernel,
        grid=(4, tiles),
        out_shape=jax.ShapeDtypeStruct((rows, depth), BF),
        in_specs=[pl.BlockSpec(left.shape, lambda j, t: (0, 0)) for left in lefts]
        + [phased(i, block(tile), make_index, tiles) for i in range(4)],
        out_specs=pl.BlockSpec((rows, tile), out_index),
        compiler_params=pltpu.CompilerParams(vmem_limit_bytes=VMEM_BYTES),
        cost_estimate=LIGHT,
        name=name,
    )(*lefts, *pieces)


def stacked_columns(lefts, pieces, name):
    count, size, inner = pieces[0].shape

    def product(parts, piece):
        return sum(dotf(parts[c], piece[c], NT) for c in range(count))

    return columns_call(
        product,
        lefts,
        pieces,
        lambda tile: (count, tile, inner),
        lambda t: (0, t, 0),
        size,
        8 * lefts[0].shape[0] * size * inner * count,
        name,
    )


def plain_columns(left, pieces, name):
    inner, size = pieces[0].shape
    return columns_call(
        lambda parts, piece: dotf(parts[0], piece[...], NN),
        [left],
        pieces,
        lambda tile: (inner, tile),
        lambda t: (0, t),
        size,
        8 * left.shape[0] * size * inner,
        name,
    )


def branch_back_kernel(shares, d_mid_ref, hidden_ref, cot_ref, scale_ref, gain_ref, *refs):
    pieces, (d_hidden_ref, d_att_ref, gain_out_ref) = refs[:4], refs[4:7]
    d_mid = d_mid_ref[...].astype(F32)
    hidden = hidden_ref[...]
    scale = scale_ref[...]
    weighted = d_mid * gain_ref[...]
    inner = jnp.sum(weighted * hidden, axis=1, keepdims=True) / hidden.shape[1]
    d_hidden = (
        cot_ref[...].astype(F32) * (1.0 / shares)
        + scale * weighted
        - hidden * (scale * scale * scale * inner)
    )
    gain_term = jnp.sum(d_mid * hidden * scale, axis=0, keepdims=True)

    @pl.when(pl.program_id(0) == 0)
    def _():
        gain_out_ref[...] = gain_term

    @pl.when(pl.program_id(0) != 0)
    def _():
        gain_out_ref[...] += gain_term

    d_hidden_ref[...] = d_hidden.astype(BF)
    heads = d_att_ref.shape[1]
    for e in range(0, heads, 512):
        columns = slice(e, e + 512)
        d_att_ref[:, columns] = piece_dot(
            d_hidden_ref, slice(None), [piece[columns, :] for piece in pieces], NT
        ).astype(BF)


def branch_back(d_mid, hidden, cot, scale, gain, pieces):
    rows, depth = hidden.shape
    heads, size = pieces[0].shape
    tile = pl.BlockSpec((QROWS, depth), lambda i: (i, 0))
    row = pl.BlockSpec((1, depth), lambda i: (0, 0))
    return pl.pallas_call(
        functools.partial(branch_back_kernel, lax.axis_size("tensor")),
        name="branch_back",
        grid=(rows // QROWS,),
        in_specs=[tile, tile, tile, pl.BlockSpec((QROWS, 1), lambda i: (i, 0)), row]
        + [pl.BlockSpec((heads, size), lambda i: (0, 0))] * 4,
        out_specs=(tile, pl.BlockSpec((QROWS, heads), lambda i: (i, 0)), row),
        out_shape=(
            jax.ShapeDtypeStruct((rows, depth), BF),
            jax.ShapeDtypeStruct((rows, heads), BF),
            jax.ShapeDtypeStruct((1, depth), F32),
        ),
        compiler_params=pltpu.CompilerParams(vmem_limit_bytes=VMEM_BYTES),
        cost_estimate=LIGHT,
    )(d_mid, hidden, cot, scale, gain, *pieces)


def grad_call(left, right, cut, place, adds, name, span=(0, 1)):
    rows = left.shape[0]
    size = (left, right)[cut].shape[1] // 4
    swept = (right, left)[cut].shape[1] // span[1]
    height, width = (size, swept) if cut == 0 else (swept, size)
    tile = min(1024, swept)
    offset = span[0] * (swept // tile)
    block = (height, tile) if cut == 0 else (tile, width)

    def owner():
        return lax.axis_index("fsdp") ^ place

    def swept_index(t):
        return (0, t) if cut == 0 else (t, 0)

    def kernel(left_ref, right_ref, *refs):
        add_refs, out_ref = refs[: len(adds)], refs[len(adds)]
        if cut == 0:
            turned = refs[-1]

            @pl.when(pl.program_id(0) == 0)
            def _():
                turned[...] = left_ref[...].T

            result = dotf(turned[...], right_ref[...], NN)
        else:
            result = dotf(left_ref[...].T, right_ref[...], NN)
        for add in add_refs:
            result = result + add[...].astype(F32)
        out_ref[...] = result.astype(BF)

    fixed = pl.BlockSpec((rows, size), lambda t: (0, owner()))
    moving = pl.BlockSpec((rows, tile), lambda t: (0, t + offset))
    return pl.pallas_call(
        kernel,
        grid=(swept // tile,),
        out_shape=jax.ShapeDtypeStruct((height, width), BF),
        in_specs=[fixed, moving] * (cut == 0)
        + [moving, fixed] * (cut == 1)
        + [pl.BlockSpec(block, swept_index)] * len(adds),
        out_specs=pl.BlockSpec(block, swept_index),
        scratch_shapes=[pltpu.VMEM((size, rows), BF)] if cut == 0 else [],
        compiler_params=pltpu.CompilerParams(vmem_limit_bytes=VMEM_BYTES),
        cost_estimate=LIGHT,
        name=name,
    )(left, right, *adds)


class Reduction:
    def __init__(self, left, right, cut, name, span=(0, 1)):
        self.args, self.name, self.span = (left, right, cut), name, span

    def call(self, place, deps, step, adds=()):
        left, right, cut = self.args
        left = after(left, *deps) if deps else left
        return grad_call(left, right, cut, place, adds, self.name + step, self.span)

    def near_far(self, *deps):
        self.three = self.call(3, deps, "_3")
        self.for_two = swap(self.three, "fsdp", 1)

    def near(self, *deps):
        self.one = self.call(1, deps, "_1")
        self.for_own = swap(self.one, "fsdp", 1)

    def far(self, *deps):
        self.two = self.call(2, deps, "_2", [self.for_two])

    def send_far(self, *deps):
        self.across = swap(after(self.two, *deps), "fsdp", 2)

    def mine(self, *deps):
        self.own = self.call(0, deps, "_0", [self.for_own, self.across])

    def send_context(self, *deps):
        self.other = swap(after(self.own, *deps), "context", 1)


def totals_kernel(slots, *refs):
    pairs, out_ref = refs[:-1], refs[-1]
    for slot in range(len(pairs) // 2):
        total = pairs[2 * slot][...].astype(F32) + pairs[2 * slot + 1][...].astype(F32)
        if slots == 0:
            out_ref[slot] = total
        else:
            out_ref[:, slot, :] = total


def totals(sums, slots, *deps):
    arrays = [array for part in sums for array in (part.own, part.other)]
    if deps:
        arrays[0] = after(arrays[0], *deps)
    rows, width = arrays[0].shape
    tile = 128
    shape = [rows, width]
    shape.insert(slots, len(sums))
    block = [tile, width]
    block.insert(slots, len(sums))
    return pl.pallas_call(
        functools.partial(totals_kernel, slots),
        grid=(rows // tile,),
        out_shape=jax.ShapeDtypeStruct(tuple(shape), F32),
        in_specs=[pl.BlockSpec((tile, width), lambda i: (i, 0))] * len(arrays),
        out_specs=pl.BlockSpec(
            tuple(block), (lambda i: (0, i, 0)) if slots == 0 else (lambda i: (i, 0, 0))
        ),
        compiler_params=pltpu.CompilerParams(vmem_limit_bytes=VMEM_BYTES),
        cost_estimate=LIGHT,
        name="totals",
    )(*arrays)


def row_sum(values_in):
    return jnp.sum(values_in, axis=1, keepdims=True)


def per_device(tokens, w_qkv, w_out, w_gate_up, w_down, gains, seq_lengths, cotangent):
    row_count, part_width = tokens.shape
    tensor_index = lax.axis_index("tensor")
    context_index = lax.axis_index("context")
    full_width = part_width * lax.axis_size("tensor")

    def features(part_in):
        return lax.all_gather(part_in, "tensor", axis=1, tiled=True)

    def feature_sum(term):
        return lax.psum_scatter(term.astype(BF), "tensor", scatter_dimension=1, tiled=True)

    def own_features(full):
        return lax.dynamic_slice_in_dim(full, tensor_index * part_width, part_width, 1)

    ending = jnp.cumsum(seq_lengths[0])
    starts = ending - seq_lengths[0]
    places = context_index * row_count + jnp.arange(row_count, dtype=jnp.int32)
    first_token = jnp.max(jnp.where(starts[None, :] <= places[:, None], starts[None, :], 0), axis=1)
    cos, sin = rope_tables(places - first_token)
    low = first_token - context_index * row_count
    low_row = low[None, :]
    need = low[::QROWS]

    token_low = features(tokens)
    gain_near, gain_full = gather_gains(gains)
    gain_attn, gain_mlp = gain_full[0:1], gain_full[1:2]

    qkv_own = jnp.swapaxes(w_qkv, 0, 1)
    half = qkv_own.shape[1] // 2
    far_half = swap(
        lax.dynamic_slice_in_dim(after(qkv_own, gain_near), context_index * half, half, 1),
        "fsdp",
        2,
    )
    other_half = swap(far_half, "context", 1)
    qkv_far = jnp.where(
        context_index == 0,
        jnp.concatenate([far_half, other_half], axis=1),
        jnp.concatenate([other_half, far_half], axis=1),
    )
    qkv_near = swap(qkv_own, "fsdp", 1)
    qkv = (qkv_own, qkv_near, qkv_far, swap(qkv_far, "fsdp", 1))

    gate_up_own = jnp.swapaxes(w_gate_up, 0, 1)
    cut = gate_up_own.shape[1] * 12 // 32
    gate_up_a = swap(after(gate_up_own[:, :cut], far_half), "fsdp", 2)
    gate_up_b = swap(after(gate_up_own[:, cut:], gate_up_a), "fsdp", 2)

    keys_values, normed_in, scale_attn = project(
        after(token_low, gate_up_a), qkv, cos, sin, gain_attn, (1.0, None), 1, True
    )
    peer_kv = lax.ppermute(keys_values, "context", [(0, 1)])
    queries = project(normed_in, qkv, cos, sin, gain_attn, (HDIM**-0.5,), 0, False)[0][0]
    part, part_log = own_forward(queries, keys_values, low_row)
    attended, logs = peer_forward(
        need, queries, peer_kv, low_row, after(part, gate_up_b), part_log
    )
    attended_full = features(attended)

    out_own = after(lax.all_gather(w_out, "tensor", axis=0, tiled=True), attended)
    out_near = swap(out_own, "fsdp", 1)
    out_far = swap(out_own, "fsdp", 2)
    out_far_near = swap(out_far, "fsdp", 1)
    out = (out_own, out_near, out_far, out_far_near)
    gate_up_own, gate_up_a, gate_up_b = lax.optimization_barrier(
        (gate_up_own, gate_up_a, gate_up_b, attended)
    )[:3]
    gate_up_far = jnp.concatenate([gate_up_a, gate_up_b], axis=1)
    gate_up_near = swap(gate_up_own, "fsdp", 1)
    gate_up = (gate_up_own, gate_up_near, gate_up_far, swap(gate_up_far, "fsdp", 1))
    cot_full = features(after(cotangent, attended_full, out_far_near, out_near))
    down_far = swap(after(w_down, attended_full, out_far_near), "fsdp", 2)
    down_near = swap(after(w_down, attended_full), "fsdp", 1)
    hidden, normed_mid, scale_mlp = add_branch(token_low, attended_full, gain_mlp, out)

    activated, by_gate, by_up = hidden_units(normed_mid, gate_up)
    down_far = after(down_far, activated)
    down = (w_down, down_near, down_far, swap(down_far, "fsdp", 1))
    mlp_term = plain_columns(activated, down, "mlp_out")
    mlp_out = feature_sum(mlp_term)
    d_gate, d_up = hidden_back(after(cot_full, mlp_term), by_gate, by_up, down)
    d_mid_term = stacked_columns([d_gate, d_up], gate_up, "d_mid")
    d_hidden_term, d_att_term, gain_mlp_term = branch_back(
        d_mid_term, hidden, cot_full, scale_mlp, gain_mlp, out
    )
    d_attended = feature_sum(after(d_att_term, mlp_out))
    d_hidden_own = feature_sum(after(d_hidden_term, d_att_term))

    down_a, down_b = (
        Reduction(activated, cot_full, 1, "grad_down", (part_index, 2)) for part_index in (0, 1)
    )
    grad_gate = Reduction(normed_mid, d_gate, 0, "grad_gate")
    grad_up = Reduction(normed_mid, d_up, 0, "grad_up")
    square = lax.axis_size("tensor") == lax.axis_size("fsdp")
    down_a.near_far(d_att_term)
    down_b.near_far(down_a.three)
    grad_gate.near_far(down_b.three)
    down_a.far(grad_gate.three)
    down_a.send_far()
    down_b.far(down_a.two)
    down_b.send_far()
    down_a.near(down_b.two)
    down_b.near(down_a.one)
    grad_gate.far(down_b.one)
    grad_gate.send_far()
    grad_gate.near(grad_gate.two)
    down_a.mine(grad_gate.one)
    down_a.send_context()
    grad_up.near_far(down_a.own)
    grad_up.near(grad_up.three)

    dq_peer, dkv_peer = peer_backward(
        need, queries, peer_kv, after(d_attended, grad_up.one), attended, low_row, logs
    )
    dkv_in = lax.ppermute(dkv_peer, "context", [(1, 0)])
    d_query, dk_own, dv_own = own_backward(
        queries, keys_values, d_attended, attended, low_row, logs, dq_peer, cos, sin
    )
    grad_query = Reduction(normed_in, d_query, 0, "grad_query")
    down_b.mine(d_query)
    down_b.send_context()
    grad_up.far(down_b.own)
    grad_up.send_far()
    d_key, d_value = finish_keys(
        dk_own, dv_own, after(dkv_in, grad_up.two, d_hidden_own), cos, sin
    )
    grad_gate.mine(d_value)
    grad_gate.send_context()
    d_in_term = stacked_columns(
        [d_query, d_key, after(d_value, grad_gate.own, down_a.other, down_b.other)], qkv, "d_in"
    )
    d_in = feature_sum(d_in_term).astype(F32)

    if square:
        grad_out = Reduction(attended_full, d_hidden_own, 0, "grad_out")
    else:
        grad_out = Reduction(attended, features(d_hidden_own), 1, "grad_out")
    grad_query.near_far(d_in_term)
    grad_query.near(grad_query.three)
    grad_up.mine(grad_query.one)
    grad_up.send_context()
    grad_key = Reduction(normed_in, d_key, 0, "grad_key")
    grad_value = Reduction(normed_in, d_value, 0, "grad_value")
    grad_query.far(grad_up.own)
    grad_query.send_far()
    grad_key.near_far(grad_query.two, grad_gate.other)
    grad_value.near_far(grad_key.three)
    grad_key.near(grad_value.three)
    grad_value.near(grad_key.one)
    grad_key.far(grad_value.one)
    grad_key.send_far()
    grad_value.far(grad_key.two)
    grad_value.send_far()
    grad_out.near_far(grad_value.two)
    grad_out.near(grad_out.three)
    grad_out.far(grad_out.one)
    grad_out.send_far()
    grad_query.mine(grad_out.two)
    grad_query.send_context()

    stream = token_low.astype(F32)
    d_in_wide = after(d_in_term, grad_query.own).astype(F32)
    weighted = d_in_wide * stream
    inner_term = jnp.sum(weighted * gain_attn, axis=1)
    gain_attn_term = jnp.sum(weighted * scale_attn, axis=0)
    parts = lax.axis_size("tensor")
    totals_small = block_totals(
        jnp.concatenate(
            [
                jnp.broadcast_to(inner_term[None, :], (parts, row_count)),
                gain_attn_term.reshape(parts, part_width),
                gain_mlp_term.reshape(parts, part_width),
            ],
            axis=1,
        )[None]
    )
    inner_in = totals_small[0, :row_count][:, None] / full_width
    gain_sums = totals_small[0, row_count:].reshape(2, part_width)
    gain_sums = exchange(gain_sums, "fsdp", 1)
    gain_sums = exchange(gain_sums, "fsdp", 2)
    gain_sums = exchange(gain_sums, "context", 1)
    gain_width = gains.shape[1]
    grad_gains = lax.dynamic_slice_in_dim(
        gain_sums, lax.axis_index("fsdp") * gain_width, gain_width, 1
    )

    grad_down_sum = totals([down_a, down_b], 0, d_in_wide).reshape(w_down.shape)
    grad_key.mine(grad_down_sum, grad_up.other)
    grad_key.send_context()
    grad_value.mine(grad_key.own)
    grad_value.send_context()
    grad_out.mine(grad_value.own)
    if square:
        count = lax.axis_size("fsdp")
        across = [(i, (i % count) * count + i // count) for i in range(count * count)]
        grad_out.own = lax.ppermute(grad_out.own, ("fsdp", "tensor"), across)
    grad_out.send_context()
    grad_gate_up_sum = totals([grad_gate, grad_up], 1, grad_value.own)
    grad_qkv = totals([grad_query, grad_key, grad_value], 0, grad_gate_up_sum)
    grad_out_sum = totals([grad_out], 0, grad_qkv)[0]

    block_out = (own_features(hidden) + mlp_out.astype(F32)).astype(BF)
    own_tokens = tokens.astype(F32)
    grad_tokens = (
        d_hidden_own.astype(F32)
        + scale_attn * own_features(gain_attn) * d_in
        - own_tokens * scale_attn * scale_attn * scale_attn * inner_in
    ).astype(BF)
    return (
        block_out,
        grad_tokens,
        jnp.swapaxes(grad_qkv, 0, 1),
        grad_out_sum,
        grad_gate_up_sum,
        grad_down_sum,
        grad_gains,
    )


def solution(mesh):
    rows = P(("fsdp", "context"), "tensor")
    inner = P("fsdp", None, "tensor")
    outer = P("tensor", "fsdp")
    gain = P(None, ("tensor", "fsdp"))
    return jax.shard_map(
        per_device,
        mesh=mesh,
        in_specs=(rows, inner, outer, inner, outer, gain, P("fsdp", None), rows),
        out_specs=(rows, rows, inner, outer, inner, outer, gain),
        check_vma=False,
    )
```

```python
import functools

import jax
import jax.numpy as jnp
from jax import lax
from jax.experimental import pallas as pl
from jax.experimental.pallas import tpu as pltpu
from jax.sharding import PartitionSpec as P

HDIM = 64
LANES = 128
QROWS = 256
norm_eps = 1e-05
rope_base = 130000.0
masked_score = -1e30
BF = jnp.bfloat16
F32 = jnp.float32
VMEM_BYTES = 56 * 1024 * 1024
LIGHT = pl.CostEstimate(flops=1, bytes_accessed=1, transcendentals=0)


def dotf(a, b, dims):
    return lax.dot_general(a, b, (dims, ((), ())), preferred_element_type=F32)


NN = ((1,), (0,))
NT = ((1,), (1,))
TN = ((0,), (0,))


def swap(value, axis, bit):
    count = lax.axis_size(axis)
    return lax.ppermute(value, axis, [(i, i ^ bit) for i in range(count)])


def after(value, *others):
    return lax.optimization_barrier((value, *others))[0]


def shifted(value, axis):
    count = lax.axis_size(axis)
    return [
        lax.ppermute(value, axis, [(i, (i + step) % count) for i in range(count)])
        for step in range(1, count)
    ]


def exchange(value, axis, bit):
    return value + swap(value, axis, bit)


def join_kernel(axis, mode, *refs):
    pieces, out_ref = refs[:-1], refs[-1]
    count = len(pieces)
    me = lax.axis_index(axis)
    for step, piece in enumerate(pieces):
        size = piece.shape[1]
        place = (me ^ step) if mode == "xor" else (me - step + count) % count
        out_ref[:, pl.ds(pl.multiple_of(place * size, size), size)] = piece[...]


def join(pieces, axis, mode):
    rows, size = pieces[0].shape
    return pl.pallas_call(
        functools.partial(join_kernel, axis, mode),
        out_shape=jax.ShapeDtypeStruct((rows, size * len(pieces)), pieces[0].dtype),
        cost_estimate=LIGHT,
        name="join",
    )(*pieces)


def gather_gains(gains):
    if lax.axis_size("tensor") > 4 or gains.shape[1] % LANES:
        whole = lax.all_gather(gains, ("tensor", "fsdp"), axis=1, tiled=True).astype(F32)
        return gains, whole
    own = gains.astype(F32)
    part = join([own] + [swap(own, "fsdp", bit) for bit in (1, 2, 3)], "fsdp", "xor")
    return part, join([part] + shifted(part, "tensor"), "tensor", "shift")


def block_totals(blocks):
    count = lax.axis_size("tensor")
    me = lax.axis_index("tensor")
    if count > 4:
        return lax.dynamic_index_in_dim(lax.psum(blocks, "tensor"), me, 1, keepdims=False)

    def pick(place):
        return lax.dynamic_index_in_dim(blocks, place, 1, keepdims=False)

    total = pick(me)
    for step in range(1, count):
        moves = [(i, (i + step) % count) for i in range(count)]
        total = total + lax.ppermute(pick((me + step) % count), "tensor", moves)
    return total


def piece_columns(j, size):
    return pl.ds(pl.multiple_of((lax.axis_index("fsdp") ^ j) * size, size), size)


def swap_halves(block):
    lane = lax.broadcasted_iota(jnp.int32, block.shape, 1)
    up = pltpu.roll(block, LANES - HDIM // 2, 1)
    down = pltpu.roll(block, HDIM // 2, 1)
    return jnp.where((lane & (HDIM - 1)) < HDIM // 2, up, down)


def rope_tables(positions):
    lane = jnp.arange(LANES, dtype=jnp.int32)
    half = lane % (HDIM // 2)
    frequencies = rope_base ** (-2.0 * half.astype(F32) / HDIM)
    angles = positions.astype(F32)[:, None] * frequencies[None, :]
    sign = jnp.where((lane % HDIM) < HDIM // 2, -1.0, 1.0)
    return jnp.cos(angles), jnp.sin(angles) * sign[None, :]


def piece_dot(x_ref, rows, pieces, dims=NN):
    total = None
    for j, piece in enumerate(pieces):
        size = piece.shape[dims[1][0]]
        term = dotf(x_ref[rows, piece_columns(j, size)], piece, dims)
        total = term if total is None else total + term
    return total


def project_kernel(kinds, normalize, x_ref, *refs):
    pieces, (cos_ref, sin_ref, gain_ref), outs = refs[:4], refs[4:7], refs[7:]
    out_ref = outs[0]
    rows, width = out_ref.shape[1:]
    step = pl.program_id(0)
    if normalize:
        normed_ref, scale_ref = outs[1], outs[2]

        @pl.when(step == 0)
        def _():
            for r in range(0, rows, QROWS):
                part = slice(r, r + QROWS)
                stream = x_ref[part, :].astype(F32)
                mean = jnp.sum(stream * stream, axis=1, keepdims=True) / x_ref.shape[1]
                scale = lax.rsqrt(mean + norm_eps)
                scale_ref[part, :] = scale
                normed_ref[part, :] = (stream * scale * gain_ref[...]).astype(BF)

        x_ref = normed_ref
    for index, scale in enumerate(kinds):

        @pl.when(step == index)
        def _():
            for r in range(0, rows, rows):
                part = slice(r, r + rows)
                result = piece_dot(x_ref, part, [piece[0] for piece in pieces])
                for c in range(0, width, LANES):
                    block = result[:, c : c + LANES]
                    if scale:
                        block = block * cos_ref[part, :] + swap_halves(block) * sin_ref[part, :]
                    low = block.astype(BF)
                    if scale and scale != 1.0:
                        low = low * jnp.asarray(scale, BF)
                    out_ref[0, part, c : c + LANES] = low


def project(x, pieces, cos, sin, gain, kinds, first, normalize):
    rows, depth = x.shape
    _, size, width = pieces[0].shape
    flops = 2 * len(kinds) * rows * depth * width
    whole = pl.BlockSpec((rows, depth), lambda i: (0, 0))
    table = pl.BlockSpec((rows, LANES), lambda i: (0, 0))
    out_shape = [jax.ShapeDtypeStruct((len(kinds), rows, width), BF)]
    out_specs = [pl.BlockSpec((1, rows, width), lambda i: (i, 0, 0))]
    if normalize:
        out_shape += [jax.ShapeDtypeStruct((rows, depth), BF), jax.ShapeDtypeStruct((rows, 1), F32)]
        out_specs += [whole, pl.BlockSpec((rows, 1), lambda i: (0, 0))]
    return pl.pallas_call(
        functools.partial(project_kernel, kinds, normalize),
        name="project_kv" if normalize else "project_q",
        grid=(len(kinds),),
        out_shape=out_shape,
        in_specs=[whole]
        + [pl.BlockSpec((1, size, width), lambda i: (i + first, 0, 0))] * 4
        + [table, table, pl.BlockSpec((1, depth), lambda i: (0, 0))],
        out_specs=out_specs,
        compiler_params=pltpu.CompilerParams(vmem_limit_bytes=VMEM_BYTES),
        cost_estimate=LIGHT,
    )(x, *pieces, cos, sin, gain)


def head_mask(block, head):
    lane = lax.broadcasted_iota(jnp.int32, block.shape, 1)
    inside = (lane < HDIM) if head == 0 else (lane >= HDIM)
    return jnp.where(inside, block, jnp.zeros_like(block))


def own_mask(key_count, row0, low_row):
    key = lax.broadcasted_iota(jnp.int32, (key_count, QROWS), 0)
    query = row0 + lax.broadcasted_iota(jnp.int32, (key_count, QROWS), 1)
    return (key >= low_row) & (key <= query)


def peer_mask(key_count, low_row, offset):
    key = lax.broadcasted_iota(jnp.int32, (key_count, QROWS), 0) - offset
    return key >= low_row


def key_windows(need, total):
    counts = list(range(QROWS, total + 1, QROWS))
    for place, count in enumerate(counts):
        chosen = need < 0 if place == 0 else need < -counts[place - 1]
        if count < total:
            chosen = jnp.logical_and(chosen, need >= -count)
        yield count, chosen


def own_forward_kernel(q_ref, k_ref, v_ref, low_ref, out_ref, log_ref):
    rows = q_ref.shape[0]
    v_t = v_ref[...].T
    for r in range(0, rows, QROWS):
        count = r + QROWS
        allowed = own_mask(count, r, low_ref[:, r : r + QROWS])
        keys = k_ref[0:count, :]
        outs = []
        for head in range(LANES // HDIM):
            scores = dotf(keys, head_mask(q_ref[r : r + QROWS, :], head), NT)
            scores = jnp.where(allowed, scores, masked_score)
            peak = jnp.max(scores, axis=0, keepdims=True)
            weights = jnp.exp(scores - peak)
            total = jnp.sum(weights, axis=0, keepdims=True)
            part = dotf(v_t[head * HDIM : (head + 1) * HDIM, 0:count], weights.astype(BF), NN)
            outs.append(part / total)
            log_ref[0, head : head + 1, r : r + QROWS] = peak + jnp.log(total)
        out_ref[r : r + QROWS, :] = jnp.concatenate(outs, axis=0).T


def peer_forward_kernel(
    need_ref, q_ref, k_ref, v_ref, low_ref, part_ref, log_in_ref, out_ref, log_ref
):
    rows = q_ref.shape[0]
    key_total = k_ref.shape[0]
    for index, r in enumerate(range(0, rows, QROWS)):
        for key_count, chosen in key_windows(need_ref[index], key_total):

            @pl.when(chosen)
            def _():
                window = slice(key_total - key_count, key_total)
                v_t = v_ref[window, :].T
                allowed = peer_mask(key_count, low_ref[:, r : r + QROWS], key_count)
                before = part_ref[r : r + QROWS, :].T
                outs = []
                for head in range(LANES // HDIM):
                    scores = dotf(k_ref[window, :], head_mask(q_ref[r : r + QROWS, :], head), NT)
                    scores = jnp.where(allowed, scores, masked_score)
                    log_own = log_in_ref[0, head : head + 1, r : r + QROWS]
                    peak = jnp.maximum(jnp.max(scores, axis=0, keepdims=True), log_own)
                    weights = jnp.exp(scores - peak)
                    own_weight = jnp.exp(log_own - peak)
                    total = jnp.sum(weights, axis=0, keepdims=True) + own_weight
                    rows_h = slice(head * HDIM, (head + 1) * HDIM)
                    part = dotf(v_t[rows_h, :], weights.astype(BF), NN)
                    outs.append((part + before[rows_h, :] * own_weight) / total)
                    log_ref[0, head : head + 1, r : r + QROWS] = peak + jnp.log(total)
                out_ref[r : r + QROWS, :] = jnp.concatenate(outs, axis=0).T.astype(BF)

        @pl.when(need_ref[index] >= 0)
        def _():
            out_ref[r : r + QROWS, :] = part_ref[r : r + QROWS, :].astype(BF)
            log_ref[:, :, r : r + QROWS] = log_in_ref[:, :, r : r + QROWS]


def pair_spec(rows):
    return pl.BlockSpec((rows, LANES), lambda i: (0, i))


def stacked_spec(rows, part):
    return pl.BlockSpec((None, rows, LANES), lambda i: (part, 0, i))


def log_spec(rows):
    return pl.BlockSpec((1, LANES // HDIM, rows), lambda i: (i, 0, 0))


def low_spec(rows):
    return pl.BlockSpec((1, rows), lambda i: (0, 0))


def own_forward(q, kv, low_row):
    rows, width = q.shape
    pairs = width // LANES
    return pl.pallas_call(
        own_forward_kernel,
        name="own_fwd",
        grid=(pairs,),
        out_shape=(
            jax.ShapeDtypeStruct((rows, width), F32),
            jax.ShapeDtypeStruct((pairs, LANES // HDIM, rows), F32),
        ),
        in_specs=[
            pair_spec(rows),
            stacked_spec(rows, 0),
            stacked_spec(rows, 1),
            low_spec(rows),
        ],
        out_specs=(pair_spec(rows), log_spec(rows)),
        compiler_params=pltpu.CompilerParams(vmem_limit_bytes=VMEM_BYTES),
        cost_estimate=LIGHT,
    )(q, kv, kv, low_row)


SMEM_SPEC = pl.BlockSpec(memory_space=pltpu.SMEM)


def peer_forward(need, q, kv, low_row, part, log_in):
    rows, width = q.shape
    pairs = width // LANES
    return pl.pallas_call(
        peer_forward_kernel,
        name="peer_fwd",
        grid=(pairs,),
        out_shape=(
            jax.ShapeDtypeStruct((rows, width), BF),
            jax.ShapeDtypeStruct((pairs, LANES // HDIM, rows), F32),
        ),
        in_specs=[
            SMEM_SPEC,
            pair_spec(rows),
            stacked_spec(rows, 0),
            stacked_spec(rows, 1),
            low_spec(rows),
            pair_spec(rows),
            log_spec(rows),
        ],
        out_specs=(pair_spec(rows), log_spec(rows)),
        compiler_params=pltpu.CompilerParams(vmem_limit_bytes=VMEM_BYTES),
        cost_estimate=LIGHT,
    )(need, q, kv, kv, low_row, part, log_in)


def backward_block(q_rows, k_rows, v_rows, k_t, do_rows, do_o_t, logs, allowed):
    d_query, d_key, d_value = [], None, None
    for head in range(LANES // HDIM):
        rows_h = slice(head * HDIM, (head + 1) * HDIM)
        q_head = head_mask(q_rows, head)
        do_head = head_mask(do_rows, head)
        scores = dotf(k_rows, q_head, NT)
        probs = jnp.exp(jnp.where(allowed, scores, masked_score) - logs[head])
        delta = jnp.sum(do_o_t[rows_h, :], axis=0, keepdims=True)
        d_probs = dotf(v_rows, do_head, NT)
        d_scores = (probs * (d_probs - delta)).astype(BF)
        d_v = dotf(probs.astype(BF), do_head, NN)
        d_k = dotf(d_scores, q_head, NN)
        d_value = d_v if d_value is None else d_value + d_v
        d_key = d_k if d_key is None else d_key + d_k
        d_query.append(dotf(k_t[rows_h, :], d_scores, NN))
    return jnp.concatenate(d_query, axis=0), d_key, d_value


def output_product(do_ref, o_ref, window):
    product = do_ref[window].astype(F32) * o_ref[window].astype(F32)
    return product.T


def peer_backward_kernel(
    need_ref, q_ref, k_ref, v_ref, do_ref, o_ref, low_ref, log_ref, dq_ref, dkv_ref, sums
):
    rows = q_ref.shape[0]
    key_total = k_ref.shape[0]
    sums[...] = jnp.zeros_like(sums)
    for index, r in enumerate(range(0, rows, QROWS)):
        rows_q = (slice(r, r + QROWS), slice(None))
        for key_count, chosen in key_windows(need_ref[index], key_total):

            @pl.when(chosen)
            def _():
                window = slice(key_total - key_count, key_total)
                allowed = peer_mask(key_count, low_ref[:, r : r + QROWS], key_count)
                logs = [log_ref[0, h : h + 1, r : r + QROWS] for h in range(LANES // HDIM)]
                d_query, d_key, d_value = backward_block(
                    q_ref[rows_q],
                    k_ref[window, :],
                    v_ref[window, :],
                    k_ref[window, :].T,
                    do_ref[rows_q],
                    output_product(do_ref, o_ref, rows_q),
                    logs,
                    allowed,
                )
                dq_ref[rows_q] = d_query.T
                sums[0, window] += d_key
                sums[1, window] += d_value

        @pl.when(need_ref[index] >= 0)
        def _():
            dq_ref[rows_q] = jnp.zeros((QROWS, LANES), F32)

    dkv_ref[...] = sums[...].astype(BF)


def peer_backward(need, q, kv, do, o, low_row, logs):
    rows, width = q.shape
    pairs = width // LANES
    return pl.pallas_call(
        peer_backward_kernel,
        name="peer_bwd",
        grid=(pairs,),
        out_shape=(
            jax.ShapeDtypeStruct((rows, width), F32),
            jax.ShapeDtypeStruct((2, rows, width), BF),
        ),
        in_specs=[
            SMEM_SPEC,
            pair_spec(rows),
            stacked_spec(rows, 0),
            stacked_spec(rows, 1),
            pair_spec(rows),
            pair_spec(rows),
            low_spec(rows),
            log_spec(rows),
        ],
        out_specs=(pair_spec(rows), pl.BlockSpec((2, rows, LANES), lambda i: (0, 0, i))),
        scratch_shapes=[pltpu.VMEM((2, rows, LANES), F32)],
        compiler_params=pltpu.CompilerParams(vmem_limit_bytes=VMEM_BYTES),
        cost_estimate=LIGHT,
    )(need, q, kv, kv, do, o, low_row, logs)


def own_backward_kernel(
    q_ref,
    k_ref,
    v_ref,
    do_ref,
    o_ref,
    low_ref,
    log_ref,
    dq_in_ref,
    cos_ref,
    sin_ref,
    dq_ref,
    dk_ref,
    dv_ref,
    sums,
):
    rows = q_ref.shape[0]
    sums[...] = jnp.zeros_like(sums)
    k_t = k_ref[...].T
    for r in range(0, rows, QROWS):
        count = r + QROWS
        window = (slice(r, r + QROWS), slice(None))
        allowed = own_mask(count, r, low_ref[:, r : r + QROWS])
        logs = [log_ref[0, h : h + 1, r : r + QROWS] for h in range(LANES // HDIM)]
        d_query, d_key, d_value = backward_block(
            q_ref[window],
            k_ref[0:count, :],
            v_ref[0:count, :],
            k_t[:, 0:count],
            do_ref[window],
            output_product(do_ref, o_ref, window),
            logs,
            allowed,
        )
        rotated = (d_query.T + dq_in_ref[window]) * (HDIM**-0.5)
        turned = rotated * cos_ref[window] - swap_halves(rotated) * sin_ref[window]
        dq_ref[window] = turned.astype(BF)
        sums[0, 0:count] += d_key
        sums[1, 0:count] += d_value
    dk_ref[...] = sums[0]
    dv_ref[...] = sums[1]


def own_backward(q, kv, do, o, low_row, logs, dq_in, cos, sin):
    rows, width = q.shape
    pairs = width // LANES
    table = pl.BlockSpec((rows, LANES), lambda i: (0, 0))
    return pl.pallas_call(
        own_backward_kernel,
        name="own_bwd",
        grid=(pairs,),
        out_shape=(
            jax.ShapeDtypeStruct((rows, width), BF),
            jax.ShapeDtypeStruct((rows, width), F32),
            jax.ShapeDtypeStruct((rows, width), F32),
        ),
        in_specs=[
            pair_spec(rows),
            stacked_spec(rows, 0),
            stacked_spec(rows, 1),
            pair_spec(rows),
            pair_spec(rows),
            low_spec(rows),
            log_spec(rows),
            pair_spec(rows),
            table,
            table,
        ],
        out_specs=(pair_spec(rows),) * 3,
        scratch_shapes=[pltpu.VMEM((2, rows, LANES), F32)],
        compiler_params=pltpu.CompilerParams(vmem_limit_bytes=VMEM_BYTES),
        cost_estimate=LIGHT,
    )(q, kv, kv, do, o, low_row, logs, dq_in, cos, sin)


def finish_keys_kernel(dk_ref, dv_ref, dk_in_ref, dv_in_ref, cos_ref, sin_ref, dk_out, dv_out):
    total = dk_ref[...] + dk_in_ref[...].astype(F32)
    turned = total * cos_ref[...] - swap_halves(total) * sin_ref[...]
    dk_out[...] = turned.astype(BF)
    dv_out[...] = (dv_ref[...] + dv_in_ref[...].astype(F32)).astype(BF)


def finish_keys(dk, dv, dkv_in, cos, sin):
    rows, width = dk.shape
    pairs = width // LANES
    table = pl.BlockSpec((rows, LANES), lambda i: (0, 0))
    return pl.pallas_call(
        finish_keys_kernel,
        name="finish_keys",
        grid=(pairs,),
        out_shape=(jax.ShapeDtypeStruct((rows, width), BF),) * 2,
        in_specs=[pair_spec(rows), pair_spec(rows), stacked_spec(rows, 0), stacked_spec(rows, 1)]
        + [table, table],
        out_specs=(pair_spec(rows),) * 2,
        cost_estimate=LIGHT,
    )(dk, dv, dkv_in, dkv_in, cos, sin)


def branch_kernel(stream_ref, att_ref, gain_ref, *refs):
    pieces, (hidden_ref, normed_ref, scale_ref) = refs[:4], refs[4:]
    for j, piece in enumerate(pieces):
        columns = piece_columns(j, piece.shape[1])
        term = dotf(att_ref[...], piece[...], NN)
        hidden_ref[:, columns] = stream_ref[:, columns].astype(F32) + term
    hidden = hidden_ref[...]
    mean = jnp.sum(hidden * hidden, axis=1, keepdims=True) / hidden.shape[1]
    scale = lax.rsqrt(mean + norm_eps)
    scale_ref[...] = scale
    normed_ref[...] = (hidden * scale * gain_ref[...]).astype(BF)


def add_branch(stream, att, gain, pieces):
    rows, depth = stream.shape
    heads = att.shape[1]
    tile = pl.BlockSpec((QROWS, depth), lambda i: (i, 0))
    return pl.pallas_call(
        branch_kernel,
        name="branch",
        grid=(rows // QROWS,),
        out_shape=(
            jax.ShapeDtypeStruct((rows, depth), F32),
            jax.ShapeDtypeStruct((rows, depth), BF),
            jax.ShapeDtypeStruct((rows, 1), F32),
        ),
        in_specs=[
            tile,
            pl.BlockSpec((QROWS, heads), lambda i: (i, 0)),
            pl.BlockSpec((1, depth), lambda i: (0, 0)),
        ]
        + [pl.BlockSpec(pieces[0].shape, lambda i: (0, 0))] * 4,
        out_specs=(tile, tile, pl.BlockSpec((QROWS, 1), lambda i: (i, 0))),
        compiler_params=pltpu.CompilerParams(vmem_limit_bytes=VMEM_BYTES),
        cost_estimate=LIGHT,
    )(stream, att, gain, *pieces)


def hidden_kernel(x_ref, *refs):
    w_in, (act_ref, by_gate_ref, by_up_ref) = refs[:4], refs[4:]
    rows = x_ref.shape[0]
    for r in range(0, rows, rows):
        part = slice(r, r + rows)
        gate = piece_dot(x_ref, part, [piece[0] for piece in w_in])
        up = piece_dot(x_ref, part, [piece[1] for piece in w_in])
        sig = jax.nn.sigmoid(gate)
        silu = gate * sig
        act_ref[part, :] = (silu * up).astype(BF)
        by_gate_ref[part, :] = (up * sig * (1.0 + gate * (1.0 - sig))).astype(BF)
        by_up_ref[part, :] = silu.astype(BF)


def hidden_units(x, w_in):
    rows, depth = x.shape
    _, size, units = w_in[0].shape
    tile = 256
    part = pl.BlockSpec((rows, tile), lambda i: (0, i))
    return pl.pallas_call(
        hidden_kernel,
        grid=(units // tile,),
        out_shape=(jax.ShapeDtypeStruct((rows, units), BF),) * 3,
        in_specs=[pl.BlockSpec((rows, depth), lambda i: (0, 0))]
        + [pl.BlockSpec((2, size, tile), lambda i: (0, 0, i))] * 4,
        out_specs=(part,) * 3,
        compiler_params=pltpu.CompilerParams(vmem_limit_bytes=VMEM_BYTES),
        cost_estimate=LIGHT,
        name="hidden",
    )(x, *w_in)


def hidden_back_kernel(cot_ref, by_gate_ref, by_up_ref, *refs):
    w_down, (dg_ref, du_ref) = refs[:4], refs[4:]
    rows = cot_ref.shape[0]
    for r in range(0, rows, rows):
        part = slice(r, r + rows)
        d_act = piece_dot(cot_ref, part, [piece[...] for piece in w_down], NT)
        dg_ref[part, :] = (d_act * by_gate_ref[part, :].astype(F32)).astype(BF)
        du_ref[part, :] = (d_act * by_up_ref[part, :].astype(F32)).astype(BF)


def hidden_back(cot, by_gate, by_up, w_down):
    rows, depth = cot.shape
    units, size = w_down[0].shape
    tile = 256
    part = pl.BlockSpec((rows, tile), lambda i: (0, i))
    return pl.pallas_call(
        hidden_back_kernel,
        grid=(units // tile,),
        out_shape=(jax.ShapeDtypeStruct((rows, units), BF),) * 2,
        in_specs=[pl.BlockSpec((rows, depth), lambda i: (0, 0)), part, part]
        + [pl.BlockSpec((tile, size), lambda i: (i, 0))] * 4,
        out_specs=(part,) * 2,
        compiler_params=pltpu.CompilerParams(vmem_limit_bytes=VMEM_BYTES),
        cost_estimate=LIGHT,
        name="hidden_back",
    )(cot, by_gate, by_up, *w_down)


def phased(i, block, make_index, tiles):
    def index_map(j, t):
        return make_index(jnp.where(j < i, 0, jnp.where(j == i, t, tiles - 1)))

    return pl.BlockSpec(block, index_map)


def columns_call(kernel_dot, lefts, pieces, block, make_index, size, flops, name):
    rows = lefts[0].shape[0]
    tile = min(size, 256)
    tiles = size // tile
    depth = size * 4

    def kernel(*refs):
        left_refs, piece_refs, out_ref = refs[: len(lefts)], refs[len(lefts) : -1], refs[-1]
        for j, piece in enumerate(piece_refs):

            @pl.when(pl.program_id(0) == j)
            def _():
                out_ref[...] = kernel_dot([left[...] for left in left_refs], piece).astype(BF)

    def out_index(j, t):
        return (0, (lax.axis_index("fsdp") ^ j) * tiles + t)

    return pl.pallas_call(
        kernel,
        grid=(4, tiles),
        out_shape=jax.ShapeDtypeStruct((rows, depth), BF),
        in_specs=[pl.BlockSpec(left.shape, lambda j, t: (0, 0)) for left in lefts]
        + [phased(i, block(tile), make_index, tiles) for i in range(4)],
        out_specs=pl.BlockSpec((rows, tile), out_index),
        compiler_params=pltpu.CompilerParams(vmem_limit_bytes=VMEM_BYTES),
        cost_estimate=LIGHT,
        name=name,
    )(*lefts, *pieces)


def stacked_columns(lefts, pieces, name):
    count, size, inner = pieces[0].shape

    def product(parts, piece):
        return sum(dotf(parts[c], piece[c], NT) for c in range(count))

    return columns_call(
        product,
        lefts,
        pieces,
        lambda tile: (count, tile, inner),
        lambda t: (0, t, 0),
        size,
        8 * lefts[0].shape[0] * size * inner * count,
        name,
    )


def plain_columns(left, pieces, name):
    inner, size = pieces[0].shape
    return columns_call(
        lambda parts, piece: dotf(parts[0], piece[...], NN),
        [left],
        pieces,
        lambda tile: (inner, tile),
        lambda t: (0, t),
        size,
        8 * left.shape[0] * size * inner,
        name,
    )


def branch_back_kernel(shares, d_mid_ref, hidden_ref, cot_ref, scale_ref, gain_ref, *refs):
    pieces, (d_hidden_ref, d_att_ref, gain_out_ref) = refs[:4], refs[4:7]
    d_mid = d_mid_ref[...].astype(F32)
    hidden = hidden_ref[...]
    scale = scale_ref[...]
    weighted = d_mid * gain_ref[...]
    inner = jnp.sum(weighted * hidden, axis=1, keepdims=True) / hidden.shape[1]
    d_hidden = (
        cot_ref[...].astype(F32) * (1.0 / shares)
        + scale * weighted
        - hidden * (scale * scale * scale * inner)
    )
    gain_term = jnp.sum(d_mid * hidden * scale, axis=0, keepdims=True)

    @pl.when(pl.program_id(0) == 0)
    def _():
        gain_out_ref[...] = gain_term

    @pl.when(pl.program_id(0) != 0)
    def _():
        gain_out_ref[...] += gain_term

    d_hidden_ref[...] = d_hidden.astype(BF)
    heads = d_att_ref.shape[1]
    for e in range(0, heads, 512):
        columns = slice(e, e + 512)
        d_att_ref[:, columns] = piece_dot(
            d_hidden_ref, slice(None), [piece[columns, :] for piece in pieces], NT
        ).astype(BF)


def branch_back(d_mid, hidden, cot, scale, gain, pieces):
    rows, depth = hidden.shape
    heads, size = pieces[0].shape
    tile = pl.BlockSpec((QROWS, depth), lambda i: (i, 0))
    row = pl.BlockSpec((1, depth), lambda i: (0, 0))
    return pl.pallas_call(
        functools.partial(branch_back_kernel, lax.axis_size("tensor")),
        name="branch_back",
        grid=(rows // QROWS,),
        in_specs=[tile, tile, tile, pl.BlockSpec((QROWS, 1), lambda i: (i, 0)), row]
        + [pl.BlockSpec((heads, size), lambda i: (0, 0))] * 4,
        out_specs=(tile, pl.BlockSpec((QROWS, heads), lambda i: (i, 0)), row),
        out_shape=(
            jax.ShapeDtypeStruct((rows, depth), BF),
            jax.ShapeDtypeStruct((rows, heads), BF),
            jax.ShapeDtypeStruct((1, depth), F32),
        ),
        compiler_params=pltpu.CompilerParams(vmem_limit_bytes=VMEM_BYTES),
        cost_estimate=LIGHT,
    )(d_mid, hidden, cot, scale, gain, *pieces)


def grad_call(left, right, cut, place, adds, name, span=(0, 1)):
    rows = left.shape[0]
    size = (left, right)[cut].shape[1] // 4
    swept = (right, left)[cut].shape[1] // span[1]
    height, width = (size, swept) if cut == 0 else (swept, size)
    tile = min(1024, swept)
    offset = span[0] * (swept // tile)
    block = (height, tile) if cut == 0 else (tile, width)

    def owner():
        return lax.axis_index("fsdp") ^ place

    def swept_index(t):
        return (0, t) if cut == 0 else (t, 0)

    def kernel(left_ref, right_ref, *refs):
        add_refs, out_ref = refs[: len(adds)], refs[len(adds)]
        if cut == 0:
            turned = refs[-1]

            @pl.when(pl.program_id(0) == 0)
            def _():
                turned[...] = left_ref[...].T

            result = dotf(turned[...], right_ref[...], NN)
        else:
            result = dotf(left_ref[...].T, right_ref[...], NN)
        for add in add_refs:
            result = result + add[...].astype(F32)
        out_ref[...] = result.astype(BF)

    fixed = pl.BlockSpec((rows, size), lambda t: (0, owner()))
    moving = pl.BlockSpec((rows, tile), lambda t: (0, t + offset))
    return pl.pallas_call(
        kernel,
        grid=(swept // tile,),
        out_shape=jax.ShapeDtypeStruct((height, width), BF),
        in_specs=[fixed, moving] * (cut == 0)
        + [moving, fixed] * (cut == 1)
        + [pl.BlockSpec(block, swept_index)] * len(adds),
        out_specs=pl.BlockSpec(block, swept_index),
        scratch_shapes=[pltpu.VMEM((size, rows), BF)] if cut == 0 else [],
        compiler_params=pltpu.CompilerParams(vmem_limit_bytes=VMEM_BYTES),
        cost_estimate=LIGHT,
        name=name,
    )(left, right, *adds)


class Reduction:
    def __init__(self, left, right, cut, name, span=(0, 1)):
        self.args, self.name, self.span = (left, right, cut), name, span

    def call(self, place, deps, step, adds=()):
        left, right, cut = self.args
        left = after(left, *deps) if deps else left
        return grad_call(left, right, cut, place, adds, self.name + step, self.span)

    def near_far(self, *deps):
        self.three = self.call(3, deps, "_3")
        self.for_two = swap(self.three, "fsdp", 1)

    def near(self, *deps):
        self.one = self.call(1, deps, "_1")
        self.for_own = swap(self.one, "fsdp", 1)

    def far(self, *deps):
        self.two = self.call(2, deps, "_2", [self.for_two])

    def send_far(self, *deps):
        self.across = swap(after(self.two, *deps), "fsdp", 2)

    def mine(self, *deps):
        self.own = self.call(0, deps, "_0", [self.for_own, self.across])

    def send_context(self, *deps):
        self.other = swap(after(self.own, *deps), "context", 1)


def totals_kernel(slots, *refs):
    pairs, out_ref = refs[:-1], refs[-1]
    for slot in range(len(pairs) // 2):
        total = pairs[2 * slot][...].astype(F32) + pairs[2 * slot + 1][...].astype(F32)
        if slots == 0:
            out_ref[slot] = total
        else:
            out_ref[:, slot, :] = total


def totals(sums, slots, *deps):
    arrays = [array for part in sums for array in (part.own, part.other)]
    if deps:
        arrays[0] = after(arrays[0], *deps)
    rows, width = arrays[0].shape
    tile = 128
    shape = [rows, width]
    shape.insert(slots, len(sums))
    block = [tile, width]
    block.insert(slots, len(sums))
    return pl.pallas_call(
        functools.partial(totals_kernel, slots),
        grid=(rows // tile,),
        out_shape=jax.ShapeDtypeStruct(tuple(shape), F32),
        in_specs=[pl.BlockSpec((tile, width), lambda i: (i, 0))] * len(arrays),
        out_specs=pl.BlockSpec(
            tuple(block), (lambda i: (0, i, 0)) if slots == 0 else (lambda i: (i, 0, 0))
        ),
        compiler_params=pltpu.CompilerParams(vmem_limit_bytes=VMEM_BYTES),
        cost_estimate=LIGHT,
        name="totals",
    )(*arrays)


def row_sum(values_in):
    return jnp.sum(values_in, axis=1, keepdims=True)


def per_device(tokens, w_qkv, w_out, w_gate_up, w_down, gains, seq_lengths, cotangent):
    row_count, part_width = tokens.shape
    tensor_index = lax.axis_index("tensor")
    context_index = lax.axis_index("context")
    full_width = part_width * lax.axis_size("tensor")

    def features(part_in):
        return lax.all_gather(part_in, "tensor", axis=1, tiled=True)

    def feature_sum(term):
        return lax.psum_scatter(term.astype(BF), "tensor", scatter_dimension=1, tiled=True)

    def own_features(full):
        return lax.dynamic_slice_in_dim(full, tensor_index * part_width, part_width, 1)

    ending = jnp.cumsum(seq_lengths[0])
    starts = ending - seq_lengths[0]
    places = context_index * row_count + jnp.arange(row_count, dtype=jnp.int32)
    first_token = jnp.max(jnp.where(starts[None, :] <= places[:, None], starts[None, :], 0), axis=1)
    cos, sin = rope_tables(places - first_token)
    low = first_token - context_index * row_count
    low_row = low[None, :]
    need = low[::QROWS]

    token_low = features(tokens)
    gain_near, gain_full = gather_gains(gains)
    gain_attn, gain_mlp = gain_full[0:1], gain_full[1:2]

    qkv_own = jnp.swapaxes(w_qkv, 0, 1)
    half = qkv_own.shape[1] // 2
    far_half = swap(
        lax.dynamic_slice_in_dim(after(qkv_own, gain_near), context_index * half, half, 1),
        "fsdp",
        2,
    )
    other_half = swap(far_half, "context", 1)
    qkv_far = jnp.where(
        context_index == 0,
        jnp.concatenate([far_half, other_half], axis=1),
        jnp.concatenate([other_half, far_half], axis=1),
    )
    qkv_near = swap(qkv_own, "fsdp", 1)
    qkv = (qkv_own, qkv_near, qkv_far, swap(qkv_far, "fsdp", 1))

    gate_up_own = jnp.swapaxes(w_gate_up, 0, 1)
    cut = gate_up_own.shape[1] * 12 // 32
    gate_up_a = swap(after(gate_up_own[:, :cut], far_half), "fsdp", 2)
    gate_up_b = swap(after(gate_up_own[:, cut:], gate_up_a), "fsdp", 2)

    keys_values, normed_in, scale_attn = project(
        after(token_low, gate_up_a), qkv, cos, sin, gain_attn, (1.0, None), 1, True
    )
    peer_kv = lax.ppermute(keys_values, "context", [(0, 1)])
    queries = project(normed_in, qkv, cos, sin, gain_attn, (HDIM**-0.5,), 0, False)[0][0]
    part, part_log = own_forward(queries, keys_values, low_row)
    attended, logs = peer_forward(
        need, queries, peer_kv, low_row, after(part, gate_up_b), part_log
    )
    attended_full = features(attended)

    out_own = after(lax.all_gather(w_out, "tensor", axis=0, tiled=True), attended)
    out_near = swap(out_own, "fsdp", 1)
    out_far = swap(out_own, "fsdp", 2)
    out_far_near = swap(out_far, "fsdp", 1)
    out = (out_own, out_near, out_far, out_far_near)
    gate_up_own, gate_up_a, gate_up_b = lax.optimization_barrier(
        (gate_up_own, gate_up_a, gate_up_b, attended)
    )[:3]
    gate_up_far = jnp.concatenate([gate_up_a, gate_up_b], axis=1)
    gate_up_near = swap(gate_up_own, "fsdp", 1)
    gate_up = (gate_up_own, gate_up_near, gate_up_far, swap(gate_up_far, "fsdp", 1))
    cot_full = features(after(cotangent, attended_full, out_far_near, out_near))
    down_far = swap(after(w_down, attended_full, out_far_near), "fsdp", 2)
    down_near = swap(after(w_down, attended_full), "fsdp", 1)
    hidden, normed_mid, scale_mlp = add_branch(token_low, attended_full, gain_mlp, out)

    activated, by_gate, by_up = hidden_units(normed_mid, gate_up)
    down_far = after(down_far, activated)
    down = (w_down, down_near, down_far, swap(down_far, "fsdp", 1))
    d_gate, d_up = hidden_back(after(cot_full, activated), by_gate, by_up, down)
    d_mid_term = stacked_columns([d_gate, d_up], gate_up, "d_mid")
    d_hidden_term, d_att_term, gain_mlp_term = branch_back(
        d_mid_term, hidden, cot_full, scale_mlp, gain_mlp, out
    )
    d_attended = feature_sum(d_att_term)
    d_hidden_own = feature_sum(after(d_hidden_term, d_att_term))

    down_a, down_b = (
        Reduction(activated, cot_full, 1, "grad_down", (part_index, 2)) for part_index in (0, 1)
    )
    grad_gate = Reduction(normed_mid, d_gate, 0, "grad_gate")
    grad_up = Reduction(normed_mid, d_up, 0, "grad_up")
    square = lax.axis_size("tensor") == lax.axis_size("fsdp")
    down_a.near_far(d_att_term)
    down_b.near_far(down_a.three)
    grad_gate.near_far(down_b.three)
    down_a.far(grad_gate.three)
    down_a.send_far()
    down_b.far(down_a.two)
    down_b.send_far()
    down_a.near(down_b.two)
    down_b.near(down_a.one)
    grad_gate.far(down_b.one)
    grad_gate.send_far()
    grad_gate.near(grad_gate.two)
    down_a.mine(grad_gate.one)
    down_a.send_context()
    grad_up.near_far(down_a.own)

    dq_peer, dkv_peer = peer_backward(
        need, queries, peer_kv, after(d_attended, grad_up.three), attended, low_row, logs
    )
    dkv_in = lax.ppermute(dkv_peer, "context", [(1, 0)])
    d_query, dk_own, dv_own = own_backward(
        queries, keys_values, d_attended, attended, low_row, logs, dq_peer, cos, sin
    )
    grad_query = Reduction(normed_in, d_query, 0, "grad_query")
    grad_up.near(d_query)
    grad_up.far(grad_up.one)
    grad_up.send_far()
    down_b.mine(grad_up.two, dkv_in)
    down_b.send_context()
    d_key, d_value = finish_keys(
        dk_own, dv_own, after(dkv_in, down_b.own, d_hidden_own), cos, sin
    )
    grad_gate.mine(d_value)
    grad_gate.send_context()
    grad_up.mine(grad_gate.own)
    grad_up.send_context()
    d_in_term = stacked_columns(
        [d_query, d_key, after(d_value, grad_up.own, down_a.other, down_b.other)], qkv, "d_in"
    )
    d_in = feature_sum(d_in_term).astype(F32)
    mlp_term = plain_columns(after(activated, d_in_term), down, "mlp_out")
    mlp_out = feature_sum(after(mlp_term, grad_gate.other))

    if square:
        grad_out = Reduction(attended_full, d_hidden_own, 0, "grad_out")
    else:
        grad_out = Reduction(attended, features(d_hidden_own), 1, "grad_out")
    grad_query.near_far(d_in_term)
    grad_query.near(grad_query.three)
    grad_key = Reduction(normed_in, d_key, 0, "grad_key")
    grad_value = Reduction(normed_in, d_value, 0, "grad_value")
    grad_query.far(grad_query.one)
    grad_query.send_far()
    grad_key.near_far(grad_query.two)
    grad_value.near_far(grad_key.three)
    grad_key.near(grad_value.three)
    grad_value.near(grad_key.one)
    grad_key.far(grad_value.one)
    grad_key.send_far()
    grad_value.far(grad_key.two, mlp_term)
    grad_value.send_far()
    grad_out.near_far(grad_value.two)
    grad_out.near(grad_out.three)
    grad_out.far(grad_out.one)
    grad_out.send_far()
    grad_query.mine(grad_out.two)
    grad_query.send_context()

    stream = token_low.astype(F32)
    d_in_wide = after(d_in_term, grad_query.own).astype(F32)
    weighted = d_in_wide * stream
    inner_term = jnp.sum(weighted * gain_attn, axis=1)
    gain_attn_term = jnp.sum(weighted * scale_attn, axis=0)
    parts = lax.axis_size("tensor")
    totals_small = block_totals(
        jnp.concatenate(
            [
                jnp.broadcast_to(inner_term[None, :], (parts, row_count)),
                gain_attn_term.reshape(parts, part_width),
                gain_mlp_term.reshape(parts, part_width),
            ],
            axis=1,
        )[None]
    )
    inner_in = totals_small[0, :row_count][:, None] / full_width
    gain_sums = totals_small[0, row_count:].reshape(2, part_width)
    gain_sums = exchange(gain_sums, "fsdp", 1)
    gain_sums = exchange(gain_sums, "fsdp", 2)
    gain_sums = exchange(gain_sums, "context", 1)
    gain_width = gains.shape[1]
    grad_gains = lax.dynamic_slice_in_dim(
        gain_sums, lax.axis_index("fsdp") * gain_width, gain_width, 1
    )

    grad_down_sum = totals([down_a, down_b], 0, d_in_wide).reshape(w_down.shape)
    grad_key.mine(grad_down_sum, grad_up.other)
    grad_key.send_context()
    grad_value.mine(grad_key.own)
    grad_value.send_context()
    grad_out.mine(grad_value.own)
    if square:
        count = lax.axis_size("fsdp")
        across = [(i, (i % count) * count + i // count) for i in range(count * count)]
        grad_out.own = lax.ppermute(grad_out.own, ("fsdp", "tensor"), across)
    grad_out.send_context()
    grad_gate_up_sum = totals([grad_gate, grad_up], 1, grad_value.own)
    grad_qkv = totals([grad_query, grad_key, grad_value], 0, grad_gate_up_sum)
    grad_out_sum = totals([grad_out], 0, grad_qkv)[0]

    block_out = (own_features(hidden) + mlp_out.astype(F32)).astype(BF)
    own_tokens = tokens.astype(F32)
    grad_tokens = (
        d_hidden_own.astype(F32)
        + scale_attn * own_features(gain_attn) * d_in
        - own_tokens * scale_attn * scale_attn * scale_attn * inner_in
    ).astype(BF)
    return (
        block_out,
        grad_tokens,
        jnp.swapaxes(grad_qkv, 0, 1),
        grad_out_sum,
        grad_gate_up_sum,
        grad_down_sum,
        grad_gains,
    )


def solution(mesh):
    rows = P(("fsdp", "context"), "tensor")
    inner = P("fsdp", None, "tensor")
    outer = P("tensor", "fsdp")
    gain = P(None, ("tensor", "fsdp"))
    return jax.shard_map(
        per_device,
        mesh=mesh,
        in_specs=(rows, inner, outer, inner, outer, gain, P("fsdp", None), rows),
        out_specs=(rows, rows, inner, outer, inner, outer, gain),
        check_vma=False,
    )
```

```python
import functools

import jax
import jax.numpy as jnp
from jax import lax
from jax.experimental import pallas as pl
from jax.experimental.pallas import tpu as pltpu
from jax.sharding import PartitionSpec as P

HDIM = 64
LANES = 128
QROWS = 256
norm_eps = 1e-05
rope_base = 130000.0
masked_score = -1e30
BF = jnp.bfloat16
F32 = jnp.float32
VMEM_BYTES = 56 * 1024 * 1024
LIGHT = pl.CostEstimate(flops=1, bytes_accessed=1, transcendentals=0)


def dotf(a, b, dims):
    return lax.dot_general(a, b, (dims, ((), ())), preferred_element_type=F32)


NN = ((1,), (0,))
NT = ((1,), (1,))
TN = ((0,), (0,))


def swap(value, axis, bit):
    count = lax.axis_size(axis)
    return lax.ppermute(value, axis, [(i, i ^ bit) for i in range(count)])


def after(value, *others):
    return lax.optimization_barrier((value, *others))[0]


def shifted(value, axis):
    count = lax.axis_size(axis)
    return [
        lax.ppermute(value, axis, [(i, (i + step) % count) for i in range(count)])
        for step in range(1, count)
    ]


def exchange(value, axis, bit):
    return value + swap(value, axis, bit)


def join_kernel(axis, mode, *refs):
    pieces, out_ref = refs[:-1], refs[-1]
    count = len(pieces)
    me = lax.axis_index(axis)
    for step, piece in enumerate(pieces):
        size = piece.shape[1]
        place = (me ^ step) if mode == "xor" else (me - step + count) % count
        out_ref[:, pl.ds(pl.multiple_of(place * size, size), size)] = piece[...]


def join(pieces, axis, mode):
    rows, size = pieces[0].shape
    return pl.pallas_call(
        functools.partial(join_kernel, axis, mode),
        out_shape=jax.ShapeDtypeStruct((rows, size * len(pieces)), pieces[0].dtype),
        cost_estimate=LIGHT,
        name="join",
    )(*pieces)


def gather_gains(gains):
    if lax.axis_size("tensor") > 4 or gains.shape[1] % LANES:
        whole = lax.all_gather(gains, ("tensor", "fsdp"), axis=1, tiled=True).astype(F32)
        return gains, whole
    own = gains.astype(F32)
    part = join([own] + [swap(own, "fsdp", bit) for bit in (1, 2, 3)], "fsdp", "xor")
    return part, join([part] + shifted(part, "tensor"), "tensor", "shift")


def block_totals(blocks):
    count = lax.axis_size("tensor")
    me = lax.axis_index("tensor")
    if count > 4:
        return lax.dynamic_index_in_dim(lax.psum(blocks, "tensor"), me, 1, keepdims=False)

    def pick(place):
        return lax.dynamic_index_in_dim(blocks, place, 1, keepdims=False)

    total = pick(me)
    for step in range(1, count):
        moves = [(i, (i + step) % count) for i in range(count)]
        total = total + lax.ppermute(pick((me + step) % count), "tensor", moves)
    return total


def piece_columns(j, size):
    return pl.ds(pl.multiple_of((lax.axis_index("fsdp") ^ j) * size, size), size)


def swap_halves(block):
    lane = lax.broadcasted_iota(jnp.int32, block.shape, 1)
    up = pltpu.roll(block, LANES - HDIM // 2, 1)
    down = pltpu.roll(block, HDIM // 2, 1)
    return jnp.where((lane & (HDIM - 1)) < HDIM // 2, up, down)


def rope_tables(positions):
    lane = jnp.arange(LANES, dtype=jnp.int32)
    half = lane % (HDIM // 2)
    frequencies = rope_base ** (-2.0 * half.astype(F32) / HDIM)
    angles = positions.astype(F32)[:, None] * frequencies[None, :]
    sign = jnp.where((lane % HDIM) < HDIM // 2, -1.0, 1.0)
    return jnp.cos(angles), jnp.sin(angles) * sign[None, :]


def piece_dot(x_ref, rows, pieces, dims=NN):
    total = None
    for j, piece in enumerate(pieces):
        size = piece.shape[dims[1][0]]
        term = dotf(x_ref[rows, piece_columns(j, size)], piece, dims)
        total = term if total is None else total + term
    return total


def project_kernel(kinds, normalize, x_ref, *refs):
    pieces, (cos_ref, sin_ref, gain_ref), outs = refs[:4], refs[4:7], refs[7:]
    out_ref = outs[0]
    rows, width = out_ref.shape[1:]
    step = pl.program_id(0)
    if normalize:
        normed_ref, scale_ref = outs[1], outs[2]

        @pl.when(step == 0)
        def _():
            for r in range(0, rows, QROWS):
                part = slice(r, r + QROWS)
                stream = x_ref[part, :].astype(F32)
                mean = jnp.sum(stream * stream, axis=1, keepdims=True) / x_ref.shape[1]
                scale = lax.rsqrt(mean + norm_eps)
                scale_ref[part, :] = scale
                normed_ref[part, :] = (stream * scale * gain_ref[...]).astype(BF)

        x_ref = normed_ref
    for index, scale in enumerate(kinds):

        @pl.when(step == index)
        def _():
            for r in range(0, rows, rows):
                part = slice(r, r + rows)
                result = piece_dot(x_ref, part, [piece[0] for piece in pieces])
                for c in range(0, width, LANES):
                    block = result[:, c : c + LANES]
                    if scale:
                        block = block * cos_ref[part, :] + swap_halves(block) * sin_ref[part, :]
                    low = block.astype(BF)
                    if scale and scale != 1.0:
                        low = low * jnp.asarray(scale, BF)
                    out_ref[0, part, c : c + LANES] = low


def project(x, pieces, cos, sin, gain, kinds, first, normalize):
    rows, depth = x.shape
    _, size, width = pieces[0].shape
    flops = 2 * len(kinds) * rows * depth * width
    whole = pl.BlockSpec((rows, depth), lambda i: (0, 0))
    table = pl.BlockSpec((rows, LANES), lambda i: (0, 0))
    out_shape = [jax.ShapeDtypeStruct((len(kinds), rows, width), BF)]
    out_specs = [pl.BlockSpec((1, rows, width), lambda i: (i, 0, 0))]
    if normalize:
        out_shape += [jax.ShapeDtypeStruct((rows, depth), BF), jax.ShapeDtypeStruct((rows, 1), F32)]
        out_specs += [whole, pl.BlockSpec((rows, 1), lambda i: (0, 0))]
    return pl.pallas_call(
        functools.partial(project_kernel, kinds, normalize),
        name="project_kv" if normalize else "project_q",
        grid=(len(kinds),),
        out_shape=out_shape,
        in_specs=[whole]
        + [pl.BlockSpec((1, size, width), lambda i: (i + first, 0, 0))] * 4
        + [table, table, pl.BlockSpec((1, depth), lambda i: (0, 0))],
        out_specs=out_specs,
        compiler_params=pltpu.CompilerParams(vmem_limit_bytes=VMEM_BYTES),
        cost_estimate=LIGHT,
    )(x, *pieces, cos, sin, gain)


def head_mask(block, head):
    lane = lax.broadcasted_iota(jnp.int32, block.shape, 1)
    inside = (lane < HDIM) if head == 0 else (lane >= HDIM)
    return jnp.where(inside, block, jnp.zeros_like(block))


def own_mask(key_count, row0, low_row):
    key = lax.broadcasted_iota(jnp.int32, (key_count, QROWS), 0)
    query = row0 + lax.broadcasted_iota(jnp.int32, (key_count, QROWS), 1)
    return (key >= low_row) & (key <= query)


def peer_mask(key_count, low_row, offset):
    key = lax.broadcasted_iota(jnp.int32, (key_count, QROWS), 0) - offset
    return key >= low_row


def key_windows(need, total):
    counts = list(range(QROWS, total + 1, QROWS))
    for place, count in enumerate(counts):
        chosen = need < 0 if place == 0 else need < -counts[place - 1]
        if count < total:
            chosen = jnp.logical_and(chosen, need >= -count)
        yield count, chosen


def own_forward_kernel(q_ref, k_ref, v_ref, low_ref, out_ref, log_ref):
    rows = q_ref.shape[0]
    v_t = v_ref[...].T
    for r in range(0, rows, QROWS):
        count = r + QROWS
        allowed = own_mask(count, r, low_ref[:, r : r + QROWS])
        keys = k_ref[0:count, :]
        outs = []
        for head in range(LANES // HDIM):
            scores = dotf(keys, head_mask(q_ref[r : r + QROWS, :], head), NT)
            scores = jnp.where(allowed, scores, masked_score)
            peak = jnp.max(scores, axis=0, keepdims=True)
            weights = jnp.exp(scores - peak)
            total = jnp.sum(weights, axis=0, keepdims=True)
            part = dotf(v_t[head * HDIM : (head + 1) * HDIM, 0:count], weights.astype(BF), NN)
            outs.append(part / total)
            log_ref[0, head : head + 1, r : r + QROWS] = peak + jnp.log(total)
        out_ref[r : r + QROWS, :] = jnp.concatenate(outs, axis=0).T


def peer_forward_kernel(
    need_ref, q_ref, k_ref, v_ref, low_ref, part_ref, log_in_ref, out_ref, log_ref
):
    rows = q_ref.shape[0]
    key_total = k_ref.shape[0]
    for index, r in enumerate(range(0, rows, QROWS)):
        for key_count, chosen in key_windows(need_ref[index], key_total):

            @pl.when(chosen)
            def _():
                window = slice(key_total - key_count, key_total)
                v_t = v_ref[window, :].T
                allowed = peer_mask(key_count, low_ref[:, r : r + QROWS], key_count)
                before = part_ref[r : r + QROWS, :].T
                outs = []
                for head in range(LANES // HDIM):
                    scores = dotf(k_ref[window, :], head_mask(q_ref[r : r + QROWS, :], head), NT)
                    scores = jnp.where(allowed, scores, masked_score)
                    log_own = log_in_ref[0, head : head + 1, r : r + QROWS]
                    peak = jnp.maximum(jnp.max(scores, axis=0, keepdims=True), log_own)
                    weights = jnp.exp(scores - peak)
                    own_weight = jnp.exp(log_own - peak)
                    total = jnp.sum(weights, axis=0, keepdims=True) + own_weight
                    rows_h = slice(head * HDIM, (head + 1) * HDIM)
                    part = dotf(v_t[rows_h, :], weights.astype(BF), NN)
                    outs.append((part + before[rows_h, :] * own_weight) / total)
                    log_ref[0, head : head + 1, r : r + QROWS] = peak + jnp.log(total)
                out_ref[r : r + QROWS, :] = jnp.concatenate(outs, axis=0).T.astype(BF)

        @pl.when(need_ref[index] >= 0)
        def _():
            out_ref[r : r + QROWS, :] = part_ref[r : r + QROWS, :].astype(BF)
            log_ref[:, :, r : r + QROWS] = log_in_ref[:, :, r : r + QROWS]


def pair_spec(rows):
    return pl.BlockSpec((rows, LANES), lambda i: (0, i))


def stacked_spec(rows, part):
    return pl.BlockSpec((None, rows, LANES), lambda i: (part, 0, i))


def log_spec(rows):
    return pl.BlockSpec((1, LANES // HDIM, rows), lambda i: (i, 0, 0))


def low_spec(rows):
    return pl.BlockSpec((1, rows), lambda i: (0, 0))


def own_forward(q, kv, low_row):
    rows, width = q.shape
    pairs = width // LANES
    return pl.pallas_call(
        own_forward_kernel,
        name="own_fwd",
        grid=(pairs,),
        out_shape=(
            jax.ShapeDtypeStruct((rows, width), F32),
            jax.ShapeDtypeStruct((pairs, LANES // HDIM, rows), F32),
        ),
        in_specs=[
            pair_spec(rows),
            stacked_spec(rows, 0),
            stacked_spec(rows, 1),
            low_spec(rows),
        ],
        out_specs=(pair_spec(rows), log_spec(rows)),
        compiler_params=pltpu.CompilerParams(vmem_limit_bytes=VMEM_BYTES),
        cost_estimate=LIGHT,
    )(q, kv, kv, low_row)


SMEM_SPEC = pl.BlockSpec(memory_space=pltpu.SMEM)


def peer_forward(need, q, kv, low_row, part, log_in):
    rows, width = q.shape
    pairs = width // LANES
    return pl.pallas_call(
        peer_forward_kernel,
        name="peer_fwd",
        grid=(pairs,),
        out_shape=(
            jax.ShapeDtypeStruct((rows, width), BF),
            jax.ShapeDtypeStruct((pairs, LANES // HDIM, rows), F32),
        ),
        in_specs=[
            SMEM_SPEC,
            pair_spec(rows),
            stacked_spec(rows, 0),
            stacked_spec(rows, 1),
            low_spec(rows),
            pair_spec(rows),
            log_spec(rows),
        ],
        out_specs=(pair_spec(rows), log_spec(rows)),
        compiler_params=pltpu.CompilerParams(vmem_limit_bytes=VMEM_BYTES),
        cost_estimate=LIGHT,
    )(need, q, kv, kv, low_row, part, log_in)


def backward_block(q_rows, k_rows, v_rows, k_t, do_rows, do_o_t, logs, allowed):
    d_query, d_key, d_value = [], None, None
    for head in range(LANES // HDIM):
        rows_h = slice(head * HDIM, (head + 1) * HDIM)
        q_head = head_mask(q_rows, head)
        do_head = head_mask(do_rows, head)
        scores = dotf(k_rows, q_head, NT)
        probs = jnp.exp(jnp.where(allowed, scores, masked_score) - logs[head])
        delta = jnp.sum(do_o_t[rows_h, :], axis=0, keepdims=True)
        d_probs = dotf(v_rows, do_head, NT)
        d_scores = (probs * (d_probs - delta)).astype(BF)
        d_v = dotf(probs.astype(BF), do_head, NN)
        d_k = dotf(d_scores, q_head, NN)
        d_value = d_v if d_value is None else d_value + d_v
        d_key = d_k if d_key is None else d_key + d_k
        d_query.append(dotf(k_t[rows_h, :], d_scores, NN))
    return jnp.concatenate(d_query, axis=0), d_key, d_value


def output_product(do_ref, o_ref, window):
    product = do_ref[window].astype(F32) * o_ref[window].astype(F32)
    return product.T


def peer_backward_kernel(
    need_ref, q_ref, k_ref, v_ref, do_ref, o_ref, low_ref, log_ref, dq_ref, dkv_ref, sums
):
    rows = q_ref.shape[0]
    key_total = k_ref.shape[0]
    sums[...] = jnp.zeros_like(sums)
    for index, r in enumerate(range(0, rows, QROWS)):
        rows_q = (slice(r, r + QROWS), slice(None))
        for key_count, chosen in key_windows(need_ref[index], key_total):

            @pl.when(chosen)
            def _():
                window = slice(key_total - key_count, key_total)
                allowed = peer_mask(key_count, low_ref[:, r : r + QROWS], key_count)
                logs = [log_ref[0, h : h + 1, r : r + QROWS] for h in range(LANES // HDIM)]
                d_query, d_key, d_value = backward_block(
                    q_ref[rows_q],
                    k_ref[window, :],
                    v_ref[window, :],
                    k_ref[window, :].T,
                    do_ref[rows_q],
                    output_product(do_ref, o_ref, rows_q),
                    logs,
                    allowed,
                )
                dq_ref[rows_q] = d_query.T
                sums[0, window] += d_key
                sums[1, window] += d_value

        @pl.when(need_ref[index] >= 0)
        def _():
            dq_ref[rows_q] = jnp.zeros((QROWS, LANES), F32)

    dkv_ref[...] = sums[...].astype(BF)


def peer_backward(need, q, kv, do, o, low_row, logs):
    rows, width = q.shape
    pairs = width // LANES
    return pl.pallas_call(
        peer_backward_kernel,
        name="peer_bwd",
        grid=(pairs,),
        out_shape=(
            jax.ShapeDtypeStruct((rows, width), F32),
            jax.ShapeDtypeStruct((2, rows, width), BF),
        ),
        in_specs=[
            SMEM_SPEC,
            pair_spec(rows),
            stacked_spec(rows, 0),
            stacked_spec(rows, 1),
            pair_spec(rows),
            pair_spec(rows),
            low_spec(rows),
            log_spec(rows),
        ],
        out_specs=(pair_spec(rows), pl.BlockSpec((2, rows, LANES), lambda i: (0, 0, i))),
        scratch_shapes=[pltpu.VMEM((2, rows, LANES), F32)],
        compiler_params=pltpu.CompilerParams(vmem_limit_bytes=VMEM_BYTES),
        cost_estimate=LIGHT,
    )(need, q, kv, kv, do, o, low_row, logs)


def own_backward_kernel(
    q_ref,
    k_ref,
    v_ref,
    do_ref,
    o_ref,
    low_ref,
    log_ref,
    dq_in_ref,
    cos_ref,
    sin_ref,
    dq_ref,
    dk_ref,
    dv_ref,
    sums,
):
    rows = q_ref.shape[0]
    sums[...] = jnp.zeros_like(sums)
    k_t = k_ref[...].T
    for r in range(0, rows, QROWS):
        count = r + QROWS
        window = (slice(r, r + QROWS), slice(None))
        allowed = own_mask(count, r, low_ref[:, r : r + QROWS])
        logs = [log_ref[0, h : h + 1, r : r + QROWS] for h in range(LANES // HDIM)]
        d_query, d_key, d_value = backward_block(
            q_ref[window],
            k_ref[0:count, :],
            v_ref[0:count, :],
            k_t[:, 0:count],
            do_ref[window],
            output_product(do_ref, o_ref, window),
            logs,
            allowed,
        )
        rotated = (d_query.T + dq_in_ref[window]) * (HDIM**-0.5)
        turned = rotated * cos_ref[window] - swap_halves(rotated) * sin_ref[window]
        dq_ref[window] = turned.astype(BF)
        sums[0, 0:count] += d_key
        sums[1, 0:count] += d_value
    dk_ref[...] = sums[0]
    dv_ref[...] = sums[1]


def own_backward(q, kv, do, o, low_row, logs, dq_in, cos, sin):
    rows, width = q.shape
    pairs = width // LANES
    table = pl.BlockSpec((rows, LANES), lambda i: (0, 0))
    return pl.pallas_call(
        own_backward_kernel,
        name="own_bwd",
        grid=(pairs,),
        out_shape=(
            jax.ShapeDtypeStruct((rows, width), BF),
            jax.ShapeDtypeStruct((rows, width), F32),
            jax.ShapeDtypeStruct((rows, width), F32),
        ),
        in_specs=[
            pair_spec(rows),
            stacked_spec(rows, 0),
            stacked_spec(rows, 1),
            pair_spec(rows),
            pair_spec(rows),
            low_spec(rows),
            log_spec(rows),
            pair_spec(rows),
            table,
            table,
        ],
        out_specs=(pair_spec(rows),) * 3,
        scratch_shapes=[pltpu.VMEM((2, rows, LANES), F32)],
        compiler_params=pltpu.CompilerParams(vmem_limit_bytes=VMEM_BYTES),
        cost_estimate=LIGHT,
    )(q, kv, kv, do, o, low_row, logs, dq_in, cos, sin)


def finish_keys_kernel(dk_ref, dv_ref, dk_in_ref, dv_in_ref, cos_ref, sin_ref, dk_out, dv_out):
    total = dk_ref[...] + dk_in_ref[...].astype(F32)
    turned = total * cos_ref[...] - swap_halves(total) * sin_ref[...]
    dk_out[...] = turned.astype(BF)
    dv_out[...] = (dv_ref[...] + dv_in_ref[...].astype(F32)).astype(BF)


def finish_keys(dk, dv, dkv_in, cos, sin):
    rows, width = dk.shape
    pairs = width // LANES
    table = pl.BlockSpec((rows, LANES), lambda i: (0, 0))
    return pl.pallas_call(
        finish_keys_kernel,
        name="finish_keys",
        grid=(pairs,),
        out_shape=(jax.ShapeDtypeStruct((rows, width), BF),) * 2,
        in_specs=[pair_spec(rows), pair_spec(rows), stacked_spec(rows, 0), stacked_spec(rows, 1)]
        + [table, table],
        out_specs=(pair_spec(rows),) * 2,
        cost_estimate=LIGHT,
    )(dk, dv, dkv_in, dkv_in, cos, sin)


def branch_kernel(stream_ref, att_ref, gain_ref, *refs):
    pieces, (hidden_ref, normed_ref, scale_ref) = refs[:4], refs[4:]
    for j, piece in enumerate(pieces):
        columns = piece_columns(j, piece.shape[1])
        term = dotf(att_ref[...], piece[...], NN)
        hidden_ref[:, columns] = stream_ref[:, columns].astype(F32) + term
    hidden = hidden_ref[...]
    mean = jnp.sum(hidden * hidden, axis=1, keepdims=True) / hidden.shape[1]
    scale = lax.rsqrt(mean + norm_eps)
    scale_ref[...] = scale
    normed_ref[...] = (hidden * scale * gain_ref[...]).astype(BF)


def add_branch(stream, att, gain, pieces):
    rows, depth = stream.shape
    heads = att.shape[1]
    tile = pl.BlockSpec((QROWS, depth), lambda i: (i, 0))
    return pl.pallas_call(
        branch_kernel,
        name="branch",
        grid=(rows // QROWS,),
        out_shape=(
            jax.ShapeDtypeStruct((rows, depth), F32),
            jax.ShapeDtypeStruct((rows, depth), BF),
            jax.ShapeDtypeStruct((rows, 1), F32),
        ),
        in_specs=[
            tile,
            pl.BlockSpec((QROWS, heads), lambda i: (i, 0)),
            pl.BlockSpec((1, depth), lambda i: (0, 0)),
        ]
        + [pl.BlockSpec(pieces[0].shape, lambda i: (0, 0))] * 4,
        out_specs=(tile, tile, pl.BlockSpec((QROWS, 1), lambda i: (i, 0))),
        compiler_params=pltpu.CompilerParams(vmem_limit_bytes=VMEM_BYTES),
        cost_estimate=LIGHT,
    )(stream, att, gain, *pieces)


def hidden_kernel(x_ref, *refs):
    w_in, (act_ref, by_gate_ref, by_up_ref) = refs[:4], refs[4:]
    rows = x_ref.shape[0]
    for r in range(0, rows, rows):
        part = slice(r, r + rows)
        gate = piece_dot(x_ref, part, [piece[0] for piece in w_in])
        up = piece_dot(x_ref, part, [piece[1] for piece in w_in])
        sig = jax.nn.sigmoid(gate)
        silu = gate * sig
        act_ref[part, :] = (silu * up).astype(BF)
        by_gate_ref[part, :] = (up * sig * (1.0 + gate * (1.0 - sig))).astype(BF)
        by_up_ref[part, :] = silu.astype(BF)


def hidden_units(x, w_in):
    rows, depth = x.shape
    _, size, units = w_in[0].shape
    tile = 256
    part = pl.BlockSpec((rows, tile), lambda i: (0, i))
    return pl.pallas_call(
        hidden_kernel,
        grid=(units // tile,),
        out_shape=(jax.ShapeDtypeStruct((rows, units), BF),) * 3,
        in_specs=[pl.BlockSpec((rows, depth), lambda i: (0, 0))]
        + [pl.BlockSpec((2, size, tile), lambda i: (0, 0, i))] * 4,
        out_specs=(part,) * 3,
        compiler_params=pltpu.CompilerParams(vmem_limit_bytes=VMEM_BYTES),
        cost_estimate=LIGHT,
        name="hidden",
    )(x, *w_in)


def hidden_back_kernel(cot_ref, by_gate_ref, by_up_ref, *refs):
    w_down, (dg_ref, du_ref) = refs[:4], refs[4:]
    rows = cot_ref.shape[0]
    for r in range(0, rows, rows):
        part = slice(r, r + rows)
        d_act = piece_dot(cot_ref, part, [piece[...] for piece in w_down], NT)
        dg_ref[part, :] = (d_act * by_gate_ref[part, :].astype(F32)).astype(BF)
        du_ref[part, :] = (d_act * by_up_ref[part, :].astype(F32)).astype(BF)


def hidden_back(cot, by_gate, by_up, w_down):
    rows, depth = cot.shape
    units, size = w_down[0].shape
    tile = 256
    part = pl.BlockSpec((rows, tile), lambda i: (0, i))
    return pl.pallas_call(
        hidden_back_kernel,
        grid=(units // tile,),
        out_shape=(jax.ShapeDtypeStruct((rows, units), BF),) * 2,
        in_specs=[pl.BlockSpec((rows, depth), lambda i: (0, 0)), part, part]
        + [pl.BlockSpec((tile, size), lambda i: (i, 0))] * 4,
        out_specs=(part,) * 2,
        compiler_params=pltpu.CompilerParams(vmem_limit_bytes=VMEM_BYTES),
        cost_estimate=LIGHT,
        name="hidden_back",
    )(cot, by_gate, by_up, *w_down)


def phased(i, block, make_index, tiles):
    def index_map(j, t):
        return make_index(jnp.where(j < i, 0, jnp.where(j == i, t, tiles - 1)))

    return pl.BlockSpec(block, index_map)


def columns_call(kernel_dot, lefts, pieces, block, make_index, size, flops, name):
    rows = lefts[0].shape[0]
    tile = min(size, 256)
    tiles = size // tile
    depth = size * 4

    def kernel(*refs):
        left_refs, piece_refs, out_ref = refs[: len(lefts)], refs[len(lefts) : -1], refs[-1]
        for j, piece in enumerate(piece_refs):

            @pl.when(pl.program_id(0) == j)
            def _():
                out_ref[...] = kernel_dot([left[...] for left in left_refs], piece).astype(BF)

    def out_index(j, t):
        return (0, (lax.axis_index("fsdp") ^ j) * tiles + t)

    return pl.pallas_call(
        kernel,
        grid=(4, tiles),
        out_shape=jax.ShapeDtypeStruct((rows, depth), BF),
        in_specs=[pl.BlockSpec(left.shape, lambda j, t: (0, 0)) for left in lefts]
        + [phased(i, block(tile), make_index, tiles) for i in range(4)],
        out_specs=pl.BlockSpec((rows, tile), out_index),
        compiler_params=pltpu.CompilerParams(vmem_limit_bytes=VMEM_BYTES),
        cost_estimate=LIGHT,
        name=name,
    )(*lefts, *pieces)


def stacked_columns(lefts, pieces, name):
    count, size, inner = pieces[0].shape

    def product(parts, piece):
        return sum(dotf(parts[c], piece[c], NT) for c in range(count))

    return columns_call(
        product,
        lefts,
        pieces,
        lambda tile: (count, tile, inner),
        lambda t: (0, t, 0),
        size,
        8 * lefts[0].shape[0] * size * inner * count,
        name,
    )


def plain_columns(left, pieces, name):
    inner, size = pieces[0].shape
    return columns_call(
        lambda parts, piece: dotf(parts[0], piece[...], NN),
        [left],
        pieces,
        lambda tile: (inner, tile),
        lambda t: (0, t),
        size,
        8 * left.shape[0] * size * inner,
        name,
    )


def branch_back_kernel(shares, d_mid_ref, hidden_ref, cot_ref, scale_ref, gain_ref, *refs):
    pieces, (d_hidden_ref, d_att_ref, gain_out_ref) = refs[:4], refs[4:7]
    d_mid = d_mid_ref[...].astype(F32)
    hidden = hidden_ref[...]
    scale = scale_ref[...]
    weighted = d_mid * gain_ref[...]
    inner = jnp.sum(weighted * hidden, axis=1, keepdims=True) / hidden.shape[1]
    d_hidden = (
        cot_ref[...].astype(F32) * (1.0 / shares)
        + scale * weighted
        - hidden * (scale * scale * scale * inner)
    )
    gain_term = jnp.sum(d_mid * hidden * scale, axis=0, keepdims=True)

    @pl.when(pl.program_id(0) == 0)
    def _():
        gain_out_ref[...] = gain_term

    @pl.when(pl.program_id(0) != 0)
    def _():
        gain_out_ref[...] += gain_term

    d_hidden_ref[...] = d_hidden.astype(BF)
    heads = d_att_ref.shape[1]
    for e in range(0, heads, 512):
        columns = slice(e, e + 512)
        d_att_ref[:, columns] = piece_dot(
            d_hidden_ref, slice(None), [piece[columns, :] for piece in pieces], NT
        ).astype(BF)


def branch_back(d_mid, hidden, cot, scale, gain, pieces):
    rows, depth = hidden.shape
    heads, size = pieces[0].shape
    tile = pl.BlockSpec((QROWS, depth), lambda i: (i, 0))
    row = pl.BlockSpec((1, depth), lambda i: (0, 0))
    return pl.pallas_call(
        functools.partial(branch_back_kernel, lax.axis_size("tensor")),
        name="branch_back",
        grid=(rows // QROWS,),
        in_specs=[tile, tile, tile, pl.BlockSpec((QROWS, 1), lambda i: (i, 0)), row]
        + [pl.BlockSpec((heads, size), lambda i: (0, 0))] * 4,
        out_specs=(tile, pl.BlockSpec((QROWS, heads), lambda i: (i, 0)), row),
        out_shape=(
            jax.ShapeDtypeStruct((rows, depth), BF),
            jax.ShapeDtypeStruct((rows, heads), BF),
            jax.ShapeDtypeStruct((1, depth), F32),
        ),
        compiler_params=pltpu.CompilerParams(vmem_limit_bytes=VMEM_BYTES),
        cost_estimate=LIGHT,
    )(d_mid, hidden, cot, scale, gain, *pieces)


def grad_call(left, right, cut, place, adds, name, span=(0, 1)):
    rows = left.shape[0]
    size = (left, right)[cut].shape[1] // 4
    swept = (right, left)[cut].shape[1] // span[1]
    height, width = (size, swept) if cut == 0 else (swept, size)
    tile = min(1024, swept)
    offset = span[0] * (swept // tile)
    block = (height, tile) if cut == 0 else (tile, width)

    def owner():
        return lax.axis_index("fsdp") ^ place

    def swept_index(t):
        return (0, t) if cut == 0 else (t, 0)

    def kernel(left_ref, right_ref, *refs):
        add_refs, out_ref = refs[: len(adds)], refs[len(adds)]
        if cut == 0:
            turned = refs[-1]

            @pl.when(pl.program_id(0) == 0)
            def _():
                turned[...] = left_ref[...].T

            result = dotf(turned[...], right_ref[...], NN)
        else:
            result = dotf(left_ref[...].T, right_ref[...], NN)
        for add in add_refs:
            result = result + add[...].astype(F32)
        out_ref[...] = result.astype(BF)

    fixed = pl.BlockSpec((rows, size), lambda t: (0, owner()))
    moving = pl.BlockSpec((rows, tile), lambda t: (0, t + offset))
    return pl.pallas_call(
        kernel,
        grid=(swept // tile,),
        out_shape=jax.ShapeDtypeStruct((height, width), BF),
        in_specs=[fixed, moving] * (cut == 0)
        + [moving, fixed] * (cut == 1)
        + [pl.BlockSpec(block, swept_index)] * len(adds),
        out_specs=pl.BlockSpec(block, swept_index),
        scratch_shapes=[pltpu.VMEM((size, rows), BF)] if cut == 0 else [],
        compiler_params=pltpu.CompilerParams(vmem_limit_bytes=VMEM_BYTES),
        cost_estimate=LIGHT,
        name=name,
    )(left, right, *adds)


class Reduction:
    def __init__(self, left, right, cut, name, span=(0, 1)):
        self.args, self.name, self.span = (left, right, cut), name, span

    def call(self, place, deps, step, adds=()):
        left, right, cut = self.args
        left = after(left, *deps) if deps else left
        return grad_call(left, right, cut, place, adds, self.name + step, self.span)

    def near_far(self, *deps):
        self.three = self.call(3, deps, "_3")
        self.for_two = swap(self.three, "fsdp", 1)

    def near(self, *deps):
        self.one = self.call(1, deps, "_1")
        self.for_own = swap(self.one, "fsdp", 1)

    def far(self, *deps):
        self.two = self.call(2, deps, "_2", [self.for_two])

    def send_far(self, *deps):
        self.across = swap(after(self.two, *deps), "fsdp", 2)

    def mine(self, *deps):
        self.own = self.call(0, deps, "_0", [self.for_own, self.across])

    def send_context(self, *deps):
        self.other = swap(after(self.own, *deps), "context", 1)


def totals_kernel(slots, *refs):
    pairs, out_ref = refs[:-1], refs[-1]
    for slot in range(len(pairs) // 2):
        total = pairs[2 * slot][...].astype(F32) + pairs[2 * slot + 1][...].astype(F32)
        if slots == 0:
            out_ref[slot] = total
        else:
            out_ref[:, slot, :] = total


def totals(sums, slots, *deps):
    arrays = [array for part in sums for array in (part.own, part.other)]
    if deps:
        arrays[0] = after(arrays[0], *deps)
    rows, width = arrays[0].shape
    tile = 128
    shape = [rows, width]
    shape.insert(slots, len(sums))
    block = [tile, width]
    block.insert(slots, len(sums))
    return pl.pallas_call(
        functools.partial(totals_kernel, slots),
        grid=(rows // tile,),
        out_shape=jax.ShapeDtypeStruct(tuple(shape), F32),
        in_specs=[pl.BlockSpec((tile, width), lambda i: (i, 0))] * len(arrays),
        out_specs=pl.BlockSpec(
            tuple(block), (lambda i: (0, i, 0)) if slots == 0 else (lambda i: (i, 0, 0))
        ),
        compiler_params=pltpu.CompilerParams(vmem_limit_bytes=VMEM_BYTES),
        cost_estimate=LIGHT,
        name="totals",
    )(*arrays)


def row_sum(values_in):
    return jnp.sum(values_in, axis=1, keepdims=True)


def per_device(tokens, w_qkv, w_out, w_gate_up, w_down, gains, seq_lengths, cotangent):
    row_count, part_width = tokens.shape
    tensor_index = lax.axis_index("tensor")
    context_index = lax.axis_index("context")
    full_width = part_width * lax.axis_size("tensor")

    def features(part_in):
        return lax.all_gather(part_in, "tensor", axis=1, tiled=True)

    def feature_sum(term):
        return lax.psum_scatter(term.astype(BF), "tensor", scatter_dimension=1, tiled=True)

    def own_features(full):
        return lax.dynamic_slice_in_dim(full, tensor_index * part_width, part_width, 1)

    ending = jnp.cumsum(seq_lengths[0])
    starts = ending - seq_lengths[0]
    places = context_index * row_count + jnp.arange(row_count, dtype=jnp.int32)
    first_token = jnp.max(jnp.where(starts[None, :] <= places[:, None], starts[None, :], 0), axis=1)
    cos, sin = rope_tables(places - first_token)
    low = first_token - context_index * row_count
    low_row = low[None, :]
    need = low[::QROWS]

    token_low = features(tokens)
    gain_near, gain_full = gather_gains(gains)
    gain_attn, gain_mlp = gain_full[0:1], gain_full[1:2]

    qkv_own = jnp.swapaxes(w_qkv, 0, 1)
    half = qkv_own.shape[1] // 2
    far_half = swap(
        lax.dynamic_slice_in_dim(after(qkv_own, gain_near), context_index * half, half, 1),
        "fsdp",
        2,
    )
    other_half = swap(far_half, "context", 1)
    qkv_far = jnp.where(
        context_index == 0,
        jnp.concatenate([far_half, other_half], axis=1),
        jnp.concatenate([other_half, far_half], axis=1),
    )
    qkv_near = swap(qkv_own, "fsdp", 1)
    qkv = (qkv_own, qkv_near, qkv_far, swap(qkv_far, "fsdp", 1))

    gate_up_own = jnp.swapaxes(w_gate_up, 0, 1)
    cut = gate_up_own.shape[1] * 12 // 32
    gate_up_a = swap(after(gate_up_own[:, :cut], far_half), "fsdp", 2)
    gate_up_b = swap(after(gate_up_own[:, cut:], gate_up_a), "fsdp", 2)

    keys_values, normed_in, scale_attn = project(
        after(token_low, gate_up_a), qkv, cos, sin, gain_attn, (1.0, None), 1, True
    )
    peer_kv = lax.ppermute(keys_values, "context", [(0, 1)])
    queries = project(normed_in, qkv, cos, sin, gain_attn, (HDIM**-0.5,), 0, False)[0][0]
    part, part_log = own_forward(queries, keys_values, low_row)
    attended, logs = peer_forward(
        need, queries, peer_kv, low_row, after(part, gate_up_b), part_log
    )
    attended_full = features(attended)

    out_own = after(lax.all_gather(w_out, "tensor", axis=0, tiled=True), attended)
    out_near = swap(out_own, "fsdp", 1)
    out_far = swap(out_own, "fsdp", 2)
    out_far_near = swap(out_far, "fsdp", 1)
    out = (out_own, out_near, out_far, out_far_near)
    gate_up_own, gate_up_a, gate_up_b = lax.optimization_barrier(
        (gate_up_own, gate_up_a, gate_up_b, attended)
    )[:3]
    gate_up_far = jnp.concatenate([gate_up_a, gate_up_b], axis=1)
    gate_up_near = swap(gate_up_own, "fsdp", 1)
    gate_up = (gate_up_own, gate_up_near, gate_up_far, swap(gate_up_far, "fsdp", 1))
    cot_full = features(after(cotangent, attended_full, out_far_near, out_near))
    down_far = swap(after(w_down, attended_full, out_far_near), "fsdp", 2)
    down_near = swap(after(w_down, attended_full), "fsdp", 1)
    hidden, normed_mid, scale_mlp = add_branch(token_low, attended_full, gain_mlp, out)

    activated, by_gate, by_up = hidden_units(normed_mid, gate_up)
    down_far = after(down_far, activated)
    down = (w_down, down_near, down_far, swap(down_far, "fsdp", 1))
    d_gate, d_up = hidden_back(after(cot_full, activated), by_gate, by_up, down)
    d_mid_term = stacked_columns([d_gate, d_up], gate_up, "d_mid")
    d_hidden_term, d_att_term, gain_mlp_term = branch_back(
        d_mid_term, hidden, cot_full, scale_mlp, gain_mlp, out
    )
    d_attended = feature_sum(d_att_term)
    d_hidden_own = feature_sum(after(d_hidden_term, d_att_term))

    down_a, down_b = (
        Reduction(activated, cot_full, 1, "grad_down", (part_index, 2)) for part_index in (0, 1)
    )
    grad_gate = Reduction(normed_mid, d_gate, 0, "grad_gate")
    grad_up = Reduction(normed_mid, d_up, 0, "grad_up")
    square = lax.axis_size("tensor") == lax.axis_size("fsdp")
    down_a.near_far(d_att_term)
    down_b.near_far(down_a.three)
    grad_gate.near_far(down_b.three)
    down_a.far(grad_gate.three)
    down_a.send_far()
    down_b.far(down_a.two)
    down_b.send_far()
    down_a.near(down_b.two)
    down_b.near(down_a.one)
    grad_gate.far(down_b.one)
    grad_gate.send_far()
    grad_gate.near(grad_gate.two)
    down_a.mine(grad_gate.one)
    down_a.send_context()
    grad_up.near_far(down_a.own)

    dq_peer, dkv_peer = peer_backward(
        need, queries, peer_kv, after(d_attended, grad_up.three), attended, low_row, logs
    )
    dkv_in = lax.ppermute(dkv_peer, "context", [(1, 0)])
    d_query, dk_own, dv_own = own_backward(
        queries, keys_values, d_attended, attended, low_row, logs, dq_peer, cos, sin
    )
    grad_query = Reduction(normed_in, d_query, 0, "grad_query")
    grad_up.near(d_query)
    grad_up.far(grad_up.one)
    grad_up.send_far()
    mlp_term = plain_columns(after(activated, grad_up.two), down, "mlp_out")
    mlp_out = feature_sum(mlp_term)
    down_b.mine(mlp_term, dkv_in)
    down_b.send_context()
    d_key, d_value = finish_keys(
        dk_own, dv_own, after(dkv_in, down_b.own, d_hidden_own), cos, sin
    )
    if square:
        grad_out = Reduction(attended_full, d_hidden_own, 0, "grad_out")
    else:
        grad_out = Reduction(attended, features(d_hidden_own), 1, "grad_out")
    grad_query.near_far(d_value)
    grad_out.near_far(grad_query.three)
    grad_query.near(grad_out.three)
    grad_out.near(grad_query.one)
    grad_query.far(grad_out.one)
    grad_out.far(grad_query.two)
    grad_gate.mine(grad_out.two, down_a.other, down_b.other)
    grad_gate.send_context()
    grad_up.mine(grad_gate.own)
    grad_up.send_context()
    d_in_term = stacked_columns(
        [d_query, d_key, after(d_value, grad_up.own, grad_gate.other)], qkv, "d_in"
    )
    d_in = feature_sum(d_in_term).astype(F32)
    grad_query.send_far(d_in_term)
    grad_out.send_far(d_in_term)
    grad_key = Reduction(normed_in, d_key, 0, "grad_key")
    grad_value = Reduction(normed_in, d_value, 0, "grad_value")
    grad_key.near_far(d_in_term)
    grad_value.near_far(grad_key.three)
    grad_key.near(grad_value.three)
    grad_value.near(grad_key.one)
    grad_key.far(grad_value.one)
    grad_key.send_far()
    grad_value.far(grad_key.two)
    grad_value.send_far()
    grad_query.mine(grad_value.two)
    grad_query.send_context()
    grad_out.mine(grad_query.own)
    if square:
        count = lax.axis_size("fsdp")
        across = [(i, (i % count) * count + i // count) for i in range(count * count)]
        grad_out.own = lax.ppermute(grad_out.own, ("fsdp", "tensor"), across)
    grad_out.send_context()

    stream = token_low.astype(F32)
    d_in_wide = after(d_in_term, grad_query.own).astype(F32)
    weighted = d_in_wide * stream
    inner_term = jnp.sum(weighted * gain_attn, axis=1)
    gain_attn_term = jnp.sum(weighted * scale_attn, axis=0)
    parts = lax.axis_size("tensor")
    totals_small = block_totals(
        jnp.concatenate(
            [
                jnp.broadcast_to(inner_term[None, :], (parts, row_count)),
                gain_attn_term.reshape(parts, part_width),
                gain_mlp_term.reshape(parts, part_width),
            ],
            axis=1,
        )[None]
    )
    inner_in = totals_small[0, :row_count][:, None] / full_width
    gain_sums = totals_small[0, row_count:].reshape(2, part_width)
    gain_sums = exchange(gain_sums, "fsdp", 1)
    gain_sums = exchange(gain_sums, "fsdp", 2)
    gain_sums = exchange(gain_sums, "context", 1)
    gain_width = gains.shape[1]
    grad_gains = lax.dynamic_slice_in_dim(
        gain_sums, lax.axis_index("fsdp") * gain_width, gain_width, 1
    )

    grad_down_sum = totals([down_a, down_b], 0, d_in_wide).reshape(w_down.shape)
    grad_key.mine(grad_down_sum, grad_up.other, mlp_out)
    grad_key.send_context()
    grad_value.mine(grad_key.own)
    grad_value.send_context()
    grad_gate_up_sum = totals([grad_gate, grad_up], 1, grad_value.own)
    grad_qkv = totals([grad_query, grad_key, grad_value], 0, grad_gate_up_sum)
    grad_out_sum = totals([grad_out], 0, grad_qkv)[0]

    block_out = (own_features(hidden) + mlp_out.astype(F32)).astype(BF)
    own_tokens = tokens.astype(F32)
    grad_tokens = (
        d_hidden_own.astype(F32)
        + scale_attn * own_features(gain_attn) * d_in
        - own_tokens * scale_attn * scale_attn * scale_attn * inner_in
    ).astype(BF)
    return (
        block_out,
        grad_tokens,
        jnp.swapaxes(grad_qkv, 0, 1),
        grad_out_sum,
        grad_gate_up_sum,
        grad_down_sum,
        grad_gains,
    )


def solution(mesh):
    rows = P(("fsdp", "context"), "tensor")
    inner = P("fsdp", None, "tensor")
    outer = P("tensor", "fsdp")
    gain = P(None, ("tensor", "fsdp"))
    return jax.shard_map(
        per_device,
        mesh=mesh,
        in_specs=(rows, inner, outer, inner, outer, gain, P("fsdp", None), rows),
        out_specs=(rows, rows, inner, outer, inner, outer, gain),
        check_vma=False,
    )
```

```python
import functools

import jax
import jax.numpy as jnp
from jax import lax
from jax.experimental import pallas as pl
from jax.experimental.pallas import tpu as pltpu
from jax.sharding import PartitionSpec as P

HDIM = 64
LANES = 128
QROWS = 256
norm_eps = 1e-05
rope_base = 130000.0
masked_score = -1e30
BF = jnp.bfloat16
F32 = jnp.float32
VMEM_BYTES = 56 * 1024 * 1024
LIGHT = pl.CostEstimate(flops=1, bytes_accessed=1, transcendentals=0)


def dotf(a, b, dims):
    return lax.dot_general(a, b, (dims, ((), ())), preferred_element_type=F32)


NN = ((1,), (0,))
NT = ((1,), (1,))
TN = ((0,), (0,))


def swap(value, axis, bit):
    count = lax.axis_size(axis)
    return lax.ppermute(value, axis, [(i, i ^ bit) for i in range(count)])


def after(value, *others):
    return lax.optimization_barrier((value, *others))[0]


def shifted(value, axis):
    count = lax.axis_size(axis)
    return [
        lax.ppermute(value, axis, [(i, (i + step) % count) for i in range(count)])
        for step in range(1, count)
    ]


def exchange(value, axis, bit):
    return value + swap(value, axis, bit)


def join_kernel(axis, mode, *refs):
    pieces, out_ref = refs[:-1], refs[-1]
    count = len(pieces)
    me = lax.axis_index(axis)
    for step, piece in enumerate(pieces):
        size = piece.shape[1]
        place = (me ^ step) if mode == "xor" else (me - step + count) % count
        out_ref[:, pl.ds(pl.multiple_of(place * size, size), size)] = piece[...]


def join(pieces, axis, mode):
    rows, size = pieces[0].shape
    return pl.pallas_call(
        functools.partial(join_kernel, axis, mode),
        out_shape=jax.ShapeDtypeStruct((rows, size * len(pieces)), pieces[0].dtype),
        cost_estimate=LIGHT,
        name="join",
    )(*pieces)


def gather_gains(gains):
    if lax.axis_size("tensor") > 4 or gains.shape[1] % LANES:
        whole = lax.all_gather(gains, ("tensor", "fsdp"), axis=1, tiled=True).astype(F32)
        return gains, whole
    own = gains.astype(F32)
    part = join([own] + [swap(own, "fsdp", bit) for bit in (1, 2, 3)], "fsdp", "xor")
    return part, join([part] + shifted(part, "tensor"), "tensor", "shift")


def block_totals(blocks):
    count = lax.axis_size("tensor")
    me = lax.axis_index("tensor")
    if count > 4:
        return lax.dynamic_index_in_dim(lax.psum(blocks, "tensor"), me, 1, keepdims=False)

    def pick(place):
        return lax.dynamic_index_in_dim(blocks, place, 1, keepdims=False)

    total = pick(me)
    for step in range(1, count):
        moves = [(i, (i + step) % count) for i in range(count)]
        total = total + lax.ppermute(pick((me + step) % count), "tensor", moves)
    return total


def piece_columns(j, size):
    return pl.ds(pl.multiple_of((lax.axis_index("fsdp") ^ j) * size, size), size)


def swap_halves(block):
    lane = lax.broadcasted_iota(jnp.int32, block.shape, 1)
    up = pltpu.roll(block, LANES - HDIM // 2, 1)
    down = pltpu.roll(block, HDIM // 2, 1)
    return jnp.where((lane & (HDIM - 1)) < HDIM // 2, up, down)


def rope_tables(positions):
    lane = jnp.arange(LANES, dtype=jnp.int32)
    half = lane % (HDIM // 2)
    frequencies = rope_base ** (-2.0 * half.astype(F32) / HDIM)
    angles = positions.astype(F32)[:, None] * frequencies[None, :]
    sign = jnp.where((lane % HDIM) < HDIM // 2, -1.0, 1.0)
    return jnp.cos(angles), jnp.sin(angles) * sign[None, :]


def piece_dot(x_ref, rows, pieces, dims=NN):
    total = None
    for j, piece in enumerate(pieces):
        size = piece.shape[dims[1][0]]
        term = dotf(x_ref[rows, piece_columns(j, size)], piece, dims)
        total = term if total is None else total + term
    return total


def project_kernel(kinds, normalize, x_ref, *refs):
    pieces, (cos_ref, sin_ref, gain_ref), outs = refs[:4], refs[4:7], refs[7:]
    out_ref = outs[0]
    rows, width = out_ref.shape[1:]
    step = pl.program_id(0)
    if normalize:
        normed_ref, scale_ref = outs[1], outs[2]

        @pl.when(step == 0)
        def _():
            for r in range(0, rows, QROWS):
                part = slice(r, r + QROWS)
                stream = x_ref[part, :].astype(F32)
                mean = jnp.sum(stream * stream, axis=1, keepdims=True) / x_ref.shape[1]
                scale = lax.rsqrt(mean + norm_eps)
                scale_ref[part, :] = scale
                normed_ref[part, :] = (stream * scale * gain_ref[...]).astype(BF)

        x_ref = normed_ref
    for index, scale in enumerate(kinds):

        @pl.when(step == index)
        def _():
            for r in range(0, rows, rows):
                part = slice(r, r + rows)
                result = piece_dot(x_ref, part, [piece[0] for piece in pieces])
                for c in range(0, width, LANES):
                    block = result[:, c : c + LANES]
                    if scale:
                        block = block * cos_ref[part, :] + swap_halves(block) * sin_ref[part, :]
                    low = block.astype(BF)
                    if scale and scale != 1.0:
                        low = low * jnp.asarray(scale, BF)
                    out_ref[0, part, c : c + LANES] = low


def project(x, pieces, cos, sin, gain, kinds, first, normalize):
    rows, depth = x.shape
    _, size, width = pieces[0].shape
    flops = 2 * len(kinds) * rows * depth * width
    whole = pl.BlockSpec((rows, depth), lambda i: (0, 0))
    table = pl.BlockSpec((rows, LANES), lambda i: (0, 0))
    out_shape = [jax.ShapeDtypeStruct((len(kinds), rows, width), BF)]
    out_specs = [pl.BlockSpec((1, rows, width), lambda i: (i, 0, 0))]
    if normalize:
        out_shape += [jax.ShapeDtypeStruct((rows, depth), BF), jax.ShapeDtypeStruct((rows, 1), F32)]
        out_specs += [whole, pl.BlockSpec((rows, 1), lambda i: (0, 0))]
    return pl.pallas_call(
        functools.partial(project_kernel, kinds, normalize),
        name="project_kv" if normalize else "project_q",
        grid=(len(kinds),),
        out_shape=out_shape,
        in_specs=[whole]
        + [pl.BlockSpec((1, size, width), lambda i: (i + first, 0, 0))] * 4
        + [table, table, pl.BlockSpec((1, depth), lambda i: (0, 0))],
        out_specs=out_specs,
        compiler_params=pltpu.CompilerParams(vmem_limit_bytes=VMEM_BYTES),
        cost_estimate=LIGHT,
    )(x, *pieces, cos, sin, gain)


def head_mask(block, head):
    lane = lax.broadcasted_iota(jnp.int32, block.shape, 1)
    inside = (lane < HDIM) if head == 0 else (lane >= HDIM)
    return jnp.where(inside, block, jnp.zeros_like(block))


def own_mask(key_count, row0, low_row):
    key = lax.broadcasted_iota(jnp.int32, (key_count, QROWS), 0)
    query = row0 + lax.broadcasted_iota(jnp.int32, (key_count, QROWS), 1)
    return (key >= low_row) & (key <= query)


def peer_mask(key_count, low_row, offset):
    key = lax.broadcasted_iota(jnp.int32, (key_count, QROWS), 0) - offset
    return key >= low_row


def key_windows(need, total):
    counts = list(range(QROWS, total + 1, QROWS))
    for place, count in enumerate(counts):
        chosen = need < 0 if place == 0 else need < -counts[place - 1]
        if count < total:
            chosen = jnp.logical_and(chosen, need >= -count)
        yield count, chosen


def own_forward_kernel(q_ref, k_ref, v_ref, low_ref, out_ref, log_ref):
    rows = q_ref.shape[0]
    v_t = v_ref[...].T
    for r in range(0, rows, QROWS):
        count = r + QROWS
        allowed = own_mask(count, r, low_ref[:, r : r + QROWS])
        keys = k_ref[0:count, :]
        outs = []
        for head in range(LANES // HDIM):
            scores = dotf(keys, head_mask(q_ref[r : r + QROWS, :], head), NT)
            scores = jnp.where(allowed, scores, masked_score)
            peak = jnp.max(scores, axis=0, keepdims=True)
            weights = jnp.exp(scores - peak)
            total = jnp.sum(weights, axis=0, keepdims=True)
            part = dotf(v_t[head * HDIM : (head + 1) * HDIM, 0:count], weights.astype(BF), NN)
            outs.append(part / total)
            log_ref[0, head : head + 1, r : r + QROWS] = peak + jnp.log(total)
        out_ref[r : r + QROWS, :] = jnp.concatenate(outs, axis=0).T


def peer_forward_kernel(
    need_ref, q_ref, k_ref, v_ref, low_ref, part_ref, log_in_ref, out_ref, log_ref
):
    rows = q_ref.shape[0]
    key_total = k_ref.shape[0]
    for index, r in enumerate(range(0, rows, QROWS)):
        for key_count, chosen in key_windows(need_ref[index], key_total):

            @pl.when(chosen)
            def _():
                window = slice(key_total - key_count, key_total)
                v_t = v_ref[window, :].T
                allowed = peer_mask(key_count, low_ref[:, r : r + QROWS], key_count)
                before = part_ref[r : r + QROWS, :].T
                outs = []
                for head in range(LANES // HDIM):
                    scores = dotf(k_ref[window, :], head_mask(q_ref[r : r + QROWS, :], head), NT)
                    scores = jnp.where(allowed, scores, masked_score)
                    log_own = log_in_ref[0, head : head + 1, r : r + QROWS]
                    peak = jnp.maximum(jnp.max(scores, axis=0, keepdims=True), log_own)
                    weights = jnp.exp(scores - peak)
                    own_weight = jnp.exp(log_own - peak)
                    total = jnp.sum(weights, axis=0, keepdims=True) + own_weight
                    rows_h = slice(head * HDIM, (head + 1) * HDIM)
                    part = dotf(v_t[rows_h, :], weights.astype(BF), NN)
                    outs.append((part + before[rows_h, :] * own_weight) / total)
                    log_ref[0, head : head + 1, r : r + QROWS] = peak + jnp.log(total)
                out_ref[r : r + QROWS, :] = jnp.concatenate(outs, axis=0).T.astype(BF)

        @pl.when(need_ref[index] >= 0)
        def _():
            out_ref[r : r + QROWS, :] = part_ref[r : r + QROWS, :].astype(BF)
            log_ref[:, :, r : r + QROWS] = log_in_ref[:, :, r : r + QROWS]


def pair_spec(rows):
    return pl.BlockSpec((rows, LANES), lambda i: (0, i))


def stacked_spec(rows, part):
    return pl.BlockSpec((None, rows, LANES), lambda i: (part, 0, i))


def log_spec(rows):
    return pl.BlockSpec((1, LANES // HDIM, rows), lambda i: (i, 0, 0))


def low_spec(rows):
    return pl.BlockSpec((1, rows), lambda i: (0, 0))


def own_forward(q, kv, low_row):
    rows, width = q.shape
    pairs = width // LANES
    return pl.pallas_call(
        own_forward_kernel,
        name="own_fwd",
        grid=(pairs,),
        out_shape=(
            jax.ShapeDtypeStruct((rows, width), F32),
            jax.ShapeDtypeStruct((pairs, LANES // HDIM, rows), F32),
        ),
        in_specs=[
            pair_spec(rows),
            stacked_spec(rows, 0),
            stacked_spec(rows, 1),
            low_spec(rows),
        ],
        out_specs=(pair_spec(rows), log_spec(rows)),
        compiler_params=pltpu.CompilerParams(vmem_limit_bytes=VMEM_BYTES),
        cost_estimate=LIGHT,
    )(q, kv, kv, low_row)


SMEM_SPEC = pl.BlockSpec(memory_space=pltpu.SMEM)


def peer_forward(need, q, kv, low_row, part, log_in):
    rows, width = q.shape
    pairs = width // LANES
    return pl.pallas_call(
        peer_forward_kernel,
        name="peer_fwd",
        grid=(pairs,),
        out_shape=(
            jax.ShapeDtypeStruct((rows, width), BF),
            jax.ShapeDtypeStruct((pairs, LANES // HDIM, rows), F32),
        ),
        in_specs=[
            SMEM_SPEC,
            pair_spec(rows),
            stacked_spec(rows, 0),
            stacked_spec(rows, 1),
            low_spec(rows),
            pair_spec(rows),
            log_spec(rows),
        ],
        out_specs=(pair_spec(rows), log_spec(rows)),
        compiler_params=pltpu.CompilerParams(vmem_limit_bytes=VMEM_BYTES),
        cost_estimate=LIGHT,
    )(need, q, kv, kv, low_row, part, log_in)


def backward_block(q_rows, k_rows, v_rows, k_t, do_rows, do_o_t, logs, allowed):
    d_query, d_key, d_value = [], None, None
    for head in range(LANES // HDIM):
        rows_h = slice(head * HDIM, (head + 1) * HDIM)
        q_head = head_mask(q_rows, head)
        do_head = head_mask(do_rows, head)
        scores = dotf(k_rows, q_head, NT)
        probs = jnp.exp(jnp.where(allowed, scores, masked_score) - logs[head])
        delta = jnp.sum(do_o_t[rows_h, :], axis=0, keepdims=True)
        d_probs = dotf(v_rows, do_head, NT)
        d_scores = (probs * (d_probs - delta)).astype(BF)
        d_v = dotf(probs.astype(BF), do_head, NN)
        d_k = dotf(d_scores, q_head, NN)
        d_value = d_v if d_value is None else d_value + d_v
        d_key = d_k if d_key is None else d_key + d_k
        d_query.append(dotf(k_t[rows_h, :], d_scores, NN))
    return jnp.concatenate(d_query, axis=0), d_key, d_value


def output_product(do_ref, o_ref, window):
    product = do_ref[window].astype(F32) * o_ref[window].astype(F32)
    return product.T


def peer_backward_kernel(
    need_ref, q_ref, k_ref, v_ref, do_ref, o_ref, low_ref, log_ref, dq_ref, dkv_ref, sums
):
    rows = q_ref.shape[0]
    key_total = k_ref.shape[0]
    sums[...] = jnp.zeros_like(sums)
    for index, r in enumerate(range(0, rows, QROWS)):
        rows_q = (slice(r, r + QROWS), slice(None))
        for key_count, chosen in key_windows(need_ref[index], key_total):

            @pl.when(chosen)
            def _():
                window = slice(key_total - key_count, key_total)
                allowed = peer_mask(key_count, low_ref[:, r : r + QROWS], key_count)
                logs = [log_ref[0, h : h + 1, r : r + QROWS] for h in range(LANES // HDIM)]
                d_query, d_key, d_value = backward_block(
                    q_ref[rows_q],
                    k_ref[window, :],
                    v_ref[window, :],
                    k_ref[window, :].T,
                    do_ref[rows_q],
                    output_product(do_ref, o_ref, rows_q),
                    logs,
                    allowed,
                )
                dq_ref[rows_q] = d_query.T
                sums[0, window] += d_key
                sums[1, window] += d_value

        @pl.when(need_ref[index] >= 0)
        def _():
            dq_ref[rows_q] = jnp.zeros((QROWS, LANES), F32)

    dkv_ref[...] = sums[...].astype(BF)


def peer_backward(need, q, kv, do, o, low_row, logs):
    rows, width = q.shape
    pairs = width // LANES
    return pl.pallas_call(
        peer_backward_kernel,
        name="peer_bwd",
        grid=(pairs,),
        out_shape=(
            jax.ShapeDtypeStruct((rows, width), F32),
            jax.ShapeDtypeStruct((2, rows, width), BF),
        ),
        in_specs=[
            SMEM_SPEC,
            pair_spec(rows),
            stacked_spec(rows, 0),
            stacked_spec(rows, 1),
            pair_spec(rows),
            pair_spec(rows),
            low_spec(rows),
            log_spec(rows),
        ],
        out_specs=(pair_spec(rows), pl.BlockSpec((2, rows, LANES), lambda i: (0, 0, i))),
        scratch_shapes=[pltpu.VMEM((2, rows, LANES), F32)],
        compiler_params=pltpu.CompilerParams(vmem_limit_bytes=VMEM_BYTES),
        cost_estimate=LIGHT,
    )(need, q, kv, kv, do, o, low_row, logs)


def own_backward_kernel(
    q_ref,
    k_ref,
    v_ref,
    do_ref,
    o_ref,
    low_ref,
    log_ref,
    dq_in_ref,
    cos_ref,
    sin_ref,
    dq_ref,
    dk_ref,
    dv_ref,
    sums,
):
    rows = q_ref.shape[0]
    sums[...] = jnp.zeros_like(sums)
    k_t = k_ref[...].T
    for r in range(0, rows, QROWS):
        count = r + QROWS
        window = (slice(r, r + QROWS), slice(None))
        allowed = own_mask(count, r, low_ref[:, r : r + QROWS])
        logs = [log_ref[0, h : h + 1, r : r + QROWS] for h in range(LANES // HDIM)]
        d_query, d_key, d_value = backward_block(
            q_ref[window],
            k_ref[0:count, :],
            v_ref[0:count, :],
            k_t[:, 0:count],
            do_ref[window],
            output_product(do_ref, o_ref, window),
            logs,
            allowed,
        )
        rotated = (d_query.T + dq_in_ref[window]) * (HDIM**-0.5)
        turned = rotated * cos_ref[window] - swap_halves(rotated) * sin_ref[window]
        dq_ref[window] = turned.astype(BF)
        sums[0, 0:count] += d_key
        sums[1, 0:count] += d_value
    dk_ref[...] = sums[0]
    dv_ref[...] = sums[1]


def own_backward(q, kv, do, o, low_row, logs, dq_in, cos, sin):
    rows, width = q.shape
    pairs = width // LANES
    table = pl.BlockSpec((rows, LANES), lambda i: (0, 0))
    return pl.pallas_call(
        own_backward_kernel,
        name="own_bwd",
        grid=(pairs,),
        out_shape=(
            jax.ShapeDtypeStruct((rows, width), BF),
            jax.ShapeDtypeStruct((rows, width), F32),
            jax.ShapeDtypeStruct((rows, width), F32),
        ),
        in_specs=[
            pair_spec(rows),
            stacked_spec(rows, 0),
            stacked_spec(rows, 1),
            pair_spec(rows),
            pair_spec(rows),
            low_spec(rows),
            log_spec(rows),
            pair_spec(rows),
            table,
            table,
        ],
        out_specs=(pair_spec(rows),) * 3,
        scratch_shapes=[pltpu.VMEM((2, rows, LANES), F32)],
        compiler_params=pltpu.CompilerParams(vmem_limit_bytes=VMEM_BYTES),
        cost_estimate=LIGHT,
    )(q, kv, kv, do, o, low_row, logs, dq_in, cos, sin)


def finish_keys_kernel(dk_ref, dv_ref, dk_in_ref, dv_in_ref, cos_ref, sin_ref, dk_out, dv_out):
    total = dk_ref[...] + dk_in_ref[...].astype(F32)
    turned = total * cos_ref[...] - swap_halves(total) * sin_ref[...]
    dk_out[...] = turned.astype(BF)
    dv_out[...] = (dv_ref[...] + dv_in_ref[...].astype(F32)).astype(BF)


def finish_keys(dk, dv, dkv_in, cos, sin):
    rows, width = dk.shape
    pairs = width // LANES
    table = pl.BlockSpec((rows, LANES), lambda i: (0, 0))
    return pl.pallas_call(
        finish_keys_kernel,
        name="finish_keys",
        grid=(pairs,),
        out_shape=(jax.ShapeDtypeStruct((rows, width), BF),) * 2,
        in_specs=[pair_spec(rows), pair_spec(rows), stacked_spec(rows, 0), stacked_spec(rows, 1)]
        + [table, table],
        out_specs=(pair_spec(rows),) * 2,
        cost_estimate=LIGHT,
    )(dk, dv, dkv_in, dkv_in, cos, sin)


def branch_kernel(stream_ref, att_ref, gain_ref, *refs):
    pieces, (hidden_ref, normed_ref, scale_ref) = refs[:4], refs[4:]
    for j, piece in enumerate(pieces):
        columns = piece_columns(j, piece.shape[1])
        term = dotf(att_ref[...], piece[...], NN)
        hidden_ref[:, columns] = stream_ref[:, columns].astype(F32) + term
    hidden = hidden_ref[...]
    mean = jnp.sum(hidden * hidden, axis=1, keepdims=True) / hidden.shape[1]
    scale = lax.rsqrt(mean + norm_eps)
    scale_ref[...] = scale
    normed_ref[...] = (hidden * scale * gain_ref[...]).astype(BF)


def add_branch(stream, att, gain, pieces):
    rows, depth = stream.shape
    heads = att.shape[1]
    tile = pl.BlockSpec((QROWS, depth), lambda i: (i, 0))
    return pl.pallas_call(
        branch_kernel,
        name="branch",
        grid=(rows // QROWS,),
        out_shape=(
            jax.ShapeDtypeStruct((rows, depth), F32),
            jax.ShapeDtypeStruct((rows, depth), BF),
            jax.ShapeDtypeStruct((rows, 1), F32),
        ),
        in_specs=[
            tile,
            pl.BlockSpec((QROWS, heads), lambda i: (i, 0)),
            pl.BlockSpec((1, depth), lambda i: (0, 0)),
        ]
        + [pl.BlockSpec(pieces[0].shape, lambda i: (0, 0))] * 4,
        out_specs=(tile, tile, pl.BlockSpec((QROWS, 1), lambda i: (i, 0))),
        compiler_params=pltpu.CompilerParams(vmem_limit_bytes=VMEM_BYTES),
        cost_estimate=LIGHT,
    )(stream, att, gain, *pieces)


def hidden_kernel(x_ref, *refs):
    w_in, (act_ref, by_gate_ref, by_up_ref) = refs[:4], refs[4:]
    rows = x_ref.shape[0]
    for r in range(0, rows, rows):
        part = slice(r, r + rows)
        gate = piece_dot(x_ref, part, [piece[0] for piece in w_in])
        up = piece_dot(x_ref, part, [piece[1] for piece in w_in])
        sig = jax.nn.sigmoid(gate)
        silu = gate * sig
        act_ref[part, :] = (silu * up).astype(BF)
        by_gate_ref[part, :] = (up * sig * (1.0 + gate * (1.0 - sig))).astype(BF)
        by_up_ref[part, :] = silu.astype(BF)


def hidden_units(x, w_in):
    rows, depth = x.shape
    _, size, units = w_in[0].shape
    tile = 256
    part = pl.BlockSpec((rows, tile), lambda i: (0, i))
    return pl.pallas_call(
        hidden_kernel,
        grid=(units // tile,),
        out_shape=(jax.ShapeDtypeStruct((rows, units), BF),) * 3,
        in_specs=[pl.BlockSpec((rows, depth), lambda i: (0, 0))]
        + [pl.BlockSpec((2, size, tile), lambda i: (0, 0, i))] * 4,
        out_specs=(part,) * 3,
        compiler_params=pltpu.CompilerParams(vmem_limit_bytes=VMEM_BYTES),
        cost_estimate=LIGHT,
        name="hidden",
    )(x, *w_in)


def hidden_back_kernel(cot_ref, by_gate_ref, by_up_ref, *refs):
    w_down, (dg_ref, du_ref) = refs[:4], refs[4:]
    rows = cot_ref.shape[0]
    for r in range(0, rows, rows):
        part = slice(r, r + rows)
        d_act = piece_dot(cot_ref, part, [piece[...] for piece in w_down], NT)
        dg_ref[part, :] = (d_act * by_gate_ref[part, :].astype(F32)).astype(BF)
        du_ref[part, :] = (d_act * by_up_ref[part, :].astype(F32)).astype(BF)


def hidden_back(cot, by_gate, by_up, w_down):
    rows, depth = cot.shape
    units, size = w_down[0].shape
    tile = 256
    part = pl.BlockSpec((rows, tile), lambda i: (0, i))
    return pl.pallas_call(
        hidden_back_kernel,
        grid=(units // tile,),
        out_shape=(jax.ShapeDtypeStruct((rows, units), BF),) * 2,
        in_specs=[pl.BlockSpec((rows, depth), lambda i: (0, 0)), part, part]
        + [pl.BlockSpec((tile, size), lambda i: (i, 0))] * 4,
        out_specs=(part,) * 2,
        compiler_params=pltpu.CompilerParams(vmem_limit_bytes=VMEM_BYTES),
        cost_estimate=LIGHT,
        name="hidden_back",
    )(cot, by_gate, by_up, *w_down)


def phased(i, block, make_index, tiles):
    def index_map(j, t):
        return make_index(jnp.where(j < i, 0, jnp.where(j == i, t, tiles - 1)))

    return pl.BlockSpec(block, index_map)


def columns_call(kernel_dot, lefts, pieces, block, make_index, size, flops, name):
    rows = lefts[0].shape[0]
    tile = min(size, 256)
    tiles = size // tile
    depth = size * 4

    def kernel(*refs):
        left_refs, piece_refs, out_ref = refs[: len(lefts)], refs[len(lefts) : -1], refs[-1]
        for j, piece in enumerate(piece_refs):

            @pl.when(pl.program_id(0) == j)
            def _():
                out_ref[...] = kernel_dot([left[...] for left in left_refs], piece).astype(BF)

    def out_index(j, t):
        return (0, (lax.axis_index("fsdp") ^ j) * tiles + t)

    return pl.pallas_call(
        kernel,
        grid=(4, tiles),
        out_shape=jax.ShapeDtypeStruct((rows, depth), BF),
        in_specs=[pl.BlockSpec(left.shape, lambda j, t: (0, 0)) for left in lefts]
        + [phased(i, block(tile), make_index, tiles) for i in range(4)],
        out_specs=pl.BlockSpec((rows, tile), out_index),
        compiler_params=pltpu.CompilerParams(vmem_limit_bytes=VMEM_BYTES),
        cost_estimate=LIGHT,
        name=name,
    )(*lefts, *pieces)


def stacked_columns(lefts, pieces, name):
    count, size, inner = pieces[0].shape

    def product(parts, piece):
        return sum(dotf(parts[c], piece[c], NT) for c in range(count))

    return columns_call(
        product,
        lefts,
        pieces,
        lambda tile: (count, tile, inner),
        lambda t: (0, t, 0),
        size,
        8 * lefts[0].shape[0] * size * inner * count,
        name,
    )


def plain_columns(left, pieces, name):
    inner, size = pieces[0].shape
    return columns_call(
        lambda parts, piece: dotf(parts[0], piece[...], NN),
        [left],
        pieces,
        lambda tile: (inner, tile),
        lambda t: (0, t),
        size,
        8 * left.shape[0] * size * inner,
        name,
    )


def branch_back_kernel(shares, d_mid_ref, hidden_ref, cot_ref, scale_ref, gain_ref, *refs):
    pieces, (d_hidden_ref, d_att_ref, gain_out_ref) = refs[:4], refs[4:7]
    d_mid = d_mid_ref[...].astype(F32)
    hidden = hidden_ref[...]
    scale = scale_ref[...]
    weighted = d_mid * gain_ref[...]
    inner = jnp.sum(weighted * hidden, axis=1, keepdims=True) / hidden.shape[1]
    d_hidden = (
        cot_ref[...].astype(F32) * (1.0 / shares)
        + scale * weighted
        - hidden * (scale * scale * scale * inner)
    )
    gain_term = jnp.sum(d_mid * hidden * scale, axis=0, keepdims=True)

    @pl.when(pl.program_id(0) == 0)
    def _():
        gain_out_ref[...] = gain_term

    @pl.when(pl.program_id(0) != 0)
    def _():
        gain_out_ref[...] += gain_term

    d_hidden_ref[...] = d_hidden.astype(BF)
    heads = d_att_ref.shape[1]
    for e in range(0, heads, 512):
        columns = slice(e, e + 512)
        d_att_ref[:, columns] = piece_dot(
            d_hidden_ref, slice(None), [piece[columns, :] for piece in pieces], NT
        ).astype(BF)


def branch_back(d_mid, hidden, cot, scale, gain, pieces):
    rows, depth = hidden.shape
    heads, size = pieces[0].shape
    tile = pl.BlockSpec((QROWS, depth), lambda i: (i, 0))
    row = pl.BlockSpec((1, depth), lambda i: (0, 0))
    return pl.pallas_call(
        functools.partial(branch_back_kernel, lax.axis_size("tensor")),
        name="branch_back",
        grid=(rows // QROWS,),
        in_specs=[tile, tile, tile, pl.BlockSpec((QROWS, 1), lambda i: (i, 0)), row]
        + [pl.BlockSpec((heads, size), lambda i: (0, 0))] * 4,
        out_specs=(tile, pl.BlockSpec((QROWS, heads), lambda i: (i, 0)), row),
        out_shape=(
            jax.ShapeDtypeStruct((rows, depth), BF),
            jax.ShapeDtypeStruct((rows, heads), BF),
            jax.ShapeDtypeStruct((1, depth), F32),
        ),
        compiler_params=pltpu.CompilerParams(vmem_limit_bytes=VMEM_BYTES),
        cost_estimate=LIGHT,
    )(d_mid, hidden, cot, scale, gain, *pieces)


def grad_call(left, right, cut, place, adds, name, span=(0, 1)):
    rows = left.shape[0]
    size = (left, right)[cut].shape[1] // 4
    swept = (right, left)[cut].shape[1] // span[1]
    height, width = (size, swept) if cut == 0 else (swept, size)
    tile = min(1024, swept)
    offset = span[0] * (swept // tile)
    block = (height, tile) if cut == 0 else (tile, width)

    def owner():
        return lax.axis_index("fsdp") ^ place

    def swept_index(t):
        return (0, t) if cut == 0 else (t, 0)

    def kernel(left_ref, right_ref, *refs):
        add_refs, out_ref = refs[: len(adds)], refs[len(adds)]
        if cut == 0:
            turned = refs[-1]

            @pl.when(pl.program_id(0) == 0)
            def _():
                turned[...] = left_ref[...].T

            result = dotf(turned[...], right_ref[...], NN)
        else:
            result = dotf(left_ref[...].T, right_ref[...], NN)
        for add in add_refs:
            result = result + add[...].astype(F32)
        out_ref[...] = result.astype(BF)

    fixed = pl.BlockSpec((rows, size), lambda t: (0, owner()))
    moving = pl.BlockSpec((rows, tile), lambda t: (0, t + offset))
    return pl.pallas_call(
        kernel,
        grid=(swept // tile,),
        out_shape=jax.ShapeDtypeStruct((height, width), BF),
        in_specs=[fixed, moving] * (cut == 0)
        + [moving, fixed] * (cut == 1)
        + [pl.BlockSpec(block, swept_index)] * len(adds),
        out_specs=pl.BlockSpec(block, swept_index),
        scratch_shapes=[pltpu.VMEM((size, rows), BF)] if cut == 0 else [],
        compiler_params=pltpu.CompilerParams(vmem_limit_bytes=VMEM_BYTES),
        cost_estimate=LIGHT,
        name=name,
    )(left, right, *adds)


class Reduction:
    def __init__(self, left, right, cut, name, span=(0, 1)):
        self.args, self.name, self.span = (left, right, cut), name, span

    def call(self, place, deps, step, adds=()):
        left, right, cut = self.args
        left = after(left, *deps) if deps else left
        return grad_call(left, right, cut, place, adds, self.name + step, self.span)

    def near_far(self, *deps):
        self.three = self.call(3, deps, "_3")
        self.for_two = swap(self.three, "fsdp", 1)

    def near(self, *deps):
        self.one = self.call(1, deps, "_1")
        self.for_own = swap(self.one, "fsdp", 1)

    def far(self, *deps):
        self.two = self.call(2, deps, "_2", [self.for_two])

    def send_far(self, *deps):
        self.across = swap(after(self.two, *deps), "fsdp", 2)

    def mine(self, *deps):
        self.own = self.call(0, deps, "_0", [self.for_own, self.across])

    def send_context(self, *deps):
        self.other = swap(after(self.own, *deps), "context", 1)


def totals_kernel(slots, *refs):
    pairs, out_ref = refs[:-1], refs[-1]
    for slot in range(len(pairs) // 2):
        total = pairs[2 * slot][...].astype(F32) + pairs[2 * slot + 1][...].astype(F32)
        if slots == 0:
            out_ref[slot] = total
        else:
            out_ref[:, slot, :] = total


def totals(sums, slots, *deps):
    arrays = [array for part in sums for array in (part.own, part.other)]
    if deps:
        arrays[0] = after(arrays[0], *deps)
    rows, width = arrays[0].shape
    tile = 128
    shape = [rows, width]
    shape.insert(slots, len(sums))
    block = [tile, width]
    block.insert(slots, len(sums))
    return pl.pallas_call(
        functools.partial(totals_kernel, slots),
        grid=(rows // tile,),
        out_shape=jax.ShapeDtypeStruct(tuple(shape), F32),
        in_specs=[pl.BlockSpec((tile, width), lambda i: (i, 0))] * len(arrays),
        out_specs=pl.BlockSpec(
            tuple(block), (lambda i: (0, i, 0)) if slots == 0 else (lambda i: (i, 0, 0))
        ),
        compiler_params=pltpu.CompilerParams(vmem_limit_bytes=VMEM_BYTES),
        cost_estimate=LIGHT,
        name="totals",
    )(*arrays)


def row_sum(values_in):
    return jnp.sum(values_in, axis=1, keepdims=True)


def per_device(tokens, w_qkv, w_out, w_gate_up, w_down, gains, seq_lengths, cotangent):
    row_count, part_width = tokens.shape
    tensor_index = lax.axis_index("tensor")
    context_index = lax.axis_index("context")
    full_width = part_width * lax.axis_size("tensor")

    def features(part_in):
        return lax.all_gather(part_in, "tensor", axis=1, tiled=True)

    def feature_sum(term):
        return lax.psum_scatter(term.astype(BF), "tensor", scatter_dimension=1, tiled=True)

    def own_features(full):
        return lax.dynamic_slice_in_dim(full, tensor_index * part_width, part_width, 1)

    ending = jnp.cumsum(seq_lengths[0])
    starts = ending - seq_lengths[0]
    places = context_index * row_count + jnp.arange(row_count, dtype=jnp.int32)
    first_token = jnp.max(jnp.where(starts[None, :] <= places[:, None], starts[None, :], 0), axis=1)
    cos, sin = rope_tables(places - first_token)
    low = first_token - context_index * row_count
    low_row = low[None, :]
    need = low[::QROWS]

    token_low = features(tokens)
    gain_near, gain_full = gather_gains(gains)
    gain_attn, gain_mlp = gain_full[0:1], gain_full[1:2]

    qkv_own = jnp.swapaxes(w_qkv, 0, 1)
    half = qkv_own.shape[1] // 2
    far_half = swap(
        lax.dynamic_slice_in_dim(after(qkv_own, gain_near), context_index * half, half, 1),
        "fsdp",
        2,
    )
    other_half = swap(far_half, "context", 1)
    qkv_far = jnp.where(
        context_index == 0,
        jnp.concatenate([far_half, other_half], axis=1),
        jnp.concatenate([other_half, far_half], axis=1),
    )
    qkv_near = swap(qkv_own, "fsdp", 1)
    qkv = (qkv_own, qkv_near, qkv_far, swap(qkv_far, "fsdp", 1))

    gate_up_own = jnp.swapaxes(w_gate_up, 0, 1)
    cut = gate_up_own.shape[1] * 12 // 32
    gate_up_a = swap(after(gate_up_own[:, :cut], far_half), "fsdp", 2)
    gate_up_b = swap(after(gate_up_own[:, cut:], gate_up_a), "fsdp", 2)

    keys_values, normed_in, scale_attn = project(
        after(token_low, gate_up_a), qkv, cos, sin, gain_attn, (1.0, None), 1, True
    )
    peer_kv = lax.ppermute(keys_values, "context", [(0, 1)])
    queries = project(normed_in, qkv, cos, sin, gain_attn, (HDIM**-0.5,), 0, False)[0][0]
    part, part_log = own_forward(queries, keys_values, low_row)
    attended, logs = peer_forward(
        need, queries, peer_kv, low_row, after(part, gate_up_b), part_log
    )
    attended_full = features(attended)

    out_own = after(lax.all_gather(w_out, "tensor", axis=0, tiled=True), attended)
    out_near = swap(out_own, "fsdp", 1)
    out_far = swap(out_own, "fsdp", 2)
    out_far_near = swap(out_far, "fsdp", 1)
    out = (out_own, out_near, out_far, out_far_near)
    gate_up_own, gate_up_a, gate_up_b = lax.optimization_barrier(
        (gate_up_own, gate_up_a, gate_up_b, attended)
    )[:3]
    gate_up_far = jnp.concatenate([gate_up_a, gate_up_b], axis=1)
    gate_up_near = swap(gate_up_own, "fsdp", 1)
    gate_up = (gate_up_own, gate_up_near, gate_up_far, swap(gate_up_far, "fsdp", 1))
    cot_full = features(after(cotangent, attended_full, out_far_near, out_near))
    down_far = swap(after(w_down, attended_full, out_far_near), "fsdp", 2)
    down_near = swap(after(w_down, attended_full), "fsdp", 1)
    hidden, normed_mid, scale_mlp = add_branch(token_low, attended_full, gain_mlp, out)

    activated, by_gate, by_up = hidden_units(normed_mid, gate_up)
    down_far = after(down_far, activated)
    down = (w_down, down_near, down_far, swap(down_far, "fsdp", 1))
    mlp_term = plain_columns(activated, down, "mlp_out")
    mlp_out = feature_sum(mlp_term)
    d_gate, d_up = hidden_back(after(cot_full, mlp_term), by_gate, by_up, down)
    d_mid_term = stacked_columns([d_gate, d_up], gate_up, "d_mid")
    d_hidden_term, d_att_term, gain_mlp_term = branch_back(
        d_mid_term, hidden, cot_full, scale_mlp, gain_mlp, out
    )
    d_attended = feature_sum(after(d_att_term, mlp_out))
    d_hidden_own = feature_sum(after(d_hidden_term, d_att_term))

    down_a, down_b = (
        Reduction(activated, cot_full, 1, "grad_down", (part_index, 2)) for part_index in (0, 1)
    )
    grad_gate = Reduction(normed_mid, d_gate, 0, "grad_gate")
    grad_up = Reduction(normed_mid, d_up, 0, "grad_up")
    square = lax.axis_size("tensor") == lax.axis_size("fsdp")
    down_a.near_far(d_att_term)
    down_b.near_far(down_a.three)
    grad_gate.near_far(down_b.three)
    down_a.far(grad_gate.three)
    down_a.send_far()
    down_b.far(down_a.two)
    down_b.send_far()
    down_a.near(down_b.two)
    down_b.near(down_a.one)
    grad_gate.far(down_b.one)
    grad_gate.send_far()
    grad_gate.near(grad_gate.two)
    down_a.mine(grad_gate.one)
    down_a.send_context()
    grad_up.near_far(down_a.own)

    dq_peer, dkv_peer = peer_backward(
        need, queries, peer_kv, after(d_attended, grad_up.three), attended, low_row, logs
    )
    dkv_in = lax.ppermute(dkv_peer, "context", [(1, 0)])
    d_query, dk_own, dv_own = own_backward(
        queries, keys_values, d_attended, attended, low_row, logs, dq_peer, cos, sin
    )
    grad_query = Reduction(normed_in, d_query, 0, "grad_query")
    grad_up.near(d_query)
    grad_up.far(grad_up.one)
    grad_up.send_far()
    down_b.mine(grad_up.two, dkv_in)
    down_b.send_context()
    d_key, d_value = finish_keys(
        dk_own, dv_own, after(dkv_in, down_b.own, d_hidden_own), cos, sin
    )
    grad_gate.mine(d_value, down_a.other, down_b.other)
    grad_gate.send_context()
    grad_up.mine(grad_gate.own)
    grad_up.send_context()
    d_in_term = stacked_columns(
        [d_query, d_key, after(d_value, grad_up.own, grad_gate.other)], qkv, "d_in"
    )
    d_in = feature_sum(d_in_term).astype(F32)

    if square:
        grad_out = Reduction(attended_full, d_hidden_own, 0, "grad_out")
    else:
        grad_out = Reduction(attended, features(d_hidden_own), 1, "grad_out")
    grad_query.near_far(d_in_term)
    grad_query.near(grad_query.three)
    grad_key = Reduction(normed_in, d_key, 0, "grad_key")
    grad_value = Reduction(normed_in, d_value, 0, "grad_value")
    grad_query.far(grad_query.one)
    grad_query.send_far()
    grad_key.near_far(grad_query.two)
    grad_value.near_far(grad_key.three)
    grad_key.near(grad_value.three)
    grad_value.near(grad_key.one)
    grad_key.far(grad_value.one)
    grad_key.send_far()
    grad_value.far(grad_key.two)
    grad_value.send_far()
    grad_out.near_far(grad_value.two)
    grad_out.near(grad_out.three)
    grad_out.far(grad_out.one)
    grad_out.send_far()
    grad_query.mine(grad_out.two)
    grad_query.send_context()

    stream = token_low.astype(F32)
    d_in_wide = after(d_in_term, grad_query.own).astype(F32)
    weighted = d_in_wide * stream
    inner_term = jnp.sum(weighted * gain_attn, axis=1)
    gain_attn_term = jnp.sum(weighted * scale_attn, axis=0)
    parts = lax.axis_size("tensor")
    totals_small = block_totals(
        jnp.concatenate(
            [
                jnp.broadcast_to(inner_term[None, :], (parts, row_count)),
                gain_attn_term.reshape(parts, part_width),
                gain_mlp_term.reshape(parts, part_width),
            ],
            axis=1,
        )[None]
    )
    inner_in = totals_small[0, :row_count][:, None] / full_width
    gain_sums = totals_small[0, row_count:].reshape(2, part_width)
    gain_sums = exchange(gain_sums, "fsdp", 1)
    gain_sums = exchange(gain_sums, "fsdp", 2)
    gain_sums = exchange(gain_sums, "context", 1)
    gain_width = gains.shape[1]
    grad_gains = lax.dynamic_slice_in_dim(
        gain_sums, lax.axis_index("fsdp") * gain_width, gain_width, 1
    )

    grad_down_sum = totals([down_a, down_b], 0, d_in_wide).reshape(w_down.shape)
    grad_key.mine(grad_down_sum, grad_up.other)
    grad_key.send_context()
    grad_value.mine(grad_key.own)
    grad_value.send_context()
    grad_out.mine(grad_value.own)
    if square:
        count = lax.axis_size("fsdp")
        across = [(i, (i % count) * count + i // count) for i in range(count * count)]
        grad_out.own = lax.ppermute(grad_out.own, ("fsdp", "tensor"), across)
    grad_out.send_context()
    grad_gate_up_sum = totals([grad_gate, grad_up], 1, grad_value.own)
    grad_qkv = totals([grad_query, grad_key, grad_value], 0, grad_gate_up_sum)
    grad_out_sum = totals([grad_out], 0, grad_qkv)[0]

    block_out = (own_features(hidden) + mlp_out.astype(F32)).astype(BF)
    own_tokens = tokens.astype(F32)
    grad_tokens = (
        d_hidden_own.astype(F32)
        + scale_attn * own_features(gain_attn) * d_in
        - own_tokens * scale_attn * scale_attn * scale_attn * inner_in
    ).astype(BF)
    return (
        block_out,
        grad_tokens,
        jnp.swapaxes(grad_qkv, 0, 1),
        grad_out_sum,
        grad_gate_up_sum,
        grad_down_sum,
        grad_gains,
    )


def solution(mesh):
    rows = P(("fsdp", "context"), "tensor")
    inner = P("fsdp", None, "tensor")
    outer = P("tensor", "fsdp")
    gain = P(None, ("tensor", "fsdp"))
    return jax.shard_map(
        per_device,
        mesh=mesh,
        in_specs=(rows, inner, outer, inner, outer, gain, P("fsdp", None), rows),
        out_specs=(rows, rows, inner, outer, inner, outer, gain),
        check_vma=False,
    )
```

```python
import functools

import jax
import jax.numpy as jnp
from jax import lax
from jax.experimental import pallas as pl
from jax.experimental.pallas import tpu as pltpu
from jax.sharding import PartitionSpec as P

HDIM = 64
LANES = 128
QROWS = 256
norm_eps = 1e-05
rope_base = 130000.0
masked_score = -1e30
BF = jnp.bfloat16
F32 = jnp.float32
VMEM_BYTES = 56 * 1024 * 1024
LIGHT = pl.CostEstimate(flops=1, bytes_accessed=1, transcendentals=0)


def dotf(a, b, dims):
    return lax.dot_general(a, b, (dims, ((), ())), preferred_element_type=F32)


NN = ((1,), (0,))
NT = ((1,), (1,))
TN = ((0,), (0,))


def swap(value, axis, bit):
    count = lax.axis_size(axis)
    return lax.ppermute(value, axis, [(i, i ^ bit) for i in range(count)])


def after(value, *others):
    return lax.optimization_barrier((value, *others))[0]


def shifted(value, axis):
    count = lax.axis_size(axis)
    return [
        lax.ppermute(value, axis, [(i, (i + step) % count) for i in range(count)])
        for step in range(1, count)
    ]


def exchange(value, axis, bit):
    return value + swap(value, axis, bit)


def join_kernel(axis, mode, *refs):
    pieces, out_ref = refs[:-1], refs[-1]
    count = len(pieces)
    me = lax.axis_index(axis)
    for step, piece in enumerate(pieces):
        size = piece.shape[1]
        place = (me ^ step) if mode == "xor" else (me - step + count) % count
        out_ref[:, pl.ds(pl.multiple_of(place * size, size), size)] = piece[...]


def join(pieces, axis, mode):
    rows, size = pieces[0].shape
    return pl.pallas_call(
        functools.partial(join_kernel, axis, mode),
        out_shape=jax.ShapeDtypeStruct((rows, size * len(pieces)), pieces[0].dtype),
        cost_estimate=LIGHT,
        name="join",
    )(*pieces)


def gather_gains(gains):
    if lax.axis_size("tensor") > 4 or gains.shape[1] % LANES:
        whole = lax.all_gather(gains, ("tensor", "fsdp"), axis=1, tiled=True).astype(F32)
        return gains, whole
    own = gains.astype(F32)
    part = join([own] + [swap(own, "fsdp", bit) for bit in (1, 2, 3)], "fsdp", "xor")
    return part, join([part] + shifted(part, "tensor"), "tensor", "shift")


def block_totals(blocks):
    count = lax.axis_size("tensor")
    me = lax.axis_index("tensor")
    if count > 4:
        return lax.dynamic_index_in_dim(lax.psum(blocks, "tensor"), me, 1, keepdims=False)

    def pick(place):
        return lax.dynamic_index_in_dim(blocks, place, 1, keepdims=False)

    total = pick(me)
    for step in range(1, count):
        moves = [(i, (i + step) % count) for i in range(count)]
        total = total + lax.ppermute(pick((me + step) % count), "tensor", moves)
    return total


def piece_columns(j, size):
    return pl.ds(pl.multiple_of((lax.axis_index("fsdp") ^ j) * size, size), size)


def swap_halves(block):
    lane = lax.broadcasted_iota(jnp.int32, block.shape, 1)
    up = pltpu.roll(block, LANES - HDIM // 2, 1)
    down = pltpu.roll(block, HDIM // 2, 1)
    return jnp.where((lane & (HDIM - 1)) < HDIM // 2, up, down)


def rope_tables(positions):
    lane = jnp.arange(LANES, dtype=jnp.int32)
    half = lane % (HDIM // 2)
    frequencies = rope_base ** (-2.0 * half.astype(F32) / HDIM)
    angles = positions.astype(F32)[:, None] * frequencies[None, :]
    sign = jnp.where((lane % HDIM) < HDIM // 2, -1.0, 1.0)
    return jnp.cos(angles), jnp.sin(angles) * sign[None, :]


def piece_dot(x_ref, rows, pieces, dims=NN):
    total = None
    for j, piece in enumerate(pieces):
        size = piece.shape[dims[1][0]]
        term = dotf(x_ref[rows, piece_columns(j, size)], piece, dims)
        total = term if total is None else total + term
    return total


def project_kernel(kinds, normalize, x_ref, *refs):
    pieces, (cos_ref, sin_ref, gain_ref), outs = refs[:4], refs[4:7], refs[7:]
    out_ref = outs[0]
    rows, width = out_ref.shape[1:]
    step = pl.program_id(0)
    if normalize:
        normed_ref, scale_ref = outs[1], outs[2]

        @pl.when(step == 0)
        def _():
            for r in range(0, rows, QROWS):
                part = slice(r, r + QROWS)
                stream = x_ref[part, :].astype(F32)
                mean = jnp.sum(stream * stream, axis=1, keepdims=True) / x_ref.shape[1]
                scale = lax.rsqrt(mean + norm_eps)
                scale_ref[part, :] = scale
                normed_ref[part, :] = (stream * scale * gain_ref[...]).astype(BF)

        x_ref = normed_ref
    for index, scale in enumerate(kinds):

        @pl.when(step == index)
        def _():
            for r in range(0, rows, rows):
                part = slice(r, r + rows)
                result = piece_dot(x_ref, part, [piece[0] for piece in pieces])
                for c in range(0, width, LANES):
                    block = result[:, c : c + LANES]
                    if scale:
                        block = block * cos_ref[part, :] + swap_halves(block) * sin_ref[part, :]
                    low = block.astype(BF)
                    if scale and scale != 1.0:
                        low = low * jnp.asarray(scale, BF)
                    out_ref[0, part, c : c + LANES] = low


def project(x, pieces, cos, sin, gain, kinds, first, normalize):
    rows, depth = x.shape
    _, size, width = pieces[0].shape
    flops = 2 * len(kinds) * rows * depth * width
    whole = pl.BlockSpec((rows, depth), lambda i: (0, 0))
    table = pl.BlockSpec((rows, LANES), lambda i: (0, 0))
    out_shape = [jax.ShapeDtypeStruct((len(kinds), rows, width), BF)]
    out_specs = [pl.BlockSpec((1, rows, width), lambda i: (i, 0, 0))]
    if normalize:
        out_shape += [jax.ShapeDtypeStruct((rows, depth), BF), jax.ShapeDtypeStruct((rows, 1), F32)]
        out_specs += [whole, pl.BlockSpec((rows, 1), lambda i: (0, 0))]
    return pl.pallas_call(
        functools.partial(project_kernel, kinds, normalize),
        name="project_kv" if normalize else "project_q",
        grid=(len(kinds),),
        out_shape=out_shape,
        in_specs=[whole]
        + [pl.BlockSpec((1, size, width), lambda i: (i + first, 0, 0))] * 4
        + [table, table, pl.BlockSpec((1, depth), lambda i: (0, 0))],
        out_specs=out_specs,
        compiler_params=pltpu.CompilerParams(vmem_limit_bytes=VMEM_BYTES),
        cost_estimate=LIGHT,
    )(x, *pieces, cos, sin, gain)


def head_mask(block, head):
    lane = lax.broadcasted_iota(jnp.int32, block.shape, 1)
    inside = (lane < HDIM) if head == 0 else (lane >= HDIM)
    return jnp.where(inside, block, jnp.zeros_like(block))


def own_mask(key_count, row0, low_row):
    key = lax.broadcasted_iota(jnp.int32, (key_count, QROWS), 0)
    query = row0 + lax.broadcasted_iota(jnp.int32, (key_count, QROWS), 1)
    return (key >= low_row) & (key <= query)


def peer_mask(key_count, low_row, offset):
    key = lax.broadcasted_iota(jnp.int32, (key_count, QROWS), 0) - offset
    return key >= low_row


def key_windows(need, total):
    counts = list(range(QROWS, total + 1, QROWS))
    for place, count in enumerate(counts):
        chosen = need < 0 if place == 0 else need < -counts[place - 1]
        if count < total:
            chosen = jnp.logical_and(chosen, need >= -count)
        yield count, chosen


def own_forward_kernel(q_ref, k_ref, v_ref, low_ref, out_ref, log_ref):
    rows = q_ref.shape[0]
    v_t = v_ref[...].T
    for r in range(0, rows, QROWS):
        count = r + QROWS
        allowed = own_mask(count, r, low_ref[:, r : r + QROWS])
        keys = k_ref[0:count, :]
        outs = []
        for head in range(LANES // HDIM):
            scores = dotf(keys, head_mask(q_ref[r : r + QROWS, :], head), NT)
            scores = jnp.where(allowed, scores, masked_score)
            peak = jnp.max(scores, axis=0, keepdims=True)
            weights = jnp.exp(scores - peak)
            total = jnp.sum(weights, axis=0, keepdims=True)
            part = dotf(v_t[head * HDIM : (head + 1) * HDIM, 0:count], weights.astype(BF), NN)
            outs.append(part / total)
            log_ref[0, head : head + 1, r : r + QROWS] = peak + jnp.log(total)
        out_ref[r : r + QROWS, :] = jnp.concatenate(outs, axis=0).T


def peer_forward_kernel(
    need_ref, q_ref, k_ref, v_ref, low_ref, part_ref, log_in_ref, out_ref, log_ref
):
    rows = q_ref.shape[0]
    key_total = k_ref.shape[0]
    for index, r in enumerate(range(0, rows, QROWS)):
        for key_count, chosen in key_windows(need_ref[index], key_total):

            @pl.when(chosen)
            def _():
                window = slice(key_total - key_count, key_total)
                v_t = v_ref[window, :].T
                allowed = peer_mask(key_count, low_ref[:, r : r + QROWS], key_count)
                before = part_ref[r : r + QROWS, :].T
                outs = []
                for head in range(LANES // HDIM):
                    scores = dotf(k_ref[window, :], head_mask(q_ref[r : r + QROWS, :], head), NT)
                    scores = jnp.where(allowed, scores, masked_score)
                    log_own = log_in_ref[0, head : head + 1, r : r + QROWS]
                    peak = jnp.maximum(jnp.max(scores, axis=0, keepdims=True), log_own)
                    weights = jnp.exp(scores - peak)
                    own_weight = jnp.exp(log_own - peak)
                    total = jnp.sum(weights, axis=0, keepdims=True) + own_weight
                    rows_h = slice(head * HDIM, (head + 1) * HDIM)
                    part = dotf(v_t[rows_h, :], weights.astype(BF), NN)
                    outs.append((part + before[rows_h, :] * own_weight) / total)
                    log_ref[0, head : head + 1, r : r + QROWS] = peak + jnp.log(total)
                out_ref[r : r + QROWS, :] = jnp.concatenate(outs, axis=0).T.astype(BF)

        @pl.when(need_ref[index] >= 0)
        def _():
            out_ref[r : r + QROWS, :] = part_ref[r : r + QROWS, :].astype(BF)
            log_ref[:, :, r : r + QROWS] = log_in_ref[:, :, r : r + QROWS]


def pair_spec(rows):
    return pl.BlockSpec((rows, LANES), lambda i: (0, i))


def stacked_spec(rows, part):
    return pl.BlockSpec((None, rows, LANES), lambda i: (part, 0, i))


def log_spec(rows):
    return pl.BlockSpec((1, LANES // HDIM, rows), lambda i: (i, 0, 0))


def low_spec(rows):
    return pl.BlockSpec((1, rows), lambda i: (0, 0))


def own_forward(q, kv, low_row):
    rows, width = q.shape
    pairs = width // LANES
    return pl.pallas_call(
        own_forward_kernel,
        name="own_fwd",
        grid=(pairs,),
        out_shape=(
            jax.ShapeDtypeStruct((rows, width), F32),
            jax.ShapeDtypeStruct((pairs, LANES // HDIM, rows), F32),
        ),
        in_specs=[
            pair_spec(rows),
            stacked_spec(rows, 0),
            stacked_spec(rows, 1),
            low_spec(rows),
        ],
        out_specs=(pair_spec(rows), log_spec(rows)),
        compiler_params=pltpu.CompilerParams(vmem_limit_bytes=VMEM_BYTES),
        cost_estimate=LIGHT,
    )(q, kv, kv, low_row)


SMEM_SPEC = pl.BlockSpec(memory_space=pltpu.SMEM)


def peer_forward(need, q, kv, low_row, part, log_in):
    rows, width = q.shape
    pairs = width // LANES
    return pl.pallas_call(
        peer_forward_kernel,
        name="peer_fwd",
        grid=(pairs,),
        out_shape=(
            jax.ShapeDtypeStruct((rows, width), BF),
            jax.ShapeDtypeStruct((pairs, LANES // HDIM, rows), F32),
        ),
        in_specs=[
            SMEM_SPEC,
            pair_spec(rows),
            stacked_spec(rows, 0),
            stacked_spec(rows, 1),
            low_spec(rows),
            pair_spec(rows),
            log_spec(rows),
        ],
        out_specs=(pair_spec(rows), log_spec(rows)),
        compiler_params=pltpu.CompilerParams(vmem_limit_bytes=VMEM_BYTES),
        cost_estimate=LIGHT,
    )(need, q, kv, kv, low_row, part, log_in)


def backward_block(q_rows, k_rows, v_rows, k_t, do_rows, do_o_t, logs, allowed):
    d_query, d_key, d_value = [], None, None
    for head in range(LANES // HDIM):
        rows_h = slice(head * HDIM, (head + 1) * HDIM)
        q_head = head_mask(q_rows, head)
        do_head = head_mask(do_rows, head)
        scores = dotf(k_rows, q_head, NT)
        probs = jnp.exp(jnp.where(allowed, scores, masked_score) - logs[head])
        delta = jnp.sum(do_o_t[rows_h, :], axis=0, keepdims=True)
        d_probs = dotf(v_rows, do_head, NT)
        d_scores = (probs * (d_probs - delta)).astype(BF)
        d_v = dotf(probs.astype(BF), do_head, NN)
        d_k = dotf(d_scores, q_head, NN)
        d_value = d_v if d_value is None else d_value + d_v
        d_key = d_k if d_key is None else d_key + d_k
        d_query.append(dotf(k_t[rows_h, :], d_scores, NN))
    return jnp.concatenate(d_query, axis=0), d_key, d_value


def output_product(do_ref, o_ref, window):
    product = do_ref[window].astype(F32) * o_ref[window].astype(F32)
    return product.T


def peer_backward_kernel(
    need_ref, q_ref, k_ref, v_ref, do_ref, o_ref, low_ref, log_ref, dq_ref, dkv_ref, sums
):
    rows = q_ref.shape[0]
    key_total = k_ref.shape[0]
    sums[...] = jnp.zeros_like(sums)
    for index, r in enumerate(range(0, rows, QROWS)):
        rows_q = (slice(r, r + QROWS), slice(None))
        for key_count, chosen in key_windows(need_ref[index], key_total):

            @pl.when(chosen)
            def _():
                window = slice(key_total - key_count, key_total)
                allowed = peer_mask(key_count, low_ref[:, r : r + QROWS], key_count)
                logs = [log_ref[0, h : h + 1, r : r + QROWS] for h in range(LANES // HDIM)]
                d_query, d_key, d_value = backward_block(
                    q_ref[rows_q],
                    k_ref[window, :],
                    v_ref[window, :],
                    k_ref[window, :].T,
                    do_ref[rows_q],
                    output_product(do_ref, o_ref, rows_q),
                    logs,
                    allowed,
                )
                dq_ref[rows_q] = d_query.T
                sums[0, window] += d_key
                sums[1, window] += d_value

        @pl.when(need_ref[index] >= 0)
        def _():
            dq_ref[rows_q] = jnp.zeros((QROWS, LANES), F32)

    dkv_ref[...] = sums[...].astype(BF)


def peer_backward(need, q, kv, do, o, low_row, logs):
    rows, width = q.shape
    pairs = width // LANES
    return pl.pallas_call(
        peer_backward_kernel,
        name="peer_bwd",
        grid=(pairs,),
        out_shape=(
            jax.ShapeDtypeStruct((rows, width), F32),
            jax.ShapeDtypeStruct((2, rows, width), BF),
        ),
        in_specs=[
            SMEM_SPEC,
            pair_spec(rows),
            stacked_spec(rows, 0),
            stacked_spec(rows, 1),
            pair_spec(rows),
            pair_spec(rows),
            low_spec(rows),
            log_spec(rows),
        ],
        out_specs=(pair_spec(rows), pl.BlockSpec((2, rows, LANES), lambda i: (0, 0, i))),
        scratch_shapes=[pltpu.VMEM((2, rows, LANES), F32)],
        compiler_params=pltpu.CompilerParams(vmem_limit_bytes=VMEM_BYTES),
        cost_estimate=LIGHT,
    )(need, q, kv, kv, do, o, low_row, logs)


def own_backward_kernel(
    q_ref,
    k_ref,
    v_ref,
    do_ref,
    o_ref,
    low_ref,
    log_ref,
    dq_in_ref,
    cos_ref,
    sin_ref,
    dq_ref,
    dk_ref,
    dv_ref,
    sums,
):
    rows = q_ref.shape[0]
    sums[...] = jnp.zeros_like(sums)
    k_t = k_ref[...].T
    for r in range(0, rows, QROWS):
        count = r + QROWS
        window = (slice(r, r + QROWS), slice(None))
        allowed = own_mask(count, r, low_ref[:, r : r + QROWS])
        logs = [log_ref[0, h : h + 1, r : r + QROWS] for h in range(LANES // HDIM)]
        d_query, d_key, d_value = backward_block(
            q_ref[window],
            k_ref[0:count, :],
            v_ref[0:count, :],
            k_t[:, 0:count],
            do_ref[window],
            output_product(do_ref, o_ref, window),
            logs,
            allowed,
        )
        rotated = (d_query.T + dq_in_ref[window]) * (HDIM**-0.5)
        turned = rotated * cos_ref[window] - swap_halves(rotated) * sin_ref[window]
        dq_ref[window] = turned.astype(BF)
        sums[0, 0:count] += d_key
        sums[1, 0:count] += d_value
    dk_ref[...] = sums[0]
    dv_ref[...] = sums[1]


def own_backward(q, kv, do, o, low_row, logs, dq_in, cos, sin):
    rows, width = q.shape
    pairs = width // LANES
    table = pl.BlockSpec((rows, LANES), lambda i: (0, 0))
    return pl.pallas_call(
        own_backward_kernel,
        name="own_bwd",
        grid=(pairs,),
        out_shape=(
            jax.ShapeDtypeStruct((rows, width), BF),
            jax.ShapeDtypeStruct((rows, width), F32),
            jax.ShapeDtypeStruct((rows, width), F32),
        ),
        in_specs=[
            pair_spec(rows),
            stacked_spec(rows, 0),
            stacked_spec(rows, 1),
            pair_spec(rows),
            pair_spec(rows),
            low_spec(rows),
            log_spec(rows),
            pair_spec(rows),
            table,
            table,
        ],
        out_specs=(pair_spec(rows),) * 3,
        scratch_shapes=[pltpu.VMEM((2, rows, LANES), F32)],
        compiler_params=pltpu.CompilerParams(vmem_limit_bytes=VMEM_BYTES),
        cost_estimate=LIGHT,
    )(q, kv, kv, do, o, low_row, logs, dq_in, cos, sin)


def finish_keys_kernel(dk_ref, dv_ref, dk_in_ref, dv_in_ref, cos_ref, sin_ref, dk_out, dv_out):
    total = dk_ref[...] + dk_in_ref[...].astype(F32)
    turned = total * cos_ref[...] - swap_halves(total) * sin_ref[...]
    dk_out[...] = turned.astype(BF)
    dv_out[...] = (dv_ref[...] + dv_in_ref[...].astype(F32)).astype(BF)


def finish_keys(dk, dv, dkv_in, cos, sin):
    rows, width = dk.shape
    pairs = width // LANES
    table = pl.BlockSpec((rows, LANES), lambda i: (0, 0))
    return pl.pallas_call(
        finish_keys_kernel,
        name="finish_keys",
        grid=(pairs,),
        out_shape=(jax.ShapeDtypeStruct((rows, width), BF),) * 2,
        in_specs=[pair_spec(rows), pair_spec(rows), stacked_spec(rows, 0), stacked_spec(rows, 1)]
        + [table, table],
        out_specs=(pair_spec(rows),) * 2,
        cost_estimate=LIGHT,
    )(dk, dv, dkv_in, dkv_in, cos, sin)


def branch_kernel(stream_ref, att_ref, gain_ref, *refs):
    pieces, (hidden_ref, normed_ref, scale_ref) = refs[:4], refs[4:]
    for j, piece in enumerate(pieces):
        columns = piece_columns(j, piece.shape[1])
        term = dotf(att_ref[...], piece[...], NN)
        hidden_ref[:, columns] = stream_ref[:, columns].astype(F32) + term
    hidden = hidden_ref[...]
    mean = jnp.sum(hidden * hidden, axis=1, keepdims=True) / hidden.shape[1]
    scale = lax.rsqrt(mean + norm_eps)
    scale_ref[...] = scale
    normed_ref[...] = (hidden * scale * gain_ref[...]).astype(BF)


def add_branch(stream, att, gain, pieces):
    rows, depth = stream.shape
    heads = att.shape[1]
    tile = pl.BlockSpec((QROWS, depth), lambda i: (i, 0))
    return pl.pallas_call(
        branch_kernel,
        name="branch",
        grid=(rows // QROWS,),
        out_shape=(
            jax.ShapeDtypeStruct((rows, depth), F32),
            jax.ShapeDtypeStruct((rows, depth), BF),
            jax.ShapeDtypeStruct((rows, 1), F32),
        ),
        in_specs=[
            tile,
            pl.BlockSpec((QROWS, heads), lambda i: (i, 0)),
            pl.BlockSpec((1, depth), lambda i: (0, 0)),
        ]
        + [pl.BlockSpec(pieces[0].shape, lambda i: (0, 0))] * 4,
        out_specs=(tile, tile, pl.BlockSpec((QROWS, 1), lambda i: (i, 0))),
        compiler_params=pltpu.CompilerParams(vmem_limit_bytes=VMEM_BYTES),
        cost_estimate=LIGHT,
    )(stream, att, gain, *pieces)


def hidden_kernel(x_ref, *refs):
    w_in, (act_ref, by_gate_ref, by_up_ref) = refs[:4], refs[4:]
    rows = x_ref.shape[0]
    for r in range(0, rows, rows):
        part = slice(r, r + rows)
        gate = piece_dot(x_ref, part, [piece[0] for piece in w_in])
        up = piece_dot(x_ref, part, [piece[1] for piece in w_in])
        sig = jax.nn.sigmoid(gate)
        silu = gate * sig
        act_ref[part, :] = (silu * up).astype(BF)
        by_gate_ref[part, :] = (up * sig * (1.0 + gate * (1.0 - sig))).astype(BF)
        by_up_ref[part, :] = silu.astype(BF)


def hidden_units(x, w_in):
    rows, depth = x.shape
    _, size, units = w_in[0].shape
    tile = 256
    part = pl.BlockSpec((rows, tile), lambda i: (0, i))
    return pl.pallas_call(
        hidden_kernel,
        grid=(units // tile,),
        out_shape=(jax.ShapeDtypeStruct((rows, units), BF),) * 3,
        in_specs=[pl.BlockSpec((rows, depth), lambda i: (0, 0))]
        + [pl.BlockSpec((2, size, tile), lambda i: (0, 0, i))] * 4,
        out_specs=(part,) * 3,
        compiler_params=pltpu.CompilerParams(vmem_limit_bytes=VMEM_BYTES),
        cost_estimate=LIGHT,
        name="hidden",
    )(x, *w_in)


def hidden_back_kernel(cot_ref, by_gate_ref, by_up_ref, *refs):
    w_down, (dg_ref, du_ref) = refs[:4], refs[4:]
    rows = cot_ref.shape[0]
    for r in range(0, rows, rows):
        part = slice(r, r + rows)
        d_act = piece_dot(cot_ref, part, [piece[...] for piece in w_down], NT)
        dg_ref[part, :] = (d_act * by_gate_ref[part, :].astype(F32)).astype(BF)
        du_ref[part, :] = (d_act * by_up_ref[part, :].astype(F32)).astype(BF)


def hidden_back(cot, by_gate, by_up, w_down):
    rows, depth = cot.shape
    units, size = w_down[0].shape
    tile = 256
    part = pl.BlockSpec((rows, tile), lambda i: (0, i))
    return pl.pallas_call(
        hidden_back_kernel,
        grid=(units // tile,),
        out_shape=(jax.ShapeDtypeStruct((rows, units), BF),) * 2,
        in_specs=[pl.BlockSpec((rows, depth), lambda i: (0, 0)), part, part]
        + [pl.BlockSpec((tile, size), lambda i: (i, 0))] * 4,
        out_specs=(part,) * 2,
        compiler_params=pltpu.CompilerParams(vmem_limit_bytes=VMEM_BYTES),
        cost_estimate=LIGHT,
        name="hidden_back",
    )(cot, by_gate, by_up, *w_down)


def phased(i, block, make_index, tiles):
    def index_map(j, t):
        return make_index(jnp.where(j < i, 0, jnp.where(j == i, t, tiles - 1)))

    return pl.BlockSpec(block, index_map)


def columns_call(kernel_dot, lefts, pieces, block, make_index, size, flops, name):
    rows = lefts[0].shape[0]
    tile = min(size, 256)
    tiles = size // tile
    depth = size * 4

    def kernel(*refs):
        left_refs, piece_refs, out_ref = refs[: len(lefts)], refs[len(lefts) : -1], refs[-1]
        for j, piece in enumerate(piece_refs):

            @pl.when(pl.program_id(0) == j)
            def _():
                out_ref[...] = kernel_dot([left[...] for left in left_refs], piece).astype(BF)

    def out_index(j, t):
        return (0, (lax.axis_index("fsdp") ^ j) * tiles + t)

    return pl.pallas_call(
        kernel,
        grid=(4, tiles),
        out_shape=jax.ShapeDtypeStruct((rows, depth), BF),
        in_specs=[pl.BlockSpec(left.shape, lambda j, t: (0, 0)) for left in lefts]
        + [phased(i, block(tile), make_index, tiles) for i in range(4)],
        out_specs=pl.BlockSpec((rows, tile), out_index),
        compiler_params=pltpu.CompilerParams(vmem_limit_bytes=VMEM_BYTES),
        cost_estimate=LIGHT,
        name=name,
    )(*lefts, *pieces)


def stacked_columns(lefts, pieces, name):
    count, size, inner = pieces[0].shape

    def product(parts, piece):
        return sum(dotf(parts[c], piece[c], NT) for c in range(count))

    return columns_call(
        product,
        lefts,
        pieces,
        lambda tile: (count, tile, inner),
        lambda t: (0, t, 0),
        size,
        8 * lefts[0].shape[0] * size * inner * count,
        name,
    )


def plain_columns(left, pieces, name):
    inner, size = pieces[0].shape
    return columns_call(
        lambda parts, piece: dotf(parts[0], piece[...], NN),
        [left],
        pieces,
        lambda tile: (inner, tile),
        lambda t: (0, t),
        size,
        8 * left.shape[0] * size * inner,
        name,
    )


def branch_back_kernel(shares, d_mid_ref, hidden_ref, cot_ref, scale_ref, gain_ref, *refs):
    pieces, (d_hidden_ref, d_att_ref, gain_out_ref) = refs[:4], refs[4:7]
    d_mid = d_mid_ref[...].astype(F32)
    hidden = hidden_ref[...]
    scale = scale_ref[...]
    weighted = d_mid * gain_ref[...]
    inner = jnp.sum(weighted * hidden, axis=1, keepdims=True) / hidden.shape[1]
    d_hidden = (
        cot_ref[...].astype(F32) * (1.0 / shares)
        + scale * weighted
        - hidden * (scale * scale * scale * inner)
    )
    gain_term = jnp.sum(d_mid * hidden * scale, axis=0, keepdims=True)

    @pl.when(pl.program_id(0) == 0)
    def _():
        gain_out_ref[...] = gain_term

    @pl.when(pl.program_id(0) != 0)
    def _():
        gain_out_ref[...] += gain_term

    d_hidden_ref[...] = d_hidden.astype(BF)
    heads = d_att_ref.shape[1]
    for e in range(0, heads, 512):
        columns = slice(e, e + 512)
        d_att_ref[:, columns] = piece_dot(
            d_hidden_ref, slice(None), [piece[columns, :] for piece in pieces], NT
        ).astype(BF)


def branch_back(d_mid, hidden, cot, scale, gain, pieces):
    rows, depth = hidden.shape
    heads, size = pieces[0].shape
    tile = pl.BlockSpec((QROWS, depth), lambda i: (i, 0))
    row = pl.BlockSpec((1, depth), lambda i: (0, 0))
    return pl.pallas_call(
        functools.partial(branch_back_kernel, lax.axis_size("tensor")),
        name="branch_back",
        grid=(rows // QROWS,),
        in_specs=[tile, tile, tile, pl.BlockSpec((QROWS, 1), lambda i: (i, 0)), row]
        + [pl.BlockSpec((heads, size), lambda i: (0, 0))] * 4,
        out_specs=(tile, pl.BlockSpec((QROWS, heads), lambda i: (i, 0)), row),
        out_shape=(
            jax.ShapeDtypeStruct((rows, depth), BF),
            jax.ShapeDtypeStruct((rows, heads), BF),
            jax.ShapeDtypeStruct((1, depth), F32),
        ),
        compiler_params=pltpu.CompilerParams(vmem_limit_bytes=VMEM_BYTES),
        cost_estimate=LIGHT,
    )(d_mid, hidden, cot, scale, gain, *pieces)


def grad_call(left, right, cut, place, adds, name, span=(0, 1)):
    rows = left.shape[0]
    size = (left, right)[cut].shape[1] // 4
    swept = (right, left)[cut].shape[1] // span[1]
    height, width = (size, swept) if cut == 0 else (swept, size)
    tile = min(1024, swept)
    offset = span[0] * (swept // tile)
    block = (height, tile) if cut == 0 else (tile, width)

    def owner():
        return lax.axis_index("fsdp") ^ place

    def swept_index(t):
        return (0, t) if cut == 0 else (t, 0)

    def kernel(left_ref, right_ref, *refs):
        add_refs, out_ref = refs[: len(adds)], refs[len(adds)]
        if cut == 0:
            turned = refs[-1]

            @pl.when(pl.program_id(0) == 0)
            def _():
                turned[...] = left_ref[...].T

            result = dotf(turned[...], right_ref[...], NN)
        else:
            result = dotf(left_ref[...].T, right_ref[...], NN)
        for add in add_refs:
            result = result + add[...].astype(F32)
        out_ref[...] = result.astype(BF)

    fixed = pl.BlockSpec((rows, size), lambda t: (0, owner()))
    moving = pl.BlockSpec((rows, tile), lambda t: (0, t + offset))
    return pl.pallas_call(
        kernel,
        grid=(swept // tile,),
        out_shape=jax.ShapeDtypeStruct((height, width), BF),
        in_specs=[fixed, moving] * (cut == 0)
        + [moving, fixed] * (cut == 1)
        + [pl.BlockSpec(block, swept_index)] * len(adds),
        out_specs=pl.BlockSpec(block, swept_index),
        scratch_shapes=[pltpu.VMEM((size, rows), BF)] if cut == 0 else [],
        compiler_params=pltpu.CompilerParams(vmem_limit_bytes=VMEM_BYTES),
        cost_estimate=LIGHT,
        name=name,
    )(left, right, *adds)


class Reduction:
    def __init__(self, left, right, cut, name, span=(0, 1)):
        self.args, self.name, self.span = (left, right, cut), name, span

    def call(self, place, deps, step, adds=()):
        left, right, cut = self.args
        left = after(left, *deps) if deps else left
        return grad_call(left, right, cut, place, adds, self.name + step, self.span)

    def near_far(self, *deps):
        self.three = self.call(3, deps, "_3")
        self.for_two = swap(self.three, "fsdp", 1)

    def near(self, *deps):
        self.one = self.call(1, deps, "_1")
        self.for_own = swap(self.one, "fsdp", 1)

    def far(self, *deps):
        self.two = self.call(2, deps, "_2", [self.for_two])

    def send_far(self, *deps):
        self.across = swap(after(self.two, *deps), "fsdp", 2)

    def mine(self, *deps):
        self.own = self.call(0, deps, "_0", [self.for_own, self.across])

    def send_context(self, *deps):
        self.other = swap(after(self.own, *deps), "context", 1)


def totals_kernel(slots, *refs):
    pairs, out_ref = refs[:-1], refs[-1]
    for slot in range(len(pairs) // 2):
        total = pairs[2 * slot][...].astype(F32) + pairs[2 * slot + 1][...].astype(F32)
        if slots == 0:
            out_ref[slot] = total
        else:
            out_ref[:, slot, :] = total


def totals(sums, slots, *deps):
    arrays = [array for part in sums for array in (part.own, part.other)]
    if deps:
        arrays[0] = after(arrays[0], *deps)
    rows, width = arrays[0].shape
    tile = 128
    shape = [rows, width]
    shape.insert(slots, len(sums))
    block = [tile, width]
    block.insert(slots, len(sums))
    return pl.pallas_call(
        functools.partial(totals_kernel, slots),
        grid=(rows // tile,),
        out_shape=jax.ShapeDtypeStruct(tuple(shape), F32),
        in_specs=[pl.BlockSpec((tile, width), lambda i: (i, 0))] * len(arrays),
        out_specs=pl.BlockSpec(
            tuple(block), (lambda i: (0, i, 0)) if slots == 0 else (lambda i: (i, 0, 0))
        ),
        compiler_params=pltpu.CompilerParams(vmem_limit_bytes=VMEM_BYTES),
        cost_estimate=LIGHT,
        name="totals",
    )(*arrays)


def row_sum(values_in):
    return jnp.sum(values_in, axis=1, keepdims=True)


def per_device(tokens, w_qkv, w_out, w_gate_up, w_down, gains, seq_lengths, cotangent):
    row_count, part_width = tokens.shape
    tensor_index = lax.axis_index("tensor")
    context_index = lax.axis_index("context")
    full_width = part_width * lax.axis_size("tensor")

    def features(part_in):
        return lax.all_gather(part_in, "tensor", axis=1, tiled=True)

    def feature_sum(term):
        return lax.psum_scatter(term.astype(BF), "tensor", scatter_dimension=1, tiled=True)

    def own_features(full):
        return lax.dynamic_slice_in_dim(full, tensor_index * part_width, part_width, 1)

    ending = jnp.cumsum(seq_lengths[0])
    starts = ending - seq_lengths[0]
    places = context_index * row_count + jnp.arange(row_count, dtype=jnp.int32)
    first_token = jnp.max(jnp.where(starts[None, :] <= places[:, None], starts[None, :], 0), axis=1)
    cos, sin = rope_tables(places - first_token)
    low = first_token - context_index * row_count
    low_row = low[None, :]
    need = low[::QROWS]

    token_low = features(tokens)
    gain_near, gain_full = gather_gains(gains)
    gain_attn, gain_mlp = gain_full[0:1], gain_full[1:2]

    qkv_own = jnp.swapaxes(w_qkv, 0, 1)
    half = qkv_own.shape[1] // 2
    far_half = swap(
        lax.dynamic_slice_in_dim(after(qkv_own, gain_near), context_index * half, half, 1),
        "fsdp",
        2,
    )
    other_half = swap(far_half, "context", 1)
    qkv_far = jnp.where(
        context_index == 0,
        jnp.concatenate([far_half, other_half], axis=1),
        jnp.concatenate([other_half, far_half], axis=1),
    )
    qkv_near = swap(qkv_own, "fsdp", 1)
    qkv = (qkv_own, qkv_near, qkv_far, swap(qkv_far, "fsdp", 1))

    gate_up_own = jnp.swapaxes(w_gate_up, 0, 1)
    cut = gate_up_own.shape[1] * 12 // 32
    gate_up_a = swap(after(gate_up_own[:, :cut], far_half), "fsdp", 2)
    gate_up_b = swap(after(gate_up_own[:, cut:], gate_up_a), "fsdp", 2)

    keys_values, normed_in, scale_attn = project(
        after(token_low, gate_up_a), qkv, cos, sin, gain_attn, (1.0, None), 1, True
    )
    peer_kv = lax.ppermute(keys_values, "context", [(0, 1)])
    queries = project(normed_in, qkv, cos, sin, gain_attn, (HDIM**-0.5,), 0, False)[0][0]
    part, part_log = own_forward(queries, keys_values, low_row)
    attended, logs = peer_forward(
        need, queries, peer_kv, low_row, after(part, gate_up_b), part_log
    )
    attended_full = features(attended)

    out_own = after(lax.all_gather(w_out, "tensor", axis=0, tiled=True), attended)
    out_near = swap(out_own, "fsdp", 1)
    out_far = swap(out_own, "fsdp", 2)
    out_far_near = swap(out_far, "fsdp", 1)
    out = (out_own, out_near, out_far, out_far_near)
    gate_up_own, gate_up_a, gate_up_b = lax.optimization_barrier(
        (gate_up_own, gate_up_a, gate_up_b, attended)
    )[:3]
    gate_up_far = jnp.concatenate([gate_up_a, gate_up_b], axis=1)
    gate_up_near = swap(gate_up_own, "fsdp", 1)
    gate_up = (gate_up_own, gate_up_near, gate_up_far, swap(gate_up_far, "fsdp", 1))
    cot_full = features(after(cotangent, attended_full, out_far_near, out_near))
    down_far = swap(after(w_down, attended_full, out_far_near), "fsdp", 2)
    down_near = swap(after(w_down, attended_full), "fsdp", 1)
    hidden, normed_mid, scale_mlp = add_branch(token_low, attended_full, gain_mlp, out)

    activated, by_gate, by_up = hidden_units(normed_mid, gate_up)
    down_far = after(down_far, activated)
    down = (w_down, down_near, down_far, swap(down_far, "fsdp", 1))
    d_gate, d_up = hidden_back(after(cot_full, activated), by_gate, by_up, down)
    d_mid_term = stacked_columns([d_gate, d_up], gate_up, "d_mid")
    d_hidden_term, d_att_term, gain_mlp_term = branch_back(
        d_mid_term, hidden, cot_full, scale_mlp, gain_mlp, out
    )
    d_attended = feature_sum(d_att_term)
    d_hidden_own = feature_sum(after(d_hidden_term, d_att_term))

    down_a, down_b = (
        Reduction(activated, cot_full, 1, "grad_down", (part_index, 2)) for part_index in (0, 1)
    )
    grad_gate = Reduction(normed_mid, d_gate, 0, "grad_gate")
    grad_up = Reduction(normed_mid, d_up, 0, "grad_up")
    square = lax.axis_size("tensor") == lax.axis_size("fsdp")
    down_a.near_far(d_att_term)
    down_b.near_far(down_a.three)
    grad_gate.near_far(down_b.three)
    down_a.far(grad_gate.three)
    down_a.send_far()
    down_b.far(down_a.two)
    down_b.send_far()
    down_a.near(down_b.two)
    down_b.near(down_a.one)
    grad_gate.far(down_b.one)
    grad_gate.send_far()
    grad_gate.near(grad_gate.two)
    down_a.mine(grad_gate.one)
    down_a.send_context()
    grad_up.near_far(down_a.own)

    dq_peer, dkv_peer = peer_backward(
        need, queries, peer_kv, after(d_attended, grad_up.three), attended, low_row, logs
    )
    dkv_in = lax.ppermute(dkv_peer, "context", [(1, 0)])
    d_query, dk_own, dv_own = own_backward(
        queries, keys_values, d_attended, attended, low_row, logs, dq_peer, cos, sin
    )
    grad_query = Reduction(normed_in, d_query, 0, "grad_query")
    grad_up.near(d_query)
    grad_up.far(grad_up.one)
    grad_up.send_far()
    down_b.mine(grad_up.two, dkv_in)
    down_b.send_context()
    d_key, d_value = finish_keys(
        dk_own, dv_own, after(dkv_in, down_b.own, d_hidden_own), cos, sin
    )
    mlp_term = plain_columns(after(activated, d_value), down, "mlp_out")
    mlp_out = feature_sum(mlp_term)
    grad_gate.mine(mlp_term, down_a.other, down_b.other)
    grad_gate.send_context()
    grad_up.mine(grad_gate.own)
    grad_up.send_context()

    if square:
        grad_out = Reduction(attended_full, d_hidden_own, 0, "grad_out")
    else:
        grad_out = Reduction(attended, features(d_hidden_own), 1, "grad_out")
    grad_query.near_far(grad_up.own)
    grad_out.near_far(grad_query.three)
    grad_query.near(grad_out.three)
    grad_out.near(grad_query.one)
    grad_query.far(grad_out.one)
    grad_out.far(grad_query.two)
    d_in_term = stacked_columns(
        [d_query, d_key, after(d_value, grad_out.two, grad_gate.other)], qkv, "d_in"
    )
    d_in = feature_sum(d_in_term).astype(F32)
    grad_query.send_far()
    grad_out.send_far()
    grad_key = Reduction(normed_in, d_key, 0, "grad_key")
    grad_value = Reduction(normed_in, d_value, 0, "grad_value")
    grad_key.near_far(d_in_term)
    grad_value.near_far(grad_key.three)
    grad_key.near(grad_value.three)
    grad_value.near(grad_key.one)
    grad_key.far(grad_value.one)
    grad_key.send_far()
    grad_value.far(grad_key.two)
    grad_value.send_far()
    grad_query.mine(grad_value.two)
    grad_query.send_context()
    grad_out.mine(grad_query.own)
    if square:
        count = lax.axis_size("fsdp")
        across = [(i, (i % count) * count + i // count) for i in range(count * count)]
        grad_out.own = lax.ppermute(grad_out.own, ("fsdp", "tensor"), across)
    grad_out.send_context()

    stream = token_low.astype(F32)
    d_in_wide = after(d_in_term, grad_query.own).astype(F32)
    weighted = d_in_wide * stream
    inner_term = jnp.sum(weighted * gain_attn, axis=1)
    gain_attn_term = jnp.sum(weighted * scale_attn, axis=0)
    parts = lax.axis_size("tensor")
    totals_small = block_totals(
        jnp.concatenate(
            [
                jnp.broadcast_to(inner_term[None, :], (parts, row_count)),
                gain_attn_term.reshape(parts, part_width),
                gain_mlp_term.reshape(parts, part_width),
            ],
            axis=1,
        )[None]
    )
    inner_in = totals_small[0, :row_count][:, None] / full_width
    gain_sums = totals_small[0, row_count:].reshape(2, part_width)
    gain_sums = exchange(gain_sums, "fsdp", 1)
    gain_sums = exchange(gain_sums, "fsdp", 2)
    gain_sums = exchange(gain_sums, "context", 1)
    gain_width = gains.shape[1]
    grad_gains = lax.dynamic_slice_in_dim(
        gain_sums, lax.axis_index("fsdp") * gain_width, gain_width, 1
    )

    grad_down_sum = totals([down_a, down_b], 0, d_in_wide).reshape(w_down.shape)
    grad_key.mine(grad_down_sum, grad_up.other)
    grad_key.send_context()
    grad_value.mine(grad_key.own)
    grad_value.send_context()
    grad_gate_up_sum = totals([grad_gate, grad_up], 1, grad_value.own)
    grad_qkv = totals([grad_query, grad_key, grad_value], 0, grad_gate_up_sum)
    grad_out_sum = totals([grad_out], 0, grad_qkv)[0]

    block_out = (own_features(hidden) + mlp_out.astype(F32)).astype(BF)
    own_tokens = tokens.astype(F32)
    grad_tokens = (
        d_hidden_own.astype(F32)
        + scale_attn * own_features(gain_attn) * d_in
        - own_tokens * scale_attn * scale_attn * scale_attn * inner_in
    ).astype(BF)
    return (
        block_out,
        grad_tokens,
        jnp.swapaxes(grad_qkv, 0, 1),
        grad_out_sum,
        grad_gate_up_sum,
        grad_down_sum,
        grad_gains,
    )


def solution(mesh):
    rows = P(("fsdp", "context"), "tensor")
    inner = P("fsdp", None, "tensor")
    outer = P("tensor", "fsdp")
    gain = P(None, ("tensor", "fsdp"))
    return jax.shard_map(
        per_device,
        mesh=mesh,
        in_specs=(rows, inner, outer, inner, outer, gain, P("fsdp", None), rows),
        out_specs=(rows, rows, inner, outer, inner, outer, gain),
        check_vma=False,
    )
```

```python
import functools

import jax
import jax.numpy as jnp
from jax import lax
from jax.experimental import pallas as pl
from jax.experimental.pallas import tpu as pltpu
from jax.sharding import PartitionSpec as P

HDIM = 64
LANES = 128
QROWS = 256
norm_eps = 1e-05
rope_base = 130000.0
masked_score = -1e30
BF = jnp.bfloat16
F32 = jnp.float32
VMEM_BYTES = 56 * 1024 * 1024
LIGHT = pl.CostEstimate(flops=1, bytes_accessed=1, transcendentals=0)


def dotf(a, b, dims):
    return lax.dot_general(a, b, (dims, ((), ())), preferred_element_type=F32)


NN = ((1,), (0,))
NT = ((1,), (1,))
TN = ((0,), (0,))


def swap(value, axis, bit):
    count = lax.axis_size(axis)
    return lax.ppermute(value, axis, [(i, i ^ bit) for i in range(count)])


def after(value, *others):
    return lax.optimization_barrier((value, *others))[0]


def shifted(value, axis):
    count = lax.axis_size(axis)
    return [
        lax.ppermute(value, axis, [(i, (i + step) % count) for i in range(count)])
        for step in range(1, count)
    ]


def exchange(value, axis, bit):
    return value + swap(value, axis, bit)


def join_kernel(axis, mode, *refs):
    pieces, out_ref = refs[:-1], refs[-1]
    count = len(pieces)
    me = lax.axis_index(axis)
    for step, piece in enumerate(pieces):
        size = piece.shape[1]
        place = (me ^ step) if mode == "xor" else (me - step + count) % count
        out_ref[:, pl.ds(pl.multiple_of(place * size, size), size)] = piece[...]


def join(pieces, axis, mode):
    rows, size = pieces[0].shape
    return pl.pallas_call(
        functools.partial(join_kernel, axis, mode),
        out_shape=jax.ShapeDtypeStruct((rows, size * len(pieces)), pieces[0].dtype),
        cost_estimate=LIGHT,
        name="join",
    )(*pieces)


def gather_gains(gains):
    if lax.axis_size("tensor") > 4 or gains.shape[1] % LANES:
        whole = lax.all_gather(gains, ("tensor", "fsdp"), axis=1, tiled=True).astype(F32)
        return gains, whole
    own = gains.astype(F32)
    part = join([own] + [swap(own, "fsdp", bit) for bit in (1, 2, 3)], "fsdp", "xor")
    return part, join([part] + shifted(part, "tensor"), "tensor", "shift")


def block_totals(blocks):
    count = lax.axis_size("tensor")
    me = lax.axis_index("tensor")
    if count > 4:
        return lax.dynamic_index_in_dim(lax.psum(blocks, "tensor"), me, 1, keepdims=False)

    def pick(place):
        return lax.dynamic_index_in_dim(blocks, place, 1, keepdims=False)

    total = pick(me)
    for step in range(1, count):
        moves = [(i, (i + step) % count) for i in range(count)]
        total = total + lax.ppermute(pick((me + step) % count), "tensor", moves)
    return total


def piece_columns(j, size):
    return pl.ds(pl.multiple_of((lax.axis_index("fsdp") ^ j) * size, size), size)


def swap_halves(block):
    lane = lax.broadcasted_iota(jnp.int32, block.shape, 1)
    up = pltpu.roll(block, LANES - HDIM // 2, 1)
    down = pltpu.roll(block, HDIM // 2, 1)
    return jnp.where((lane & (HDIM - 1)) < HDIM // 2, up, down)


def rope_tables(positions):
    lane = jnp.arange(LANES, dtype=jnp.int32)
    half = lane % (HDIM // 2)
    frequencies = rope_base ** (-2.0 * half.astype(F32) / HDIM)
    angles = positions.astype(F32)[:, None] * frequencies[None, :]
    sign = jnp.where((lane % HDIM) < HDIM // 2, -1.0, 1.0)
    return jnp.cos(angles), jnp.sin(angles) * sign[None, :]


def piece_dot(x_ref, rows, pieces, dims=NN):
    total = None
    for j, piece in enumerate(pieces):
        size = piece.shape[dims[1][0]]
        term = dotf(x_ref[rows, piece_columns(j, size)], piece, dims)
        total = term if total is None else total + term
    return total


def project_kernel(kinds, normalize, x_ref, *refs):
    pieces, (cos_ref, sin_ref, gain_ref), outs = refs[:4], refs[4:7], refs[7:]
    out_ref = outs[0]
    rows, width = out_ref.shape[1:]
    step = pl.program_id(0)
    if normalize:
        normed_ref, scale_ref = outs[1], outs[2]

        @pl.when(step == 0)
        def _():
            for r in range(0, rows, QROWS):
                part = slice(r, r + QROWS)
                stream = x_ref[part, :].astype(F32)
                mean = jnp.sum(stream * stream, axis=1, keepdims=True) / x_ref.shape[1]
                scale = lax.rsqrt(mean + norm_eps)
                scale_ref[part, :] = scale
                normed_ref[part, :] = (stream * scale * gain_ref[...]).astype(BF)

        x_ref = normed_ref
    for index, scale in enumerate(kinds):

        @pl.when(step == index)
        def _():
            for r in range(0, rows, rows):
                part = slice(r, r + rows)
                result = piece_dot(x_ref, part, [piece[0] for piece in pieces])
                for c in range(0, width, LANES):
                    block = result[:, c : c + LANES]
                    if scale:
                        block = block * cos_ref[part, :] + swap_halves(block) * sin_ref[part, :]
                    low = block.astype(BF)
                    if scale and scale != 1.0:
                        low = low * jnp.asarray(scale, BF)
                    out_ref[0, part, c : c + LANES] = low


def project(x, pieces, cos, sin, gain, kinds, first, normalize):
    rows, depth = x.shape
    _, size, width = pieces[0].shape
    flops = 2 * len(kinds) * rows * depth * width
    whole = pl.BlockSpec((rows, depth), lambda i: (0, 0))
    table = pl.BlockSpec((rows, LANES), lambda i: (0, 0))
    out_shape = [jax.ShapeDtypeStruct((len(kinds), rows, width), BF)]
    out_specs = [pl.BlockSpec((1, rows, width), lambda i: (i, 0, 0))]
    if normalize:
        out_shape += [jax.ShapeDtypeStruct((rows, depth), BF), jax.ShapeDtypeStruct((rows, 1), F32)]
        out_specs += [whole, pl.BlockSpec((rows, 1), lambda i: (0, 0))]
    return pl.pallas_call(
        functools.partial(project_kernel, kinds, normalize),
        name="project_kv" if normalize else "project_q",
        grid=(len(kinds),),
        out_shape=out_shape,
        in_specs=[whole]
        + [pl.BlockSpec((1, size, width), lambda i: (i + first, 0, 0))] * 4
        + [table, table, pl.BlockSpec((1, depth), lambda i: (0, 0))],
        out_specs=out_specs,
        compiler_params=pltpu.CompilerParams(vmem_limit_bytes=VMEM_BYTES),
        cost_estimate=LIGHT,
    )(x, *pieces, cos, sin, gain)


def head_mask(block, head):
    lane = lax.broadcasted_iota(jnp.int32, block.shape, 1)
    inside = (lane < HDIM) if head == 0 else (lane >= HDIM)
    return jnp.where(inside, block, jnp.zeros_like(block))


def own_mask(key_count, row0, low_row):
    key = lax.broadcasted_iota(jnp.int32, (key_count, QROWS), 0)
    query = row0 + lax.broadcasted_iota(jnp.int32, (key_count, QROWS), 1)
    return (key >= low_row) & (key <= query)


def peer_mask(key_count, low_row, offset):
    key = lax.broadcasted_iota(jnp.int32, (key_count, QROWS), 0) - offset
    return key >= low_row


def key_windows(need, total):
    counts = list(range(QROWS, total + 1, QROWS))
    for place, count in enumerate(counts):
        chosen = need < 0 if place == 0 else need < -counts[place - 1]
        if count < total:
            chosen = jnp.logical_and(chosen, need >= -count)
        yield count, chosen


def own_forward_kernel(q_ref, k_ref, v_ref, low_ref, out_ref, log_ref):
    rows = q_ref.shape[0]
    v_t = v_ref[...].T
    for r in range(0, rows, QROWS):
        count = r + QROWS
        allowed = own_mask(count, r, low_ref[:, r : r + QROWS])
        keys = k_ref[0:count, :]
        outs = []
        for head in range(LANES // HDIM):
            scores = dotf(keys, head_mask(q_ref[r : r + QROWS, :], head), NT)
            scores = jnp.where(allowed, scores, masked_score)
            peak = jnp.max(scores, axis=0, keepdims=True)
            weights = jnp.exp(scores - peak)
            total = jnp.sum(weights, axis=0, keepdims=True)
            part = dotf(v_t[head * HDIM : (head + 1) * HDIM, 0:count], weights.astype(BF), NN)
            outs.append(part / total)
            log_ref[0, head : head + 1, r : r + QROWS] = peak + jnp.log(total)
        out_ref[r : r + QROWS, :] = jnp.concatenate(outs, axis=0).T


def peer_forward_kernel(
    need_ref, q_ref, k_ref, v_ref, low_ref, part_ref, log_in_ref, out_ref, log_ref
):
    rows = q_ref.shape[0]
    key_total = k_ref.shape[0]
    for index, r in enumerate(range(0, rows, QROWS)):
        for key_count, chosen in key_windows(need_ref[index], key_total):

            @pl.when(chosen)
            def _():
                window = slice(key_total - key_count, key_total)
                v_t = v_ref[window, :].T
                allowed = peer_mask(key_count, low_ref[:, r : r + QROWS], key_count)
                before = part_ref[r : r + QROWS, :].T
                outs = []
                for head in range(LANES // HDIM):
                    scores = dotf(k_ref[window, :], head_mask(q_ref[r : r + QROWS, :], head), NT)
                    scores = jnp.where(allowed, scores, masked_score)
                    log_own = log_in_ref[0, head : head + 1, r : r + QROWS]
                    peak = jnp.maximum(jnp.max(scores, axis=0, keepdims=True), log_own)
                    weights = jnp.exp(scores - peak)
                    own_weight = jnp.exp(log_own - peak)
                    total = jnp.sum(weights, axis=0, keepdims=True) + own_weight
                    rows_h = slice(head * HDIM, (head + 1) * HDIM)
                    part = dotf(v_t[rows_h, :], weights.astype(BF), NN)
                    outs.append((part + before[rows_h, :] * own_weight) / total)
                    log_ref[0, head : head + 1, r : r + QROWS] = peak + jnp.log(total)
                out_ref[r : r + QROWS, :] = jnp.concatenate(outs, axis=0).T.astype(BF)

        @pl.when(need_ref[index] >= 0)
        def _():
            out_ref[r : r + QROWS, :] = part_ref[r : r + QROWS, :].astype(BF)
            log_ref[:, :, r : r + QROWS] = log_in_ref[:, :, r : r + QROWS]


def pair_spec(rows):
    return pl.BlockSpec((rows, LANES), lambda i: (0, i))


def stacked_spec(rows, part):
    return pl.BlockSpec((None, rows, LANES), lambda i: (part, 0, i))


def log_spec(rows):
    return pl.BlockSpec((1, LANES // HDIM, rows), lambda i: (i, 0, 0))


def low_spec(rows):
    return pl.BlockSpec((1, rows), lambda i: (0, 0))


def own_forward(q, kv, low_row):
    rows, width = q.shape
    pairs = width // LANES
    return pl.pallas_call(
        own_forward_kernel,
        name="own_fwd",
        grid=(pairs,),
        out_shape=(
            jax.ShapeDtypeStruct((rows, width), F32),
            jax.ShapeDtypeStruct((pairs, LANES // HDIM, rows), F32),
        ),
        in_specs=[
            pair_spec(rows),
            stacked_spec(rows, 0),
            stacked_spec(rows, 1),
            low_spec(rows),
        ],
        out_specs=(pair_spec(rows), log_spec(rows)),
        compiler_params=pltpu.CompilerParams(vmem_limit_bytes=VMEM_BYTES),
        cost_estimate=LIGHT,
    )(q, kv, kv, low_row)


SMEM_SPEC = pl.BlockSpec(memory_space=pltpu.SMEM)


def peer_forward(need, q, kv, low_row, part, log_in):
    rows, width = q.shape
    pairs = width // LANES
    return pl.pallas_call(
        peer_forward_kernel,
        name="peer_fwd",
        grid=(pairs,),
        out_shape=(
            jax.ShapeDtypeStruct((rows, width), BF),
            jax.ShapeDtypeStruct((pairs, LANES // HDIM, rows), F32),
        ),
        in_specs=[
            SMEM_SPEC,
            pair_spec(rows),
            stacked_spec(rows, 0),
            stacked_spec(rows, 1),
            low_spec(rows),
            pair_spec(rows),
            log_spec(rows),
        ],
        out_specs=(pair_spec(rows), log_spec(rows)),
        compiler_params=pltpu.CompilerParams(vmem_limit_bytes=VMEM_BYTES),
        cost_estimate=LIGHT,
    )(need, q, kv, kv, low_row, part, log_in)


def backward_block(q_rows, k_rows, v_rows, k_t, do_rows, do_o_t, logs, allowed):
    d_query, d_key, d_value = [], None, None
    for head in range(LANES // HDIM):
        rows_h = slice(head * HDIM, (head + 1) * HDIM)
        q_head = head_mask(q_rows, head)
        do_head = head_mask(do_rows, head)
        scores = dotf(k_rows, q_head, NT)
        probs = jnp.exp(jnp.where(allowed, scores, masked_score) - logs[head])
        delta = jnp.sum(do_o_t[rows_h, :], axis=0, keepdims=True)
        d_probs = dotf(v_rows, do_head, NT)
        d_scores = (probs * (d_probs - delta)).astype(BF)
        d_v = dotf(probs.astype(BF), do_head, NN)
        d_k = dotf(d_scores, q_head, NN)
        d_value = d_v if d_value is None else d_value + d_v
        d_key = d_k if d_key is None else d_key + d_k
        d_query.append(dotf(k_t[rows_h, :], d_scores, NN))
    return jnp.concatenate(d_query, axis=0), d_key, d_value


def output_product(do_ref, o_ref, window):
    product = do_ref[window].astype(F32) * o_ref[window].astype(F32)
    return product.T


def peer_backward_kernel(
    need_ref, q_ref, k_ref, v_ref, do_ref, o_ref, low_ref, log_ref, dq_ref, dkv_ref, sums
):
    rows = q_ref.shape[0]
    key_total = k_ref.shape[0]
    sums[...] = jnp.zeros_like(sums)
    for index, r in enumerate(range(0, rows, QROWS)):
        rows_q = (slice(r, r + QROWS), slice(None))
        for key_count, chosen in key_windows(need_ref[index], key_total):

            @pl.when(chosen)
            def _():
                window = slice(key_total - key_count, key_total)
                allowed = peer_mask(key_count, low_ref[:, r : r + QROWS], key_count)
                logs = [log_ref[0, h : h + 1, r : r + QROWS] for h in range(LANES // HDIM)]
                d_query, d_key, d_value = backward_block(
                    q_ref[rows_q],
                    k_ref[window, :],
                    v_ref[window, :],
                    k_ref[window, :].T,
                    do_ref[rows_q],
                    output_product(do_ref, o_ref, rows_q),
                    logs,
                    allowed,
                )
                dq_ref[rows_q] = d_query.T
                sums[0, window] += d_key
                sums[1, window] += d_value

        @pl.when(need_ref[index] >= 0)
        def _():
            dq_ref[rows_q] = jnp.zeros((QROWS, LANES), F32)

    dkv_ref[...] = sums[...].astype(BF)


def peer_backward(need, q, kv, do, o, low_row, logs):
    rows, width = q.shape
    pairs = width // LANES
    return pl.pallas_call(
        peer_backward_kernel,
        name="peer_bwd",
        grid=(pairs,),
        out_shape=(
            jax.ShapeDtypeStruct((rows, width), F32),
            jax.ShapeDtypeStruct((2, rows, width), BF),
        ),
        in_specs=[
            SMEM_SPEC,
            pair_spec(rows),
            stacked_spec(rows, 0),
            stacked_spec(rows, 1),
            pair_spec(rows),
            pair_spec(rows),
            low_spec(rows),
            log_spec(rows),
        ],
        out_specs=(pair_spec(rows), pl.BlockSpec((2, rows, LANES), lambda i: (0, 0, i))),
        scratch_shapes=[pltpu.VMEM((2, rows, LANES), F32)],
        compiler_params=pltpu.CompilerParams(vmem_limit_bytes=VMEM_BYTES),
        cost_estimate=LIGHT,
    )(need, q, kv, kv, do, o, low_row, logs)


def own_backward_kernel(
    q_ref,
    k_ref,
    v_ref,
    do_ref,
    o_ref,
    low_ref,
    log_ref,
    dq_in_ref,
    cos_ref,
    sin_ref,
    dq_ref,
    dk_ref,
    dv_ref,
    sums,
):
    rows = q_ref.shape[0]
    sums[...] = jnp.zeros_like(sums)
    k_t = k_ref[...].T
    for r in range(0, rows, QROWS):
        count = r + QROWS
        window = (slice(r, r + QROWS), slice(None))
        allowed = own_mask(count, r, low_ref[:, r : r + QROWS])
        logs = [log_ref[0, h : h + 1, r : r + QROWS] for h in range(LANES // HDIM)]
        d_query, d_key, d_value = backward_block(
            q_ref[window],
            k_ref[0:count, :],
            v_ref[0:count, :],
            k_t[:, 0:count],
            do_ref[window],
            output_product(do_ref, o_ref, window),
            logs,
            allowed,
        )
        rotated = (d_query.T + dq_in_ref[window]) * (HDIM**-0.5)
        turned = rotated * cos_ref[window] - swap_halves(rotated) * sin_ref[window]
        dq_ref[window] = turned.astype(BF)
        sums[0, 0:count] += d_key
        sums[1, 0:count] += d_value
    dk_ref[...] = sums[0]
    dv_ref[...] = sums[1]


def own_backward(q, kv, do, o, low_row, logs, dq_in, cos, sin):
    rows, width = q.shape
    pairs = width // LANES
    table = pl.BlockSpec((rows, LANES), lambda i: (0, 0))
    return pl.pallas_call(
        own_backward_kernel,
        name="own_bwd",
        grid=(pairs,),
        out_shape=(
            jax.ShapeDtypeStruct((rows, width), BF),
            jax.ShapeDtypeStruct((rows, width), F32),
            jax.ShapeDtypeStruct((rows, width), F32),
        ),
        in_specs=[
            pair_spec(rows),
            stacked_spec(rows, 0),
            stacked_spec(rows, 1),
            pair_spec(rows),
            pair_spec(rows),
            low_spec(rows),
            log_spec(rows),
            pair_spec(rows),
            table,
            table,
        ],
        out_specs=(pair_spec(rows),) * 3,
        scratch_shapes=[pltpu.VMEM((2, rows, LANES), F32)],
        compiler_params=pltpu.CompilerParams(vmem_limit_bytes=VMEM_BYTES),
        cost_estimate=LIGHT,
    )(q, kv, kv, do, o, low_row, logs, dq_in, cos, sin)


def finish_keys_kernel(dk_ref, dv_ref, dk_in_ref, dv_in_ref, cos_ref, sin_ref, dk_out, dv_out):
    total = dk_ref[...] + dk_in_ref[...].astype(F32)
    turned = total * cos_ref[...] - swap_halves(total) * sin_ref[...]
    dk_out[...] = turned.astype(BF)
    dv_out[...] = (dv_ref[...] + dv_in_ref[...].astype(F32)).astype(BF)


def finish_keys(dk, dv, dkv_in, cos, sin):
    rows, width = dk.shape
    pairs = width // LANES
    table = pl.BlockSpec((rows, LANES), lambda i: (0, 0))
    return pl.pallas_call(
        finish_keys_kernel,
        name="finish_keys",
        grid=(pairs,),
        out_shape=(jax.ShapeDtypeStruct((rows, width), BF),) * 2,
        in_specs=[pair_spec(rows), pair_spec(rows), stacked_spec(rows, 0), stacked_spec(rows, 1)]
        + [table, table],
        out_specs=(pair_spec(rows),) * 2,
        cost_estimate=LIGHT,
    )(dk, dv, dkv_in, dkv_in, cos, sin)


def branch_kernel(stream_ref, att_ref, gain_ref, *refs):
    pieces, (hidden_ref, normed_ref, scale_ref) = refs[:4], refs[4:]
    for j, piece in enumerate(pieces):
        columns = piece_columns(j, piece.shape[1])
        term = dotf(att_ref[...], piece[...], NN)
        hidden_ref[:, columns] = stream_ref[:, columns].astype(F32) + term
    hidden = hidden_ref[...]
    mean = jnp.sum(hidden * hidden, axis=1, keepdims=True) / hidden.shape[1]
    scale = lax.rsqrt(mean + norm_eps)
    scale_ref[...] = scale
    normed_ref[...] = (hidden * scale * gain_ref[...]).astype(BF)


def add_branch(stream, att, gain, pieces):
    rows, depth = stream.shape
    heads = att.shape[1]
    tile = pl.BlockSpec((QROWS, depth), lambda i: (i, 0))
    return pl.pallas_call(
        branch_kernel,
        name="branch",
        grid=(rows // QROWS,),
        out_shape=(
            jax.ShapeDtypeStruct((rows, depth), F32),
            jax.ShapeDtypeStruct((rows, depth), BF),
            jax.ShapeDtypeStruct((rows, 1), F32),
        ),
        in_specs=[
            tile,
            pl.BlockSpec((QROWS, heads), lambda i: (i, 0)),
            pl.BlockSpec((1, depth), lambda i: (0, 0)),
        ]
        + [pl.BlockSpec(pieces[0].shape, lambda i: (0, 0))] * 4,
        out_specs=(tile, tile, pl.BlockSpec((QROWS, 1), lambda i: (i, 0))),
        compiler_params=pltpu.CompilerParams(vmem_limit_bytes=VMEM_BYTES),
        cost_estimate=LIGHT,
    )(stream, att, gain, *pieces)


def hidden_kernel(x_ref, *refs):
    w_in, (act_ref, by_gate_ref, by_up_ref) = refs[:4], refs[4:]
    rows = x_ref.shape[0]
    for r in range(0, rows, rows):
        part = slice(r, r + rows)
        gate = piece_dot(x_ref, part, [piece[0] for piece in w_in])
        up = piece_dot(x_ref, part, [piece[1] for piece in w_in])
        sig = jax.nn.sigmoid(gate)
        silu = gate * sig
        act_ref[part, :] = (silu * up).astype(BF)
        by_gate_ref[part, :] = (up * sig * (1.0 + gate * (1.0 - sig))).astype(BF)
        by_up_ref[part, :] = silu.astype(BF)


def hidden_units(x, w_in):
    rows, depth = x.shape
    _, size, units = w_in[0].shape
    tile = 256
    part = pl.BlockSpec((rows, tile), lambda i: (0, i))
    return pl.pallas_call(
        hidden_kernel,
        grid=(units // tile,),
        out_shape=(jax.ShapeDtypeStruct((rows, units), BF),) * 3,
        in_specs=[pl.BlockSpec((rows, depth), lambda i: (0, 0))]
        + [pl.BlockSpec((2, size, tile), lambda i: (0, 0, i))] * 4,
        out_specs=(part,) * 3,
        compiler_params=pltpu.CompilerParams(vmem_limit_bytes=VMEM_BYTES),
        cost_estimate=LIGHT,
        name="hidden",
    )(x, *w_in)


def hidden_back_kernel(cot_ref, by_gate_ref, by_up_ref, *refs):
    w_down, (dg_ref, du_ref) = refs[:4], refs[4:]
    rows = cot_ref.shape[0]
    for r in range(0, rows, rows):
        part = slice(r, r + rows)
        d_act = piece_dot(cot_ref, part, [piece[...] for piece in w_down], NT)
        dg_ref[part, :] = (d_act * by_gate_ref[part, :].astype(F32)).astype(BF)
        du_ref[part, :] = (d_act * by_up_ref[part, :].astype(F32)).astype(BF)


def hidden_back(cot, by_gate, by_up, w_down):
    rows, depth = cot.shape
    units, size = w_down[0].shape
    tile = 256
    part = pl.BlockSpec((rows, tile), lambda i: (0, i))
    return pl.pallas_call(
        hidden_back_kernel,
        grid=(units // tile,),
        out_shape=(jax.ShapeDtypeStruct((rows, units), BF),) * 2,
        in_specs=[pl.BlockSpec((rows, depth), lambda i: (0, 0)), part, part]
        + [pl.BlockSpec((tile, size), lambda i: (i, 0))] * 4,
        out_specs=(part,) * 2,
        compiler_params=pltpu.CompilerParams(vmem_limit_bytes=VMEM_BYTES),
        cost_estimate=LIGHT,
        name="hidden_back",
    )(cot, by_gate, by_up, *w_down)


def phased(i, block, make_index, tiles):
    def index_map(j, t):
        return make_index(jnp.where(j < i, 0, jnp.where(j == i, t, tiles - 1)))

    return pl.BlockSpec(block, index_map)


def columns_call(kernel_dot, lefts, pieces, block, make_index, size, flops, name):
    rows = lefts[0].shape[0]
    tile = min(size, 256)
    tiles = size // tile
    depth = size * 4

    def kernel(*refs):
        left_refs, piece_refs, out_ref = refs[: len(lefts)], refs[len(lefts) : -1], refs[-1]
        for j, piece in enumerate(piece_refs):

            @pl.when(pl.program_id(0) == j)
            def _():
                out_ref[...] = kernel_dot([left[...] for left in left_refs], piece).astype(BF)

    def out_index(j, t):
        return (0, (lax.axis_index("fsdp") ^ j) * tiles + t)

    return pl.pallas_call(
        kernel,
        grid=(4, tiles),
        out_shape=jax.ShapeDtypeStruct((rows, depth), BF),
        in_specs=[pl.BlockSpec(left.shape, lambda j, t: (0, 0)) for left in lefts]
        + [phased(i, block(tile), make_index, tiles) for i in range(4)],
        out_specs=pl.BlockSpec((rows, tile), out_index),
        compiler_params=pltpu.CompilerParams(vmem_limit_bytes=VMEM_BYTES),
        cost_estimate=LIGHT,
        name=name,
    )(*lefts, *pieces)


def stacked_columns(lefts, pieces, name):
    count, size, inner = pieces[0].shape

    def product(parts, piece):
        return sum(dotf(parts[c], piece[c], NT) for c in range(count))

    return columns_call(
        product,
        lefts,
        pieces,
        lambda tile: (count, tile, inner),
        lambda t: (0, t, 0),
        size,
        8 * lefts[0].shape[0] * size * inner * count,
        name,
    )


def plain_columns(left, pieces, name):
    inner, size = pieces[0].shape
    return columns_call(
        lambda parts, piece: dotf(parts[0], piece[...], NN),
        [left],
        pieces,
        lambda tile: (inner, tile),
        lambda t: (0, t),
        size,
        8 * left.shape[0] * size * inner,
        name,
    )


def branch_back_kernel(shares, d_mid_ref, hidden_ref, cot_ref, scale_ref, gain_ref, *refs):
    pieces, (d_hidden_ref, d_att_ref, gain_out_ref) = refs[:4], refs[4:7]
    d_mid = d_mid_ref[...].astype(F32)
    hidden = hidden_ref[...]
    scale = scale_ref[...]
    weighted = d_mid * gain_ref[...]
    inner = jnp.sum(weighted * hidden, axis=1, keepdims=True) / hidden.shape[1]
    d_hidden = (
        cot_ref[...].astype(F32) * (1.0 / shares)
        + scale * weighted
        - hidden * (scale * scale * scale * inner)
    )
    gain_term = jnp.sum(d_mid * hidden * scale, axis=0, keepdims=True)

    @pl.when(pl.program_id(0) == 0)
    def _():
        gain_out_ref[...] = gain_term

    @pl.when(pl.program_id(0) != 0)
    def _():
        gain_out_ref[...] += gain_term

    d_hidden_ref[...] = d_hidden.astype(BF)
    heads = d_att_ref.shape[1]
    for e in range(0, heads, 512):
        columns = slice(e, e + 512)
        d_att_ref[:, columns] = piece_dot(
            d_hidden_ref, slice(None), [piece[columns, :] for piece in pieces], NT
        ).astype(BF)


def branch_back(d_mid, hidden, cot, scale, gain, pieces):
    rows, depth = hidden.shape
    heads, size = pieces[0].shape
    tile = pl.BlockSpec((QROWS, depth), lambda i: (i, 0))
    row = pl.BlockSpec((1, depth), lambda i: (0, 0))
    return pl.pallas_call(
        functools.partial(branch_back_kernel, lax.axis_size("tensor")),
        name="branch_back",
        grid=(rows // QROWS,),
        in_specs=[tile, tile, tile, pl.BlockSpec((QROWS, 1), lambda i: (i, 0)), row]
        + [pl.BlockSpec((heads, size), lambda i: (0, 0))] * 4,
        out_specs=(tile, pl.BlockSpec((QROWS, heads), lambda i: (i, 0)), row),
        out_shape=(
            jax.ShapeDtypeStruct((rows, depth), BF),
            jax.ShapeDtypeStruct((rows, heads), BF),
            jax.ShapeDtypeStruct((1, depth), F32),
        ),
        compiler_params=pltpu.CompilerParams(vmem_limit_bytes=VMEM_BYTES),
        cost_estimate=LIGHT,
    )(d_mid, hidden, cot, scale, gain, *pieces)


def grad_call(left, right, cut, place, adds, name, span=(0, 1)):
    rows = left.shape[0]
    size = (left, right)[cut].shape[1] // 4
    swept = (right, left)[cut].shape[1] // span[1]
    height, width = (size, swept) if cut == 0 else (swept, size)
    tile = min(1024, swept)
    offset = span[0] * (swept // tile)
    block = (height, tile) if cut == 0 else (tile, width)

    def owner():
        return lax.axis_index("fsdp") ^ place

    def swept_index(t):
        return (0, t) if cut == 0 else (t, 0)

    def kernel(left_ref, right_ref, *refs):
        add_refs, out_ref = refs[: len(adds)], refs[len(adds)]
        if cut == 0:
            turned = refs[-1]

            @pl.when(pl.program_id(0) == 0)
            def _():
                turned[...] = left_ref[...].T

            result = dotf(turned[...], right_ref[...], NN)
        else:
            result = dotf(left_ref[...].T, right_ref[...], NN)
        for add in add_refs:
            result = result + add[...].astype(F32)
        out_ref[...] = result.astype(BF)

    fixed = pl.BlockSpec((rows, size), lambda t: (0, owner()))
    moving = pl.BlockSpec((rows, tile), lambda t: (0, t + offset))
    return pl.pallas_call(
        kernel,
        grid=(swept // tile,),
        out_shape=jax.ShapeDtypeStruct((height, width), BF),
        in_specs=[fixed, moving] * (cut == 0)
        + [moving, fixed] * (cut == 1)
        + [pl.BlockSpec(block, swept_index)] * len(adds),
        out_specs=pl.BlockSpec(block, swept_index),
        scratch_shapes=[pltpu.VMEM((size, rows), BF)] if cut == 0 else [],
        compiler_params=pltpu.CompilerParams(vmem_limit_bytes=VMEM_BYTES),
        cost_estimate=LIGHT,
        name=name,
    )(left, right, *adds)


class Reduction:
    def __init__(self, left, right, cut, name, span=(0, 1)):
        self.args, self.name, self.span = (left, right, cut), name, span

    def call(self, place, deps, step, adds=()):
        left, right, cut = self.args
        left = after(left, *deps) if deps else left
        return grad_call(left, right, cut, place, adds, self.name + step, self.span)

    def near_far(self, *deps):
        self.three = self.call(3, deps, "_3")
        self.for_two = swap(self.three, "fsdp", 1)

    def near(self, *deps):
        self.one = self.call(1, deps, "_1")
        self.for_own = swap(self.one, "fsdp", 1)

    def far(self, *deps):
        self.two = self.call(2, deps, "_2", [self.for_two])

    def send_far(self, *deps):
        self.across = swap(after(self.two, *deps), "fsdp", 2)

    def mine(self, *deps):
        self.own = self.call(0, deps, "_0", [self.for_own, self.across])

    def send_context(self, *deps):
        self.other = swap(after(self.own, *deps), "context", 1)


def totals_kernel(slots, *refs):
    pairs, out_ref = refs[:-1], refs[-1]
    for slot in range(len(pairs) // 2):
        total = pairs[2 * slot][...].astype(F32) + pairs[2 * slot + 1][...].astype(F32)
        if slots == 0:
            out_ref[slot] = total
        else:
            out_ref[:, slot, :] = total


def totals(sums, slots, *deps):
    arrays = [array for part in sums for array in (part.own, part.other)]
    if deps:
        arrays[0] = after(arrays[0], *deps)
    rows, width = arrays[0].shape
    tile = 128
    shape = [rows, width]
    shape.insert(slots, len(sums))
    block = [tile, width]
    block.insert(slots, len(sums))
    return pl.pallas_call(
        functools.partial(totals_kernel, slots),
        grid=(rows // tile,),
        out_shape=jax.ShapeDtypeStruct(tuple(shape), F32),
        in_specs=[pl.BlockSpec((tile, width), lambda i: (i, 0))] * len(arrays),
        out_specs=pl.BlockSpec(
            tuple(block), (lambda i: (0, i, 0)) if slots == 0 else (lambda i: (i, 0, 0))
        ),
        compiler_params=pltpu.CompilerParams(vmem_limit_bytes=VMEM_BYTES),
        cost_estimate=LIGHT,
        name="totals",
    )(*arrays)


def row_sum(values_in):
    return jnp.sum(values_in, axis=1, keepdims=True)


def per_device(tokens, w_qkv, w_out, w_gate_up, w_down, gains, seq_lengths, cotangent):
    row_count, part_width = tokens.shape
    tensor_index = lax.axis_index("tensor")
    context_index = lax.axis_index("context")
    full_width = part_width * lax.axis_size("tensor")

    def features(part_in):
        return lax.all_gather(part_in, "tensor", axis=1, tiled=True)

    def feature_sum(term):
        return lax.psum_scatter(term.astype(BF), "tensor", scatter_dimension=1, tiled=True)

    def own_features(full):
        return lax.dynamic_slice_in_dim(full, tensor_index * part_width, part_width, 1)

    ending = jnp.cumsum(seq_lengths[0])
    starts = ending - seq_lengths[0]
    places = context_index * row_count + jnp.arange(row_count, dtype=jnp.int32)
    first_token = jnp.max(jnp.where(starts[None, :] <= places[:, None], starts[None, :], 0), axis=1)
    cos, sin = rope_tables(places - first_token)
    low = first_token - context_index * row_count
    low_row = low[None, :]
    need = low[::QROWS]

    token_low = features(tokens)
    gain_near, gain_full = gather_gains(gains)
    gain_attn, gain_mlp = gain_full[0:1], gain_full[1:2]

    qkv_own = jnp.swapaxes(w_qkv, 0, 1)
    half = qkv_own.shape[1] // 2
    far_half = swap(
        lax.dynamic_slice_in_dim(after(qkv_own, gain_near), context_index * half, half, 1),
        "fsdp",
        2,
    )
    other_half = swap(far_half, "context", 1)
    qkv_far = jnp.where(
        context_index == 0,
        jnp.concatenate([far_half, other_half], axis=1),
        jnp.concatenate([other_half, far_half], axis=1),
    )
    qkv_near = swap(qkv_own, "fsdp", 1)
    qkv = (qkv_own, qkv_near, qkv_far, swap(qkv_far, "fsdp", 1))

    gate_up_own = jnp.swapaxes(w_gate_up, 0, 1)
    cut = gate_up_own.shape[1] * 12 // 32
    gate_up_a = swap(after(gate_up_own[:, :cut], far_half), "fsdp", 2)
    gate_up_b = swap(after(gate_up_own[:, cut:], gate_up_a), "fsdp", 2)

    keys_values, normed_in, scale_attn = project(
        after(token_low, gate_up_a), qkv, cos, sin, gain_attn, (1.0, None), 1, True
    )
    peer_kv = lax.ppermute(keys_values, "context", [(0, 1)])
    queries = project(normed_in, qkv, cos, sin, gain_attn, (HDIM**-0.5,), 0, False)[0][0]
    part, part_log = own_forward(queries, keys_values, low_row)
    attended, logs = peer_forward(
        need, queries, peer_kv, low_row, after(part, gate_up_b), part_log
    )
    attended_full = features(attended)

    out_own = after(lax.all_gather(w_out, "tensor", axis=0, tiled=True), attended)
    out_near = swap(out_own, "fsdp", 1)
    out_far = swap(out_own, "fsdp", 2)
    out_far_near = swap(out_far, "fsdp", 1)
    out = (out_own, out_near, out_far, out_far_near)
    gate_up_own, gate_up_a, gate_up_b = lax.optimization_barrier(
        (gate_up_own, gate_up_a, gate_up_b, attended)
    )[:3]
    gate_up_far = jnp.concatenate([gate_up_a, gate_up_b], axis=1)
    gate_up_near = swap(gate_up_own, "fsdp", 1)
    gate_up = (gate_up_own, gate_up_near, gate_up_far, swap(gate_up_far, "fsdp", 1))
    cot_full = features(after(cotangent, attended_full, out_far_near, out_near))
    down_far = swap(after(w_down, attended_full, out_far_near), "fsdp", 2)
    down_near = swap(after(w_down, attended_full), "fsdp", 1)
    hidden, normed_mid, scale_mlp = add_branch(token_low, attended_full, gain_mlp, out)

    activated, by_gate, by_up = hidden_units(normed_mid, gate_up)
    down_far = after(down_far, activated)
    down = (w_down, down_near, down_far, swap(down_far, "fsdp", 1))
    mlp_term = plain_columns(activated, down, "mlp_out")
    mlp_out = feature_sum(mlp_term)
    d_gate, d_up = hidden_back(after(cot_full, mlp_term), by_gate, by_up, down)
    d_mid_term = stacked_columns([d_gate, d_up], gate_up, "d_mid")
    d_hidden_term, d_att_term, gain_mlp_term = branch_back(
        d_mid_term, hidden, cot_full, scale_mlp, gain_mlp, out
    )
    d_attended = feature_sum(after(d_att_term, mlp_out))
    d_hidden_own = feature_sum(after(d_hidden_term, d_att_term))

    down_a, down_b = (
        Reduction(activated, cot_full, 1, "grad_down", (part_index, 2)) for part_index in (0, 1)
    )
    grad_gate = Reduction(normed_mid, d_gate, 0, "grad_gate")
    grad_up = Reduction(normed_mid, d_up, 0, "grad_up")
    square = lax.axis_size("tensor") == lax.axis_size("fsdp")
    down_a.near_far(d_att_term)
    down_b.near_far(down_a.three)
    grad_gate.near_far(down_b.three)
    down_a.far(grad_gate.three)
    down_a.send_far()
    down_b.far(down_a.two)
    down_b.send_far()
    down_a.near(down_b.two)
    down_b.near(down_a.one)
    grad_gate.far(down_b.one)
    grad_gate.send_far()
    grad_gate.near(grad_gate.two)
    down_a.mine(grad_gate.one)
    down_a.send_context()
    grad_up.near_far(down_a.own)

    dq_peer, dkv_peer = peer_backward(
        need, queries, peer_kv, after(d_attended, grad_up.three), attended, low_row, logs
    )
    dkv_in = lax.ppermute(dkv_peer, "context", [(1, 0)])
    d_query, dk_own, dv_own = own_backward(
        queries, keys_values, d_attended, attended, low_row, logs, dq_peer, cos, sin
    )
    grad_query = Reduction(normed_in, d_query, 0, "grad_query")
    grad_up.near(d_query)
    grad_up.far(grad_up.one)
    grad_up.send_far()
    down_b.mine(grad_up.two, dkv_in)
    down_b.send_context()
    d_key, d_value = finish_keys(
        dk_own, dv_own, after(dkv_in, down_b.own, d_hidden_own), cos, sin
    )
    grad_gate.mine(d_value, down_a.other, down_b.other)
    grad_gate.send_context()
    grad_up.mine(grad_gate.own)
    grad_up.send_context()

    if square:
        grad_out = Reduction(attended_full, d_hidden_own, 0, "grad_out")
    else:
        grad_out = Reduction(attended, features(d_hidden_own), 1, "grad_out")
    grad_query.near_far(grad_up.own)
    grad_out.near_far(grad_query.three)
    grad_query.near(grad_out.three)
    grad_out.near(grad_query.one)
    grad_query.far(grad_out.one)
    grad_out.far(grad_query.two)
    d_in_term = stacked_columns(
        [d_query, d_key, after(d_value, grad_out.two, grad_gate.other)], qkv, "d_in"
    )
    d_in = feature_sum(d_in_term).astype(F32)
    grad_query.send_far()
    grad_out.send_far()
    grad_key = Reduction(normed_in, d_key, 0, "grad_key")
    grad_value = Reduction(normed_in, d_value, 0, "grad_value")
    grad_key.near_far(d_in_term)
    grad_value.near_far(grad_key.three)
    grad_key.near(grad_value.three)
    grad_value.near(grad_key.one)
    grad_key.far(grad_value.one)
    grad_key.send_far()
    grad_value.far(grad_key.two)
    grad_value.send_far()
    grad_query.mine(grad_value.two)
    grad_query.send_context()
    grad_out.mine(grad_query.own)
    if square:
        count = lax.axis_size("fsdp")
        across = [(i, (i % count) * count + i // count) for i in range(count * count)]
        grad_out.own = lax.ppermute(grad_out.own, ("fsdp", "tensor"), across)
    grad_out.send_context()
    grad_key.mine(grad_out.own, grad_up.other)
    grad_key.send_context()
    grad_value.mine(grad_key.own)
    grad_value.send_context()

    stream = token_low.astype(F32)
    d_in_wide = after(d_in_term, grad_value.own).astype(F32)
    weighted = d_in_wide * stream
    inner_term = jnp.sum(weighted * gain_attn, axis=1)
    gain_attn_term = jnp.sum(weighted * scale_attn, axis=0)
    parts = lax.axis_size("tensor")
    totals_small = block_totals(
        jnp.concatenate(
            [
                jnp.broadcast_to(inner_term[None, :], (parts, row_count)),
                gain_attn_term.reshape(parts, part_width),
                gain_mlp_term.reshape(parts, part_width),
            ],
            axis=1,
        )[None]
    )
    inner_in = totals_small[0, :row_count][:, None] / full_width
    gain_sums = totals_small[0, row_count:].reshape(2, part_width)
    gain_sums = exchange(gain_sums, "fsdp", 1)
    gain_sums = exchange(gain_sums, "fsdp", 2)
    gain_sums = exchange(gain_sums, "context", 1)
    gain_width = gains.shape[1]
    grad_gains = lax.dynamic_slice_in_dim(
        gain_sums, lax.axis_index("fsdp") * gain_width, gain_width, 1
    )

    grad_down_sum = totals([down_a, down_b], 0, grad_value.own).reshape(w_down.shape)
    grad_gate_up_sum = totals([grad_gate, grad_up], 1, grad_down_sum)
    grad_qkv = totals([grad_query, grad_key, grad_value], 0, grad_gate_up_sum)
    grad_out_sum = totals([grad_out], 0, grad_qkv)[0]

    block_out = (own_features(hidden) + mlp_out.astype(F32)).astype(BF)
    own_tokens = tokens.astype(F32)
    grad_tokens = (
        d_hidden_own.astype(F32)
        + scale_attn * own_features(gain_attn) * d_in
        - own_tokens * scale_attn * scale_attn * scale_attn * inner_in
    ).astype(BF)
    return (
        block_out,
        grad_tokens,
        jnp.swapaxes(grad_qkv, 0, 1),
        grad_out_sum,
        grad_gate_up_sum,
        grad_down_sum,
        grad_gains,
    )


def solution(mesh):
    rows = P(("fsdp", "context"), "tensor")
    inner = P("fsdp", None, "tensor")
    outer = P("tensor", "fsdp")
    gain = P(None, ("tensor", "fsdp"))
    return jax.shard_map(
        per_device,
        mesh=mesh,
        in_specs=(rows, inner, outer, inner, outer, gain, P("fsdp", None), rows),
        out_specs=(rows, rows, inner, outer, inner, outer, gain),
        check_vma=False,
    )
```

```python
import functools

import jax
import jax.numpy as jnp
from jax import lax
from jax.experimental import pallas as pl
from jax.experimental.pallas import tpu as pltpu
from jax.sharding import PartitionSpec as P

HDIM = 64
LANES = 128
QROWS = 256
norm_eps = 1e-05
rope_base = 130000.0
masked_score = -1e30
BF = jnp.bfloat16
F32 = jnp.float32
VMEM_BYTES = 56 * 1024 * 1024
LIGHT = pl.CostEstimate(flops=1, bytes_accessed=1, transcendentals=0)


def dotf(a, b, dims):
    return lax.dot_general(a, b, (dims, ((), ())), preferred_element_type=F32)


NN = ((1,), (0,))
NT = ((1,), (1,))
TN = ((0,), (0,))


def swap(value, axis, bit):
    count = lax.axis_size(axis)
    return lax.ppermute(value, axis, [(i, i ^ bit) for i in range(count)])


def after(value, *others):
    return lax.optimization_barrier((value, *others))[0]


def shifted(value, axis):
    count = lax.axis_size(axis)
    return [
        lax.ppermute(value, axis, [(i, (i + step) % count) for i in range(count)])
        for step in range(1, count)
    ]


def exchange(value, axis, bit):
    return value + swap(value, axis, bit)


def join_kernel(axis, mode, *refs):
    pieces, out_ref = refs[:-1], refs[-1]
    count = len(pieces)
    me = lax.axis_index(axis)
    for step, piece in enumerate(pieces):
        size = piece.shape[1]
        place = (me ^ step) if mode == "xor" else (me - step + count) % count
        out_ref[:, pl.ds(pl.multiple_of(place * size, size), size)] = piece[...]


def join(pieces, axis, mode):
    rows, size = pieces[0].shape
    return pl.pallas_call(
        functools.partial(join_kernel, axis, mode),
        out_shape=jax.ShapeDtypeStruct((rows, size * len(pieces)), pieces[0].dtype),
        cost_estimate=LIGHT,
        name="join",
    )(*pieces)


def gather_gains(gains):
    if lax.axis_size("tensor") > 4 or gains.shape[1] % LANES:
        whole = lax.all_gather(gains, ("tensor", "fsdp"), axis=1, tiled=True).astype(F32)
        return gains, whole
    own = gains.astype(F32)
    part = join([own] + [swap(own, "fsdp", bit) for bit in (1, 2, 3)], "fsdp", "xor")
    return part, join([part] + shifted(part, "tensor"), "tensor", "shift")


def block_totals(blocks):
    count = lax.axis_size("tensor")
    me = lax.axis_index("tensor")
    if count > 4:
        return lax.dynamic_index_in_dim(lax.psum(blocks, "tensor"), me, 1, keepdims=False)

    def pick(place):
        return lax.dynamic_index_in_dim(blocks, place, 1, keepdims=False)

    total = pick(me)
    for step in range(1, count):
        moves = [(i, (i + step) % count) for i in range(count)]
        total = total + lax.ppermute(pick((me + step) % count), "tensor", moves)
    return total


def piece_columns(j, size):
    return pl.ds(pl.multiple_of((lax.axis_index("fsdp") ^ j) * size, size), size)


def swap_halves(block):
    lane = lax.broadcasted_iota(jnp.int32, block.shape, 1)
    up = pltpu.roll(block, LANES - HDIM // 2, 1)
    down = pltpu.roll(block, HDIM // 2, 1)
    return jnp.where((lane & (HDIM - 1)) < HDIM // 2, up, down)


def rope_tables(positions):
    lane = jnp.arange(LANES, dtype=jnp.int32)
    half = lane % (HDIM // 2)
    frequencies = rope_base ** (-2.0 * half.astype(F32) / HDIM)
    angles = positions.astype(F32)[:, None] * frequencies[None, :]
    sign = jnp.where((lane % HDIM) < HDIM // 2, -1.0, 1.0)
    return jnp.cos(angles), jnp.sin(angles) * sign[None, :]


def piece_dot(x_ref, rows, pieces, dims=NN):
    total = None
    for j, piece in enumerate(pieces):
        size = piece.shape[dims[1][0]]
        term = dotf(x_ref[rows, piece_columns(j, size)], piece, dims)
        total = term if total is None else total + term
    return total


def project_kernel(kinds, normalize, x_ref, *refs):
    pieces, (cos_ref, sin_ref, gain_ref), outs = refs[:4], refs[4:7], refs[7:]
    out_ref = outs[0]
    rows, width = out_ref.shape[1:]
    step = pl.program_id(0)
    if normalize:
        normed_ref, scale_ref = outs[1], outs[2]

        @pl.when(step == 0)
        def _():
            for r in range(0, rows, QROWS):
                part = slice(r, r + QROWS)
                stream = x_ref[part, :].astype(F32)
                mean = jnp.sum(stream * stream, axis=1, keepdims=True) / x_ref.shape[1]
                scale = lax.rsqrt(mean + norm_eps)
                scale_ref[part, :] = scale
                normed_ref[part, :] = (stream * scale * gain_ref[...]).astype(BF)

        x_ref = normed_ref
    for index, scale in enumerate(kinds):

        @pl.when(step == index)
        def _():
            for r in range(0, rows, rows):
                part = slice(r, r + rows)
                result = piece_dot(x_ref, part, [piece[0] for piece in pieces])
                for c in range(0, width, LANES):
                    block = result[:, c : c + LANES]
                    if scale:
                        block = block * cos_ref[part, :] + swap_halves(block) * sin_ref[part, :]
                    low = block.astype(BF)
                    if scale and scale != 1.0:
                        low = low * jnp.asarray(scale, BF)
                    out_ref[0, part, c : c + LANES] = low


def project(x, pieces, cos, sin, gain, kinds, first, normalize):
    rows, depth = x.shape
    _, size, width = pieces[0].shape
    flops = 2 * len(kinds) * rows * depth * width
    whole = pl.BlockSpec((rows, depth), lambda i: (0, 0))
    table = pl.BlockSpec((rows, LANES), lambda i: (0, 0))
    out_shape = [jax.ShapeDtypeStruct((len(kinds), rows, width), BF)]
    out_specs = [pl.BlockSpec((1, rows, width), lambda i: (i, 0, 0))]
    if normalize:
        out_shape += [jax.ShapeDtypeStruct((rows, depth), BF), jax.ShapeDtypeStruct((rows, 1), F32)]
        out_specs += [whole, pl.BlockSpec((rows, 1), lambda i: (0, 0))]
    return pl.pallas_call(
        functools.partial(project_kernel, kinds, normalize),
        name="project_kv" if normalize else "project_q",
        grid=(len(kinds),),
        out_shape=out_shape,
        in_specs=[whole]
        + [pl.BlockSpec((1, size, width), lambda i: (i + first, 0, 0))] * 4
        + [table, table, pl.BlockSpec((1, depth), lambda i: (0, 0))],
        out_specs=out_specs,
        compiler_params=pltpu.CompilerParams(vmem_limit_bytes=VMEM_BYTES),
        cost_estimate=LIGHT,
    )(x, *pieces, cos, sin, gain)


def head_mask(block, head):
    lane = lax.broadcasted_iota(jnp.int32, block.shape, 1)
    inside = (lane < HDIM) if head == 0 else (lane >= HDIM)
    return jnp.where(inside, block, jnp.zeros_like(block))


def own_mask(key_count, row0, low_row):
    key = lax.broadcasted_iota(jnp.int32, (key_count, QROWS), 0)
    query = row0 + lax.broadcasted_iota(jnp.int32, (key_count, QROWS), 1)
    return (key >= low_row) & (key <= query)


def peer_mask(key_count, low_row, offset):
    key = lax.broadcasted_iota(jnp.int32, (key_count, QROWS), 0) - offset
    return key >= low_row


def key_windows(need, total):
    counts = list(range(QROWS, total + 1, QROWS))
    for place, count in enumerate(counts):
        chosen = need < 0 if place == 0 else need < -counts[place - 1]
        if count < total:
            chosen = jnp.logical_and(chosen, need >= -count)
        yield count, chosen


def own_forward_kernel(q_ref, k_ref, v_ref, low_ref, out_ref, log_ref):
    rows = q_ref.shape[0]
    v_t = v_ref[...].T
    for r in range(0, rows, QROWS):
        count = r + QROWS
        allowed = own_mask(count, r, low_ref[:, r : r + QROWS])
        keys = k_ref[0:count, :]
        outs = []
        for head in range(LANES // HDIM):
            scores = dotf(keys, head_mask(q_ref[r : r + QROWS, :], head), NT)
            scores = jnp.where(allowed, scores, masked_score)
            peak = jnp.max(scores, axis=0, keepdims=True)
            weights = jnp.exp(scores - peak)
            total = jnp.sum(weights, axis=0, keepdims=True)
            part = dotf(v_t[head * HDIM : (head + 1) * HDIM, 0:count], weights.astype(BF), NN)
            outs.append(part / total)
            log_ref[0, head : head + 1, r : r + QROWS] = peak + jnp.log(total)
        out_ref[r : r + QROWS, :] = jnp.concatenate(outs, axis=0).T


def peer_forward_kernel(
    need_ref, q_ref, k_ref, v_ref, low_ref, part_ref, log_in_ref, out_ref, log_ref
):
    rows = q_ref.shape[0]
    key_total = k_ref.shape[0]
    for index, r in enumerate(range(0, rows, QROWS)):
        for key_count, chosen in key_windows(need_ref[index], key_total):

            @pl.when(chosen)
            def _():
                window = slice(key_total - key_count, key_total)
                v_t = v_ref[window, :].T
                allowed = peer_mask(key_count, low_ref[:, r : r + QROWS], key_count)
                before = part_ref[r : r + QROWS, :].T
                outs = []
                for head in range(LANES // HDIM):
                    scores = dotf(k_ref[window, :], head_mask(q_ref[r : r + QROWS, :], head), NT)
                    scores = jnp.where(allowed, scores, masked_score)
                    log_own = log_in_ref[0, head : head + 1, r : r + QROWS]
                    peak = jnp.maximum(jnp.max(scores, axis=0, keepdims=True), log_own)
                    weights = jnp.exp(scores - peak)
                    own_weight = jnp.exp(log_own - peak)
                    total = jnp.sum(weights, axis=0, keepdims=True) + own_weight
                    rows_h = slice(head * HDIM, (head + 1) * HDIM)
                    part = dotf(v_t[rows_h, :], weights.astype(BF), NN)
                    outs.append((part + before[rows_h, :] * own_weight) / total)
                    log_ref[0, head : head + 1, r : r + QROWS] = peak + jnp.log(total)
                out_ref[r : r + QROWS, :] = jnp.concatenate(outs, axis=0).T.astype(BF)

        @pl.when(need_ref[index] >= 0)
        def _():
            out_ref[r : r + QROWS, :] = part_ref[r : r + QROWS, :].astype(BF)
            log_ref[:, :, r : r + QROWS] = log_in_ref[:, :, r : r + QROWS]


def pair_spec(rows):
    return pl.BlockSpec((rows, LANES), lambda i: (0, i))


def stacked_spec(rows, part):
    return pl.BlockSpec((None, rows, LANES), lambda i: (part, 0, i))


def log_spec(rows):
    return pl.BlockSpec((1, LANES // HDIM, rows), lambda i: (i, 0, 0))


def low_spec(rows):
    return pl.BlockSpec((1, rows), lambda i: (0, 0))


def own_forward(q, kv, low_row):
    rows, width = q.shape
    pairs = width // LANES
    return pl.pallas_call(
        own_forward_kernel,
        name="own_fwd",
        grid=(pairs,),
        out_shape=(
            jax.ShapeDtypeStruct((rows, width), F32),
            jax.ShapeDtypeStruct((pairs, LANES // HDIM, rows), F32),
        ),
        in_specs=[
            pair_spec(rows),
            stacked_spec(rows, 0),
            stacked_spec(rows, 1),
            low_spec(rows),
        ],
        out_specs=(pair_spec(rows), log_spec(rows)),
        compiler_params=pltpu.CompilerParams(vmem_limit_bytes=VMEM_BYTES),
        cost_estimate=LIGHT,
    )(q, kv, kv, low_row)


SMEM_SPEC = pl.BlockSpec(memory_space=pltpu.SMEM)


def peer_forward(need, q, kv, low_row, part, log_in):
    rows, width = q.shape
    pairs = width // LANES
    return pl.pallas_call(
        peer_forward_kernel,
        name="peer_fwd",
        grid=(pairs,),
        out_shape=(
            jax.ShapeDtypeStruct((rows, width), BF),
            jax.ShapeDtypeStruct((pairs, LANES // HDIM, rows), F32),
        ),
        in_specs=[
            SMEM_SPEC,
            pair_spec(rows),
            stacked_spec(rows, 0),
            stacked_spec(rows, 1),
            low_spec(rows),
            pair_spec(rows),
            log_spec(rows),
        ],
        out_specs=(pair_spec(rows), log_spec(rows)),
        compiler_params=pltpu.CompilerParams(vmem_limit_bytes=VMEM_BYTES),
        cost_estimate=LIGHT,
    )(need, q, kv, kv, low_row, part, log_in)


def backward_block(q_rows, k_rows, v_rows, k_t, do_rows, do_o_t, logs, allowed):
    d_query, d_key, d_value = [], None, None
    for head in range(LANES // HDIM):
        rows_h = slice(head * HDIM, (head + 1) * HDIM)
        q_head = head_mask(q_rows, head)
        do_head = head_mask(do_rows, head)
        scores = dotf(k_rows, q_head, NT)
        probs = jnp.exp(jnp.where(allowed, scores, masked_score) - logs[head])
        delta = jnp.sum(do_o_t[rows_h, :], axis=0, keepdims=True)
        d_probs = dotf(v_rows, do_head, NT)
        d_scores = (probs * (d_probs - delta)).astype(BF)
        d_v = dotf(probs.astype(BF), do_head, NN)
        d_k = dotf(d_scores, q_head, NN)
        d_value = d_v if d_value is None else d_value + d_v
        d_key = d_k if d_key is None else d_key + d_k
        d_query.append(dotf(k_t[rows_h, :], d_scores, NN))
    return jnp.concatenate(d_query, axis=0), d_key, d_value


def output_product(do_ref, o_ref, window):
    product = do_ref[window].astype(F32) * o_ref[window].astype(F32)
    return product.T


def peer_backward_kernel(
    need_ref, q_ref, k_ref, v_ref, do_ref, o_ref, low_ref, log_ref, dq_ref, dkv_ref, sums
):
    rows = q_ref.shape[0]
    key_total = k_ref.shape[0]
    sums[...] = jnp.zeros_like(sums)
    for index, r in enumerate(range(0, rows, QROWS)):
        rows_q = (slice(r, r + QROWS), slice(None))
        for key_count, chosen in key_windows(need_ref[index], key_total):

            @pl.when(chosen)
            def _():
                window = slice(key_total - key_count, key_total)
                allowed = peer_mask(key_count, low_ref[:, r : r + QROWS], key_count)
                logs = [log_ref[0, h : h + 1, r : r + QROWS] for h in range(LANES // HDIM)]
                d_query, d_key, d_value = backward_block(
                    q_ref[rows_q],
                    k_ref[window, :],
                    v_ref[window, :],
                    k_ref[window, :].T,
                    do_ref[rows_q],
                    output_product(do_ref, o_ref, rows_q),
                    logs,
                    allowed,
                )
                dq_ref[rows_q] = d_query.T
                sums[0, window] += d_key
                sums[1, window] += d_value

        @pl.when(need_ref[index] >= 0)
        def _():
            dq_ref[rows_q] = jnp.zeros((QROWS, LANES), F32)

    dkv_ref[...] = sums[...].astype(BF)


def peer_backward(need, q, kv, do, o, low_row, logs):
    rows, width = q.shape
    pairs = width // LANES
    return pl.pallas_call(
        peer_backward_kernel,
        name="peer_bwd",
        grid=(pairs,),
        out_shape=(
            jax.ShapeDtypeStruct((rows, width), F32),
            jax.ShapeDtypeStruct((2, rows, width), BF),
        ),
        in_specs=[
            SMEM_SPEC,
            pair_spec(rows),
            stacked_spec(rows, 0),
            stacked_spec(rows, 1),
            pair_spec(rows),
            pair_spec(rows),
            low_spec(rows),
            log_spec(rows),
        ],
        out_specs=(pair_spec(rows), pl.BlockSpec((2, rows, LANES), lambda i: (0, 0, i))),
        scratch_shapes=[pltpu.VMEM((2, rows, LANES), F32)],
        compiler_params=pltpu.CompilerParams(vmem_limit_bytes=VMEM_BYTES),
        cost_estimate=LIGHT,
    )(need, q, kv, kv, do, o, low_row, logs)


def own_backward_kernel(
    q_ref,
    k_ref,
    v_ref,
    do_ref,
    o_ref,
    low_ref,
    log_ref,
    dq_in_ref,
    cos_ref,
    sin_ref,
    dq_ref,
    dk_ref,
    dv_ref,
    sums,
):
    rows = q_ref.shape[0]
    sums[...] = jnp.zeros_like(sums)
    k_t = k_ref[...].T
    for r in range(0, rows, QROWS):
        count = r + QROWS
        window = (slice(r, r + QROWS), slice(None))
        allowed = own_mask(count, r, low_ref[:, r : r + QROWS])
        logs = [log_ref[0, h : h + 1, r : r + QROWS] for h in range(LANES // HDIM)]
        d_query, d_key, d_value = backward_block(
            q_ref[window],
            k_ref[0:count, :],
            v_ref[0:count, :],
            k_t[:, 0:count],
            do_ref[window],
            output_product(do_ref, o_ref, window),
            logs,
            allowed,
        )
        rotated = (d_query.T + dq_in_ref[window]) * (HDIM**-0.5)
        turned = rotated * cos_ref[window] - swap_halves(rotated) * sin_ref[window]
        dq_ref[window] = turned.astype(BF)
        sums[0, 0:count] += d_key
        sums[1, 0:count] += d_value
    dk_ref[...] = sums[0]
    dv_ref[...] = sums[1]


def own_backward(q, kv, do, o, low_row, logs, dq_in, cos, sin):
    rows, width = q.shape
    pairs = width // LANES
    table = pl.BlockSpec((rows, LANES), lambda i: (0, 0))
    return pl.pallas_call(
        own_backward_kernel,
        name="own_bwd",
        grid=(pairs,),
        out_shape=(
            jax.ShapeDtypeStruct((rows, width), BF),
            jax.ShapeDtypeStruct((rows, width), F32),
            jax.ShapeDtypeStruct((rows, width), F32),
        ),
        in_specs=[
            pair_spec(rows),
            stacked_spec(rows, 0),
            stacked_spec(rows, 1),
            pair_spec(rows),
            pair_spec(rows),
            low_spec(rows),
            log_spec(rows),
            pair_spec(rows),
            table,
            table,
        ],
        out_specs=(pair_spec(rows),) * 3,
        scratch_shapes=[pltpu.VMEM((2, rows, LANES), F32)],
        compiler_params=pltpu.CompilerParams(vmem_limit_bytes=VMEM_BYTES),
        cost_estimate=LIGHT,
    )(q, kv, kv, do, o, low_row, logs, dq_in, cos, sin)


def finish_keys_kernel(dk_ref, dv_ref, dk_in_ref, dv_in_ref, cos_ref, sin_ref, dk_out, dv_out):
    total = dk_ref[...] + dk_in_ref[...].astype(F32)
    turned = total * cos_ref[...] - swap_halves(total) * sin_ref[...]
    dk_out[...] = turned.astype(BF)
    dv_out[...] = (dv_ref[...] + dv_in_ref[...].astype(F32)).astype(BF)


def finish_keys(dk, dv, dkv_in, cos, sin):
    rows, width = dk.shape
    pairs = width // LANES
    table = pl.BlockSpec((rows, LANES), lambda i: (0, 0))
    return pl.pallas_call(
        finish_keys_kernel,
        name="finish_keys",
        grid=(pairs,),
        out_shape=(jax.ShapeDtypeStruct((rows, width), BF),) * 2,
        in_specs=[pair_spec(rows), pair_spec(rows), stacked_spec(rows, 0), stacked_spec(rows, 1)]
        + [table, table],
        out_specs=(pair_spec(rows),) * 2,
        cost_estimate=LIGHT,
    )(dk, dv, dkv_in, dkv_in, cos, sin)


def branch_kernel(stream_ref, att_ref, gain_ref, *refs):
    pieces, (hidden_ref, normed_ref, scale_ref) = refs[:4], refs[4:]
    for j, piece in enumerate(pieces):
        columns = piece_columns(j, piece.shape[1])
        term = dotf(att_ref[...], piece[...], NN)
        hidden_ref[:, columns] = stream_ref[:, columns].astype(F32) + term
    hidden = hidden_ref[...]
    mean = jnp.sum(hidden * hidden, axis=1, keepdims=True) / hidden.shape[1]
    scale = lax.rsqrt(mean + norm_eps)
    scale_ref[...] = scale
    normed_ref[...] = (hidden * scale * gain_ref[...]).astype(BF)


def add_branch(stream, att, gain, pieces):
    rows, depth = stream.shape
    heads = att.shape[1]
    tile = pl.BlockSpec((QROWS, depth), lambda i: (i, 0))
    return pl.pallas_call(
        branch_kernel,
        name="branch",
        grid=(rows // QROWS,),
        out_shape=(
            jax.ShapeDtypeStruct((rows, depth), F32),
            jax.ShapeDtypeStruct((rows, depth), BF),
            jax.ShapeDtypeStruct((rows, 1), F32),
        ),
        in_specs=[
            tile,
            pl.BlockSpec((QROWS, heads), lambda i: (i, 0)),
            pl.BlockSpec((1, depth), lambda i: (0, 0)),
        ]
        + [pl.BlockSpec(pieces[0].shape, lambda i: (0, 0))] * 4,
        out_specs=(tile, tile, pl.BlockSpec((QROWS, 1), lambda i: (i, 0))),
        compiler_params=pltpu.CompilerParams(vmem_limit_bytes=VMEM_BYTES),
        cost_estimate=LIGHT,
    )(stream, att, gain, *pieces)


def hidden_kernel(x_ref, *refs):
    w_in, (act_ref, by_gate_ref, by_up_ref) = refs[:4], refs[4:]
    rows = x_ref.shape[0]
    for r in range(0, rows, rows):
        part = slice(r, r + rows)
        gate = piece_dot(x_ref, part, [piece[0] for piece in w_in])
        up = piece_dot(x_ref, part, [piece[1] for piece in w_in])
        sig = jax.nn.sigmoid(gate)
        silu = gate * sig
        act_ref[part, :] = (silu * up).astype(BF)
        by_gate_ref[part, :] = (up * sig * (1.0 + gate * (1.0 - sig))).astype(BF)
        by_up_ref[part, :] = silu.astype(BF)


def hidden_units(x, w_in):
    rows, depth = x.shape
    _, size, units = w_in[0].shape
    tile = 256
    part = pl.BlockSpec((rows, tile), lambda i: (0, i))
    return pl.pallas_call(
        hidden_kernel,
        grid=(units // tile,),
        out_shape=(jax.ShapeDtypeStruct((rows, units), BF),) * 3,
        in_specs=[pl.BlockSpec((rows, depth), lambda i: (0, 0))]
        + [pl.BlockSpec((2, size, tile), lambda i: (0, 0, i))] * 4,
        out_specs=(part,) * 3,
        compiler_params=pltpu.CompilerParams(vmem_limit_bytes=VMEM_BYTES),
        cost_estimate=LIGHT,
        name="hidden",
    )(x, *w_in)


def hidden_back_kernel(cot_ref, by_gate_ref, by_up_ref, *refs):
    w_down, (dg_ref, du_ref) = refs[:4], refs[4:]
    rows = cot_ref.shape[0]
    for r in range(0, rows, rows):
        part = slice(r, r + rows)
        d_act = piece_dot(cot_ref, part, [piece[...] for piece in w_down], NT)
        dg_ref[part, :] = (d_act * by_gate_ref[part, :].astype(F32)).astype(BF)
        du_ref[part, :] = (d_act * by_up_ref[part, :].astype(F32)).astype(BF)


def hidden_back(cot, by_gate, by_up, w_down):
    rows, depth = cot.shape
    units, size = w_down[0].shape
    tile = 256
    part = pl.BlockSpec((rows, tile), lambda i: (0, i))
    return pl.pallas_call(
        hidden_back_kernel,
        grid=(units // tile,),
        out_shape=(jax.ShapeDtypeStruct((rows, units), BF),) * 2,
        in_specs=[pl.BlockSpec((rows, depth), lambda i: (0, 0)), part, part]
        + [pl.BlockSpec((tile, size), lambda i: (i, 0))] * 4,
        out_specs=(part,) * 2,
        compiler_params=pltpu.CompilerParams(vmem_limit_bytes=VMEM_BYTES),
        cost_estimate=LIGHT,
        name="hidden_back",
    )(cot, by_gate, by_up, *w_down)


def phased(i, block, make_index, tiles):
    def index_map(j, t):
        return make_index(jnp.where(j < i, 0, jnp.where(j == i, t, tiles - 1)))

    return pl.BlockSpec(block, index_map)


def columns_call(kernel_dot, lefts, pieces, block, make_index, size, flops, name):
    rows = lefts[0].shape[0]
    tile = min(size, 256)
    tiles = size // tile
    depth = size * 4

    def kernel(*refs):
        left_refs, piece_refs, out_ref = refs[: len(lefts)], refs[len(lefts) : -1], refs[-1]
        for j, piece in enumerate(piece_refs):

            @pl.when(pl.program_id(0) == j)
            def _():
                out_ref[...] = kernel_dot([left[...] for left in left_refs], piece).astype(BF)

    def out_index(j, t):
        return (0, (lax.axis_index("fsdp") ^ j) * tiles + t)

    return pl.pallas_call(
        kernel,
        grid=(4, tiles),
        out_shape=jax.ShapeDtypeStruct((rows, depth), BF),
        in_specs=[pl.BlockSpec(left.shape, lambda j, t: (0, 0)) for left in lefts]
        + [phased(i, block(tile), make_index, tiles) for i in range(4)],
        out_specs=pl.BlockSpec((rows, tile), out_index),
        compiler_params=pltpu.CompilerParams(vmem_limit_bytes=VMEM_BYTES),
        cost_estimate=LIGHT,
        name=name,
    )(*lefts, *pieces)


def stacked_columns(lefts, pieces, name):
    count, size, inner = pieces[0].shape

    def product(parts, piece):
        return sum(dotf(parts[c], piece[c], NT) for c in range(count))

    return columns_call(
        product,
        lefts,
        pieces,
        lambda tile: (count, tile, inner),
        lambda t: (0, t, 0),
        size,
        8 * lefts[0].shape[0] * size * inner * count,
        name,
    )


def plain_columns(left, pieces, name):
    inner, size = pieces[0].shape
    return columns_call(
        lambda parts, piece: dotf(parts[0], piece[...], NN),
        [left],
        pieces,
        lambda tile: (inner, tile),
        lambda t: (0, t),
        size,
        8 * left.shape[0] * size * inner,
        name,
    )


def branch_back_kernel(shares, d_mid_ref, hidden_ref, cot_ref, scale_ref, gain_ref, *refs):
    pieces, (d_hidden_ref, d_att_ref, gain_out_ref) = refs[:4], refs[4:7]
    d_mid = d_mid_ref[...].astype(F32)
    hidden = hidden_ref[...]
    scale = scale_ref[...]
    weighted = d_mid * gain_ref[...]
    inner = jnp.sum(weighted * hidden, axis=1, keepdims=True) / hidden.shape[1]
    d_hidden = (
        cot_ref[...].astype(F32) * (1.0 / shares)
        + scale * weighted
        - hidden * (scale * scale * scale * inner)
    )
    gain_term = jnp.sum(d_mid * hidden * scale, axis=0, keepdims=True)

    @pl.when(pl.program_id(0) == 0)
    def _():
        gain_out_ref[...] = gain_term

    @pl.when(pl.program_id(0) != 0)
    def _():
        gain_out_ref[...] += gain_term

    d_hidden_ref[...] = d_hidden.astype(BF)
    heads = d_att_ref.shape[1]
    for e in range(0, heads, 512):
        columns = slice(e, e + 512)
        d_att_ref[:, columns] = piece_dot(
            d_hidden_ref, slice(None), [piece[columns, :] for piece in pieces], NT
        ).astype(BF)


def branch_back(d_mid, hidden, cot, scale, gain, pieces):
    rows, depth = hidden.shape
    heads, size = pieces[0].shape
    tile = pl.BlockSpec((QROWS, depth), lambda i: (i, 0))
    row = pl.BlockSpec((1, depth), lambda i: (0, 0))
    return pl.pallas_call(
        functools.partial(branch_back_kernel, lax.axis_size("tensor")),
        name="branch_back",
        grid=(rows // QROWS,),
        in_specs=[tile, tile, tile, pl.BlockSpec((QROWS, 1), lambda i: (i, 0)), row]
        + [pl.BlockSpec((heads, size), lambda i: (0, 0))] * 4,
        out_specs=(tile, pl.BlockSpec((QROWS, heads), lambda i: (i, 0)), row),
        out_shape=(
            jax.ShapeDtypeStruct((rows, depth), BF),
            jax.ShapeDtypeStruct((rows, heads), BF),
            jax.ShapeDtypeStruct((1, depth), F32),
        ),
        compiler_params=pltpu.CompilerParams(vmem_limit_bytes=VMEM_BYTES),
        cost_estimate=LIGHT,
    )(d_mid, hidden, cot, scale, gain, *pieces)


def grad_call(left, right, cut, places, adds, name, span=(0, 1)):
    rows = left.shape[0]
    size = (left, right)[cut].shape[1] // 4
    swept = (right, left)[cut].shape[1] // span[1]
    height, width = (size, swept) if cut == 0 else (swept, size)
    tile = min(1024, swept)
    offset = span[0] * (swept // tile)
    block = (height, tile) if cut == 0 else (tile, width)

    def owner(i):
        return lax.axis_index("fsdp") ^ (places[0] + 2 * i)

    def swept_index(t):
        return (0, t) if cut == 0 else (t, 0)

    def kernel(left_ref, right_ref, *refs):
        add_refs, out_ref = refs[: len(adds)], refs[len(adds)]
        if cut == 0:
            turned = refs[-1]

            @pl.when(pl.program_id(1) == 0)
            def _():
                turned[...] = left_ref[...].T

            result = dotf(turned[...], right_ref[...], NN)
        else:
            result = dotf(left_ref[...].T, right_ref[...], NN)
        for add in add_refs:
            result = result + add[...].astype(F32)
        out_ref[...] = result.astype(BF)

    fixed = pl.BlockSpec((rows, size), lambda i, t: (0, owner(i)))
    moving = pl.BlockSpec((rows, tile), lambda i, t: (0, t + offset))
    add_specs = []
    for _, slot in adds:
        if slot is None:
            add_specs.append(pl.BlockSpec(block, lambda i, t: swept_index(t)))
        else:
            add_specs.append(
                pl.BlockSpec((None, *block), lambda i, t, slot=slot: (slot, *swept_index(t)))
            )
    if len(places) > 1:
        out_shape = jax.ShapeDtypeStruct((len(places), height, width), BF)
        out_spec = pl.BlockSpec((None, *block), lambda i, t: (i, *swept_index(t)))
    else:
        out_shape = jax.ShapeDtypeStruct((height, width), BF)
        out_spec = pl.BlockSpec(block, lambda i, t: swept_index(t))
    return pl.pallas_call(
        kernel,
        grid=(len(places), swept // tile),
        out_shape=out_shape,
        in_specs=[fixed, moving] * (cut == 0) + [moving, fixed] * (cut == 1) + add_specs,
        out_specs=out_spec,
        scratch_shapes=[pltpu.VMEM((size, rows), BF)] if cut == 0 else [],
        compiler_params=pltpu.CompilerParams(vmem_limit_bytes=VMEM_BYTES),
        cost_estimate=LIGHT,
        name=name,
    )(left, right, *[array for array, _ in adds])


class Reduction:
    def __init__(self, left, right, cut, name, span=(0, 1)):
        self.args, self.name, self.span = (left, right, cut), name, span

    def call(self, places, deps, step, adds=()):
        left, right, cut = self.args
        left = after(left, *deps) if deps else left
        return grad_call(left, right, cut, places, adds, self.name + step, self.span)

    def near(self, *deps):
        self.sent = self.call((1, 3), deps, "_near")
        self.beside = swap(self.sent, "fsdp", 1)

    def far(self, *deps):
        self.two = self.call((2,), deps, "_far", [(self.beside, 1)])

    def send_far(self, *deps):
        self.across = swap(after(self.two, *deps), "fsdp", 2)

    def mine(self, *deps):
        self.own = self.call((0,), deps, "_own", [(self.beside, 0), (self.across, None)])

    def send_context(self, *deps):
        self.other = swap(after(self.own, *deps), "context", 1)


def totals_kernel(slots, *refs):
    pairs, out_ref = refs[:-1], refs[-1]
    for slot in range(len(pairs) // 2):
        total = pairs[2 * slot][...].astype(F32) + pairs[2 * slot + 1][...].astype(F32)
        if slots == 0:
            out_ref[slot] = total
        else:
            out_ref[:, slot, :] = total


def totals(sums, slots, *deps):
    arrays = [array for part in sums for array in (part.own, part.other)]
    if deps:
        arrays[0] = after(arrays[0], *deps)
    rows, width = arrays[0].shape
    tile = 128
    shape = [rows, width]
    shape.insert(slots, len(sums))
    block = [tile, width]
    block.insert(slots, len(sums))
    return pl.pallas_call(
        functools.partial(totals_kernel, slots),
        grid=(rows // tile,),
        out_shape=jax.ShapeDtypeStruct(tuple(shape), F32),
        in_specs=[pl.BlockSpec((tile, width), lambda i: (i, 0))] * len(arrays),
        out_specs=pl.BlockSpec(
            tuple(block), (lambda i: (0, i, 0)) if slots == 0 else (lambda i: (i, 0, 0))
        ),
        compiler_params=pltpu.CompilerParams(vmem_limit_bytes=VMEM_BYTES),
        cost_estimate=LIGHT,
        name="totals",
    )(*arrays)


def row_sum(values_in):
    return jnp.sum(values_in, axis=1, keepdims=True)


def per_device(tokens, w_qkv, w_out, w_gate_up, w_down, gains, seq_lengths, cotangent):
    row_count, part_width = tokens.shape
    tensor_index = lax.axis_index("tensor")
    context_index = lax.axis_index("context")
    full_width = part_width * lax.axis_size("tensor")

    def features(part_in):
        return lax.all_gather(part_in, "tensor", axis=1, tiled=True)

    def feature_sum(term):
        return lax.psum_scatter(term.astype(BF), "tensor", scatter_dimension=1, tiled=True)

    def own_features(full):
        return lax.dynamic_slice_in_dim(full, tensor_index * part_width, part_width, 1)

    ending = jnp.cumsum(seq_lengths[0])
    starts = ending - seq_lengths[0]
    places = context_index * row_count + jnp.arange(row_count, dtype=jnp.int32)
    first_token = jnp.max(jnp.where(starts[None, :] <= places[:, None], starts[None, :], 0), axis=1)
    cos, sin = rope_tables(places - first_token)
    low = first_token - context_index * row_count
    low_row = low[None, :]
    need = low[::QROWS]

    token_low = features(tokens)
    gain_near, gain_full = gather_gains(gains)
    gain_attn, gain_mlp = gain_full[0:1], gain_full[1:2]

    qkv_own = jnp.swapaxes(w_qkv, 0, 1)
    half = qkv_own.shape[1] // 2
    far_half = swap(
        lax.dynamic_slice_in_dim(after(qkv_own, gain_near), context_index * half, half, 1),
        "fsdp",
        2,
    )
    other_half = swap(far_half, "context", 1)
    qkv_far = jnp.where(
        context_index == 0,
        jnp.concatenate([far_half, other_half], axis=1),
        jnp.concatenate([other_half, far_half], axis=1),
    )
    qkv_near = swap(qkv_own, "fsdp", 1)
    qkv = (qkv_own, qkv_near, qkv_far, swap(qkv_far, "fsdp", 1))

    gate_up_own = jnp.swapaxes(w_gate_up, 0, 1)
    cut = gate_up_own.shape[1] * 12 // 32
    gate_up_a = swap(after(gate_up_own[:, :cut], far_half), "fsdp", 2)
    gate_up_b = swap(after(gate_up_own[:, cut:], gate_up_a), "fsdp", 2)

    keys_values, normed_in, scale_attn = project(
        after(token_low, gate_up_a), qkv, cos, sin, gain_attn, (1.0, None), 1, True
    )
    peer_kv = lax.ppermute(keys_values, "context", [(0, 1)])
    queries = project(normed_in, qkv, cos, sin, gain_attn, (HDIM**-0.5,), 0, False)[0][0]
    part, part_log = own_forward(queries, keys_values, low_row)
    attended, logs = peer_forward(
        need, queries, peer_kv, low_row, after(part, gate_up_b), part_log
    )
    attended_full = features(attended)

    out_own = after(lax.all_gather(w_out, "tensor", axis=0, tiled=True), attended)
    out_near = swap(out_own, "fsdp", 1)
    out_far = swap(out_own, "fsdp", 2)
    out_far_near = swap(out_far, "fsdp", 1)
    out = (out_own, out_near, out_far, out_far_near)
    gate_up_own, gate_up_a, gate_up_b = lax.optimization_barrier(
        (gate_up_own, gate_up_a, gate_up_b, attended)
    )[:3]
    gate_up_far = jnp.concatenate([gate_up_a, gate_up_b], axis=1)
    gate_up_near = swap(gate_up_own, "fsdp", 1)
    gate_up = (gate_up_own, gate_up_near, gate_up_far, swap(gate_up_far, "fsdp", 1))
    cot_full = features(after(cotangent, attended_full, out_far_near, out_near))
    down_far = swap(after(w_down, attended_full, out_far_near), "fsdp", 2)
    down_near = swap(after(w_down, attended_full), "fsdp", 1)
    hidden, normed_mid, scale_mlp = add_branch(token_low, attended_full, gain_mlp, out)

    activated, by_gate, by_up = hidden_units(normed_mid, gate_up)
    down_far = after(down_far, activated)
    down = (w_down, down_near, down_far, swap(down_far, "fsdp", 1))
    mlp_term = plain_columns(activated, down, "mlp_out")
    mlp_out = feature_sum(mlp_term)
    d_gate, d_up = hidden_back(after(cot_full, mlp_term), by_gate, by_up, down)
    d_mid_term = stacked_columns([d_gate, d_up], gate_up, "d_mid")
    d_hidden_term, d_att_term, gain_mlp_term = branch_back(
        d_mid_term, hidden, cot_full, scale_mlp, gain_mlp, out
    )
    d_attended = feature_sum(after(d_att_term, mlp_out))
    d_hidden_own = feature_sum(after(d_hidden_term, d_att_term))

    down_a, down_b = (
        Reduction(activated, cot_full, 1, "grad_down", (part_index, 2)) for part_index in (0, 1)
    )
    grad_gate = Reduction(normed_mid, d_gate, 0, "grad_gate")
    grad_up = Reduction(normed_mid, d_up, 0, "grad_up")
    square = lax.axis_size("tensor") == lax.axis_size("fsdp")
    down_a.near(d_att_term)
    down_b.near(down_a.sent)
    down_a.far(down_b.sent)
    down_a.send_far()
    grad_gate.near(down_a.two)
    down_b.far(grad_gate.sent)
    down_b.send_far()
    grad_gate.far(down_b.two)
    grad_gate.send_far()
    down_a.mine(grad_gate.two)
    down_a.send_context()
    grad_up.near(down_a.own)

    dq_peer, dkv_peer = peer_backward(
        need, queries, peer_kv, after(d_attended, grad_up.sent), attended, low_row, logs
    )
    dkv_in = lax.ppermute(dkv_peer, "context", [(1, 0)])
    d_query, dk_own, dv_own = own_backward(
        queries, keys_values, d_attended, attended, low_row, logs, dq_peer, cos, sin
    )
    grad_query = Reduction(normed_in, d_query, 0, "grad_query")
    grad_up.far(d_query)
    grad_up.send_far()
    down_b.mine(grad_up.two, dkv_in)
    down_b.send_context()
    d_key, d_value = finish_keys(
        dk_own, dv_own, after(dkv_in, down_b.own, d_hidden_own), cos, sin
    )
    grad_gate.mine(d_value, down_a.other, down_b.other)
    grad_gate.send_context()
    grad_up.mine(grad_gate.own)
    grad_up.send_context()

    if square:
        grad_out = Reduction(attended_full, d_hidden_own, 0, "grad_out")
    else:
        grad_out = Reduction(attended, features(d_hidden_own), 1, "grad_out")
    grad_query.near(grad_up.own)
    grad_out.near(grad_query.sent)
    grad_query.far(grad_out.sent)
    grad_out.far(grad_query.two)
    d_in_term = stacked_columns(
        [d_query, d_key, after(d_value, grad_out.two, grad_gate.other)], qkv, "d_in"
    )
    d_in = feature_sum(d_in_term).astype(F32)
    grad_query.send_far()
    grad_out.send_far()
    grad_key = Reduction(normed_in, d_key, 0, "grad_key")
    grad_value = Reduction(normed_in, d_value, 0, "grad_value")
    grad_key.near(d_in_term)
    grad_value.near(grad_key.sent)
    grad_key.far(grad_value.sent)
    grad_key.send_far()
    grad_value.far(grad_key.two)
    grad_value.send_far()
    grad_query.mine(grad_value.two)
    grad_query.send_context()
    grad_out.mine(grad_query.own)
    if square:
        count = lax.axis_size("fsdp")
        across = [(i, (i % count) * count + i // count) for i in range(count * count)]
        grad_out.own = lax.ppermute(grad_out.own, ("fsdp", "tensor"), across)
    grad_out.send_context()
    grad_key.mine(grad_out.own, grad_up.other)
    grad_key.send_context()
    grad_value.mine(grad_key.own, grad_query.other, grad_out.other)
    grad_value.send_context()

    stream = token_low.astype(F32)
    d_in_wide = after(d_in_term, grad_value.own).astype(F32)
    weighted = d_in_wide * stream
    inner_term = jnp.sum(weighted * gain_attn, axis=1)
    gain_attn_term = jnp.sum(weighted * scale_attn, axis=0)
    parts = lax.axis_size("tensor")
    totals_small = block_totals(
        jnp.concatenate(
            [
                jnp.broadcast_to(inner_term[None, :], (parts, row_count)),
                gain_attn_term.reshape(parts, part_width),
                gain_mlp_term.reshape(parts, part_width),
            ],
            axis=1,
        )[None]
    )
    inner_in = totals_small[0, :row_count][:, None] / full_width
    gain_sums = totals_small[0, row_count:].reshape(2, part_width)
    gain_sums = exchange(gain_sums, "fsdp", 1)
    gain_sums = exchange(gain_sums, "fsdp", 2)
    gain_sums = exchange(gain_sums, "context", 1)
    gain_width = gains.shape[1]
    grad_gains = lax.dynamic_slice_in_dim(
        gain_sums, lax.axis_index("fsdp") * gain_width, gain_width, 1
    )

    grad_down_sum = totals([down_a, down_b], 0, grad_value.own).reshape(w_down.shape)
    grad_gate_up_sum = totals([grad_gate, grad_up], 1, grad_down_sum)
    grad_qkv = totals([grad_query, grad_key, grad_value], 0, grad_gate_up_sum)
    grad_out_sum = totals([grad_out], 0, grad_qkv)[0]

    block_out = (own_features(hidden) + mlp_out.astype(F32)).astype(BF)
    own_tokens = tokens.astype(F32)
    grad_tokens = (
        d_hidden_own.astype(F32)
        + scale_attn * own_features(gain_attn) * d_in
        - own_tokens * scale_attn * scale_attn * scale_attn * inner_in
    ).astype(BF)
    return (
        block_out,
        grad_tokens,
        jnp.swapaxes(grad_qkv, 0, 1),
        grad_out_sum,
        grad_gate_up_sum,
        grad_down_sum,
        grad_gains,
    )


def solution(mesh):
    rows = P(("fsdp", "context"), "tensor")
    inner = P("fsdp", None, "tensor")
    outer = P("tensor", "fsdp")
    gain = P(None, ("tensor", "fsdp"))
    return jax.shard_map(
        per_device,
        mesh=mesh,
        in_specs=(rows, inner, outer, inner, outer, gain, P("fsdp", None), rows),
        out_specs=(rows, rows, inner, outer, inner, outer, gain),
        check_vma=False,
    )
```

```python
import functools

import jax
import jax.numpy as jnp
from jax import lax
from jax.experimental import pallas as pl
from jax.experimental.pallas import tpu as pltpu
from jax.sharding import PartitionSpec as P

HDIM = 64
LANES = 128
QROWS = 256
norm_eps = 1e-05
rope_base = 130000.0
masked_score = -1e30
BF = jnp.bfloat16
F32 = jnp.float32
VMEM_BYTES = 56 * 1024 * 1024
LIGHT = pl.CostEstimate(flops=1, bytes_accessed=1, transcendentals=0)


def dotf(a, b, dims):
    return lax.dot_general(a, b, (dims, ((), ())), preferred_element_type=F32)


NN = ((1,), (0,))
NT = ((1,), (1,))
TN = ((0,), (0,))


def swap(value, axis, bit):
    count = lax.axis_size(axis)
    return lax.ppermute(value, axis, [(i, i ^ bit) for i in range(count)])


def after(value, *others):
    return lax.optimization_barrier((value, *others))[0]


def shifted(value, axis):
    count = lax.axis_size(axis)
    return [
        lax.ppermute(value, axis, [(i, (i + step) % count) for i in range(count)])
        for step in range(1, count)
    ]


def exchange(value, axis, bit):
    return value + swap(value, axis, bit)


def join_kernel(axis, mode, *refs):
    pieces, out_ref = refs[:-1], refs[-1]
    count = len(pieces)
    me = lax.axis_index(axis)
    for step, piece in enumerate(pieces):
        size = piece.shape[1]
        place = (me ^ step) if mode == "xor" else (me - step + count) % count
        out_ref[:, pl.ds(pl.multiple_of(place * size, size), size)] = piece[...]


def join(pieces, axis, mode):
    rows, size = pieces[0].shape
    return pl.pallas_call(
        functools.partial(join_kernel, axis, mode),
        out_shape=jax.ShapeDtypeStruct((rows, size * len(pieces)), pieces[0].dtype),
        cost_estimate=LIGHT,
        name="join",
    )(*pieces)


def gather_gains(gains):
    if lax.axis_size("tensor") > 4 or gains.shape[1] % LANES:
        whole = lax.all_gather(gains, ("tensor", "fsdp"), axis=1, tiled=True).astype(F32)
        return gains, whole
    own = gains.astype(F32)
    part = join([own] + [swap(own, "fsdp", bit) for bit in (1, 2, 3)], "fsdp", "xor")
    return part, join([part] + shifted(part, "tensor"), "tensor", "shift")


def block_totals(blocks):
    count = lax.axis_size("tensor")
    me = lax.axis_index("tensor")
    if count > 4:
        return lax.dynamic_index_in_dim(lax.psum(blocks, "tensor"), me, 1, keepdims=False)

    def pick(place):
        return lax.dynamic_index_in_dim(blocks, place, 1, keepdims=False)

    total = pick(me)
    for step in range(1, count):
        moves = [(i, (i + step) % count) for i in range(count)]
        total = total + lax.ppermute(pick((me + step) % count), "tensor", moves)
    return total


def piece_columns(j, size):
    return pl.ds(pl.multiple_of((lax.axis_index("fsdp") ^ j) * size, size), size)


def swap_halves(block):
    lane = lax.broadcasted_iota(jnp.int32, block.shape, 1)
    up = pltpu.roll(block, LANES - HDIM // 2, 1)
    down = pltpu.roll(block, HDIM // 2, 1)
    return jnp.where((lane & (HDIM - 1)) < HDIM // 2, up, down)


def rope_tables(positions):
    lane = jnp.arange(LANES, dtype=jnp.int32)
    half = lane % (HDIM // 2)
    frequencies = rope_base ** (-2.0 * half.astype(F32) / HDIM)
    angles = positions.astype(F32)[:, None] * frequencies[None, :]
    sign = jnp.where((lane % HDIM) < HDIM // 2, -1.0, 1.0)
    return jnp.cos(angles), jnp.sin(angles) * sign[None, :]


def piece_dot(x_ref, rows, pieces, dims=NN):
    total = None
    for j, piece in enumerate(pieces):
        size = piece.shape[dims[1][0]]
        term = dotf(x_ref[rows, piece_columns(j, size)], piece, dims)
        total = term if total is None else total + term
    return total


def project_kernel(kinds, normalize, x_ref, *refs):
    pieces, (cos_ref, sin_ref, gain_ref), outs = refs[:4], refs[4:7], refs[7:]
    out_ref = outs[0]
    rows, width = out_ref.shape[1:]
    step = pl.program_id(0)
    if normalize:
        normed_ref, scale_ref = outs[1], outs[2]

        @pl.when(step == 0)
        def _():
            for r in range(0, rows, QROWS):
                part = slice(r, r + QROWS)
                stream = x_ref[part, :].astype(F32)
                mean = jnp.sum(stream * stream, axis=1, keepdims=True) / x_ref.shape[1]
                scale = lax.rsqrt(mean + norm_eps)
                scale_ref[part, :] = scale
                normed_ref[part, :] = (stream * scale * gain_ref[...]).astype(BF)

        x_ref = normed_ref
    for index, scale in enumerate(kinds):

        @pl.when(step == index)
        def _():
            for r in range(0, rows, rows):
                part = slice(r, r + rows)
                result = piece_dot(x_ref, part, [piece[0] for piece in pieces])
                for c in range(0, width, LANES):
                    block = result[:, c : c + LANES]
                    if scale:
                        block = block * cos_ref[part, :] + swap_halves(block) * sin_ref[part, :]
                    low = block.astype(BF)
                    if scale and scale != 1.0:
                        low = low * jnp.asarray(scale, BF)
                    out_ref[0, part, c : c + LANES] = low


def project(x, pieces, cos, sin, gain, kinds, first, normalize):
    rows, depth = x.shape
    _, size, width = pieces[0].shape
    flops = 2 * len(kinds) * rows * depth * width
    whole = pl.BlockSpec((rows, depth), lambda i: (0, 0))
    table = pl.BlockSpec((rows, LANES), lambda i: (0, 0))
    out_shape = [jax.ShapeDtypeStruct((len(kinds), rows, width), BF)]
    out_specs = [pl.BlockSpec((1, rows, width), lambda i: (i, 0, 0))]
    if normalize:
        out_shape += [jax.ShapeDtypeStruct((rows, depth), BF), jax.ShapeDtypeStruct((rows, 1), F32)]
        out_specs += [whole, pl.BlockSpec((rows, 1), lambda i: (0, 0))]
    return pl.pallas_call(
        functools.partial(project_kernel, kinds, normalize),
        name="project_kv" if normalize else "project_q",
        grid=(len(kinds),),
        out_shape=out_shape,
        in_specs=[whole]
        + [pl.BlockSpec((1, size, width), lambda i: (i + first, 0, 0))] * 4
        + [table, table, pl.BlockSpec((1, depth), lambda i: (0, 0))],
        out_specs=out_specs,
        compiler_params=pltpu.CompilerParams(vmem_limit_bytes=VMEM_BYTES),
        cost_estimate=LIGHT,
    )(x, *pieces, cos, sin, gain)


def head_mask(block, head):
    lane = lax.broadcasted_iota(jnp.int32, block.shape, 1)
    inside = (lane < HDIM) if head == 0 else (lane >= HDIM)
    return jnp.where(inside, block, jnp.zeros_like(block))


def own_mask(key_count, row0, low_row):
    key = lax.broadcasted_iota(jnp.int32, (key_count, QROWS), 0)
    query = row0 + lax.broadcasted_iota(jnp.int32, (key_count, QROWS), 1)
    return (key >= low_row) & (key <= query)


def peer_mask(key_count, low_row, offset):
    key = lax.broadcasted_iota(jnp.int32, (key_count, QROWS), 0) - offset
    return key >= low_row


def key_windows(need, total):
    counts = list(range(QROWS, total + 1, QROWS))
    for place, count in enumerate(counts):
        chosen = need < 0 if place == 0 else need < -counts[place - 1]
        if count < total:
            chosen = jnp.logical_and(chosen, need >= -count)
        yield count, chosen


def own_forward_kernel(q_ref, k_ref, v_ref, low_ref, out_ref, log_ref):
    rows = q_ref.shape[0]
    v_t = v_ref[...].T
    for r in range(0, rows, QROWS):
        count = r + QROWS
        allowed = own_mask(count, r, low_ref[:, r : r + QROWS])
        keys = k_ref[0:count, :]
        outs = []
        for head in range(LANES // HDIM):
            scores = dotf(keys, head_mask(q_ref[r : r + QROWS, :], head), NT)
            scores = jnp.where(allowed, scores, masked_score)
            peak = jnp.max(scores, axis=0, keepdims=True)
            weights = jnp.exp(scores - peak)
            total = jnp.sum(weights, axis=0, keepdims=True)
            part = dotf(v_t[head * HDIM : (head + 1) * HDIM, 0:count], weights.astype(BF), NN)
            outs.append(part / total)
            log_ref[0, head : head + 1, r : r + QROWS] = peak + jnp.log(total)
        out_ref[r : r + QROWS, :] = jnp.concatenate(outs, axis=0).T


def peer_forward_kernel(
    need_ref, q_ref, k_ref, v_ref, low_ref, part_ref, log_in_ref, out_ref, log_ref
):
    rows = q_ref.shape[0]
    key_total = k_ref.shape[0]
    for index, r in enumerate(range(0, rows, QROWS)):
        for key_count, chosen in key_windows(need_ref[index], key_total):

            @pl.when(chosen)
            def _():
                window = slice(key_total - key_count, key_total)
                v_t = v_ref[window, :].T
                allowed = peer_mask(key_count, low_ref[:, r : r + QROWS], key_count)
                before = part_ref[r : r + QROWS, :].T
                outs = []
                for head in range(LANES // HDIM):
                    scores = dotf(k_ref[window, :], head_mask(q_ref[r : r + QROWS, :], head), NT)
                    scores = jnp.where(allowed, scores, masked_score)
                    log_own = log_in_ref[0, head : head + 1, r : r + QROWS]
                    peak = jnp.maximum(jnp.max(scores, axis=0, keepdims=True), log_own)
                    weights = jnp.exp(scores - peak)
                    own_weight = jnp.exp(log_own - peak)
                    total = jnp.sum(weights, axis=0, keepdims=True) + own_weight
                    rows_h = slice(head * HDIM, (head + 1) * HDIM)
                    part = dotf(v_t[rows_h, :], weights.astype(BF), NN)
                    outs.append((part + before[rows_h, :] * own_weight) / total)
                    log_ref[0, head : head + 1, r : r + QROWS] = peak + jnp.log(total)
                out_ref[r : r + QROWS, :] = jnp.concatenate(outs, axis=0).T.astype(BF)

        @pl.when(need_ref[index] >= 0)
        def _():
            out_ref[r : r + QROWS, :] = part_ref[r : r + QROWS, :].astype(BF)
            log_ref[:, :, r : r + QROWS] = log_in_ref[:, :, r : r + QROWS]


def pair_spec(rows):
    return pl.BlockSpec((rows, LANES), lambda i: (0, i))


def stacked_spec(rows, part):
    return pl.BlockSpec((None, rows, LANES), lambda i: (part, 0, i))


def log_spec(rows):
    return pl.BlockSpec((1, LANES // HDIM, rows), lambda i: (i, 0, 0))


def low_spec(rows):
    return pl.BlockSpec((1, rows), lambda i: (0, 0))


def own_forward(q, kv, low_row):
    rows, width = q.shape
    pairs = width // LANES
    return pl.pallas_call(
        own_forward_kernel,
        name="own_fwd",
        grid=(pairs,),
        out_shape=(
            jax.ShapeDtypeStruct((rows, width), F32),
            jax.ShapeDtypeStruct((pairs, LANES // HDIM, rows), F32),
        ),
        in_specs=[
            pair_spec(rows),
            stacked_spec(rows, 0),
            stacked_spec(rows, 1),
            low_spec(rows),
        ],
        out_specs=(pair_spec(rows), log_spec(rows)),
        compiler_params=pltpu.CompilerParams(vmem_limit_bytes=VMEM_BYTES),
        cost_estimate=LIGHT,
    )(q, kv, kv, low_row)


SMEM_SPEC = pl.BlockSpec(memory_space=pltpu.SMEM)


def peer_forward(need, q, kv, low_row, part, log_in):
    rows, width = q.shape
    pairs = width // LANES
    return pl.pallas_call(
        peer_forward_kernel,
        name="peer_fwd",
        grid=(pairs,),
        out_shape=(
            jax.ShapeDtypeStruct((rows, width), BF),
            jax.ShapeDtypeStruct((pairs, LANES // HDIM, rows), F32),
        ),
        in_specs=[
            SMEM_SPEC,
            pair_spec(rows),
            stacked_spec(rows, 0),
            stacked_spec(rows, 1),
            low_spec(rows),
            pair_spec(rows),
            log_spec(rows),
        ],
        out_specs=(pair_spec(rows), log_spec(rows)),
        compiler_params=pltpu.CompilerParams(vmem_limit_bytes=VMEM_BYTES),
        cost_estimate=LIGHT,
    )(need, q, kv, kv, low_row, part, log_in)


def backward_block(q_rows, k_rows, v_rows, k_t, do_rows, do_o_t, logs, allowed):
    d_query, d_key, d_value = [], None, None
    for head in range(LANES // HDIM):
        rows_h = slice(head * HDIM, (head + 1) * HDIM)
        q_head = head_mask(q_rows, head)
        do_head = head_mask(do_rows, head)
        scores = dotf(k_rows, q_head, NT)
        probs = jnp.exp(jnp.where(allowed, scores, masked_score) - logs[head])
        delta = jnp.sum(do_o_t[rows_h, :], axis=0, keepdims=True)
        d_probs = dotf(v_rows, do_head, NT)
        d_scores = (probs * (d_probs - delta)).astype(BF)
        d_v = dotf(probs.astype(BF), do_head, NN)
        d_k = dotf(d_scores, q_head, NN)
        d_value = d_v if d_value is None else d_value + d_v
        d_key = d_k if d_key is None else d_key + d_k
        d_query.append(dotf(k_t[rows_h, :], d_scores, NN))
    return jnp.concatenate(d_query, axis=0), d_key, d_value


def output_product(do_ref, o_ref, window):
    product = do_ref[window].astype(F32) * o_ref[window].astype(F32)
    return product.T


def peer_backward_kernel(
    need_ref, q_ref, k_ref, v_ref, do_ref, o_ref, low_ref, log_ref, dq_ref, dkv_ref, sums
):
    rows = q_ref.shape[0]
    key_total = k_ref.shape[0]
    sums[...] = jnp.zeros_like(sums)
    for index, r in enumerate(range(0, rows, QROWS)):
        rows_q = (slice(r, r + QROWS), slice(None))
        for key_count, chosen in key_windows(need_ref[index], key_total):

            @pl.when(chosen)
            def _():
                window = slice(key_total - key_count, key_total)
                allowed = peer_mask(key_count, low_ref[:, r : r + QROWS], key_count)
                logs = [log_ref[0, h : h + 1, r : r + QROWS] for h in range(LANES // HDIM)]
                d_query, d_key, d_value = backward_block(
                    q_ref[rows_q],
                    k_ref[window, :],
                    v_ref[window, :],
                    k_ref[window, :].T,
                    do_ref[rows_q],
                    output_product(do_ref, o_ref, rows_q),
                    logs,
                    allowed,
                )
                dq_ref[rows_q] = d_query.T
                sums[0, window] += d_key
                sums[1, window] += d_value

        @pl.when(need_ref[index] >= 0)
        def _():
            dq_ref[rows_q] = jnp.zeros((QROWS, LANES), F32)

    dkv_ref[...] = sums[...].astype(BF)


def peer_backward(need, q, kv, do, o, low_row, logs):
    rows, width = q.shape
    pairs = width // LANES
    return pl.pallas_call(
        peer_backward_kernel,
        name="peer_bwd",
        grid=(pairs,),
        out_shape=(
            jax.ShapeDtypeStruct((rows, width), F32),
            jax.ShapeDtypeStruct((2, rows, width), BF),
        ),
        in_specs=[
            SMEM_SPEC,
            pair_spec(rows),
            stacked_spec(rows, 0),
            stacked_spec(rows, 1),
            pair_spec(rows),
            pair_spec(rows),
            low_spec(rows),
            log_spec(rows),
        ],
        out_specs=(pair_spec(rows), pl.BlockSpec((2, rows, LANES), lambda i: (0, 0, i))),
        scratch_shapes=[pltpu.VMEM((2, rows, LANES), F32)],
        compiler_params=pltpu.CompilerParams(vmem_limit_bytes=VMEM_BYTES),
        cost_estimate=LIGHT,
    )(need, q, kv, kv, do, o, low_row, logs)


def own_backward_kernel(
    q_ref,
    k_ref,
    v_ref,
    do_ref,
    o_ref,
    low_ref,
    log_ref,
    dq_in_ref,
    cos_ref,
    sin_ref,
    dq_ref,
    dk_ref,
    dv_ref,
    sums,
):
    rows = q_ref.shape[0]
    sums[...] = jnp.zeros_like(sums)
    k_t = k_ref[...].T
    for r in range(0, rows, QROWS):
        count = r + QROWS
        window = (slice(r, r + QROWS), slice(None))
        allowed = own_mask(count, r, low_ref[:, r : r + QROWS])
        logs = [log_ref[0, h : h + 1, r : r + QROWS] for h in range(LANES // HDIM)]
        d_query, d_key, d_value = backward_block(
            q_ref[window],
            k_ref[0:count, :],
            v_ref[0:count, :],
            k_t[:, 0:count],
            do_ref[window],
            output_product(do_ref, o_ref, window),
            logs,
            allowed,
        )
        rotated = (d_query.T + dq_in_ref[window]) * (HDIM**-0.5)
        turned = rotated * cos_ref[window] - swap_halves(rotated) * sin_ref[window]
        dq_ref[window] = turned.astype(BF)
        sums[0, 0:count] += d_key
        sums[1, 0:count] += d_value
    dk_ref[...] = sums[0]
    dv_ref[...] = sums[1]


def own_backward(q, kv, do, o, low_row, logs, dq_in, cos, sin):
    rows, width = q.shape
    pairs = width // LANES
    table = pl.BlockSpec((rows, LANES), lambda i: (0, 0))
    return pl.pallas_call(
        own_backward_kernel,
        name="own_bwd",
        grid=(pairs,),
        out_shape=(
            jax.ShapeDtypeStruct((rows, width), BF),
            jax.ShapeDtypeStruct((rows, width), F32),
            jax.ShapeDtypeStruct((rows, width), F32),
        ),
        in_specs=[
            pair_spec(rows),
            stacked_spec(rows, 0),
            stacked_spec(rows, 1),
            pair_spec(rows),
            pair_spec(rows),
            low_spec(rows),
            log_spec(rows),
            pair_spec(rows),
            table,
            table,
        ],
        out_specs=(pair_spec(rows),) * 3,
        scratch_shapes=[pltpu.VMEM((2, rows, LANES), F32)],
        compiler_params=pltpu.CompilerParams(vmem_limit_bytes=VMEM_BYTES),
        cost_estimate=LIGHT,
    )(q, kv, kv, do, o, low_row, logs, dq_in, cos, sin)


def finish_keys_kernel(dk_ref, dv_ref, dk_in_ref, dv_in_ref, cos_ref, sin_ref, dk_out, dv_out):
    total = dk_ref[...] + dk_in_ref[...].astype(F32)
    turned = total * cos_ref[...] - swap_halves(total) * sin_ref[...]
    dk_out[...] = turned.astype(BF)
    dv_out[...] = (dv_ref[...] + dv_in_ref[...].astype(F32)).astype(BF)


def finish_keys(dk, dv, dkv_in, cos, sin):
    rows, width = dk.shape
    pairs = width // LANES
    table = pl.BlockSpec((rows, LANES), lambda i: (0, 0))
    return pl.pallas_call(
        finish_keys_kernel,
        name="finish_keys",
        grid=(pairs,),
        out_shape=(jax.ShapeDtypeStruct((rows, width), BF),) * 2,
        in_specs=[pair_spec(rows), pair_spec(rows), stacked_spec(rows, 0), stacked_spec(rows, 1)]
        + [table, table],
        out_specs=(pair_spec(rows),) * 2,
        cost_estimate=LIGHT,
    )(dk, dv, dkv_in, dkv_in, cos, sin)


def branch_kernel(stream_ref, att_ref, gain_ref, *refs):
    pieces, (hidden_ref, normed_ref, scale_ref) = refs[:4], refs[4:]
    for j, piece in enumerate(pieces):
        columns = piece_columns(j, piece.shape[1])
        term = dotf(att_ref[...], piece[...], NN)
        hidden_ref[:, columns] = stream_ref[:, columns].astype(F32) + term
    hidden = hidden_ref[...]
    mean = jnp.sum(hidden * hidden, axis=1, keepdims=True) / hidden.shape[1]
    scale = lax.rsqrt(mean + norm_eps)
    scale_ref[...] = scale
    normed_ref[...] = (hidden * scale * gain_ref[...]).astype(BF)


def add_branch(stream, att, gain, pieces):
    rows, depth = stream.shape
    heads = att.shape[1]
    tile = pl.BlockSpec((QROWS, depth), lambda i: (i, 0))
    return pl.pallas_call(
        branch_kernel,
        name="branch",
        grid=(rows // QROWS,),
        out_shape=(
            jax.ShapeDtypeStruct((rows, depth), F32),
            jax.ShapeDtypeStruct((rows, depth), BF),
            jax.ShapeDtypeStruct((rows, 1), F32),
        ),
        in_specs=[
            tile,
            pl.BlockSpec((QROWS, heads), lambda i: (i, 0)),
            pl.BlockSpec((1, depth), lambda i: (0, 0)),
        ]
        + [pl.BlockSpec(pieces[0].shape, lambda i: (0, 0))] * 4,
        out_specs=(tile, tile, pl.BlockSpec((QROWS, 1), lambda i: (i, 0))),
        compiler_params=pltpu.CompilerParams(vmem_limit_bytes=VMEM_BYTES),
        cost_estimate=LIGHT,
    )(stream, att, gain, *pieces)


def hidden_kernel(x_ref, *refs):
    w_in, (act_ref, by_gate_ref, by_up_ref) = refs[:4], refs[4:]
    rows = x_ref.shape[0]
    for r in range(0, rows, rows):
        part = slice(r, r + rows)
        gate = piece_dot(x_ref, part, [piece[0] for piece in w_in])
        up = piece_dot(x_ref, part, [piece[1] for piece in w_in])
        sig = jax.nn.sigmoid(gate)
        silu = gate * sig
        act_ref[part, :] = (silu * up).astype(BF)
        by_gate_ref[part, :] = (up * sig * (1.0 + gate * (1.0 - sig))).astype(BF)
        by_up_ref[part, :] = silu.astype(BF)


def hidden_units(x, w_in):
    rows, depth = x.shape
    _, size, units = w_in[0].shape
    tile = 256
    part = pl.BlockSpec((rows, tile), lambda i: (0, i))
    return pl.pallas_call(
        hidden_kernel,
        grid=(units // tile,),
        out_shape=(jax.ShapeDtypeStruct((rows, units), BF),) * 3,
        in_specs=[pl.BlockSpec((rows, depth), lambda i: (0, 0))]
        + [pl.BlockSpec((2, size, tile), lambda i: (0, 0, i))] * 4,
        out_specs=(part,) * 3,
        compiler_params=pltpu.CompilerParams(vmem_limit_bytes=VMEM_BYTES),
        cost_estimate=LIGHT,
        name="hidden",
    )(x, *w_in)


def hidden_back_kernel(cot_ref, by_gate_ref, by_up_ref, *refs):
    w_down, (dg_ref, du_ref) = refs[:4], refs[4:]
    rows = cot_ref.shape[0]
    for r in range(0, rows, rows):
        part = slice(r, r + rows)
        d_act = piece_dot(cot_ref, part, [piece[...] for piece in w_down], NT)
        dg_ref[part, :] = (d_act * by_gate_ref[part, :].astype(F32)).astype(BF)
        du_ref[part, :] = (d_act * by_up_ref[part, :].astype(F32)).astype(BF)


def hidden_back(cot, by_gate, by_up, w_down):
    rows, depth = cot.shape
    units, size = w_down[0].shape
    tile = 256
    part = pl.BlockSpec((rows, tile), lambda i: (0, i))
    return pl.pallas_call(
        hidden_back_kernel,
        grid=(units // tile,),
        out_shape=(jax.ShapeDtypeStruct((rows, units), BF),) * 2,
        in_specs=[pl.BlockSpec((rows, depth), lambda i: (0, 0)), part, part]
        + [pl.BlockSpec((tile, size), lambda i: (i, 0))] * 4,
        out_specs=(part,) * 2,
        compiler_params=pltpu.CompilerParams(vmem_limit_bytes=VMEM_BYTES),
        cost_estimate=LIGHT,
        name="hidden_back",
    )(cot, by_gate, by_up, *w_down)


def phased(i, block, make_index, tiles):
    def index_map(j, t):
        return make_index(jnp.where(j < i, 0, jnp.where(j == i, t, tiles - 1)))

    return pl.BlockSpec(block, index_map)


def columns_call(kernel_dot, lefts, pieces, block, make_index, size, flops, name):
    rows = lefts[0].shape[0]
    tile = min(size, 256)
    tiles = size // tile
    depth = size * 4

    def kernel(*refs):
        left_refs, piece_refs, out_ref = refs[: len(lefts)], refs[len(lefts) : -1], refs[-1]
        for j, piece in enumerate(piece_refs):

            @pl.when(pl.program_id(0) == j)
            def _():
                out_ref[...] = kernel_dot([left[...] for left in left_refs], piece).astype(BF)

    def out_index(j, t):
        return (0, (lax.axis_index("fsdp") ^ j) * tiles + t)

    return pl.pallas_call(
        kernel,
        grid=(4, tiles),
        out_shape=jax.ShapeDtypeStruct((rows, depth), BF),
        in_specs=[pl.BlockSpec(left.shape, lambda j, t: (0, 0)) for left in lefts]
        + [phased(i, block(tile), make_index, tiles) for i in range(4)],
        out_specs=pl.BlockSpec((rows, tile), out_index),
        compiler_params=pltpu.CompilerParams(vmem_limit_bytes=VMEM_BYTES),
        cost_estimate=LIGHT,
        name=name,
    )(*lefts, *pieces)


def stacked_columns(lefts, pieces, name):
    count, size, inner = pieces[0].shape

    def product(parts, piece):
        return sum(dotf(parts[c], piece[c], NT) for c in range(count))

    return columns_call(
        product,
        lefts,
        pieces,
        lambda tile: (count, tile, inner),
        lambda t: (0, t, 0),
        size,
        8 * lefts[0].shape[0] * size * inner * count,
        name,
    )


def plain_columns(left, pieces, name):
    inner, size = pieces[0].shape
    return columns_call(
        lambda parts, piece: dotf(parts[0], piece[...], NN),
        [left],
        pieces,
        lambda tile: (inner, tile),
        lambda t: (0, t),
        size,
        8 * left.shape[0] * size * inner,
        name,
    )


def branch_back_kernel(shares, d_mid_ref, hidden_ref, cot_ref, scale_ref, gain_ref, *refs):
    pieces, (d_hidden_ref, d_att_ref, gain_out_ref) = refs[:4], refs[4:7]
    d_mid = d_mid_ref[...].astype(F32)
    hidden = hidden_ref[...]
    scale = scale_ref[...]
    weighted = d_mid * gain_ref[...]
    inner = jnp.sum(weighted * hidden, axis=1, keepdims=True) / hidden.shape[1]
    d_hidden = (
        cot_ref[...].astype(F32) * (1.0 / shares)
        + scale * weighted
        - hidden * (scale * scale * scale * inner)
    )
    gain_term = jnp.sum(d_mid * hidden * scale, axis=0, keepdims=True)

    @pl.when(pl.program_id(0) == 0)
    def _():
        gain_out_ref[...] = gain_term

    @pl.when(pl.program_id(0) != 0)
    def _():
        gain_out_ref[...] += gain_term

    d_hidden_ref[...] = d_hidden.astype(BF)
    heads = d_att_ref.shape[1]
    for e in range(0, heads, 512):
        columns = slice(e, e + 512)
        d_att_ref[:, columns] = piece_dot(
            d_hidden_ref, slice(None), [piece[columns, :] for piece in pieces], NT
        ).astype(BF)


def branch_back(d_mid, hidden, cot, scale, gain, pieces):
    rows, depth = hidden.shape
    heads, size = pieces[0].shape
    tile = pl.BlockSpec((QROWS, depth), lambda i: (i, 0))
    row = pl.BlockSpec((1, depth), lambda i: (0, 0))
    return pl.pallas_call(
        functools.partial(branch_back_kernel, lax.axis_size("tensor")),
        name="branch_back",
        grid=(rows // QROWS,),
        in_specs=[tile, tile, tile, pl.BlockSpec((QROWS, 1), lambda i: (i, 0)), row]
        + [pl.BlockSpec((heads, size), lambda i: (0, 0))] * 4,
        out_specs=(tile, pl.BlockSpec((QROWS, heads), lambda i: (i, 0)), row),
        out_shape=(
            jax.ShapeDtypeStruct((rows, depth), BF),
            jax.ShapeDtypeStruct((rows, heads), BF),
            jax.ShapeDtypeStruct((1, depth), F32),
        ),
        compiler_params=pltpu.CompilerParams(vmem_limit_bytes=VMEM_BYTES),
        cost_estimate=LIGHT,
    )(d_mid, hidden, cot, scale, gain, *pieces)


def grad_call(left, right, cut, places, adds, name, span=(0, 1)):
    rows = left.shape[0]
    size = (left, right)[cut].shape[1] // 4
    swept = (right, left)[cut].shape[1] // span[1]
    height, width = (size, swept) if cut == 0 else (swept, size)
    tile = swept if swept <= 1024 else 1024 if swept % 1024 == 0 else 512
    offset = span[0] * (swept // tile)
    block = (height, tile) if cut == 0 else (tile, width)

    def owner(i):
        return lax.axis_index("fsdp") ^ (places[0] + 2 * i)

    def swept_index(t):
        return (0, t) if cut == 0 else (t, 0)

    def kernel(left_ref, right_ref, *refs):
        add_refs, out_ref = refs[: len(adds)], refs[len(adds)]
        if cut == 0:
            turned = refs[-1]

            @pl.when(pl.program_id(1) == 0)
            def _():
                turned[...] = left_ref[...].T

            result = dotf(turned[...], right_ref[...], NN)
        else:
            result = dotf(left_ref[...].T, right_ref[...], NN)
        for add in add_refs:
            result = result + add[...].astype(F32)
        out_ref[...] = result.astype(BF)

    fixed = pl.BlockSpec((rows, size), lambda i, t: (0, owner(i)))
    moving = pl.BlockSpec((rows, tile), lambda i, t: (0, t + offset))
    add_specs = []
    for _, slot in adds:
        if slot is None:
            add_specs.append(pl.BlockSpec(block, lambda i, t: swept_index(t)))
        else:
            add_specs.append(
                pl.BlockSpec((None, *block), lambda i, t, slot=slot: (slot, *swept_index(t)))
            )
    if len(places) > 1:
        out_shape = jax.ShapeDtypeStruct((len(places), height, width), BF)
        out_spec = pl.BlockSpec((None, *block), lambda i, t: (i, *swept_index(t)))
    else:
        out_shape = jax.ShapeDtypeStruct((height, width), BF)
        out_spec = pl.BlockSpec(block, lambda i, t: swept_index(t))
    return pl.pallas_call(
        kernel,
        grid=(len(places), swept // tile),
        out_shape=out_shape,
        in_specs=[fixed, moving] * (cut == 0) + [moving, fixed] * (cut == 1) + add_specs,
        out_specs=out_spec,
        scratch_shapes=[pltpu.VMEM((size, rows), BF)] if cut == 0 else [],
        compiler_params=pltpu.CompilerParams(vmem_limit_bytes=VMEM_BYTES),
        cost_estimate=LIGHT,
        name=name,
    )(left, right, *[array for array, _ in adds])


class Reduction:
    def __init__(self, left, right, cut, name, span=(0, 1)):
        self.args, self.name, self.span = (left, right, cut), name, span

    def call(self, places, deps, step, adds=()):
        left, right, cut = self.args
        left = after(left, *deps) if deps else left
        return grad_call(left, right, cut, places, adds, self.name + step, self.span)

    def near(self, *deps):
        self.sent = self.call((1, 3), deps, "_near")
        self.beside = swap(self.sent, "fsdp", 1)

    def far(self, *deps):
        self.two = self.call((2,), deps, "_far", [(self.beside, 1)])

    def send_far(self, *deps):
        self.across = swap(after(self.two, *deps), "fsdp", 2)

    def mine(self, *deps):
        self.own = self.call((0,), deps, "_own", [(self.beside, 0), (self.across, None)])

    def send_context(self, *deps):
        self.other = swap(after(self.own, *deps), "context", 1)


def totals_kernel(slots, *refs):
    pairs, out_ref = refs[:-1], refs[-1]
    for slot in range(len(pairs) // 2):
        total = pairs[2 * slot][...].astype(F32) + pairs[2 * slot + 1][...].astype(F32)
        if slots == 0:
            out_ref[slot] = total
        else:
            out_ref[:, slot, :] = total


def totals(sums, slots, *deps):
    arrays = [array for part in sums for array in (part.own, part.other)]
    if deps:
        arrays[0] = after(arrays[0], *deps)
    rows, width = arrays[0].shape
    tile = 128
    shape = [rows, width]
    shape.insert(slots, len(sums))
    block = [tile, width]
    block.insert(slots, len(sums))
    return pl.pallas_call(
        functools.partial(totals_kernel, slots),
        grid=(rows // tile,),
        out_shape=jax.ShapeDtypeStruct(tuple(shape), F32),
        in_specs=[pl.BlockSpec((tile, width), lambda i: (i, 0))] * len(arrays),
        out_specs=pl.BlockSpec(
            tuple(block), (lambda i: (0, i, 0)) if slots == 0 else (lambda i: (i, 0, 0))
        ),
        compiler_params=pltpu.CompilerParams(vmem_limit_bytes=VMEM_BYTES),
        cost_estimate=LIGHT,
        name="totals",
    )(*arrays)


def split_totals_kernel(own_ref, other_ref, out_ref):
    width = out_ref.shape[2]
    for slot in range(out_ref.shape[0]):
        columns = slice(slot * width, (slot + 1) * width)
        out_ref[slot] = own_ref[:, columns].astype(F32) + other_ref[:, columns].astype(F32)


def split_totals(part, count, *deps):
    own = after(part.own, *deps)
    rows, width = own.shape
    tile = 128
    return pl.pallas_call(
        split_totals_kernel,
        grid=(rows // tile,),
        out_shape=jax.ShapeDtypeStruct((count, rows, width // count), F32),
        in_specs=[pl.BlockSpec((tile, width), lambda i: (i, 0))] * 2,
        out_specs=pl.BlockSpec((count, tile, width // count), lambda i: (0, i, 0)),
        compiler_params=pltpu.CompilerParams(vmem_limit_bytes=VMEM_BYTES),
        cost_estimate=LIGHT,
        name="split_totals",
    )(own, part.other)


def row_sum(values_in):
    return jnp.sum(values_in, axis=1, keepdims=True)


def per_device(tokens, w_qkv, w_out, w_gate_up, w_down, gains, seq_lengths, cotangent):
    row_count, part_width = tokens.shape
    tensor_index = lax.axis_index("tensor")
    context_index = lax.axis_index("context")
    full_width = part_width * lax.axis_size("tensor")

    def features(part_in):
        return lax.all_gather(part_in, "tensor", axis=1, tiled=True)

    def feature_sum(term):
        return lax.psum_scatter(term.astype(BF), "tensor", scatter_dimension=1, tiled=True)

    def own_features(full):
        return lax.dynamic_slice_in_dim(full, tensor_index * part_width, part_width, 1)

    ending = jnp.cumsum(seq_lengths[0])
    starts = ending - seq_lengths[0]
    places = context_index * row_count + jnp.arange(row_count, dtype=jnp.int32)
    first_token = jnp.max(jnp.where(starts[None, :] <= places[:, None], starts[None, :], 0), axis=1)
    cos, sin = rope_tables(places - first_token)
    low = first_token - context_index * row_count
    low_row = low[None, :]
    need = low[::QROWS]

    token_low = features(tokens)
    gain_near, gain_full = gather_gains(gains)
    gain_attn, gain_mlp = gain_full[0:1], gain_full[1:2]

    qkv_own = jnp.swapaxes(w_qkv, 0, 1)
    half = qkv_own.shape[1] // 2
    far_half = swap(
        lax.dynamic_slice_in_dim(after(qkv_own, gain_near), context_index * half, half, 1),
        "fsdp",
        2,
    )
    other_half = swap(far_half, "context", 1)
    qkv_far = jnp.where(
        context_index == 0,
        jnp.concatenate([far_half, other_half], axis=1),
        jnp.concatenate([other_half, far_half], axis=1),
    )
    qkv_near = swap(qkv_own, "fsdp", 1)
    qkv = (qkv_own, qkv_near, qkv_far, swap(qkv_far, "fsdp", 1))

    gate_up_own = jnp.swapaxes(w_gate_up, 0, 1)
    cut = gate_up_own.shape[1] * 12 // 32
    gate_up_a = swap(after(gate_up_own[:, :cut], far_half), "fsdp", 2)
    gate_up_b = swap(after(gate_up_own[:, cut:], gate_up_a), "fsdp", 2)

    keys_values, normed_in, scale_attn = project(
        after(token_low, gate_up_a), qkv, cos, sin, gain_attn, (1.0, None), 1, True
    )
    peer_kv = lax.ppermute(keys_values, "context", [(0, 1)])
    queries = project(normed_in, qkv, cos, sin, gain_attn, (HDIM**-0.5,), 0, False)[0][0]
    part, part_log = own_forward(queries, keys_values, low_row)
    attended, logs = peer_forward(
        need, queries, peer_kv, low_row, after(part, gate_up_b), part_log
    )
    attended_full = features(attended)

    out_own = after(lax.all_gather(w_out, "tensor", axis=0, tiled=True), attended)
    out_near = swap(out_own, "fsdp", 1)
    out_far = swap(out_own, "fsdp", 2)
    out_far_near = swap(out_far, "fsdp", 1)
    out = (out_own, out_near, out_far, out_far_near)
    gate_up_own, gate_up_a, gate_up_b = lax.optimization_barrier(
        (gate_up_own, gate_up_a, gate_up_b, attended)
    )[:3]
    gate_up_far = jnp.concatenate([gate_up_a, gate_up_b], axis=1)
    gate_up_near = swap(gate_up_own, "fsdp", 1)
    gate_up = (gate_up_own, gate_up_near, gate_up_far, swap(gate_up_far, "fsdp", 1))
    cot_full = features(after(cotangent, attended_full, out_far_near, out_near))
    down_far = swap(after(w_down, attended_full, out_far_near), "fsdp", 2)
    down_near = swap(after(w_down, attended_full), "fsdp", 1)
    hidden, normed_mid, scale_mlp = add_branch(token_low, attended_full, gain_mlp, out)

    activated, by_gate, by_up = hidden_units(normed_mid, gate_up)
    down_far = after(down_far, activated)
    down = (w_down, down_near, down_far, swap(down_far, "fsdp", 1))
    mlp_term = plain_columns(activated, down, "mlp_out")
    mlp_out = feature_sum(mlp_term)
    d_gate, d_up = hidden_back(after(cot_full, mlp_term), by_gate, by_up, down)
    d_mid_term = stacked_columns([d_gate, d_up], gate_up, "d_mid")
    d_hidden_term, d_att_term, gain_mlp_term = branch_back(
        d_mid_term, hidden, cot_full, scale_mlp, gain_mlp, out
    )
    d_attended = feature_sum(after(d_att_term, mlp_out))
    d_hidden_own = feature_sum(after(d_hidden_term, d_att_term))

    down_a, down_b = (
        Reduction(activated, cot_full, 1, "grad_down", (part_index, 2)) for part_index in (0, 1)
    )
    grad_gate = Reduction(normed_mid, d_gate, 0, "grad_gate")
    grad_up = Reduction(normed_mid, d_up, 0, "grad_up")
    square = lax.axis_size("tensor") == lax.axis_size("fsdp")
    down_a.near(d_att_term)
    down_b.near(down_a.sent)
    down_a.far(down_b.sent)
    down_a.send_far()
    grad_gate.near(down_a.two)
    down_b.far(grad_gate.sent)
    down_b.send_far()
    grad_gate.far(down_b.two)
    grad_gate.send_far()
    down_a.mine(grad_gate.two)
    down_a.send_context()
    grad_up.near(down_a.own)

    dq_peer, dkv_peer = peer_backward(
        need, queries, peer_kv, after(d_attended, grad_up.sent), attended, low_row, logs
    )
    dkv_in = lax.ppermute(dkv_peer, "context", [(1, 0)])
    d_query, dk_own, dv_own = own_backward(
        queries, keys_values, d_attended, attended, low_row, logs, dq_peer, cos, sin
    )
    grad_up.far(d_query)
    grad_up.send_far()
    d_key, d_value = finish_keys(dk_own, dv_own, after(dkv_in, grad_up.two), cos, sin)
    d_in_term = stacked_columns([d_query, d_key, d_value], qkv, "d_in")
    d_in = feature_sum(d_in_term).astype(F32)

    down_b.mine(d_in_term, dkv_in)
    down_b.send_context()
    d_parts = jnp.concatenate([d_query, d_key, d_value], axis=1)
    grad_qkv = Reduction(normed_in, d_parts, 0, "grad_qkv")
    if square:
        grad_out = Reduction(attended_full, d_hidden_own, 0, "grad_out")
    else:
        grad_out = Reduction(attended, features(d_hidden_own), 1, "grad_out")
    grad_qkv.near(down_b.own)
    grad_out.near(grad_qkv.sent)
    grad_gate.mine(grad_out.sent, down_a.other, down_b.other)
    grad_gate.send_context()
    grad_qkv.far(grad_gate.own)
    grad_qkv.send_far()
    grad_out.far(grad_qkv.two)
    grad_out.send_far()
    grad_up.mine(grad_out.two, grad_gate.other)
    grad_up.send_context()
    grad_qkv.mine(grad_up.own, grad_up.other)
    grad_qkv.send_context()
    grad_out.mine(grad_qkv.own)
    out_sum = grad_out.own
    if square:
        count = lax.axis_size("fsdp")
        across = [(i, (i % count) * count + i // count) for i in range(count * count)]
        grad_out.own = lax.ppermute(grad_out.own, ("fsdp", "tensor"), across)
    grad_out.send_context()

    stream = token_low.astype(F32)
    d_in_wide = after(d_in_term, out_sum).astype(F32)
    weighted = d_in_wide * stream
    inner_term = jnp.sum(weighted * gain_attn, axis=1)
    gain_attn_term = jnp.sum(weighted * scale_attn, axis=0)
    parts = lax.axis_size("tensor")
    totals_small = block_totals(
        jnp.concatenate(
            [
                jnp.broadcast_to(inner_term[None, :], (parts, row_count)),
                gain_attn_term.reshape(parts, part_width),
                gain_mlp_term.reshape(parts, part_width),
            ],
            axis=1,
        )[None]
    )
    inner_in = totals_small[0, :row_count][:, None] / full_width
    gain_sums = totals_small[0, row_count:].reshape(2, part_width)
    gain_sums = exchange(gain_sums, "fsdp", 1)
    gain_sums = exchange(gain_sums, "fsdp", 2)
    gain_sums = exchange(gain_sums, "context", 1)
    gain_width = gains.shape[1]
    grad_gains = lax.dynamic_slice_in_dim(
        gain_sums, lax.axis_index("fsdp") * gain_width, gain_width, 1
    )

    grad_down_sum = totals([down_a, down_b], 0, out_sum).reshape(w_down.shape)
    grad_gate_up_sum = totals([grad_gate, grad_up], 1, grad_down_sum)
    grad_qkv_sum = split_totals(grad_qkv, 3, grad_gate_up_sum)
    grad_out_sum = totals([grad_out], 0, grad_qkv_sum)[0]

    block_out = (own_features(hidden) + mlp_out.astype(F32)).astype(BF)
    own_tokens = tokens.astype(F32)
    grad_tokens = (
        d_hidden_own.astype(F32)
        + scale_attn * own_features(gain_attn) * d_in
        - own_tokens * scale_attn * scale_attn * scale_attn * inner_in
    ).astype(BF)
    return (
        block_out,
        grad_tokens,
        jnp.swapaxes(grad_qkv_sum, 0, 1),
        grad_out_sum,
        grad_gate_up_sum,
        grad_down_sum,
        grad_gains,
    )


def solution(mesh):
    rows = P(("fsdp", "context"), "tensor")
    inner = P("fsdp", None, "tensor")
    outer = P("tensor", "fsdp")
    gain = P(None, ("tensor", "fsdp"))
    return jax.shard_map(
        per_device,
        mesh=mesh,
        in_specs=(rows, inner, outer, inner, outer, gain, P("fsdp", None), rows),
        out_specs=(rows, rows, inner, outer, inner, outer, gain),
        check_vma=False,
    )
```

```python
import functools

import jax
import jax.numpy as jnp
from jax import lax
from jax.experimental import pallas as pl
from jax.experimental.pallas import tpu as pltpu
from jax.sharding import PartitionSpec as P

HDIM = 64
LANES = 128
QROWS = 256
norm_eps = 1e-05
rope_base = 130000.0
masked_score = -1e30
BF = jnp.bfloat16
F32 = jnp.float32
VMEM_BYTES = 56 * 1024 * 1024
LIGHT = pl.CostEstimate(flops=1, bytes_accessed=1, transcendentals=0)


def dotf(a, b, dims):
    return lax.dot_general(a, b, (dims, ((), ())), preferred_element_type=F32)


NN = ((1,), (0,))
NT = ((1,), (1,))
TN = ((0,), (0,))


def swap(value, axis, bit):
    count = lax.axis_size(axis)
    return lax.ppermute(value, axis, [(i, i ^ bit) for i in range(count)])


def after(value, *others):
    return lax.optimization_barrier((value, *others))[0]


def shifted(value, axis):
    count = lax.axis_size(axis)
    return [
        lax.ppermute(value, axis, [(i, (i + step) % count) for i in range(count)])
        for step in range(1, count)
    ]


def exchange(value, axis, bit):
    return value + swap(value, axis, bit)


def join_kernel(axis, mode, *refs):
    pieces, out_ref = refs[:-1], refs[-1]
    count = len(pieces)
    me = lax.axis_index(axis)
    for step, piece in enumerate(pieces):
        size = piece.shape[1]
        place = (me ^ step) if mode == "xor" else (me - step + count) % count
        out_ref[:, pl.ds(pl.multiple_of(place * size, size), size)] = piece[...]


def join(pieces, axis, mode):
    rows, size = pieces[0].shape
    return pl.pallas_call(
        functools.partial(join_kernel, axis, mode),
        out_shape=jax.ShapeDtypeStruct((rows, size * len(pieces)), pieces[0].dtype),
        cost_estimate=LIGHT,
        name="join",
    )(*pieces)


def gather_gains(gains):
    if lax.axis_size("tensor") > 4 or gains.shape[1] % LANES:
        whole = lax.all_gather(gains, ("tensor", "fsdp"), axis=1, tiled=True).astype(F32)
        return gains, whole
    own = gains.astype(F32)
    part = join([own] + [swap(own, "fsdp", bit) for bit in (1, 2, 3)], "fsdp", "xor")
    return part, join([part] + shifted(part, "tensor"), "tensor", "shift")


def block_totals(blocks):
    count = lax.axis_size("tensor")
    me = lax.axis_index("tensor")
    if count > 4:
        return lax.dynamic_index_in_dim(lax.psum(blocks, "tensor"), me, 1, keepdims=False)

    def pick(place):
        return lax.dynamic_index_in_dim(blocks, place, 1, keepdims=False)

    total = pick(me)
    for step in range(1, count):
        moves = [(i, (i + step) % count) for i in range(count)]
        total = total + lax.ppermute(pick((me + step) % count), "tensor", moves)
    return total


def piece_columns(j, size):
    return pl.ds(pl.multiple_of((lax.axis_index("fsdp") ^ j) * size, size), size)


def swap_halves(block):
    lane = lax.broadcasted_iota(jnp.int32, block.shape, 1)
    up = pltpu.roll(block, LANES - HDIM // 2, 1)
    down = pltpu.roll(block, HDIM // 2, 1)
    return jnp.where((lane & (HDIM - 1)) < HDIM // 2, up, down)


def rope_tables(positions):
    lane = jnp.arange(LANES, dtype=jnp.int32)
    half = lane % (HDIM // 2)
    frequencies = rope_base ** (-2.0 * half.astype(F32) / HDIM)
    angles = positions.astype(F32)[:, None] * frequencies[None, :]
    sign = jnp.where((lane % HDIM) < HDIM // 2, -1.0, 1.0)
    return jnp.cos(angles), jnp.sin(angles) * sign[None, :]


def piece_dot(x_ref, rows, pieces, dims=NN):
    total = None
    for j, piece in enumerate(pieces):
        size = piece.shape[dims[1][0]]
        term = dotf(x_ref[rows, piece_columns(j, size)], piece, dims)
        total = term if total is None else total + term
    return total


def project_kernel(kinds, normalize, x_ref, *refs):
    pieces, (cos_ref, sin_ref, gain_ref), outs = refs[:4], refs[4:7], refs[7:]
    out_ref = outs[0]
    rows, width = out_ref.shape[1:]
    step = pl.program_id(0)
    if normalize:
        normed_ref, scale_ref = outs[1], outs[2]

        @pl.when(step == 0)
        def _():
            for r in range(0, rows, QROWS):
                part = slice(r, r + QROWS)
                stream = x_ref[part, :].astype(F32)
                mean = jnp.sum(stream * stream, axis=1, keepdims=True) / x_ref.shape[1]
                scale = lax.rsqrt(mean + norm_eps)
                scale_ref[part, :] = scale
                normed_ref[part, :] = (stream * scale * gain_ref[...]).astype(BF)

        x_ref = normed_ref
    for index, scale in enumerate(kinds):

        @pl.when(step == index)
        def _():
            for r in range(0, rows, rows):
                part = slice(r, r + rows)
                result = piece_dot(x_ref, part, [piece[0] for piece in pieces])
                for c in range(0, width, LANES):
                    block = result[:, c : c + LANES]
                    if scale:
                        block = block * cos_ref[part, :] + swap_halves(block) * sin_ref[part, :]
                    low = block.astype(BF)
                    if scale and scale != 1.0:
                        low = low * jnp.asarray(scale, BF)
                    out_ref[0, part, c : c + LANES] = low


def project(x, pieces, cos, sin, gain, kinds, first, normalize):
    rows, depth = x.shape
    _, size, width = pieces[0].shape
    flops = 2 * len(kinds) * rows * depth * width
    whole = pl.BlockSpec((rows, depth), lambda i: (0, 0))
    table = pl.BlockSpec((rows, LANES), lambda i: (0, 0))
    out_shape = [jax.ShapeDtypeStruct((len(kinds), rows, width), BF)]
    out_specs = [pl.BlockSpec((1, rows, width), lambda i: (i, 0, 0))]
    if normalize:
        out_shape += [jax.ShapeDtypeStruct((rows, depth), BF), jax.ShapeDtypeStruct((rows, 1), F32)]
        out_specs += [whole, pl.BlockSpec((rows, 1), lambda i: (0, 0))]
    return pl.pallas_call(
        functools.partial(project_kernel, kinds, normalize),
        name="project_kv" if normalize else "project_q",
        grid=(len(kinds),),
        out_shape=out_shape,
        in_specs=[whole]
        + [pl.BlockSpec((1, size, width), lambda i: (i + first, 0, 0))] * 4
        + [table, table, pl.BlockSpec((1, depth), lambda i: (0, 0))],
        out_specs=out_specs,
        compiler_params=pltpu.CompilerParams(vmem_limit_bytes=VMEM_BYTES),
        cost_estimate=LIGHT,
    )(x, *pieces, cos, sin, gain)


def head_mask(block, head):
    lane = lax.broadcasted_iota(jnp.int32, block.shape, 1)
    inside = (lane < HDIM) if head == 0 else (lane >= HDIM)
    return jnp.where(inside, block, jnp.zeros_like(block))


def own_mask(key_count, row0, low_row):
    key = lax.broadcasted_iota(jnp.int32, (key_count, QROWS), 0)
    query = row0 + lax.broadcasted_iota(jnp.int32, (key_count, QROWS), 1)
    return (key >= low_row) & (key <= query)


def peer_mask(key_count, low_row, offset):
    key = lax.broadcasted_iota(jnp.int32, (key_count, QROWS), 0) - offset
    return key >= low_row


def key_windows(need, total):
    counts = list(range(QROWS, total + 1, QROWS))
    for place, count in enumerate(counts):
        chosen = need < 0 if place == 0 else need < -counts[place - 1]
        if count < total:
            chosen = jnp.logical_and(chosen, need >= -count)
        yield count, chosen


def own_forward_kernel(q_ref, k_ref, v_ref, low_ref, out_ref, log_ref):
    rows = q_ref.shape[0]
    v_t = v_ref[...].T
    for r in range(0, rows, QROWS):
        count = r + QROWS
        allowed = own_mask(count, r, low_ref[:, r : r + QROWS])
        keys = k_ref[0:count, :]
        outs = []
        for head in range(LANES // HDIM):
            scores = dotf(keys, head_mask(q_ref[r : r + QROWS, :], head), NT)
            scores = jnp.where(allowed, scores, masked_score)
            peak = jnp.max(scores, axis=0, keepdims=True)
            weights = jnp.exp(scores - peak)
            total = jnp.sum(weights, axis=0, keepdims=True)
            part = dotf(v_t[head * HDIM : (head + 1) * HDIM, 0:count], weights.astype(BF), NN)
            outs.append(part / total)
            log_ref[0, head : head + 1, r : r + QROWS] = peak + jnp.log(total)
        out_ref[r : r + QROWS, :] = jnp.concatenate(outs, axis=0).T


def peer_forward_kernel(
    need_ref, q_ref, k_ref, v_ref, low_ref, part_ref, log_in_ref, out_ref, log_ref
):
    rows = q_ref.shape[0]
    key_total = k_ref.shape[0]
    for index, r in enumerate(range(0, rows, QROWS)):
        for key_count, chosen in key_windows(need_ref[index], key_total):

            @pl.when(chosen)
            def _():
                window = slice(key_total - key_count, key_total)
                v_t = v_ref[window, :].T
                allowed = peer_mask(key_count, low_ref[:, r : r + QROWS], key_count)
                before = part_ref[r : r + QROWS, :].T
                outs = []
                for head in range(LANES // HDIM):
                    scores = dotf(k_ref[window, :], head_mask(q_ref[r : r + QROWS, :], head), NT)
                    scores = jnp.where(allowed, scores, masked_score)
                    log_own = log_in_ref[0, head : head + 1, r : r + QROWS]
                    peak = jnp.maximum(jnp.max(scores, axis=0, keepdims=True), log_own)
                    weights = jnp.exp(scores - peak)
                    own_weight = jnp.exp(log_own - peak)
                    total = jnp.sum(weights, axis=0, keepdims=True) + own_weight
                    rows_h = slice(head * HDIM, (head + 1) * HDIM)
                    part = dotf(v_t[rows_h, :], weights.astype(BF), NN)
                    outs.append((part + before[rows_h, :] * own_weight) / total)
                    log_ref[0, head : head + 1, r : r + QROWS] = peak + jnp.log(total)
                out_ref[r : r + QROWS, :] = jnp.concatenate(outs, axis=0).T.astype(BF)

        @pl.when(need_ref[index] >= 0)
        def _():
            out_ref[r : r + QROWS, :] = part_ref[r : r + QROWS, :].astype(BF)
            log_ref[:, :, r : r + QROWS] = log_in_ref[:, :, r : r + QROWS]


def pair_spec(rows):
    return pl.BlockSpec((rows, LANES), lambda i: (0, i))


def stacked_spec(rows, part):
    return pl.BlockSpec((None, rows, LANES), lambda i: (part, 0, i))


def log_spec(rows):
    return pl.BlockSpec((1, LANES // HDIM, rows), lambda i: (i, 0, 0))


def low_spec(rows):
    return pl.BlockSpec((1, rows), lambda i: (0, 0))


def own_forward(q, kv, low_row):
    rows, width = q.shape
    pairs = width // LANES
    return pl.pallas_call(
        own_forward_kernel,
        name="own_fwd",
        grid=(pairs,),
        out_shape=(
            jax.ShapeDtypeStruct((rows, width), F32),
            jax.ShapeDtypeStruct((pairs, LANES // HDIM, rows), F32),
        ),
        in_specs=[
            pair_spec(rows),
            stacked_spec(rows, 0),
            stacked_spec(rows, 1),
            low_spec(rows),
        ],
        out_specs=(pair_spec(rows), log_spec(rows)),
        compiler_params=pltpu.CompilerParams(vmem_limit_bytes=VMEM_BYTES),
        cost_estimate=LIGHT,
    )(q, kv, kv, low_row)


SMEM_SPEC = pl.BlockSpec(memory_space=pltpu.SMEM)


def peer_forward(need, q, kv, low_row, part, log_in):
    rows, width = q.shape
    pairs = width // LANES
    return pl.pallas_call(
        peer_forward_kernel,
        name="peer_fwd",
        grid=(pairs,),
        out_shape=(
            jax.ShapeDtypeStruct((rows, width), BF),
            jax.ShapeDtypeStruct((pairs, LANES // HDIM, rows), F32),
        ),
        in_specs=[
            SMEM_SPEC,
            pair_spec(rows),
            stacked_spec(rows, 0),
            stacked_spec(rows, 1),
            low_spec(rows),
            pair_spec(rows),
            log_spec(rows),
        ],
        out_specs=(pair_spec(rows), log_spec(rows)),
        compiler_params=pltpu.CompilerParams(vmem_limit_bytes=VMEM_BYTES),
        cost_estimate=LIGHT,
    )(need, q, kv, kv, low_row, part, log_in)


def backward_block(q_rows, k_rows, v_rows, k_t, do_rows, do_o_t, logs, allowed):
    d_query, d_key, d_value = [], None, None
    for head in range(LANES // HDIM):
        rows_h = slice(head * HDIM, (head + 1) * HDIM)
        q_head = head_mask(q_rows, head)
        do_head = head_mask(do_rows, head)
        scores = dotf(k_rows, q_head, NT)
        probs = jnp.exp(jnp.where(allowed, scores, masked_score) - logs[head])
        delta = jnp.sum(do_o_t[rows_h, :], axis=0, keepdims=True)
        d_probs = dotf(v_rows, do_head, NT)
        d_scores = (probs * (d_probs - delta)).astype(BF)
        d_v = dotf(probs.astype(BF), do_head, NN)
        d_k = dotf(d_scores, q_head, NN)
        d_value = d_v if d_value is None else d_value + d_v
        d_key = d_k if d_key is None else d_key + d_k
        d_query.append(dotf(k_t[rows_h, :], d_scores, NN))
    return jnp.concatenate(d_query, axis=0), d_key, d_value


def output_product(do_ref, o_ref, window):
    product = do_ref[window].astype(F32) * o_ref[window].astype(F32)
    return product.T


def peer_backward_kernel(
    need_ref, q_ref, k_ref, v_ref, do_ref, o_ref, low_ref, log_ref, dq_ref, dkv_ref, sums
):
    rows = q_ref.shape[0]
    key_total = k_ref.shape[0]
    sums[...] = jnp.zeros_like(sums)
    for index, r in enumerate(range(0, rows, QROWS)):
        rows_q = (slice(r, r + QROWS), slice(None))
        for key_count, chosen in key_windows(need_ref[index], key_total):

            @pl.when(chosen)
            def _():
                window = slice(key_total - key_count, key_total)
                allowed = peer_mask(key_count, low_ref[:, r : r + QROWS], key_count)
                logs = [log_ref[0, h : h + 1, r : r + QROWS] for h in range(LANES // HDIM)]
                d_query, d_key, d_value = backward_block(
                    q_ref[rows_q],
                    k_ref[window, :],
                    v_ref[window, :],
                    k_ref[window, :].T,
                    do_ref[rows_q],
                    output_product(do_ref, o_ref, rows_q),
                    logs,
                    allowed,
                )
                dq_ref[rows_q] = d_query.T
                sums[0, window] += d_key
                sums[1, window] += d_value

        @pl.when(need_ref[index] >= 0)
        def _():
            dq_ref[rows_q] = jnp.zeros((QROWS, LANES), F32)

    dkv_ref[...] = sums[...].astype(BF)


def peer_backward(need, q, kv, do, o, low_row, logs):
    rows, width = q.shape
    pairs = width // LANES
    return pl.pallas_call(
        peer_backward_kernel,
        name="peer_bwd",
        grid=(pairs,),
        out_shape=(
            jax.ShapeDtypeStruct((rows, width), F32),
            jax.ShapeDtypeStruct((2, rows, width), BF),
        ),
        in_specs=[
            SMEM_SPEC,
            pair_spec(rows),
            stacked_spec(rows, 0),
            stacked_spec(rows, 1),
            pair_spec(rows),
            pair_spec(rows),
            low_spec(rows),
            log_spec(rows),
        ],
        out_specs=(pair_spec(rows), pl.BlockSpec((2, rows, LANES), lambda i: (0, 0, i))),
        scratch_shapes=[pltpu.VMEM((2, rows, LANES), F32)],
        compiler_params=pltpu.CompilerParams(vmem_limit_bytes=VMEM_BYTES),
        cost_estimate=LIGHT,
    )(need, q, kv, kv, do, o, low_row, logs)


def own_backward_kernel(
    q_ref,
    k_ref,
    v_ref,
    do_ref,
    o_ref,
    low_ref,
    log_ref,
    dq_in_ref,
    cos_ref,
    sin_ref,
    dq_ref,
    dk_ref,
    dv_ref,
    sums,
):
    rows = q_ref.shape[0]
    sums[...] = jnp.zeros_like(sums)
    k_t = k_ref[...].T
    for r in range(0, rows, QROWS):
        count = r + QROWS
        window = (slice(r, r + QROWS), slice(None))
        allowed = own_mask(count, r, low_ref[:, r : r + QROWS])
        logs = [log_ref[0, h : h + 1, r : r + QROWS] for h in range(LANES // HDIM)]
        d_query, d_key, d_value = backward_block(
            q_ref[window],
            k_ref[0:count, :],
            v_ref[0:count, :],
            k_t[:, 0:count],
            do_ref[window],
            output_product(do_ref, o_ref, window),
            logs,
            allowed,
        )
        rotated = (d_query.T + dq_in_ref[window]) * (HDIM**-0.5)
        turned = rotated * cos_ref[window] - swap_halves(rotated) * sin_ref[window]
        dq_ref[window] = turned.astype(BF)
        sums[0, 0:count] += d_key
        sums[1, 0:count] += d_value
    dk_ref[...] = sums[0]
    dv_ref[...] = sums[1]


def own_backward(q, kv, do, o, low_row, logs, dq_in, cos, sin):
    rows, width = q.shape
    pairs = width // LANES
    table = pl.BlockSpec((rows, LANES), lambda i: (0, 0))
    return pl.pallas_call(
        own_backward_kernel,
        name="own_bwd",
        grid=(pairs,),
        out_shape=(
            jax.ShapeDtypeStruct((rows, width), BF),
            jax.ShapeDtypeStruct((rows, width), F32),
            jax.ShapeDtypeStruct((rows, width), F32),
        ),
        in_specs=[
            pair_spec(rows),
            stacked_spec(rows, 0),
            stacked_spec(rows, 1),
            pair_spec(rows),
            pair_spec(rows),
            low_spec(rows),
            log_spec(rows),
            pair_spec(rows),
            table,
            table,
        ],
        out_specs=(pair_spec(rows),) * 3,
        scratch_shapes=[pltpu.VMEM((2, rows, LANES), F32)],
        compiler_params=pltpu.CompilerParams(vmem_limit_bytes=VMEM_BYTES),
        cost_estimate=LIGHT,
    )(q, kv, kv, do, o, low_row, logs, dq_in, cos, sin)


def finish_keys_kernel(dk_ref, dv_ref, dk_in_ref, dv_in_ref, cos_ref, sin_ref, dk_out, dv_out):
    total = dk_ref[...] + dk_in_ref[...].astype(F32)
    turned = total * cos_ref[...] - swap_halves(total) * sin_ref[...]
    dk_out[...] = turned.astype(BF)
    dv_out[...] = (dv_ref[...] + dv_in_ref[...].astype(F32)).astype(BF)


def finish_keys(dk, dv, dkv_in, cos, sin):
    rows, width = dk.shape
    pairs = width // LANES
    table = pl.BlockSpec((rows, LANES), lambda i: (0, 0))
    return pl.pallas_call(
        finish_keys_kernel,
        name="finish_keys",
        grid=(pairs,),
        out_shape=(jax.ShapeDtypeStruct((rows, width), BF),) * 2,
        in_specs=[pair_spec(rows), pair_spec(rows), stacked_spec(rows, 0), stacked_spec(rows, 1)]
        + [table, table],
        out_specs=(pair_spec(rows),) * 2,
        cost_estimate=LIGHT,
    )(dk, dv, dkv_in, dkv_in, cos, sin)


def branch_kernel(stream_ref, att_ref, gain_ref, *refs):
    pieces, (hidden_ref, normed_ref, scale_ref) = refs[:4], refs[4:]
    for j, piece in enumerate(pieces):
        columns = piece_columns(j, piece.shape[1])
        term = dotf(att_ref[...], piece[...], NN)
        hidden_ref[:, columns] = stream_ref[:, columns].astype(F32) + term
    hidden = hidden_ref[...]
    mean = jnp.sum(hidden * hidden, axis=1, keepdims=True) / hidden.shape[1]
    scale = lax.rsqrt(mean + norm_eps)
    scale_ref[...] = scale
    normed_ref[...] = (hidden * scale * gain_ref[...]).astype(BF)


def add_branch(stream, att, gain, pieces):
    rows, depth = stream.shape
    heads = att.shape[1]
    tile = pl.BlockSpec((QROWS, depth), lambda i: (i, 0))
    return pl.pallas_call(
        branch_kernel,
        name="branch",
        grid=(rows // QROWS,),
        out_shape=(
            jax.ShapeDtypeStruct((rows, depth), F32),
            jax.ShapeDtypeStruct((rows, depth), BF),
            jax.ShapeDtypeStruct((rows, 1), F32),
        ),
        in_specs=[
            tile,
            pl.BlockSpec((QROWS, heads), lambda i: (i, 0)),
            pl.BlockSpec((1, depth), lambda i: (0, 0)),
        ]
        + [pl.BlockSpec(pieces[0].shape, lambda i: (0, 0))] * 4,
        out_specs=(tile, tile, pl.BlockSpec((QROWS, 1), lambda i: (i, 0))),
        compiler_params=pltpu.CompilerParams(vmem_limit_bytes=VMEM_BYTES),
        cost_estimate=LIGHT,
    )(stream, att, gain, *pieces)


def hidden_kernel(x_ref, *refs):
    w_in, (act_ref, by_gate_ref, by_up_ref) = refs[:4], refs[4:]
    rows = x_ref.shape[0]
    for r in range(0, rows, rows):
        part = slice(r, r + rows)
        gate = piece_dot(x_ref, part, [piece[0] for piece in w_in])
        up = piece_dot(x_ref, part, [piece[1] for piece in w_in])
        sig = jax.nn.sigmoid(gate)
        silu = gate * sig
        act_ref[part, :] = (silu * up).astype(BF)
        by_gate_ref[part, :] = (up * sig * (1.0 + gate * (1.0 - sig))).astype(BF)
        by_up_ref[part, :] = silu.astype(BF)


def hidden_units(x, w_in):
    rows, depth = x.shape
    _, size, units = w_in[0].shape
    tile = 256
    part = pl.BlockSpec((rows, tile), lambda i: (0, i))
    return pl.pallas_call(
        hidden_kernel,
        grid=(units // tile,),
        out_shape=(jax.ShapeDtypeStruct((rows, units), BF),) * 3,
        in_specs=[pl.BlockSpec((rows, depth), lambda i: (0, 0))]
        + [pl.BlockSpec((2, size, tile), lambda i: (0, 0, i))] * 4,
        out_specs=(part,) * 3,
        compiler_params=pltpu.CompilerParams(vmem_limit_bytes=VMEM_BYTES),
        cost_estimate=LIGHT,
        name="hidden",
    )(x, *w_in)


def hidden_back_kernel(cot_ref, by_gate_ref, by_up_ref, *refs):
    w_down, (dg_ref, du_ref) = refs[:4], refs[4:]
    rows = cot_ref.shape[0]
    for r in range(0, rows, rows):
        part = slice(r, r + rows)
        d_act = piece_dot(cot_ref, part, [piece[...] for piece in w_down], NT)
        dg_ref[part, :] = (d_act * by_gate_ref[part, :].astype(F32)).astype(BF)
        du_ref[part, :] = (d_act * by_up_ref[part, :].astype(F32)).astype(BF)


def hidden_back(cot, by_gate, by_up, w_down):
    rows, depth = cot.shape
    units, size = w_down[0].shape
    tile = 256
    part = pl.BlockSpec((rows, tile), lambda i: (0, i))
    return pl.pallas_call(
        hidden_back_kernel,
        grid=(units // tile,),
        out_shape=(jax.ShapeDtypeStruct((rows, units), BF),) * 2,
        in_specs=[pl.BlockSpec((rows, depth), lambda i: (0, 0)), part, part]
        + [pl.BlockSpec((tile, size), lambda i: (i, 0))] * 4,
        out_specs=(part,) * 2,
        compiler_params=pltpu.CompilerParams(vmem_limit_bytes=VMEM_BYTES),
        cost_estimate=LIGHT,
        name="hidden_back",
    )(cot, by_gate, by_up, *w_down)


def phased(i, block, make_index, tiles):
    def index_map(j, t):
        return make_index(jnp.where(j < i, 0, jnp.where(j == i, t, tiles - 1)))

    return pl.BlockSpec(block, index_map)


def columns_call(kernel_dot, lefts, pieces, block, make_index, size, flops, name):
    rows = lefts[0].shape[0]
    tile = min(size, 256)
    tiles = size // tile
    depth = size * 4

    def kernel(*refs):
        left_refs, piece_refs, out_ref = refs[: len(lefts)], refs[len(lefts) : -1], refs[-1]
        for j, piece in enumerate(piece_refs):

            @pl.when(pl.program_id(0) == j)
            def _():
                out_ref[...] = kernel_dot([left[...] for left in left_refs], piece).astype(BF)

    def out_index(j, t):
        return (0, (lax.axis_index("fsdp") ^ j) * tiles + t)

    return pl.pallas_call(
        kernel,
        grid=(4, tiles),
        out_shape=jax.ShapeDtypeStruct((rows, depth), BF),
        in_specs=[pl.BlockSpec(left.shape, lambda j, t: (0, 0)) for left in lefts]
        + [phased(i, block(tile), make_index, tiles) for i in range(4)],
        out_specs=pl.BlockSpec((rows, tile), out_index),
        compiler_params=pltpu.CompilerParams(vmem_limit_bytes=VMEM_BYTES),
        cost_estimate=LIGHT,
        name=name,
    )(*lefts, *pieces)


def stacked_columns(lefts, pieces, name):
    count, size, inner = pieces[0].shape

    def product(parts, piece):
        return sum(dotf(parts[c], piece[c], NT) for c in range(count))

    return columns_call(
        product,
        lefts,
        pieces,
        lambda tile: (count, tile, inner),
        lambda t: (0, t, 0),
        size,
        8 * lefts[0].shape[0] * size * inner * count,
        name,
    )


def plain_columns(left, pieces, name):
    inner, size = pieces[0].shape
    return columns_call(
        lambda parts, piece: dotf(parts[0], piece[...], NN),
        [left],
        pieces,
        lambda tile: (inner, tile),
        lambda t: (0, t),
        size,
        8 * left.shape[0] * size * inner,
        name,
    )


def branch_back_kernel(shares, d_mid_ref, hidden_ref, cot_ref, scale_ref, gain_ref, *refs):
    pieces, (d_hidden_ref, d_att_ref, gain_out_ref) = refs[:4], refs[4:7]
    d_mid = d_mid_ref[...].astype(F32)
    hidden = hidden_ref[...]
    scale = scale_ref[...]
    weighted = d_mid * gain_ref[...]
    inner = jnp.sum(weighted * hidden, axis=1, keepdims=True) / hidden.shape[1]
    d_hidden = (
        cot_ref[...].astype(F32) * (1.0 / shares)
        + scale * weighted
        - hidden * (scale * scale * scale * inner)
    )
    gain_term = jnp.sum(d_mid * hidden * scale, axis=0, keepdims=True)

    @pl.when(pl.program_id(0) == 0)
    def _():
        gain_out_ref[...] = gain_term

    @pl.when(pl.program_id(0) != 0)
    def _():
        gain_out_ref[...] += gain_term

    d_hidden_ref[...] = d_hidden.astype(BF)
    heads = d_att_ref.shape[1]
    for e in range(0, heads, 512):
        columns = slice(e, e + 512)
        d_att_ref[:, columns] = piece_dot(
            d_hidden_ref, slice(None), [piece[columns, :] for piece in pieces], NT
        ).astype(BF)


def branch_back(d_mid, hidden, cot, scale, gain, pieces):
    rows, depth = hidden.shape
    heads, size = pieces[0].shape
    tile = pl.BlockSpec((QROWS, depth), lambda i: (i, 0))
    row = pl.BlockSpec((1, depth), lambda i: (0, 0))
    return pl.pallas_call(
        functools.partial(branch_back_kernel, lax.axis_size("tensor")),
        name="branch_back",
        grid=(rows // QROWS,),
        in_specs=[tile, tile, tile, pl.BlockSpec((QROWS, 1), lambda i: (i, 0)), row]
        + [pl.BlockSpec((heads, size), lambda i: (0, 0))] * 4,
        out_specs=(tile, pl.BlockSpec((QROWS, heads), lambda i: (i, 0)), row),
        out_shape=(
            jax.ShapeDtypeStruct((rows, depth), BF),
            jax.ShapeDtypeStruct((rows, heads), BF),
            jax.ShapeDtypeStruct((1, depth), F32),
        ),
        compiler_params=pltpu.CompilerParams(vmem_limit_bytes=VMEM_BYTES),
        cost_estimate=LIGHT,
    )(d_mid, hidden, cot, scale, gain, *pieces)


def grad_call(left, right, cut, places, adds, name, span=(0, 1)):
    rows = left.shape[0]
    size = (left, right)[cut].shape[1] // 4
    swept = (right, left)[cut].shape[1] // span[1]
    height, width = (size, swept) if cut == 0 else (swept, size)
    tile = swept if swept <= 1024 else 1024 if swept % 1024 == 0 else 512
    offset = span[0] * (swept // tile)
    block = (height, tile) if cut == 0 else (tile, width)

    def owner(i):
        return lax.axis_index("fsdp") ^ (places[0] + 2 * i)

    def swept_index(t):
        return (0, t) if cut == 0 else (t, 0)

    def kernel(left_ref, right_ref, *refs):
        add_refs, out_ref = refs[: len(adds)], refs[len(adds)]
        if cut == 0:
            turned = refs[-1]

            @pl.when(pl.program_id(1) == 0)
            def _():
                turned[...] = left_ref[...].T

            result = dotf(turned[...], right_ref[...], NN)
        else:
            result = dotf(left_ref[...].T, right_ref[...], NN)
        for add in add_refs:
            result = result + add[...].astype(F32)
        out_ref[...] = result.astype(BF)

    fixed = pl.BlockSpec((rows, size), lambda i, t: (0, owner(i)))
    moving = pl.BlockSpec((rows, tile), lambda i, t: (0, t + offset))
    add_specs = []
    for _, slot in adds:
        if slot is None:
            add_specs.append(pl.BlockSpec(block, lambda i, t: swept_index(t)))
        else:
            add_specs.append(
                pl.BlockSpec((None, *block), lambda i, t, slot=slot: (slot, *swept_index(t)))
            )
    if len(places) > 1:
        out_shape = jax.ShapeDtypeStruct((len(places), height, width), BF)
        out_spec = pl.BlockSpec((None, *block), lambda i, t: (i, *swept_index(t)))
    else:
        out_shape = jax.ShapeDtypeStruct((height, width), BF)
        out_spec = pl.BlockSpec(block, lambda i, t: swept_index(t))
    return pl.pallas_call(
        kernel,
        grid=(len(places), swept // tile),
        out_shape=out_shape,
        in_specs=[fixed, moving] * (cut == 0) + [moving, fixed] * (cut == 1) + add_specs,
        out_specs=out_spec,
        scratch_shapes=[pltpu.VMEM((size, rows), BF)] if cut == 0 else [],
        compiler_params=pltpu.CompilerParams(vmem_limit_bytes=VMEM_BYTES),
        cost_estimate=LIGHT,
        name=name,
    )(left, right, *[array for array, _ in adds])


class Reduction:
    def __init__(self, left, right, cut, name, span=(0, 1)):
        self.args, self.name, self.span = (left, right, cut), name, span

    def call(self, places, deps, step, adds=()):
        left, right, cut = self.args
        left = after(left, *deps) if deps else left
        return grad_call(left, right, cut, places, adds, self.name + step, self.span)

    def near(self, *deps):
        self.sent = self.call((1, 3), deps, "_near")
        self.beside = swap(self.sent, "fsdp", 1)

    def far(self, *deps):
        self.two = self.call((2,), deps, "_far", [(self.beside, 1)])

    def send_far(self, *deps):
        self.across = swap(after(self.two, *deps), "fsdp", 2)

    def mine(self, *deps):
        self.own = self.call((0,), deps, "_own", [(self.beside, 0), (self.across, None)])

    def send_context(self, *deps):
        self.other = swap(after(self.own, *deps), "context", 1)


def totals_kernel(slots, *refs):
    pairs, out_ref = refs[:-1], refs[-1]
    for slot in range(len(pairs) // 2):
        total = pairs[2 * slot][...].astype(F32) + pairs[2 * slot + 1][...].astype(F32)
        if slots == 0:
            out_ref[slot] = total
        else:
            out_ref[:, slot, :] = total


def totals(sums, slots, *deps):
    arrays = [array for part in sums for array in (part.own, part.other)]
    if deps:
        arrays[0] = after(arrays[0], *deps)
    rows, width = arrays[0].shape
    tile = 128
    shape = [rows, width]
    shape.insert(slots, len(sums))
    block = [tile, width]
    block.insert(slots, len(sums))
    return pl.pallas_call(
        functools.partial(totals_kernel, slots),
        grid=(rows // tile,),
        out_shape=jax.ShapeDtypeStruct(tuple(shape), F32),
        in_specs=[pl.BlockSpec((tile, width), lambda i: (i, 0))] * len(arrays),
        out_specs=pl.BlockSpec(
            tuple(block), (lambda i: (0, i, 0)) if slots == 0 else (lambda i: (i, 0, 0))
        ),
        compiler_params=pltpu.CompilerParams(vmem_limit_bytes=VMEM_BYTES),
        cost_estimate=LIGHT,
        name="totals",
    )(*arrays)


def split_totals_kernel(own_ref, other_ref, out_ref):
    width = out_ref.shape[2]
    for slot in range(out_ref.shape[0]):
        columns = slice(slot * width, (slot + 1) * width)
        out_ref[slot] = own_ref[:, columns].astype(F32) + other_ref[:, columns].astype(F32)


def split_totals(part, count, *deps):
    own = after(part.own, *deps)
    rows, width = own.shape
    tile = 128
    return pl.pallas_call(
        split_totals_kernel,
        grid=(rows // tile,),
        out_shape=jax.ShapeDtypeStruct((count, rows, width // count), F32),
        in_specs=[pl.BlockSpec((tile, width), lambda i: (i, 0))] * 2,
        out_specs=pl.BlockSpec((count, tile, width // count), lambda i: (0, i, 0)),
        compiler_params=pltpu.CompilerParams(vmem_limit_bytes=VMEM_BYTES),
        cost_estimate=LIGHT,
        name="split_totals",
    )(own, part.other)


def row_sum(values_in):
    return jnp.sum(values_in, axis=1, keepdims=True)


def per_device(tokens, w_qkv, w_out, w_gate_up, w_down, gains, seq_lengths, cotangent):
    row_count, part_width = tokens.shape
    tensor_index = lax.axis_index("tensor")
    context_index = lax.axis_index("context")
    full_width = part_width * lax.axis_size("tensor")

    def features(part_in):
        return lax.all_gather(part_in, "tensor", axis=1, tiled=True)

    def feature_sum(term):
        return lax.psum_scatter(term.astype(BF), "tensor", scatter_dimension=1, tiled=True)

    def own_features(full):
        return lax.dynamic_slice_in_dim(full, tensor_index * part_width, part_width, 1)

    ending = jnp.cumsum(seq_lengths[0])
    starts = ending - seq_lengths[0]
    places = context_index * row_count + jnp.arange(row_count, dtype=jnp.int32)
    first_token = jnp.max(jnp.where(starts[None, :] <= places[:, None], starts[None, :], 0), axis=1)
    cos, sin = rope_tables(places - first_token)
    low = first_token - context_index * row_count
    low_row = low[None, :]
    need = low[::QROWS]

    token_low = features(tokens)
    gain_near, gain_full = gather_gains(gains)
    gain_attn, gain_mlp = gain_full[0:1], gain_full[1:2]

    qkv_own = jnp.swapaxes(w_qkv, 0, 1)
    half = qkv_own.shape[1] // 2
    far_half = swap(
        lax.dynamic_slice_in_dim(after(qkv_own, gain_near), context_index * half, half, 1),
        "fsdp",
        2,
    )
    other_half = swap(far_half, "context", 1)
    qkv_far = jnp.where(
        context_index == 0,
        jnp.concatenate([far_half, other_half], axis=1),
        jnp.concatenate([other_half, far_half], axis=1),
    )
    qkv_near = swap(qkv_own, "fsdp", 1)
    qkv = (qkv_own, qkv_near, qkv_far, swap(qkv_far, "fsdp", 1))

    gate_up_own = jnp.swapaxes(w_gate_up, 0, 1)
    cut = gate_up_own.shape[1] * 12 // 32
    gate_up_a = swap(after(gate_up_own[:, :cut], far_half), "fsdp", 2)
    gate_up_b = swap(after(gate_up_own[:, cut:], gate_up_a), "fsdp", 2)

    keys_values, normed_in, scale_attn = project(
        after(token_low, gate_up_a), qkv, cos, sin, gain_attn, (1.0, None), 1, True
    )
    peer_kv = lax.ppermute(keys_values, "context", [(0, 1)])
    queries = project(normed_in, qkv, cos, sin, gain_attn, (HDIM**-0.5,), 0, False)[0][0]
    part, part_log = own_forward(queries, keys_values, low_row)
    attended, logs = peer_forward(
        need, queries, peer_kv, low_row, after(part, gate_up_b), part_log
    )
    attended_full = features(attended)

    out_own = after(lax.all_gather(w_out, "tensor", axis=0, tiled=True), attended)
    out_near = swap(out_own, "fsdp", 1)
    out_far = swap(out_own, "fsdp", 2)
    out_far_near = swap(out_far, "fsdp", 1)
    out = (out_own, out_near, out_far, out_far_near)
    gate_up_own, gate_up_a, gate_up_b = lax.optimization_barrier(
        (gate_up_own, gate_up_a, gate_up_b, attended)
    )[:3]
    gate_up_far = jnp.concatenate([gate_up_a, gate_up_b], axis=1)
    gate_up_near = swap(gate_up_own, "fsdp", 1)
    gate_up = (gate_up_own, gate_up_near, gate_up_far, swap(gate_up_far, "fsdp", 1))
    cot_full = features(after(cotangent, attended_full, out_far_near, out_near))
    down_far = swap(after(w_down, attended_full, out_far_near), "fsdp", 2)
    down_near = swap(after(w_down, attended_full), "fsdp", 1)
    hidden, normed_mid, scale_mlp = add_branch(token_low, attended_full, gain_mlp, out)

    activated, by_gate, by_up = hidden_units(normed_mid, gate_up)
    down_far = after(down_far, activated)
    down = (w_down, down_near, down_far, swap(down_far, "fsdp", 1))
    mlp_term = plain_columns(activated, down, "mlp_out")
    mlp_out = feature_sum(mlp_term)
    d_gate, d_up = hidden_back(after(cot_full, mlp_term), by_gate, by_up, down)
    d_mid_term = stacked_columns([d_gate, d_up], gate_up, "d_mid")
    d_hidden_term, d_att_term, gain_mlp_term = branch_back(
        d_mid_term, hidden, cot_full, scale_mlp, gain_mlp, out
    )
    d_attended = feature_sum(after(d_att_term, mlp_out))
    d_hidden_own = feature_sum(after(d_hidden_term, d_att_term))

    down_a, down_b = (
        Reduction(activated, cot_full, 1, "grad_down", (part_index, 2)) for part_index in (0, 1)
    )
    grad_gate = Reduction(normed_mid, d_gate, 0, "grad_gate")
    grad_up = Reduction(normed_mid, d_up, 0, "grad_up")
    square = lax.axis_size("tensor") == lax.axis_size("fsdp")
    down_a.near(d_att_term)
    down_b.near(down_a.sent)
    down_a.far(down_b.sent)
    down_a.send_far()
    grad_gate.near(down_a.two)
    down_b.far(grad_gate.sent)
    down_b.send_far()
    grad_gate.far(down_b.two)
    grad_gate.send_far()
    down_a.mine(grad_gate.two)
    grad_up.near(down_a.own)

    dq_peer, dkv_peer = peer_backward(
        need, queries, peer_kv, after(d_attended, grad_up.sent), attended, low_row, logs
    )
    dkv_in = lax.ppermute(dkv_peer, "context", [(1, 0)])
    d_query, dk_own, dv_own = own_backward(
        queries, keys_values, d_attended, attended, low_row, logs, dq_peer, cos, sin
    )
    grad_up.far(d_query)
    grad_up.send_far()
    down_a.send_context(d_query)
    down_b.mine(grad_up.two)
    down_b.send_context()
    d_key, d_value = finish_keys(dk_own, dv_own, after(dkv_in, down_b.own), cos, sin)
    d_in_term = stacked_columns([d_query, d_key, d_value], qkv, "d_in")
    d_in = feature_sum(d_in_term).astype(F32)

    d_parts = jnp.concatenate([d_query, d_key, d_value], axis=1)
    grad_qkv = Reduction(normed_in, d_parts, 0, "grad_qkv")
    if square:
        grad_out = Reduction(attended_full, d_hidden_own, 0, "grad_out")
    else:
        grad_out = Reduction(attended, features(d_hidden_own), 1, "grad_out")
    grad_qkv.near(d_in_term)
    grad_out.near(grad_qkv.sent)
    grad_gate.mine(grad_out.sent, down_a.other, down_b.other)
    grad_gate.send_context()
    grad_qkv.far(grad_gate.own)
    grad_qkv.send_far()
    grad_out.far(grad_qkv.two)
    grad_out.send_far()
    grad_up.mine(grad_out.two, grad_gate.other)
    grad_up.send_context()
    grad_qkv.mine(grad_up.own, grad_up.other)
    grad_qkv.send_context()
    grad_out.mine(grad_qkv.own)
    out_sum = grad_out.own
    if square:
        count = lax.axis_size("fsdp")
        across = [(i, (i % count) * count + i // count) for i in range(count * count)]
        grad_out.own = lax.ppermute(grad_out.own, ("fsdp", "tensor"), across)
    grad_out.send_context()

    stream = token_low.astype(F32)
    d_in_wide = after(d_in_term, out_sum).astype(F32)
    weighted = d_in_wide * stream
    inner_term = jnp.sum(weighted * gain_attn, axis=1)
    gain_attn_term = jnp.sum(weighted * scale_attn, axis=0)
    parts = lax.axis_size("tensor")
    totals_small = block_totals(
        jnp.concatenate(
            [
                jnp.broadcast_to(inner_term[None, :], (parts, row_count)),
                gain_attn_term.reshape(parts, part_width),
                gain_mlp_term.reshape(parts, part_width),
            ],
            axis=1,
        )[None]
    )
    inner_in = totals_small[0, :row_count][:, None] / full_width
    gain_sums = totals_small[0, row_count:].reshape(2, part_width)
    gain_sums = exchange(gain_sums, "fsdp", 1)
    gain_sums = exchange(gain_sums, "fsdp", 2)
    gain_sums = exchange(gain_sums, "context", 1)
    gain_width = gains.shape[1]
    grad_gains = lax.dynamic_slice_in_dim(
        gain_sums, lax.axis_index("fsdp") * gain_width, gain_width, 1
    )

    grad_down_sum = totals([down_a, down_b], 0, out_sum).reshape(w_down.shape)
    grad_gate_up_sum = totals([grad_gate, grad_up], 1, grad_down_sum)
    grad_qkv_sum = split_totals(grad_qkv, 3, grad_gate_up_sum)
    grad_out_sum = totals([grad_out], 0, grad_qkv_sum)[0]

    block_out = (own_features(hidden) + mlp_out.astype(F32)).astype(BF)
    own_tokens = tokens.astype(F32)
    grad_tokens = (
        d_hidden_own.astype(F32)
        + scale_attn * own_features(gain_attn) * d_in
        - own_tokens * scale_attn * scale_attn * scale_attn * inner_in
    ).astype(BF)
    return (
        block_out,
        grad_tokens,
        jnp.swapaxes(grad_qkv_sum, 0, 1),
        grad_out_sum,
        grad_gate_up_sum,
        grad_down_sum,
        grad_gains,
    )


def solution(mesh):
    rows = P(("fsdp", "context"), "tensor")
    inner = P("fsdp", None, "tensor")
    outer = P("tensor", "fsdp")
    gain = P(None, ("tensor", "fsdp"))
    return jax.shard_map(
        per_device,
        mesh=mesh,
        in_specs=(rows, inner, outer, inner, outer, gain, P("fsdp", None), rows),
        out_specs=(rows, rows, inner, outer, inner, outer, gain),
        check_vma=False,
    )
```
